32 devices in a mesh: dp: 8 (over y, x, core), fsdp: 4 (over z).
Axes of the slice: x: 2, y: 2, z: 4, core: 2. Of those that a mesh axis runs over, the one named last changes fastest.
Arguments:
- tokens: bfloat16 [8, 1024, 960], P('dp', 'fsdp'), may hold values from -6 to 6
- segment_ids: int32 [8, 1024], P('dp', 'fsdp'), may hold values from 0 to 7, never falling along the last dimension, each value on 1 to 512 neighbouring positions
- attn_gain: bfloat16 [960], P('fsdp'), may hold values from 0.5 to 1.5
- query_weight: bfloat16 [960, 960], P('fsdp'), may hold values from -0.1875 to 0.1875
- key_weight: bfloat16 [960, 320], P('fsdp'), may hold values from -0.1875 to 0.1875
- value_weight: bfloat16 [960, 320], P('fsdp'), may hold values from -0.1875 to 0.1875
- out_weight: bfloat16 [960, 960], P('fsdp'), may hold values from -0.75 to 0.75
- ffn_gain: bfloat16 [960], P('fsdp'), may hold values from 0.5 to 1.5
- gate_weight: bfloat16 [960, 2560], P('fsdp'), may hold values from -0.1875 to 0.1875
- up_weight: bfloat16 [960, 2560], P('fsdp'), may hold values from -0.1875 to 0.1875
- down_weight: bfloat16 [2560, 960], P('fsdp'), may hold values from -0.125 to 0.125
- cotangent: bfloat16 [8, 1024, 960], P('dp', 'fsdp'), may hold values from -6 to 6
Outputs:
- output: bfloat16 [8, 1024, 960], P('dp', 'fsdp')
- grad_tokens: float32 [8, 1024, 960], P('dp', 'fsdp')
- grad_attn_gain: float32 [960], P('fsdp')
- grad_query: float32 [960, 960], P('fsdp')
- grad_key: float32 [960, 320], P('fsdp')
- grad_value: float32 [960, 320], P('fsdp')
- grad_out: float32 [960, 960], P('fsdp')
- grad_ffn_gain: float32 [960], P('fsdp')
- grad_gate: float32 [960, 2560], P('fsdp')
- grad_up: float32 [960, 2560], P('fsdp')
- grad_down: float32 [2560, 960], P('fsdp')
The draws below stay inside these ranges and needn't reach their ends.
Inputs may be any that keep to these rules, and one draw needn't show every extreme that they name: `segment_ids`: along each row the ids never fall; each document spans 1 to 512 positions, and one document of each row spans exactly 512.
All inputs are finite; a program needn't handle non-finite values.
Results may differ from the reference program's by a relative error of at most 0.023.
Values may be sent and summed in bfloat16 or wider, within the bound.
No kernel may reach another device: no remote copies, remote signals or barrier semaphores. Data moves between devices by JAX's collectives and lax.ppermute only.
A program may use at most 256 MiB of HBM per device.

```python
import math
import jax
import jax.numpy as jnp
import numpy as np
from jax import lax

D = 960
HEADS = 15
KV_HEADS = 5
HEAD_DIM = 64
FF = 2560
RUNS = 2
GROUP = 3
KVW = 320
LEN = 1024
ROWS = 8


def shard_levels(key, shape, shards, least, top_value):
    loudness = 1.0
    for dim, blocks in shards:
        heights = jax.random.uniform(jax.random.fold_in(jax.random.fold_in(key, 6), dim), (blocks,), jnp.float32, least / len(shards), top_value / len(shards))
        loudness = loudness * jnp.repeat(jnp.exp(heights), shape[dim] // blocks).reshape((-1,) + (1,) * (len(shape) - 1 - dim))
    return loudness


def split_up(count, total, bound, skew):
    portions = [(1 << 20) // math.isqrt(standing ** skew) + 1 for standing in range(2, count + 1)]
    rest, counts = total - bound - (count - 1), [1] * (count - 1)
    while rest > 0:
        movable = [i for i in range(count - 1) if counts[i] < bound]
        pool, remaining = sum([portions[i] for i in movable]), rest
        for i in movable:
            extra = min(bound - counts[i], max(1, remaining * portions[i] // pool), rest)
            counts[i] = counts[i] + extra
            rest = rest - extra
    return np.array([bound] + counts)


def ragged(stream_key, number_of, total, reach, slope):
    if number_of == 2:
        one = jax.random.randint(stream_key, (), max(1, total - reach), min(reach, total - 1) + 1)
        return jnp.stack([one, total - one])
    tallies = jnp.asarray(split_up(number_of, total, reach, slope), jnp.int32)
    pairs = (number_of - 1) // 2
    giver, receiver = tallies[1:1 + 2 * pairs:2], tallies[2:2 + 2 * pairs:2]
    slack = jnp.minimum(giver - 1, reach - receiver)
    shifted = jax.random.randint(jax.random.fold_in(stream_key, 1), (pairs,), 0, 1 << 20) % (slack + 1)
    tallies = tallies.at[1:1 + 2 * pairs:2].set(giver - shifted).at[2:2 + 2 * pairs:2].set(receiver + shifted)
    return tallies[jax.random.permutation(jax.random.fold_in(stream_key, 2), number_of)]


def bell_draw(stream_key, shape, width, limit, pieces=(), kind=jnp.bfloat16):
    entries = width * jax.random.normal(stream_key, shape, jnp.float32)
    if pieces:
        entries = entries * shard_levels(stream_key, shape, pieces, -0.22, 0.18)
    return jnp.clip(entries, -limit, limit).astype(kind)


def setup_inputs(seed: int = 0) -> dict:
    streams_of = jax.random.split(jax.random.key(seed), 13)
    tokens = bell_draw(streams_of[0], (ROWS, LEN, D), 1.0, 6.0, ((0, 8), (1, 4)))
    segment_ids = jax.vmap(lambda own: jnp.searchsorted(jnp.cumsum(ragged(own, 8, LEN, LEN // 2, 1)), jnp.arange(LEN), side="right"))(jax.random.split(streams_of[1], ROWS)).reshape((ROWS, LEN)).astype(jnp.int32)
    attn_gain = jnp.clip(1.0 + 0.1 * jax.random.normal(streams_of[2], (D,), jnp.float32), 0.5, 1.5).astype(jnp.bfloat16)
    query_weight = bell_draw(streams_of[3], (D, D), D ** -0.5, 0.1875, ((0, 4),))
    key_weight = bell_draw(streams_of[4], (D, KVW), D ** -0.5, 0.1875, ((0, 4),))
    value_weight = bell_draw(streams_of[5], (D, KVW), D ** -0.5, 0.1875, ((0, 4),))
    out_weight = bell_draw(streams_of[6], (D, D), (D // 16) ** -0.5, 0.75, ((0, 4),))
    ffn_gain = jnp.clip(1.0 + 0.1 * jax.random.normal(streams_of[7], (D,), jnp.float32), 0.5, 1.5).astype(jnp.bfloat16)
    gate_weight = bell_draw(streams_of[8], (D, FF), D ** -0.5, 0.1875, ((0, 4),))
    up_weight = bell_draw(streams_of[9], (D, FF), D ** -0.5, 0.1875, ((0, 4),))
    down_weight = bell_draw(streams_of[10], (FF, D), FF ** -0.5, 0.125, ((0, 4),))
    cotangent = bell_draw(streams_of[11], (ROWS, LEN, D), 1.0, 6.0, ((0, 8), (1, 4)))
    return {"tokens": tokens, "segment_ids": segment_ids, "attn_gain": attn_gain, "query_weight": query_weight, "key_weight": key_weight, "value_weight": value_weight, "out_weight": out_weight, "ffn_gain": ffn_gain, "gate_weight": gate_weight, "up_weight": up_weight, "down_weight": down_weight, "cotangent": cotangent}


@jax.custom_vjp
def low(v):
    return lax.optimization_barrier(v.astype(jnp.bfloat16)).astype(jnp.float32)

@jax.custom_vjp
def low_back(v):
    return v

def low_keep(v):
    return (low(v), None)

def low_pass(kept, grad):
    return (grad,)

def back_keep(v):
    return (v, None)

def back_low(kept, grad):
    return (low(grad),)
low.defvjp(low_keep, low_pass)
low_back.defvjp(back_keep, back_low)
eps = 1e-05
rope_base = 10000.0
big_negative = -1e+30

def matmul(left, right):
    return jnp.dot(left, right, precision=lax.Precision.HIGHEST)

def rms_norm(hidden_state, gain):
    return hidden_state * lax.rsqrt(lax.optimization_barrier(jnp.mean(hidden_state * hidden_state, axis=-1, keepdims=True)) + eps) * gain

def rotate(values, cos_table, sin_table):
    half = values.shape[-1] // 2
    turned = jnp.concatenate([-values[..., half:], values[..., :half]], axis=-1)
    return values * cos_table + turned * sin_table

def rope_tables(positions):
    freq = rope_base ** (-2.0 * jnp.arange(HEAD_DIM // 2, dtype=jnp.float32) / HEAD_DIM)
    angle = positions.astype(jnp.float32)[..., None] * freq
    angle = jnp.concatenate([angle, angle], axis=-1)
    return (jnp.cos(angle)[..., None, :], jnp.sin(angle)[..., None, :])

def apply_block(state, params, cos_table, sin_table, allowed):
    attn_gain, query_weight, key_weight, value_weight, out_weight, ffn_gain, gate_weight, up_weight, down_weight = params
    length = state.shape[0]
    normed = low(rms_norm(state, attn_gain))
    queries = low(rotate(low_back(matmul(normed, query_weight)).reshape(length, HEADS, HEAD_DIM), cos_table, sin_table))
    keys = low(rotate(low_back(matmul(normed, key_weight)).reshape(length, KV_HEADS, HEAD_DIM), cos_table, sin_table))
    values = low(low_back(matmul(normed, value_weight))).reshape(length, KV_HEADS, HEAD_DIM)
    grouped = queries.reshape(length, KV_HEADS, GROUP, HEAD_DIM)
    scores = jnp.einsum('qkgd,lkd->kgql', grouped, keys, precision=lax.Precision.HIGHEST) * HEAD_DIM ** (-0.5)
    scores = jnp.where(allowed, low_back(scores), big_negative)
    top = lax.optimization_barrier(jnp.max(scores, axis=-1, keepdims=True))
    expo = jnp.exp(scores - top)
    probs = low(expo / lax.optimization_barrier(jnp.sum(expo, axis=-1, keepdims=True)))
    mixed = jnp.einsum('kgql,lkd->qkgd', probs, values, precision=lax.Precision.HIGHEST).reshape(length, D)
    mixed = low(low_back(mixed))
    state = state + low_back(matmul(mixed, out_weight))
    normed = low(rms_norm(state, ffn_gain))
    gate = low_back(matmul(normed, gate_weight))
    up_part = low_back(matmul(normed, up_weight))
    hidden = low(jax.nn.silu(gate) * up_part)
    return state + low_back(matmul(hidden, down_weight))

def reference(tokens, segment_ids, attn_gain, query_weight, key_weight, value_weight, out_weight, ffn_gain, gate_weight, up_weight, down_weight, cotangent):
    params = tuple((w.astype(jnp.float32) for w in (attn_gain, query_weight, key_weight, value_weight, out_weight, ffn_gain, gate_weight, up_weight, down_weight)))
    inputs = tokens.astype(jnp.float32)

    def forward(inputs, params):

        def one_row(pair):
            state, seg_row = pair
            length = seg_row.shape[0]
            index = jnp.arange(length, dtype=jnp.int32)
            starts = lax.optimization_barrier(jnp.sum((seg_row[None, :] < seg_row[:, None]).astype(jnp.int32), axis=1))
            cos_table, sin_table = rope_tables(index - starts)
            allowed = (seg_row[:, None] == seg_row[None, :]) & (index[None, :] <= index[:, None])
            for step in range(RUNS):
                state = apply_block(state, params, cos_table, sin_table, allowed)
            return state
        return lax.map(jax.checkpoint(one_row), (inputs, segment_ids))
    result, pullback = jax.vjp(forward, inputs, params)
    grad_inputs, grads = pullback(cotangent.astype(jnp.float32))
    return (result.astype(jnp.bfloat16), grad_inputs, grads[0], grads[1], grads[2], grads[3], grads[4], grads[5], grads[6], grads[7], grads[8])
```

```python
import jax
import jax.numpy as jnp
from jax import lax
from jax.sharding import PartitionSpec as P

HEADS = 15
KV_HEADS = 5
HEAD_DIM = 64
RUNS = 2
GROUP = 3
KVW = 320
CORE, SIDE, BACK = 1, 2, 4

eps = 1e-05
rope_base = 10000.0
big_negative = -1e30
f32, bf16 = jnp.float32, jnp.bfloat16


def flip(value, bit):
    count = lax.axis_size("dp")
    return lax.ppermute(value, "dp", [(i, i ^ bit) for i in range(count)])


def turn_z(value, step):
    count = lax.axis_size("fsdp")
    return lax.ppermute(value, "fsdp", [(i, (i + step) % count) for i in range(count)])


def home_to_work(value, back=False):
    count, depth = lax.axis_size("dp"), lax.axis_size("fsdp")
    pairs = []
    for d in range(count):
        for z in range(depth):
            there = (d & ~1) | (z & 1), 2 * (d & 1) + (z >> 1)
            pair = (d * depth + z, there[0] * depth + there[1])
            pairs.append(pair[::-1] if back else pair)
    return lax.ppermute(value, ("dp", "fsdp"), pairs)


def place():
    d, z = lax.axis_index("dp"), lax.axis_index("fsdp")
    return d & 1, (d >> 1) & 3, z


def ring_gather(shard):
    z = lax.axis_index("fsdp")
    depth = lax.axis_size("fsdp")
    parts = [shard] + [turn_z(shard, s) for s in range(1, depth)]
    full = jnp.zeros((depth,) + shard.shape, shard.dtype)
    for s, part in enumerate(parts):
        full = lax.dynamic_update_index_in_dim(full, part, (z - s) % depth, 0)
    return full


def plane_gather(piece):
    core, chip, _ = place()
    half = piece.shape[0] // 2
    top, bottom = piece[:half], piece[half:]
    x_top, y_top = flip(top, SIDE), flip(top, BACK)
    x_bottom, y_bottom = flip(bottom, SIDE), flip(bottom, BACK)
    d_top, d_bottom = flip(x_top, BACK), flip(y_bottom, SIDE)
    full = jnp.zeros((2, 4) + piece.shape, piece.dtype)
    rest = (0,) * (piece.ndim - 1)
    for who, (t, b) in enumerate(
        ((top, bottom), (x_top, x_bottom), (y_top, y_bottom), (d_top, d_bottom))
    ):
        at = chip ^ who
        full = lax.dynamic_update_slice(full, t[None, None], (core, at, 0) + rest)
        full = lax.dynamic_update_slice(full, b[None, None], (core, at, half) + rest)
        t2, b2 = flip(t, CORE), flip(b, CORE)
        full = lax.dynamic_update_slice(full, t2[None, None], (1 - core, at, 0) + rest)
        full = lax.dynamic_update_slice(full, b2[None, None], (1 - core, at, half) + rest)
    return full


def gather_weights(query, key, value, out, gate, up, down):
    core, chip, _ = place()
    rows = query.shape[0]
    depth = lax.axis_size("fsdp")
    which = core * 4 + chip
    width = query.shape[1]
    first = jnp.concatenate([query, key, value, out], axis=1)
    n = first.shape[1] // 8
    piece = lax.dynamic_slice(first, (0, n * which), (rows, n))
    piece = ring_gather(piece).reshape(depth * rows, n)
    first = plane_gather(piece)
    first = jnp.concatenate([first[c, m] for c in range(2) for m in range(4)], axis=1)
    query = first[:, :width]
    key = first[:, width : width + KVW]
    value = first[:, width + KVW : width + 2 * KVW]
    out = first[:, width + 2 * KVW :]
    n = gate.shape[1] // 4
    mine = jnp.where(core == 0, gate, up)
    piece = lax.dynamic_slice(mine, (0, n * chip), (rows, n))
    piece = ring_gather(piece).reshape(depth * rows, n)
    both = plane_gather(piece)
    n = down.shape[0] // 2
    piece = lax.dynamic_slice(down, (n * core, 0), (n, width))
    piece = ring_gather(piece)
    other = flip(piece, CORE)
    full = jnp.zeros((depth, 2) + piece.shape[1:], piece.dtype)
    full = lax.dynamic_update_slice(full, piece[:, None], (0, core, 0, 0))
    full = lax.dynamic_update_slice(full, other[:, None], (0, 1 - core, 0, 0))
    return query, key, value, out, both[0], both[1], full.reshape(depth, 2 * n, width)


def rms_norm(hidden_state, gain):
    return (
        hidden_state
        * lax.rsqrt(jnp.mean(hidden_state * hidden_state, axis=-1, keepdims=True) + eps)
        * gain
    )


def rotate(values, cos_table, sin_table):
    half = values.shape[-1] // 2
    turned = jnp.concatenate([-values[..., half:], values[..., :half]], axis=-1)
    return values * cos_table + turned * sin_table


def rotate_back(values, cos_table, sin_table):
    half = values.shape[-1] // 2
    scaled = values * sin_table
    turned = jnp.concatenate([scaled[..., half:], -scaled[..., :half]], axis=-1)
    return values * cos_table + turned


def rope_tables(positions):
    freq = rope_base ** (-2.0 * jnp.arange(HEAD_DIM // 2, dtype=f32) / HEAD_DIM)
    angle = positions.astype(f32)[..., None] * freq
    angle = jnp.concatenate([angle, angle], axis=-1)
    return (jnp.cos(angle)[..., None, :], jnp.sin(angle)[..., None, :])


def window(own):
    core = lax.axis_index("dp") & 1
    count, depth = lax.axis_size("dp"), lax.axis_size("fsdp")
    ups = [(z, z + 1) for z in range(0, depth, 2)]
    far = lax.ppermute(own, "fsdp", ups)
    near = flip(jnp.where(core == 0, own, far), CORE)
    return jnp.concatenate([far, near, own], axis=0)


def unwindow(grads):
    n = grads.shape[0] // 3
    core = lax.axis_index("dp") & 1
    depth = lax.axis_size("fsdp")
    downs = [(z + 1, z) for z in range(0, depth, 2)]
    far, near, own = grads[:n], grads[n : 2 * n], grads[2 * n :]
    near = flip(near.astype(bf16), CORE).astype(f32)
    far = jnp.where(core == 1, far + near, far).astype(bf16)
    own = jnp.where(core == 0, own + near, own)
    return own + lax.ppermute(far, "fsdp", downs).astype(f32)


def attention_scores(queries, keys_all, allowed):
    stretch = queries.shape[0]
    grouped = queries.reshape(stretch, KV_HEADS, GROUP, HEAD_DIM)
    scores = jnp.einsum(
        "ckgd,lkd->kgcl", grouped, keys_all, preferred_element_type=f32
    ) * HEAD_DIM ** (-0.5)
    return (grouped, jnp.where(allowed, scores, big_negative))


def dot(a, b):
    return jnp.dot(a, b, preferred_element_type=f32)


def forward_run(flat, weights, tables, allowed):
    attn_gain, query_weight, key_weight, value_weight, out_weight, ffn_gain, gate_weight, up_weight, down_weight = weights
    cos_table, sin_table = tables
    stretch, width = flat.shape
    normed = rms_norm(flat, attn_gain.astype(f32)).astype(bf16)
    query_pre = dot(normed, query_weight).reshape(stretch, HEADS, HEAD_DIM)
    key_pre = dot(normed, key_weight).reshape(stretch, KV_HEADS, HEAD_DIM)
    value_local = dot(normed, value_weight).astype(bf16)
    queries = rotate(query_pre, cos_table, sin_table).astype(bf16)
    keys = rotate(key_pre, cos_table, sin_table).astype(bf16).reshape(stretch, KVW)
    keys_all = window(keys).reshape(-1, KV_HEADS, HEAD_DIM)
    values_all = window(value_local).reshape(-1, KV_HEADS, HEAD_DIM)
    grouped, scores = attention_scores(queries, keys_all, allowed)
    top = jnp.max(scores, axis=-1, keepdims=True)
    expo = jnp.exp(scores - top)
    total = jnp.sum(expo, axis=-1, keepdims=True)
    probs = (expo / total).astype(bf16)
    log_total = top + jnp.log(total)
    mixed = jnp.einsum("kgcl,lkd->ckgd", probs, values_all, preferred_element_type=f32)
    mixed = mixed.astype(bf16).reshape(stretch, width)
    after_attn = flat + dot(mixed, out_weight)
    normed_ffn = rms_norm(after_attn, ffn_gain.astype(f32)).astype(bf16)
    gate = [dot(normed_ffn, gate_weight[m]) for m in range(4)]
    up_part = [dot(normed_ffn, up_weight[m]) for m in range(4)]
    hidden = [(jax.nn.silu(g) * u).astype(bf16) for g, u in zip(gate, up_part)]
    result = after_attn
    for m in range(4):
        result = result + dot(hidden[m], down_weight[m])
    saved = (flat, normed, queries, keys_all, values_all, log_total, mixed, after_attn, normed_ffn, gate, up_part, hidden)
    return result, saved


def backward_ffn(grad_next, saved, weights):
    attn_gain, query_weight, key_weight, value_weight, out_weight, ffn_gain, gate_weight, up_weight, down_weight = weights
    flat, normed, queries, keys_all, values_all, log_total, mixed, after_attn, normed_ffn, gate, up_part, hidden = saved
    grad_low = grad_next.astype(bf16)
    grad_normed_ffn = None
    d_gate, d_up = [], []
    for m in range(4):
        grad_hidden = jnp.einsum("td,fd->tf", grad_low, down_weight[m], preferred_element_type=f32)
        _, act_back = jax.vjp(lambda g_in, u_in: jax.nn.silu(g_in) * u_in, gate[m], up_part[m])
        dg, du = act_back(grad_hidden)
        dg, du = dg.astype(bf16), du.astype(bf16)
        part = jnp.einsum("tf,df->td", dg, gate_weight[m], preferred_element_type=f32)
        part = part + jnp.einsum("tf,df->td", du, up_weight[m], preferred_element_type=f32)
        grad_normed_ffn = part if grad_normed_ffn is None else grad_normed_ffn + part
        d_gate.append(dg)
        d_up.append(du)
    _, norm_back = jax.vjp(rms_norm, after_attn, ffn_gain.astype(f32))
    grad_after_part, grad_ffn_gain = norm_back(grad_normed_ffn)
    grad_after = grad_next + grad_after_part
    return grad_after, grad_ffn_gain, (normed_ffn, jnp.concatenate(d_gate, 1), jnp.concatenate(d_up, 1), jnp.concatenate(hidden, 1), grad_low)


def backward_attention(grad_after, saved, weights, tables, allowed):
    attn_gain, query_weight, key_weight, value_weight, out_weight, ffn_gain, gate_weight, up_weight, down_weight = weights
    flat, normed, queries, keys_all, values_all, log_total, mixed, after_attn, normed_ffn, gate, up_part, hidden = saved
    cos_table, sin_table = tables
    stretch, width = flat.shape
    low = grad_after.astype(bf16)
    grad_mixed = jnp.einsum("te,de->td", low, out_weight, preferred_element_type=f32)
    grad_mixed = grad_mixed.astype(bf16).reshape(stretch, KV_HEADS, GROUP, HEAD_DIM)
    grouped, scores = attention_scores(queries, keys_all, allowed)
    probs_full = jnp.exp(scores - log_total)
    probs = probs_full.astype(bf16)
    grad_probs = jnp.einsum("ckgd,lkd->kgcl", grad_mixed, values_all, preferred_element_type=f32)
    grad_values_all = jnp.einsum("kgcl,ckgd->lkd", probs, grad_mixed, preferred_element_type=f32)
    inner = jnp.sum(probs_full * grad_probs, axis=-1, keepdims=True)
    grad_scores = (probs_full * (grad_probs - inner)).astype(bf16)
    grad_queries = jnp.einsum("kgcl,lkd->ckgd", grad_scores, keys_all, preferred_element_type=f32) * HEAD_DIM ** (-0.5)
    grad_keys_all = jnp.einsum("kgcl,ckgd->lkd", grad_scores, grouped, preferred_element_type=f32) * HEAD_DIM ** (-0.5)
    grad_keys = unwindow(grad_keys_all.reshape(-1, KVW)).reshape(stretch, KV_HEADS, HEAD_DIM)
    grad_value_pre = unwindow(grad_values_all.reshape(-1, KVW)).astype(bf16)
    grad_queries = grad_queries.reshape(stretch, HEADS, HEAD_DIM)
    grad_query_pre = rotate_back(grad_queries, cos_table, sin_table).astype(bf16).reshape(stretch, width)
    grad_key_pre = rotate_back(grad_keys, cos_table, sin_table).astype(bf16).reshape(stretch, KVW)
    grad_normed = jnp.einsum("te,de->td", grad_query_pre, query_weight, preferred_element_type=f32)
    grad_normed = grad_normed + jnp.einsum("te,de->td", grad_key_pre, key_weight, preferred_element_type=f32)
    grad_normed = grad_normed + jnp.einsum("te,de->td", grad_value_pre, value_weight, preferred_element_type=f32)
    _, norm_first_back = jax.vjp(rms_norm, flat, attn_gain.astype(f32))
    grad_flat_part, grad_attn_gain = norm_first_back(grad_normed)
    grad_input = grad_after + grad_flat_part
    return grad_input, grad_attn_gain, (normed, grad_query_pre, grad_key_pre, grad_value_pre, mixed, low)


def over_groups(value):
    bit = 8
    while bit < lax.axis_size("dp"):
        value = value + flip(value, bit)
        bit *= 2
    return value


def tokens_dot(left, right):
    return jnp.einsum("td,tf->df", left, right, preferred_element_type=f32)


def plane_reduce(make):
    _, chip, _ = place()
    dg, xn = make(chip ^ 3).astype(bf16), make(chip ^ 1).astype(bf16)
    yn, own = make(chip ^ 2).astype(bf16), make(chip)
    half = own.shape[0] // 2
    dg_x, xn_x = flip(dg[:half], SIDE), flip(xn[:half], SIDE)
    dg_y, yn_y = flip(dg[half:], BACK), flip(yn[half:], BACK)
    yn_top = (yn[:half].astype(f32) + dg_x.astype(f32)).astype(bf16)
    xn_bottom = (xn[half:].astype(f32) + dg_y.astype(f32)).astype(bf16)
    yn_top, xn_bottom = flip(yn_top, BACK), flip(xn_bottom, SIDE)
    top = own[:half] + xn_x.astype(f32) + yn_top.astype(f32)
    bottom = own[half:] + yn_y.astype(f32) + xn_bottom.astype(f32)
    return jnp.concatenate([top, bottom], axis=0)


def ring_reduce(parts):
    z = lax.axis_index("fsdp")
    depth = lax.axis_size("fsdp")
    low = parts.astype(bf16)
    total = lax.dynamic_index_in_dim(parts, z, 0, keepdims=False)
    for s in range(1, depth):
        part = lax.dynamic_index_in_dim(low, (z + s) % depth, 0, keepdims=False)
        total = total + turn_z(part, s).astype(f32)
    return total


def chips_gather(piece, axis):
    _, chip, _ = place()
    x, y, dg = flip(piece, SIDE), flip(piece, BACK), flip(piece, SIDE | BACK)
    shape = list(piece.shape)
    n = shape[axis]
    shape[axis] *= 4
    full = jnp.zeros((4,) + piece.shape, piece.dtype)
    for who, part in enumerate((piece, x, y, dg)):
        full = lax.dynamic_update_index_in_dim(full, part, chip ^ who, 0)
    return full


def split_reduce(make):
    core, _, _ = place()
    depth = lax.axis_size("fsdp")
    piece = plane_reduce(make)
    piece = piece.reshape((depth, piece.shape[0] // depth) + piece.shape[1:])
    piece = over_groups(ring_reduce(piece)).astype(bf16)
    mine = chips_gather(piece, 1)
    other = flip(mine, CORE)
    return jnp.where(core == 0, mine, other), jnp.where(core == 0, other, mine)


def pair_tokens(mine_first, mine_second, core):
    sent = jnp.where(core == 0, mine_second, mine_first)
    kept = jnp.where(core == 0, mine_first, mine_second)
    return jnp.concatenate([kept, flip(sent, CORE)], axis=0)


def both_tokens(value):
    return jnp.concatenate([value, flip(value, CORE)], axis=0)


def join(parts):
    return jnp.concatenate([parts[m] for m in range(4)], axis=1).astype(f32)


def reduce_ffn(saves):
    core, chip, z = place()
    depth = lax.axis_size("fsdp")
    normed, dg, du, hidden, low = (jnp.concatenate(v, axis=0) for v in zip(*saves))
    width = normed.shape[1]
    rows = hidden.shape[1] // depth
    half = 2 * rows
    z_both = pair_tokens(hidden[:, :half], hidden[:, half:], core)
    low_both = both_tokens(low)
    down = tokens_dot(z_both, low_both).reshape(2, rows, width)
    low_down = down.astype(bf16)
    total = jnp.where((z >> 1) == core, lax.dynamic_index_in_dim(down, z & 1, 0, keepdims=False), 0.0)
    count = lax.axis_size("dp")
    for s in range(1, depth):
        part = lax.dynamic_index_in_dim(low_down, (z + s) & 1, 0, keepdims=False)
        pairs = []
        for d in range(count):
            for a in range(depth):
                b = (a + s) % depth
                if (b >> 1) == (d & 1):
                    pairs.append((d * depth + a, d * depth + b))
        total = total + lax.ppermute(part, ("dp", "fsdp"), pairs).astype(f32)
    n = rows // 8
    owner = (z >> 1) == core
    mine = total.reshape(2, rows // 2, width)
    given = flip(mine.astype(bf16), CORE).astype(f32)
    mine = lax.dynamic_index_in_dim(jnp.where(owner, mine, given), core, 0, keepdims=False)
    mine = mine.reshape(4, n, width)
    summed = over_groups(plane_reduce(lambda m: lax.dynamic_index_in_dim(mine, m, 0, keepdims=False))).astype(bf16)
    summed = chips_gather(summed, 0).reshape(rows // 2, width)
    other = flip(summed, CORE)
    grad_down = jnp.where(core == 0, jnp.concatenate([summed, other]), jnp.concatenate([other, summed])).astype(f32)
    act = pair_tokens(dg, du, core)
    b_both = both_tokens(normed)
    n = act.shape[1] // 4

    def make(m):
        return tokens_dot(b_both, lax.dynamic_slice_in_dim(act, m * n, n, 1))

    grad_gate, grad_up = split_reduce(make)
    return join(grad_gate), join(grad_up), grad_down


def reduce_attention(saves):
    core, chip, z = place()
    normed, dq, dk, dv, mixed, low = (jnp.concatenate(v, axis=0) for v in zip(*saves))
    width = normed.shape[1]
    n = KVW
    zero = jnp.zeros_like(low)
    first = jnp.concatenate([dq, dk], axis=1)
    second = jnp.concatenate([dv, low], axis=1)
    right = pair_tokens(first, second, core)
    left_a = both_tokens(normed)
    left_o = both_tokens(mixed)

    def make(m):
        cols = lax.dynamic_slice_in_dim(right, m * n, n, 1)
        left = jnp.where((core == 1) & (m > 0), left_o, left_a)
        return tokens_dot(left, cols)

    qk, vo = split_reduce(make)
    qk, vo = join(qk), join(vo)
    return qk[:, :width], qk[:, width:], vo[:, :KVW], vo[:, KVW:]


def reduce_gains(gains):
    z = lax.axis_index("fsdp")
    depth = lax.axis_size("fsdp")
    total = jnp.stack(gains)
    bit = 1
    while bit < lax.axis_size("dp"):
        total = total + flip(total, bit)
        bit *= 2
    rows = total.shape[1] // depth
    total = total + sum(turn_z(total, s) for s in range(1, depth))
    mine = lax.dynamic_slice_in_dim(total, z * rows, rows, 1)
    return mine[0], mine[1]


def body(tokens, segment_ids, attn_gain, query_weight, key_weight, value_weight, out_weight, ffn_gain, gate_weight, up_weight, down_weight, cotangent):
    core, chip, z = place()
    _, stretch, width = tokens.shape
    depth = lax.axis_size("fsdp")
    gains = ring_gather(jnp.stack([attn_gain, ffn_gain]))
    gains = jnp.moveaxis(gains, 0, 1).reshape(2, width)
    tokens = home_to_work(tokens[0])
    row = ring_gather(segment_ids[0]).reshape(-1)
    other = flip(row, CORE)
    row = jnp.where((z >> 1) == core, row, other)
    block = 2 * (z & 1) + core
    padded = jnp.concatenate([jnp.full((2 * stretch,), -1, row.dtype), row])
    key_segments = lax.dynamic_slice(padded, (block * stretch,), (3 * stretch,))
    own_segments = key_segments[2 * stretch :]
    key_index = jnp.arange(3 * stretch, dtype=jnp.int32)
    query_index = 2 * stretch + jnp.arange(stretch, dtype=jnp.int32)
    allowed = (own_segments[:, None] == key_segments[None, :]) & (key_index[None, :] <= query_index[:, None])
    positions = jnp.sum(allowed.astype(jnp.int32), axis=1) - 1
    tables = rope_tables(positions)
    allowed = allowed[None, None]
    q, k, v, o, g, u, dn = gather_weights(query_weight, key_weight, value_weight, out_weight, gate_weight, up_weight, down_weight)
    weights = (gains[0], q, k, v, o, gains[1], g, u, dn)
    cot = home_to_work(cotangent[0])
    state = tokens.astype(f32)
    saved_runs = []
    for step in range(RUNS):
        state, saved = forward_run(state, weights, tables, allowed)
        saved_runs.append(saved)
    output = home_to_work(state.astype(bf16), back=True)
    grad_state = cot.astype(f32)
    ffn_saves, attn_saves = [], []
    gain_attn = gain_ffn = 0.0
    for saved in reversed(saved_runs):
        grad_state, gain, save = backward_ffn(grad_state, saved, weights)
        gain_ffn = gain_ffn + gain
        ffn_saves.append(save)
        grad_state, gain, save = backward_attention(grad_state, saved, weights, tables, allowed)
        gain_attn = gain_attn + gain
        attn_saves.append(save)
    grad_tokens = home_to_work(grad_state.astype(bf16), back=True).astype(f32)
    grad_gate, grad_up, grad_down = reduce_ffn(ffn_saves)
    grad_query, grad_key, grad_value, grad_out = reduce_attention(attn_saves)
    gain_attn, gain_ffn = reduce_gains((gain_attn, gain_ffn))
    return (output[None], grad_tokens[None], gain_attn, grad_query, grad_key, grad_value, grad_out, gain_ffn, grad_gate, grad_up, grad_down)


def solution(mesh):
    wide, rows, shard = P("dp", "fsdp", None), P("dp", "fsdp"), P("fsdp", None)
    in_specs = (wide, rows, P("fsdp"), shard, shard, shard, shard, P("fsdp"), shard, shard, shard, wide)
    out_specs = (wide, wide, P("fsdp"), shard, shard, shard, shard, P("fsdp"), shard, shard, shard)
    return jax.shard_map(body, mesh=mesh, in_specs=in_specs, out_specs=out_specs, check_vma=False)
```

```python
import functools
import jax
import jax.numpy as jnp
from jax import lax
from jax.sharding import PartitionSpec as P
from jax.experimental import pallas as pl
from jax.experimental.pallas import tpu as pltpu

f32, bf16 = jnp.float32, jnp.bfloat16
eps = 1e-05
HEADS, KV_HEADS, HEAD_DIM, GROUP, KVW = 15, 5, 64, 3, 320
MIB = 1 << 20
WHOLE = pl.BlockSpec(memory_space=pltpu.VMEM)
LEFT = pl.BlockSpec(memory_space=pl.ANY)
SCALARS = pl.BlockSpec(memory_space=pltpu.SMEM)


def contract(a, b, i, j):
    return lax.dot_general(a, b, (((i,), (j,)), ((), ())), preferred_element_type=f32)


def nn(a, b):
    return contract(a, b, 1, 0)


def nt(a, b):
    return contract(a, b, 1, 1)


def tn(a, b):
    return contract(a, b, 0, 0)


def fetch(mine, other, kept, sems, core, chip):
    for who in range(4):
        at = chip ^ who
        pltpu.make_async_copy(mine[who], kept.at[core, at], sems.at[core, at]).start()
    for who in range(4):
        at = chip ^ who
        pltpu.make_async_copy(other[who], kept.at[1 - core, at], sems.at[1 - core, at]).start()


def arrived(kept, sems, *at):
    pltpu.make_async_copy(kept.at[at], kept.at[at], sems.at[at]).wait()


def normed(x, gain):
    return x * lax.rsqrt(jnp.mean(x * x, axis=-1, keepdims=True) + eps) * gain


def norm_back(x, gain, grad):
    r = lax.rsqrt(jnp.mean(x * x, axis=-1, keepdims=True) + eps)
    hat = x * r
    scaled = grad * gain
    dx = r * (scaled - hat * jnp.mean(scaled * hat, axis=-1, keepdims=True))
    return dx, jnp.sum(grad * hat, axis=0, keepdims=True)


def rope(u, cos, sin, back):
    heads = u.shape[0] // HEAD_DIM
    half = HEAD_DIM // 2
    out = []
    for h in range(heads):
        u1, u2 = u[h * HEAD_DIM : h * HEAD_DIM + half], u[h * HEAD_DIM + half : (h + 1) * HEAD_DIM]
        if back:
            out += [u1 * cos + u2 * sin, u2 * cos - u1 * sin]
        else:
            out += [u1 * cos - u2 * sin, u2 * cos + u1 * sin]
    return jnp.concatenate(out, axis=0)


def project(state, gain_ref, cos_ref, sin_ref, kept, sems, a_ref, q_ref, kv_ref):
    a = normed(state, gain_ref[...]).astype(bf16)
    a_ref[...] = a
    cos, sin = cos_ref[...], sin_ref[...]
    arrived(kept, sems, 0, 3)
    kv_ref[:KVW, :] = rope(nn(a, kept[0, 3]).T, cos, sin, False).astype(bf16)
    arrived(kept, sems, 1, 0)
    kv_ref[KVW:, :] = nn(a, kept[1, 0]).T.astype(bf16)
    for m in range(3):
        arrived(kept, sems, 0, m)
        q_ref[pl.ds(m * KVW, KVW), :] = rope(nn(a, kept[0, m]).T, cos, sin, False).astype(bf16)


def pre_kernel(sc, h_ref, gain_ref, cos_ref, sin_ref, *rest):
    mine, other = rest[:4], rest[4:8]
    a_ref, q_ref, kv_ref, kept, sems = rest[8:]
    core, chip = sc[0], sc[1]
    fetch(mine, other, kept, sems, core, chip)
    project(h_ref[...].astype(f32), gain_ref, cos_ref, sin_ref, kept, sems, a_ref, q_ref, kv_ref)
    for m in range(1, 4):
        arrived(kept, sems, 1, m)


def scratch_a(width):
    return [pltpu.VMEM((2, 4, width, KVW), bf16), pltpu.SemaphoreType.DMA((2, 4))]


def shape(s, d):
    return jax.ShapeDtypeStruct(s, d)


def pre(sc, h, gain, cos, sin, mine_a, other_a):
    n, width = h.shape
    return pl.pallas_call(
        pre_kernel,
        out_shape=(shape((n, width), bf16), shape((width, n), bf16), shape((2 * KVW, n), bf16)),
        in_specs=[SCALARS] + [WHOLE] * 4 + [LEFT] * 8,
        out_specs=(WHOLE,) * 3,
        scratch_shapes=scratch_a(width),
        compiler_params=pltpu.CompilerParams(vmem_limit_bytes=24 * MIB),
        name="pre",
    )(sc, h, gain, cos, sin, *mine_a, *other_a)


def bias_of(seg_k, seg_q):
    keys, n = seg_k.shape[0], seg_q.shape[1]
    j = lax.broadcasted_iota(jnp.int32, (keys, n), 0)
    i = lax.broadcasted_iota(jnp.int32, (keys, n), 1) + (keys - n)
    return jnp.where((seg_k == seg_q) & (j <= i), 0.0, -1e30).astype(f32)


def window_of(parts, whole):
    n = parts[0].shape[1]
    for w, part in enumerate(parts):
        whole[:, w * n : (w + 1) * n] = part[...]


def attend_kernel(q_ref, kv0, kv1, kv2, sk_ref, sq_ref, o_ref, lse_ref, bias, kv):
    bias[...] = bias_of(sk_ref[...], sq_ref[...])
    window_of((kv0, kv1, kv2), kv)

    def head(e, _):
        row = pl.multiple_of(e * HEAD_DIM, HEAD_DIM)
        k = kv[pl.ds(row, HEAD_DIM), :]
        v = kv[pl.ds(row + KVW, HEAD_DIM), :]
        for g in range(GROUP):
            at = pl.multiple_of((e * GROUP + g) * HEAD_DIM, HEAD_DIM)
            q = q_ref[pl.ds(at, HEAD_DIM), :]
            s = tn(k, q) * HEAD_DIM ** (-0.5) + bias[...]
            top = jnp.max(s, axis=0, keepdims=True)
            expo = jnp.exp(s - top)
            total = jnp.sum(expo, axis=0, keepdims=True)
            probs = (expo * (1.0 / total)).astype(bf16)
            o_ref[pl.ds(at, HEAD_DIM), :] = nn(v, probs).astype(bf16)
            lse_ref[pl.ds(e * GROUP + g, 1), :] = top + jnp.log(total)
        return 0

    lax.fori_loop(0, KV_HEADS, head, 0)


def attend(q, kvs, seg_k, seg_q):
    width, n = q.shape
    return pl.pallas_call(
        attend_kernel,
        out_shape=(shape((width, n), bf16), shape((HEADS, n), f32)),
        in_specs=[WHOLE] * 6,
        out_specs=(WHOLE,) * 2,
        scratch_shapes=[pltpu.VMEM((3 * n, n), f32), pltpu.VMEM((2 * KVW, 3 * n), bf16)],
        compiler_params=pltpu.CompilerParams(vmem_limit_bytes=24 * MIB),
        name="attend",
    )(q, *kvs, seg_k, seg_q)


def attend_back_kernel(q_ref, kv0, kv1, kv2, sk_ref, sq_ref, lse_ref, do_ref, cos_ref, sin_ref, dq_ref, far_ref, near_ref, own_ref, bias, kv, dqs):
    n = q_ref.shape[1]
    bias[...] = bias_of(sk_ref[...], sq_ref[...])
    window_of((kv0, kv1, kv2), kv)
    scale = HEAD_DIM ** (-0.5)

    def head(e, _):
        row = pl.multiple_of(e * HEAD_DIM, HEAD_DIM)
        k = kv[pl.ds(row, HEAD_DIM), :]
        v = kv[pl.ds(row + KVW, HEAD_DIM), :]
        dk = dv = None
        for g in range(GROUP):
            at = pl.multiple_of((e * GROUP + g) * HEAD_DIM, HEAD_DIM)
            q = q_ref[pl.ds(at, HEAD_DIM), :]
            do = do_ref[pl.ds(at, HEAD_DIM), :]
            s = tn(k, q) * scale + bias[...]
            probs = jnp.exp(s - lse_ref[pl.ds(e * GROUP + g, 1), :])
            dp = tn(v, do)
            inner = jnp.sum(probs * dp, axis=0, keepdims=True)
            ds = (probs * (dp - inner)).astype(bf16)
            dvg, dkg = nt(do, probs.astype(bf16)), nt(q, ds)
            dv, dk = (dvg, dkg) if g == 0 else (dv + dvg, dk + dkg)
            dqs[pl.ds(at, HEAD_DIM), :] = nn(k, ds)
        for at, grad in ((row, dk * scale), (row + KVW, dv)):
            far_ref[pl.ds(at, HEAD_DIM), :] = grad[:, :n]
            near_ref[pl.ds(at, HEAD_DIM), :] = grad[:, n : 2 * n].astype(bf16)
            own_ref[pl.ds(at, HEAD_DIM), :] = grad[:, 2 * n :]
        return 0

    lax.fori_loop(0, KV_HEADS, head, 0)
    cos, sin = cos_ref[...] * scale, sin_ref[...] * scale
    for m in range(3):
        dq_ref[m] = rope(dqs[m * KVW : (m + 1) * KVW, :], cos, sin, True).T.astype(bf16)


def attend_back(q, kvs, seg_k, seg_q, lse, do, cos, sin):
    width, n = q.shape
    block = (2 * KVW, n)
    return pl.pallas_call(
        attend_back_kernel,
        out_shape=(shape((3, n, KVW), bf16), shape(block, f32), shape(block, bf16), shape(block, f32)),
        in_specs=[WHOLE] * 10,
        out_specs=(WHOLE,) * 4,
        scratch_shapes=[pltpu.VMEM((3 * n, n), f32), pltpu.VMEM((2 * KVW, 3 * n), bf16), pltpu.VMEM((width, n), f32)],
        compiler_params=pltpu.CompilerParams(vmem_limit_bytes=32 * MIB),
        name="attend_back",
    )(q, *kvs, seg_k, seg_q, lse, do, cos, sin)


def fetch_ffn(mine_b, other_b, mine_d, other_d, wb, wd, sem_b, sem_d, core, chip):
    fetch(mine_b, other_b, wb, sem_b, core, chip)
    pltpu.make_async_copy(mine_d, wd.at[:, core], sem_d.at[0]).start()
    pltpu.make_async_copy(other_d, wd.at[:, 1 - core], sem_d.at[1]).start()


def arrived_down(mine_d, wd, sem_d):
    for c in range(2):
        pltpu.make_async_copy(mine_d, wd.at[:, c], sem_d.at[c]).wait()


def down_of(wd, m):
    rows = wd.shape[1] * wd.shape[2]
    return wd[m].reshape(rows, wd.shape[3])


def scratch_ffn(width, n, rows):
    return [
        pltpu.VMEM((2, 4, width, n), bf16),
        pltpu.SemaphoreType.DMA((2, 4)),
        pltpu.VMEM((4, 2, rows, width), bf16),
        pltpu.SemaphoreType.DMA((2,)),
    ]


def post_kernel(last, sc, ot_ref, h_ref, gain_ref, gain_a, cos_ref, sin_ref, *rest):
    mine_a, other_a, mine_b, other_b = rest[:4], rest[4:8], rest[8:12], rest[12:16]
    mine_d, other_d = rest[16:18]
    o_ref, h1_ref, b_ref, gate_ref, up_ref, z_ref, next_ref = rest[18:25]
    more, rest = rest[25 : 25 + (0 if last else 3)], rest[25 + (0 if last else 3) :]
    wa, sem_a, wb, sem_b, wd, sem_d = rest
    core, chip = sc[0], sc[1]
    fetch(mine_a, other_a, wa, sem_a, core, chip)
    fetch_ffn(mine_b, other_b, mine_d, other_d, wb, wd, sem_b, sem_d, core, chip)
    o = ot_ref[...].T
    o_ref[...] = o
    for m in range(1, 4):
        arrived(wa, sem_a, 1, m)
    h1 = h_ref[...].astype(f32) + jnp.concatenate([nn(o, wa[1, m]) for m in range(1, 4)], axis=1)
    h1_ref[...] = h1
    b = normed(h1, gain_ref[...]).astype(bf16)
    b_ref[...] = b
    n = wb.shape[3]
    total = h1
    for m in range(4):
        cols = slice(m * n, (m + 1) * n)
        arrived(wb, sem_b, 0, m)
        gate = nn(b, wb[0, m])
        arrived(wb, sem_b, 1, m)
        up = nn(b, wb[1, m])
        gate_ref[:, cols] = gate.astype(bf16)
        up_ref[:, cols] = up.astype(bf16)
        z = (gate / (1.0 + jnp.exp(-gate)) * up).astype(bf16)
        z_ref[:, cols] = z
        if m == 0:
            arrived_down(mine_d, wd, sem_d)
        total = total + nn(z, down_of(wd, m))
    next_ref[...] = total.astype(next_ref.dtype)
    if last:
        arrived(wa, sem_a, 1, 0)
        for m in range(4):
            arrived(wa, sem_a, 0, m)
    else:
        project(total, gain_a, cos_ref, sin_ref, wa, sem_a, *more)


def post(last, sc, ot, h, gain, gain_a, cos, sin, wa, wb, wd):
    width, n = ot.shape
    hidden = wb[0][0].shape[1] * 4
    outs = [shape((n, width), bf16), shape((n, width), f32), shape((n, width), bf16)] + [shape((n, hidden), bf16)] * 3
    outs += [shape((n, width), bf16 if last else f32)]
    if not last:
        outs += [shape((n, width), bf16), shape((width, n), bf16), shape((2 * KVW, n), bf16)]
    return pl.pallas_call(
        functools.partial(post_kernel, last),
        out_shape=tuple(outs),
        in_specs=[SCALARS] + [WHOLE] * 6 + [LEFT] * 18,
        out_specs=(WHOLE,) * len(outs),
        scratch_shapes=scratch_a(width) + scratch_ffn(width, hidden // 4, wd[0].shape[1]),
        compiler_params=pltpu.CompilerParams(vmem_limit_bytes=56 * MIB),
        name="post",
    )(sc, ot, h, gain, gain_a, cos, sin, *wa[0], *wa[1], *wb[0], *wb[1], *wd)


def ffn_back(state, core, refs, weights, mine_d):
    gate_ref, up_ref, h1_ref, gain_ref, z_ref, gb_ref, keep_ref, send_ref, zk_ref, zs_ref, g1_ref, p_ref, dgain_ref, do_ref = refs
    wa, sem_a, wb, sem_b, wd, sem_d = weights
    gb = state.astype(bf16)
    gb_ref[...] = gb
    n = wb.shape[3]
    half = 2 * n
    first = core == 0
    low, high = z_ref[:, :half], z_ref[:, half:]
    zk_ref[...] = jnp.where(first, low, high)
    zs_ref[...] = jnp.where(first, high, low)
    arrived_down(mine_d, wd, sem_d)
    db = None
    for m in range(4):
        cols = slice(m * n, (m + 1) * n)
        dz = nt(gb, down_of(wd, m))
        gate, up = gate_ref[:, cols].astype(f32), up_ref[:, cols].astype(f32)
        sig = 1.0 / (1.0 + jnp.exp(-gate))
        dup = (dz * (gate * sig)).astype(bf16)
        dgate = (dz * up * (sig * (1.0 + gate * (1.0 - sig)))).astype(bf16)
        keep_ref[:, cols] = jnp.where(first, dgate, dup)
        send_ref[:, cols] = jnp.where(first, dup, dgate)
        arrived(wb, sem_b, 0, m)
        part = nt(dgate, wb[0, m])
        arrived(wb, sem_b, 1, m)
        part = part + nt(dup, wb[1, m])
        db = part if m == 0 else db + part
    dx, dgain = norm_back(h1_ref[...], gain_ref[...], db)
    dgain_ref[...] = dgain
    g1 = state + dx
    g1_ref[...] = g1
    low = g1.astype(bf16)
    do = None
    for p in range(3):
        part = low[:, p * KVW : (p + 1) * KVW]
        p_ref[p] = part
        arrived(wa, sem_a, 1, p + 1)
        part = nt(wa[1, p + 1], part)
        do = part if p == 0 else do + part
    do_ref[...] = do.astype(bf16)


def finish_a(wa, sem_a, *left):
    for at in left:
        arrived(wa, sem_a, *at)


def query_back(dq_ref, wa, sem_a):
    da = None
    for m in range(3):
        arrived(wa, sem_a, 0, m)
        part = nt(dq_ref[m], wa[0, m])
        da = part if m == 0 else da + part
    return da


def project_back(da, own_ref, near_ref, far_ref, core, cos_ref, sin_ref, dk_ref, dv_ref, h, gain, wa, sem_a):
    cos, sin = cos_ref[...], sin_ref[...]
    grad = own_ref[...] + far_ref[...].astype(f32) + jnp.where(core == 0, near_ref[...].astype(f32), 0.0)
    dk = rope(grad[:KVW], cos, sin, True).T.astype(bf16)
    dv = grad[KVW:].T.astype(bf16)
    dk_ref[...] = dk
    dv_ref[...] = dv
    arrived(wa, sem_a, 0, 3)
    arrived(wa, sem_a, 1, 0)
    da = da + nt(dk, wa[0, 3]) + nt(dv, wa[1, 0])
    return norm_back(h, gain, da)


def back_kernel(start, end, sc, *rest):
    rest = list(rest)

    def take(n):
        out = rest[:n]
        del rest[:n]
        return out

    core, chip = sc[0], sc[1]
    mine_a, other_a = take(4), take(4)
    if not end:
        mine_b, other_b = take(4), take(4)
        mine_d, other_d = take(2)
    if start:
        (g_ref,) = take(1)
    else:
        g1_in, dq_ref, own_ref, near_ref, far_ref, h_ref, gain_a, cos_ref, sin_ref = take(9)
    if not end:
        ins = take(5)
    if not start:
        dk_ref, dv_ref, dgain_a = take(3)
    if end:
        (g_out,) = take(1)
    else:
        outs = take(9)
    wa, sem_a = take(2)
    fetch(mine_a, other_a, wa, sem_a, core, chip)
    if not end:
        wb, sem_b, wd, sem_d = take(4)
        fetch_ffn(mine_b, other_b, mine_d, other_d, wb, wd, sem_b, sem_d, core, chip)
    if start:
        state = g_ref[...].astype(f32)
    else:
        da = query_back(dq_ref, wa, sem_a)
        dx, dgain = project_back(da, own_ref, near_ref, far_ref, core, cos_ref, sin_ref, dk_ref, dv_ref, h_ref[...].astype(f32), gain_a[...], wa, sem_a)
        dgain_a[...] = dgain
        state = g1_in[...] + dx
    if end:
        g_out[...] = state.astype(bf16)
        finish_a(wa, sem_a, (1, 1), (1, 2), (1, 3))
    else:
        ffn_back(state, core, (*ins, *outs), (wa, sem_a, wb, sem_b, wd, sem_d), mine_d)
        if start:
            finish_a(wa, sem_a, (1, 0), (0, 0), (0, 1), (0, 2), (0, 3))


def back(start, end, sc, weights, tail, ffn):
    wa, wb, wd = weights
    width = wa[0][0].shape[0]
    args = [sc, *wa[0], *wa[1]]
    specs = [SCALARS] + [LEFT] * 8
    scratch = scratch_a(width)
    if not end:
        args += [*wb[0], *wb[1], *wd]
        specs += [LEFT] * 10
        scratch += scratch_ffn(width, wb[0][0].shape[1], wd[0].shape[1])
    args += list(tail)
    specs += [WHOLE] * len(tail)
    n = tail[0].shape[0]
    outs = []
    if not end:
        args += list(ffn)
        specs += [WHOLE] * len(ffn)
    if not start:
        outs += [shape((n, KVW), bf16), shape((n, KVW), bf16), shape((1, width), f32)]
    if end:
        outs += [shape((n, width), bf16)]
    else:
        hidden = ffn[0].shape[1]
        outs += [shape((n, width), bf16), shape((n, hidden), bf16), shape((n, hidden), bf16), shape((n, hidden // 2), bf16), shape((n, hidden // 2), bf16)]
        outs += [shape((n, width), f32), shape((3, n, KVW), bf16), shape((1, width), f32), shape((width, n), bf16)]
    return pl.pallas_call(
        functools.partial(back_kernel, start, end),
        out_shape=tuple(outs),
        in_specs=specs,
        out_specs=(WHOLE,) * len(outs),
        scratch_shapes=scratch,
        compiler_params=pltpu.CompilerParams(vmem_limit_bytes=(24 if end else 56) * MIB),
        name="back_end" if end else ("back_start" if start else "back_join"),
    )(*args)


def by_turn(core, chip):
    one = 1 + core
    return chip ^ one, chip ^ 3, chip, chip ^ (3 - one)


def turned(dst, blocks):
    n = blocks[0].shape[0]
    for i, block in enumerate(blocks):
        dst[:, i * n : (i + 1) * n] = block[...].T


def grad_ffn_kernel(sc, *rest):
    lefts, rights = rest[:4], rest[4:8]
    send_ref, keep_ref, left, right = rest[8:]
    core, chip = sc[0], sc[1]
    n, cols = rights[0].shape[0], right.shape[1]
    turned(left, lefts)
    for i, m in enumerate(by_turn(core, chip)):
        at = pl.multiple_of(m * cols, 128)
        for j, block in enumerate(rights):
            right[j * n : (j + 1) * n, :] = block[:, pl.ds(at, cols)]
        out = send_ref if i < 2 else keep_ref
        out[i % 2] = nn(left[...], right[...]).astype(bf16)


def grad_ffn(sc, lefts, rights):
    n, width = lefts[0].shape
    cols = rights[0].shape[1] // 4
    out = shape((2, width, cols), bf16)
    return pl.pallas_call(
        grad_ffn_kernel,
        out_shape=(out, out),
        in_specs=[SCALARS] + [WHOLE] * 8,
        out_specs=(WHOLE,) * 2,
        scratch_shapes=[pltpu.VMEM((width, 4 * n), bf16), pltpu.VMEM((4 * n, cols), bf16)],
        compiler_params=pltpu.CompilerParams(vmem_limit_bytes=48 * MIB),
        name="grad_ffn",
    )(sc, *lefts, *rights)


def grad_down_kernel(*rest):
    lefts, rights = rest[:4], rest[4:8]
    out_ref, left, right = rest[8:]
    n, rows = rights[0].shape[0], out_ref.shape[1]
    turned(left, lefts)
    for j, block in enumerate(rights):
        right[j * n : (j + 1) * n, :] = block[...]
    for i in range(2):
        out_ref[i] = nn(left[i * rows : (i + 1) * rows, :], right[...]).astype(bf16)


def grad_down(lefts, rights):
    n, rows = lefts[0].shape
    width = rights[0].shape[1]
    return pl.pallas_call(
        grad_down_kernel,
        out_shape=shape((2, rows // 2, width), bf16),
        in_specs=[WHOLE] * 8,
        out_specs=WHOLE,
        scratch_shapes=[pltpu.VMEM((rows, 4 * n), bf16), pltpu.VMEM((4 * n, width), bf16)],
        compiler_params=pltpu.CompilerParams(vmem_limit_bytes=40 * MIB),
        name="grad_down",
    )(*lefts, *rights)


def grad_attention_kernel(sc, *rest):
    a_refs, o_refs, rights = rest[:4], rest[4:8], rest[8:12]
    send_ref, keep_ref, left, right = rest[12:]
    core, chip = sc[0], sc[1]
    n = rights[0].shape[1]
    turned(left.at[0], a_refs)

    @pl.when(core == 1)
    def _():
        turned(left.at[1], o_refs)

    for i, m in enumerate(by_turn(core, chip)):
        for j, block in enumerate(rights):
            right[j * n : (j + 1) * n, :] = block[m]
        out = send_ref if i < 2 else keep_ref
        which = jnp.where(m > 0, core, 0)
        out[i % 2] = nn(left[which], right[...]).astype(bf16)


def grad_attention(sc, a, o, rights):
    n, width = a[0].shape
    cols = rights[0].shape[2]
    out = shape((2, width, cols), bf16)
    return pl.pallas_call(
        grad_attention_kernel,
        out_shape=(out, out),
        in_specs=[SCALARS] + [WHOLE] * 12,
        out_specs=(WHOLE,) * 2,
        scratch_shapes=[pltpu.VMEM((2, width, 4 * n), bf16), pltpu.VMEM((4 * n, cols), bf16)],
        compiler_params=pltpu.CompilerParams(vmem_limit_bytes=40 * MIB),
        name="grad_attention",
    )(sc, *a, *o, *rights)


def lay_kernel(sc, *rest):
    mine, other, outs, kept = rest[:4], rest[4:8], rest[8:-1], rest[-1]
    core, chip = sc[0], sc[1]
    for who in range(4):
        kept[core, chip ^ who] = mine[who][...]
        kept[1 - core, chip ^ who] = other[who][...]
    cols = [jnp.concatenate([kept[c, m].astype(f32) for m in range(4)], axis=1) for c in range(2)]
    if len(outs) == 2:
        outs[0][...] = cols[0]
        outs[1][...] = cols[1]
    else:
        n = kept.shape[3]
        outs[0][...] = cols[0][:, : 3 * n]
        outs[1][...] = cols[0][:, 3 * n :]
        outs[2][...] = cols[1][:, :n]
        outs[3][...] = cols[1][:, n:]


def lay(sc, mine, other, pieces):
    rows, n = mine[0].shape
    outs = tuple(shape((rows, p * n), f32) for p in pieces)
    return pl.pallas_call(
        lay_kernel,
        out_shape=outs,
        in_specs=[SCALARS] + [WHOLE] * 8,
        out_specs=(WHOLE,) * len(outs),
        scratch_shapes=[pltpu.VMEM((2, 4, rows, n), bf16)],
        compiler_params=pltpu.CompilerParams(vmem_limit_bytes=32 * MIB),
        name="lay",
    )(sc, *mine, *other)


CORE, SIDE, BACK = 1, 2, 4
rope_base = 10000.0
RUNS = 2


def flip(value, bit, bit1=None):
    count = lax.axis_size("dp")
    bits = (bit, bit if bit1 is None else bit1)
    return lax.ppermute(value, "dp", [(i, i ^ bits[i & 1]) for i in range(count)])


def turn_z(value, step):
    count = lax.axis_size("fsdp")
    return lax.ppermute(value, "fsdp", [(i, (i + step) % count) for i in range(count)])


def home_to_work(value, back=False):
    count, depth = lax.axis_size("dp"), lax.axis_size("fsdp")
    pairs = []
    for d in range(count):
        for z in range(depth):
            there = (d & ~1) | (z & 1), 2 * (d & 1) + (z >> 1)
            pair = (d * depth + z, there[0] * depth + there[1])
            pairs.append(pair[::-1] if back else pair)
    return lax.ppermute(value, ("dp", "fsdp"), pairs)


def place():
    d, z = lax.axis_index("dp"), lax.axis_index("fsdp")
    return d & 1, (d >> 1) & 3, z


def ring_gather(shard):
    z = lax.axis_index("fsdp")
    depth = lax.axis_size("fsdp")
    parts = [shard] + [turn_z(shard, s) for s in range(1, depth)]
    full = jnp.zeros((depth,) + shard.shape, shard.dtype)
    for s, part in enumerate(parts):
        full = lax.dynamic_update_index_in_dim(full, part, (z - s) % depth, 0)
    return full


def plane_gather(piece):
    core, _, _ = place()
    x, y = flip(piece, SIDE), flip(piece, BACK)
    opposite = flip(jnp.where(core == 0, x, y), BACK, SIDE)
    mine = (piece, x, y, opposite)
    return mine, tuple(flip(p, CORE) for p in mine)


def gather_weights(query, key, value, out, gate, up, down):
    core, chip, _ = place()
    rows, width = query.shape
    depth = lax.axis_size("fsdp")
    first = jnp.concatenate([query, key, value, out], axis=1)
    n = first.shape[1] // 8
    piece = lax.dynamic_slice(first, (0, n * (core * 4 + chip)), (rows, n))
    wa = plane_gather(ring_gather(piece).reshape(depth * rows, n))
    n = gate.shape[1] // 4
    piece = lax.dynamic_slice(jnp.where(core == 0, gate, up), (0, n * chip), (rows, n))
    wb = plane_gather(ring_gather(piece).reshape(depth * rows, n))
    n = down.shape[0] // 2
    piece = ring_gather(lax.dynamic_slice(down, (n * core, 0), (n, width)))
    return wa, wb, (piece, flip(piece, CORE))


def window(own):
    core, _, _ = place()
    depth = lax.axis_size("fsdp")
    far = lax.ppermute(own, "fsdp", [(z, z + 1) for z in range(0, depth, 2)])
    near = flip(jnp.where(core == 0, own, far), CORE)
    return far, near, own


def unwindow(far, near):
    core, _, _ = place()
    depth = lax.axis_size("fsdp")
    near = flip(near, CORE)
    far = jnp.where(core == 1, far + near.astype(f32), far).astype(bf16)
    return near, lax.ppermute(far, "fsdp", [(z + 1, z) for z in range(0, depth, 2)])


def over_groups(value):
    bit = 8
    while bit < lax.axis_size("dp"):
        value = value + flip(value.astype(bf16), bit).astype(f32)
        bit *= 2
    return value


def plane_reduce(send, keep):
    got = flip(send, SIDE, BACK)
    later = (keep[1].astype(f32) + got[1].astype(f32)).astype(bf16)
    own = keep[0].astype(f32) + got[0].astype(f32)
    return own + flip(later, BACK, SIDE).astype(f32)


def ring_reduce(parts):
    _, _, z = place()
    depth = lax.axis_size("fsdp")
    low = parts.astype(bf16)
    total = lax.dynamic_index_in_dim(parts, z, 0, keepdims=False)
    for s in range(1, depth):
        part = lax.dynamic_index_in_dim(low, (z + s) % depth, 0, keepdims=False)
        total = total + turn_z(part, s).astype(f32)
    return total


def spread(piece):
    mine = (piece, flip(piece, SIDE), flip(piece, BACK), flip(piece, SIDE | BACK))
    return mine, tuple(flip(p, CORE) for p in mine)


def reduce_pieces(sc, send, keep, pieces):
    depth = lax.axis_size("fsdp")
    own = plane_reduce(send, keep)
    own = own.reshape((depth, own.shape[0] // depth) + own.shape[1:])
    own = over_groups(ring_reduce(own)).astype(bf16)
    return lay(sc, *spread(own), pieces)


def reduce_down(parts):
    core, chip, z = place()
    depth, count = lax.axis_size("fsdp"), lax.axis_size("dp")
    _, rows, width = parts.shape
    owner = (z >> 1) == core
    total = lax.dynamic_index_in_dim(parts, z & 1, 0, keepdims=False).astype(f32)
    for s in range(1, depth):
        part = lax.dynamic_index_in_dim(parts, (z + s) & 1, 0, keepdims=False)
        pairs = []
        for d in range(count):
            for a in range(depth):
                b = (a + s) % depth
                if (b >> 1) == (d & 1):
                    pairs.append((d * depth + a, d * depth + b))
        total = total + lax.ppermute(part, ("dp", "fsdp"), pairs).astype(f32)
    halves = total.astype(bf16).reshape(2, rows // 2, width)
    given = flip(lax.dynamic_index_in_dim(halves, 1 - core, 0, keepdims=False), CORE)
    kept = lax.dynamic_index_in_dim(halves, core, 0, keepdims=False)
    mine = jnp.where(owner, kept, given).reshape(4, rows // 8, width)
    order = by_turn(core, chip)
    picked = [lax.dynamic_index_in_dim(mine, m, 0, keepdims=False) for m in order]
    own = over_groups(plane_reduce(jnp.stack(picked[:2]), picked[2:])).astype(bf16)
    full = jnp.zeros((2, 4, rows // 8, width), bf16)
    for c, parts in ((core, spread(own)[0]),):
        for who, part in enumerate(parts):
            full = lax.dynamic_update_slice(full, part[None, None], (c, chip ^ who, 0, 0))
    mine = lax.dynamic_index_in_dim(full, core, 0, keepdims=True)
    full = lax.dynamic_update_slice(full, flip(mine, CORE), (1 - core, 0, 0, 0))
    return full.reshape(rows, width).astype(f32)


def reduce_gains(total):
    z = lax.axis_index("fsdp")
    depth = lax.axis_size("fsdp")
    bit = 1
    while bit < lax.axis_size("dp"):
        total = total + flip(total, bit)
        bit *= 2
    rows = total.shape[1] // depth
    total = total + sum(turn_z(total, s) for s in range(1, depth))
    mine = lax.dynamic_slice_in_dim(total, z * rows, rows, 1)
    return mine[0], mine[1]


def body(tokens, segment_ids, attn_gain, query_weight, key_weight, value_weight, out_weight, ffn_gain, gate_weight, up_weight, down_weight, cotangent):
    core, chip, z = place()
    sc = jnp.stack([core, chip]).astype(jnp.int32)
    _, stretch, width = tokens.shape
    tokens = home_to_work(tokens[0])
    gains = ring_gather(jnp.stack([attn_gain, ffn_gain]))
    gains = jnp.moveaxis(gains, 0, 1).reshape(2, 1, width).astype(f32)
    gain_a, gain_f = gains[0], gains[1]
    row = ring_gather(segment_ids[0]).reshape(-1)
    row = jnp.where((z >> 1) == core, row, flip(row, CORE))
    block = 2 * (z & 1) + core
    padded = jnp.concatenate([jnp.full((2 * stretch,), -1, row.dtype), row])
    seg_k = lax.dynamic_slice(padded, (block * stretch,), (3 * stretch,))
    seg_q = seg_k[2 * stretch :]
    ahead = jnp.arange(3 * stretch)[:, None] < 2 * stretch + jnp.arange(stretch)[None, :]
    seg_k, seg_q = seg_k[:, None], seg_q[None, :]
    positions = jnp.sum(((seg_k == seg_q) & ahead).astype(f32), axis=0)
    freq = rope_base ** (-2.0 * jnp.arange(HEAD_DIM // 2, dtype=f32) / HEAD_DIM)
    angle = freq[:, None] * positions[None, :]
    cos, sin = jnp.cos(angle), jnp.sin(angle)
    weights = gather_weights(query_weight, key_weight, value_weight, out_weight, gate_weight, up_weight, down_weight)
    wa, wb, wd = weights
    cot = home_to_work(cotangent[0])

    a0, q0, own = pre(sc, tokens, gain_a, cos, sin, *wa)
    kv0 = window(own)
    o0, lse0 = attend(q0, kv0, seg_k, seg_q)
    mixed0, h1_0, b0, gate0, up0, z0, h_1, a1, q1, own = post(False, sc, o0, tokens, gain_f, gain_a, cos, sin, *weights)
    kv1 = window(own)
    o1, lse1 = attend(q1, kv1, seg_k, seg_q)
    mixed1, h1_1, b1, gate1, up1, z1, output = post(True, sc, o1, h_1, gain_f, gain_a, cos, sin, *weights)
    output = home_to_work(output, back=True)

    gb1, act1, away1, zk1, zs1, g1, p1, dgain_f1, do = back(True, False, sc, weights, [cot], [gate1, up1, h1_1, gain_f, z1])
    dq1, far, near, own = attend_back(q1, kv1, seg_k, seg_q, lse1, do, cos, sin)
    near, far = unwindow(far, near)
    tail = [g1, dq1, own, near, far, h_1, gain_a, cos, sin]
    dk1, dv1, dgain_a1, gb0, act0, away0, zk0, zs0, g1, p0, dgain_f0, do = back(False, False, sc, weights, tail, [gate0, up0, h1_0, gain_f, z0])

    def pair(*own):
        return [*own, *(flip(v, CORE) for v in own)]

    lefts, mid = pair(b1, b0), [act1, act0, flip(away1, CORE), flip(away0, CORE)]
    send_b, keep_b = grad_ffn(sc, lefts, mid)
    down_parts = grad_down([zk1, zk0, flip(zs1, CORE), flip(zs0, CORE)], pair(gb1, gb0))
    grad_gate, grad_up = reduce_pieces(sc, send_b, keep_b, (4, 4))
    grad_down_ = reduce_down(down_parts)

    dq0, far, near, own = attend_back(q0, kv0, seg_k, seg_q, lse0, do, cos, sin)
    near, far = unwindow(far, near)
    tail = [g1, dq0, own, near, far, tokens, gain_a, cos, sin]
    dk0, dv0, dgain_a0, grad_tokens = back(False, True, sc, weights, tail, None)
    grad_tokens = home_to_work(grad_tokens, back=True).astype(f32)

    kept, sent = [], []
    for dq, dk, dv, p in ((dq1, dk1, dv1, p1), (dq0, dk0, dv0, p0)):
        first, second = jnp.concatenate([dq, dk[None]]), jnp.concatenate([dv[None], p])
        kept.append(jnp.where(core == 0, first, second))
        sent.append(flip(jnp.where(core == 0, second, first), CORE))
    send_a, keep_a = grad_attention(sc, pair(a1, a0), pair(mixed1, mixed0), kept + sent)
    grad_query, grad_key, grad_value, grad_out = reduce_pieces(sc, send_a, keep_a, (3, 1, 1, 3))
    dgain_a, dgain_f = reduce_gains(jnp.concatenate([dgain_a1 + dgain_a0, dgain_f1 + dgain_f0]))
    return (output[None], grad_tokens[None], dgain_a, grad_query, grad_key, grad_value, grad_out, dgain_f, grad_gate, grad_up, grad_down_)


def solution(mesh):
    wide, rows, shard = P("dp", "fsdp", None), P("dp", "fsdp"), P("fsdp", None)
    in_specs = (wide, rows, P("fsdp"), shard, shard, shard, shard, P("fsdp"), shard, shard, shard, wide)
    out_specs = (wide, wide, P("fsdp"), shard, shard, shard, shard, P("fsdp"), shard, shard, shard)
    return jax.shard_map(body, mesh=mesh, in_specs=in_specs, out_specs=out_specs, check_vma=False)
```

```python
import functools
import jax
import jax.numpy as jnp
from jax import lax
from jax.sharding import PartitionSpec as P
from jax.experimental import pallas as pl
from jax.experimental.pallas import tpu as pltpu

f32, bf16 = jnp.float32, jnp.bfloat16
eps = 1e-05
HEADS, KV_HEADS, HEAD_DIM, GROUP, KVW = 15, 5, 64, 3, 320
PIECE = 384
LIMIT = 58 << 20
WHOLE = pl.BlockSpec(memory_space=pltpu.VMEM)
LEFT = pl.BlockSpec(memory_space=pl.ANY)
SCALARS = pl.BlockSpec(memory_space=pltpu.SMEM)


def contract(a, b, i, j):
    return lax.dot_general(a, b, (((i,), (j,)), ((), ())), preferred_element_type=f32)


def nn(a, b):
    return contract(a, b, 1, 0)


def nt(a, b):
    return contract(a, b, 1, 1)


def tn(a, b):
    return contract(a, b, 0, 0)


def whose(core):
    return 0, 1 + core, 2 - core, 3


def fetch(mine, other, kept, sems, core, chip):
    for kind, pieces in ((core, mine), (1 - core, other)):
        for who, piece in zip(whose(kind), pieces):
            at = chip ^ who
            pltpu.make_async_copy(piece, kept.at[kind, at], sems.at[kind, at]).start()


def arrived(kept, sems, *at):
    pltpu.make_async_copy(kept.at[at], kept.at[at], sems.at[at]).wait()


def normed(x, gain):
    return x * lax.rsqrt(jnp.mean(x * x, axis=-1, keepdims=True) + eps) * gain


def norm_back(x, gain, grad):
    r = lax.rsqrt(jnp.mean(x * x, axis=-1, keepdims=True) + eps)
    hat = x * r
    scaled = grad * gain
    dx = r * (scaled - hat * jnp.mean(scaled * hat, axis=-1, keepdims=True))
    return dx, jnp.sum(grad * hat, axis=0, keepdims=True)


def widened(x):
    return jnp.concatenate([x, jnp.zeros((x.shape[0], PIECE - x.shape[1]), x.dtype)], axis=1)


def rope(u, cos, sin, back):
    heads = u.shape[0] // HEAD_DIM
    half = HEAD_DIM // 2
    out = []
    for h in range(heads):
        u1, u2 = u[h * HEAD_DIM : h * HEAD_DIM + half], u[h * HEAD_DIM + half : (h + 1) * HEAD_DIM]
        if back:
            out += [u1 * cos + u2 * sin, u2 * cos - u1 * sin]
        else:
            out += [u1 * cos - u2 * sin, u2 * cos + u1 * sin]
    return jnp.concatenate(out, axis=0)


def project(state, gain_ref, cos_ref, sin_ref, kept, sems, a_ref, q_ref, kv_ref):
    a = normed(state, gain_ref[...]).astype(bf16)
    a_ref[...] = a
    cos, sin = cos_ref[...], sin_ref[...]
    arrived(kept, sems, 0, 3)
    kv_ref[:KVW, :] = rope(nn(a, kept[0, 3, :, :KVW]).T, cos, sin, False).astype(bf16)
    arrived(kept, sems, 1, 0)
    kv_ref[KVW:, :] = nn(a, kept[1, 0, :, :KVW]).T.astype(bf16)
    for m in range(3):
        arrived(kept, sems, 0, m)
        q_ref[pl.ds(m * KVW, KVW), :] = rope(nn(a, kept[0, m, :, :KVW]).T, cos, sin, False).astype(bf16)


def pre_kernel(sc, ht_ref, gain_ref, cos_ref, sin_ref, *rest):
    mine, other = rest[:4], rest[4:8]
    h_ref, a_ref, q_ref, kv_ref, kept, sems = rest[-6:]
    core, chip = sc[0], sc[1]
    fetch(mine, other, kept, sems, core, chip)
    h = ht_ref[...].T
    h_ref[...] = h
    project(h.astype(f32), gain_ref, cos_ref, sin_ref, kept, sems, a_ref, q_ref, kv_ref)
    for m in range(1, 4):
        arrived(kept, sems, 1, m)


def scratch_a(width):
    return [pltpu.VMEM((2, 4, width, PIECE), bf16), pltpu.SemaphoreType.DMA((2, 4))]


def shape(s, d):
    return jax.ShapeDtypeStruct(s, d)


def pre(sc, ht, gain, cos, sin, mine_a, other_a, after):
    width, n = ht.shape
    return pl.pallas_call(
        pre_kernel,
        out_shape=(shape((n, width), bf16), shape((n, width), bf16), shape((width, n), bf16), shape((2 * KVW, n), bf16)),
        in_specs=[SCALARS] + [WHOLE] * 4 + [LEFT] * (8 + len(after)),
        out_specs=(WHOLE,) * 4,
        scratch_shapes=scratch_a(width),
        compiler_params=pltpu.CompilerParams(vmem_limit_bytes=LIMIT),
        name="pre",
    )(sc, ht, gain, cos, sin, *mine_a, *other_a, *after)


def bias_of(seg_k, seg_q):
    keys, n = seg_k.shape[0], seg_q.shape[1]
    j = lax.broadcasted_iota(jnp.int32, (keys, n), 0)
    i = lax.broadcasted_iota(jnp.int32, (keys, n), 1) + (keys - n)
    return jnp.where((seg_k == seg_q) & (j <= i), 0.0, -1e30).astype(f32)


def window_of(parts, whole):
    n = parts[0].shape[1]
    for w, part in enumerate(parts):
        whole[:, w * n : (w + 1) * n] = part[...]


def attend_kernel(q_ref, kv0, kv1, kv2, sk_ref, sq_ref, o_ref, lse_ref, bias, kv):
    bias[...] = bias_of(sk_ref[...], sq_ref[...])
    window_of((kv0, kv1, kv2), kv)

    def head(e, _):
        row = pl.multiple_of(e * HEAD_DIM, HEAD_DIM)
        k = kv[pl.ds(row, HEAD_DIM), :]
        v = kv[pl.ds(row + KVW, HEAD_DIM), :]
        for g in range(GROUP):
            at = pl.multiple_of((e * GROUP + g) * HEAD_DIM, HEAD_DIM)
            q = q_ref[pl.ds(at, HEAD_DIM), :]
            s = tn(k, q) * HEAD_DIM ** (-0.5) + bias[...]
            top = jnp.max(s, axis=0, keepdims=True)
            expo = jnp.exp(s - top)
            total = jnp.sum(expo, axis=0, keepdims=True)
            probs = (expo * (1.0 / total)).astype(bf16)
            o_ref[pl.ds(at, HEAD_DIM), :] = nn(v, probs).astype(bf16)
            lse_ref[pl.ds(e * GROUP + g, 1), :] = top + jnp.log(total)
        return 0

    lax.fori_loop(0, KV_HEADS, head, 0)


def attend(q, kvs, seg_k, seg_q):
    width, n = q.shape
    return pl.pallas_call(
        attend_kernel,
        out_shape=(shape((width, n), bf16), shape((HEADS, n), f32)),
        in_specs=[WHOLE] * 6,
        out_specs=(WHOLE,) * 2,
        scratch_shapes=[pltpu.VMEM((3 * n, n), f32), pltpu.VMEM((2 * KVW, 3 * n), bf16)],
        compiler_params=pltpu.CompilerParams(vmem_limit_bytes=LIMIT),
        name="attend",
    )(q, *kvs, seg_k, seg_q)


def attend_back_kernel(q_ref, kv0, kv1, kv2, sk_ref, sq_ref, lse_ref, do_ref, cos_ref, sin_ref, *rest):
    dq_ref, far_ref, near_ref, own_ref, bias, kv, dqs = rest[-7:]
    n = q_ref.shape[1]
    bias[...] = bias_of(sk_ref[...], sq_ref[...])
    window_of((kv0, kv1, kv2), kv)
    scale = HEAD_DIM ** (-0.5)

    def head(e, _):
        row = pl.multiple_of(e * HEAD_DIM, HEAD_DIM)
        k = kv[pl.ds(row, HEAD_DIM), :]
        v = kv[pl.ds(row + KVW, HEAD_DIM), :]
        dk = dv = None
        for g in range(GROUP):
            at = pl.multiple_of((e * GROUP + g) * HEAD_DIM, HEAD_DIM)
            q = q_ref[pl.ds(at, HEAD_DIM), :]
            do = do_ref[pl.ds(at, HEAD_DIM), :]
            s = tn(k, q) * scale + bias[...]
            probs = jnp.exp(s - lse_ref[pl.ds(e * GROUP + g, 1), :])
            dp = tn(v, do)
            inner = jnp.sum(probs * dp, axis=0, keepdims=True)
            ds = (probs * (dp - inner)).astype(bf16)
            dvg, dkg = nt(do, probs.astype(bf16)), nt(q, ds)
            dv, dk = (dvg, dkg) if g == 0 else (dv + dvg, dk + dkg)
            dqs[pl.ds(at, HEAD_DIM), :] = nn(k, ds)
        for at, grad in ((row, dk * scale), (row + KVW, dv)):
            far_ref[pl.ds(at, HEAD_DIM), :] = grad[:, :n]
            near_ref[pl.ds(at, HEAD_DIM), :] = grad[:, n : 2 * n].astype(bf16)
            own_ref[pl.ds(at, HEAD_DIM), :] = grad[:, 2 * n :]
        return 0

    lax.fori_loop(0, KV_HEADS, head, 0)
    cos, sin = cos_ref[...] * scale, sin_ref[...] * scale
    for m in range(3):
        dq_ref[m] = widened(rope(dqs[m * KVW : (m + 1) * KVW, :], cos, sin, True).T.astype(bf16))


def attend_back(q, kvs, seg_k, seg_q, lse, do, cos, sin, after=()):
    width, n = q.shape
    block = (2 * KVW, n)
    return pl.pallas_call(
        attend_back_kernel,
        out_shape=(shape((3, n, PIECE), bf16), shape(block, f32), shape(block, bf16), shape(block, f32)),
        in_specs=[WHOLE] * 10 + [LEFT] * len(after),
        out_specs=(WHOLE,) * 4,
        scratch_shapes=[pltpu.VMEM((3 * n, n), f32), pltpu.VMEM((2 * KVW, 3 * n), bf16), pltpu.VMEM((width, n), f32)],
        compiler_params=pltpu.CompilerParams(vmem_limit_bytes=LIMIT),
        name="attend_back",
    )(q, *kvs, seg_k, seg_q, lse, do, cos, sin, *after)


def fetch_ffn(mine_b, other_b, mine_d, other_d, wb, wd, sem_b, sem_d, core, chip):
    fetch(mine_b, other_b, wb, sem_b, core, chip)
    half = mine_d.shape[1]
    for c, part, sem in ((core, mine_d, 0), (1 - core, other_d, 1)):
        rows = pl.ds(pl.multiple_of(c * half, half), half)
        pltpu.make_async_copy(part, wd.at[:, rows], sem_d.at[sem]).start()


def arrived_down(mine_d, wd, sem_d):
    half = mine_d.shape[1]
    for c in range(2):
        pltpu.make_async_copy(mine_d, wd.at[:, c * half : (c + 1) * half], sem_d.at[c]).wait()


def scratch_ffn(width, n):
    return [
        pltpu.VMEM((2, 4, width, n), bf16),
        pltpu.SemaphoreType.DMA((2, 4)),
        pltpu.VMEM((4, width, n), bf16),
        pltpu.SemaphoreType.DMA((2,)),
    ]


def post_kernel(last, sc, ot_ref, h_ref, gain_ref, gain_a, cos_ref, sin_ref, *rest):
    mine_a, other_a, mine_b, other_b = rest[:4], rest[4:8], rest[8:12], rest[12:16]
    mine_d, other_d = rest[16:18]
    o_ref, h1_ref, b_ref, gate_ref, up_ref, z_ref, next_ref = rest[18:25]
    more, rest = rest[25 : 25 + (0 if last else 3)], rest[25 + (0 if last else 3) :]
    wa, sem_a, wb, sem_b, wd, sem_d = rest
    core, chip = sc[0], sc[1]
    fetch(mine_a, other_a, wa, sem_a, core, chip)
    fetch_ffn(mine_b, other_b, mine_d, other_d, wb, wd, sem_b, sem_d, core, chip)
    o = ot_ref[...].T
    o_ref[...] = o
    for m in range(1, 4):
        arrived(wa, sem_a, 1, m)
    h1 = h_ref[...].astype(f32) + jnp.concatenate([nn(o, wa[1, m, :, :KVW]) for m in range(1, 4)], axis=1)
    h1_ref[...] = h1
    b = normed(h1, gain_ref[...]).astype(bf16)
    b_ref[...] = b
    n = wb.shape[3]
    total = h1
    for m in range(4):
        cols = slice(m * n, (m + 1) * n)
        arrived(wb, sem_b, 0, m)
        gate = nn(b, wb[0, m])
        arrived(wb, sem_b, 1, m)
        up = nn(b, wb[1, m])
        gate_ref[:, cols] = gate.astype(bf16)
        up_ref[:, cols] = up.astype(bf16)
        z = (gate / (1.0 + jnp.exp(-gate)) * up).astype(bf16)
        z_ref[:, cols] = z
        if m == 0:
            arrived_down(mine_d, wd, sem_d)
        total = total + nt(z, wd[m])
    next_ref[...] = total.astype(bf16).T if last else total
    if last:
        arrived(wa, sem_a, 1, 0)
        for m in range(4):
            arrived(wa, sem_a, 0, m)
    else:
        project(total, gain_a, cos_ref, sin_ref, wa, sem_a, *more)


def post(last, sc, ot, h, gain, gain_a, cos, sin, wa, wb, wd):
    width, n = ot.shape
    hidden = wb[0][0].shape[1] * 4
    outs = [shape((n, width), bf16), shape((n, width), f32), shape((n, width), bf16)] + [shape((n, hidden), bf16)] * 3
    outs += [shape((width, n), bf16) if last else shape((n, width), f32)]
    if not last:
        outs += [shape((n, width), bf16), shape((width, n), bf16), shape((2 * KVW, n), bf16)]
    return pl.pallas_call(
        functools.partial(post_kernel, last),
        out_shape=tuple(outs),
        in_specs=[SCALARS] + [WHOLE] * 6 + [LEFT] * 18,
        out_specs=(WHOLE,) * len(outs),
        scratch_shapes=scratch_a(width) + scratch_ffn(width, hidden // 4),
        compiler_params=pltpu.CompilerParams(vmem_limit_bytes=LIMIT),
        name="post",
    )(sc, ot, h, gain, gain_a, cos, sin, *wa[0], *wa[1], *wb[0], *wb[1], *wd)


def ffn_back(state, core, refs, weights, mine_d):
    gate_ref, up_ref, h1_ref, gain_ref, z_ref, gb_ref, keep_ref, send_ref, zk_ref, zs_ref, g1_ref, p_ref, dgain_ref, do_ref = refs
    wa, sem_a, wb, sem_b, wd, sem_d = weights
    gb = state.astype(bf16)
    gb_ref[...] = gb
    n = wb.shape[3]
    half = 2 * n
    first = core == 0
    low, high = z_ref[:, :half], z_ref[:, half:]
    zk_ref[...] = jnp.where(first, low, high)
    zs_ref[...] = jnp.where(first, high, low)
    arrived_down(mine_d, wd, sem_d)
    db = None
    for m in range(4):
        cols = slice(m * n, (m + 1) * n)
        dz = nn(gb, wd[m])
        gate, up = gate_ref[:, cols].astype(f32), up_ref[:, cols].astype(f32)
        sig = 1.0 / (1.0 + jnp.exp(-gate))
        dup = (dz * (gate * sig)).astype(bf16)
        dgate = (dz * up * (sig * (1.0 + gate * (1.0 - sig)))).astype(bf16)
        keep_ref[:, cols] = jnp.where(first, dgate, dup)
        send_ref[:, cols] = jnp.where(first, dup, dgate)
        arrived(wb, sem_b, 0, m)
        part = nt(dgate, wb[0, m])
        arrived(wb, sem_b, 1, m)
        part = part + nt(dup, wb[1, m])
        db = part if m == 0 else db + part
    dx, dgain = norm_back(h1_ref[...], gain_ref[...], db)
    dgain_ref[...] = dgain
    g1 = state + dx
    g1_ref[...] = g1
    low = g1.astype(bf16)
    do = None
    for p in range(3):
        part = low[:, p * KVW : (p + 1) * KVW]
        p_ref[p] = widened(part)
        arrived(wa, sem_a, 1, p + 1)
        part = nt(wa[1, p + 1, :, :KVW], part)
        do = part if p == 0 else do + part
    do_ref[...] = do.astype(bf16)


def finish_a(wa, sem_a, *left):
    for at in left:
        arrived(wa, sem_a, *at)


def query_back(dq_ref, wa, sem_a):
    da = None
    for m in range(3):
        arrived(wa, sem_a, 0, m)
        part = nt(dq_ref[m, :, :KVW], wa[0, m, :, :KVW])
        da = part if m == 0 else da + part
    return da


def project_back(da, own_ref, near_ref, far_ref, core, cos_ref, sin_ref, dk_ref, dv_ref, h, gain, wa, sem_a):
    cos, sin = cos_ref[...], sin_ref[...]
    grad = own_ref[...] + far_ref[...].astype(f32) + jnp.where(core == 0, near_ref[...].astype(f32), 0.0)
    dk = rope(grad[:KVW], cos, sin, True).T.astype(bf16)
    dv = grad[KVW:].T.astype(bf16)
    dk_ref[...] = widened(dk)
    dv_ref[...] = widened(dv)
    arrived(wa, sem_a, 0, 3)
    arrived(wa, sem_a, 1, 0)
    da = da + nt(dk, wa[0, 3, :, :KVW]) + nt(dv, wa[1, 0, :, :KVW])
    return norm_back(h, gain, da)


def back_kernel(start, end, sc, *rest):
    rest = list(rest)

    def take(n):
        out = rest[:n]
        del rest[:n]
        return out

    core, chip = sc[0], sc[1]
    mine_a, other_a = take(4), take(4)
    if not end:
        mine_b, other_b = take(4), take(4)
        mine_d, other_d = take(2)
    if start:
        (g_ref,) = take(1)
    else:
        g1_in, dq_ref, own_ref, near_ref, far_ref, h_ref, gain_a, cos_ref, sin_ref = take(9)
    if not end:
        ins = take(5)
    if not start:
        dk_ref, dv_ref, dgain_a = take(3)
    if end:
        (g_out,) = take(1)
    else:
        outs = take(9)
    wa, sem_a = take(2)
    fetch(mine_a, other_a, wa, sem_a, core, chip)
    if not end:
        wb, sem_b, wd, sem_d = take(4)
        fetch_ffn(mine_b, other_b, mine_d, other_d, wb, wd, sem_b, sem_d, core, chip)
    if start:
        state = g_ref[...].T.astype(f32)
    else:
        da = query_back(dq_ref, wa, sem_a)
        dx, dgain = project_back(da, own_ref, near_ref, far_ref, core, cos_ref, sin_ref, dk_ref, dv_ref, h_ref[...].astype(f32), gain_a[...], wa, sem_a)
        dgain_a[...] = dgain
        state = g1_in[...] + dx
    if end:
        g_out[...] = state.astype(bf16).T
        finish_a(wa, sem_a, (1, 1), (1, 2), (1, 3))
    else:
        ffn_back(state, core, (*ins, *outs), (wa, sem_a, wb, sem_b, wd, sem_d), mine_d)
        if start:
            finish_a(wa, sem_a, (1, 0), (0, 0), (0, 1), (0, 2), (0, 3))


def back(start, end, sc, weights, tail, ffn):
    wa, wb, wd = weights
    width = wa[0][0].shape[0]
    args = [sc, *wa[0], *wa[1]]
    specs = [SCALARS] + [LEFT] * 8
    scratch = scratch_a(width)
    if not end:
        args += [*wb[0], *wb[1], *wd]
        specs += [LEFT] * 10
        scratch += scratch_ffn(width, wb[0][0].shape[1])
    args += list(tail)
    specs += [WHOLE] * len(tail)
    n = tail[0].shape[1 if start else 0]
    outs = []
    if not end:
        args += list(ffn)
        specs += [WHOLE] * len(ffn)
    if not start:
        outs += [shape((n, PIECE), bf16), shape((n, PIECE), bf16), shape((1, width), f32)]
    if end:
        outs += [shape((width, n), bf16)]
    else:
        hidden = ffn[0].shape[1]
        outs += [shape((n, width), bf16), shape((n, hidden), bf16), shape((n, hidden), bf16), shape((n, hidden // 2), bf16), shape((n, hidden // 2), bf16)]
        outs += [shape((n, width), f32), shape((3, n, PIECE), bf16), shape((1, width), f32), shape((width, n), bf16)]
    return pl.pallas_call(
        functools.partial(back_kernel, start, end),
        out_shape=tuple(outs),
        in_specs=specs,
        out_specs=(WHOLE,) * len(outs),
        scratch_shapes=scratch,
        compiler_params=pltpu.CompilerParams(vmem_limit_bytes=LIMIT),
        name="back_end" if end else ("back_start" if start else "back_join"),
    )(*args)


def by_turn(core, chip):
    one = 1 + core
    return chip ^ one, chip ^ 3, chip, chip ^ (3 - one)


def turned(dst, blocks):
    n = blocks[0].shape[0]
    for i, block in enumerate(blocks):
        dst[:, i * n : (i + 1) * n] = block[...].T


def grad_ffn_kernel(first, sc, *rest):
    lefts, rights = rest[:4], rest[4:8]
    out_ref, left, right = rest[-3:]
    core, chip = sc[0], sc[1]
    n, cols = rights[0].shape[0], right.shape[1]
    turned(left, lefts)
    for i, m in enumerate(by_turn(core, chip)[first : first + 2]):
        at = pl.multiple_of(m * cols, 128)
        for j, block in enumerate(rights):
            right[j * n : (j + 1) * n, :] = block[:, pl.ds(at, cols)]
        out_ref[i] = nn(left[...], right[...]).astype(bf16)


def grad_ffn(first, sc, lefts, rights, after=()):
    n, width = lefts[0].shape
    cols = rights[0].shape[1] // 4
    return pl.pallas_call(
        functools.partial(grad_ffn_kernel, first),
        out_shape=shape((2, width, cols), bf16),
        in_specs=[SCALARS] + [WHOLE] * 8 + [LEFT] * len(after),
        out_specs=WHOLE,
        scratch_shapes=[pltpu.VMEM((width, 4 * n), bf16), pltpu.VMEM((4 * n, cols), bf16)],
        compiler_params=pltpu.CompilerParams(vmem_limit_bytes=LIMIT),
        name="grad_ffn",
    )(sc, *lefts, *rights, *after)


def grad_down_kernel(*rest):
    lefts, rights = rest[:4], rest[4:8]
    out_ref, left, right = rest[-3:]
    n, cols = rights[0].shape[0], right.shape[1]
    turned(left, lefts)
    for i in range(2):
        for j, block in enumerate(rights):
            right[j * n : (j + 1) * n, :] = block[:, i * cols : (i + 1) * cols]
        out_ref[i] = nn(left[...], right[...]).astype(bf16)


def grad_down(lefts, rights, after=()):
    n, width = lefts[0].shape
    cols = rights[0].shape[1] // 2
    return pl.pallas_call(
        grad_down_kernel,
        out_shape=shape((2, width, cols), bf16),
        in_specs=[WHOLE] * 8 + [LEFT] * len(after),
        out_specs=WHOLE,
        scratch_shapes=[pltpu.VMEM((width, 4 * n), bf16), pltpu.VMEM((4 * n, cols), bf16)],
        compiler_params=pltpu.CompilerParams(vmem_limit_bytes=LIMIT),
        name="grad_down",
    )(*lefts, *rights, *after)


def grad_attention_kernel(sc, *rest):
    a_refs, o_refs, rights = rest[:4], rest[4:8], rest[8:12]
    send_ref, keep_ref, left, right = rest[12:]
    core, chip = sc[0], sc[1]
    n = rights[0].shape[1]
    turned(left.at[0], a_refs)

    @pl.when(core == 1)
    def _():
        turned(left.at[1], o_refs)

    for i, m in enumerate(by_turn(core, chip)):
        for j, block in enumerate(rights):
            right[j * n : (j + 1) * n, :] = block[m]
        out = send_ref if i < 2 else keep_ref
        which = jnp.where(m > 0, core, 0)
        out[i % 2] = nn(left[which], right[...]).astype(bf16)


def grad_attention(sc, a, o, rights):
    n, width = a[0].shape
    cols = rights[0].shape[2]
    out = shape((2, width, cols), bf16)
    return pl.pallas_call(
        grad_attention_kernel,
        out_shape=(out, out),
        in_specs=[SCALARS] + [WHOLE] * 12,
        out_specs=(WHOLE,) * 2,
        scratch_shapes=[pltpu.VMEM((2, width, 4 * n), bf16), pltpu.VMEM((4 * n, cols), bf16)],
        compiler_params=pltpu.CompilerParams(vmem_limit_bytes=LIMIT),
        name="grad_attention",
    )(sc, *a, *o, *rights)


def lay_kernel(sc, *rest):
    mine, other, outs, kept = rest[:4], rest[4:8], rest[8:-1], rest[-1]
    core, chip = sc[0], sc[1]
    for kind, pieces in ((core, mine), (1 - core, other)):
        for who, piece in zip(whose(kind), pieces):
            kept[kind, chip ^ who] = piece[...]
    n = sum(o.shape[1] for o in outs) // 8
    cols = [jnp.concatenate([kept[c, m, :, :n].astype(f32) for m in range(4)], axis=1) for c in range(2)]
    if len(outs) == 2:
        outs[0][...] = cols[0]
        outs[1][...] = cols[1]
    else:
        outs[0][...] = cols[0][:, : 3 * n]
        outs[1][...] = cols[0][:, 3 * n :]
        outs[2][...] = cols[1][:, :n]
        outs[3][...] = cols[1][:, n:]


def lay(sc, mine, other, widths):
    rows, n = mine[0].shape
    outs = tuple(shape((rows, w), f32) for w in widths)
    return pl.pallas_call(
        lay_kernel,
        out_shape=outs,
        in_specs=[SCALARS] + [WHOLE] * 8,
        out_specs=(WHOLE,) * len(outs),
        scratch_shapes=[pltpu.VMEM((2, 4, rows, n), bf16)],
        compiler_params=pltpu.CompilerParams(vmem_limit_bytes=LIMIT),
        name="lay",
    )(sc, *mine, *other)


def pick_kernel(sc, gate, up, down, *rest):
    b_ref, d_ref, sems = rest[-3:]
    core, chip = sc[0], sc[1]
    cols, half = b_ref.shape[1], d_ref.shape[0]
    at = pl.ds(pl.multiple_of(chip * cols, 128), cols)
    rows = pl.ds(pl.multiple_of(core * half, half), half)
    copy = pltpu.make_async_copy(down.at[rows, :], d_ref, sems.at[1])
    copy.start()
    for c, source in ((0, gate), (1, up)):

        @pl.when(core == c)
        def _():
            pltpu.make_async_copy(source.at[:, at], b_ref, sems.at[0]).start()

    pltpu.make_async_copy(gate.at[:, at], b_ref, sems.at[0]).wait()
    copy.wait()


def pick(sc, gate, up, down, after):
    return pl.pallas_call(
        pick_kernel,
        out_shape=(shape((gate.shape[0], gate.shape[1] // 4), bf16), shape((down.shape[0] // 2, down.shape[1]), bf16)),
        in_specs=[SCALARS] + [LEFT] * (3 + len(after)),
        out_specs=(LEFT, LEFT),
        scratch_shapes=[pltpu.SemaphoreType.DMA((2,))],
        compiler_params=pltpu.CompilerParams(vmem_limit_bytes=LIMIT),
        name="pick",
    )(sc, gate, up, down, *after)


def stack_kernel(sc, *rest):
    parts, out_ref, sems = rest[:4], rest[-2], rest[-1]
    copies = [pltpu.make_async_copy(p, out_ref.at[(sc[2] - s) & 3], sems.at[s]) for s, p in enumerate(parts)]
    for copy in copies:
        copy.start()
    for copy in copies:
        copy.wait()


def stack(sc, parts, after=()):
    return pl.pallas_call(
        stack_kernel,
        out_shape=shape((4,) + parts[0].shape, parts[0].dtype),
        in_specs=[SCALARS] + [LEFT] * (4 + len(after)),
        out_specs=LEFT,
        scratch_shapes=[pltpu.SemaphoreType.DMA((4,))],
        compiler_params=pltpu.CompilerParams(vmem_limit_bytes=LIMIT),
        name="stack",
    )(sc, *parts, *after)


CORE, SIDE, BACK = 1, 2, 4
rope_base = 10000.0
RUNS = 2


def flip(value, bit, bit1=None):
    count = lax.axis_size("dp")
    bits = (bit, bit if bit1 is None else bit1)
    return lax.ppermute(value, "dp", [(i, i ^ bits[i & 1]) for i in range(count)])


def turn_z(value, step):
    count = lax.axis_size("fsdp")
    return lax.ppermute(value, "fsdp", [(i, (i + step) % count) for i in range(count)])


def home_to_work(value, back=False):
    count, depth = lax.axis_size("dp"), lax.axis_size("fsdp")
    pairs = []
    for d in range(count):
        for z in range(depth):
            there = (d & ~1) | (z & 1), 2 * (d & 1) + (z >> 1)
            pair = (d * depth + z, there[0] * depth + there[1])
            pairs.append(pair[::-1] if back else pair)
    return lax.ppermute(value, ("dp", "fsdp"), pairs)


def place():
    d, z = lax.axis_index("dp"), lax.axis_index("fsdp")
    return d & 1, (d >> 1) & 3, z


def turns(shard):
    return [shard] + [turn_z(shard, s) for s in range(1, lax.axis_size("fsdp"))]


def plane_gather(piece):
    first, second = flip(piece, SIDE, BACK), flip(piece, BACK, SIDE)
    mine = (piece, first, second, flip(first, BACK, SIDE))
    return mine, tuple(flip(p, CORE) for p in mine)


def small_gather(shard):
    z = lax.axis_index("fsdp")
    full = jnp.zeros((lax.axis_size("fsdp"),) + shard.shape, shard.dtype)
    for s, part in enumerate(turns(shard)):
        full = lax.dynamic_update_index_in_dim(full, part, (z - s) % full.shape[0], 0)
    return full


def window(own):
    core, _, _ = place()
    depth = lax.axis_size("fsdp")
    far = lax.ppermute(own, "fsdp", [(z, z + 1) for z in range(0, depth, 2)])
    near = flip(jnp.where(core == 0, own, far), CORE)
    return far, near, own


def unwindow(far, near):
    core, _, _ = place()
    depth = lax.axis_size("fsdp")
    near = flip(near, CORE)
    far = jnp.where(core == 1, far + near.astype(f32), far).astype(bf16)
    return near, lax.ppermute(far, "fsdp", [(z + 1, z) for z in range(0, depth, 2)])


def over_groups(value):
    bit = 8
    while bit < lax.axis_size("dp"):
        value = value + flip(value.astype(bf16), bit).astype(f32)
        bit *= 2
    return value


def plane_reduce(send, keep):
    got = flip(send, SIDE, BACK)
    later = (keep[1].astype(f32) + got[1].astype(f32)).astype(bf16)
    own = keep[0].astype(f32) + got[0].astype(f32)
    return own + flip(later, BACK, SIDE).astype(f32)


def ring_reduce(parts):
    _, _, z = place()
    depth = lax.axis_size("fsdp")
    low = parts.astype(bf16)
    total = lax.dynamic_index_in_dim(parts, z, 0, keepdims=False)
    for s in range(1, depth):
        part = lax.dynamic_index_in_dim(low, (z + s) % depth, 0, keepdims=False)
        total = total + turn_z(part, s).astype(f32)
    return total


def spread(piece, both=True):
    mine = (piece, flip(piece, SIDE, BACK), flip(piece, BACK, SIDE), flip(piece, SIDE | BACK))
    return (mine, tuple(flip(p, CORE) for p in mine)) if both else mine


def reduce_pieces(sc, send, keep, widths):
    depth = lax.axis_size("fsdp")
    own = plane_reduce(send, keep)
    own = own.reshape((depth, own.shape[0] // depth) + own.shape[1:])
    own = over_groups(ring_reduce(own)).astype(bf16)
    return lay(sc, *spread(own), widths)


def reduce_down(parts):
    core, chip, z = place()
    depth, count = lax.axis_size("fsdp"), lax.axis_size("dp")
    _, rows, cols = parts.shape
    owner = (z >> 1) == core
    total = lax.dynamic_index_in_dim(parts, z & 1, 0, keepdims=False).astype(f32)
    for s in range(1, depth):
        part = lax.dynamic_index_in_dim(parts, (z + s) & 1, 0, keepdims=False)
        pairs = []
        for d in range(count):
            for a in range(depth):
                b = (a + s) % depth
                if (b >> 1) == (d & 1):
                    pairs.append((d * depth + a, d * depth + b))
        total = total + lax.ppermute(part, ("dp", "fsdp"), pairs).astype(f32)
    half, n = rows // 2, rows // 8
    halves = total.astype(bf16).reshape(2, half, cols)
    given = flip(lax.dynamic_index_in_dim(halves, 1 - core, 0, keepdims=False), CORE)
    kept = lax.dynamic_index_in_dim(halves, core, 0, keepdims=False)
    mine = jnp.where(owner, kept, given).reshape(4, n, cols)
    picked = [lax.dynamic_index_in_dim(mine, m, 0, keepdims=False) for m in by_turn(core, chip)]
    own = over_groups(plane_reduce(jnp.stack(picked[:2]), picked[2:])).astype(bf16)
    mine = jnp.zeros((4, n, cols), bf16)
    for who, part in zip(whose(core), spread(own, False)):
        mine = lax.dynamic_update_index_in_dim(mine, part, chip ^ who, 0)
    other = flip(mine, CORE)
    full = jnp.where(core == 0, jnp.concatenate([mine, other]), jnp.concatenate([other, mine]))
    return full.reshape(rows, cols).astype(f32).T


def reduce_gains(total):
    z = lax.axis_index("fsdp")
    depth = lax.axis_size("fsdp")
    bit = 1
    while bit < lax.axis_size("dp"):
        total = total + flip(total, bit)
        bit *= 2
    rows = total.shape[1] // depth
    total = total + sum(turn_z(total, s) for s in range(1, depth))
    mine = lax.dynamic_slice_in_dim(total, z * rows, rows, 1)
    return mine[0], mine[1]


def body(tokens, segment_ids, attn_gain, query_weight, key_weight, value_weight, out_weight, ffn_gain, gate_weight, up_weight, down_weight, cotangent):
    core, chip, z = place()
    sc = jnp.stack([core, chip, z]).astype(jnp.int32)
    _, stretch, width = tokens.shape
    rows, depth = query_weight.shape[0], lax.axis_size("fsdp")

    first = jnp.concatenate([query_weight, key_weight, value_weight, out_weight], axis=1)
    first = jnp.pad(first, ((0, 0), (0, PIECE - KVW)))
    parts_a = turns(lax.dynamic_slice(first, (0, KVW * (core * 4 + chip)), (rows, PIECE)))
    wa = plane_gather(stack(sc, parts_a).reshape(depth * rows, PIECE))
    piece_b, piece_d = pick(sc, gate_weight, up_weight, down_weight.T, parts_a[1:])
    whole_b = stack(sc, turns(piece_b)).reshape(depth * rows, piece_b.shape[1])
    wb = plane_gather(whole_b)
    whole_d = stack(sc, turns(piece_d))
    wd = whole_d, flip(whole_d, CORE)
    weights = wa, wb, wd

    tokens = home_to_work(tokens[0].T)
    gains = small_gather(jnp.stack([attn_gain, ffn_gain]))
    gains = jnp.moveaxis(gains, 0, 1).reshape(2, 1, width).astype(f32)
    gain_a, gain_f = gains[0], gains[1]
    row = small_gather(segment_ids[0]).reshape(-1)
    row = jnp.where((z >> 1) == core, row, flip(row, CORE))
    block = 2 * (z & 1) + core
    padded = jnp.concatenate([jnp.full((2 * stretch,), -1, row.dtype), row])
    seg_k = lax.dynamic_slice(padded, (block * stretch,), (3 * stretch,))
    seg_q = seg_k[2 * stretch :]
    ahead = jnp.arange(3 * stretch)[:, None] < 2 * stretch + jnp.arange(stretch)[None, :]
    seg_k, seg_q = seg_k[:, None], seg_q[None, :]
    positions = jnp.sum(((seg_k == seg_q) & ahead).astype(f32), axis=0)
    freq = rope_base ** (-2.0 * jnp.arange(HEAD_DIM // 2, dtype=f32) / HEAD_DIM)
    angle = freq[:, None] * positions[None, :]
    cos, sin = jnp.cos(angle), jnp.sin(angle)
    cot = home_to_work(cotangent[0].T)

    h_0, a0, q0, own = pre(sc, tokens, gain_a, cos, sin, *wa, [whole_b])
    kv0 = window(own)
    o0, lse0 = attend(q0, kv0, seg_k, seg_q)
    mixed0, h1_0, b0, gate0, up0, z0, h_1, a1, q1, own = post(False, sc, o0, h_0, gain_f, gain_a, cos, sin, *weights)
    kv1 = window(own)
    o1, lse1 = attend(q1, kv1, seg_k, seg_q)
    mixed1, h1_1, b1, gate1, up1, z1, output = post(True, sc, o1, h_1, gain_f, gain_a, cos, sin, *weights)
    output = home_to_work(output, back=True).T

    gb1, act1, away1, zk1, zs1, g1, p1, dgain_f1, do = back(True, False, sc, weights, [cot], [gate1, up1, h1_1, gain_f, z1])
    dq1, far, near, own = attend_back(q1, kv1, seg_k, seg_q, lse1, do, cos, sin)
    near, far = unwindow(far, near)
    tail = [g1, dq1, own, near, far, h_1, gain_a, cos, sin]
    dk1, dv1, dgain_a1, gb0, act0, away0, zk0, zs0, g1, p0, dgain_f0, do = back(False, False, sc, weights, tail, [gate0, up0, h1_0, gain_f, z0])

    def pair(*own):
        return [*own, *(flip(v, CORE) for v in own)]

    lefts, mid = pair(b1, b0), [act1, act0, flip(away1, CORE), flip(away0, CORE)]
    send_b = grad_ffn(0, sc, lefts, mid)
    parts_d = grad_down(pair(gb1, gb0), [zk1, zk0, flip(zs1, CORE), flip(zs0, CORE)], [send_b])
    keep_b = grad_ffn(2, sc, lefts, mid, [parts_d])
    grad_gate, grad_up = reduce_pieces(sc, send_b, keep_b, (gate_weight.shape[1],) * 2)
    grad_down_ = reduce_down(parts_d)

    dq0, far, near, own = attend_back(q0, kv0, seg_k, seg_q, lse0, do, cos, sin, [keep_b])
    near, far = unwindow(far, near)
    tail = [g1, dq0, own, near, far, h_0, gain_a, cos, sin]
    dk0, dv0, dgain_a0, grad_tokens = back(False, True, sc, weights, tail, None)
    grad_tokens = home_to_work(grad_tokens, back=True).astype(f32).T

    kept, sent = [], []
    for dq, dk, dv, p in ((dq1, dk1, dv1, p1), (dq0, dk0, dv0, p0)):
        first, second = jnp.concatenate([dq, dk[None]]), jnp.concatenate([dv[None], p])
        kept.append(jnp.where(core == 0, first, second))
        sent.append(flip(jnp.where(core == 0, second, first), CORE))
    send_a, keep_a = grad_attention(sc, pair(a1, a0), pair(mixed1, mixed0), kept + sent)
    grad_query, grad_key, grad_value, grad_out = reduce_pieces(sc, send_a, keep_a, (width, KVW, KVW, width))
    dgain_a, dgain_f = reduce_gains(jnp.concatenate([dgain_a1 + dgain_a0, dgain_f1 + dgain_f0]))
    return (output[None], grad_tokens[None], dgain_a, grad_query, grad_key, grad_value, grad_out, dgain_f, grad_gate, grad_up, grad_down_)


def solution(mesh):
    wide, rows, shard = P("dp", "fsdp", None), P("dp", "fsdp"), P("fsdp", None)
    in_specs = (wide, rows, P("fsdp"), shard, shard, shard, shard, P("fsdp"), shard, shard, shard, wide)
    out_specs = (wide, wide, P("fsdp"), shard, shard, shard, shard, P("fsdp"), shard, shard, shard)
    return jax.shard_map(body, mesh=mesh, in_specs=in_specs, out_specs=out_specs, check_vma=False)
```

```python
import functools
import jax
import jax.numpy as jnp
from jax import lax
from jax.sharding import PartitionSpec as P
from jax.experimental import pallas as pl
from jax.experimental.pallas import tpu as pltpu

f32, bf16 = jnp.float32, jnp.bfloat16
eps = 1e-05
HEADS, KV_HEADS, HEAD_DIM, GROUP, KVW = 15, 5, 64, 3, 320
PIECE = 384
LIMIT = 58 << 20
WHOLE = pl.BlockSpec(memory_space=pltpu.VMEM)
LEFT = pl.BlockSpec(memory_space=pl.ANY)
SCALARS = pl.BlockSpec(memory_space=pltpu.SMEM)


def contract(a, b, i, j):
    return lax.dot_general(a, b, (((i,), (j,)), ((), ())), preferred_element_type=f32)


def nn(a, b):
    return contract(a, b, 1, 0)


def nt(a, b):
    return contract(a, b, 1, 1)


def tn(a, b):
    return contract(a, b, 0, 0)


def whose(core):
    return 0, 1 + core, 2 - core, 3


def fetch(mine, other, kept, sems, core, chip):
    for kind, pieces in ((core, mine), (1 - core, other)):
        for who, piece in zip(whose(kind), pieces):
            at = chip ^ who
            pltpu.make_async_copy(piece, kept.at[kind, at], sems.at[kind, at]).start()


def arrived(kept, sems, *at):
    pltpu.make_async_copy(kept.at[at], kept.at[at], sems.at[at]).wait()


def normed(x, gain):
    return x * lax.rsqrt(jnp.mean(x * x, axis=-1, keepdims=True) + eps) * gain


def norm_back(x, gain, grad):
    r = lax.rsqrt(jnp.mean(x * x, axis=-1, keepdims=True) + eps)
    hat = x * r
    scaled = grad * gain
    dx = r * (scaled - hat * jnp.mean(scaled * hat, axis=-1, keepdims=True))
    return dx, jnp.sum(grad * hat, axis=0, keepdims=True)


def widened(x):
    return jnp.concatenate([x, jnp.zeros((x.shape[0], PIECE - x.shape[1]), x.dtype)], axis=1)


def rope(u, cos, sin, back):
    heads = u.shape[0] // HEAD_DIM
    half = HEAD_DIM // 2
    out = []
    for h in range(heads):
        u1, u2 = u[h * HEAD_DIM : h * HEAD_DIM + half], u[h * HEAD_DIM + half : (h + 1) * HEAD_DIM]
        if back:
            out += [u1 * cos + u2 * sin, u2 * cos - u1 * sin]
        else:
            out += [u1 * cos - u2 * sin, u2 * cos + u1 * sin]
    return jnp.concatenate(out, axis=0)


def project(state, gain_ref, cos_ref, sin_ref, kept, sems, a_ref, q_ref, kv_ref):
    a = normed(state, gain_ref[...]).astype(bf16)
    a_ref[...] = a
    cos, sin = cos_ref[...], sin_ref[...]
    arrived(kept, sems, 0, 3)
    kv_ref[:KVW, :] = rope(nn(a, kept[0, 3, :, :KVW]).T, cos, sin, False).astype(bf16)
    arrived(kept, sems, 1, 0)
    kv_ref[KVW:, :] = nn(a, kept[1, 0, :, :KVW]).T.astype(bf16)
    for m in range(3):
        arrived(kept, sems, 0, m)
        q_ref[pl.ds(m * KVW, KVW), :] = rope(nn(a, kept[0, m, :, :KVW]).T, cos, sin, False).astype(bf16)


def pre_kernel(sc, ht_ref, gain_ref, cos_ref, sin_ref, *rest):
    mine, other = rest[:4], rest[4:8]
    h_ref, a_ref, q_ref, kv_ref, kept, sems = rest[-6:]
    core, chip = sc[0], sc[1]
    fetch(mine, other, kept, sems, core, chip)
    h = ht_ref[...].T
    h_ref[...] = h
    project(h.astype(f32), gain_ref, cos_ref, sin_ref, kept, sems, a_ref, q_ref, kv_ref)
    for m in range(1, 4):
        arrived(kept, sems, 1, m)


def scratch_a(width):
    return [pltpu.VMEM((2, 4, width, PIECE), bf16), pltpu.SemaphoreType.DMA((2, 4))]


def shape(s, d):
    return jax.ShapeDtypeStruct(s, d)


def pre(sc, ht, gain, cos, sin, mine_a, other_a, after):
    width, n = ht.shape
    return pl.pallas_call(
        pre_kernel,
        out_shape=(shape((n, width), bf16), shape((n, width), bf16), shape((width, n), bf16), shape((2 * KVW, n), bf16)),
        in_specs=[SCALARS] + [WHOLE] * 4 + [LEFT] * (8 + len(after)),
        out_specs=(WHOLE,) * 4,
        scratch_shapes=scratch_a(width),
        compiler_params=pltpu.CompilerParams(vmem_limit_bytes=LIMIT),
        name="pre",
    )(sc, ht, gain, cos, sin, *mine_a, *other_a, *after)


def bias_of(seg_k, seg_q):
    keys, n = seg_k.shape[0], seg_q.shape[1]
    j = lax.broadcasted_iota(jnp.int32, (keys, n), 0)
    i = lax.broadcasted_iota(jnp.int32, (keys, n), 1) + (keys - n)
    return jnp.where((seg_k == seg_q) & (j <= i), 0.0, -1e30).astype(f32)


def window_of(parts, whole):
    n = parts[0].shape[1]
    for w, part in enumerate(parts):
        whole[:, w * n : (w + 1) * n] = part[...]


def attend_kernel(q_ref, kv0, kv1, kv2, sk_ref, sq_ref, o_ref, lse_ref, bias, kv):
    bias[...] = bias_of(sk_ref[...], sq_ref[...])
    window_of((kv0, kv1, kv2), kv)

    def head(e, _):
        row = pl.multiple_of(e * HEAD_DIM, HEAD_DIM)
        k = kv[pl.ds(row, HEAD_DIM), :]
        v = kv[pl.ds(row + KVW, HEAD_DIM), :]
        for g in range(GROUP):
            at = pl.multiple_of((e * GROUP + g) * HEAD_DIM, HEAD_DIM)
            q = q_ref[pl.ds(at, HEAD_DIM), :]
            s = tn(k, q) * HEAD_DIM ** (-0.5) + bias[...]
            top = jnp.max(s, axis=0, keepdims=True)
            expo = jnp.exp(s - top)
            total = jnp.sum(expo, axis=0, keepdims=True)
            probs = (expo * (1.0 / total)).astype(bf16)
            o_ref[pl.ds(at, HEAD_DIM), :] = nn(v, probs).astype(bf16)
            lse_ref[pl.ds(e * GROUP + g, 1), :] = top + jnp.log(total)
        return 0

    lax.fori_loop(0, KV_HEADS, head, 0)


def attend(q, kvs, seg_k, seg_q):
    width, n = q.shape
    return pl.pallas_call(
        attend_kernel,
        out_shape=(shape((width, n), bf16), shape((HEADS, n), f32)),
        in_specs=[WHOLE] * 6,
        out_specs=(WHOLE,) * 2,
        scratch_shapes=[pltpu.VMEM((3 * n, n), f32), pltpu.VMEM((2 * KVW, 3 * n), bf16)],
        compiler_params=pltpu.CompilerParams(vmem_limit_bytes=24 << 20),
        name="attend",
    )(q, *kvs, seg_k, seg_q)


def attend_back_kernel(sc, p_ref, q_ref, kv0, kv1, kv2, sk_ref, sq_ref, lse_ref, do_ref, cos_ref, sin_ref, *rest):
    dq_ref, three_ref, far_ref, near_ref, own_ref, bias, kv, dqs = rest[-8:]
    n = q_ref.shape[1]
    bias[...] = bias_of(sk_ref[...], sq_ref[...])
    window_of((kv0, kv1, kv2), kv)
    scale = HEAD_DIM ** (-0.5)

    def head(e, _):
        row = pl.multiple_of(e * HEAD_DIM, HEAD_DIM)
        k = kv[pl.ds(row, HEAD_DIM), :]
        v = kv[pl.ds(row + KVW, HEAD_DIM), :]
        dk = dv = None
        for g in range(GROUP):
            at = pl.multiple_of((e * GROUP + g) * HEAD_DIM, HEAD_DIM)
            q = q_ref[pl.ds(at, HEAD_DIM), :]
            do = do_ref[pl.ds(at, HEAD_DIM), :]
            s = tn(k, q) * scale + bias[...]
            probs = jnp.exp(s - lse_ref[pl.ds(e * GROUP + g, 1), :])
            dp = tn(v, do)
            inner = jnp.sum(probs * dp, axis=0, keepdims=True)
            ds = (probs * (dp - inner)).astype(bf16)
            dvg, dkg = nt(do, probs.astype(bf16)), nt(q, ds)
            dv, dk = (dvg, dkg) if g == 0 else (dv + dvg, dk + dkg)
            dqs[pl.ds(at, HEAD_DIM), :] = nn(k, ds)
        for at, grad in ((row, dk * scale), (row + KVW, dv)):
            far_ref[pl.ds(at, HEAD_DIM), :] = grad[:, :n]
            near_ref[pl.ds(at, HEAD_DIM), :] = grad[:, n : 2 * n].astype(bf16)
            own_ref[pl.ds(at, HEAD_DIM), :] = grad[:, 2 * n :]
        return 0

    lax.fori_loop(0, KV_HEADS, head, 0)
    cos, sin = cos_ref[...] * scale, sin_ref[...] * scale
    for m in range(3):
        dq = widened(rope(dqs[m * KVW : (m + 1) * KVW, :], cos, sin, True).T.astype(bf16))
        dq_ref[m] = dq
        three_ref[m] = jnp.where(sc[0] == 0, p_ref[m], dq)


def attend_back(sc, p, q, kvs, seg_k, seg_q, lse, do, cos, sin, after=()):
    width, n = q.shape
    block = (2 * KVW, n)
    return pl.pallas_call(
        attend_back_kernel,
        out_shape=(shape((3, n, PIECE), bf16), shape((3, n, PIECE), bf16), shape(block, f32), shape(block, bf16), shape(block, f32)),
        in_specs=[SCALARS] + [WHOLE] * 11 + [LEFT] * len(after),
        out_specs=(WHOLE,) * 5,
        scratch_shapes=[pltpu.VMEM((3 * n, n), f32), pltpu.VMEM((2 * KVW, 3 * n), bf16), pltpu.VMEM((width, n), f32)],
        compiler_params=pltpu.CompilerParams(vmem_limit_bytes=32 << 20),
        name="attend_back",
    )(sc, p, q, *kvs, seg_k, seg_q, lse, do, cos, sin, *after)


def fetch_ffn(mine_b, other_b, mine_d, other_d, wb, wd, sem_b, sem_d, core, chip):
    fetch(mine_b, other_b, wb, sem_b, core, chip)
    half = mine_d.shape[1]
    for c, part, sem in ((core, mine_d, 0), (1 - core, other_d, 1)):
        rows = pl.ds(pl.multiple_of(c * half, half), half)
        pltpu.make_async_copy(part, wd.at[:, rows], sem_d.at[sem]).start()


def arrived_down(mine_d, wd, sem_d):
    half = mine_d.shape[1]
    for c in range(2):
        pltpu.make_async_copy(mine_d, wd.at[:, c * half : (c + 1) * half], sem_d.at[c]).wait()


def scratch_ffn(width, n):
    return [
        pltpu.VMEM((2, 4, width, n), bf16),
        pltpu.SemaphoreType.DMA((2, 4)),
        pltpu.VMEM((4, width, n), bf16),
        pltpu.SemaphoreType.DMA((2,)),
    ]


def post_kernel(last, sc, ot_ref, h_ref, gain_ref, gain_a, cos_ref, sin_ref, *rest):
    mine_a, other_a, mine_b, other_b = rest[:4], rest[4:8], rest[8:12], rest[12:16]
    mine_d, other_d = rest[16:18]
    o_ref, h1_ref, b_ref, gate_ref, up_ref, z_ref, next_ref = rest[18:25]
    more, rest = rest[25 : 25 + (0 if last else 3)], rest[25 + (0 if last else 3) :]
    wa, sem_a, wb, sem_b, wd, sem_d = rest
    core, chip = sc[0], sc[1]
    fetch(mine_a, other_a, wa, sem_a, core, chip)
    fetch_ffn(mine_b, other_b, mine_d, other_d, wb, wd, sem_b, sem_d, core, chip)
    o = ot_ref[...].T
    o_ref[...] = o
    for m in range(1, 4):
        arrived(wa, sem_a, 1, m)
    h1 = h_ref[...].astype(f32) + jnp.concatenate([nn(o, wa[1, m, :, :KVW]) for m in range(1, 4)], axis=1)
    h1_ref[...] = h1
    b = normed(h1, gain_ref[...]).astype(bf16)
    b_ref[...] = b
    n = wb.shape[3]
    total = h1
    for m in range(4):
        cols = slice(m * n, (m + 1) * n)
        arrived(wb, sem_b, 0, m)
        gate = nn(b, wb[0, m])
        arrived(wb, sem_b, 1, m)
        up = nn(b, wb[1, m])
        gate_ref[:, cols] = gate.astype(bf16)
        up_ref[:, cols] = up.astype(bf16)
        z = (gate / (1.0 + jnp.exp(-gate)) * up).astype(bf16)
        z_ref[:, cols] = z
        if m == 0:
            arrived_down(mine_d, wd, sem_d)
        total = total + nt(z, wd[m])
    next_ref[...] = total.astype(bf16).T if last else total
    if last:
        arrived(wa, sem_a, 1, 0)
        for m in range(4):
            arrived(wa, sem_a, 0, m)
    else:
        project(total, gain_a, cos_ref, sin_ref, wa, sem_a, *more)


def post(last, sc, ot, h, gain, gain_a, cos, sin, wa, wb, wd):
    width, n = ot.shape
    hidden = wb[0][0].shape[1] * 4
    outs = [shape((n, width), bf16), shape((n, width), f32), shape((n, width), bf16)] + [shape((n, hidden), bf16)] * 3
    outs += [shape((width, n), bf16) if last else shape((n, width), f32)]
    if not last:
        outs += [shape((n, width), bf16), shape((width, n), bf16), shape((2 * KVW, n), bf16)]
    return pl.pallas_call(
        functools.partial(post_kernel, last),
        out_shape=tuple(outs),
        in_specs=[SCALARS] + [WHOLE] * 6 + [LEFT] * 18,
        out_specs=(WHOLE,) * len(outs),
        scratch_shapes=scratch_a(width) + scratch_ffn(width, hidden // 4),
        compiler_params=pltpu.CompilerParams(vmem_limit_bytes=LIMIT),
        name="post",
    )(sc, ot, h, gain, gain_a, cos, sin, *wa[0], *wa[1], *wb[0], *wb[1], *wd)


def ffn_back(state, core, refs, weights, mine_d):
    gate_ref, up_ref, h1_ref, gain_ref, z_ref, gb_ref, keep_ref, send_ref, zk_ref, zs_ref, g1_ref, p_ref, dgain_ref, do_ref = refs
    wa, sem_a, wb, sem_b, wd, sem_d = weights
    gb = state.astype(bf16)
    gb_ref[...] = gb
    n = wb.shape[3]
    half = 2 * n
    first = core == 0
    low, high = z_ref[:, :half], z_ref[:, half:]
    zk_ref[...] = jnp.where(first, low, high)
    zs_ref[...] = jnp.where(first, high, low)
    arrived_down(mine_d, wd, sem_d)
    db = None
    for m in range(4):
        cols = slice(m * n, (m + 1) * n)
        dz = nn(gb, wd[m])
        gate, up = gate_ref[:, cols].astype(f32), up_ref[:, cols].astype(f32)
        sig = 1.0 / (1.0 + jnp.exp(-gate))
        dup = (dz * (gate * sig)).astype(bf16)
        dgate = (dz * up * (sig * (1.0 + gate * (1.0 - sig)))).astype(bf16)
        keep_ref[:, cols] = jnp.where(first, dgate, dup)
        send_ref[:, cols] = jnp.where(first, dup, dgate)
        arrived(wb, sem_b, 0, m)
        part = nt(dgate, wb[0, m])
        arrived(wb, sem_b, 1, m)
        part = part + nt(dup, wb[1, m])
        db = part if m == 0 else db + part
    dx, dgain = norm_back(h1_ref[...], gain_ref[...], db)
    dgain_ref[...] = dgain
    g1 = state + dx
    g1_ref[...] = g1
    low = g1.astype(bf16)
    do = None
    for p in range(3):
        part = low[:, p * KVW : (p + 1) * KVW]
        p_ref[p] = widened(part)
        arrived(wa, sem_a, 1, p + 1)
        part = nt(wa[1, p + 1, :, :KVW], part)
        do = part if p == 0 else do + part
    do_ref[...] = do.astype(bf16)


def finish_a(wa, sem_a, *left):
    for at in left:
        arrived(wa, sem_a, *at)


def query_back(dq_ref, wa, sem_a):
    da = None
    for m in range(3):
        arrived(wa, sem_a, 0, m)
        part = nt(dq_ref[m, :, :KVW], wa[0, m, :, :KVW])
        da = part if m == 0 else da + part
    return da


def project_back(da, own_ref, near_ref, far_ref, core, cos_ref, sin_ref, dk_ref, dv_ref, one_ref, h, gain, wa, sem_a):
    cos, sin = cos_ref[...], sin_ref[...]
    grad = own_ref[...] + far_ref[...].astype(f32) + jnp.where(core == 0, near_ref[...].astype(f32), 0.0)
    dk = rope(grad[:KVW], cos, sin, True).T.astype(bf16)
    dv = grad[KVW:].T.astype(bf16)
    dk_ref[...] = widened(dk)
    dv_ref[...] = widened(dv)
    one_ref[...] = widened(jnp.where(core == 0, dv, dk))
    arrived(wa, sem_a, 0, 3)
    arrived(wa, sem_a, 1, 0)
    da = da + nt(dk, wa[0, 3, :, :KVW]) + nt(dv, wa[1, 0, :, :KVW])
    return norm_back(h, gain, da)


def back_kernel(start, end, after, sc, *rest):
    rest = list(rest)

    def take(n):
        out = rest[:n]
        del rest[:n]
        return out

    core, chip = sc[0], sc[1]
    mine_a, other_a = take(4), take(4)
    if not end:
        mine_b, other_b = take(4), take(4)
        mine_d, other_d = take(2)
    if start:
        (g_ref,) = take(1)
    else:
        g1_in, dq_ref, own_ref, near_ref, far_ref, h_ref, gain_a, cos_ref, sin_ref = take(9)
    if not end:
        ins = take(5)
    take(after)
    if not start:
        dk_ref, dv_ref, one_ref, dgain_a = take(4)
    if end:
        (g_out,) = take(1)
    else:
        outs = take(9)
    wa, sem_a = take(2)
    fetch(mine_a, other_a, wa, sem_a, core, chip)
    if not end:
        wb, sem_b, wd, sem_d = take(4)
        fetch_ffn(mine_b, other_b, mine_d, other_d, wb, wd, sem_b, sem_d, core, chip)
    if start:
        state = g_ref[...].T.astype(f32)
    else:
        da = query_back(dq_ref, wa, sem_a)
        dx, dgain = project_back(da, own_ref, near_ref, far_ref, core, cos_ref, sin_ref, dk_ref, dv_ref, one_ref, h_ref[...].astype(f32), gain_a[...], wa, sem_a)
        dgain_a[...] = dgain
        state = g1_in[...] + dx
    if end:
        g_out[...] = state.astype(bf16).T
        finish_a(wa, sem_a, (1, 1), (1, 2), (1, 3))
    else:
        ffn_back(state, core, (*ins, *outs), (wa, sem_a, wb, sem_b, wd, sem_d), mine_d)
        if start:
            finish_a(wa, sem_a, (1, 0), (0, 0), (0, 1), (0, 2), (0, 3))


def back(start, end, sc, weights, tail, ffn, after=()):
    wa, wb, wd = weights
    width = wa[0][0].shape[0]
    args = [sc, *wa[0], *wa[1]]
    specs = [SCALARS] + [LEFT] * 8
    scratch = scratch_a(width)
    if not end:
        args += [*wb[0], *wb[1], *wd]
        specs += [LEFT] * 10
        scratch += scratch_ffn(width, wb[0][0].shape[1])
    args += list(tail)
    specs += [WHOLE] * len(tail)
    n = tail[0].shape[1 if start else 0]
    outs = []
    if not end:
        args += list(ffn)
        specs += [WHOLE] * len(ffn)
    if not start:
        outs += [shape((n, PIECE), bf16)] * 3 + [shape((1, width), f32)]
    if end:
        outs += [shape((width, n), bf16)]
    else:
        hidden = ffn[0].shape[1]
        outs += [shape((n, width), bf16), shape((n, hidden), bf16), shape((n, hidden), bf16), shape((n, hidden // 2), bf16), shape((n, hidden // 2), bf16)]
        outs += [shape((n, width), f32), shape((3, n, PIECE), bf16), shape((1, width), f32), shape((width, n), bf16)]
    args += list(after)
    specs += [LEFT] * len(after)
    return pl.pallas_call(
        functools.partial(back_kernel, start, end, len(after)),
        out_shape=tuple(outs),
        in_specs=specs,
        out_specs=(WHOLE,) * len(outs),
        scratch_shapes=scratch,
        compiler_params=pltpu.CompilerParams(vmem_limit_bytes=LIMIT),
        name="back_end" if end else ("back_start" if start else "back_join"),
    )(*args)


def by_turn(core, chip):
    one = 1 + core
    return chip ^ one, chip ^ 3, chip, chip ^ (3 - one)


def turned(dst, blocks):
    n = blocks[0].shape[0]
    for i, block in enumerate(blocks):
        dst[:, i * n : (i + 1) * n] = block[...].T


def grad_ffn_kernel(sc, *rest):
    lefts, rights = rest[:4], rest[4:8]
    send_ref, keep_ref, left, right = rest[-4:]
    core, chip = sc[0], sc[1]
    n, cols = rights[0].shape[0], right.shape[1]
    turned(left, lefts)
    for i, m in enumerate(by_turn(core, chip)):
        at = pl.multiple_of(m * cols, 128)
        for j, block in enumerate(rights):
            right[j * n : (j + 1) * n, :] = block[:, pl.ds(at, cols)]
        out = send_ref if i < 2 else keep_ref
        out[i % 2] = nn(left[...], right[...]).astype(bf16)


def grad_ffn(sc, lefts, rights):
    n, width = lefts[0].shape
    cols = rights[0].shape[1] // 4
    out = shape((2, width, cols), bf16)
    return pl.pallas_call(
        grad_ffn_kernel,
        out_shape=(out, out),
        in_specs=[SCALARS] + [WHOLE] * 8,
        out_specs=(WHOLE,) * 2,
        scratch_shapes=[pltpu.VMEM((width, 4 * n), bf16), pltpu.VMEM((4 * n, cols), bf16)],
        compiler_params=pltpu.CompilerParams(vmem_limit_bytes=36 << 20),
        name="grad_ffn",
    )(sc, *lefts, *rights)


def grad_down_kernel(sc, *rest):
    lefts, rights = rest[:4], rest[4:8]
    outs, left, right = rest[-4:-2], rest[-2], rest[-1]
    n, cols = rights[0].shape[0], right.shape[1]
    turned(left, lefts)
    for i, out in enumerate(outs):
        at = pl.multiple_of(((sc[2] + i) & 1) * cols, 128)
        for j, block in enumerate(rights):
            right[j * n : (j + 1) * n, :] = block[:, pl.ds(at, cols)]
        out[...] = nn(left[...], right[...]).astype(bf16)


def grad_down(sc, lefts, rights, after):
    n, width = lefts[0].shape
    cols = rights[0].shape[1] // 2
    return pl.pallas_call(
        grad_down_kernel,
        out_shape=(shape((width, cols), bf16),) * 2,
        in_specs=[SCALARS] + [WHOLE] * 8 + [LEFT] * len(after),
        out_specs=(WHOLE,) * 2,
        scratch_shapes=[pltpu.VMEM((width, 4 * n), bf16), pltpu.VMEM((4 * n, cols), bf16)],
        compiler_params=pltpu.CompilerParams(vmem_limit_bytes=32 << 20),
        name="grad_down",
    )(sc, *lefts, *rights, *after)


def grad_attention_kernel(sc, *rest):
    a_refs, o_refs, rest = rest[:4], rest[4:8], rest[8:]
    queries, keys, values, outs, threes, ones = (rest[i : i + 2] for i in range(0, 12, 2))
    send_ref, keep_ref, left, right = rest[-4:]
    core, chip = sc[0], sc[1]
    n = a_refs[0].shape[0]
    turned(left.at[0], a_refs)

    def fill(at, of_three, own_three, own_one, single):
        for j in range(2):
            for i in range(3):
                right[of_three + i, j * n : (j + 1) * n, :] = own_three[j][i]
                right[of_three + i, (j + 2) * n : (j + 3) * n, :] = threes[j][i]
            right[single, j * n : (j + 1) * n, :] = own_one[j][...]
            right[single, (j + 2) * n : (j + 3) * n, :] = ones[j][...]

    @pl.when(core == 0)
    def _():
        fill(0, 0, queries, keys, 3)

    @pl.when(core == 1)
    def _():
        turned(left.at[1], o_refs)
        fill(0, 1, outs, values, 0)

    for i, m in enumerate(by_turn(core, chip)):
        out = send_ref if i < 2 else keep_ref
        which = jnp.where(m > 0, core, 0)
        out[i % 2] = nn(left[which], right[m]).astype(bf16)


def grad_attention(sc, a, o, own, got, after):
    n, width = a[0].shape
    out = shape((2, width, PIECE), bf16)
    return pl.pallas_call(
        grad_attention_kernel,
        out_shape=(out, out),
        in_specs=[SCALARS] + [WHOLE] * 20 + [LEFT] * len(after),
        out_specs=(WHOLE,) * 2,
        scratch_shapes=[pltpu.VMEM((2, width, 4 * n), bf16), pltpu.VMEM((4, 4 * n, PIECE), bf16)],
        compiler_params=pltpu.CompilerParams(vmem_limit_bytes=36 << 20),
        name="grad_attention",
    )(sc, *a, *o, *own, *got, *after)


def lay_kernel(count, sc, *rest):
    mine, other, outs, kept = rest[:4], rest[4:8], rest[-1 - count : -1], rest[-1]
    core, chip = sc[0], sc[1]
    for kind, pieces in ((core, mine), (1 - core, other)):
        for who, piece in zip(whose(kind), pieces):
            kept[kind, chip ^ who] = piece[...]
    n = sum(o.shape[1] for o in outs) // 8
    cols = [jnp.concatenate([kept[c, m, :, :n].astype(f32) for m in range(4)], axis=1) for c in range(2)]
    if len(outs) == 2:
        outs[0][...] = cols[0]
        outs[1][...] = cols[1]
    else:
        outs[0][...] = cols[0][:, : 3 * n]
        outs[1][...] = cols[0][:, 3 * n :]
        outs[2][...] = cols[1][:, :n]
        outs[3][...] = cols[1][:, n:]


def lay(sc, mine, other, widths, after):
    rows, n = mine[0].shape
    outs = tuple(shape((rows, w), f32) for w in widths)
    return pl.pallas_call(
        functools.partial(lay_kernel, len(widths)),
        out_shape=outs,
        in_specs=[SCALARS] + [WHOLE] * 8 + [LEFT] * len(after),
        out_specs=(WHOLE,) * len(outs),
        scratch_shapes=[pltpu.VMEM((2, 4, rows, n), bf16)],
        compiler_params=pltpu.CompilerParams(vmem_limit_bytes=24 << 20),
        name="lay",
    )(sc, *mine, *other, *after)


def pick_kernel(by_core, sc, *rest):
    sources, (out_ref, sem) = rest[:2], rest[-2:]
    core, chip = sc[0], sc[1]
    if by_core:
        cols = out_ref.shape[1]
        at = pl.ds(pl.multiple_of(chip * cols, 128), cols)
        views = [source.at[:, at] for source in sources]
    else:
        half = out_ref.shape[0]
        views = [source.at[c * half : (c + 1) * half, :] for c, source in enumerate(sources)]
    for c in range(2):

        @pl.when(core == c)
        def _():
            pltpu.make_async_copy(views[c], out_ref, sem).start()

    pltpu.make_async_copy(views[0], out_ref, sem).wait()


def pick(sc, sources, out, by_core, after):
    return pl.pallas_call(
        functools.partial(pick_kernel, by_core),
        out_shape=shape(out, bf16),
        in_specs=[SCALARS] + [LEFT] * (2 + len(after)),
        out_specs=WHOLE,
        scratch_shapes=[pltpu.SemaphoreType.DMA],
        compiler_params=pltpu.CompilerParams(vmem_limit_bytes=16 << 20),
        name="pick",
    )(sc, *sources, *after)


def stack_kernel(sc, *rest):
    parts, out_ref, sems = rest[:4], rest[-2], rest[-1]
    copies = [pltpu.make_async_copy(p, out_ref.at[(sc[2] - s) & 3], sems.at[s]) for s, p in enumerate(parts)]
    for copy in copies:
        copy.start()
    for copy in copies:
        copy.wait()


def stack(sc, parts, after=()):
    return pl.pallas_call(
        stack_kernel,
        out_shape=shape((4,) + parts[0].shape, parts[0].dtype),
        in_specs=[SCALARS] + [LEFT] * (4 + len(after)),
        out_specs=WHOLE,
        scratch_shapes=[pltpu.SemaphoreType.DMA((4,))],
        compiler_params=pltpu.CompilerParams(vmem_limit_bytes=16 << 20),
        name="stack",
    )(sc, *parts, *after)


def small(kernel, sc, args, outs, scratch, after, name):
    return pl.pallas_call(
        kernel,
        out_shape=tuple(outs),
        in_specs=[SCALARS] + [WHOLE] * len(args) + [LEFT] * len(after),
        out_specs=(WHOLE,) * len(outs),
        scratch_shapes=scratch,
        compiler_params=pltpu.CompilerParams(vmem_limit_bytes=32 << 20),
        name=name,
    )(sc, *args, *after)


def sum_first(sc, keep, got, after):
    def kernel(sc, keep_ref, got_ref, *rest):
        later_ref, own_ref = rest[-2:]
        later_ref[...] = (keep_ref[1].astype(f32) + got_ref[1].astype(f32)).astype(bf16)
        own_ref[...] = keep_ref[0].astype(f32) + got_ref[0].astype(f32)

    block = keep.shape[1:]
    return small(kernel, sc, [keep, got], [shape(block, bf16), shape(block, f32)], [], after, "sum_first")


def sum_second(sc, own, got, after):
    def kernel(sc, own_ref, got_ref, *rest):
        outs, total = rest[-5:-1], rest[-1]
        n = total.shape[1]
        for j in range(4):
            rows = slice(j * n, (j + 1) * n)
            total[j] = own_ref[rows, :] + got_ref[rows, :].astype(f32)
        for s, out in enumerate(outs):
            out[...] = total[(sc[2] + s) & 3].astype(out.dtype)

    rows, cols = own.shape
    part = (rows // 4, cols)
    outs = [shape(part, f32)] + [shape(part, bf16)] * 3
    return small(kernel, sc, [own, got], outs, [pltpu.VMEM((4,) + part, f32)], after, "sum_second")


def sum_ring(sc, own, got, after):
    def kernel(sc, own_ref, *rest):
        out_ref = rest[-1]
        out_ref[...] = (own_ref[...] + sum(g[...].astype(f32) for g in rest[:3])).astype(bf16)

    return small(kernel, sc, [own, *got], [shape(own.shape, bf16)], [], after, "sum_ring")[0]


def down_ring(sc, own, got, after):
    def kernel(sc, own_ref, *rest):
        give_ref, keep_ref, total = rest[-3:]
        half = give_ref.shape[0]
        total[...] = own_ref[...].astype(f32) + sum(g[...].astype(f32) for g in rest[:3])
        give_ref[...] = total[pl.ds(pl.multiple_of((1 - sc[0]) * half, half), half), :].astype(bf16)
        keep_ref[...] = total[pl.ds(pl.multiple_of(sc[0] * half, half), half), :].astype(bf16)

    rows, cols = own.shape
    half = shape((rows // 2, cols), bf16)
    return small(kernel, sc, [own, *got], [half, half], [pltpu.VMEM((rows, cols), f32)], after, "down_ring")


def down_split(sc, keep, given, after):
    def kernel(sc, keep_ref, given_ref, *rest):
        send_ref, kept_ref, total = rest[-3:]
        n = total.shape[1]
        owner = (sc[2] >> 1) == sc[0]
        for m in range(4):
            rows = slice(m * n, (m + 1) * n)
            total[m] = jnp.where(owner, keep_ref[rows, :].astype(f32), given_ref[rows, :].astype(f32))
        for i, m in enumerate(by_turn(sc[0], sc[1])):
            out = send_ref if i < 2 else kept_ref
            out[i % 2] = total[m].astype(bf16)

    rows, cols = keep.shape
    out = shape((2, rows // 4, cols), bf16)
    return small(kernel, sc, [keep, given], [out, out], [pltpu.VMEM((4, rows // 4, cols), f32)], after, "down_split")


def sum_two(sc, own, got, after):
    def kernel(sc, own_ref, got_ref, *rest):
        rest[-1][...] = (own_ref[...] + got_ref[...].astype(f32)).astype(bf16)

    return small(kernel, sc, [own, got], [shape(own.shape, bf16)], [], after, "sum_two")[0]


def lay_down(sc, mine, other, after):
    def kernel(sc, *rest):
        out_ref, total = rest[-2:]
        n = total.shape[2]
        for kind, pieces in ((sc[0], rest[:4]), (1 - sc[0], rest[4:8])):
            for who, piece in zip(whose(kind), pieces):
                total[kind, sc[1] ^ who] = piece[...].astype(f32)
        for c in range(2):
            for m in range(4):
                at = (c * 4 + m) * n
                out_ref[at : at + n, :] = total[c, m]

    n, cols = mine[0].shape
    return small(kernel, sc, [*mine, *other], [shape((8 * n, cols), f32)], [pltpu.VMEM((2, 4, n, cols), f32)], after, "lay_down")[0]


CORE, SIDE, BACK = 1, 2, 4
rope_base = 10000.0
RUNS = 2


def flip(value, bit, bit1=None):
    count = lax.axis_size("dp")
    bits = (bit, bit if bit1 is None else bit1)
    return lax.ppermute(value, "dp", [(i, i ^ bits[i & 1]) for i in range(count)])


def turn_z(value, step):
    count = lax.axis_size("fsdp")
    return lax.ppermute(value, "fsdp", [(i, (i + step) % count) for i in range(count)])


def home_to_work(value, back=False):
    count, depth = lax.axis_size("dp"), lax.axis_size("fsdp")
    pairs = []
    for d in range(count):
        for z in range(depth):
            there = (d & ~1) | (z & 1), 2 * (d & 1) + (z >> 1)
            pair = (d * depth + z, there[0] * depth + there[1])
            pairs.append(pair[::-1] if back else pair)
    return lax.ppermute(value, ("dp", "fsdp"), pairs)


def place():
    d, z = lax.axis_index("dp"), lax.axis_index("fsdp")
    return d & 1, (d >> 1) & 3, z


def turns(shard):
    return [shard] + [turn_z(shard, s) for s in range(1, lax.axis_size("fsdp"))]


def plane_gather(piece):
    first, second = flip(piece, SIDE, BACK), flip(piece, BACK, SIDE)
    mine = (piece, first, second, flip(first, BACK, SIDE))
    return mine, tuple(flip(p, CORE) for p in mine)


def small_gather(shard):
    z = lax.axis_index("fsdp")
    full = jnp.zeros((lax.axis_size("fsdp"),) + shard.shape, shard.dtype)
    for s, part in enumerate(turns(shard)):
        full = lax.dynamic_update_index_in_dim(full, part, (z - s) % full.shape[0], 0)
    return full


def window(own):
    core, _, _ = place()
    depth = lax.axis_size("fsdp")
    far = lax.ppermute(own, "fsdp", [(z, z + 1) for z in range(0, depth, 2)])
    near = flip(jnp.where(core == 0, own, far), CORE)
    return far, near, own


def unwindow(far, near):
    core, _, _ = place()
    depth = lax.axis_size("fsdp")
    near = flip(near, CORE)
    far = jnp.where(core == 1, far + near.astype(f32), far).astype(bf16)
    return near, lax.ppermute(far, "fsdp", [(z + 1, z) for z in range(0, depth, 2)])


def over_groups(value):
    bit = 8
    while bit < lax.axis_size("dp"):
        value = (value.astype(f32) + flip(value, bit).astype(f32)).astype(bf16)
        bit *= 2
    return value


def spread(piece):
    return piece, flip(piece, SIDE, BACK), flip(piece, BACK, SIDE), flip(piece, SIDE | BACK)


def across(pieces):
    return tuple(flip(p, CORE) for p in pieces)


def to_owners(part, step):
    count, depth = lax.axis_size("dp"), lax.axis_size("fsdp")
    pairs = []
    for d in range(count):
        for a in range(depth):
            b = (a + step) % depth
            if (b >> 1) == (d & 1):
                pairs.append((d * depth + a, d * depth + b))
    return lax.ppermute(part, ("dp", "fsdp"), pairs)


def reduce_gains(total):
    z = lax.axis_index("fsdp")
    depth = lax.axis_size("fsdp")
    bit = 1
    while bit < lax.axis_size("dp"):
        total = total + flip(total, bit)
        bit *= 2
    rows = total.shape[1] // depth
    total = total + sum(turn_z(total, s) for s in range(1, depth))
    mine = lax.dynamic_slice_in_dim(total, z * rows, rows, 1)
    return mine[0], mine[1]


def body(tokens, segment_ids, attn_gain, query_weight, key_weight, value_weight, out_weight, ffn_gain, gate_weight, up_weight, down_weight, cotangent):
    core, chip, z = place()
    sc = jnp.stack([core, chip, z]).astype(jnp.int32)
    _, stretch, width = tokens.shape
    rows, depth = query_weight.shape[0], lax.axis_size("fsdp")

    first = jnp.concatenate([query_weight, key_weight, value_weight, out_weight], axis=1)
    first = jnp.pad(first, ((0, 0), (0, PIECE - KVW)))
    parts_a = turns(lax.dynamic_slice(first, (0, KVW * (core * 4 + chip)), (rows, PIECE)))
    wa = plane_gather(stack(sc, parts_a).reshape(depth * rows, PIECE))
    piece_b = pick(sc, [gate_weight, up_weight], (rows, gate_weight.shape[1] // 4), True, parts_a[1:])
    whole_b = stack(sc, turns(piece_b)).reshape(depth * rows, piece_b.shape[1])
    wb = plane_gather(whole_b)
    piece_d = pick(sc, [down_weight.T] * 2, (width // 2, down_weight.shape[0]), False, [whole_b])
    whole_d = stack(sc, turns(piece_d))
    wd = whole_d, flip(whole_d, CORE)
    weights = wa, wb, wd

    tokens = home_to_work(tokens[0].T)
    gains = small_gather(jnp.stack([attn_gain, ffn_gain]))
    gains = jnp.moveaxis(gains, 0, 1).reshape(2, 1, width).astype(f32)
    gain_a, gain_f = gains[0], gains[1]
    row = small_gather(segment_ids[0]).reshape(-1)
    row = jnp.where((z >> 1) == core, row, flip(row, CORE))
    block = 2 * (z & 1) + core
    padded = jnp.concatenate([jnp.full((2 * stretch,), -1, row.dtype), row])
    seg_k = lax.dynamic_slice(padded, (block * stretch,), (3 * stretch,))
    seg_q = seg_k[2 * stretch :]
    ahead = jnp.arange(3 * stretch)[:, None] < 2 * stretch + jnp.arange(stretch)[None, :]
    seg_k, seg_q = seg_k[:, None], seg_q[None, :]
    positions = jnp.sum(((seg_k == seg_q) & ahead).astype(f32), axis=0)
    freq = rope_base ** (-2.0 * jnp.arange(HEAD_DIM // 2, dtype=f32) / HEAD_DIM)
    angle = freq[:, None] * positions[None, :]
    cos, sin = jnp.cos(angle), jnp.sin(angle)
    cot = home_to_work(cotangent[0].T)

    h_0, a0, q0, own = pre(sc, tokens, gain_a, cos, sin, *wa, [whole_b])
    kv0 = window(own)
    o0, lse0 = attend(q0, kv0, seg_k, seg_q)
    mixed0, h1_0, b0, gate0, up0, z0, h_1, a1, q1, own = post(False, sc, o0, h_0, gain_f, gain_a, cos, sin, *weights)
    kv1 = window(own)
    o1, lse1 = attend(q1, kv1, seg_k, seg_q)
    mixed1, h1_1, b1, gate1, up1, z1, output = post(True, sc, o1, h_1, gain_f, gain_a, cos, sin, *weights)
    output = home_to_work(output, back=True).T

    gb1, act1, away1, zk1, zs1, g1, p1, dgain_f1, do = back(True, False, sc, weights, [cot], [gate1, up1, h1_1, gain_f, z1])
    dq1, three1, far, near, own = attend_back(sc, p1, q1, kv1, seg_k, seg_q, lse1, do, cos, sin)
    near, far = unwindow(far, near)
    tail = [g1, dq1, own, near, far, h_1, gain_a, cos, sin]
    dk1, dv1, one1, dgain_a1, gb0, act0, away0, zk0, zs0, g1, p0, dgain_f0, do = back(False, False, sc, weights, tail, [gate0, up0, h1_0, gain_f, z0])

    def pair(*own):
        return [*own, *across(own)]

    send_b, keep_b = grad_ffn(sc, pair(b1, b0), [act1, act0, *across((away1, away0))])
    got_b = flip(send_b, SIDE, BACK)
    like_d, unlike_d = grad_down(sc, pair(gb1, gb0), [zk1, zk0, *across((zs1, zs0))], [send_b])
    got_d = [to_owners(unlike_d, 1), to_owners(like_d, 2), to_owners(unlike_d, 3)]
    owner = (z >> 1) == core
    own_d = jnp.where(owner, like_d, jnp.zeros_like(like_d))

    dq0, three0, far, near, own = attend_back(sc, p0, q0, kv0, seg_k, seg_q, lse0, do, cos, sin, [like_d])
    near, far = unwindow(far, near)
    later_b, own_b = sum_first(sc, keep_b, got_b, [own])
    more_b = flip(later_b, BACK, SIDE)
    tail = [g1, dq0, own, near, far, h_0, gain_a, cos, sin]
    dk0, dv0, one0, dgain_a0, grad_tokens = back(False, True, sc, weights, tail, None, [later_b])
    grad_tokens = home_to_work(grad_tokens, back=True).astype(f32).T

    own = [dq1, dq0, dk1, dk0, dv1, dv0, p1, p0]
    send_a, keep_a = grad_attention(sc, pair(a1, a0), pair(mixed1, mixed0), own, across((three1, three0, one1, one0)), [])
    got_a = flip(send_a, SIDE, BACK)
    ring_b = sum_second(sc, own_b, more_b, [send_a])
    ring_b, parts_b = ring_b[0], [turn_z(v, s + 1) for s, v in enumerate(ring_b[1:])]
    later_a, own_a = sum_first(sc, keep_a, got_a, [ring_b])
    more_a = flip(later_a, BACK, SIDE)
    give, keep = down_ring(sc, own_d, got_d, [later_a])
    send_d, keep_d = down_split(sc, keep, flip(give, CORE), [])
    got_d = flip(send_d, SIDE, BACK)
    ring_a = sum_second(sc, own_a, more_a, [send_d])
    ring_a, parts_a = ring_a[0], [turn_z(v, s + 1) for s, v in enumerate(ring_a[1:])]
    later_d, own_d = sum_first(sc, keep_d, got_d, [ring_a])
    more_d = flip(later_d, BACK, SIDE)
    piece_b = over_groups(sum_ring(sc, ring_b, parts_b, [later_d]))
    all_b = spread(piece_b)
    piece_d = over_groups(sum_two(sc, own_d, more_d, [piece_b]))
    all_d = spread(piece_d)
    piece_a = over_groups(sum_ring(sc, ring_a, parts_a, [piece_d]))
    all_a = spread(piece_a)
    grad_gate, grad_up = lay(sc, all_b, across(all_b), (gate_weight.shape[1],) * 2, [piece_a])
    grad_down_ = lay_down(sc, all_d, across(all_d), [grad_gate])
    grad_query, grad_key, grad_value, grad_out = lay(sc, all_a, across(all_a), (width, KVW, KVW, width), [grad_down_])
    dgain_a, dgain_f = reduce_gains(jnp.concatenate([dgain_a1 + dgain_a0, dgain_f1 + dgain_f0]))
    return (output[None], grad_tokens[None], dgain_a, grad_query, grad_key, grad_value, grad_out, dgain_f, grad_gate, grad_up, grad_down_.T)


def solution(mesh):
    wide, rows, shard = P("dp", "fsdp", None), P("dp", "fsdp"), P("fsdp", None)
    in_specs = (wide, rows, P("fsdp"), shard, shard, shard, shard, P("fsdp"), shard, shard, shard, wide)
    out_specs = (wide, wide, P("fsdp"), shard, shard, shard, shard, P("fsdp"), shard, shard, shard)
    return jax.shard_map(body, mesh=mesh, in_specs=in_specs, out_specs=out_specs, check_vma=False)
```

```python
import functools
import jax
import jax.numpy as jnp
from jax import lax
from jax.sharding import PartitionSpec as P
from jax.experimental import pallas as pl
from jax.experimental.pallas import tpu as pltpu

f32, bf16 = jnp.float32, jnp.bfloat16
eps = 1e-05
HEADS, KV_HEADS, HEAD_DIM, GROUP, KVW = 15, 5, 64, 3, 320
IDS = 16
PIECE = 384
LIMIT = 58 << 20
WHOLE = pl.BlockSpec(memory_space=pltpu.VMEM)
LEFT = pl.BlockSpec(memory_space=pl.ANY)
SCALARS = pl.BlockSpec(memory_space=pltpu.SMEM)
BRIEF = pl.CostEstimate(flops=1024, bytes_accessed=1024, transcendentals=0)


def contract(a, b, i, j):
    return lax.dot_general(a, b, (((i,), (j,)), ((), ())), preferred_element_type=f32)


def nn(a, b):
    return contract(a, b, 1, 0)


def nt(a, b):
    return contract(a, b, 1, 1)


def tn(a, b):
    return contract(a, b, 0, 0)


def whose(core):
    return 0, 1 + core, 2 - core, 3


def fetch(mine, other, kept, sems, core, chip):
    for kind, pieces in ((core, mine), (1 - core, other)):
        for who, piece in zip(whose(kind), pieces):
            at = chip ^ who
            pltpu.make_async_copy(piece, kept.at[kind, at], sems.at[kind, at]).start()


def arrived(kept, sems, *at):
    pltpu.make_async_copy(kept.at[at], kept.at[at], sems.at[at]).wait()


def normed(x, gain):
    return x * lax.rsqrt(jnp.mean(x * x, axis=-1, keepdims=True) + eps) * gain


def norm_back(x, gain, grad):
    r = lax.rsqrt(jnp.mean(x * x, axis=-1, keepdims=True) + eps)
    hat = x * r
    scaled = grad * gain
    dx = r * (scaled - hat * jnp.mean(scaled * hat, axis=-1, keepdims=True))
    return dx, jnp.sum(grad * hat, axis=0, keepdims=True)


def widened(x):
    return jnp.concatenate([x, jnp.zeros((x.shape[0], PIECE - x.shape[1]), x.dtype)], axis=1)


def rope(u, cos, sin, back):
    heads = u.shape[0] // HEAD_DIM
    half = HEAD_DIM // 2
    out = []
    for h in range(heads):
        u1, u2 = u[h * HEAD_DIM : h * HEAD_DIM + half], u[h * HEAD_DIM + half : (h + 1) * HEAD_DIM]
        if back:
            out += [u1 * cos + u2 * sin, u2 * cos - u1 * sin]
        else:
            out += [u1 * cos - u2 * sin, u2 * cos + u1 * sin]
    return jnp.concatenate(out, axis=0)


def project(state, gain_ref, cos_ref, sin_ref, ids, kept, sems, a_ref, q_ref, kv_ref):
    a = normed(state, gain_ref[...]).astype(bf16)
    a_ref[...] = a
    cos, sin = cos_ref[...], sin_ref[...]
    arrived(kept, sems, 0, 3)
    kv_ref[:KVW, :] = rope(nn(a, kept[0, 3, :, :KVW]).T, cos, sin, False).astype(bf16)
    arrived(kept, sems, 1, 0)
    kv_ref[2 * KVW :, :] = ids
    kv_ref[KVW : 2 * KVW, :] = nn(a, kept[1, 0, :, :KVW]).T.astype(bf16)
    for m in range(3):
        arrived(kept, sems, 0, m)
        q_ref[pl.ds(m * KVW, KVW), :] = rope(nn(a, kept[0, m, :, :KVW]).T, cos, sin, False).astype(bf16)


def pre_kernel(sc, ht_ref, gain_ref, cos_ref, sin_ref, *rest):
    width = ht_ref.shape[0] - IDS
    mine, other = rest[:4], rest[4:8]
    h_ref, a_ref, q_ref, kv_ref, kept, sems = rest[-6:]
    core, chip = sc[0], sc[1]
    fetch(mine, other, kept, sems, core, chip)
    h = ht_ref[:width, :].T
    h_ref[...] = h
    project(h.astype(f32), gain_ref, cos_ref, sin_ref, ht_ref[width:, :], kept, sems, a_ref, q_ref, kv_ref)
    for m in range(1, 4):
        arrived(kept, sems, 1, m)


def scratch_a(width):
    return [pltpu.VMEM((2, 4, width, PIECE), bf16), pltpu.SemaphoreType.DMA((2, 4))]


def shape(s, d):
    return jax.ShapeDtypeStruct(s, d)


def pre(sc, ht, gain, cos, sin, mine_a, other_a, after):
    width, n = ht.shape[0] - IDS, ht.shape[1]
    return pl.pallas_call(
        pre_kernel,
        out_shape=(shape((n, width), bf16), shape((n, width), bf16), shape((width, n), bf16), shape((2 * KVW + IDS, n), bf16)),
        in_specs=[SCALARS] + [WHOLE] * 4 + [LEFT] * (8 + len(after)),
        out_specs=(WHOLE,) * 4,
        scratch_shapes=scratch_a(width),
        cost_estimate=BRIEF,
        compiler_params=pltpu.CompilerParams(vmem_limit_bytes=LIMIT),
        name="pre",
    )(sc, ht, gain, cos, sin, *mine_a, *other_a, *after)


def bias_of(kv):
    keys, n = kv.shape[1], kv.shape[1] // 3
    ids = kv[2 * KVW :, :].astype(f32)
    seg_k, seg_q = ids.T[:, :1], ids[:1, 2 * n :]
    j = lax.broadcasted_iota(jnp.int32, (keys, n), 0)
    i = lax.broadcasted_iota(jnp.int32, (keys, n), 1) + (keys - n)
    return jnp.where((seg_k == seg_q) & (j <= i), 0.0, -1e30).astype(f32)


def window_of(parts, whole):
    n = parts[0].shape[1]
    for w, part in enumerate(parts):
        whole[:, w * n : (w + 1) * n] = part[...]


def attend_kernel(q_ref, kv0, kv1, kv2, o_ref, lse_ref, bias, kv):
    window_of((kv0, kv1, kv2), kv)
    bias[...] = bias_of(kv)

    def head(e, _):
        row = pl.multiple_of(e * HEAD_DIM, HEAD_DIM)
        k = kv[pl.ds(row, HEAD_DIM), :]
        v = kv[pl.ds(row + KVW, HEAD_DIM), :]
        for g in range(GROUP):
            at = pl.multiple_of((e * GROUP + g) * HEAD_DIM, HEAD_DIM)
            q = q_ref[pl.ds(at, HEAD_DIM), :]
            s = tn(k, q) * HEAD_DIM ** (-0.5) + bias[...]
            top = jnp.max(s, axis=0, keepdims=True)
            expo = jnp.exp(s - top)
            total = jnp.sum(expo, axis=0, keepdims=True)
            probs = (expo * (1.0 / total)).astype(bf16)
            o_ref[pl.ds(at, HEAD_DIM), :] = nn(v, probs).astype(bf16)
            lse_ref[pl.ds(e * GROUP + g, 1), :] = top + jnp.log(total)
        return 0

    lax.fori_loop(0, KV_HEADS, head, 0)


def attend(q, kvs):
    width, n = q.shape
    return pl.pallas_call(
        attend_kernel,
        out_shape=(shape((width, n), bf16), shape((HEADS, n), f32)),
        in_specs=[WHOLE] * 4,
        out_specs=(WHOLE,) * 2,
        scratch_shapes=[pltpu.VMEM((3 * n, n), f32), pltpu.VMEM((2 * KVW + IDS, 3 * n), bf16)],
        cost_estimate=BRIEF,
        compiler_params=pltpu.CompilerParams(vmem_limit_bytes=24 << 20),
        name="attend",
    )(q, *kvs)


def attend_back_kernel(sc, p_ref, q_ref, kv0, kv1, kv2, lse_ref, do_ref, cos_ref, sin_ref, *rest):
    dq_ref, three_ref, far_ref, near_ref, own_ref, bias, kv, dqs = rest[-8:]
    n = q_ref.shape[1]
    window_of((kv0, kv1, kv2), kv)
    bias[...] = bias_of(kv)
    scale = HEAD_DIM ** (-0.5)

    def head(e, _):
        row = pl.multiple_of(e * HEAD_DIM, HEAD_DIM)
        k = kv[pl.ds(row, HEAD_DIM), :]
        v = kv[pl.ds(row + KVW, HEAD_DIM), :]
        dk = dv = None
        for g in range(GROUP):
            at = pl.multiple_of((e * GROUP + g) * HEAD_DIM, HEAD_DIM)
            q = q_ref[pl.ds(at, HEAD_DIM), :]
            do = do_ref[pl.ds(at, HEAD_DIM), :]
            s = tn(k, q) * scale + bias[...]
            probs = jnp.exp(s - lse_ref[pl.ds(e * GROUP + g, 1), :])
            dp = tn(v, do)
            inner = jnp.sum(probs * dp, axis=0, keepdims=True)
            ds = (probs * (dp - inner)).astype(bf16)
            dvg, dkg = nt(do, probs.astype(bf16)), nt(q, ds)
            dv, dk = (dvg, dkg) if g == 0 else (dv + dvg, dk + dkg)
            dqs[pl.ds(at, HEAD_DIM), :] = nn(k, ds)
        for at, grad in ((row, dk * scale), (row + KVW, dv)):
            far_ref[pl.ds(at, HEAD_DIM), :] = grad[:, :n]
            near_ref[pl.ds(at, HEAD_DIM), :] = grad[:, n : 2 * n].astype(bf16)
            own_ref[pl.ds(at, HEAD_DIM), :] = grad[:, 2 * n :]
        return 0

    lax.fori_loop(0, KV_HEADS, head, 0)
    cos, sin = cos_ref[...] * scale, sin_ref[...] * scale
    for m in range(3):
        dq = widened(rope(dqs[m * KVW : (m + 1) * KVW, :], cos, sin, True).T.astype(bf16))
        dq_ref[m] = dq
        three_ref[m] = jnp.where(sc[0] == 0, p_ref[m], dq)


def attend_back(sc, p, q, kvs, lse, do, cos, sin, after=()):
    width, n = q.shape
    block = (2 * KVW, n)
    return pl.pallas_call(
        attend_back_kernel,
        out_shape=(shape((3, n, PIECE), bf16), shape((3, n, PIECE), bf16), shape(block, f32), shape(block, bf16), shape(block, f32)),
        in_specs=[SCALARS] + [WHOLE] * 9 + [LEFT] * len(after),
        out_specs=(WHOLE,) * 5,
        scratch_shapes=[pltpu.VMEM((3 * n, n), f32), pltpu.VMEM((2 * KVW + IDS, 3 * n), bf16), pltpu.VMEM((width, n), f32)],
        cost_estimate=BRIEF,
        compiler_params=pltpu.CompilerParams(vmem_limit_bytes=32 << 20),
        name="attend_back",
    )(sc, p, q, *kvs, lse, do, cos, sin, *after)


def fetch_ffn(mine_b, other_b, down, wb, wd, sem_b, sem_d, core, chip):
    fetch(mine_b, other_b, wb, sem_b, core, chip)
    half, n, width = down[0].shape[1], down[2].shape[1], wd.shape[1]

    def copy(part, row, size):
        rows = pl.ds(pl.multiple_of(row, 16), size)
        pltpu.make_async_copy(part, wd.at[:, rows], sem_d).start()

    copy(down[0], core * half, half)
    copy(down[1], (1 - core) * half, half)
    for kind, parts in ((core, down[2:6]), (1 - core, down[6:10])):
        for who, part in zip(whose(kind), parts):
            copy(part, 2 * half + (kind * 4 + (chip ^ who)) * n, n)


def arrived_down(wd, sem_d):
    pltpu.make_async_copy(wd, wd, sem_d).wait()


def scratch_ffn(width, n):
    return [
        pltpu.VMEM((2, 4, width, n), bf16),
        pltpu.SemaphoreType.DMA((2, 4)),
        pltpu.VMEM((4, width, n), bf16),
        pltpu.SemaphoreType.DMA,
    ]


def post_kernel(last, sc, ot_ref, h_ref, gain_ref, gain_a, cos_ref, sin_ref, *rest):
    mine_a, other_a, mine_b, other_b = rest[:4], rest[4:8], rest[8:12], rest[12:16]
    down, ids_ref = rest[16:26], rest[26]
    o_ref, h1_ref, b_ref, gate_ref, up_ref, z_ref, next_ref = rest[27:34]
    more, rest = rest[34 : 34 + (0 if last else 3)], rest[34 + (0 if last else 3) :]
    wa, sem_a, wb, sem_b, wd, sem_d = rest
    core, chip = sc[0], sc[1]
    fetch(mine_a, other_a, wa, sem_a, core, chip)
    fetch_ffn(mine_b, other_b, down, wb, wd, sem_b, sem_d, core, chip)
    o = ot_ref[...].T
    o_ref[...] = o
    for m in range(1, 4):
        arrived(wa, sem_a, 1, m)
    h1 = h_ref[...].astype(f32) + jnp.concatenate([nn(o, wa[1, m, :, :KVW]) for m in range(1, 4)], axis=1)
    h1_ref[...] = h1
    b = normed(h1, gain_ref[...]).astype(bf16)
    b_ref[...] = b
    n = wb.shape[3]
    total = h1
    for m in range(4):
        cols = slice(m * n, (m + 1) * n)
        arrived(wb, sem_b, 0, m)
        gate = nn(b, wb[0, m])
        arrived(wb, sem_b, 1, m)
        up = nn(b, wb[1, m])
        gate_ref[:, cols] = gate.astype(bf16)
        up_ref[:, cols] = up.astype(bf16)
        z = (gate / (1.0 + jnp.exp(-gate)) * up).astype(bf16)
        z_ref[:, cols] = z
        if m == 0:
            arrived_down(wd, sem_d)
        total = total + nt(z, wd[m])
    next_ref[...] = total.astype(bf16).T if last else total
    if last:
        arrived(wa, sem_a, 1, 0)
        for m in range(4):
            arrived(wa, sem_a, 0, m)
    else:
        project(total, gain_a, cos_ref, sin_ref, ids_ref[2 * KVW :, :], wa, sem_a, *more)


def post(last, sc, ot, h, gain, gain_a, cos, sin, kv, wa, wb, wd):
    width, n = ot.shape
    hidden = wb[0][0].shape[1] * 4
    outs = [shape((n, width), bf16), shape((n, width), f32), shape((n, width), bf16)] + [shape((n, hidden), bf16)] * 3
    outs += [shape((width, n), bf16) if last else shape((n, width), f32)]
    if not last:
        outs += [shape((n, width), bf16), shape((width, n), bf16), shape((2 * KVW + IDS, n), bf16)]
    return pl.pallas_call(
        functools.partial(post_kernel, last),
        out_shape=tuple(outs),
        in_specs=[SCALARS] + [WHOLE] * 6 + [LEFT] * 26 + [WHOLE],
        out_specs=(WHOLE,) * len(outs),
        scratch_shapes=scratch_a(width) + scratch_ffn(width, hidden // 4),
        cost_estimate=BRIEF,
        compiler_params=pltpu.CompilerParams(vmem_limit_bytes=LIMIT),
        name="post",
    )(sc, ot, h, gain, gain_a, cos, sin, *wa[0], *wa[1], *wb[0], *wb[1], *wd, kv)


def ffn_back(state, core, refs, weights):
    gate_ref, up_ref, h1_ref, gain_ref, z_ref, gb_ref, keep_ref, send_ref, zk_ref, zs_ref, g1_ref, p_ref, dgain_ref, do_ref = refs
    wa, sem_a, wb, sem_b, wd, sem_d = weights
    gb = state.astype(bf16)
    gb_ref[...] = gb
    n = wb.shape[3]
    half = 2 * n
    first = core == 0
    low, high = z_ref[:, :half], z_ref[:, half:]
    zk_ref[...] = jnp.where(first, low, high)
    zs_ref[...] = jnp.where(first, high, low)
    arrived_down(wd, sem_d)
    db = None
    for m in range(4):
        cols = slice(m * n, (m + 1) * n)
        dz = nn(gb, wd[m])
        gate, up = gate_ref[:, cols].astype(f32), up_ref[:, cols].astype(f32)
        sig = 1.0 / (1.0 + jnp.exp(-gate))
        dup = (dz * (gate * sig)).astype(bf16)
        dgate = (dz * up * (sig * (1.0 + gate * (1.0 - sig)))).astype(bf16)
        keep_ref[:, cols] = jnp.where(first, dgate, dup)
        send_ref[:, cols] = jnp.where(first, dup, dgate)
        arrived(wb, sem_b, 0, m)
        part = nt(dgate, wb[0, m])
        arrived(wb, sem_b, 1, m)
        part = part + nt(dup, wb[1, m])
        db = part if m == 0 else db + part
    dx, dgain = norm_back(h1_ref[...], gain_ref[...], db)
    dgain_ref[...] = dgain
    g1 = state + dx
    g1_ref[...] = g1
    low = g1.astype(bf16)
    do = None
    for p in range(3):
        part = low[:, p * KVW : (p + 1) * KVW]
        p_ref[p] = widened(part)
        arrived(wa, sem_a, 1, p + 1)
        part = nt(wa[1, p + 1, :, :KVW], part)
        do = part if p == 0 else do + part
    do_ref[...] = do.astype(bf16)


def finish_a(wa, sem_a, *left):
    for at in left:
        arrived(wa, sem_a, *at)


def query_back(dq_ref, wa, sem_a):
    da = None
    for m in range(3):
        arrived(wa, sem_a, 0, m)
        part = nt(dq_ref[m, :, :KVW], wa[0, m, :, :KVW])
        da = part if m == 0 else da + part
    return da


def project_back(da, own_ref, near_ref, far_ref, core, cos_ref, sin_ref, dk_ref, dv_ref, one_ref, h, gain, wa, sem_a):
    cos, sin = cos_ref[...], sin_ref[...]
    grad = own_ref[...] + far_ref[...].astype(f32) + jnp.where(core == 0, near_ref[...].astype(f32), 0.0)
    dk = rope(grad[:KVW], cos, sin, True).T.astype(bf16)
    dv = grad[KVW:].T.astype(bf16)
    dk_ref[...] = widened(dk)
    dv_ref[...] = widened(dv)
    one_ref[...] = widened(jnp.where(core == 0, dv, dk))
    arrived(wa, sem_a, 0, 3)
    arrived(wa, sem_a, 1, 0)
    da = da + nt(dk, wa[0, 3, :, :KVW]) + nt(dv, wa[1, 0, :, :KVW])
    return norm_back(h, gain, da)


def back_kernel(start, end, after, sc, *rest):
    rest = list(rest)

    def take(n):
        out = rest[:n]
        del rest[:n]
        return out

    core, chip = sc[0], sc[1]
    mine_a, other_a = take(4), take(4)
    if not end:
        mine_b, other_b = take(4), take(4)
        down = take(10)
    if start:
        (g_ref,) = take(1)
    else:
        g1_in, dq_ref, own_ref, near_ref, far_ref, h_ref, gain_a, cos_ref, sin_ref = take(9)
    if not end:
        ins = take(5)
    take(after)
    if not start:
        dk_ref, dv_ref, one_ref, dgain_a = take(4)
    if end:
        (g_out,) = take(1)
    else:
        outs = take(9)
    wa, sem_a = take(2)
    fetch(mine_a, other_a, wa, sem_a, core, chip)
    if not end:
        wb, sem_b, wd, sem_d = take(4)
        fetch_ffn(mine_b, other_b, down, wb, wd, sem_b, sem_d, core, chip)
    if start:
        state = g_ref[...].T.astype(f32)
    else:
        da = query_back(dq_ref, wa, sem_a)
        dx, dgain = project_back(da, own_ref, near_ref, far_ref, core, cos_ref, sin_ref, dk_ref, dv_ref, one_ref, h_ref[...].astype(f32), gain_a[...], wa, sem_a)
        dgain_a[...] = dgain
        state = g1_in[...] + dx
    if end:
        g_out[...] = state.astype(bf16).T
        finish_a(wa, sem_a, (1, 1), (1, 2), (1, 3))
    else:
        ffn_back(state, core, (*ins, *outs), (wa, sem_a, wb, sem_b, wd, sem_d))
        if start:
            finish_a(wa, sem_a, (1, 0), (0, 0), (0, 1), (0, 2), (0, 3))


def back(start, end, sc, weights, tail, ffn, after=()):
    wa, wb, wd = weights
    width = wa[0][0].shape[0]
    args = [sc, *wa[0], *wa[1]]
    specs = [SCALARS] + [LEFT] * 8
    scratch = scratch_a(width)
    if not end:
        args += [*wb[0], *wb[1], *wd]
        specs += [LEFT] * 18
        scratch += scratch_ffn(width, wb[0][0].shape[1])
    args += list(tail)
    specs += [WHOLE] * len(tail)
    n = tail[0].shape[1 if start else 0]
    outs = []
    if not end:
        args += list(ffn)
        specs += [WHOLE] * len(ffn)
    if not start:
        outs += [shape((n, PIECE), bf16)] * 3 + [shape((1, width), f32)]
    if end:
        outs += [shape((width, n), bf16)]
    else:
        hidden = ffn[0].shape[1]
        outs += [shape((n, width), bf16), shape((n, hidden), bf16), shape((n, hidden), bf16), shape((n, hidden // 2), bf16), shape((n, hidden // 2), bf16)]
        outs += [shape((n, width), f32), shape((3, n, PIECE), bf16), shape((1, width), f32), shape((width, n), bf16)]
    args += list(after)
    specs += [LEFT] * len(after)
    return pl.pallas_call(
        functools.partial(back_kernel, start, end, len(after)),
        out_shape=tuple(outs),
        in_specs=specs,
        out_specs=(WHOLE,) * len(outs),
        scratch_shapes=scratch,
        cost_estimate=BRIEF,
        compiler_params=pltpu.CompilerParams(vmem_limit_bytes=LIMIT),
        name="back_end" if end else ("back_start" if start else "back_join"),
    )(*args)


def by_turn(core, chip):
    one = 1 + core
    return chip ^ one, chip ^ 3, chip, chip ^ (3 - one)


def turned(dst, blocks):
    n = blocks[0].shape[0]
    for i, block in enumerate(blocks):
        dst[:, i * n : (i + 1) * n] = block[...].T


def grad_ffn_kernel(sc, *rest):
    lefts, rights = rest[:4], rest[4:8]
    send_ref, keep_ref, left, right = rest[-4:]
    core, chip = sc[0], sc[1]
    n, cols = rights[0].shape[0], right.shape[1]
    turned(left, lefts)
    for i, m in enumerate(by_turn(core, chip)):
        at = pl.multiple_of(m * cols, 128)
        for j, block in enumerate(rights):
            right[j * n : (j + 1) * n, :] = block[:, pl.ds(at, cols)]
        out = send_ref if i < 2 else keep_ref
        out[i % 2] = nn(left[...], right[...]).astype(bf16)


def grad_ffn(sc, lefts, rights):
    n, width = lefts[0].shape
    cols = rights[0].shape[1] // 4
    out = shape((2, width, cols), bf16)
    return pl.pallas_call(
        grad_ffn_kernel,
        out_shape=(out, out),
        in_specs=[SCALARS] + [WHOLE] * 8,
        out_specs=(WHOLE,) * 2,
        scratch_shapes=[pltpu.VMEM((width, 4 * n), bf16), pltpu.VMEM((4 * n, cols), bf16)],
        cost_estimate=BRIEF,
        compiler_params=pltpu.CompilerParams(vmem_limit_bytes=36 << 20),
        name="grad_ffn",
    )(sc, *lefts, *rights)


def grad_down_kernel(sc, *rest):
    lefts, rights = rest[:4], rest[4:8]
    outs, left, right = rest[-4:-2], rest[-2], rest[-1]
    n, cols = rights[0].shape[0], right.shape[1]
    turned(left, lefts)
    for i, out in enumerate(outs):
        at = pl.multiple_of(((sc[2] + i) & 1) * cols, 128)
        for j, block in enumerate(rights):
            right[j * n : (j + 1) * n, :] = block[:, pl.ds(at, cols)]
        out[...] = nn(left[...], right[...]).astype(bf16)


def grad_down(sc, lefts, rights, after):
    n, width = lefts[0].shape
    cols = rights[0].shape[1] // 2
    return pl.pallas_call(
        grad_down_kernel,
        out_shape=(shape((width, cols), bf16),) * 2,
        in_specs=[SCALARS] + [WHOLE] * 8 + [LEFT] * len(after),
        out_specs=(WHOLE,) * 2,
        scratch_shapes=[pltpu.VMEM((width, 4 * n), bf16), pltpu.VMEM((4 * n, cols), bf16)],
        cost_estimate=BRIEF,
        compiler_params=pltpu.CompilerParams(vmem_limit_bytes=32 << 20),
        name="grad_down",
    )(sc, *lefts, *rights, *after)


def grad_attention_kernel(sc, *rest):
    a_refs, o_refs, rest = rest[:4], rest[4:8], rest[8:]
    queries, keys, values, outs, threes, ones = (rest[i : i + 2] for i in range(0, 12, 2))
    gain_a, gain_f = (rest[i : i + 2] for i in (12, 14))
    send_ref, keep_ref, left, right = rest[-4:]
    core, chip = sc[0], sc[1]
    n, width = a_refs[0].shape
    turned(left.at[0], a_refs)
    gains = [g[0][...] + g[1][...] for g in (gain_a, gain_f)]
    gains = jnp.concatenate([*gains, jnp.zeros((6, width), f32)], axis=0).T
    gains = jnp.concatenate([gains, jnp.zeros((width, PIECE - KVW - 8), f32)], axis=1).astype(bf16)

    def fill(at, of_three, own_three, own_one, single):
        for j in range(2):
            for i in range(3):
                right[of_three + i, j * n : (j + 1) * n, :] = own_three[j][i]
                right[of_three + i, (j + 2) * n : (j + 3) * n, :] = threes[j][i]
            right[single, j * n : (j + 1) * n, :] = own_one[j][...]
            right[single, (j + 2) * n : (j + 3) * n, :] = ones[j][...]

    @pl.when(core == 0)
    def _():
        fill(0, 0, queries, keys, 3)

    @pl.when(core == 1)
    def _():
        turned(left.at[1], o_refs)
        fill(0, 1, outs, values, 0)

    for i, m in enumerate(by_turn(core, chip)):
        out = send_ref if i < 2 else keep_ref
        which = jnp.where(m > 0, core, 0)
        out[i % 2] = nn(left[which], right[m]).astype(bf16)
        out[i % 2, :, KVW:] = gains


def grad_attention(sc, a, o, own, got, gains, after):
    n, width = a[0].shape
    out = shape((2, width, PIECE), bf16)
    return pl.pallas_call(
        grad_attention_kernel,
        out_shape=(out, out),
        in_specs=[SCALARS] + [WHOLE] * 24 + [LEFT] * len(after),
        out_specs=(WHOLE,) * 2,
        scratch_shapes=[pltpu.VMEM((2, width, 4 * n), bf16), pltpu.VMEM((4, 4 * n, PIECE), bf16)],
        cost_estimate=BRIEF,
        compiler_params=pltpu.CompilerParams(vmem_limit_bytes=36 << 20),
        name="grad_attention",
    )(sc, *a, *o, *own, *got, *gains, *after)


def lay_kernel(count, sc, *rest):
    mine, other, outs, kept = rest[:4], rest[4:8], rest[-1 - count : -1], rest[-1]
    core, chip = sc[0], sc[1]
    for kind, pieces in ((core, mine), (1 - core, other)):
        for who, piece in zip(whose(kind), pieces):
            kept[kind, chip ^ who] = piece[...]
    n = sum(o.shape[1] for o in outs[: 4 if len(outs) > 2 else 2]) // 8
    cols = [jnp.concatenate([kept[c, m, :, :n].astype(f32) for m in range(4)], axis=1) for c in range(2)]
    if len(outs) == 2:
        outs[0][...] = cols[0]
        outs[1][...] = cols[1]
    else:
        outs[0][...] = cols[0][:, : 3 * n]
        outs[1][...] = cols[0][:, 3 * n :]
        outs[2][...] = cols[1][:, :n]
        outs[3][...] = cols[1][:, n:]
        gains = kept[0, 0, :, n : n + 8].astype(f32) + kept[1, 0, :, n : n + 8].astype(f32)
        outs[4][...] = gains.T[:2]


def lay(sc, mine, other, widths, after):
    rows, n = mine[0].shape
    outs = tuple(shape((rows, w), f32) for w in widths)
    if len(widths) > 2:
        outs += (shape((2, rows), f32),)
    return pl.pallas_call(
        functools.partial(lay_kernel, len(outs)),
        out_shape=outs,
        in_specs=[SCALARS] + [WHOLE] * 8 + [LEFT] * len(after),
        out_specs=(WHOLE,) * len(outs),
        scratch_shapes=[pltpu.VMEM((2, 4, rows, n), bf16)],
        cost_estimate=BRIEF,
        compiler_params=pltpu.CompilerParams(vmem_limit_bytes=24 << 20),
        name="lay",
    )(sc, *mine, *other, *after)


def pick_first_kernel(sc, q_ref, k_ref, v_ref, o_ref, gain_ref, out_ref):
    rows = out_ref.shape[0]
    which = sc[0] * 4 + sc[1]
    pad = jnp.zeros((6, rows), f32)
    gains = jnp.concatenate([gain_ref[...], pad], axis=0).T.astype(bf16)
    rest = jnp.zeros((rows, PIECE - KVW - 8), bf16)
    for at in range(8):

        @pl.when(which == at)
        def _():
            if at in (3, 4):
                piece = (k_ref if at == 3 else v_ref)[...].T
            else:
                source, m = (q_ref, at) if at < 3 else (o_ref, at - 5)
                piece = source[:, m * KVW : (m + 1) * KVW]
            out_ref[...] = jnp.concatenate([piece, gains, rest], axis=1)


def pick_first(sc, query, key, value, out, gains):
    return pl.pallas_call(
        pick_first_kernel,
        out_shape=shape((query.shape[0], PIECE), bf16),
        in_specs=[SCALARS] + [WHOLE] * 5,
        out_specs=WHOLE,
        cost_estimate=BRIEF,
        compiler_params=pltpu.CompilerParams(vmem_limit_bytes=16 << 20),
        name="pick_first",
    )(sc, query, key, value, out, gains)


def pick_kernel(sc, gate, up, *rest):
    out_ref, sem = rest[-2:]
    cols = out_ref.shape[1]
    at = pl.ds(pl.multiple_of(sc[1] * cols, 128), cols)
    for c, source in ((0, gate), (1, up)):

        @pl.when(sc[0] == c)
        def _():
            pltpu.make_async_copy(source.at[:, at], out_ref, sem).start()

    pltpu.make_async_copy(gate.at[:, at], out_ref, sem).wait()


def pick(sc, gate, up, after):
    return pl.pallas_call(
        pick_kernel,
        out_shape=shape((gate.shape[0], gate.shape[1] // 4), bf16),
        in_specs=[SCALARS] + [LEFT] * (2 + len(after)),
        out_specs=WHOLE,
        scratch_shapes=[pltpu.SemaphoreType.DMA],
        cost_estimate=BRIEF,
        compiler_params=pltpu.CompilerParams(vmem_limit_bytes=16 << 20),
        name="pick",
    )(sc, gate, up, *after)


def pick_down_kernel(sc, down, *rest):
    far_ref, near_ref, sems = rest[-3:]
    half, n = far_ref.shape[0], near_ref.shape[0]
    copies = []
    for i, (out, row) in enumerate(((far_ref, sc[0] * half), (near_ref, 2 * half + (sc[0] * 4 + sc[1]) * n))):
        rows = pl.ds(pl.multiple_of(row, 16), out.shape[0])
        copies.append(pltpu.make_async_copy(down.at[rows, :], out, sems.at[i]))
    for copy in copies:
        copy.start()
    for copy in copies:
        copy.wait()


def pick_down(sc, down, after):
    rows, cols = down.shape
    n = rows // 240 * 16
    return pl.pallas_call(
        pick_down_kernel,
        out_shape=(shape((rows // 2 - 4 * n, cols), bf16), shape((n, cols), bf16)),
        in_specs=[SCALARS] + [LEFT] * (1 + len(after)),
        out_specs=(WHOLE, WHOLE),
        scratch_shapes=[pltpu.SemaphoreType.DMA((2,))],
        cost_estimate=BRIEF,
        compiler_params=pltpu.CompilerParams(vmem_limit_bytes=16 << 20),
        name="pick_down",
    )(sc, down, *after)


def gains_kernel(first_ref, out_ref):
    for j in range(4):
        n = first_ref.shape[1]
        out_ref[:, j * n : (j + 1) * n] = first_ref[j, :, KVW : KVW + 8].astype(f32).T[:2]


def gains_of(first):
    return pl.pallas_call(
        gains_kernel,
        out_shape=shape((2, 4 * first.shape[1]), f32),
        in_specs=[WHOLE],
        out_specs=WHOLE,
        cost_estimate=BRIEF,
        compiler_params=pltpu.CompilerParams(vmem_limit_bytes=16 << 20),
        name="gains",
    )(first)


def stack_kernel(sc, *rest):
    parts, out_ref, sems = rest[:4], rest[-2], rest[-1]
    copies = [pltpu.make_async_copy(p, out_ref.at[(sc[2] - s) & 3], sems.at[s]) for s, p in enumerate(parts)]
    for copy in copies:
        copy.start()
    for copy in copies:
        copy.wait()


def stack(sc, parts, after=()):
    return pl.pallas_call(
        stack_kernel,
        out_shape=shape((4,) + parts[0].shape, parts[0].dtype),
        in_specs=[SCALARS] + [LEFT] * (4 + len(after)),
        out_specs=WHOLE,
        scratch_shapes=[pltpu.SemaphoreType.DMA((4,))],
        cost_estimate=BRIEF,
        compiler_params=pltpu.CompilerParams(vmem_limit_bytes=16 << 20),
        name="stack",
    )(sc, *parts, *after)


def small(kernel, sc, args, outs, scratch, after, name):
    return pl.pallas_call(
        kernel,
        out_shape=tuple(outs),
        in_specs=[SCALARS] + [WHOLE] * len(args) + [LEFT] * len(after),
        out_specs=(WHOLE,) * len(outs),
        scratch_shapes=scratch,
        cost_estimate=BRIEF,
        compiler_params=pltpu.CompilerParams(vmem_limit_bytes=32 << 20),
        name=name,
    )(sc, *args, *after)


def sum_first(sc, keep, got, after):
    def kernel(sc, keep_ref, got_ref, *rest):
        later_ref, own_ref = rest[-2:]
        later_ref[...] = (keep_ref[1].astype(f32) + got_ref[1].astype(f32)).astype(bf16)
        own_ref[...] = keep_ref[0].astype(f32) + got_ref[0].astype(f32)

    block = keep.shape[1:]
    return small(kernel, sc, [keep, got], [shape(block, bf16), shape(block, f32)], [], after, "sum_first")


def sum_second(sc, own, got, after):
    def kernel(sc, own_ref, got_ref, *rest):
        outs, total = rest[-5:-1], rest[-1]
        n = total.shape[1]
        for j in range(4):
            rows = slice(j * n, (j + 1) * n)
            total[j] = own_ref[rows, :] + got_ref[rows, :].astype(f32)
        for s, out in enumerate(outs):
            out[...] = total[(sc[2] + s) & 3].astype(out.dtype)

    rows, cols = own.shape
    part = (rows // 4, cols)
    outs = [shape(part, f32)] + [shape(part, bf16)] * 3
    return small(kernel, sc, [own, got], outs, [pltpu.VMEM((4,) + part, f32)], after, "sum_second")


def sum_ring(sc, own, got, after):
    def kernel(sc, own_ref, *rest):
        out_ref = rest[-1]
        out_ref[...] = (own_ref[...] + sum(g[...].astype(f32) for g in rest[:3])).astype(bf16)

    return small(kernel, sc, [own, *got], [shape(own.shape, bf16)], [], after, "sum_ring")[0]


def down_ring(sc, own, got, after):
    def kernel(sc, own_ref, *rest):
        give_ref, keep_ref, total = rest[-3:]
        half = give_ref.shape[0]
        total[...] = own_ref[...].astype(f32) + sum(g[...].astype(f32) for g in rest[:3])
        give_ref[...] = total[pl.ds(pl.multiple_of((1 - sc[0]) * half, half), half), :].astype(bf16)
        keep_ref[...] = total[pl.ds(pl.multiple_of(sc[0] * half, half), half), :].astype(bf16)

    rows, cols = own.shape
    half = shape((rows // 2, cols), bf16)
    return small(kernel, sc, [own, *got], [half, half], [pltpu.VMEM((rows, cols), f32)], after, "down_ring")


def down_split(sc, keep, given, after):
    def kernel(sc, keep_ref, given_ref, *rest):
        send_ref, kept_ref, total = rest[-3:]
        n = total.shape[1]
        owner = (sc[2] >> 1) == sc[0]
        for m in range(4):
            rows = slice(m * n, (m + 1) * n)
            total[m] = jnp.where(owner, keep_ref[rows, :].astype(f32), given_ref[rows, :].astype(f32))
        for i, m in enumerate(by_turn(sc[0], sc[1])):
            out = send_ref if i < 2 else kept_ref
            out[i % 2] = total[m].astype(bf16)

    rows, cols = keep.shape
    out = shape((2, rows // 4, cols), bf16)
    return small(kernel, sc, [keep, given], [out, out], [pltpu.VMEM((4, rows // 4, cols), f32)], after, "down_split")


def sum_two(sc, own, got, after):
    def kernel(sc, own_ref, got_ref, *rest):
        rest[-1][...] = (own_ref[...] + got_ref[...].astype(f32)).astype(bf16)

    return small(kernel, sc, [own, got], [shape(own.shape, bf16)], [], after, "sum_two")[0]


def lay_down(sc, mine, other, after):
    def kernel(sc, *rest):
        out_ref, total = rest[-2:]
        n = total.shape[2]
        for kind, pieces in ((sc[0], rest[:4]), (1 - sc[0], rest[4:8])):
            for who, piece in zip(whose(kind), pieces):
                total[kind, sc[1] ^ who] = piece[...].astype(f32)
        for c in range(2):
            for m in range(4):
                at = (c * 4 + m) * n
                out_ref[at : at + n, :] = total[c, m]

    n, cols = mine[0].shape
    return small(kernel, sc, [*mine, *other], [shape((8 * n, cols), f32)], [pltpu.VMEM((2, 4, n, cols), f32)], after, "lay_down")[0]


CORE, SIDE, BACK = 1, 2, 4
rope_base = 10000.0
RUNS = 2


def flip(value, bit, bit1=None):
    count = lax.axis_size("dp")
    bits = (bit, bit if bit1 is None else bit1)
    return lax.ppermute(value, "dp", [(i, i ^ bits[i & 1]) for i in range(count)])


def turn_z(value, step):
    count = lax.axis_size("fsdp")
    return lax.ppermute(value, "fsdp", [(i, (i + step) % count) for i in range(count)])


def home_to_work(value, back=False):
    count, depth = lax.axis_size("dp"), lax.axis_size("fsdp")
    pairs = []
    for d in range(count):
        for z in range(depth):
            there = (d & ~1) | (z & 1), 2 * (d & 1) + (z >> 1)
            pair = (d * depth + z, there[0] * depth + there[1])
            pairs.append(pair[::-1] if back else pair)
    return lax.ppermute(value, ("dp", "fsdp"), pairs)


def place():
    d, z = lax.axis_index("dp"), lax.axis_index("fsdp")
    return d & 1, (d >> 1) & 3, z


def turns(shard):
    return [shard] + [turn_z(shard, s) for s in range(1, lax.axis_size("fsdp"))]


def plane_gather(piece):
    first, second = flip(piece, SIDE, BACK), flip(piece, BACK, SIDE)
    mine = (piece, first, second, flip(first, BACK, SIDE))
    return mine, tuple(flip(p, CORE) for p in mine)


def window(own):
    core, _, _ = place()
    depth = lax.axis_size("fsdp")
    far = lax.ppermute(own, "fsdp", [(z, z + 1) for z in range(0, depth, 2)])
    near = flip(jnp.where(core == 0, own, far), CORE)
    return far, near, own


def unwindow(far, near):
    core, _, _ = place()
    depth = lax.axis_size("fsdp")
    near = flip(near, CORE)
    far = jnp.where(core == 1, far + near.astype(f32), far).astype(bf16)
    return near, lax.ppermute(far, "fsdp", [(z + 1, z) for z in range(0, depth, 2)])


def over_groups(value):
    bit = 8
    while bit < lax.axis_size("dp"):
        value = (value.astype(f32) + flip(value, bit).astype(f32)).astype(bf16)
        bit *= 2
    return value


def spread(piece):
    return piece, flip(piece, SIDE, BACK), flip(piece, BACK, SIDE), flip(piece, SIDE | BACK)


def across(pieces):
    return tuple(flip(p, CORE) for p in pieces)


def to_owners(part, step):
    count, depth = lax.axis_size("dp"), lax.axis_size("fsdp")
    pairs = []
    for d in range(count):
        for a in range(depth):
            b = (a + step) % depth
            if (b >> 1) == (d & 1):
                pairs.append((d * depth + a, d * depth + b))
    return lax.ppermute(part, ("dp", "fsdp"), pairs)


def body(tokens, segment_ids, attn_gain, query_weight, key_weight, value_weight, out_weight, ffn_gain, gate_weight, up_weight, down_weight, cotangent):
    core, chip, z = place()
    sc = jnp.stack([core, chip, z]).astype(jnp.int32)
    _, stretch, width = tokens.shape
    rows, depth = query_weight.shape[0], lax.axis_size("fsdp")
    block = 2 * (z & 1) + core
    positions = (block * stretch + jnp.arange(stretch)).astype(f32)
    freq = rope_base ** (-2.0 * jnp.arange(HEAD_DIM // 2, dtype=f32) / HEAD_DIM)
    angle = freq[:, None] * positions[None, :]
    cos, sin = jnp.cos(angle), jnp.sin(angle)

    gains = jnp.stack([attn_gain, ffn_gain]).astype(f32)
    parts_a = turns(pick_first(sc, query_weight, key_weight.T, value_weight.T, out_weight, gains))
    ids = jnp.broadcast_to((segment_ids[0] + 1).astype(bf16), (IDS, stretch))
    tokens = home_to_work(jnp.concatenate([tokens[0].T, ids]))
    whole_a = stack(sc, parts_a)
    gains = gains_of(whole_a)
    gain_a, gain_f = gains[:1], gains[1:]
    wa = plane_gather(whole_a.reshape(depth * rows, PIECE))
    piece_b = pick(sc, gate_weight, up_weight, [whole_a])
    whole_b = stack(sc, turns(piece_b)).reshape(depth * rows, piece_b.shape[1])
    wb = plane_gather(whole_b)
    far_d, near_d = pick_down(sc, down_weight.T, [whole_b])
    parts_n, parts_f = turns(near_d), turns(far_d)

    h_0, a0, q0, own = pre(sc, tokens, gain_a, cos, sin, *wa, [whole_b])
    kv0 = window(own)
    near_d = plane_gather(stack(sc, parts_n, [q0]))
    o0, lse0 = attend(q0, kv0)
    far_d = stack(sc, parts_f, [o0])
    weights = wa, wb, (far_d, flip(far_d, CORE), *near_d[0], *near_d[1])
    cot = home_to_work(cotangent[0].T)
    mixed0, h1_0, b0, gate0, up0, z0, h_1, a1, q1, own = post(False, sc, o0, h_0, gain_f, gain_a, cos, sin, own, *weights)
    kv1 = window(own)
    o1, lse1 = attend(q1, kv1)
    mixed1, h1_1, b1, gate1, up1, z1, output = post(True, sc, o1, h_1, gain_f, gain_a, cos, sin, own, *weights)
    output = home_to_work(output, back=True).T

    gb1, act1, away1, zk1, zs1, g1, p1, dgain_f1, do = back(True, False, sc, weights, [cot], [gate1, up1, h1_1, gain_f, z1])
    dq1, three1, far, near, own = attend_back(sc, p1, q1, kv1, lse1, do, cos, sin)
    near, far = unwindow(far, near)
    tail = [g1, dq1, own, near, far, h_1, gain_a, cos, sin]
    dk1, dv1, one1, dgain_a1, gb0, act0, away0, zk0, zs0, g1, p0, dgain_f0, do = back(False, False, sc, weights, tail, [gate0, up0, h1_0, gain_f, z0])

    def pair(*own):
        return [*own, *across(own)]

    send_b, keep_b = grad_ffn(sc, pair(b1, b0), [act1, act0, *across((away1, away0))])
    got_b = flip(send_b, SIDE, BACK)
    like_d, unlike_d = grad_down(sc, pair(gb1, gb0), [zk1, zk0, *across((zs1, zs0))], [send_b])
    got_d = [to_owners(unlike_d, 1), to_owners(like_d, 2), to_owners(unlike_d, 3)]
    owner = (z >> 1) == core
    own_d = jnp.where(owner, like_d, jnp.zeros_like(like_d))

    dq0, three0, far, near, own = attend_back(sc, p0, q0, kv0, lse0, do, cos, sin, [like_d])
    near, far = unwindow(far, near)
    later_b, own_b = sum_first(sc, keep_b, got_b, [own])
    more_b = flip(later_b, BACK, SIDE)
    tail = [g1, dq0, own, near, far, h_0, gain_a, cos, sin]
    dk0, dv0, one0, dgain_a0, grad_tokens = back(False, True, sc, weights, tail, None, [later_b])
    grad_tokens = home_to_work(grad_tokens, back=True).astype(f32).T

    own = [dq1, dq0, dk1, dk0, dv1, dv0, p1, p0]
    send_a, keep_a = grad_attention(sc, pair(a1, a0), pair(mixed1, mixed0), own, across((three1, three0, one1, one0)), [dgain_a1, dgain_a0, dgain_f1, dgain_f0], [])
    got_a = flip(send_a, SIDE, BACK)
    ring_b = sum_second(sc, own_b, more_b, [send_a])
    ring_b, parts_b = ring_b[0], [turn_z(v, s + 1) for s, v in enumerate(ring_b[1:])]
    later_a, own_a = sum_first(sc, keep_a, got_a, [ring_b])
    more_a = flip(later_a, BACK, SIDE)
    give, keep = down_ring(sc, own_d, got_d, [later_a])
    send_d, keep_d = down_split(sc, keep, flip(give, CORE), [])
    got_d = flip(send_d, SIDE, BACK)
    ring_a = sum_second(sc, own_a, more_a, [send_d])
    ring_a, parts_a = ring_a[0], [turn_z(v, s + 1) for s, v in enumerate(ring_a[1:])]
    later_d, own_d = sum_first(sc, keep_d, got_d, [ring_a])
    more_d = flip(later_d, BACK, SIDE)
    piece_b = over_groups(sum_ring(sc, ring_b, parts_b, [later_d]))
    all_b = spread(piece_b)
    piece_d = over_groups(sum_two(sc, own_d, more_d, [piece_b]))
    all_d = spread(piece_d)
    piece_a = over_groups(sum_ring(sc, ring_a, parts_a, [piece_d]))
    all_a = spread(piece_a)
    grad_gate, grad_up = lay(sc, all_b, across(all_b), (gate_weight.shape[1],) * 2, [piece_a])
    grad_down_ = lay_down(sc, all_d, across(all_d), [grad_gate])
    grad_query, grad_key, grad_value, grad_out, dgains = lay(sc, all_a, across(all_a), (width, KVW, KVW, width), [grad_down_])
    return (output[None], grad_tokens[None], dgains[0], grad_query, grad_key, grad_value, grad_out, dgains[1], grad_gate, grad_up, grad_down_.T)


def solution(mesh):
    wide, rows, shard = P("dp", "fsdp", None), P("dp", "fsdp"), P("fsdp", None)
    in_specs = (wide, rows, P("fsdp"), shard, shard, shard, shard, P("fsdp"), shard, shard, shard, wide)
    out_specs = (wide, wide, P("fsdp"), shard, shard, shard, shard, P("fsdp"), shard, shard, shard)
    return jax.shard_map(body, mesh=mesh, in_specs=in_specs, out_specs=out_specs, check_vma=False)
```

```python
import functools
import jax
import jax.numpy as jnp
from jax import lax
from jax.sharding import PartitionSpec as P
from jax.experimental import pallas as pl
from jax.experimental.pallas import tpu as pltpu

f32, bf16 = jnp.float32, jnp.bfloat16
eps = 1e-05
HEADS, KV_HEADS, HEAD_DIM, GROUP, KVW = 15, 5, 64, 3, 320
IDS = 16
PIECE = 384
LIMIT = 58 << 20
WHOLE = pl.BlockSpec(memory_space=pltpu.VMEM)
LEFT = pl.BlockSpec(memory_space=pl.ANY)
SCALARS = pl.BlockSpec(memory_space=pltpu.SMEM)
BRIEF = pl.CostEstimate(flops=1024, bytes_accessed=1024, transcendentals=0)


def contract(a, b, i, j):
    return lax.dot_general(a, b, (((i,), (j,)), ((), ())), preferred_element_type=f32)


def nn(a, b):
    return contract(a, b, 1, 0)


def nt(a, b):
    return contract(a, b, 1, 1)


def tn(a, b):
    return contract(a, b, 0, 0)


def whose(core):
    return 0, 1 + core, 2 - core, 3


def fetch(mine, other, kept, sems, core, chip):
    for kind, pieces in ((core, mine), (1 - core, other)):
        for who, piece in zip(whose(kind), pieces):
            at = chip ^ who
            pltpu.make_async_copy(piece, kept.at[kind, at], sems.at[kind, at]).start()


def arrived(kept, sems, *at):
    pltpu.make_async_copy(kept.at[at], kept.at[at], sems.at[at]).wait()


def normed(x, gain):
    return x * lax.rsqrt(jnp.mean(x * x, axis=-1, keepdims=True) + eps) * gain


def norm_back(x, gain, grad):
    r = lax.rsqrt(jnp.mean(x * x, axis=-1, keepdims=True) + eps)
    hat = x * r
    scaled = grad * gain
    dx = r * (scaled - hat * jnp.mean(scaled * hat, axis=-1, keepdims=True))
    return dx, jnp.sum(grad * hat, axis=0, keepdims=True)


def widened(x):
    return jnp.concatenate([x, jnp.zeros((x.shape[0], PIECE - x.shape[1]), x.dtype)], axis=1)


def rope(u, cos, sin, back):
    heads = u.shape[0] // HEAD_DIM
    half = HEAD_DIM // 2
    out = []
    for h in range(heads):
        u1, u2 = u[h * HEAD_DIM : h * HEAD_DIM + half], u[h * HEAD_DIM + half : (h + 1) * HEAD_DIM]
        if back:
            out += [u1 * cos + u2 * sin, u2 * cos - u1 * sin]
        else:
            out += [u1 * cos - u2 * sin, u2 * cos + u1 * sin]
    return jnp.concatenate(out, axis=0)


def project(state, gain_ref, cos_ref, sin_ref, ids, kept, sems, a_ref, q_ref, kv_ref):
    a = normed(state, gain_ref[...]).astype(bf16)
    a_ref[...] = a
    cos, sin = cos_ref[...], sin_ref[...]
    arrived(kept, sems, 0, 3)
    kv_ref[:KVW, :] = rope(nn(a, kept[0, 3, :, :KVW]).T, cos, sin, False).astype(bf16)
    arrived(kept, sems, 1, 0)
    kv_ref[2 * KVW :, :] = ids
    kv_ref[KVW : 2 * KVW, :] = nn(a, kept[1, 0, :, :KVW]).T.astype(bf16)
    for m in range(3):
        arrived(kept, sems, 0, m)
        q_ref[pl.ds(m * KVW, KVW), :] = rope(nn(a, kept[0, m, :, :KVW]).T, cos, sin, False).astype(bf16)


def pre_kernel(sc, ht_ref, gain_ref, cos_ref, sin_ref, *rest):
    width = ht_ref.shape[0] - IDS
    mine, other = rest[:4], rest[4:8]
    h_ref, a_ref, q_ref, kv_ref, kept, sems = rest[-6:]
    core, chip = sc[0], sc[1]
    fetch(mine, other, kept, sems, core, chip)
    h = ht_ref[:width, :].T
    h_ref[...] = h
    project(h.astype(f32), gain_ref, cos_ref, sin_ref, ht_ref[width:, :], kept, sems, a_ref, q_ref, kv_ref)
    for m in range(1, 4):
        arrived(kept, sems, 1, m)


def scratch_a(width):
    return [pltpu.VMEM((2, 4, width, PIECE), bf16), pltpu.SemaphoreType.DMA((2, 4))]


def shape(s, d):
    return jax.ShapeDtypeStruct(s, d)


def pre(sc, ht, gain, cos, sin, mine_a, other_a, after):
    width, n = ht.shape[0] - IDS, ht.shape[1]
    return pl.pallas_call(
        pre_kernel,
        out_shape=(shape((n, width), bf16), shape((n, width), bf16), shape((width, n), bf16), shape((2 * KVW + IDS, n), bf16)),
        in_specs=[SCALARS] + [WHOLE] * 4 + [LEFT] * (8 + len(after)),
        out_specs=(WHOLE,) * 4,
        scratch_shapes=scratch_a(width),
        cost_estimate=BRIEF,
        compiler_params=pltpu.CompilerParams(vmem_limit_bytes=LIMIT),
        name="pre",
    )(sc, ht, gain, cos, sin, *mine_a, *other_a, *after)


def bias_of(kv):
    keys, n = kv.shape[1], kv.shape[1] // 3
    ids = kv[2 * KVW :, :].astype(f32)
    seg_k, seg_q = ids.T[:, :1], ids[:1, 2 * n :]
    j = lax.broadcasted_iota(jnp.int32, (keys, n), 0)
    i = lax.broadcasted_iota(jnp.int32, (keys, n), 1) + (keys - n)
    return jnp.where((seg_k == seg_q) & (j <= i), 0.0, -1e30).astype(f32)


def window_of(parts, whole):
    n = parts[0].shape[1]
    for w, part in enumerate(parts):
        whole[:, w * n : (w + 1) * n] = part[...]


def attend_kernel(q_ref, kv0, kv1, kv2, *rest):
    o_ref, lse_ref, bias, kv = rest[-4:]
    window_of((kv0, kv1, kv2), kv)
    bias[...] = bias_of(kv)

    def head(e, _):
        row = pl.multiple_of(e * HEAD_DIM, HEAD_DIM)
        k = kv[pl.ds(row, HEAD_DIM), :]
        v = kv[pl.ds(row + KVW, HEAD_DIM), :]
        for g in range(GROUP):
            at = pl.multiple_of((e * GROUP + g) * HEAD_DIM, HEAD_DIM)
            q = q_ref[pl.ds(at, HEAD_DIM), :]
            s = tn(k, q) * HEAD_DIM ** (-0.5) + bias[...]
            top = jnp.max(s, axis=0, keepdims=True)
            expo = jnp.exp(s - top)
            total = jnp.sum(expo, axis=0, keepdims=True)
            probs = (expo * (1.0 / total)).astype(bf16)
            o_ref[pl.ds(at, HEAD_DIM), :] = nn(v, probs).astype(bf16)
            lse_ref[pl.ds(e * GROUP + g, 1), :] = top + jnp.log(total)
        return 0

    lax.fori_loop(0, KV_HEADS, head, 0)


def attend(q, kvs, after=()):
    width, n = q.shape
    return pl.pallas_call(
        attend_kernel,
        out_shape=(shape((width, n), bf16), shape((HEADS, n), f32)),
        in_specs=[WHOLE] * 4 + [LEFT] * len(after),
        out_specs=(WHOLE,) * 2,
        scratch_shapes=[pltpu.VMEM((3 * n, n), f32), pltpu.VMEM((2 * KVW + IDS, 3 * n), bf16)],
        cost_estimate=BRIEF,
        compiler_params=pltpu.CompilerParams(vmem_limit_bytes=24 << 20),
        name="attend",
    )(q, *kvs, *after)


def attend_back_kernel(sc, p_ref, q_ref, kv0, kv1, kv2, lse_ref, do_ref, cos_ref, sin_ref, *rest):
    dq_ref, three_ref, far_ref, near_ref, own_ref, bias, kv, dqs = rest[-8:]
    n = q_ref.shape[1]
    window_of((kv0, kv1, kv2), kv)
    bias[...] = bias_of(kv)
    scale = HEAD_DIM ** (-0.5)

    def head(e, _):
        row = pl.multiple_of(e * HEAD_DIM, HEAD_DIM)
        k = kv[pl.ds(row, HEAD_DIM), :]
        v = kv[pl.ds(row + KVW, HEAD_DIM), :]
        dk = dv = None
        for g in range(GROUP):
            at = pl.multiple_of((e * GROUP + g) * HEAD_DIM, HEAD_DIM)
            q = q_ref[pl.ds(at, HEAD_DIM), :]
            do = do_ref[pl.ds(at, HEAD_DIM), :]
            s = tn(k, q) * scale + bias[...]
            probs = jnp.exp(s - lse_ref[pl.ds(e * GROUP + g, 1), :])
            dp = tn(v, do)
            inner = jnp.sum(probs * dp, axis=0, keepdims=True)
            ds = (probs * (dp - inner)).astype(bf16)
            dvg, dkg = nt(do, probs.astype(bf16)), nt(q, ds)
            dv, dk = (dvg, dkg) if g == 0 else (dv + dvg, dk + dkg)
            dqs[pl.ds(at, HEAD_DIM), :] = nn(k, ds)
        for at, grad in ((row, dk * scale), (row + KVW, dv)):
            far_ref[pl.ds(at, HEAD_DIM), :] = grad[:, :n]
            near_ref[pl.ds(at, HEAD_DIM), :] = grad[:, n : 2 * n].astype(bf16)
            own_ref[pl.ds(at, HEAD_DIM), :] = grad[:, 2 * n :]
        return 0

    lax.fori_loop(0, KV_HEADS, head, 0)
    cos, sin = cos_ref[...] * scale, sin_ref[...] * scale
    for m in range(3):
        dq = widened(rope(dqs[m * KVW : (m + 1) * KVW, :], cos, sin, True).T.astype(bf16))
        dq_ref[m] = dq
        three_ref[m] = jnp.where(sc[0] == 0, p_ref[m], dq)


def attend_back(sc, p, q, kvs, lse, do, cos, sin, after=()):
    width, n = q.shape
    block = (2 * KVW, n)
    return pl.pallas_call(
        attend_back_kernel,
        out_shape=(shape((3, n, PIECE), bf16), shape((3, n, PIECE), bf16), shape(block, f32), shape(block, bf16), shape(block, f32)),
        in_specs=[SCALARS] + [WHOLE] * 9 + [LEFT] * len(after),
        out_specs=(WHOLE,) * 5,
        scratch_shapes=[pltpu.VMEM((3 * n, n), f32), pltpu.VMEM((2 * KVW + IDS, 3 * n), bf16), pltpu.VMEM((width, n), f32)],
        cost_estimate=BRIEF,
        compiler_params=pltpu.CompilerParams(vmem_limit_bytes=32 << 20),
        name="attend_back",
    )(sc, p, q, *kvs, lse, do, cos, sin, *after)


def fetch_ffn(mine_b, other_b, down, wb, wd, sem_b, sem_d, core, chip):
    fetch(mine_b, other_b, wb, sem_b, core, chip)
    half = down[0].shape[1]
    for c, part in ((core, down[0]), (1 - core, down[1])):
        rows = pl.ds(pl.multiple_of(c * half, half), half)
        pltpu.make_async_copy(part, wd.at[:, rows], sem_d).start()


def arrived_down(wd, sem_d):
    pltpu.make_async_copy(wd, wd, sem_d).wait()


def scratch_ffn(width, n):
    return [
        pltpu.VMEM((2, 4, width, n), bf16),
        pltpu.SemaphoreType.DMA((2, 4)),
        pltpu.VMEM((4, width, n), bf16),
        pltpu.SemaphoreType.DMA,
    ]


def post_kernel(last, sc, ot_ref, h_ref, gain_ref, gain_a, cos_ref, sin_ref, *rest):
    mine_a, other_a, mine_b, other_b = rest[:4], rest[4:8], rest[8:12], rest[12:16]
    down, ids_ref = rest[16:18], rest[18]
    o_ref, h1_ref, b_ref, gate_ref, up_ref, z_ref, next_ref = rest[19:26]
    more, rest = rest[26 : 26 + (0 if last else 3)], rest[26 + (0 if last else 3) :]
    wa, sem_a, wb, sem_b, wd, sem_d = rest
    core, chip = sc[0], sc[1]
    fetch(mine_a, other_a, wa, sem_a, core, chip)
    fetch_ffn(mine_b, other_b, down, wb, wd, sem_b, sem_d, core, chip)
    o = ot_ref[...].T
    o_ref[...] = o
    for m in range(1, 4):
        arrived(wa, sem_a, 1, m)
    h1 = h_ref[...].astype(f32) + jnp.concatenate([nn(o, wa[1, m, :, :KVW]) for m in range(1, 4)], axis=1)
    h1_ref[...] = h1
    b = normed(h1, gain_ref[...]).astype(bf16)
    b_ref[...] = b
    n = wb.shape[3]
    total = h1
    for m in range(4):
        cols = slice(m * n, (m + 1) * n)
        arrived(wb, sem_b, 0, m)
        gate = nn(b, wb[0, m])
        arrived(wb, sem_b, 1, m)
        up = nn(b, wb[1, m])
        gate_ref[:, cols] = gate.astype(bf16)
        up_ref[:, cols] = up.astype(bf16)
        z = (gate / (1.0 + jnp.exp(-gate)) * up).astype(bf16)
        z_ref[:, cols] = z
        if m == 0:
            arrived_down(wd, sem_d)
        total = total + nt(z, wd[m])
    next_ref[...] = total.astype(bf16).T if last else total
    if last:
        arrived(wa, sem_a, 1, 0)
        for m in range(4):
            arrived(wa, sem_a, 0, m)
    else:
        project(total, gain_a, cos_ref, sin_ref, ids_ref[2 * KVW :, :], wa, sem_a, *more)


def post(last, sc, ot, h, gain, gain_a, cos, sin, kv, wa, wb, wd):
    width, n = ot.shape
    hidden = wb[0][0].shape[1] * 4
    outs = [shape((n, width), bf16), shape((n, width), f32), shape((n, width), bf16)] + [shape((n, hidden), bf16)] * 3
    outs += [shape((width, n), bf16) if last else shape((n, width), f32)]
    if not last:
        outs += [shape((n, width), bf16), shape((width, n), bf16), shape((2 * KVW + IDS, n), bf16)]
    return pl.pallas_call(
        functools.partial(post_kernel, last),
        out_shape=tuple(outs),
        in_specs=[SCALARS] + [WHOLE] * 6 + [LEFT] * 18 + [WHOLE],
        out_specs=(WHOLE,) * len(outs),
        scratch_shapes=scratch_a(width) + scratch_ffn(width, hidden // 4),
        cost_estimate=BRIEF,
        compiler_params=pltpu.CompilerParams(vmem_limit_bytes=LIMIT),
        name="post",
    )(sc, ot, h, gain, gain_a, cos, sin, *wa[0], *wa[1], *wb[0], *wb[1], *wd, kv)


def ffn_back(state, core, refs, weights):
    gate_ref, up_ref, h1_ref, gain_ref, z_ref, gb_ref, keep_ref, send_ref, zk_ref, zs_ref, g1_ref, p_ref, dgain_ref, do_ref = refs
    wa, sem_a, wb, sem_b, wd, sem_d = weights
    gb = state.astype(bf16)
    gb_ref[...] = gb
    n = wb.shape[3]
    half = 2 * n
    first = core == 0
    low, high = z_ref[:, :half], z_ref[:, half:]
    zk_ref[...] = jnp.where(first, low, high)
    zs_ref[...] = jnp.where(first, high, low)
    arrived_down(wd, sem_d)
    db = None
    for m in range(4):
        cols = slice(m * n, (m + 1) * n)
        dz = nn(gb, wd[m])
        gate, up = gate_ref[:, cols].astype(f32), up_ref[:, cols].astype(f32)
        sig = 1.0 / (1.0 + jnp.exp(-gate))
        dup = (dz * (gate * sig)).astype(bf16)
        dgate = (dz * up * (sig * (1.0 + gate * (1.0 - sig)))).astype(bf16)
        keep_ref[:, cols] = jnp.where(first, dgate, dup)
        send_ref[:, cols] = jnp.where(first, dup, dgate)
        arrived(wb, sem_b, 0, m)
        part = nt(dgate, wb[0, m])
        arrived(wb, sem_b, 1, m)
        part = part + nt(dup, wb[1, m])
        db = part if m == 0 else db + part
    dx, dgain = norm_back(h1_ref[...], gain_ref[...], db)
    dgain_ref[...] = dgain
    g1 = state + dx
    g1_ref[...] = g1
    low = g1.astype(bf16)
    do = None
    for p in range(3):
        part = low[:, p * KVW : (p + 1) * KVW]
        p_ref[p] = widened(part)
        arrived(wa, sem_a, 1, p + 1)
        part = nt(wa[1, p + 1, :, :KVW], part)
        do = part if p == 0 else do + part
    do_ref[...] = do.astype(bf16)


def finish_a(wa, sem_a, *left):
    for at in left:
        arrived(wa, sem_a, *at)


def query_back(dq_ref, wa, sem_a):
    da = None
    for m in range(3):
        arrived(wa, sem_a, 0, m)
        part = nt(dq_ref[m, :, :KVW], wa[0, m, :, :KVW])
        da = part if m == 0 else da + part
    return da


def project_back(da, own_ref, near_ref, far_ref, core, cos_ref, sin_ref, dk_ref, dv_ref, one_ref, h, gain, wa, sem_a):
    cos, sin = cos_ref[...], sin_ref[...]
    grad = own_ref[...] + far_ref[...].astype(f32) + jnp.where(core == 0, near_ref[...].astype(f32), 0.0)
    dk = rope(grad[:KVW], cos, sin, True).T.astype(bf16)
    dv = grad[KVW:].T.astype(bf16)
    dk_ref[...] = widened(dk)
    dv_ref[...] = widened(dv)
    one_ref[...] = widened(jnp.where(core == 0, dv, dk))
    arrived(wa, sem_a, 0, 3)
    arrived(wa, sem_a, 1, 0)
    da = da + nt(dk, wa[0, 3, :, :KVW]) + nt(dv, wa[1, 0, :, :KVW])
    return norm_back(h, gain, da)


def back_kernel(start, end, after, sc, *rest):
    rest = list(rest)

    def take(n):
        out = rest[:n]
        del rest[:n]
        return out

    core, chip = sc[0], sc[1]
    mine_a, other_a = take(4), take(4)
    if not end:
        mine_b, other_b = take(4), take(4)
        down = take(2)
    if start:
        (g_ref,) = take(1)
    else:
        g1_in, dq_ref, own_ref, near_ref, far_ref, h_ref, gain_a, cos_ref, sin_ref = take(9)
    if not end:
        ins = take(5)
    take(after)
    if not start:
        dk_ref, dv_ref, one_ref, dgain_a = take(4)
    if end:
        (g_out,) = take(1)
    else:
        outs = take(9)
    wa, sem_a = take(2)
    fetch(mine_a, other_a, wa, sem_a, core, chip)
    if not end:
        wb, sem_b, wd, sem_d = take(4)
        fetch_ffn(mine_b, other_b, down, wb, wd, sem_b, sem_d, core, chip)
    if start:
        state = g_ref[...].T.astype(f32)
    else:
        da = query_back(dq_ref, wa, sem_a)
        dx, dgain = project_back(da, own_ref, near_ref, far_ref, core, cos_ref, sin_ref, dk_ref, dv_ref, one_ref, h_ref[...].astype(f32), gain_a[...], wa, sem_a)
        dgain_a[...] = dgain
        state = g1_in[...] + dx
    if end:
        g_out[...] = state.astype(bf16).T
        finish_a(wa, sem_a, (1, 1), (1, 2), (1, 3))
    else:
        ffn_back(state, core, (*ins, *outs), (wa, sem_a, wb, sem_b, wd, sem_d))
        if start:
            finish_a(wa, sem_a, (1, 0), (0, 0), (0, 1), (0, 2), (0, 3))


def back(start, end, sc, weights, tail, ffn, after=()):
    wa, wb, wd = weights
    width = wa[0][0].shape[0]
    args = [sc, *wa[0], *wa[1]]
    specs = [SCALARS] + [LEFT] * 8
    scratch = scratch_a(width)
    if not end:
        args += [*wb[0], *wb[1], *wd]
        specs += [LEFT] * 10
        scratch += scratch_ffn(width, wb[0][0].shape[1])
    args += list(tail)
    specs += [WHOLE] * len(tail)
    n = tail[0].shape[1 if start else 0]
    outs = []
    if not end:
        args += list(ffn)
        specs += [WHOLE] * len(ffn)
    if not start:
        outs += [shape((n, PIECE), bf16)] * 3 + [shape((1, width), f32)]
    if end:
        outs += [shape((width, n), bf16)]
    else:
        hidden = ffn[0].shape[1]
        outs += [shape((n, width), bf16), shape((n, hidden), bf16), shape((n, hidden), bf16), shape((n, hidden // 2), bf16), shape((n, hidden // 2), bf16)]
        outs += [shape((n, width), f32), shape((3, n, PIECE), bf16), shape((1, width), f32), shape((width, n), bf16)]
    args += list(after)
    specs += [LEFT] * len(after)
    return pl.pallas_call(
        functools.partial(back_kernel, start, end, len(after)),
        out_shape=tuple(outs),
        in_specs=specs,
        out_specs=(WHOLE,) * len(outs),
        scratch_shapes=scratch,
        cost_estimate=BRIEF,
        compiler_params=pltpu.CompilerParams(vmem_limit_bytes=LIMIT),
        name="back_end" if end else ("back_start" if start else "back_join"),
    )(*args)


def by_turn(core, chip):
    one = 1 + core
    return chip ^ one, chip ^ 3, chip, chip ^ (3 - one)


def turned(dst, blocks):
    n = blocks[0].shape[0]
    for i, block in enumerate(blocks):
        dst[:, i * n : (i + 1) * n] = block[...].T


def grad_ffn_kernel(sc, *rest):
    lefts, rights = rest[:4], rest[4:8]
    send_ref, keep_ref, left, right = rest[-4:]
    core, chip = sc[0], sc[1]
    n, cols = rights[0].shape[0], right.shape[1]
    turned(left, lefts)
    for i, m in enumerate(by_turn(core, chip)):
        at = pl.multiple_of(m * cols, 128)
        for j, block in enumerate(rights):
            right[j * n : (j + 1) * n, :] = block[:, pl.ds(at, cols)]
        out = send_ref if i < 2 else keep_ref
        out[i % 2] = nn(left[...], right[...]).astype(bf16)


def grad_ffn(sc, lefts, rights):
    n, width = lefts[0].shape
    cols = rights[0].shape[1] // 4
    out = shape((2, width, cols), bf16)
    return pl.pallas_call(
        grad_ffn_kernel,
        out_shape=(out, out),
        in_specs=[SCALARS] + [WHOLE] * 8,
        out_specs=(WHOLE,) * 2,
        scratch_shapes=[pltpu.VMEM((width, 4 * n), bf16), pltpu.VMEM((4 * n, cols), bf16)],
        cost_estimate=BRIEF,
        compiler_params=pltpu.CompilerParams(vmem_limit_bytes=36 << 20),
        name="grad_ffn",
    )(sc, *lefts, *rights)


def grad_down_kernel(sc, *rest):
    lefts, rights = rest[:4], rest[4:8]
    outs, left, right = rest[-4:-2], rest[-2], rest[-1]
    n, cols = rights[0].shape[0], right.shape[1]
    turned(left, lefts)
    for i, out in enumerate(outs):
        at = pl.multiple_of(((sc[2] + i) & 1) * cols, 128)
        for j, block in enumerate(rights):
            right[j * n : (j + 1) * n, :] = block[:, pl.ds(at, cols)]
        out[...] = nn(left[...], right[...]).astype(bf16)


def grad_down(sc, lefts, rights, after):
    n, width = lefts[0].shape
    cols = rights[0].shape[1] // 2
    return pl.pallas_call(
        grad_down_kernel,
        out_shape=(shape((width, cols), bf16),) * 2,
        in_specs=[SCALARS] + [WHOLE] * 8 + [LEFT] * len(after),
        out_specs=(WHOLE,) * 2,
        scratch_shapes=[pltpu.VMEM((width, 4 * n), bf16), pltpu.VMEM((4 * n, cols), bf16)],
        cost_estimate=BRIEF,
        compiler_params=pltpu.CompilerParams(vmem_limit_bytes=32 << 20),
        name="grad_down",
    )(sc, *lefts, *rights, *after)


def grad_attention_kernel(sc, *rest):
    a_refs, o_refs, rest = rest[:4], rest[4:8], rest[8:]
    queries, keys, values, outs, threes, ones = (rest[i : i + 2] for i in range(0, 12, 2))
    gain_a, gain_f = (rest[i : i + 2] for i in (12, 14))
    send_ref, keep_ref, left, right = rest[-4:]
    core, chip = sc[0], sc[1]
    n, width = a_refs[0].shape
    turned(left.at[0], a_refs)
    gains = [g[0][...] + g[1][...] for g in (gain_a, gain_f)]
    gains = jnp.concatenate([*gains, jnp.zeros((6, width), f32)], axis=0).T
    gains = jnp.concatenate([gains, jnp.zeros((width, PIECE - KVW - 8), f32)], axis=1).astype(bf16)

    def fill(at, of_three, own_three, own_one, single):
        for j in range(2):
            for i in range(3):
                right[of_three + i, j * n : (j + 1) * n, :] = own_three[j][i]
                right[of_three + i, (j + 2) * n : (j + 3) * n, :] = threes[j][i]
            right[single, j * n : (j + 1) * n, :] = own_one[j][...]
            right[single, (j + 2) * n : (j + 3) * n, :] = ones[j][...]

    @pl.when(core == 0)
    def _():
        fill(0, 0, queries, keys, 3)

    @pl.when(core == 1)
    def _():
        turned(left.at[1], o_refs)
        fill(0, 1, outs, values, 0)

    for i, m in enumerate(by_turn(core, chip)):
        out = send_ref if i < 2 else keep_ref
        which = jnp.where(m > 0, core, 0)
        out[i % 2] = nn(left[which], right[m]).astype(bf16)
        out[i % 2, :, KVW:] = gains


def grad_attention(sc, a, o, own, got, gains, after):
    n, width = a[0].shape
    out = shape((2, width, PIECE), bf16)
    return pl.pallas_call(
        grad_attention_kernel,
        out_shape=(out, out),
        in_specs=[SCALARS] + [WHOLE] * 24 + [LEFT] * len(after),
        out_specs=(WHOLE,) * 2,
        scratch_shapes=[pltpu.VMEM((2, width, 4 * n), bf16), pltpu.VMEM((4, 4 * n, PIECE), bf16)],
        cost_estimate=BRIEF,
        compiler_params=pltpu.CompilerParams(vmem_limit_bytes=36 << 20),
        name="grad_attention",
    )(sc, *a, *o, *own, *got, *gains, *after)


def lay_kernel(count, sc, *rest):
    mine, other, outs, kept = rest[:4], rest[4:8], rest[-1 - count : -1], rest[-1]
    core, chip = sc[0], sc[1]
    for kind, pieces in ((core, mine), (1 - core, other)):
        for who, piece in zip(whose(kind), pieces):
            kept[kind, chip ^ who] = piece[...]
    n = sum(o.shape[1] for o in outs[: 4 if len(outs) > 2 else 2]) // 8
    cols = [jnp.concatenate([kept[c, m, :, :n].astype(f32) for m in range(4)], axis=1) for c in range(2)]
    if len(outs) == 2:
        outs[0][...] = cols[0]
        outs[1][...] = cols[1]
    else:
        outs[0][...] = cols[0][:, : 3 * n]
        outs[1][...] = cols[0][:, 3 * n :]
        outs[2][...] = cols[1][:, :n]
        outs[3][...] = cols[1][:, n:]
        gains = kept[0, 0, :, n : n + 8].astype(f32) + kept[1, 0, :, n : n + 8].astype(f32)
        outs[4][...] = gains.T[:2]


def lay(sc, mine, other, widths, after):
    rows, n = mine[0].shape
    outs = tuple(shape((rows, w), f32) for w in widths)
    if len(widths) > 2:
        outs += (shape((2, rows), f32),)
    return pl.pallas_call(
        functools.partial(lay_kernel, len(outs)),
        out_shape=outs,
        in_specs=[SCALARS] + [WHOLE] * 8 + [LEFT] * len(after),
        out_specs=(WHOLE,) * len(outs),
        scratch_shapes=[pltpu.VMEM((2, 4, rows, n), bf16)],
        cost_estimate=BRIEF,
        compiler_params=pltpu.CompilerParams(vmem_limit_bytes=24 << 20),
        name="lay",
    )(sc, *mine, *other, *after)


def pick_first_kernel(sc, q_ref, k_ref, v_ref, o_ref, gain_ref, out_ref):
    rows = out_ref.shape[0]
    which = sc[0] * 4 + sc[1]
    pad = jnp.zeros((6, rows), f32)
    gains = jnp.concatenate([gain_ref[...], pad], axis=0).T.astype(bf16)
    rest = jnp.zeros((rows, PIECE - KVW - 8), bf16)
    for at in range(8):

        @pl.when(which == at)
        def _():
            if at in (3, 4):
                piece = (k_ref if at == 3 else v_ref)[...].T
            else:
                source, m = (q_ref, at) if at < 3 else (o_ref, at - 5)
                piece = source[:, m * KVW : (m + 1) * KVW]
            out_ref[...] = jnp.concatenate([piece, gains, rest], axis=1)


def pick_first(sc, query, key, value, out, gains):
    return pl.pallas_call(
        pick_first_kernel,
        out_shape=shape((query.shape[0], PIECE), bf16),
        in_specs=[SCALARS] + [WHOLE] * 5,
        out_specs=WHOLE,
        cost_estimate=BRIEF,
        compiler_params=pltpu.CompilerParams(vmem_limit_bytes=16 << 20),
        name="pick_first",
    )(sc, query, key, value, out, gains)


def pick_kernel(sc, gate, up, *rest):
    out_ref, sem = rest[-2:]
    cols = out_ref.shape[1]
    at = pl.ds(pl.multiple_of(sc[1] * cols, 128), cols)
    for c, source in ((0, gate), (1, up)):

        @pl.when(sc[0] == c)
        def _():
            pltpu.make_async_copy(source.at[:, at], out_ref, sem).start()

    pltpu.make_async_copy(gate.at[:, at], out_ref, sem).wait()


def pick(sc, gate, up, after):
    return pl.pallas_call(
        pick_kernel,
        out_shape=shape((gate.shape[0], gate.shape[1] // 4), bf16),
        in_specs=[SCALARS] + [LEFT] * (2 + len(after)),
        out_specs=WHOLE,
        scratch_shapes=[pltpu.SemaphoreType.DMA],
        cost_estimate=BRIEF,
        compiler_params=pltpu.CompilerParams(vmem_limit_bytes=16 << 20),
        name="pick",
    )(sc, gate, up, *after)


def pick_down_kernel(sc, down, *rest):
    out_ref, sem = rest[-2:]
    half = out_ref.shape[0]
    copy = pltpu.make_async_copy(down.at[pl.ds(pl.multiple_of(sc[0] * half, half), half), :], out_ref, sem)
    copy.start()
    copy.wait()


def pick_down(sc, down, after):
    rows, cols = down.shape
    return pl.pallas_call(
        pick_down_kernel,
        out_shape=shape((rows // 2, cols), bf16),
        in_specs=[SCALARS] + [LEFT] * (1 + len(after)),
        out_specs=WHOLE,
        scratch_shapes=[pltpu.SemaphoreType.DMA],
        cost_estimate=BRIEF,
        compiler_params=pltpu.CompilerParams(vmem_limit_bytes=16 << 20),
        name="pick_down",
    )(sc, down, *after)


def gains_kernel(first_ref, out_ref):
    for j in range(4):
        n = first_ref.shape[1]
        out_ref[:, j * n : (j + 1) * n] = first_ref[j, :, KVW : KVW + 8].astype(f32).T[:2]


def gains_of(first):
    return pl.pallas_call(
        gains_kernel,
        out_shape=shape((2, 4 * first.shape[1]), f32),
        in_specs=[WHOLE],
        out_specs=WHOLE,
        cost_estimate=BRIEF,
        compiler_params=pltpu.CompilerParams(vmem_limit_bytes=16 << 20),
        name="gains",
    )(first)


def stack_kernel(sc, *rest):
    parts, out_ref, sems = rest[:4], rest[-2], rest[-1]
    copies = [pltpu.make_async_copy(p, out_ref.at[sc[2] ^ s], sems.at[s]) for s, p in enumerate(parts)]
    for copy in copies:
        copy.start()
    for copy in copies:
        copy.wait()


def stack(sc, parts, after=()):
    return pl.pallas_call(
        stack_kernel,
        out_shape=shape((4,) + parts[0].shape, parts[0].dtype),
        in_specs=[SCALARS] + [LEFT] * (4 + len(after)),
        out_specs=WHOLE,
        scratch_shapes=[pltpu.SemaphoreType.DMA((4,))],
        cost_estimate=BRIEF,
        compiler_params=pltpu.CompilerParams(vmem_limit_bytes=16 << 20),
        name="stack",
    )(sc, *parts, *after)


def small(kernel, sc, args, outs, scratch, after, name):
    return pl.pallas_call(
        kernel,
        out_shape=tuple(outs),
        in_specs=[SCALARS] + [WHOLE] * len(args) + [LEFT] * len(after),
        out_specs=(WHOLE,) * len(outs),
        scratch_shapes=scratch,
        cost_estimate=BRIEF,
        compiler_params=pltpu.CompilerParams(vmem_limit_bytes=32 << 20),
        name=name,
    )(sc, *args, *after)


def sum_first(sc, keep, got, after):
    def kernel(sc, keep_ref, got_ref, *rest):
        later_ref, own_ref = rest[-2:]
        later_ref[...] = (keep_ref[1].astype(f32) + got_ref[1].astype(f32)).astype(bf16)
        own_ref[...] = keep_ref[0].astype(f32) + got_ref[0].astype(f32)

    block = keep.shape[1:]
    return small(kernel, sc, [keep, got], [shape(block, bf16), shape(block, f32)], [], after, "sum_first")


def sum_second(sc, own, got, after):
    def kernel(sc, own_ref, got_ref, *rest):
        send_ref, keep_ref, total = rest[-3:]
        n = total.shape[1]
        for j in range(4):
            rows = slice(j * n, (j + 1) * n)
            total[j] = own_ref[rows, :] + got_ref[rows, :].astype(f32)
        like = sc[2] & 1
        for h in range(2):
            send_ref[h] = total[2 * h + 1 - like].astype(bf16)
            keep_ref[h] = total[2 * h + like]

    rows, cols = own.shape
    part = (rows // 4, cols)
    outs = [shape((2,) + part, bf16), shape((2,) + part, f32)]
    return small(kernel, sc, [own, got], outs, [pltpu.VMEM((4,) + part, f32)], after, "sum_second")


def sum_third(sc, keep, got, after):
    def kernel(sc, keep_ref, got_ref, *rest):
        send_ref, own_ref = rest[-2:]
        h = sc[2] >> 1
        send_ref[...] = (keep_ref[1 - h] + got_ref[1 - h].astype(f32)).astype(bf16)
        own_ref[...] = keep_ref[h] + got_ref[h].astype(f32)

    part = keep.shape[1:]
    return small(kernel, sc, [keep, got], [shape(part, bf16), shape(part, f32)], [], after, "sum_third")


def down_pair(sc, own, got, after):
    def kernel(sc, own_ref, got_ref, *rest):
        rest[-1][...] = (own_ref[...].astype(f32) + got_ref[...].astype(f32)).astype(bf16)

    return small(kernel, sc, [own, got], [shape(own.shape, bf16)], [], after, "down_pair")[0]


def down_ring(sc, own, got, after):
    def kernel(sc, own_ref, got_ref, *rest):
        give_ref, keep_ref = rest[-2:]
        half = give_ref.shape[0]
        for out, c in ((give_ref, 1 - sc[0]), (keep_ref, sc[0])):
            rows = pl.ds(pl.multiple_of(c * half, half), half)
            out[...] = (own_ref[rows, :].astype(f32) + got_ref[rows, :].astype(f32)).astype(bf16)

    rows, cols = own.shape
    half = shape((rows // 2, cols), bf16)
    return small(kernel, sc, [own, got], [half, half], [], after, "down_ring")


def down_split(sc, keep, given, after):
    def kernel(sc, keep_ref, given_ref, *rest):
        send_ref, kept_ref, total = rest[-3:]
        n = total.shape[1]
        owner = (sc[2] >> 1) == sc[0]
        for m in range(4):
            rows = slice(m * n, (m + 1) * n)
            total[m] = jnp.where(owner, keep_ref[rows, :].astype(f32), given_ref[rows, :].astype(f32))
        for i, m in enumerate(by_turn(sc[0], sc[1])):
            out = send_ref if i < 2 else kept_ref
            out[i % 2] = total[m].astype(bf16)

    rows, cols = keep.shape
    out = shape((2, rows // 4, cols), bf16)
    return small(kernel, sc, [keep, given], [out, out], [pltpu.VMEM((4, rows // 4, cols), f32)], after, "down_split")


def sum_two(sc, own, got, after):
    def kernel(sc, own_ref, got_ref, *rest):
        rest[-1][...] = (own_ref[...] + got_ref[...].astype(f32)).astype(bf16)

    return small(kernel, sc, [own, got], [shape(own.shape, bf16)], [], after, "sum_two")[0]


def lay_down(sc, mine, other, after):
    def kernel(sc, *rest):
        out_ref, total = rest[-2:]
        n = total.shape[2]
        for kind, pieces in ((sc[0], rest[:4]), (1 - sc[0], rest[4:8])):
            for who, piece in zip(whose(kind), pieces):
                total[kind, sc[1] ^ who] = piece[...].astype(f32)
        for c in range(2):
            for m in range(4):
                at = (c * 4 + m) * n
                out_ref[at : at + n, :] = total[c, m]

    n, cols = mine[0].shape
    return small(kernel, sc, [*mine, *other], [shape((8 * n, cols), f32)], [pltpu.VMEM((2, 4, n, cols), f32)], after, "lay_down")[0]


CORE, SIDE, BACK = 1, 2, 4
rope_base = 10000.0
RUNS = 2


def flip(value, bit, bit1=None):
    count = lax.axis_size("dp")
    bits = (bit, bit if bit1 is None else bit1)
    return lax.ppermute(value, "dp", [(i, i ^ bits[i & 1]) for i in range(count)])


def flip_z(value, bit, where=lambda d, z: True):
    count, depth = lax.axis_size("dp"), lax.axis_size("fsdp")
    pairs = [(d * depth + z, d * depth + (z ^ bit)) for d in range(count) for z in range(depth) if where(d, z)]
    return lax.ppermute(value, ("dp", "fsdp"), pairs)


def home_to_work(value, back=False):
    count, depth = lax.axis_size("dp"), lax.axis_size("fsdp")
    pairs = []
    for d in range(count):
        for z in range(depth):
            there = (d & ~1) | (z & 1), 2 * (d & 1) + (z >> 1)
            pair = (d * depth + z, there[0] * depth + there[1])
            pairs.append(pair[::-1] if back else pair)
    return lax.ppermute(value, ("dp", "fsdp"), pairs)


def place():
    d, z = lax.axis_index("dp"), lax.axis_index("fsdp")
    return d & 1, (d >> 1) & 3, z


def turns(shard):
    far = flip_z(shard, 2)
    return shard, flip_z(shard, 1), far, flip_z(far, 1)


def plane_gather(piece):
    first, second = flip(piece, SIDE, BACK), flip(piece, BACK, SIDE)
    mine = (piece, first, second, flip(first, BACK, SIDE))
    return mine, tuple(flip(p, CORE) for p in mine)


def window(own):
    core, _, _ = place()
    depth = lax.axis_size("fsdp")
    far = lax.ppermute(own, "fsdp", [(z, z + 1) for z in range(0, depth, 2)])
    near = flip(jnp.where(core == 0, own, far), CORE)
    return far, near, own


def unwindow(far, near):
    core, _, _ = place()
    depth = lax.axis_size("fsdp")
    near = flip(near, CORE)
    far = jnp.where(core == 1, far + near.astype(f32), far).astype(bf16)
    return near, lax.ppermute(far, "fsdp", [(z + 1, z) for z in range(0, depth, 2)])


def over_groups(value):
    bit = 8
    while bit < lax.axis_size("dp"):
        value = (value.astype(f32) + flip(value, bit).astype(f32)).astype(bf16)
        bit *= 2
    return value


def spread(piece):
    return piece, flip(piece, SIDE, BACK), flip(piece, BACK, SIDE), flip(piece, SIDE | BACK)


def across(pieces):
    return tuple(flip(p, CORE) for p in pieces)


def body(tokens, segment_ids, attn_gain, query_weight, key_weight, value_weight, out_weight, ffn_gain, gate_weight, up_weight, down_weight, cotangent):
    core, chip, z = place()
    sc = jnp.stack([core, chip, z]).astype(jnp.int32)
    _, stretch, width = tokens.shape
    rows, depth = query_weight.shape[0], lax.axis_size("fsdp")
    block = 2 * (z & 1) + core
    positions = (block * stretch + jnp.arange(stretch)).astype(f32)
    freq = rope_base ** (-2.0 * jnp.arange(HEAD_DIM // 2, dtype=f32) / HEAD_DIM)
    angle = freq[:, None] * positions[None, :]
    cos, sin = jnp.cos(angle), jnp.sin(angle)

    gains = jnp.stack([attn_gain, ffn_gain]).astype(f32)
    parts_a = turns(pick_first(sc, query_weight, key_weight.T, value_weight.T, out_weight, gains))
    ids = jnp.broadcast_to((segment_ids[0] + 1).astype(bf16), (IDS, stretch))
    tokens = home_to_work(jnp.concatenate([tokens[0].T, ids]))
    whole_a = stack(sc, parts_a)
    gains = gains_of(whole_a)
    gain_a, gain_f = gains[:1], gains[1:]
    wa = plane_gather(whole_a.reshape(depth * rows, PIECE))
    piece_b = pick(sc, gate_weight, up_weight, [whole_a])
    whole_b = stack(sc, turns(piece_b)).reshape(depth * rows, piece_b.shape[1])
    wb = plane_gather(whole_b)
    parts_d = turns(pick_down(sc, down_weight.T, [whole_b]))

    h_0, a0, q0, own = pre(sc, tokens, gain_a, cos, sin, *wa, [whole_b])
    kv0 = window(own)
    o0, lse0 = attend(q0, kv0)
    whole_d = stack(sc, parts_d, [o0])
    weights = wa, wb, (whole_d, flip(whole_d, CORE))
    cot = home_to_work(cotangent[0].T)
    mixed0, h1_0, b0, gate0, up0, z0, h_1, a1, q1, own = post(False, sc, o0, h_0, gain_f, gain_a, cos, sin, own, *weights)
    kv1 = window(own)
    across_0 = across((a0, b0, mixed0))
    o1, lse1 = attend(q1, kv1, across_0)
    mixed1, h1_1, b1, gate1, up1, z1, output = post(True, sc, o1, h_1, gain_f, gain_a, cos, sin, own, *weights)
    output = home_to_work(output, back=True)
    across_1 = across((a1, b1, mixed1))

    gb1, act1, away1, zk1, zs1, g1, p1, dgain_f1, do = back(True, False, sc, weights, [cot], [gate1, up1, h1_1, gain_f, z1])
    across_2 = across((gb1, away1, zs1))
    dq1, three1, far, near, own = attend_back(sc, p1, q1, kv1, lse1, do, cos, sin, [output, *across_1])
    near, far = unwindow(far, near)
    (three1,) = across((three1,))
    tail = [g1, dq1, own, near, far, h_1, gain_a, cos, sin]
    dk1, dv1, one1, dgain_a1, gb0, act0, away0, zk0, zs0, g1, p0, dgain_f0, do = back(False, False, sc, weights, tail, [gate0, up0, h1_0, gain_f, z0], [three1, *across_2])

    away0, gb0_, zs0, one1 = across((away0, gb0, zs0, one1))
    send_b, keep_b = grad_ffn(sc, [b1, b0, across_1[1], across_0[1]], [act1, act0, across_2[1], away0])
    got_b = flip(send_b, SIDE, BACK)
    like_d, unlike_d = grad_down(sc, [gb1, gb0, across_2[0], gb0_], [zk1, zk0, across_2[2], zs0], [send_b])
    got_d = flip_z(unlike_d, 1)

    dq0, three0, far, near, own = attend_back(sc, p0, q0, kv0, lse0, do, cos, sin, [like_d, one1])
    near, far = unwindow(far, near)
    (three0,) = across((three0,))
    later_b, own_b = sum_first(sc, keep_b, got_b, [own, three0])
    more_b = flip(later_b, BACK, SIDE)
    tail = [g1, dq0, own, near, far, h_0, gain_a, cos, sin]
    dk0, dv0, one0, dgain_a0, grad_tokens = back(False, True, sc, weights, tail, None, [later_b])
    grad_tokens = home_to_work(grad_tokens, back=True)

    pair_d = down_pair(sc, like_d, got_d, [one0])
    got_d = flip_z(pair_d, 2, lambda d, z: (z >> 1) != (d & 1))
    own = [dq1, dq0, dk1, dk0, dv1, dv0, p1, p0]
    got = [three1, three0, one1, flip(one0, CORE)]
    send_a, keep_a = grad_attention(sc, [a1, a0, across_1[0], across_0[0]], [mixed1, mixed0, across_1[2], across_0[2]], own, got, [dgain_a1, dgain_a0, dgain_f1, dgain_f0], [pair_d])
    got_a = flip(send_a, SIDE, BACK)
    send_b, ring_b = sum_second(sc, own_b, more_b, [send_a])
    got_b = flip_z(send_b, 1)
    later_a, own_a = sum_first(sc, keep_a, got_a, [ring_b, grad_tokens])
    more_a = flip(later_a, BACK, SIDE)
    send_b, ring_b = sum_third(sc, ring_b, got_b, [later_a])
    got_b = flip_z(send_b, 2)
    give, keep = down_ring(sc, pair_d, got_d, [send_b])
    send_d, keep_d = down_split(sc, keep, flip(give, CORE), [])
    got_d = flip(send_d, SIDE, BACK)
    send_a, ring_a = sum_second(sc, own_a, more_a, [send_d])
    got_a = flip_z(send_a, 1)
    later_d, own_d = sum_first(sc, keep_d, got_d, [ring_a])
    more_d = flip(later_d, BACK, SIDE)
    piece_b = over_groups(sum_two(sc, ring_b, got_b, [later_d]))
    all_b = spread(piece_b)
    send_a, ring_a = sum_third(sc, ring_a, got_a, [piece_b])
    got_a = flip_z(send_a, 2)
    piece_d = over_groups(sum_two(sc, own_d, more_d, [send_a]))
    grad_gate, grad_up = lay(sc, all_b, across(all_b), (gate_weight.shape[1],) * 2, [piece_d])
    all_d = spread(piece_d)
    piece_a = over_groups(sum_two(sc, ring_a, got_a, [grad_gate]))
    all_a = spread(piece_a)
    grad_down_ = lay_down(sc, all_d, across(all_d), [piece_a])
    grad_query, grad_key, grad_value, grad_out, dgains = lay(sc, all_a, across(all_a), (width, KVW, KVW, width), [grad_down_])
    grad_tokens, output = grad_tokens.astype(f32).T, output.T
    return (output[None], grad_tokens[None], dgains[0], grad_query, grad_key, grad_value, grad_out, dgains[1], grad_gate, grad_up, grad_down_.T)


def solution(mesh):
    wide, rows, shard = P("dp", "fsdp", None), P("dp", "fsdp"), P("fsdp", None)
    in_specs = (wide, rows, P("fsdp"), shard, shard, shard, shard, P("fsdp"), shard, shard, shard, wide)
    out_specs = (wide, wide, P("fsdp"), shard, shard, shard, shard, P("fsdp"), shard, shard, shard)
    return jax.shard_map(body, mesh=mesh, in_specs=in_specs, out_specs=out_specs, check_vma=False)
```

```python
import functools
import jax
import jax.numpy as jnp
from jax import lax
from jax.sharding import PartitionSpec as P
from jax.experimental import pallas as pl
from jax.experimental.pallas import tpu as pltpu

f32, bf16 = jnp.float32, jnp.bfloat16
eps = 1e-05
HEADS, KV_HEADS, HEAD_DIM, GROUP, KVW = 15, 5, 64, 3, 320
IDS = 16
PIECE = 384
LIMIT = 58 << 20
WHOLE = pl.BlockSpec(memory_space=pltpu.VMEM)
LEFT = pl.BlockSpec(memory_space=pl.ANY)
SCALARS = pl.BlockSpec(memory_space=pltpu.SMEM)
BRIEF = pl.CostEstimate(flops=1024, bytes_accessed=1024, transcendentals=0)


def contract(a, b, i, j):
    return lax.dot_general(a, b, (((i,), (j,)), ((), ())), preferred_element_type=f32)


def nn(a, b):
    return contract(a, b, 1, 0)


def nt(a, b):
    return contract(a, b, 1, 1)


def tn(a, b):
    return contract(a, b, 0, 0)


def whose(core):
    return 0, 1 + core, 2 - core, 3


def fetch(mine, other, kept, sems, core, chip):
    for kind, pieces in ((core, mine), (1 - core, other)):
        for who, piece in zip(whose(kind), pieces):
            at = chip ^ who
            pltpu.make_async_copy(piece, kept.at[kind, at], sems.at[kind, at]).start()


def arrived(kept, sems, *at):
    pltpu.make_async_copy(kept.at[at], kept.at[at], sems.at[at]).wait()


def normed(x, gain):
    return x * lax.rsqrt(jnp.mean(x * x, axis=-1, keepdims=True) + eps) * gain


def norm_back(x, gain, grad):
    r = lax.rsqrt(jnp.mean(x * x, axis=-1, keepdims=True) + eps)
    hat = x * r
    scaled = grad * gain
    dx = r * (scaled - hat * jnp.mean(scaled * hat, axis=-1, keepdims=True))
    return dx, jnp.sum(grad * hat, axis=0, keepdims=True)


def widened(x):
    return jnp.concatenate([x, jnp.zeros((x.shape[0], PIECE - x.shape[1]), x.dtype)], axis=1)


def rope(u, cos, sin, back):
    heads = u.shape[0] // HEAD_DIM
    half = HEAD_DIM // 2
    out = []
    for h in range(heads):
        u1, u2 = u[h * HEAD_DIM : h * HEAD_DIM + half], u[h * HEAD_DIM + half : (h + 1) * HEAD_DIM]
        if back:
            out += [u1 * cos + u2 * sin, u2 * cos - u1 * sin]
        else:
            out += [u1 * cos - u2 * sin, u2 * cos + u1 * sin]
    return jnp.concatenate(out, axis=0)


def project(state, gain_ref, cos_ref, sin_ref, ids, kept, sems, a_ref, q_ref, kv_ref):
    a = normed(state, gain_ref[...]).astype(bf16)
    a_ref[...] = a
    cos, sin = cos_ref[...], sin_ref[...]
    arrived(kept, sems, 0, 3)
    kv_ref[:KVW, :] = rope(nn(a, kept[0, 3, :, :KVW]).T, cos, sin, False).astype(bf16)
    arrived(kept, sems, 1, 0)
    kv_ref[2 * KVW :, :] = ids
    kv_ref[KVW : 2 * KVW, :] = nn(a, kept[1, 0, :, :KVW]).T.astype(bf16)
    for m in range(3):
        arrived(kept, sems, 0, m)
        q_ref[pl.ds(m * KVW, KVW), :] = rope(nn(a, kept[0, m, :, :KVW]).T, cos, sin, False).astype(bf16)


def pre_kernel(sc, ht_ref, gain_ref, cos_ref, sin_ref, *rest):
    width = ht_ref.shape[0] - IDS
    mine, other = rest[:4], rest[4:8]
    h_ref, a_ref, q_ref, kv_ref, kept, sems = rest[-6:]
    core, chip = sc[0], sc[1]
    fetch(mine, other, kept, sems, core, chip)
    h = ht_ref[:width, :].T
    h_ref[...] = h
    project(h.astype(f32), gain_ref, cos_ref, sin_ref, ht_ref[width:, :], kept, sems, a_ref, q_ref, kv_ref)
    for m in range(1, 4):
        arrived(kept, sems, 1, m)


def scratch_a(width):
    return [pltpu.VMEM((2, 4, width, PIECE), bf16), pltpu.SemaphoreType.DMA((2, 4))]


def shape(s, d):
    return jax.ShapeDtypeStruct(s, d)


def pre(sc, ht, gain, cos, sin, mine_a, other_a, after):
    width, n = ht.shape[0] - IDS, ht.shape[1]
    return pl.pallas_call(
        pre_kernel,
        out_shape=(shape((n, width), bf16), shape((n, width), bf16), shape((width, n), bf16), shape((2 * KVW + IDS, n), bf16)),
        in_specs=[SCALARS] + [WHOLE] * 4 + [LEFT] * (8 + len(after)),
        out_specs=(WHOLE,) * 4,
        scratch_shapes=scratch_a(width),
        cost_estimate=BRIEF,
        compiler_params=pltpu.CompilerParams(vmem_limit_bytes=LIMIT),
        name="pre",
    )(sc, ht, gain, cos, sin, *mine_a, *other_a, *after)


def bias_of(kv):
    keys, n = kv.shape[1], kv.shape[1] // 3
    ids = kv[2 * KVW :, :].astype(f32)
    seg_k, seg_q = ids.T[:, :1], ids[:1, 2 * n :]
    j = lax.broadcasted_iota(jnp.int32, (keys, n), 0)
    i = lax.broadcasted_iota(jnp.int32, (keys, n), 1) + (keys - n)
    return jnp.where((seg_k == seg_q) & (j <= i), 0.0, -1e30).astype(f32)


def window_of(parts, whole):
    n = parts[0].shape[1]
    for w, part in enumerate(parts):
        whole[:, w * n : (w + 1) * n] = part[...]


def attend_kernel(q_ref, kv0, kv1, kv2, *rest):
    o_ref, lse_ref, bias, kv = rest[-4:]
    window_of((kv0, kv1, kv2), kv)
    bias[...] = bias_of(kv)

    def head(e, _):
        row = pl.multiple_of(e * HEAD_DIM, HEAD_DIM)
        k = kv[pl.ds(row, HEAD_DIM), :]
        v = kv[pl.ds(row + KVW, HEAD_DIM), :]
        for g in range(GROUP):
            at = pl.multiple_of((e * GROUP + g) * HEAD_DIM, HEAD_DIM)
            q = q_ref[pl.ds(at, HEAD_DIM), :]
            s = tn(k, q) * HEAD_DIM ** (-0.5) + bias[...]
            top = jnp.max(s, axis=0, keepdims=True)
            expo = jnp.exp(s - top)
            total = jnp.sum(expo, axis=0, keepdims=True)
            probs = (expo * (1.0 / total)).astype(bf16)
            o_ref[pl.ds(at, HEAD_DIM), :] = nn(v, probs).astype(bf16)
            lse_ref[pl.ds(e * GROUP + g, 1), :] = top + jnp.log(total)
        return 0

    lax.fori_loop(0, KV_HEADS, head, 0)


def attend(q, kvs, after=()):
    width, n = q.shape
    return pl.pallas_call(
        attend_kernel,
        out_shape=(shape((width, n), bf16), shape((HEADS, n), f32)),
        in_specs=[WHOLE] * 4 + [LEFT] * len(after),
        out_specs=(WHOLE,) * 2,
        scratch_shapes=[pltpu.VMEM((3 * n, n), f32), pltpu.VMEM((2 * KVW + IDS, 3 * n), bf16)],
        cost_estimate=BRIEF,
        compiler_params=pltpu.CompilerParams(vmem_limit_bytes=24 << 20),
        name="attend",
    )(q, *kvs, *after)


def attend_back_kernel(sc, p_ref, q_ref, kv0, kv1, kv2, lse_ref, do_ref, cos_ref, sin_ref, *rest):
    dq_ref, three_ref, far_ref, near_ref, own_ref, bias, kv, dqs = rest[-8:]
    n = q_ref.shape[1]
    window_of((kv0, kv1, kv2), kv)
    bias[...] = bias_of(kv)
    scale = HEAD_DIM ** (-0.5)

    def head(e, _):
        row = pl.multiple_of(e * HEAD_DIM, HEAD_DIM)
        k = kv[pl.ds(row, HEAD_DIM), :]
        v = kv[pl.ds(row + KVW, HEAD_DIM), :]
        dk = dv = None
        for g in range(GROUP):
            at = pl.multiple_of((e * GROUP + g) * HEAD_DIM, HEAD_DIM)
            q = q_ref[pl.ds(at, HEAD_DIM), :]
            do = do_ref[pl.ds(at, HEAD_DIM), :]
            s = tn(k, q) * scale + bias[...]
            probs = jnp.exp(s - lse_ref[pl.ds(e * GROUP + g, 1), :])
            dp = tn(v, do)
            inner = jnp.sum(probs * dp, axis=0, keepdims=True)
            ds = (probs * (dp - inner)).astype(bf16)
            dvg, dkg = nt(do, probs.astype(bf16)), nt(q, ds)
            dv, dk = (dvg, dkg) if g == 0 else (dv + dvg, dk + dkg)
            dqs[pl.ds(at, HEAD_DIM), :] = nn(k, ds)
        for at, grad in ((row, dk * scale), (row + KVW, dv)):
            far_ref[pl.ds(at, HEAD_DIM), :] = grad[:, :n]
            near_ref[pl.ds(at, HEAD_DIM), :] = grad[:, n : 2 * n].astype(bf16)
            own_ref[pl.ds(at, HEAD_DIM), :] = grad[:, 2 * n :]
        return 0

    lax.fori_loop(0, KV_HEADS, head, 0)
    cos, sin = cos_ref[...] * scale, sin_ref[...] * scale
    for m in range(3):
        dq = widened(rope(dqs[m * KVW : (m + 1) * KVW, :], cos, sin, True).T.astype(bf16))
        dq_ref[m] = dq
        three_ref[m] = jnp.where(sc[0] == 0, p_ref[m], dq)


def attend_back(sc, p, q, kvs, lse, do, cos, sin, after=()):
    width, n = q.shape
    block = (2 * KVW, n)
    return pl.pallas_call(
        attend_back_kernel,
        out_shape=(shape((3, n, PIECE), bf16), shape((3, n, PIECE), bf16), shape(block, f32), shape(block, bf16), shape(block, f32)),
        in_specs=[SCALARS] + [WHOLE] * 9 + [LEFT] * len(after),
        out_specs=(WHOLE,) * 5,
        scratch_shapes=[pltpu.VMEM((3 * n, n), f32), pltpu.VMEM((2 * KVW + IDS, 3 * n), bf16), pltpu.VMEM((width, n), f32)],
        cost_estimate=BRIEF,
        compiler_params=pltpu.CompilerParams(vmem_limit_bytes=32 << 20),
        name="attend_back",
    )(sc, p, q, *kvs, lse, do, cos, sin, *after)


def fetch_ffn(mine_b, other_b, down, wb, wd, sem_b, sem_d, core, chip):
    fetch(mine_b, other_b, wb, sem_b, core, chip)
    half = down[0].shape[1]
    for c, part in ((core, down[0]), (1 - core, down[1])):
        rows = pl.ds(pl.multiple_of(c * half, half), half)
        pltpu.make_async_copy(part, wd.at[:, rows], sem_d).start()


def arrived_down(wd, sem_d):
    pltpu.make_async_copy(wd, wd, sem_d).wait()


def scratch_ffn(width, n):
    return [
        pltpu.VMEM((2, 4, width, n), bf16),
        pltpu.SemaphoreType.DMA((2, 4)),
        pltpu.VMEM((4, width, n), bf16),
        pltpu.SemaphoreType.DMA,
    ]


def post_kernel(last, sc, ot_ref, h_ref, gain_ref, gain_a, cos_ref, sin_ref, *rest):
    mine_a, other_a, mine_b, other_b = rest[:4], rest[4:8], rest[8:12], rest[12:16]
    down, ids_ref = rest[16:18], rest[18]
    o_ref, h1_ref, b_ref, gate_ref, up_ref, z_ref, next_ref = rest[19:26]
    more, rest = rest[26 : 26 + (0 if last else 3)], rest[26 + (0 if last else 3) :]
    wa, sem_a, wb, sem_b, wd, sem_d = rest
    core, chip = sc[0], sc[1]
    fetch(mine_a, other_a, wa, sem_a, core, chip)
    fetch_ffn(mine_b, other_b, down, wb, wd, sem_b, sem_d, core, chip)
    o = ot_ref[...].T
    o_ref[...] = o
    for m in range(1, 4):
        arrived(wa, sem_a, 1, m)
    h1 = h_ref[...].astype(f32) + jnp.concatenate([nn(o, wa[1, m, :, :KVW]) for m in range(1, 4)], axis=1)
    h1_ref[...] = h1
    b = normed(h1, gain_ref[...]).astype(bf16)
    b_ref[...] = b
    n = wb.shape[3]
    total = h1
    for m in range(4):
        cols = slice(m * n, (m + 1) * n)
        arrived(wb, sem_b, 0, m)
        gate = nn(b, wb[0, m])
        arrived(wb, sem_b, 1, m)
        up = nn(b, wb[1, m])
        gate_ref[:, cols] = gate.astype(bf16)
        up_ref[:, cols] = up.astype(bf16)
        z = (gate / (1.0 + jnp.exp(-gate)) * up).astype(bf16)
        z_ref[:, cols] = z
        if m == 0:
            arrived_down(wd, sem_d)
        total = total + nt(z, wd[m])
    next_ref[...] = total.astype(bf16).T if last else total
    if last:
        arrived(wa, sem_a, 1, 0)
        for m in range(4):
            arrived(wa, sem_a, 0, m)
    else:
        project(total, gain_a, cos_ref, sin_ref, ids_ref[2 * KVW :, :], wa, sem_a, *more)


def post(last, sc, ot, h, gain, gain_a, cos, sin, kv, wa, wb, wd):
    width, n = ot.shape
    hidden = wb[0][0].shape[1] * 4
    outs = [shape((n, width), bf16), shape((n, width), f32), shape((n, width), bf16)] + [shape((n, hidden), bf16)] * 3
    outs += [shape((width, n), bf16) if last else shape((n, width), f32)]
    if not last:
        outs += [shape((n, width), bf16), shape((width, n), bf16), shape((2 * KVW + IDS, n), bf16)]
    return pl.pallas_call(
        functools.partial(post_kernel, last),
        out_shape=tuple(outs),
        in_specs=[SCALARS] + [WHOLE] * 6 + [LEFT] * 18 + [WHOLE],
        out_specs=(WHOLE,) * len(outs),
        scratch_shapes=scratch_a(width) + scratch_ffn(width, hidden // 4),
        cost_estimate=BRIEF,
        compiler_params=pltpu.CompilerParams(vmem_limit_bytes=LIMIT),
        name="post",
    )(sc, ot, h, gain, gain_a, cos, sin, *wa[0], *wa[1], *wb[0], *wb[1], *wd, kv)


def ffn_back(state, core, refs, weights):
    gate_ref, up_ref, h1_ref, gain_ref, z_ref, gb_ref, keep_ref, send_ref, zk_ref, zs_ref, g1_ref, p_ref, dgain_ref, do_ref = refs
    wa, sem_a, wb, sem_b, wd, sem_d = weights
    gb = state.astype(bf16)
    gb_ref[...] = gb
    n = wb.shape[3]
    half = 2 * n
    first = core == 0
    low, high = z_ref[:, :half], z_ref[:, half:]
    zk_ref[...] = jnp.where(first, low, high)
    zs_ref[...] = jnp.where(first, high, low)
    arrived_down(wd, sem_d)
    db = None
    for m in range(4):
        cols = slice(m * n, (m + 1) * n)
        dz = nn(gb, wd[m])
        gate, up = gate_ref[:, cols].astype(f32), up_ref[:, cols].astype(f32)
        sig = 1.0 / (1.0 + jnp.exp(-gate))
        dup = (dz * (gate * sig)).astype(bf16)
        dgate = (dz * up * (sig * (1.0 + gate * (1.0 - sig)))).astype(bf16)
        keep_ref[:, cols] = jnp.where(first, dgate, dup)
        send_ref[:, cols] = jnp.where(first, dup, dgate)
        arrived(wb, sem_b, 0, m)
        part = nt(dgate, wb[0, m])
        arrived(wb, sem_b, 1, m)
        part = part + nt(dup, wb[1, m])
        db = part if m == 0 else db + part
    dx, dgain = norm_back(h1_ref[...], gain_ref[...], db)
    dgain_ref[...] = dgain
    g1 = state + dx
    g1_ref[...] = g1
    low = g1.astype(bf16)
    do = None
    for p in range(3):
        part = low[:, p * KVW : (p + 1) * KVW]
        p_ref[p] = widened(part)
        arrived(wa, sem_a, 1, p + 1)
        part = nt(wa[1, p + 1, :, :KVW], part)
        do = part if p == 0 else do + part
    do_ref[...] = do.astype(bf16)


def finish_a(wa, sem_a, *left):
    for at in left:
        arrived(wa, sem_a, *at)


def query_back(dq_ref, wa, sem_a):
    da = None
    for m in range(3):
        arrived(wa, sem_a, 0, m)
        part = nt(dq_ref[m, :, :KVW], wa[0, m, :, :KVW])
        da = part if m == 0 else da + part
    return da


def project_back(da, own_ref, near_ref, far_ref, core, cos_ref, sin_ref, dk_ref, dv_ref, one_ref, h, gain, wa, sem_a):
    cos, sin = cos_ref[...], sin_ref[...]
    grad = own_ref[...] + far_ref[...].astype(f32) + jnp.where(core == 0, near_ref[...].astype(f32), 0.0)
    dk = rope(grad[:KVW], cos, sin, True).T.astype(bf16)
    dv = grad[KVW:].T.astype(bf16)
    dk_ref[...] = widened(dk)
    dv_ref[...] = widened(dv)
    one_ref[...] = widened(jnp.where(core == 0, dv, dk))
    arrived(wa, sem_a, 0, 3)
    arrived(wa, sem_a, 1, 0)
    da = da + nt(dk, wa[0, 3, :, :KVW]) + nt(dv, wa[1, 0, :, :KVW])
    return norm_back(h, gain, da)


def back_kernel(start, end, after, sc, *rest):
    rest = list(rest)

    def take(n):
        out = rest[:n]
        del rest[:n]
        return out

    core, chip = sc[0], sc[1]
    mine_a, other_a = take(4), take(4)
    if not end:
        mine_b, other_b = take(4), take(4)
        down = take(2)
    if start:
        (g_ref,) = take(1)
    else:
        g1_in, dq_ref, own_ref, near_ref, far_ref, h_ref, gain_a, cos_ref, sin_ref = take(9)
    if not end:
        ins = take(5)
    take(after)
    if not start:
        dk_ref, dv_ref, one_ref, dgain_a = take(4)
    if end:
        (g_out,) = take(1)
    else:
        outs = take(9)
    wa, sem_a = take(2)
    fetch(mine_a, other_a, wa, sem_a, core, chip)
    if not end:
        wb, sem_b, wd, sem_d = take(4)
        fetch_ffn(mine_b, other_b, down, wb, wd, sem_b, sem_d, core, chip)
    if start:
        state = g_ref[...].T.astype(f32)
    else:
        da = query_back(dq_ref, wa, sem_a)
        dx, dgain = project_back(da, own_ref, near_ref, far_ref, core, cos_ref, sin_ref, dk_ref, dv_ref, one_ref, h_ref[...].astype(f32), gain_a[...], wa, sem_a)
        dgain_a[...] = dgain
        state = g1_in[...] + dx
    if end:
        g_out[...] = state.astype(bf16).T
        finish_a(wa, sem_a, (1, 1), (1, 2), (1, 3))
    else:
        ffn_back(state, core, (*ins, *outs), (wa, sem_a, wb, sem_b, wd, sem_d))
        if start:
            finish_a(wa, sem_a, (1, 0), (0, 0), (0, 1), (0, 2), (0, 3))


def back(start, end, sc, weights, tail, ffn, after=()):
    wa, wb, wd = weights
    width = wa[0][0].shape[0]
    args = [sc, *wa[0], *wa[1]]
    specs = [SCALARS] + [LEFT] * 8
    scratch = scratch_a(width)
    if not end:
        args += [*wb[0], *wb[1], *wd]
        specs += [LEFT] * 10
        scratch += scratch_ffn(width, wb[0][0].shape[1])
    args += list(tail)
    specs += [WHOLE] * len(tail)
    n = tail[0].shape[1 if start else 0]
    outs = []
    if not end:
        args += list(ffn)
        specs += [WHOLE] * len(ffn)
    if not start:
        outs += [shape((n, PIECE), bf16)] * 3 + [shape((1, width), f32)]
    if end:
        outs += [shape((width, n), bf16)]
    else:
        hidden = ffn[0].shape[1]
        outs += [shape((n, width), bf16), shape((n, hidden), bf16), shape((n, hidden), bf16), shape((n, hidden // 2), bf16), shape((n, hidden // 2), bf16)]
        outs += [shape((n, width), f32), shape((3, n, PIECE), bf16), shape((1, width), f32), shape((width, n), bf16)]
    args += list(after)
    specs += [LEFT] * len(after)
    return pl.pallas_call(
        functools.partial(back_kernel, start, end, len(after)),
        out_shape=tuple(outs),
        in_specs=specs,
        out_specs=(WHOLE,) * len(outs),
        scratch_shapes=scratch,
        cost_estimate=BRIEF,
        compiler_params=pltpu.CompilerParams(vmem_limit_bytes=LIMIT),
        name="back_end" if end else ("back_start" if start else "back_join"),
    )(*args)


def by_turn(core, chip):
    one = 1 + core
    return chip ^ one, chip ^ 3, chip, chip ^ (3 - one)


def turned(dst, blocks):
    n = blocks[0].shape[0]
    for i, block in enumerate(blocks):
        dst[:, i * n : (i + 1) * n] = block[...].T


def grad_ffn_kernel(sc, *rest):
    lefts, rights = rest[:4], rest[4:8]
    send_ref, keep_ref, left, right = rest[-4:]
    core, chip = sc[0], sc[1]
    n, cols = rights[0].shape[0], right.shape[1]
    turned(left, lefts)
    for i, m in enumerate(by_turn(core, chip)):
        at = pl.multiple_of(m * cols, 128)
        for j, block in enumerate(rights):
            right[j * n : (j + 1) * n, :] = block[:, pl.ds(at, cols)]
        out = send_ref if i < 2 else keep_ref
        out[i % 2] = nn(left[...], right[...]).astype(bf16)


def grad_ffn(sc, lefts, rights, after):
    n, width = lefts[0].shape
    cols = rights[0].shape[1] // 4
    out = shape((2, width, cols), bf16)
    return pl.pallas_call(
        grad_ffn_kernel,
        out_shape=(out, out),
        in_specs=[SCALARS] + [WHOLE] * 8 + [LEFT] * len(after),
        out_specs=(WHOLE,) * 2,
        scratch_shapes=[pltpu.VMEM((width, 4 * n), bf16), pltpu.VMEM((4 * n, cols), bf16)],
        cost_estimate=BRIEF,
        compiler_params=pltpu.CompilerParams(vmem_limit_bytes=36 << 20),
        name="grad_ffn",
    )(sc, *lefts, *rights, *after)


def grad_down_kernel(sc, *rest):
    lefts, rights = rest[:4], rest[4:8]
    outs, left, right = rest[-4:-2], rest[-2], rest[-1]
    n, cols = rights[0].shape[0], right.shape[1]
    turned(left, lefts)
    for i, out in enumerate(outs):
        at = pl.multiple_of(((sc[2] + i) & 1) * cols, 128)
        for j, block in enumerate(rights):
            right[j * n : (j + 1) * n, :] = block[:, pl.ds(at, cols)]
        out[...] = nn(left[...], right[...]).astype(bf16)


def grad_down(sc, lefts, rights, after):
    n, width = lefts[0].shape
    cols = rights[0].shape[1] // 2
    return pl.pallas_call(
        grad_down_kernel,
        out_shape=(shape((width, cols), bf16),) * 2,
        in_specs=[SCALARS] + [WHOLE] * 8 + [LEFT] * len(after),
        out_specs=(WHOLE,) * 2,
        scratch_shapes=[pltpu.VMEM((width, 4 * n), bf16), pltpu.VMEM((4 * n, cols), bf16)],
        cost_estimate=BRIEF,
        compiler_params=pltpu.CompilerParams(vmem_limit_bytes=32 << 20),
        name="grad_down",
    )(sc, *lefts, *rights, *after)


def grad_attention_kernel(sc, *rest):
    a_refs, o_refs, rest = rest[:4], rest[4:8], rest[8:]
    queries, keys, values, outs, threes, ones = (rest[i : i + 2] for i in range(0, 12, 2))
    gain_a, gain_f = (rest[i : i + 2] for i in (12, 14))
    send_ref, keep_ref, left, right = rest[-4:]
    core, chip = sc[0], sc[1]
    n, width = a_refs[0].shape
    turned(left.at[0], a_refs)
    gains = [g[0][...] + g[1][...] for g in (gain_a, gain_f)]
    gains = jnp.concatenate([*gains, jnp.zeros((6, width), f32)], axis=0).T
    gains = jnp.concatenate([gains, jnp.zeros((width, PIECE - KVW - 8), f32)], axis=1).astype(bf16)

    def fill(at, of_three, own_three, own_one, single):
        for j in range(2):
            for i in range(3):
                right[of_three + i, j * n : (j + 1) * n, :] = own_three[j][i]
                right[of_three + i, (j + 2) * n : (j + 3) * n, :] = threes[j][i]
            right[single, j * n : (j + 1) * n, :] = own_one[j][...]
            right[single, (j + 2) * n : (j + 3) * n, :] = ones[j][...]

    @pl.when(core == 0)
    def _():
        fill(0, 0, queries, keys, 3)

    @pl.when(core == 1)
    def _():
        turned(left.at[1], o_refs)
        fill(0, 1, outs, values, 0)

    for i, m in enumerate(by_turn(core, chip)):
        out = send_ref if i < 2 else keep_ref
        which = jnp.where(m > 0, core, 0)
        out[i % 2] = nn(left[which], right[m]).astype(bf16)
        out[i % 2, :, KVW:] = gains


def grad_attention(sc, a, o, own, got, gains, after):
    n, width = a[0].shape
    out = shape((2, width, PIECE), bf16)
    return pl.pallas_call(
        grad_attention_kernel,
        out_shape=(out, out),
        in_specs=[SCALARS] + [WHOLE] * 24 + [LEFT] * len(after),
        out_specs=(WHOLE,) * 2,
        scratch_shapes=[pltpu.VMEM((2, width, 4 * n), bf16), pltpu.VMEM((4, 4 * n, PIECE), bf16)],
        cost_estimate=BRIEF,
        compiler_params=pltpu.CompilerParams(vmem_limit_bytes=36 << 20),
        name="grad_attention",
    )(sc, *a, *o, *own, *got, *gains, *after)


def lay_kernel(count, sc, *rest):
    mine, other, outs, kept = rest[:4], rest[4:8], rest[-1 - count : -1], rest[-1]
    core, chip = sc[0], sc[1]
    for kind, pieces in ((core, mine), (1 - core, other)):
        for who, piece in zip(whose(kind), pieces):
            kept[kind, chip ^ who] = piece[...]
    n = sum(o.shape[1] for o in outs[: 4 if len(outs) > 2 else 2]) // 8
    cols = [jnp.concatenate([kept[c, m, :, :n].astype(f32) for m in range(4)], axis=1) for c in range(2)]
    if len(outs) == 2:
        outs[0][...] = cols[0]
        outs[1][...] = cols[1]
    else:
        outs[0][...] = cols[0][:, : 3 * n]
        outs[1][...] = cols[0][:, 3 * n :]
        outs[2][...] = cols[1][:, :n]
        outs[3][...] = cols[1][:, n:]
        gains = kept[0, 0, :, n : n + 8].astype(f32) + kept[1, 0, :, n : n + 8].astype(f32)
        outs[4][...] = gains.T[:2]


def lay(sc, mine, other, widths, after):
    rows, n = mine[0].shape
    outs = tuple(shape((rows, w), f32) for w in widths)
    if len(widths) > 2:
        outs += (shape((2, rows), f32),)
    return pl.pallas_call(
        functools.partial(lay_kernel, len(outs)),
        out_shape=outs,
        in_specs=[SCALARS] + [WHOLE] * 8 + [LEFT] * len(after),
        out_specs=(WHOLE,) * len(outs),
        scratch_shapes=[pltpu.VMEM((2, 4, rows, n), bf16)],
        cost_estimate=BRIEF,
        compiler_params=pltpu.CompilerParams(vmem_limit_bytes=24 << 20),
        name="lay",
    )(sc, *mine, *other, *after)


def pick_first_kernel(sc, q_ref, k_ref, v_ref, o_ref, gain_ref, out_ref):
    rows = out_ref.shape[0]
    which = sc[0] * 4 + sc[1]
    pad = jnp.zeros((6, rows), f32)
    gains = jnp.concatenate([gain_ref[...], pad], axis=0).T.astype(bf16)
    rest = jnp.zeros((rows, PIECE - KVW - 8), bf16)
    for at in range(8):

        @pl.when(which == at)
        def _():
            if at in (3, 4):
                piece = (k_ref if at == 3 else v_ref)[...].T
            else:
                source, m = (q_ref, at) if at < 3 else (o_ref, at - 5)
                piece = source[:, m * KVW : (m + 1) * KVW]
            out_ref[...] = jnp.concatenate([piece, gains, rest], axis=1)


def pick_first(sc, query, key, value, out, gains):
    return pl.pallas_call(
        pick_first_kernel,
        out_shape=shape((query.shape[0], PIECE), bf16),
        in_specs=[SCALARS] + [WHOLE] * 5,
        out_specs=WHOLE,
        cost_estimate=BRIEF,
        compiler_params=pltpu.CompilerParams(vmem_limit_bytes=16 << 20),
        name="pick_first",
    )(sc, query, key, value, out, gains)


def pick_kernel(sc, gate, up, *rest):
    out_ref, sem = rest[-2:]
    cols = out_ref.shape[1]
    at = pl.ds(pl.multiple_of(sc[1] * cols, 128), cols)
    for c, source in ((0, gate), (1, up)):

        @pl.when(sc[0] == c)
        def _():
            pltpu.make_async_copy(source.at[:, at], out_ref, sem).start()

    pltpu.make_async_copy(gate.at[:, at], out_ref, sem).wait()


def pick(sc, gate, up, after):
    return pl.pallas_call(
        pick_kernel,
        out_shape=shape((gate.shape[0], gate.shape[1] // 4), bf16),
        in_specs=[SCALARS] + [LEFT] * (2 + len(after)),
        out_specs=WHOLE,
        scratch_shapes=[pltpu.SemaphoreType.DMA],
        cost_estimate=BRIEF,
        compiler_params=pltpu.CompilerParams(vmem_limit_bytes=16 << 20),
        name="pick",
    )(sc, gate, up, *after)


def pick_down_kernel(sc, down, *rest):
    out_ref, sem = rest[-2:]
    half = out_ref.shape[0]
    copy = pltpu.make_async_copy(down.at[pl.ds(pl.multiple_of(sc[0] * half, half), half), :], out_ref, sem)
    copy.start()
    copy.wait()


def pick_down(sc, down, after):
    rows, cols = down.shape
    return pl.pallas_call(
        pick_down_kernel,
        out_shape=shape((rows // 2, cols), bf16),
        in_specs=[SCALARS] + [LEFT] * (1 + len(after)),
        out_specs=WHOLE,
        scratch_shapes=[pltpu.SemaphoreType.DMA],
        cost_estimate=BRIEF,
        compiler_params=pltpu.CompilerParams(vmem_limit_bytes=16 << 20),
        name="pick_down",
    )(sc, down, *after)


def gains_kernel(first_ref, out_ref):
    for j in range(4):
        n = first_ref.shape[1]
        out_ref[:, j * n : (j + 1) * n] = first_ref[j, :, KVW : KVW + 8].astype(f32).T[:2]


def gains_of(first):
    return pl.pallas_call(
        gains_kernel,
        out_shape=shape((2, 4 * first.shape[1]), f32),
        in_specs=[WHOLE],
        out_specs=WHOLE,
        cost_estimate=BRIEF,
        compiler_params=pltpu.CompilerParams(vmem_limit_bytes=16 << 20),
        name="gains",
    )(first)


def stack_kernel(sc, *rest):
    parts, out_ref, sems = rest[:4], rest[-2], rest[-1]
    copies = [pltpu.make_async_copy(p, out_ref.at[sc[2] ^ s], sems.at[s]) for s, p in enumerate(parts)]
    for copy in copies:
        copy.start()
    for copy in copies:
        copy.wait()


def stack(sc, parts, after=()):
    return pl.pallas_call(
        stack_kernel,
        out_shape=shape((4,) + parts[0].shape, parts[0].dtype),
        in_specs=[SCALARS] + [LEFT] * (4 + len(after)),
        out_specs=WHOLE,
        scratch_shapes=[pltpu.SemaphoreType.DMA((4,))],
        cost_estimate=BRIEF,
        compiler_params=pltpu.CompilerParams(vmem_limit_bytes=16 << 20),
        name="stack",
    )(sc, *parts, *after)


def small(kernel, sc, args, outs, scratch, after, name):
    return pl.pallas_call(
        kernel,
        out_shape=tuple(outs),
        in_specs=[SCALARS] + [WHOLE] * len(args) + [LEFT] * len(after),
        out_specs=(WHOLE,) * len(outs),
        scratch_shapes=scratch,
        cost_estimate=BRIEF,
        compiler_params=pltpu.CompilerParams(vmem_limit_bytes=32 << 20),
        name=name,
    )(sc, *args, *after)


def sum_first(sc, keep, got, after):
    def kernel(sc, keep_ref, got_ref, *rest):
        later_ref, own_ref = rest[-2:]
        later_ref[...] = (keep_ref[1].astype(f32) + got_ref[1].astype(f32)).astype(bf16)
        own_ref[...] = keep_ref[0].astype(f32) + got_ref[0].astype(f32)

    block = keep.shape[1:]
    return small(kernel, sc, [keep, got], [shape(block, bf16), shape(block, f32)], [], after, "sum_first")


def sum_second(sc, own, got, after):
    def kernel(sc, own_ref, got_ref, *rest):
        send_ref, keep_ref, total = rest[-3:]
        n = total.shape[1]
        for j in range(4):
            rows = slice(j * n, (j + 1) * n)
            total[j] = own_ref[rows, :] + got_ref[rows, :].astype(f32)
        like = sc[2] & 1
        for h in range(2):
            send_ref[h] = total[2 * h + 1 - like].astype(bf16)
            keep_ref[h] = total[2 * h + like]

    rows, cols = own.shape
    part = (rows // 4, cols)
    outs = [shape((2,) + part, bf16), shape((2,) + part, f32)]
    return small(kernel, sc, [own, got], outs, [pltpu.VMEM((4,) + part, f32)], after, "sum_second")


def sum_third(sc, keep, got, after):
    def kernel(sc, keep_ref, got_ref, *rest):
        send_ref, own_ref = rest[-2:]
        h = sc[2] >> 1
        send_ref[...] = (keep_ref[1 - h] + got_ref[1 - h].astype(f32)).astype(bf16)
        own_ref[...] = keep_ref[h] + got_ref[h].astype(f32)

    part = keep.shape[1:]
    return small(kernel, sc, [keep, got], [shape(part, bf16), shape(part, f32)], [], after, "sum_third")


def down_pair(sc, own, got, after):
    def kernel(sc, own_ref, got_ref, *rest):
        rest[-1][...] = (own_ref[...].astype(f32) + got_ref[...].astype(f32)).astype(bf16)

    return small(kernel, sc, [own, got], [shape(own.shape, bf16)], [], after, "down_pair")[0]


def down_ring(sc, own, got, after):
    def kernel(sc, own_ref, got_ref, *rest):
        give_ref, keep_ref = rest[-2:]
        half = give_ref.shape[0]
        for out, c in ((give_ref, 1 - sc[0]), (keep_ref, sc[0])):
            rows = pl.ds(pl.multiple_of(c * half, half), half)
            out[...] = (own_ref[rows, :].astype(f32) + got_ref[rows, :].astype(f32)).astype(bf16)

    rows, cols = own.shape
    half = shape((rows // 2, cols), bf16)
    return small(kernel, sc, [own, got], [half, half], [], after, "down_ring")


def down_split(sc, keep, given, after):
    def kernel(sc, keep_ref, given_ref, *rest):
        send_ref, kept_ref, total = rest[-3:]
        n = total.shape[1]
        owner = (sc[2] >> 1) == sc[0]
        for m in range(4):
            rows = slice(m * n, (m + 1) * n)
            total[m] = jnp.where(owner, keep_ref[rows, :].astype(f32), given_ref[rows, :].astype(f32))
        for i, m in enumerate(by_turn(sc[0], sc[1])):
            out = send_ref if i < 2 else kept_ref
            out[i % 2] = total[m].astype(bf16)

    rows, cols = keep.shape
    out = shape((2, rows // 4, cols), bf16)
    return small(kernel, sc, [keep, given], [out, out], [pltpu.VMEM((4, rows // 4, cols), f32)], after, "down_split")


def sum_two(sc, own, got, after):
    def kernel(sc, own_ref, got_ref, *rest):
        rest[-1][...] = (own_ref[...] + got_ref[...].astype(f32)).astype(bf16)

    return small(kernel, sc, [own, got], [shape(own.shape, bf16)], [], after, "sum_two")[0]


def lay_down(sc, mine, other, after):
    def kernel(sc, *rest):
        out_ref, total = rest[-2:]
        n = total.shape[2]
        for kind, pieces in ((sc[0], rest[:4]), (1 - sc[0], rest[4:8])):
            for who, piece in zip(whose(kind), pieces):
                total[kind, sc[1] ^ who] = piece[...].astype(f32)
        for c in range(2):
            for m in range(4):
                at = (c * 4 + m) * n
                out_ref[at : at + n, :] = total[c, m]

    n, cols = mine[0].shape
    return small(kernel, sc, [*mine, *other], [shape((8 * n, cols), f32)], [pltpu.VMEM((2, 4, n, cols), f32)], after, "lay_down")[0]


def hold(value, after):
    return pl.pallas_call(
        lambda *refs: None,
        out_shape=shape(value.shape, value.dtype),
        in_specs=[LEFT] * (1 + len(after)),
        out_specs=LEFT,
        input_output_aliases={0: 0},
        cost_estimate=BRIEF,
        compiler_params=pltpu.CompilerParams(vmem_limit_bytes=1 << 20),
        name="hold",
    )(value, *after)


def far_sum(sc, far, near, after):
    def kernel(sc, far_ref, near_ref, *rest):
        rest[-1][...] = (far_ref[...] + jnp.where(sc[0] == 1, near_ref[...].astype(f32), 0.0)).astype(bf16)

    return small(kernel, sc, [far, near], [shape(far.shape, bf16)], [], after, "far_sum")[0]


CORE, SIDE, BACK = 1, 2, 4
rope_base = 10000.0
RUNS = 2


def flip(value, bit, bit1=None):
    count = lax.axis_size("dp")
    bits = (bit, bit if bit1 is None else bit1)
    return lax.ppermute(value, "dp", [(i, i ^ bits[i & 1]) for i in range(count)])


def flip_z(value, bit, where=lambda d, z: True):
    count, depth = lax.axis_size("dp"), lax.axis_size("fsdp")
    pairs = [(d * depth + z, d * depth + (z ^ bit)) for d in range(count) for z in range(depth) if where(d, z)]
    return lax.ppermute(value, ("dp", "fsdp"), pairs)


def home_to_work(value, back=False):
    count, depth = lax.axis_size("dp"), lax.axis_size("fsdp")
    pairs = []
    for d in range(count):
        for z in range(depth):
            there = (d & ~1) | (z & 1), 2 * (d & 1) + (z >> 1)
            pair = (d * depth + z, there[0] * depth + there[1])
            pairs.append(pair[::-1] if back else pair)
    return lax.ppermute(value, ("dp", "fsdp"), pairs)


def place():
    d, z = lax.axis_index("dp"), lax.axis_index("fsdp")
    return d & 1, (d >> 1) & 3, z


def turns(shard):
    far = flip_z(shard, 2)
    return shard, flip_z(shard, 1), far, flip_z(far, 1)


def plane_gather(piece):
    first, second = flip(piece, SIDE, BACK), flip(piece, BACK, SIDE)
    mine = (piece, first, second, flip(first, BACK, SIDE))
    return mine, tuple(flip(p, CORE) for p in mine)


def window(own):
    core, _, _ = place()
    depth = lax.axis_size("fsdp")
    far = lax.ppermute(own, "fsdp", [(z, z + 1) for z in range(0, depth, 2)])
    near = flip(jnp.where(core == 0, own, far), CORE)
    return far, near, own


def unwindow(sc, far, near, after=()):
    depth = lax.axis_size("fsdp")
    near = flip(near, CORE)
    far = far_sum(sc, far, near, after)
    return near, far, lax.ppermute(far, "fsdp", [(z + 1, z) for z in range(0, depth, 2)])


def over_groups(value):
    bit = 8
    while bit < lax.axis_size("dp"):
        value = (value.astype(f32) + flip(value, bit).astype(f32)).astype(bf16)
        bit *= 2
    return value


def spread(piece):
    return piece, flip(piece, SIDE, BACK), flip(piece, BACK, SIDE), flip(piece, SIDE | BACK)


def across(pieces):
    return tuple(flip(p, CORE) for p in pieces)


def body(tokens, segment_ids, attn_gain, query_weight, key_weight, value_weight, out_weight, ffn_gain, gate_weight, up_weight, down_weight, cotangent):
    core, chip, z = place()
    sc = jnp.stack([core, chip, z]).astype(jnp.int32)
    _, stretch, width = tokens.shape
    rows, depth = query_weight.shape[0], lax.axis_size("fsdp")
    block = 2 * (z & 1) + core
    positions = (block * stretch + jnp.arange(stretch)).astype(f32)
    freq = rope_base ** (-2.0 * jnp.arange(HEAD_DIM // 2, dtype=f32) / HEAD_DIM)
    angle = freq[:, None] * positions[None, :]
    cos, sin = jnp.cos(angle), jnp.sin(angle)

    gains = jnp.stack([attn_gain, ffn_gain]).astype(f32)
    parts_a = turns(pick_first(sc, query_weight, key_weight.T, value_weight.T, out_weight, gains))
    ids = jnp.broadcast_to((segment_ids[0] + 1).astype(bf16), (IDS, stretch))
    tokens = home_to_work(jnp.concatenate([tokens[0].T, ids]))
    piece_b = pick(sc, gate_weight, up_weight, parts_a[1:2])
    parts_b = turns(piece_b)
    whole_a = stack(sc, parts_a, [piece_b])
    gains = gains_of(whole_a)
    gain_a, gain_f = gains[:1], gains[1:]
    wa = plane_gather(whole_a.reshape(depth * rows, PIECE))
    whole_b = stack(sc, parts_b, [wa[0][1], wa[0][2]]).reshape(depth * rows, piece_b.shape[1])
    wb = plane_gather(whole_b)
    piece_d = pick_down(sc, down_weight.T, [whole_b])

    h_0, a0, q0, own = pre(sc, tokens, gain_a, cos, sin, *wa, [wb[0][1], wb[0][2], piece_d])
    kv0 = window(own)
    far_d = hold(flip_z(piece_d, 2), [kv0[1], wb[0][3]])
    parts_d = piece_d, flip_z(piece_d, 1), far_d, flip_z(far_d, 1)
    o0, lse0 = attend(q0, kv0)
    whole_d = stack(sc, parts_d, [o0])
    weights = wa, wb, (whole_d, flip(whole_d, CORE))
    mixed0, h1_0, b0, gate0, up0, z0, h_1, a1, q1, own = post(False, sc, o0, h_0, gain_f, gain_a, cos, sin, own, *weights)
    kv1 = window(own)
    across_0 = across((a0, b0, mixed0))
    o1, lse1 = attend(q1, kv1, across_0)
    cot = home_to_work(hold(cotangent[0].T, [o1]))
    mixed1, h1_1, b1, gate1, up1, z1, output = post(True, sc, o1, h_1, gain_f, gain_a, cos, sin, own, *weights)
    output = home_to_work(output, back=True)
    across_1 = across((a1, b1, mixed1))

    gb1, act1, away1, zk1, zs1, g1, p1, dgain_f1, do = back(True, False, sc, weights, [cot], [gate1, up1, h1_1, gain_f, z1])
    across_2 = across((gb1, away1, zs1))
    dq1, three1, far, near, own = attend_back(sc, p1, q1, kv1, lse1, do, cos, sin, [output, *across_1])
    near, _, far = unwindow(sc, far, near)
    (three1,) = across((three1,))
    tail = [g1, dq1, own, near, far, h_1, gain_a, cos, sin]
    dk1, dv1, one1, dgain_a1, gb0, act0, away0, zk0, zs0, g1, p0, dgain_f0, do = back(False, False, sc, weights, tail, [gate0, up0, h1_0, gain_f, z0], [three1, *across_2])

    away0, gb0_, zs0, one1 = across((away0, gb0, zs0, one1))
    dq0, three0, far, near, own = attend_back(sc, p0, q0, kv0, lse0, do, cos, sin, [one1])
    near, down_far, far = unwindow(sc, far, near)
    send_b, keep_b = grad_ffn(sc, [b1, b0, across_1[1], across_0[1]], [act1, act0, across_2[1], away0], [down_far])
    got_b = flip(send_b, SIDE, BACK)
    like_d, unlike_d = grad_down(sc, [gb1, gb0, across_2[0], gb0_], [zk1, zk0, across_2[2], zs0], [send_b])
    got_d = flip_z(unlike_d, 1)
    (three0,) = across((three0,))
    tail = [g1, dq0, own, near, far, h_0, gain_a, cos, sin]
    dk0, dv0, one0, dgain_a0, grad_tokens = back(False, True, sc, weights, tail, None, [like_d, three0])

    own = [dq1, dq0, dk1, dk0, dv1, dv0, p1, p0]
    got = [three1, three0, one1, flip(one0, CORE)]
    send_a, keep_a = grad_attention(sc, [a1, a0, across_1[0], across_0[0]], [mixed1, mixed0, across_1[2], across_0[2]], own, got, [dgain_a1, dgain_a0, dgain_f1, dgain_f0], [])
    got_a = flip(send_a, SIDE, BACK)
    later_b, own_b = sum_first(sc, keep_b, got_b, [send_a])
    more_b = flip(later_b, BACK, SIDE)
    pair_d = down_pair(sc, like_d, got_d, [later_b])
    got_d = flip_z(pair_d, 2, lambda d, z: (z >> 1) != (d & 1))
    later_a, own_a = sum_first(sc, keep_a, got_a, [pair_d])
    more_a = flip(later_a, BACK, SIDE)
    send_b, ring_b = sum_second(sc, own_b, more_b, [later_a])
    got_b = flip_z(send_b, 1)
    send_a, ring_a = sum_second(sc, own_a, more_a, [send_b])
    got_a = flip_z(send_a, 1)
    send_b, ring_b = sum_third(sc, ring_b, got_b, [send_a])
    got_b = flip_z(send_b, 2)
    give, keep = down_ring(sc, pair_d, got_d, [send_b])
    given = flip(give, CORE)
    send_a, ring_a = sum_third(sc, ring_a, got_a, [give])
    got_a = flip_z(send_a, 2)
    send_d, keep_d = down_split(sc, keep, given, [send_a])
    got_d = flip(send_d, SIDE, BACK)
    piece_b = over_groups(sum_two(sc, ring_b, got_b, [send_d]))
    all_b = spread(piece_b)
    later_d, own_d = sum_first(sc, keep_d, got_d, [piece_b])
    more_d = flip(later_d, BACK, SIDE)
    piece_a = over_groups(sum_two(sc, ring_a, got_a, [later_d]))
    all_a = spread(piece_a)
    piece_d = over_groups(sum_two(sc, own_d, more_d, [piece_a]))
    grad_gate, grad_up = lay(sc, all_b, across(all_b), (gate_weight.shape[1],) * 2, [piece_d])
    all_d = spread(piece_d)
    grad_query, grad_key, grad_value, grad_out, dgains = lay(sc, all_a, across(all_a), (width, KVW, KVW, width), [grad_gate])
    grad_down_ = lay_down(sc, all_d, across(all_d), [grad_query])
    grad_tokens = home_to_work(hold(grad_tokens, [piece_b]), back=True)
    grad_tokens, output = grad_tokens.astype(f32).T, output.T
    return (output[None], grad_tokens[None], dgains[0], grad_query, grad_key, grad_value, grad_out, dgains[1], grad_gate, grad_up, grad_down_.T)


def solution(mesh):
    wide, rows, shard = P("dp", "fsdp", None), P("dp", "fsdp"), P("fsdp", None)
    in_specs = (wide, rows, P("fsdp"), shard, shard, shard, shard, P("fsdp"), shard, shard, shard, wide)
    out_specs = (wide, wide, P("fsdp"), shard, shard, shard, shard, P("fsdp"), shard, shard, shard)
    return jax.shard_map(body, mesh=mesh, in_specs=in_specs, out_specs=out_specs, check_vma=False)
```

```python
import functools
import jax
import jax.numpy as jnp
from jax import lax
from jax.sharding import PartitionSpec as P
from jax.experimental import pallas as pl
from jax.experimental.pallas import tpu as pltpu

f32, bf16 = jnp.float32, jnp.bfloat16
eps = 1e-05
HEADS, KV_HEADS, HEAD_DIM, GROUP, KVW = 15, 5, 64, 3, 320
IDS = 16
PIECE = 384
LIMIT = 58 << 20
WHOLE = pl.BlockSpec(memory_space=pltpu.VMEM)
LEFT = pl.BlockSpec(memory_space=pl.ANY)
SCALARS = pl.BlockSpec(memory_space=pltpu.SMEM)
BRIEF = pl.CostEstimate(flops=1024, bytes_accessed=1024, transcendentals=0)


def contract(a, b, i, j):
    return lax.dot_general(a, b, (((i,), (j,)), ((), ())), preferred_element_type=f32)


def nn(a, b):
    return contract(a, b, 1, 0)


def nt(a, b):
    return contract(a, b, 1, 1)


def tn(a, b):
    return contract(a, b, 0, 0)


def whose(core):
    return 0, 1 + core, 2 - core, 3


def fetch(mine, other, kept, sems, core, chip):
    for kind, pieces in ((core, mine), (1 - core, other)):
        for who, piece in zip(whose(kind), pieces):
            at = chip ^ who
            pltpu.make_async_copy(piece, kept.at[kind, at], sems.at[kind, at]).start()


def arrived(kept, sems, *at):
    pltpu.make_async_copy(kept.at[at], kept.at[at], sems.at[at]).wait()


def normed(x, gain):
    return x * lax.rsqrt(jnp.mean(x * x, axis=-1, keepdims=True) + eps) * gain


def norm_back(x, gain, grad):
    r = lax.rsqrt(jnp.mean(x * x, axis=-1, keepdims=True) + eps)
    hat = x * r
    scaled = grad * gain
    dx = r * (scaled - hat * jnp.mean(scaled * hat, axis=-1, keepdims=True))
    return dx, jnp.sum(grad * hat, axis=0, keepdims=True)


def widened(x):
    return jnp.concatenate([x, jnp.zeros((x.shape[0], PIECE - x.shape[1]), x.dtype)], axis=1)


def rope(u, cos, sin, back):
    heads = u.shape[0] // HEAD_DIM
    half = HEAD_DIM // 2
    out = []
    for h in range(heads):
        u1, u2 = u[h * HEAD_DIM : h * HEAD_DIM + half], u[h * HEAD_DIM + half : (h + 1) * HEAD_DIM]
        if back:
            out += [u1 * cos + u2 * sin, u2 * cos - u1 * sin]
        else:
            out += [u1 * cos - u2 * sin, u2 * cos + u1 * sin]
    return jnp.concatenate(out, axis=0)


def project(state, gain_ref, cos_ref, sin_ref, ids, kept, sems, a_ref, q_ref, kv_ref):
    a = normed(state, gain_ref[...]).astype(bf16)
    a_ref[...] = a
    cos, sin = cos_ref[...], sin_ref[...]
    arrived(kept, sems, 0, 3)
    kv_ref[:KVW, :] = rope(nn(a, kept[0, 3, :, :KVW]).T, cos, sin, False).astype(bf16)
    arrived(kept, sems, 1, 0)
    kv_ref[2 * KVW :, :] = ids
    kv_ref[KVW : 2 * KVW, :] = nn(a, kept[1, 0, :, :KVW]).T.astype(bf16)
    for m in range(3):
        arrived(kept, sems, 0, m)
        q_ref[pl.ds(m * KVW, KVW), :] = rope(nn(a, kept[0, m, :, :KVW]).T, cos, sin, False).astype(bf16)


def pre_kernel(sc, ht_ref, gain_ref, cos_ref, sin_ref, *rest):
    width = ht_ref.shape[0] - IDS
    mine, other = rest[:4], rest[4:8]
    h_ref, a_ref, q_ref, kv_ref, kept, sems = rest[-6:]
    core, chip = sc[0], sc[1]
    fetch(mine, other, kept, sems, core, chip)
    h = ht_ref[:width, :].T
    h_ref[...] = h
    project(h.astype(f32), gain_ref, cos_ref, sin_ref, ht_ref[width:, :], kept, sems, a_ref, q_ref, kv_ref)
    for m in range(1, 4):
        arrived(kept, sems, 1, m)


def scratch_a(width):
    return [pltpu.VMEM((2, 4, width, PIECE), bf16), pltpu.SemaphoreType.DMA((2, 4))]


def shape(s, d):
    return jax.ShapeDtypeStruct(s, d)


def pre(sc, ht, gain, cos, sin, mine_a, other_a, after):
    width, n = ht.shape[0] - IDS, ht.shape[1]
    return pl.pallas_call(
        pre_kernel,
        out_shape=(shape((n, width), bf16), shape((n, width), bf16), shape((width, n), bf16), shape((2 * KVW + IDS, n), bf16)),
        in_specs=[SCALARS] + [WHOLE] * 4 + [LEFT] * (8 + len(after)),
        out_specs=(WHOLE,) * 4,
        scratch_shapes=scratch_a(width),
        cost_estimate=BRIEF,
        compiler_params=pltpu.CompilerParams(vmem_limit_bytes=LIMIT),
        name="pre",
    )(sc, ht, gain, cos, sin, *mine_a, *other_a, *after)


def bias_of(kv):
    keys, n = kv.shape[1], kv.shape[1] // 3
    ids = kv[2 * KVW :, :].astype(f32)
    seg_k, seg_q = ids.T[:, :1], ids[:1, 2 * n :]
    j = lax.broadcasted_iota(jnp.int32, (keys, n), 0)
    i = lax.broadcasted_iota(jnp.int32, (keys, n), 1) + (keys - n)
    return jnp.where((seg_k == seg_q) & (j <= i), 0.0, -1e30).astype(f32)


def window_of(parts, whole):
    n = parts[0].shape[1]
    for w, part in enumerate(parts):
        whole[:, w * n : (w + 1) * n] = part[...]


def attend_kernel(q_ref, kv0, kv1, kv2, *rest):
    o_ref, lse_ref, bias, kv = rest[-4:]
    window_of((kv0, kv1, kv2), kv)
    bias[...] = bias_of(kv)

    def head(e, _):
        row = pl.multiple_of(e * HEAD_DIM, HEAD_DIM)
        k = kv[pl.ds(row, HEAD_DIM), :]
        v = kv[pl.ds(row + KVW, HEAD_DIM), :]
        for g in range(GROUP):
            at = pl.multiple_of((e * GROUP + g) * HEAD_DIM, HEAD_DIM)
            q = q_ref[pl.ds(at, HEAD_DIM), :]
            s = tn(k, q) * HEAD_DIM ** (-0.5) + bias[...]
            top = jnp.max(s, axis=0, keepdims=True)
            expo = jnp.exp(s - top)
            total = jnp.sum(expo, axis=0, keepdims=True)
            probs = (expo * (1.0 / total)).astype(bf16)
            o_ref[pl.ds(at, HEAD_DIM), :] = nn(v, probs).astype(bf16)
            lse_ref[pl.ds(e * GROUP + g, 1), :] = top + jnp.log(total)
        return 0

    lax.fori_loop(0, KV_HEADS, head, 0)


def attend(q, kvs, after=()):
    width, n = q.shape
    return pl.pallas_call(
        attend_kernel,
        out_shape=(shape((width, n), bf16), shape((HEADS, n), f32)),
        in_specs=[WHOLE] * 4 + [LEFT] * len(after),
        out_specs=(WHOLE,) * 2,
        scratch_shapes=[pltpu.VMEM((3 * n, n), f32), pltpu.VMEM((2 * KVW + IDS, 3 * n), bf16)],
        cost_estimate=BRIEF,
        compiler_params=pltpu.CompilerParams(vmem_limit_bytes=24 << 20),
        name="attend",
    )(q, *kvs, *after)


def attend_back_kernel(sc, p_ref, q_ref, kv0, kv1, kv2, lse_ref, do_ref, cos_ref, sin_ref, *rest):
    dq_ref, three_ref, far_ref, near_ref, own_ref, bias, kv, dqs = rest[-8:]
    n = q_ref.shape[1]
    window_of((kv0, kv1, kv2), kv)
    bias[...] = bias_of(kv)
    scale = HEAD_DIM ** (-0.5)

    def head(e, _):
        row = pl.multiple_of(e * HEAD_DIM, HEAD_DIM)
        k = kv[pl.ds(row, HEAD_DIM), :]
        v = kv[pl.ds(row + KVW, HEAD_DIM), :]
        dk = dv = None
        for g in range(GROUP):
            at = pl.multiple_of((e * GROUP + g) * HEAD_DIM, HEAD_DIM)
            q = q_ref[pl.ds(at, HEAD_DIM), :]
            do = do_ref[pl.ds(at, HEAD_DIM), :]
            s = tn(k, q) * scale + bias[...]
            probs = jnp.exp(s - lse_ref[pl.ds(e * GROUP + g, 1), :])
            dp = tn(v, do)
            inner = jnp.sum(probs * dp, axis=0, keepdims=True)
            ds = (probs * (dp - inner)).astype(bf16)
            dvg, dkg = nt(do, probs.astype(bf16)), nt(q, ds)
            dv, dk = (dvg, dkg) if g == 0 else (dv + dvg, dk + dkg)
            dqs[pl.ds(at, HEAD_DIM), :] = nn(k, ds)
        for at, grad in ((row, dk * scale), (row + KVW, dv)):
            far_ref[pl.ds(at, HEAD_DIM), :] = grad[:, :n]
            near_ref[pl.ds(at, HEAD_DIM), :] = grad[:, n : 2 * n].astype(bf16)
            own_ref[pl.ds(at, HEAD_DIM), :] = grad[:, 2 * n :]
        return 0

    lax.fori_loop(0, KV_HEADS, head, 0)
    cos, sin = cos_ref[...] * scale, sin_ref[...] * scale
    for m in range(3):
        dq = widened(rope(dqs[m * KVW : (m + 1) * KVW, :], cos, sin, True).T.astype(bf16))
        dq_ref[m] = dq
        three_ref[m] = jnp.where(sc[0] == 0, p_ref[m], dq)


def attend_back(sc, p, q, kvs, lse, do, cos, sin, after=()):
    width, n = q.shape
    block = (2 * KVW, n)
    return pl.pallas_call(
        attend_back_kernel,
        out_shape=(shape((3, n, PIECE), bf16), shape((3, n, PIECE), bf16), shape(block, f32), shape(block, bf16), shape(block, f32)),
        in_specs=[SCALARS] + [WHOLE] * 9 + [LEFT] * len(after),
        out_specs=(WHOLE,) * 5,
        scratch_shapes=[pltpu.VMEM((3 * n, n), f32), pltpu.VMEM((2 * KVW + IDS, 3 * n), bf16), pltpu.VMEM((width, n), f32)],
        cost_estimate=BRIEF,
        compiler_params=pltpu.CompilerParams(vmem_limit_bytes=32 << 20),
        name="attend_back",
    )(sc, p, q, *kvs, lse, do, cos, sin, *after)


def fetch_ffn(mine_b, other_b, down, wb, wd, sem_b, sem_d, core, chip):
    fetch(mine_b, other_b, wb, sem_b, core, chip)
    half = down[0].shape[1]
    for c, part in ((core, down[0]), (1 - core, down[1])):
        rows = pl.ds(pl.multiple_of(c * half, half), half)
        pltpu.make_async_copy(part, wd.at[:, rows], sem_d).start()


def arrived_down(wd, sem_d):
    pltpu.make_async_copy(wd, wd, sem_d).wait()


def scratch_ffn(width, n):
    return [
        pltpu.VMEM((2, 4, width, n), bf16),
        pltpu.SemaphoreType.DMA((2, 4)),
        pltpu.VMEM((4, width, n), bf16),
        pltpu.SemaphoreType.DMA,
    ]


def post_kernel(last, sc, ot_ref, h_ref, gain_ref, gain_a, cos_ref, sin_ref, *rest):
    mine_a, other_a, mine_b, other_b = rest[:4], rest[4:8], rest[8:12], rest[12:16]
    down, ids_ref = rest[16:18], rest[18]
    o_ref, h1_ref, b_ref, gate_ref, up_ref, z_ref, next_ref = rest[19:26]
    more, rest = rest[26 : 26 + (0 if last else 3)], rest[26 + (0 if last else 3) :]
    wa, sem_a, wb, sem_b, wd, sem_d = rest
    core, chip = sc[0], sc[1]
    fetch(mine_a, other_a, wa, sem_a, core, chip)
    fetch_ffn(mine_b, other_b, down, wb, wd, sem_b, sem_d, core, chip)
    o = ot_ref[...].T
    o_ref[...] = o
    for m in range(1, 4):
        arrived(wa, sem_a, 1, m)
    h1 = h_ref[...].astype(f32) + jnp.concatenate([nn(o, wa[1, m, :, :KVW]) for m in range(1, 4)], axis=1)
    h1_ref[...] = h1
    b = normed(h1, gain_ref[...]).astype(bf16)
    b_ref[...] = b
    n = wb.shape[3]
    total = h1
    for m in range(4):
        cols = slice(m * n, (m + 1) * n)
        arrived(wb, sem_b, 0, m)
        gate = nn(b, wb[0, m])
        arrived(wb, sem_b, 1, m)
        up = nn(b, wb[1, m])
        gate_ref[:, cols] = gate.astype(bf16)
        up_ref[:, cols] = up.astype(bf16)
        z = (gate / (1.0 + jnp.exp(-gate)) * up).astype(bf16)
        z_ref[:, cols] = z
        if m == 0:
            arrived_down(wd, sem_d)
        total = total + nt(z, wd[m])
    next_ref[...] = total.astype(bf16).T if last else total
    if last:
        arrived(wa, sem_a, 1, 0)
        for m in range(4):
            arrived(wa, sem_a, 0, m)
    else:
        project(total, gain_a, cos_ref, sin_ref, ids_ref[2 * KVW :, :], wa, sem_a, *more)


def post(last, sc, ot, h, gain, gain_a, cos, sin, kv, wa, wb, wd):
    width, n = ot.shape
    hidden = wb[0][0].shape[1] * 4
    outs = [shape((n, width), bf16), shape((n, width), f32), shape((n, width), bf16)] + [shape((n, hidden), bf16)] * 3
    outs += [shape((width, n), bf16) if last else shape((n, width), f32)]
    if not last:
        outs += [shape((n, width), bf16), shape((width, n), bf16), shape((2 * KVW + IDS, n), bf16)]
    return pl.pallas_call(
        functools.partial(post_kernel, last),
        out_shape=tuple(outs),
        in_specs=[SCALARS] + [WHOLE] * 6 + [LEFT] * 18 + [WHOLE],
        out_specs=(WHOLE,) * len(outs),
        scratch_shapes=scratch_a(width) + scratch_ffn(width, hidden // 4),
        cost_estimate=BRIEF,
        compiler_params=pltpu.CompilerParams(vmem_limit_bytes=LIMIT),
        name="post",
    )(sc, ot, h, gain, gain_a, cos, sin, *wa[0], *wa[1], *wb[0], *wb[1], *wd, kv)


def ffn_back(state, core, refs, weights):
    gate_ref, up_ref, h1_ref, gain_ref, z_ref, gb_ref, keep_ref, send_ref, zk_ref, zs_ref, g1_ref, p_ref, dgain_ref, do_ref = refs
    wa, sem_a, wb, sem_b, wd, sem_d = weights
    gb = state.astype(bf16)
    gb_ref[...] = gb
    n = wb.shape[3]
    half = 2 * n
    first = core == 0
    low, high = z_ref[:, :half], z_ref[:, half:]
    zk_ref[...] = jnp.where(first, low, high)
    zs_ref[...] = jnp.where(first, high, low)
    arrived_down(wd, sem_d)
    db = None
    for m in range(4):
        cols = slice(m * n, (m + 1) * n)
        dz = nn(gb, wd[m])
        gate, up = gate_ref[:, cols].astype(f32), up_ref[:, cols].astype(f32)
        sig = 1.0 / (1.0 + jnp.exp(-gate))
        dup = (dz * (gate * sig)).astype(bf16)
        dgate = (dz * up * (sig * (1.0 + gate * (1.0 - sig)))).astype(bf16)
        keep_ref[:, cols] = jnp.where(first, dgate, dup)
        send_ref[:, cols] = jnp.where(first, dup, dgate)
        arrived(wb, sem_b, 0, m)
        part = nt(dgate, wb[0, m])
        arrived(wb, sem_b, 1, m)
        part = part + nt(dup, wb[1, m])
        db = part if m == 0 else db + part
    dx, dgain = norm_back(h1_ref[...], gain_ref[...], db)
    dgain_ref[...] = dgain
    g1 = state + dx
    g1_ref[...] = g1
    low = g1.astype(bf16)
    do = None
    for p in range(3):
        part = low[:, p * KVW : (p + 1) * KVW]
        p_ref[p] = widened(part)
        arrived(wa, sem_a, 1, p + 1)
        part = nt(wa[1, p + 1, :, :KVW], part)
        do = part if p == 0 else do + part
    do_ref[...] = do.astype(bf16)


def finish_a(wa, sem_a, *left):
    for at in left:
        arrived(wa, sem_a, *at)


def query_back(dq_ref, wa, sem_a):
    da = None
    for m in range(3):
        arrived(wa, sem_a, 0, m)
        part = nt(dq_ref[m, :, :KVW], wa[0, m, :, :KVW])
        da = part if m == 0 else da + part
    return da


def project_back(da, own_ref, near_ref, far_ref, core, cos_ref, sin_ref, dk_ref, dv_ref, one_ref, h, gain, wa, sem_a):
    cos, sin = cos_ref[...], sin_ref[...]
    grad = own_ref[...] + far_ref[...].astype(f32) + jnp.where(core == 0, near_ref[...].astype(f32), 0.0)
    dk = rope(grad[:KVW], cos, sin, True).T.astype(bf16)
    dv = grad[KVW:].T.astype(bf16)
    dk_ref[...] = widened(dk)
    dv_ref[...] = widened(dv)
    one_ref[...] = widened(jnp.where(core == 0, dv, dk))
    arrived(wa, sem_a, 0, 3)
    arrived(wa, sem_a, 1, 0)
    da = da + nt(dk, wa[0, 3, :, :KVW]) + nt(dv, wa[1, 0, :, :KVW])
    return norm_back(h, gain, da)


def back_kernel(start, end, after, sc, *rest):
    rest = list(rest)

    def take(n):
        out = rest[:n]
        del rest[:n]
        return out

    core, chip = sc[0], sc[1]
    mine_a, other_a = take(4), take(4)
    if not end:
        mine_b, other_b = take(4), take(4)
        down = take(2)
    if start:
        (g_ref,) = take(1)
    else:
        g1_in, dq_ref, own_ref, near_ref, far_ref, h_ref, gain_a, cos_ref, sin_ref = take(9)
    if not end:
        ins = take(5)
    take(after)
    if not start:
        dk_ref, dv_ref, one_ref, dgain_a = take(4)
    if end:
        (g_out,) = take(1)
    else:
        outs = take(9)
    wa, sem_a = take(2)
    fetch(mine_a, other_a, wa, sem_a, core, chip)
    if not end:
        wb, sem_b, wd, sem_d = take(4)
        fetch_ffn(mine_b, other_b, down, wb, wd, sem_b, sem_d, core, chip)
    if start:
        state = g_ref[...].T.astype(f32)
    else:
        da = query_back(dq_ref, wa, sem_a)
        dx, dgain = project_back(da, own_ref, near_ref, far_ref, core, cos_ref, sin_ref, dk_ref, dv_ref, one_ref, h_ref[...].astype(f32), gain_a[...], wa, sem_a)
        dgain_a[...] = dgain
        state = g1_in[...] + dx
    if end:
        g_out[...] = state.astype(bf16).T
        finish_a(wa, sem_a, (1, 1), (1, 2), (1, 3))
    else:
        ffn_back(state, core, (*ins, *outs), (wa, sem_a, wb, sem_b, wd, sem_d))
        if start:
            finish_a(wa, sem_a, (1, 0), (0, 0), (0, 1), (0, 2), (0, 3))


def back(start, end, sc, weights, tail, ffn, after=()):
    wa, wb, wd = weights
    width = wa[0][0].shape[0]
    args = [sc, *wa[0], *wa[1]]
    specs = [SCALARS] + [LEFT] * 8
    scratch = scratch_a(width)
    if not end:
        args += [*wb[0], *wb[1], *wd]
        specs += [LEFT] * 10
        scratch += scratch_ffn(width, wb[0][0].shape[1])
    args += list(tail)
    specs += [WHOLE] * len(tail)
    n = tail[0].shape[1 if start else 0]
    outs = []
    if not end:
        args += list(ffn)
        specs += [WHOLE] * len(ffn)
    if not start:
        outs += [shape((n, PIECE), bf16)] * 3 + [shape((1, width), f32)]
    if end:
        outs += [shape((width, n), bf16)]
    else:
        hidden = ffn[0].shape[1]
        outs += [shape((n, width), bf16), shape((n, hidden), bf16), shape((n, hidden), bf16), shape((n, hidden // 2), bf16), shape((n, hidden // 2), bf16)]
        outs += [shape((n, width), f32), shape((3, n, PIECE), bf16), shape((1, width), f32), shape((width, n), bf16)]
    args += list(after)
    specs += [LEFT] * len(after)
    return pl.pallas_call(
        functools.partial(back_kernel, start, end, len(after)),
        out_shape=tuple(outs),
        in_specs=specs,
        out_specs=(WHOLE,) * len(outs),
        scratch_shapes=scratch,
        cost_estimate=BRIEF,
        compiler_params=pltpu.CompilerParams(vmem_limit_bytes=LIMIT),
        name="back_end" if end else ("back_start" if start else "back_join"),
    )(*args)


def by_turn(core, chip):
    one = 1 + core
    return chip ^ one, chip ^ 3, chip, chip ^ (3 - one)


def turned(dst, blocks):
    n = blocks[0].shape[0]
    for i, block in enumerate(blocks):
        dst[:, i * n : (i + 1) * n] = block[...].T


def grad_ffn_kernel(sc, *rest):
    lefts, rights = rest[:4], rest[4:8]
    send_ref, keep_ref, left, right = rest[-4:]
    core, chip = sc[0], sc[1]
    n, cols = rights[0].shape[0], right.shape[1]
    turned(left, lefts)
    for i, m in enumerate(by_turn(core, chip)):
        at = pl.multiple_of(m * cols, 128)
        for j, block in enumerate(rights):
            right[j * n : (j + 1) * n, :] = block[:, pl.ds(at, cols)]
        out = send_ref if i < 2 else keep_ref
        out[i % 2] = nn(left[...], right[...]).astype(bf16)


def grad_ffn(sc, lefts, rights, after):
    n, width = lefts[0].shape
    cols = rights[0].shape[1] // 4
    out = shape((2, width, cols), bf16)
    return pl.pallas_call(
        grad_ffn_kernel,
        out_shape=(out, out),
        in_specs=[SCALARS] + [WHOLE] * 8 + [LEFT] * len(after),
        out_specs=(WHOLE,) * 2,
        scratch_shapes=[pltpu.VMEM((width, 4 * n), bf16), pltpu.VMEM((4 * n, cols), bf16)],
        cost_estimate=BRIEF,
        compiler_params=pltpu.CompilerParams(vmem_limit_bytes=LIMIT),
        name="grad_ffn",
    )(sc, *lefts, *rights, *after)


def grad_down_kernel(sc, *rest):
    lefts, rights = rest[:4], rest[4:8]
    outs, left, right = rest[-4:-2], rest[-2], rest[-1]
    n, cols = rights[0].shape[0], right.shape[1]
    turned(left, lefts)
    for i, out in enumerate(outs):
        at = pl.multiple_of(((sc[2] + i) & 1) * cols, 128)
        for j, block in enumerate(rights):
            right[j * n : (j + 1) * n, :] = block[:, pl.ds(at, cols)]
        out[...] = nn(left[...], right[...]).astype(bf16)


def grad_down(sc, lefts, rights, after):
    n, width = lefts[0].shape
    cols = rights[0].shape[1] // 2
    return pl.pallas_call(
        grad_down_kernel,
        out_shape=(shape((width, cols), bf16),) * 2,
        in_specs=[SCALARS] + [WHOLE] * 8 + [LEFT] * len(after),
        out_specs=(WHOLE,) * 2,
        scratch_shapes=[pltpu.VMEM((width, 4 * n), bf16), pltpu.VMEM((4 * n, cols), bf16)],
        cost_estimate=BRIEF,
        compiler_params=pltpu.CompilerParams(vmem_limit_bytes=LIMIT),
        name="grad_down",
    )(sc, *lefts, *rights, *after)


def grad_attention_kernel(sc, *rest):
    a_refs, o_refs, rest = rest[:4], rest[4:8], rest[8:]
    queries, keys, values, outs, threes, ones = (rest[i : i + 2] for i in range(0, 12, 2))
    gain_a, gain_f = (rest[i : i + 2] for i in (12, 14))
    send_ref, keep_ref, left, right = rest[-4:]
    core, chip = sc[0], sc[1]
    n, width = a_refs[0].shape
    turned(left.at[0], a_refs)
    gains = [g[0][...] + g[1][...] for g in (gain_a, gain_f)]
    gains = jnp.concatenate([*gains, jnp.zeros((6, width), f32)], axis=0).T
    gains = jnp.concatenate([gains, jnp.zeros((width, PIECE - KVW - 8), f32)], axis=1).astype(bf16)

    def fill(at, of_three, own_three, own_one, single):
        for j in range(2):
            for i in range(3):
                right[of_three + i, j * n : (j + 1) * n, :] = own_three[j][i]
                right[of_three + i, (j + 2) * n : (j + 3) * n, :] = threes[j][i]
            right[single, j * n : (j + 1) * n, :] = own_one[j][...]
            right[single, (j + 2) * n : (j + 3) * n, :] = ones[j][...]

    @pl.when(core == 0)
    def _():
        fill(0, 0, queries, keys, 3)

    @pl.when(core == 1)
    def _():
        turned(left.at[1], o_refs)
        fill(0, 1, outs, values, 0)

    for i, m in enumerate(by_turn(core, chip)):
        out = send_ref if i < 2 else keep_ref
        which = jnp.where(m > 0, core, 0)
        out[i % 2] = nn(left[which], right[m]).astype(bf16)
        out[i % 2, :, KVW:] = gains


def grad_attention(sc, a, o, own, got, gains, after):
    n, width = a[0].shape
    out = shape((2, width, PIECE), bf16)
    return pl.pallas_call(
        grad_attention_kernel,
        out_shape=(out, out),
        in_specs=[SCALARS] + [WHOLE] * 24 + [LEFT] * len(after),
        out_specs=(WHOLE,) * 2,
        scratch_shapes=[pltpu.VMEM((2, width, 4 * n), bf16), pltpu.VMEM((4, 4 * n, PIECE), bf16)],
        cost_estimate=BRIEF,
        compiler_params=pltpu.CompilerParams(vmem_limit_bytes=LIMIT),
        name="grad_attention",
    )(sc, *a, *o, *own, *got, *gains, *after)


def lay_kernel(count, sc, *rest):
    mine, other, outs, kept = rest[:4], rest[4:8], rest[-1 - count : -1], rest[-1]
    core, chip = sc[0], sc[1]
    for kind, pieces in ((core, mine), (1 - core, other)):
        for who, piece in zip(whose(kind), pieces):
            kept[kind, chip ^ who] = piece[...]
    n = sum(o.shape[1] for o in outs[: 4 if len(outs) > 2 else 2]) // 8
    cols = [jnp.concatenate([kept[c, m, :, :n].astype(f32) for m in range(4)], axis=1) for c in range(2)]
    if len(outs) == 2:
        outs[0][...] = cols[0]
        outs[1][...] = cols[1]
    else:
        outs[0][...] = cols[0][:, : 3 * n]
        outs[1][...] = cols[0][:, 3 * n :]
        outs[2][...] = cols[1][:, :n]
        outs[3][...] = cols[1][:, n:]
        gains = kept[0, 0, :, n : n + 8].astype(f32) + kept[1, 0, :, n : n + 8].astype(f32)
        outs[4][...] = gains.T[:2]


def lay(sc, mine, other, widths, after):
    rows, n = mine[0].shape
    outs = tuple(shape((rows, w), f32) for w in widths)
    if len(widths) > 2:
        outs += (shape((2, rows), f32),)
    return pl.pallas_call(
        functools.partial(lay_kernel, len(outs)),
        out_shape=outs,
        in_specs=[SCALARS] + [WHOLE] * 8 + [LEFT] * len(after),
        out_specs=(WHOLE,) * len(outs),
        scratch_shapes=[pltpu.VMEM((2, 4, rows, n), bf16)],
        cost_estimate=BRIEF,
        compiler_params=pltpu.CompilerParams(vmem_limit_bytes=24 << 20),
        name="lay",
    )(sc, *mine, *other, *after)


def pick_first_kernel(sc, q_ref, k_ref, v_ref, o_ref, gain_ref, out_ref):
    rows = out_ref.shape[0]
    which = sc[0] * 4 + sc[1]
    pad = jnp.zeros((6, rows), f32)
    gains = jnp.concatenate([gain_ref[...], pad], axis=0).T.astype(bf16)
    rest = jnp.zeros((rows, PIECE - KVW - 8), bf16)
    for at in range(8):

        @pl.when(which == at)
        def _():
            if at in (3, 4):
                piece = (k_ref if at == 3 else v_ref)[...].T
            else:
                source, m = (q_ref, at) if at < 3 else (o_ref, at - 5)
                piece = source[:, m * KVW : (m + 1) * KVW]
            out_ref[...] = jnp.concatenate([piece, gains, rest], axis=1)


def pick_first(sc, query, key, value, out, gains):
    return pl.pallas_call(
        pick_first_kernel,
        out_shape=shape((query.shape[0], PIECE), bf16),
        in_specs=[SCALARS] + [WHOLE] * 5,
        out_specs=WHOLE,
        cost_estimate=BRIEF,
        compiler_params=pltpu.CompilerParams(vmem_limit_bytes=16 << 20),
        name="pick_first",
    )(sc, query, key, value, out, gains)


def pick_kernel(sc, gate, up, *rest):
    out_ref, sem = rest[-2:]
    cols = out_ref.shape[1]
    at = pl.ds(pl.multiple_of(sc[1] * cols, 128), cols)
    for c, source in ((0, gate), (1, up)):

        @pl.when(sc[0] == c)
        def _():
            pltpu.make_async_copy(source.at[:, at], out_ref, sem).start()

    pltpu.make_async_copy(gate.at[:, at], out_ref, sem).wait()


def pick(sc, gate, up, after):
    return pl.pallas_call(
        pick_kernel,
        out_shape=shape((gate.shape[0], gate.shape[1] // 4), bf16),
        in_specs=[SCALARS] + [LEFT] * (2 + len(after)),
        out_specs=WHOLE,
        scratch_shapes=[pltpu.SemaphoreType.DMA],
        cost_estimate=BRIEF,
        compiler_params=pltpu.CompilerParams(vmem_limit_bytes=16 << 20),
        name="pick",
    )(sc, gate, up, *after)


def pick_down_kernel(sc, down, *rest):
    out_ref, sem = rest[-2:]
    half = out_ref.shape[0]
    copy = pltpu.make_async_copy(down.at[pl.ds(pl.multiple_of(sc[0] * half, half), half), :], out_ref, sem)
    copy.start()
    copy.wait()


def pick_down(sc, down, after):
    rows, cols = down.shape
    return pl.pallas_call(
        pick_down_kernel,
        out_shape=shape((rows // 2, cols), bf16),
        in_specs=[SCALARS] + [LEFT] * (1 + len(after)),
        out_specs=WHOLE,
        scratch_shapes=[pltpu.SemaphoreType.DMA],
        cost_estimate=BRIEF,
        compiler_params=pltpu.CompilerParams(vmem_limit_bytes=16 << 20),
        name="pick_down",
    )(sc, down, *after)


def gains_kernel(first_ref, out_ref):
    for j in range(4):
        n = first_ref.shape[1]
        out_ref[:, j * n : (j + 1) * n] = first_ref[j, :, KVW : KVW + 8].astype(f32).T[:2]


def gains_of(first):
    return pl.pallas_call(
        gains_kernel,
        out_shape=shape((2, 4 * first.shape[1]), f32),
        in_specs=[WHOLE],
        out_specs=WHOLE,
        cost_estimate=BRIEF,
        compiler_params=pltpu.CompilerParams(vmem_limit_bytes=16 << 20),
        name="gains",
    )(first)


def stack_kernel(sc, *rest):
    parts, out_ref, sems = rest[:4], rest[-2], rest[-1]
    copies = [pltpu.make_async_copy(p, out_ref.at[sc[2] ^ s], sems.at[s]) for s, p in enumerate(parts)]
    for copy in copies:
        copy.start()
    for copy in copies:
        copy.wait()


def stack(sc, parts, after=()):
    return pl.pallas_call(
        stack_kernel,
        out_shape=shape((4,) + parts[0].shape, parts[0].dtype),
        in_specs=[SCALARS] + [LEFT] * (4 + len(after)),
        out_specs=WHOLE,
        scratch_shapes=[pltpu.SemaphoreType.DMA((4,))],
        cost_estimate=BRIEF,
        compiler_params=pltpu.CompilerParams(vmem_limit_bytes=16 << 20),
        name="stack",
    )(sc, *parts, *after)


def small(kernel, sc, args, outs, scratch, after, name):
    return pl.pallas_call(
        kernel,
        out_shape=tuple(outs),
        in_specs=[SCALARS] + [WHOLE] * len(args) + [LEFT] * len(after),
        out_specs=(WHOLE,) * len(outs),
        scratch_shapes=scratch,
        cost_estimate=BRIEF,
        compiler_params=pltpu.CompilerParams(vmem_limit_bytes=32 << 20),
        name=name,
    )(sc, *args, *after)


def sum_first(sc, keep, got, after):
    def kernel(sc, keep_ref, got_ref, *rest):
        later_ref, own_ref = rest[-2:]
        later_ref[...] = (keep_ref[1].astype(f32) + got_ref[1].astype(f32)).astype(bf16)
        own_ref[...] = keep_ref[0].astype(f32) + got_ref[0].astype(f32)

    block = keep.shape[1:]
    return small(kernel, sc, [keep, got], [shape(block, bf16), shape(block, f32)], [], after, "sum_first")


def sum_second(sc, own, got, after):
    def kernel(sc, own_ref, got_ref, *rest):
        send_ref, keep_ref, total = rest[-3:]
        n = total.shape[1]
        for j in range(4):
            rows = slice(j * n, (j + 1) * n)
            total[j] = own_ref[rows, :] + got_ref[rows, :].astype(f32)
        like = sc[2] & 1
        for h in range(2):
            send_ref[h] = total[2 * h + 1 - like].astype(bf16)
            keep_ref[h] = total[2 * h + like]

    rows, cols = own.shape
    part = (rows // 4, cols)
    outs = [shape((2,) + part, bf16), shape((2,) + part, f32)]
    return small(kernel, sc, [own, got], outs, [pltpu.VMEM((4,) + part, f32)], after, "sum_second")


def sum_third(sc, keep, got, after):
    def kernel(sc, keep_ref, got_ref, *rest):
        send_ref, own_ref = rest[-2:]
        h = sc[2] >> 1
        send_ref[...] = (keep_ref[1 - h] + got_ref[1 - h].astype(f32)).astype(bf16)
        own_ref[...] = keep_ref[h] + got_ref[h].astype(f32)

    part = keep.shape[1:]
    return small(kernel, sc, [keep, got], [shape(part, bf16), shape(part, f32)], [], after, "sum_third")


def down_pair(sc, own, got, after):
    def kernel(sc, own_ref, got_ref, *rest):
        rest[-1][...] = (own_ref[...].astype(f32) + got_ref[...].astype(f32)).astype(bf16)

    return small(kernel, sc, [own, got], [shape(own.shape, bf16)], [], after, "down_pair")[0]


def down_ring(sc, own, got, after):
    def kernel(sc, own_ref, got_ref, *rest):
        give_ref, keep_ref = rest[-2:]
        half = give_ref.shape[0]
        for out, c in ((give_ref, 1 - sc[0]), (keep_ref, sc[0])):
            rows = pl.ds(pl.multiple_of(c * half, half), half)
            out[...] = (own_ref[rows, :].astype(f32) + got_ref[rows, :].astype(f32)).astype(bf16)

    rows, cols = own.shape
    half = shape((rows // 2, cols), bf16)
    return small(kernel, sc, [own, got], [half, half], [], after, "down_ring")


def down_split(sc, keep, given, after):
    def kernel(sc, keep_ref, given_ref, *rest):
        send_ref, kept_ref, total = rest[-3:]
        n = total.shape[1]
        owner = (sc[2] >> 1) == sc[0]
        for m in range(4):
            rows = slice(m * n, (m + 1) * n)
            total[m] = jnp.where(owner, keep_ref[rows, :].astype(f32), given_ref[rows, :].astype(f32))
        for i, m in enumerate(by_turn(sc[0], sc[1])):
            out = send_ref if i < 2 else kept_ref
            out[i % 2] = total[m].astype(bf16)

    rows, cols = keep.shape
    out = shape((2, rows // 4, cols), bf16)
    return small(kernel, sc, [keep, given], [out, out], [pltpu.VMEM((4, rows // 4, cols), f32)], after, "down_split")


def sum_two(sc, own, got, after):
    def kernel(sc, own_ref, got_ref, *rest):
        rest[-1][...] = (own_ref[...] + got_ref[...].astype(f32)).astype(bf16)

    return small(kernel, sc, [own, got], [shape(own.shape, bf16)], [], after, "sum_two")[0]


def lay_down(sc, mine, other, after):
    def kernel(sc, *rest):
        out_ref, total = rest[-2:]
        n = total.shape[2]
        for kind, pieces in ((sc[0], rest[:4]), (1 - sc[0], rest[4:8])):
            for who, piece in zip(whose(kind), pieces):
                total[kind, sc[1] ^ who] = piece[...].astype(f32)
        for c in range(2):
            for m in range(4):
                at = (c * 4 + m) * n
                out_ref[at : at + n, :] = total[c, m]

    n, cols = mine[0].shape
    return small(kernel, sc, [*mine, *other], [shape((8 * n, cols), f32)], [pltpu.VMEM((2, 4, n, cols), f32)], after, "lay_down")[0]


def hold(value, after):
    return pl.pallas_call(
        lambda *refs: None,
        out_shape=shape(value.shape, value.dtype),
        in_specs=[LEFT] * (1 + len(after)),
        out_specs=LEFT,
        input_output_aliases={0: 0},
        cost_estimate=BRIEF,
        compiler_params=pltpu.CompilerParams(vmem_limit_bytes=1 << 20),
        name="hold",
    )(value, *after)


def far_sum(sc, far, near, after):
    def kernel(sc, far_ref, near_ref, *rest):
        rest[-1][...] = (far_ref[...] + jnp.where(sc[0] == 1, near_ref[...].astype(f32), 0.0)).astype(bf16)

    return small(kernel, sc, [far, near], [shape(far.shape, bf16)], [], after, "far_sum")[0]


CORE, SIDE, BACK = 1, 2, 4
rope_base = 10000.0
RUNS = 2


def flip(value, bit, bit1=None):
    count = lax.axis_size("dp")
    bits = (bit, bit if bit1 is None else bit1)
    return lax.ppermute(value, "dp", [(i, i ^ bits[i & 1]) for i in range(count)])


def flip_z(value, bit, where=lambda d, z: True):
    count, depth = lax.axis_size("dp"), lax.axis_size("fsdp")
    pairs = [(d * depth + z, d * depth + (z ^ bit)) for d in range(count) for z in range(depth) if where(d, z)]
    return lax.ppermute(value, ("dp", "fsdp"), pairs)


def home_to_work(value, back=False):
    count, depth = lax.axis_size("dp"), lax.axis_size("fsdp")
    pairs = []
    for d in range(count):
        for z in range(depth):
            there = (d & ~1) | (z & 1), 2 * (d & 1) + (z >> 1)
            pair = (d * depth + z, there[0] * depth + there[1])
            pairs.append(pair[::-1] if back else pair)
    return lax.ppermute(value, ("dp", "fsdp"), pairs)


def place():
    d, z = lax.axis_index("dp"), lax.axis_index("fsdp")
    return d & 1, (d >> 1) & 3, z


def turns(shard):
    far = flip_z(shard, 2)
    return shard, flip_z(shard, 1), far, flip_z(far, 1)


def plane_gather(piece):
    first, second = flip(piece, SIDE, BACK), flip(piece, BACK, SIDE)
    mine = (piece, first, second, flip(first, BACK, SIDE))
    return mine, tuple(flip(p, CORE) for p in mine)


def window(own):
    core, _, _ = place()
    depth = lax.axis_size("fsdp")
    far = lax.ppermute(own, "fsdp", [(z, z + 1) for z in range(0, depth, 2)])
    near = flip(jnp.where(core == 0, own, far), CORE)
    return far, near, own


def unwindow(sc, far, near, after=()):
    depth = lax.axis_size("fsdp")
    near = flip(near, CORE)
    far = far_sum(sc, far, near, after)
    return near, far, lax.ppermute(far, "fsdp", [(z + 1, z) for z in range(0, depth, 2)])


def over_groups(value):
    bit = 8
    while bit < lax.axis_size("dp"):
        value = (value.astype(f32) + flip(value, bit).astype(f32)).astype(bf16)
        bit *= 2
    return value


def spread(piece):
    return piece, flip(piece, SIDE, BACK), flip(piece, BACK, SIDE), flip(piece, SIDE | BACK)


def across(pieces):
    return tuple(flip(p, CORE) for p in pieces)


def body(tokens, segment_ids, attn_gain, query_weight, key_weight, value_weight, out_weight, ffn_gain, gate_weight, up_weight, down_weight, cotangent):
    core, chip, z = place()
    sc = jnp.stack([core, chip, z]).astype(jnp.int32)
    _, stretch, width = tokens.shape
    rows, depth = query_weight.shape[0], lax.axis_size("fsdp")
    block = 2 * (z & 1) + core
    positions = (block * stretch + jnp.arange(stretch)).astype(f32)
    freq = rope_base ** (-2.0 * jnp.arange(HEAD_DIM // 2, dtype=f32) / HEAD_DIM)
    angle = freq[:, None] * positions[None, :]
    cos, sin = jnp.cos(angle), jnp.sin(angle)

    gains = jnp.stack([attn_gain, ffn_gain]).astype(f32)
    parts_a = turns(pick_first(sc, query_weight, key_weight.T, value_weight.T, out_weight, gains))
    ids = jnp.broadcast_to((segment_ids[0] + 1).astype(bf16), (IDS, stretch))
    tokens = home_to_work(jnp.concatenate([tokens[0].T, ids]))
    piece_b = pick(sc, gate_weight, up_weight, parts_a[1:2])
    whole_a = stack(sc, parts_a, [piece_b])
    gains = gains_of(whole_a)
    gain_a, gain_f = gains[:1], gains[1:]
    wa = plane_gather(whole_a.reshape(depth * rows, PIECE))
    far_b = hold(flip_z(piece_b, 2), [wa[0][1], wa[0][2]])
    parts_b = piece_b, flip_z(piece_b, 1), far_b, flip_z(far_b, 1)
    whole_b = stack(sc, parts_b).reshape(depth * rows, piece_b.shape[1])
    wb = plane_gather(whole_b)
    piece_d = pick_down(sc, down_weight.T, [whole_b])

    h_0, a0, q0, own = pre(sc, tokens, gain_a, cos, sin, *wa, [whole_b, piece_d])
    kv0 = window(own)
    o0, lse0 = attend(q0, kv0, [wb[0][1], wb[0][2]])
    far_d = hold(flip_z(piece_d, 2), [o0])
    parts_d = piece_d, flip_z(piece_d, 1), far_d, flip_z(far_d, 1)
    whole_d = stack(sc, parts_d)
    weights = wa, wb, (whole_d, flip(whole_d, CORE))
    mixed0, h1_0, b0, gate0, up0, z0, h_1, a1, q1, own = post(False, sc, o0, h_0, gain_f, gain_a, cos, sin, own, *weights)
    kv1 = window(own)
    across_0 = across((a0, b0, mixed0))
    o1, lse1 = attend(q1, kv1, across_0)
    cot = home_to_work(hold(cotangent[0].T, [o1]))
    mixed1, h1_1, b1, gate1, up1, z1, output = post(True, sc, o1, h_1, gain_f, gain_a, cos, sin, own, *weights)
    output = home_to_work(output, back=True)
    across_1 = across((a1, b1, mixed1))

    gb1, act1, away1, zk1, zs1, g1, p1, dgain_f1, do = back(True, False, sc, weights, [cot], [gate1, up1, h1_1, gain_f, z1])
    across_2 = across((gb1, away1, zs1))
    dq1, three1, far, near, own = attend_back(sc, p1, q1, kv1, lse1, do, cos, sin, [*across_1])
    near, _, far = unwindow(sc, far, near)
    (three1,) = across((three1,))
    tail = [g1, dq1, own, near, far, h_1, gain_a, cos, sin]
    dk1, dv1, one1, dgain_a1, gb0, act0, away0, zk0, zs0, g1, p0, dgain_f0, do = back(False, False, sc, weights, tail, [gate0, up0, h1_0, gain_f, z0], [output, three1, *across_2])

    away0, gb0_, zs0, one1 = across((away0, gb0, zs0, one1))
    dq0, three0, far, near, own = attend_back(sc, p0, q0, kv0, lse0, do, cos, sin, [one1])
    near, down_far, far = unwindow(sc, far, near)
    send_b, keep_b = grad_ffn(sc, [b1, b0, across_1[1], across_0[1]], [act1, act0, across_2[1], away0], [down_far])
    got_b = flip(send_b, SIDE, BACK)
    like_d, unlike_d = grad_down(sc, [gb1, gb0, across_2[0], gb0_], [zk1, zk0, across_2[2], zs0], [send_b])
    got_d = flip_z(unlike_d, 1)
    (three0,) = across((three0,))
    tail = [g1, dq0, own, near, far, h_0, gain_a, cos, sin]
    dk0, dv0, one0, dgain_a0, grad_tokens = back(False, True, sc, weights, tail, None, [like_d, three0])

    own = [dq1, dq0, dk1, dk0, dv1, dv0, p1, p0]
    got = [three1, three0, one1, flip(one0, CORE)]
    send_a, keep_a = grad_attention(sc, [a1, a0, across_1[0], across_0[0]], [mixed1, mixed0, across_1[2], across_0[2]], own, got, [dgain_a1, dgain_a0, dgain_f1, dgain_f0], [])
    got_a = flip(send_a, SIDE, BACK)
    later_b, own_b = sum_first(sc, keep_b, got_b, [send_a])
    more_b = flip(later_b, BACK, SIDE)
    pair_d = down_pair(sc, like_d, got_d, [later_b])
    got_d = flip_z(pair_d, 2, lambda d, z: (z >> 1) != (d & 1))
    later_a, own_a = sum_first(sc, keep_a, got_a, [pair_d])
    more_a = flip(later_a, BACK, SIDE)
    send_b, ring_b = sum_second(sc, own_b, more_b, [later_a])
    got_b = flip_z(send_b, 1)
    send_a, ring_a = sum_second(sc, own_a, more_a, [send_b])
    got_a = flip_z(send_a, 1)
    send_b, ring_b = sum_third(sc, ring_b, got_b, [send_a])
    got_b = flip_z(send_b, 2)
    give, keep = down_ring(sc, pair_d, got_d, [send_b])
    given = flip(give, CORE)
    send_a, ring_a = sum_third(sc, ring_a, got_a, [give])
    got_a = flip_z(send_a, 2)
    send_d, keep_d = down_split(sc, keep, given, [send_a])
    got_d = flip(send_d, SIDE, BACK)
    piece_b = over_groups(sum_two(sc, ring_b, got_b, [send_d]))
    all_b = spread(piece_b)
    later_d, own_d = sum_first(sc, keep_d, got_d, [piece_b])
    more_d = flip(later_d, BACK, SIDE)
    piece_a = over_groups(sum_two(sc, ring_a, got_a, [later_d]))
    all_a = spread(piece_a)
    piece_d = over_groups(sum_two(sc, own_d, more_d, [piece_a]))
    grad_gate, grad_up = lay(sc, all_b, across(all_b), (gate_weight.shape[1],) * 2, [piece_d])
    all_d = spread(piece_d)
    grad_query, grad_key, grad_value, grad_out, dgains = lay(sc, all_a, across(all_a), (width, KVW, KVW, width), [grad_gate])
    grad_down_ = lay_down(sc, all_d, across(all_d), [grad_query])
    grad_tokens = home_to_work(hold(grad_tokens, [piece_b]), back=True)
    grad_tokens, output = grad_tokens.astype(f32).T, output.T
    return (output[None], grad_tokens[None], dgains[0], grad_query, grad_key, grad_value, grad_out, dgains[1], grad_gate, grad_up, grad_down_.T)


def solution(mesh):
    wide, rows, shard = P("dp", "fsdp", None), P("dp", "fsdp"), P("fsdp", None)
    in_specs = (wide, rows, P("fsdp"), shard, shard, shard, shard, P("fsdp"), shard, shard, shard, wide)
    out_specs = (wide, wide, P("fsdp"), shard, shard, shard, shard, P("fsdp"), shard, shard, shard)
    return jax.shard_map(body, mesh=mesh, in_specs=in_specs, out_specs=out_specs, check_vma=False)
```

```python
import functools
import jax
import jax.numpy as jnp
from jax import lax
from jax.sharding import PartitionSpec as P
from jax.experimental import pallas as pl
from jax.experimental.pallas import tpu as pltpu

f32, bf16 = jnp.float32, jnp.bfloat16
eps = 1e-05
HEADS, KV_HEADS, HEAD_DIM, GROUP, KVW = 15, 5, 64, 3, 320
IDS = 16
PIECE = 384
LIMIT = 58 << 20
WHOLE = pl.BlockSpec(memory_space=pltpu.VMEM)
LEFT = pl.BlockSpec(memory_space=pl.ANY)
SCALARS = pl.BlockSpec(memory_space=pltpu.SMEM)
BRIEF = pl.CostEstimate(flops=1024, bytes_accessed=1024, transcendentals=0)


def contract(a, b, i, j):
    return lax.dot_general(a, b, (((i,), (j,)), ((), ())), preferred_element_type=f32)


def nn(a, b):
    return contract(a, b, 1, 0)


def nt(a, b):
    return contract(a, b, 1, 1)


def tn(a, b):
    return contract(a, b, 0, 0)


def whose(core):
    return 0, 1 + core, 2 - core, 3


def fetch(mine, other, kept, sems, core, chip):
    for kind, pieces in ((core, mine), (1 - core, other)):
        for who, piece in zip(whose(kind), pieces):
            at = chip ^ who
            pltpu.make_async_copy(piece, kept.at[kind, at], sems.at[kind, at]).start()


def arrived(kept, sems, *at):
    pltpu.make_async_copy(kept.at[at], kept.at[at], sems.at[at]).wait()


def normed(x, gain):
    return x * lax.rsqrt(jnp.mean(x * x, axis=-1, keepdims=True) + eps) * gain


def norm_back(x, gain, grad):
    r = lax.rsqrt(jnp.mean(x * x, axis=-1, keepdims=True) + eps)
    hat = x * r
    scaled = grad * gain
    dx = r * (scaled - hat * jnp.mean(scaled * hat, axis=-1, keepdims=True))
    return dx, jnp.sum(grad * hat, axis=0, keepdims=True)


def widened(x):
    return jnp.concatenate([x, jnp.zeros((x.shape[0], PIECE - x.shape[1]), x.dtype)], axis=1)


def rope(u, cos, sin, back):
    heads = u.shape[0] // HEAD_DIM
    half = HEAD_DIM // 2
    out = []
    for h in range(heads):
        u1, u2 = u[h * HEAD_DIM : h * HEAD_DIM + half], u[h * HEAD_DIM + half : (h + 1) * HEAD_DIM]
        if back:
            out += [u1 * cos + u2 * sin, u2 * cos - u1 * sin]
        else:
            out += [u1 * cos - u2 * sin, u2 * cos + u1 * sin]
    return jnp.concatenate(out, axis=0)


def project(state, gain_ref, cos_ref, sin_ref, ids, kept, sems, a_ref, q_ref, kv_ref):
    a = normed(state, gain_ref[...]).astype(bf16)
    a_ref[...] = a
    cos, sin = cos_ref[...], sin_ref[...]
    arrived(kept, sems, 0, 3)
    kv_ref[:KVW, :] = rope(nn(a, kept[0, 3, :, :KVW]).T, cos, sin, False).astype(bf16)
    arrived(kept, sems, 1, 0)
    kv_ref[2 * KVW :, :] = ids
    kv_ref[KVW : 2 * KVW, :] = nn(a, kept[1, 0, :, :KVW]).T.astype(bf16)
    for m in range(3):
        arrived(kept, sems, 0, m)
        q_ref[pl.ds(m * KVW, KVW), :] = rope(nn(a, kept[0, m, :, :KVW]).T, cos, sin, False).astype(bf16)


def pre_kernel(sc, ht_ref, gain_ref, cos_ref, sin_ref, *rest):
    width = ht_ref.shape[0] - IDS
    mine, other = rest[:4], rest[4:8]
    h_ref, a_ref, q_ref, kv_ref, kept, sems = rest[-6:]
    core, chip = sc[0], sc[1]
    fetch(mine, other, kept, sems, core, chip)
    h = ht_ref[:width, :].T
    h_ref[...] = h
    project(h.astype(f32), gain_ref, cos_ref, sin_ref, ht_ref[width:, :], kept, sems, a_ref, q_ref, kv_ref)
    for m in range(1, 4):
        arrived(kept, sems, 1, m)


def scratch_a(width):
    return [pltpu.VMEM((2, 4, width, PIECE), bf16), pltpu.SemaphoreType.DMA((2, 4))]


def shape(s, d):
    return jax.ShapeDtypeStruct(s, d)


def pre(sc, ht, gain, cos, sin, mine_a, other_a, after):
    width, n = ht.shape[0] - IDS, ht.shape[1]
    return pl.pallas_call(
        pre_kernel,
        out_shape=(shape((n, width), bf16), shape((n, width), bf16), shape((width, n), bf16), shape((2 * KVW + IDS, n), bf16)),
        in_specs=[SCALARS] + [WHOLE] * 4 + [LEFT] * (8 + len(after)),
        out_specs=(WHOLE,) * 4,
        scratch_shapes=scratch_a(width),
        cost_estimate=BRIEF,
        compiler_params=pltpu.CompilerParams(vmem_limit_bytes=LIMIT),
        name="pre",
    )(sc, ht, gain, cos, sin, *mine_a, *other_a, *after)


def bias_of(kv):
    keys, n = kv.shape[1], kv.shape[1] // 3
    ids = kv[2 * KVW :, :].astype(f32)
    seg_k, seg_q = ids.T[:, :1], ids[:1, 2 * n :]
    j = lax.broadcasted_iota(jnp.int32, (keys, n), 0)
    i = lax.broadcasted_iota(jnp.int32, (keys, n), 1) + (keys - n)
    return jnp.where((seg_k == seg_q) & (j <= i), 0.0, -1e30).astype(f32)


def window_of(parts, whole):
    n = parts[0].shape[1]
    for w, part in enumerate(parts):
        whole[:, w * n : (w + 1) * n] = part[...]


def attend_kernel(q_ref, kv0, kv1, kv2, *rest):
    o_ref, lse_ref, bias, kv = rest[-4:]
    window_of((kv0, kv1, kv2), kv)
    bias[...] = bias_of(kv)

    def head(e, _):
        row = pl.multiple_of(e * HEAD_DIM, HEAD_DIM)
        k = kv[pl.ds(row, HEAD_DIM), :]
        v = kv[pl.ds(row + KVW, HEAD_DIM), :]
        for g in range(GROUP):
            at = pl.multiple_of((e * GROUP + g) * HEAD_DIM, HEAD_DIM)
            q = q_ref[pl.ds(at, HEAD_DIM), :]
            s = tn(k, q) * HEAD_DIM ** (-0.5) + bias[...]
            top = jnp.max(s, axis=0, keepdims=True)
            expo = jnp.exp(s - top)
            total = jnp.sum(expo, axis=0, keepdims=True)
            probs = (expo * (1.0 / total)).astype(bf16)
            o_ref[pl.ds(at, HEAD_DIM), :] = nn(v, probs).astype(bf16)
            lse_ref[pl.ds(e * GROUP + g, 1), :] = top + jnp.log(total)
        return 0

    lax.fori_loop(0, KV_HEADS, head, 0)


def attend(q, kvs, after=()):
    width, n = q.shape
    return pl.pallas_call(
        attend_kernel,
        out_shape=(shape((width, n), bf16), shape((HEADS, n), f32)),
        in_specs=[WHOLE] * 4 + [LEFT] * len(after),
        out_specs=(WHOLE,) * 2,
        scratch_shapes=[pltpu.VMEM((3 * n, n), f32), pltpu.VMEM((2 * KVW + IDS, 3 * n), bf16)],
        cost_estimate=BRIEF,
        compiler_params=pltpu.CompilerParams(vmem_limit_bytes=24 << 20),
        name="attend",
    )(q, *kvs, *after)


def attend_back_kernel(sc, p_ref, q_ref, kv0, kv1, kv2, lse_ref, do_ref, cos_ref, sin_ref, *rest):
    dq_ref, three_ref, far_ref, near_ref, own_ref, bias, kv, dqs = rest[-8:]
    n = q_ref.shape[1]
    window_of((kv0, kv1, kv2), kv)
    bias[...] = bias_of(kv)
    scale = HEAD_DIM ** (-0.5)

    def head(e, _):
        row = pl.multiple_of(e * HEAD_DIM, HEAD_DIM)
        k = kv[pl.ds(row, HEAD_DIM), :]
        v = kv[pl.ds(row + KVW, HEAD_DIM), :]
        dk = dv = None
        for g in range(GROUP):
            at = pl.multiple_of((e * GROUP + g) * HEAD_DIM, HEAD_DIM)
            q = q_ref[pl.ds(at, HEAD_DIM), :]
            do = do_ref[pl.ds(at, HEAD_DIM), :]
            s = tn(k, q) * scale + bias[...]
            probs = jnp.exp(s - lse_ref[pl.ds(e * GROUP + g, 1), :])
            dp = tn(v, do)
            inner = jnp.sum(probs * dp, axis=0, keepdims=True)
            ds = (probs * (dp - inner)).astype(bf16)
            dvg, dkg = nt(do, probs.astype(bf16)), nt(q, ds)
            dv, dk = (dvg, dkg) if g == 0 else (dv + dvg, dk + dkg)
            dqs[pl.ds(at, HEAD_DIM), :] = nn(k, ds)
        for at, grad in ((row, dk * scale), (row + KVW, dv)):
            far_ref[pl.ds(at, HEAD_DIM), :] = grad[:, :n]
            near_ref[pl.ds(at, HEAD_DIM), :] = grad[:, n : 2 * n].astype(bf16)
            own_ref[pl.ds(at, HEAD_DIM), :] = grad[:, 2 * n :]
        return 0

    lax.fori_loop(0, KV_HEADS, head, 0)
    cos, sin = cos_ref[...] * scale, sin_ref[...] * scale
    for m in range(3):
        dq = widened(rope(dqs[m * KVW : (m + 1) * KVW, :], cos, sin, True).T.astype(bf16))
        dq_ref[m] = dq
        three_ref[m] = jnp.where(sc[0] == 0, p_ref[m], dq)


def attend_back(sc, p, q, kvs, lse, do, cos, sin, after=()):
    width, n = q.shape
    block = (2 * KVW, n)
    return pl.pallas_call(
        attend_back_kernel,
        out_shape=(shape((3, n, PIECE), bf16), shape((3, n, PIECE), bf16), shape(block, f32), shape(block, bf16), shape(block, f32)),
        in_specs=[SCALARS] + [WHOLE] * 9 + [LEFT] * len(after),
        out_specs=(WHOLE,) * 5,
        scratch_shapes=[pltpu.VMEM((3 * n, n), f32), pltpu.VMEM((2 * KVW + IDS, 3 * n), bf16), pltpu.VMEM((width, n), f32)],
        cost_estimate=BRIEF,
        compiler_params=pltpu.CompilerParams(vmem_limit_bytes=32 << 20),
        name="attend_back",
    )(sc, p, q, *kvs, lse, do, cos, sin, *after)


def fetch_ffn(mine_b, other_b, down, wb, wd, sem_b, sem_d, core, chip):
    fetch(mine_b, other_b, wb, sem_b, core, chip)
    half = down[0].shape[1]
    for c, part in ((core, down[0]), (1 - core, down[1])):
        rows = pl.ds(pl.multiple_of(c * half, half), half)
        pltpu.make_async_copy(part, wd.at[:, rows], sem_d).start()


def arrived_down(wd, sem_d):
    pltpu.make_async_copy(wd, wd, sem_d).wait()


def scratch_ffn(width, n):
    return [
        pltpu.VMEM((2, 4, width, n), bf16),
        pltpu.SemaphoreType.DMA((2, 4)),
        pltpu.VMEM((4, width, n), bf16),
        pltpu.SemaphoreType.DMA,
    ]


def post_kernel(last, after, sc, ot_ref, h_ref, gain_ref, gain_a, cos_ref, sin_ref, *rest):
    mine_a, other_a, mine_b, other_b = rest[:4], rest[4:8], rest[8:12], rest[12:16]
    down, ids_ref, rest = rest[16:18], rest[18], rest[19 + after :]
    o_ref, h1_ref, b_ref, gate_ref, up_ref, z_ref, next_ref = rest[:7]
    more, rest = rest[7 : 7 + (0 if last else 3)], rest[7 + (0 if last else 3) :]
    wa, sem_a, wb, sem_b, wd, sem_d = rest
    core, chip = sc[0], sc[1]
    fetch(mine_a, other_a, wa, sem_a, core, chip)
    fetch_ffn(mine_b, other_b, down, wb, wd, sem_b, sem_d, core, chip)
    o = ot_ref[...].T
    o_ref[...] = o
    for m in range(1, 4):
        arrived(wa, sem_a, 1, m)
    h1 = h_ref[...].astype(f32) + jnp.concatenate([nn(o, wa[1, m, :, :KVW]) for m in range(1, 4)], axis=1)
    h1_ref[...] = h1
    b = normed(h1, gain_ref[...]).astype(bf16)
    b_ref[...] = b
    n = wb.shape[3]
    total = h1
    for m in range(4):
        cols = slice(m * n, (m + 1) * n)
        arrived(wb, sem_b, 0, m)
        gate = nn(b, wb[0, m])
        arrived(wb, sem_b, 1, m)
        up = nn(b, wb[1, m])
        gate_ref[:, cols] = gate.astype(bf16)
        up_ref[:, cols] = up.astype(bf16)
        z = (gate / (1.0 + jnp.exp(-gate)) * up).astype(bf16)
        z_ref[:, cols] = z
        if m == 0:
            arrived_down(wd, sem_d)
        total = total + nt(z, wd[m])
    next_ref[...] = total.astype(bf16).T if last else total
    if last:
        arrived(wa, sem_a, 1, 0)
        for m in range(4):
            arrived(wa, sem_a, 0, m)
    else:
        project(total, gain_a, cos_ref, sin_ref, ids_ref[2 * KVW :, :], wa, sem_a, *more)


def post(last, after, sc, ot, h, gain, gain_a, cos, sin, kv, wa, wb, wd):
    width, n = ot.shape
    hidden = wb[0][0].shape[1] * 4
    outs = [shape((n, width), bf16), shape((n, width), f32), shape((n, width), bf16)] + [shape((n, hidden), bf16)] * 3
    outs += [shape((width, n), bf16) if last else shape((n, width), f32)]
    if not last:
        outs += [shape((n, width), bf16), shape((width, n), bf16), shape((2 * KVW + IDS, n), bf16)]
    return pl.pallas_call(
        functools.partial(post_kernel, last, len(after)),
        out_shape=tuple(outs),
        in_specs=[SCALARS] + [WHOLE] * 6 + [LEFT] * 18 + [WHOLE] + [LEFT] * len(after),
        out_specs=(WHOLE,) * len(outs),
        scratch_shapes=scratch_a(width) + scratch_ffn(width, hidden // 4),
        cost_estimate=BRIEF,
        compiler_params=pltpu.CompilerParams(vmem_limit_bytes=LIMIT),
        name="post",
    )(sc, ot, h, gain, gain_a, cos, sin, *wa[0], *wa[1], *wb[0], *wb[1], *wd, kv, *after)


def ffn_back(state, core, refs, weights):
    gate_ref, up_ref, h1_ref, gain_ref, gb_ref, keep_ref, send_ref, g1_ref, p_ref, dgain_ref, do_ref = refs
    wa, sem_a, wb, sem_b, wd, sem_d = weights
    gb = state.astype(bf16)
    gb_ref[...] = gb
    n = wb.shape[3]
    first = core == 0
    arrived_down(wd, sem_d)
    db = None
    for m in range(4):
        cols = slice(m * n, (m + 1) * n)
        dz = nn(gb, wd[m])
        gate, up = gate_ref[:, cols].astype(f32), up_ref[:, cols].astype(f32)
        sig = 1.0 / (1.0 + jnp.exp(-gate))
        dup = (dz * (gate * sig)).astype(bf16)
        dgate = (dz * up * (sig * (1.0 + gate * (1.0 - sig)))).astype(bf16)
        keep_ref[:, cols] = jnp.where(first, dgate, dup)
        send_ref[:, cols] = jnp.where(first, dup, dgate)
        arrived(wb, sem_b, 0, m)
        part = nt(dgate, wb[0, m])
        arrived(wb, sem_b, 1, m)
        part = part + nt(dup, wb[1, m])
        db = part if m == 0 else db + part
    dx, dgain = norm_back(h1_ref[...], gain_ref[...], db)
    dgain_ref[...] = dgain
    g1 = state + dx
    g1_ref[...] = g1
    low = g1.astype(bf16)
    do = None
    for p in range(3):
        part = low[:, p * KVW : (p + 1) * KVW]
        p_ref[p] = widened(part)
        arrived(wa, sem_a, 1, p + 1)
        part = nt(wa[1, p + 1, :, :KVW], part)
        do = part if p == 0 else do + part
    do_ref[...] = do.astype(bf16)


def finish_a(wa, sem_a, *left):
    for at in left:
        arrived(wa, sem_a, *at)


def query_back(dq_ref, wa, sem_a):
    da = None
    for m in range(3):
        arrived(wa, sem_a, 0, m)
        part = nt(dq_ref[m, :, :KVW], wa[0, m, :, :KVW])
        da = part if m == 0 else da + part
    return da


def project_back(da, own_ref, near_ref, far_ref, core, cos_ref, sin_ref, dk_ref, dv_ref, one_ref, h, gain, wa, sem_a):
    cos, sin = cos_ref[...], sin_ref[...]
    grad = own_ref[...] + far_ref[...].astype(f32) + jnp.where(core == 0, near_ref[...].astype(f32), 0.0)
    dk = rope(grad[:KVW], cos, sin, True).T.astype(bf16)
    dv = grad[KVW:].T.astype(bf16)
    dk_ref[...] = widened(dk)
    dv_ref[...] = widened(dv)
    one_ref[...] = widened(jnp.where(core == 0, dv, dk))
    arrived(wa, sem_a, 0, 3)
    arrived(wa, sem_a, 1, 0)
    da = da + nt(dk, wa[0, 3, :, :KVW]) + nt(dv, wa[1, 0, :, :KVW])
    return norm_back(h, gain, da)


def back_kernel(start, end, after, sc, *rest):
    rest = list(rest)

    def take(n):
        out = rest[:n]
        del rest[:n]
        return out

    core, chip = sc[0], sc[1]
    mine_a, other_a = take(4), take(4)
    if not end:
        mine_b, other_b = take(4), take(4)
        down = take(2)
    if start:
        (g_ref,) = take(1)
    else:
        g1_in, dq_ref, own_ref, near_ref, far_ref, h_ref, gain_a, cos_ref, sin_ref = take(9)
    if not end:
        ins = take(4)
    take(after)
    if not start:
        dk_ref, dv_ref, one_ref, dgain_a = take(4)
    if end:
        (g_out,) = take(1)
    else:
        outs = take(7)
    wa, sem_a = take(2)
    fetch(mine_a, other_a, wa, sem_a, core, chip)
    if not end:
        wb, sem_b, wd, sem_d = take(4)
        fetch_ffn(mine_b, other_b, down, wb, wd, sem_b, sem_d, core, chip)
    if start:
        state = g_ref[...].T.astype(f32)
    else:
        da = query_back(dq_ref, wa, sem_a)
        dx, dgain = project_back(da, own_ref, near_ref, far_ref, core, cos_ref, sin_ref, dk_ref, dv_ref, one_ref, h_ref[...].astype(f32), gain_a[...], wa, sem_a)
        dgain_a[...] = dgain
        state = g1_in[...] + dx
    if end:
        g_out[...] = state.astype(bf16).T
        finish_a(wa, sem_a, (1, 1), (1, 2), (1, 3))
    else:
        ffn_back(state, core, (*ins, *outs), (wa, sem_a, wb, sem_b, wd, sem_d))
        if start:
            finish_a(wa, sem_a, (1, 0), (0, 0), (0, 1), (0, 2), (0, 3))


def back(start, end, sc, weights, tail, ffn, after=()):
    wa, wb, wd = weights
    width = wa[0][0].shape[0]
    args = [sc, *wa[0], *wa[1]]
    specs = [SCALARS] + [LEFT] * 8
    scratch = scratch_a(width)
    if not end:
        args += [*wb[0], *wb[1], *wd]
        specs += [LEFT] * 10
        scratch += scratch_ffn(width, wb[0][0].shape[1])
    args += list(tail)
    specs += [WHOLE] * len(tail)
    n = tail[0].shape[1 if start else 0]
    outs = []
    if not end:
        args += list(ffn)
        specs += [WHOLE] * len(ffn)
    if not start:
        outs += [shape((n, PIECE), bf16)] * 3 + [shape((1, width), f32)]
    if end:
        outs += [shape((width, n), bf16)]
    else:
        hidden = ffn[0].shape[1]
        outs += [shape((n, width), bf16), shape((n, hidden), bf16), shape((n, hidden), bf16)]
        outs += [shape((n, width), f32), shape((3, n, PIECE), bf16), shape((1, width), f32), shape((width, n), bf16)]
    args += list(after)
    specs += [LEFT] * len(after)
    return pl.pallas_call(
        functools.partial(back_kernel, start, end, len(after)),
        out_shape=tuple(outs),
        in_specs=specs,
        out_specs=(WHOLE,) * len(outs),
        scratch_shapes=scratch,
        cost_estimate=BRIEF,
        compiler_params=pltpu.CompilerParams(vmem_limit_bytes=LIMIT),
        name="back_end" if end else ("back_start" if start else "back_join"),
    )(*args)


def by_turn(core, chip):
    one = 1 + core
    return chip ^ one, chip ^ 3, chip, chip ^ (3 - one)


def turned(dst, blocks):
    n = blocks[0].shape[0]
    for i, block in enumerate(blocks):
        dst[:, i * n : (i + 1) * n] = block[...].T


def grad_ffn_kernel(sc, *rest):
    lefts, rights = rest[:4], rest[4:8]
    send_ref, keep_ref, left, right = rest[-4:]
    core, chip = sc[0], sc[1]
    n, cols = rights[0].shape[0], right.shape[1]
    turned(left, lefts)
    for i, m in enumerate(by_turn(core, chip)):
        at = pl.multiple_of(m * cols, 128)
        for j, block in enumerate(rights):
            right[j * n : (j + 1) * n, :] = block[:, pl.ds(at, cols)]
        out = send_ref if i < 2 else keep_ref
        out[i % 2] = nn(left[...], right[...]).astype(bf16)


def grad_ffn(sc, lefts, rights, after):
    n, width = lefts[0].shape
    cols = rights[0].shape[1] // 4
    out = shape((2, width, cols), bf16)
    return pl.pallas_call(
        grad_ffn_kernel,
        out_shape=(out, out),
        in_specs=[SCALARS] + [WHOLE] * 8 + [LEFT] * len(after),
        out_specs=(WHOLE,) * 2,
        scratch_shapes=[pltpu.VMEM((width, 4 * n), bf16), pltpu.VMEM((4 * n, cols), bf16)],
        cost_estimate=BRIEF,
        compiler_params=pltpu.CompilerParams(vmem_limit_bytes=LIMIT),
        name="grad_ffn",
    )(sc, *lefts, *rights, *after)


def grad_down_kernel(sc, *rest):
    lefts, rights = rest[:4], rest[4:8]
    out_ref, left, right = rest[-3:]
    n, (_, half, cols) = rights[0].shape[0], out_ref.shape
    turned(left, lefts)
    rows = pl.ds(pl.multiple_of(sc[0] * half, half), half)
    for i in range(4):
        for j, block in enumerate(rights):
            right[j * n : (j + 1) * n, :] = block[:, i * cols : (i + 1) * cols]
        out_ref[i] = nn(left[rows, :], right[...]).astype(bf16)


def grad_down(sc, lefts, rights, after):
    n, width = lefts[0].shape
    cols = rights[0].shape[1] // 4
    return pl.pallas_call(
        grad_down_kernel,
        out_shape=shape((4, width // 2, cols), bf16),
        in_specs=[SCALARS] + [WHOLE] * 8 + [LEFT] * len(after),
        out_specs=WHOLE,
        scratch_shapes=[pltpu.VMEM((width, 4 * n), bf16), pltpu.VMEM((4 * n, cols), bf16)],
        cost_estimate=BRIEF,
        compiler_params=pltpu.CompilerParams(vmem_limit_bytes=LIMIT),
        name="grad_down",
    )(sc, *lefts, *rights, *after)


def grad_attention_kernel(sc, *rest):
    a_refs, o_refs, rest = rest[:4], rest[4:8], rest[8:]
    queries, keys, values, outs, threes, ones = (rest[i : i + 2] for i in range(0, 12, 2))
    gain_a, gain_f = (rest[i : i + 2] for i in (12, 14))
    send_ref, keep_ref, left, right = rest[-4:]
    core, chip = sc[0], sc[1]
    n, width = a_refs[0].shape
    turned(left.at[0], a_refs)
    gains = [g[0][...] + g[1][...] for g in (gain_a, gain_f)]
    gains = jnp.concatenate([*gains, jnp.zeros((6, width), f32)], axis=0).T
    gains = jnp.concatenate([gains, jnp.zeros((width, PIECE - KVW - 8), f32)], axis=1).astype(bf16)

    def fill(at, of_three, own_three, own_one, single):
        for j in range(2):
            for i in range(3):
                right[of_three + i, j * n : (j + 1) * n, :] = own_three[j][i]
                right[of_three + i, (j + 2) * n : (j + 3) * n, :] = threes[j][i]
            right[single, j * n : (j + 1) * n, :] = own_one[j][...]
            right[single, (j + 2) * n : (j + 3) * n, :] = ones[j][...]

    @pl.when(core == 0)
    def _():
        fill(0, 0, queries, keys, 3)

    @pl.when(core == 1)
    def _():
        turned(left.at[1], o_refs)
        fill(0, 1, outs, values, 0)

    for i, m in enumerate(by_turn(core, chip)):
        out = send_ref if i < 2 else keep_ref
        which = jnp.where(m > 0, core, 0)
        out[i % 2] = nn(left[which], right[m]).astype(bf16)
        out[i % 2, :, KVW:] = gains


def grad_attention(sc, a, o, own, got, gains, after):
    n, width = a[0].shape
    out = shape((2, width, PIECE), bf16)
    return pl.pallas_call(
        grad_attention_kernel,
        out_shape=(out, out),
        in_specs=[SCALARS] + [WHOLE] * 24 + [LEFT] * len(after),
        out_specs=(WHOLE,) * 2,
        scratch_shapes=[pltpu.VMEM((2, width, 4 * n), bf16), pltpu.VMEM((4, 4 * n, PIECE), bf16)],
        cost_estimate=BRIEF,
        compiler_params=pltpu.CompilerParams(vmem_limit_bytes=LIMIT),
        name="grad_attention",
    )(sc, *a, *o, *own, *got, *gains, *after)


def lay_kernel(count, sc, *rest):
    mine, other, outs, kept = rest[:4], rest[4:8], rest[-1 - count : -1], rest[-1]
    core, chip = sc[0], sc[1]
    for kind, pieces in ((core, mine), (1 - core, other)):
        for who, piece in zip(whose(kind), pieces):
            kept[kind, chip ^ who] = piece[...]
    n = sum(o.shape[1] for o in outs[: 4 if len(outs) > 2 else 2]) // 8
    cols = [jnp.concatenate([kept[c, m, :, :n].astype(f32) for m in range(4)], axis=1) for c in range(2)]
    if len(outs) == 2:
        outs[0][...] = cols[0]
        outs[1][...] = cols[1]
    else:
        outs[0][...] = cols[0][:, : 3 * n]
        outs[1][...] = cols[0][:, 3 * n :]
        outs[2][...] = cols[1][:, :n]
        outs[3][...] = cols[1][:, n:]
        gains = kept[0, 0, :, n : n + 8].astype(f32) + kept[1, 0, :, n : n + 8].astype(f32)
        outs[4][...] = gains.T[:2]


def lay(sc, mine, other, widths, after):
    rows, n = mine[0].shape
    outs = tuple(shape((rows, w), f32) for w in widths)
    if len(widths) > 2:
        outs += (shape((2, rows), f32),)
    return pl.pallas_call(
        functools.partial(lay_kernel, len(outs)),
        out_shape=outs,
        in_specs=[SCALARS] + [WHOLE] * 8 + [LEFT] * len(after),
        out_specs=(WHOLE,) * len(outs),
        scratch_shapes=[pltpu.VMEM((2, 4, rows, n), bf16)],
        cost_estimate=BRIEF,
        compiler_params=pltpu.CompilerParams(vmem_limit_bytes=24 << 20),
        name="lay",
    )(sc, *mine, *other, *after)


def pick_first_kernel(sc, q_ref, k_ref, v_ref, o_ref, gain_ref, out_ref):
    rows = out_ref.shape[0]
    which = sc[0] * 4 + sc[1]
    pad = jnp.zeros((6, rows), f32)
    gains = jnp.concatenate([gain_ref[...], pad], axis=0).T.astype(bf16)
    rest = jnp.zeros((rows, PIECE - KVW - 8), bf16)
    for at in range(8):

        @pl.when(which == at)
        def _():
            if at in (3, 4):
                piece = (k_ref if at == 3 else v_ref)[...].T
            else:
                source, m = (q_ref, at) if at < 3 else (o_ref, at - 5)
                piece = source[:, m * KVW : (m + 1) * KVW]
            out_ref[...] = jnp.concatenate([piece, gains, rest], axis=1)


def pick_first(sc, query, key, value, out, gains):
    return pl.pallas_call(
        pick_first_kernel,
        out_shape=shape((query.shape[0], PIECE), bf16),
        in_specs=[SCALARS] + [WHOLE] * 5,
        out_specs=WHOLE,
        cost_estimate=BRIEF,
        compiler_params=pltpu.CompilerParams(vmem_limit_bytes=16 << 20),
        name="pick_first",
    )(sc, query, key, value, out, gains)


def pick_kernel(sc, gate, up, *rest):
    out_ref, sem = rest[-2:]
    cols = out_ref.shape[1]
    at = pl.ds(pl.multiple_of(sc[1] * cols, 128), cols)
    for c, source in ((0, gate), (1, up)):

        @pl.when(sc[0] == c)
        def _():
            pltpu.make_async_copy(source.at[:, at], out_ref, sem).start()

    pltpu.make_async_copy(gate.at[:, at], out_ref, sem).wait()


def pick(sc, gate, up, after):
    return pl.pallas_call(
        pick_kernel,
        out_shape=shape((gate.shape[0], gate.shape[1] // 4), bf16),
        in_specs=[SCALARS] + [LEFT] * (2 + len(after)),
        out_specs=WHOLE,
        scratch_shapes=[pltpu.SemaphoreType.DMA],
        cost_estimate=BRIEF,
        compiler_params=pltpu.CompilerParams(vmem_limit_bytes=16 << 20),
        name="pick",
    )(sc, gate, up, *after)


def pick_down_kernel(sc, down, *rest):
    out_ref, sem = rest[-2:]
    half = out_ref.shape[0]
    copy = pltpu.make_async_copy(down.at[pl.ds(pl.multiple_of(sc[0] * half, half), half), :], out_ref, sem)
    copy.start()
    copy.wait()


def pick_down(sc, down, after):
    rows, cols = down.shape
    return pl.pallas_call(
        pick_down_kernel,
        out_shape=shape((rows // 2, cols), bf16),
        in_specs=[SCALARS] + [LEFT] * (1 + len(after)),
        out_specs=WHOLE,
        scratch_shapes=[pltpu.SemaphoreType.DMA],
        cost_estimate=BRIEF,
        compiler_params=pltpu.CompilerParams(vmem_limit_bytes=16 << 20),
        name="pick_down",
    )(sc, down, *after)


def gains_kernel(first_ref, out_ref):
    for j in range(4):
        n = first_ref.shape[1]
        out_ref[:, j * n : (j + 1) * n] = first_ref[j, :, KVW : KVW + 8].astype(f32).T[:2]


def gains_of(first):
    return pl.pallas_call(
        gains_kernel,
        out_shape=shape((2, 4 * first.shape[1]), f32),
        in_specs=[WHOLE],
        out_specs=WHOLE,
        cost_estimate=BRIEF,
        compiler_params=pltpu.CompilerParams(vmem_limit_bytes=16 << 20),
        name="gains",
    )(first)


def stack_kernel(sc, *rest):
    parts, out_ref, sems = rest[:4], rest[-2], rest[-1]
    copies = [pltpu.make_async_copy(p, out_ref.at[sc[2] ^ s], sems.at[s]) for s, p in enumerate(parts)]
    for copy in copies:
        copy.start()
    for copy in copies:
        copy.wait()


def stack(sc, parts, after=()):
    return pl.pallas_call(
        stack_kernel,
        out_shape=shape((4,) + parts[0].shape, parts[0].dtype),
        in_specs=[SCALARS] + [LEFT] * (4 + len(after)),
        out_specs=WHOLE,
        scratch_shapes=[pltpu.SemaphoreType.DMA((4,))],
        cost_estimate=BRIEF,
        compiler_params=pltpu.CompilerParams(vmem_limit_bytes=16 << 20),
        name="stack",
    )(sc, *parts, *after)


def small(kernel, sc, args, outs, scratch, after, name):
    return pl.pallas_call(
        kernel,
        out_shape=tuple(outs),
        in_specs=[SCALARS] + [WHOLE] * len(args) + [LEFT] * len(after),
        out_specs=(WHOLE,) * len(outs),
        scratch_shapes=scratch,
        cost_estimate=BRIEF,
        compiler_params=pltpu.CompilerParams(vmem_limit_bytes=32 << 20),
        name=name,
    )(sc, *args, *after)


def sum_first(sc, keep, got, after):
    def kernel(sc, keep_ref, got_ref, *rest):
        later_ref, own_ref = rest[-2:]
        later_ref[...] = (keep_ref[1].astype(f32) + got_ref[1].astype(f32)).astype(bf16)
        own_ref[...] = keep_ref[0].astype(f32) + got_ref[0].astype(f32)

    block = keep.shape[1:]
    return small(kernel, sc, [keep, got], [shape(block, bf16), shape(block, f32)], [], after, "sum_first")


def sum_second(sc, own, got, after):
    def kernel(sc, own_ref, got_ref, *rest):
        send_ref, keep_ref, total = rest[-3:]
        n = total.shape[1]
        for j in range(4):
            rows = slice(j * n, (j + 1) * n)
            total[j] = own_ref[rows, :] + got_ref[rows, :].astype(f32)
        like = sc[2] & 1
        for h in range(2):
            send_ref[h] = total[2 * h + 1 - like].astype(bf16)
            keep_ref[h] = total[2 * h + like]

    rows, cols = own.shape
    part = (rows // 4, cols)
    outs = [shape((2,) + part, bf16), shape((2,) + part, f32)]
    return small(kernel, sc, [own, got], outs, [pltpu.VMEM((4,) + part, f32)], after, "sum_second")


def sum_third(sc, keep, got, after):
    def kernel(sc, keep_ref, got_ref, *rest):
        send_ref, own_ref = rest[-2:]
        h = sc[2] >> 1
        send_ref[...] = (keep_ref[1 - h] + got_ref[1 - h].astype(f32)).astype(bf16)
        own_ref[...] = keep_ref[h] + got_ref[h].astype(f32)

    part = keep.shape[1:]
    return small(kernel, sc, [keep, got], [shape(part, bf16), shape(part, f32)], [], after, "sum_third")


def down_split(sc, half, after):
    def kernel(sc, half_ref, *rest):
        send_ref, kept_ref, total = rest[-3:]
        n = total.shape[1]
        for m in range(4):
            total[m] = half_ref[m * n : (m + 1) * n, :].astype(f32)
        for i, m in enumerate(by_turn(sc[0], sc[1])):
            out = send_ref if i < 2 else kept_ref
            out[i % 2] = total[m].astype(bf16)

    rows, cols = half.shape
    out = shape((2, rows // 4, cols), bf16)
    return small(kernel, sc, [half], [out, out], [pltpu.VMEM((4, rows // 4, cols), f32)], after, "down_split")


def sum_two(sc, own, got, after):
    def kernel(sc, own_ref, got_ref, *rest):
        rest[-1][...] = (own_ref[...] + got_ref[...].astype(f32)).astype(bf16)

    return small(kernel, sc, [own, got], [shape(own.shape, bf16)], [], after, "sum_two")[0]


def lay_down(sc, mine, other, after):
    def kernel(sc, *rest):
        out_ref, total = rest[-2:]
        n = total.shape[2]
        for kind, pieces in ((sc[0], rest[:4]), (1 - sc[0], rest[4:8])):
            for who, piece in zip(whose(kind), pieces):
                total[kind, sc[1] ^ who] = piece[...].astype(f32)
        for c in range(2):
            for m in range(4):
                at = (c * 4 + m) * n
                out_ref[at : at + n, :] = total[c, m]

    n, cols = mine[0].shape
    return small(kernel, sc, [*mine, *other], [shape((8 * n, cols), f32)], [pltpu.VMEM((2, 4, n, cols), f32)], after, "lay_down")[0]


def hold(value, after):
    return pl.pallas_call(
        lambda *refs: None,
        out_shape=shape(value.shape, value.dtype),
        in_specs=[LEFT] * (1 + len(after)),
        out_specs=LEFT,
        input_output_aliases={0: 0},
        cost_estimate=BRIEF,
        compiler_params=pltpu.CompilerParams(vmem_limit_bytes=1 << 20),
        name="hold",
    )(value, *after)


def far_sum(sc, far, near, after):
    def kernel(sc, far_ref, near_ref, *rest):
        rest[-1][...] = (far_ref[...] + jnp.where(sc[0] == 1, near_ref[...].astype(f32), 0.0)).astype(bf16)

    return small(kernel, sc, [far, near], [shape(far.shape, bf16)], [], after, "far_sum")[0]


CORE, SIDE, BACK = 1, 2, 4
rope_base = 10000.0
RUNS = 2


def flip(value, bit, bit1=None):
    count = lax.axis_size("dp")
    bits = (bit, bit if bit1 is None else bit1)
    return lax.ppermute(value, "dp", [(i, i ^ bits[i & 1]) for i in range(count)])


def flip_z(value, bit, where=lambda d, z: True):
    count, depth = lax.axis_size("dp"), lax.axis_size("fsdp")
    pairs = [(d * depth + z, d * depth + (z ^ bit)) for d in range(count) for z in range(depth) if where(d, z)]
    return lax.ppermute(value, ("dp", "fsdp"), pairs)


def home_to_work(value, back=False):
    count, depth = lax.axis_size("dp"), lax.axis_size("fsdp")
    pairs = []
    for d in range(count):
        for z in range(depth):
            there = (d & ~1) | (z & 1), 2 * (d & 1) + (z >> 1)
            pair = (d * depth + z, there[0] * depth + there[1])
            pairs.append(pair[::-1] if back else pair)
    return lax.ppermute(value, ("dp", "fsdp"), pairs)


def place():
    d, z = lax.axis_index("dp"), lax.axis_index("fsdp")
    return d & 1, (d >> 1) & 3, z


def turns(shard):
    far = flip_z(shard, 2)
    return shard, flip_z(shard, 1), far, flip_z(far, 1)


def plane_gather(piece):
    first, second = flip(piece, SIDE, BACK), flip(piece, BACK, SIDE)
    mine = (piece, first, second, flip(first, BACK, SIDE))
    return mine, tuple(flip(p, CORE) for p in mine)


def window(own):
    core, _, _ = place()
    depth = lax.axis_size("fsdp")
    far = lax.ppermute(own, "fsdp", [(z, z + 1) for z in range(0, depth, 2)])
    near = flip(jnp.where(core == 0, own, far), CORE)
    return far, near, own


def unwindow(sc, far, near, after=()):
    depth = lax.axis_size("fsdp")
    near = flip(near, CORE)
    far = far_sum(sc, far, near, after)
    return near, far, lax.ppermute(far, "fsdp", [(z + 1, z) for z in range(0, depth, 2)])


def over_groups(value):
    bit = 8
    while bit < lax.axis_size("dp"):
        value = (value.astype(f32) + flip(value, bit).astype(f32)).astype(bf16)
        bit *= 2
    return value


def spread(piece):
    return piece, flip(piece, SIDE, BACK), flip(piece, BACK, SIDE), flip(piece, SIDE | BACK)


def across(pieces):
    return tuple(flip(p, CORE) for p in pieces)


def body(tokens, segment_ids, attn_gain, query_weight, key_weight, value_weight, out_weight, ffn_gain, gate_weight, up_weight, down_weight, cotangent):
    core, chip, z = place()
    sc = jnp.stack([core, chip, z]).astype(jnp.int32)
    _, stretch, width = tokens.shape
    rows, depth = query_weight.shape[0], lax.axis_size("fsdp")
    block = 2 * (z & 1) + core
    positions = (block * stretch + jnp.arange(stretch)).astype(f32)
    freq = rope_base ** (-2.0 * jnp.arange(HEAD_DIM // 2, dtype=f32) / HEAD_DIM)
    angle = freq[:, None] * positions[None, :]
    cos, sin = jnp.cos(angle), jnp.sin(angle)

    gains = jnp.stack([attn_gain, ffn_gain]).astype(f32)
    parts_a = turns(pick_first(sc, query_weight, key_weight.T, value_weight.T, out_weight, gains))
    ids = jnp.broadcast_to((segment_ids[0] + 1).astype(bf16), (IDS, stretch))
    tokens = home_to_work(jnp.concatenate([tokens[0].T, ids]))
    piece_b = pick(sc, gate_weight, up_weight, parts_a[1:2])
    whole_a = stack(sc, parts_a, [piece_b])
    gains = gains_of(whole_a)
    gain_a, gain_f = gains[:1], gains[1:]
    wa = plane_gather(whole_a.reshape(depth * rows, PIECE))
    far_b = hold(flip_z(piece_b, 2), [wa[0][1], wa[0][2]])
    parts_b = piece_b, flip_z(piece_b, 1), far_b, flip_z(far_b, 1)
    whole_b = stack(sc, parts_b).reshape(depth * rows, piece_b.shape[1])
    wb = plane_gather(whole_b)
    piece_d = pick_down(sc, down_weight.T, [whole_a])
    whole_d = lax.all_gather(piece_d, "fsdp", axis=0)

    h_0, a0, q0, own = pre(sc, tokens, gain_a, cos, sin, *wa, [whole_b])
    kv0 = window(own)
    o0, lse0 = attend(q0, kv0, [wb[0][1], wb[0][2]])
    whole_d = hold(whole_d, [o0])
    weights = wa, wb, (whole_d, flip(whole_d, CORE))
    mixed0, h1_0, b0, gate0, up0, z0, h_1, a1, q1, own = post(False, [], sc, o0, h_0, gain_f, gain_a, cos, sin, own, *weights)
    kv1 = window(own)
    across_0 = across((a0, b0, mixed0, z0))
    cot = home_to_work(hold(cotangent[0].T, [kv1[1]]))
    o1, lse1 = attend(q1, kv1, across_0)
    mixed1, h1_1, b1, gate1, up1, z1, output = post(True, [cot], sc, o1, h_1, gain_f, gain_a, cos, sin, own, *weights)
    across_1 = across((a1, b1, mixed1, z1))

    gb1, act1, away1, g1, p1, dgain_f1, do = back(True, False, sc, weights, [cot], [gate1, up1, h1_1, gain_f])
    across_2 = across((gb1, away1))
    dq1, three1, far, near, own = attend_back(sc, p1, q1, kv1, lse1, do, cos, sin, [*across_1])
    near, _, far = unwindow(sc, far, near)
    (three1,) = across((three1,))
    output = home_to_work(hold(output, [far]), back=True)
    tail = [g1, dq1, own, near, far, h_1, gain_a, cos, sin]
    dk1, dv1, one1, dgain_a1, gb0, act0, away0, g1, p0, dgain_f0, do = back(False, False, sc, weights, tail, [gate0, up0, h1_0, gain_f], [three1, *across_2])

    away0, gb0_, one1 = across((away0, gb0, one1))
    dq0, three0, far, near, own = attend_back(sc, p0, q0, kv0, lse0, do, cos, sin, [one1, output])
    near, down_far, far = unwindow(sc, far, near)
    parts_d = grad_down(sc, [gb1, gb0, across_2[0], gb0_], [z1, z0, across_1[3], across_0[3]], [down_far])
    half_d = lax.psum_scatter(parts_d, "fsdp", scatter_dimension=0, tiled=False)
    send_b, keep_b = grad_ffn(sc, [b1, b0, across_1[1], across_0[1]], [act1, act0, across_2[1], away0], [parts_d, far])
    got_b = flip(send_b, SIDE, BACK)
    (three0,) = across((three0,))
    tail = [g1, dq0, own, near, far, h_0, gain_a, cos, sin]
    dk0, dv0, one0, dgain_a0, grad_tokens = back(False, True, sc, weights, tail, None, [send_b, three0])

    own = [dq1, dq0, dk1, dk0, dv1, dv0, p1, p0]
    got = [three1, three0, one1, flip(one0, CORE)]
    send_a, keep_a = grad_attention(sc, [a1, a0, across_1[0], across_0[0]], [mixed1, mixed0, across_1[2], across_0[2]], own, got, [dgain_a1, dgain_a0, dgain_f1, dgain_f0], [])
    got_a = flip(send_a, SIDE, BACK)
    later_b, own_b = sum_first(sc, keep_b, got_b, [send_a])
    more_b = flip(later_b, BACK, SIDE)
    grad_tokens = home_to_work(hold(grad_tokens, [later_b]), back=True)
    later_a, own_a = sum_first(sc, keep_a, got_a, [later_b])
    more_a = flip(later_a, BACK, SIDE)
    send_b, ring_b = sum_second(sc, own_b, more_b, [later_a])
    got_b = flip_z(send_b, 1)
    send_a, ring_a = sum_second(sc, own_a, more_a, [send_b])
    got_a = flip_z(send_a, 1)
    send_d, keep_d = down_split(sc, half_d, [send_a])
    got_d = flip(send_d, SIDE, BACK)
    send_b, ring_b = sum_third(sc, ring_b, got_b, [send_d, grad_tokens])
    got_b = flip_z(send_b, 2)
    send_a, ring_a = sum_third(sc, ring_a, got_a, [send_b])
    got_a = flip_z(send_a, 2)
    piece_b = over_groups(sum_two(sc, ring_b, got_b, [send_a]))
    all_b = spread(piece_b)
    later_d, own_d = sum_first(sc, keep_d, got_d, [piece_b])
    more_d = flip(later_d, BACK, SIDE)
    piece_a = over_groups(sum_two(sc, ring_a, got_a, [later_d]))
    all_a = spread(piece_a)
    piece_d = over_groups(sum_two(sc, own_d, more_d, [piece_a]))
    grad_gate, grad_up = lay(sc, all_b, across(all_b), (gate_weight.shape[1],) * 2, [piece_d])
    all_d = spread(piece_d)
    grad_query, grad_key, grad_value, grad_out, dgains = lay(sc, all_a, across(all_a), (width, KVW, KVW, width), [grad_gate])
    grad_down_ = lay_down(sc, all_d, across(all_d), [grad_query])
    grad_tokens, output = grad_tokens.astype(f32).T, output.T
    return (output[None], grad_tokens[None], dgains[0], grad_query, grad_key, grad_value, grad_out, dgains[1], grad_gate, grad_up, grad_down_.T)


def solution(mesh):
    wide, rows, shard = P("dp", "fsdp", None), P("dp", "fsdp"), P("fsdp", None)
    in_specs = (wide, rows, P("fsdp"), shard, shard, shard, shard, P("fsdp"), shard, shard, shard, wide)
    out_specs = (wide, wide, P("fsdp"), shard, shard, shard, shard, P("fsdp"), shard, shard, shard)
    return jax.shard_map(body, mesh=mesh, in_specs=in_specs, out_specs=out_specs, check_vma=False)
```

```python
import functools
import jax
import jax.numpy as jnp
from jax import lax
from jax.sharding import PartitionSpec as P
from jax.experimental import pallas as pl
from jax.experimental.pallas import tpu as pltpu

f32, bf16 = jnp.float32, jnp.bfloat16
eps = 1e-05
HEADS, KV_HEADS, HEAD_DIM, GROUP, KVW = 15, 5, 64, 3, 320
IDS = 16
ROWS = 128
PIECE = 384
LIMIT = 58 << 20
WHOLE = pl.BlockSpec(memory_space=pltpu.VMEM)
LEFT = pl.BlockSpec(memory_space=pl.ANY)
SCALARS = pl.BlockSpec(memory_space=pltpu.SMEM)
BRIEF = pl.CostEstimate(flops=1024, bytes_accessed=1024, transcendentals=0)


def contract(a, b, i, j):
    return lax.dot_general(a, b, (((i,), (j,)), ((), ())), preferred_element_type=f32)


def nn(a, b):
    return contract(a, b, 1, 0)


def nt(a, b):
    return contract(a, b, 1, 1)


def tn(a, b):
    return contract(a, b, 0, 0)


def whose(core):
    return 0, 1 + core, 2 - core, 3


def fetch(mine, other, kept, sems, core, chip):
    for kind, pieces in ((core, mine), (1 - core, other)):
        for who, piece in zip(whose(kind), pieces):
            at = chip ^ who
            pltpu.make_async_copy(piece, kept.at[kind, at], sems.at[kind, at]).start()


def arrived(kept, sems, *at):
    pltpu.make_async_copy(kept.at[at], kept.at[at], sems.at[at]).wait()


def normed(x, gain):
    return x * lax.rsqrt(jnp.mean(x * x, axis=-1, keepdims=True) + eps) * gain


def norm_back(x, gain, grad):
    r = lax.rsqrt(jnp.mean(x * x, axis=-1, keepdims=True) + eps)
    hat = x * r
    scaled = grad * gain
    dx = r * (scaled - hat * jnp.mean(scaled * hat, axis=-1, keepdims=True))
    return dx, jnp.sum(grad * hat, axis=0, keepdims=True)


def widened(x):
    return jnp.concatenate([x, jnp.zeros((x.shape[0], PIECE - x.shape[1]), x.dtype)], axis=1)


def rope(u, cos, sin, back):
    heads = u.shape[0] // HEAD_DIM
    half = HEAD_DIM // 2
    out = []
    for h in range(heads):
        u1, u2 = u[h * HEAD_DIM : h * HEAD_DIM + half], u[h * HEAD_DIM + half : (h + 1) * HEAD_DIM]
        if back:
            out += [u1 * cos + u2 * sin, u2 * cos - u1 * sin]
        else:
            out += [u1 * cos - u2 * sin, u2 * cos + u1 * sin]
    return jnp.concatenate(out, axis=0)


def project(state, gain_ref, cos_ref, sin_ref, ids, kept, sems, a_ref, q_ref, kv_ref):
    a = normed(state, gain_ref[...]).astype(bf16)
    a_ref[...] = a
    cos, sin = cos_ref[...], sin_ref[...]
    arrived(kept, sems, 0, 3)
    kv_ref[:KVW, :] = rope(nn(a, kept[0, 3, :, :KVW]).T, cos, sin, False).astype(bf16)
    arrived(kept, sems, 1, 0)
    kv_ref[2 * KVW :, :] = ids
    kv_ref[KVW : 2 * KVW, :] = nn(a, kept[1, 0, :, :KVW]).T.astype(bf16)
    for m in range(3):
        arrived(kept, sems, 0, m)
        q_ref[pl.ds(m * KVW, KVW), :] = rope(nn(a, kept[0, m, :, :KVW]).T, cos, sin, False).astype(bf16)


def pre_kernel(sc, ht_ref, gain_ref, cos_ref, sin_ref, *rest):
    width = ht_ref.shape[0] - IDS
    mine, other = rest[:4], rest[4:8]
    h_ref, a_ref, q_ref, kv_ref, kept, sems = rest[-6:]
    core, chip = sc[0], sc[1]
    fetch(mine, other, kept, sems, core, chip)
    h = ht_ref[:width, :].T
    h_ref[...] = h
    project(h.astype(f32), gain_ref, cos_ref, sin_ref, ht_ref[width:, :], kept, sems, a_ref, q_ref, kv_ref)
    for m in range(1, 4):
        arrived(kept, sems, 1, m)


def scratch_a(width):
    return [pltpu.VMEM((2, 4, width, PIECE), bf16), pltpu.SemaphoreType.DMA((2, 4))]


def shape(s, d):
    return jax.ShapeDtypeStruct(s, d)


def pre(sc, ht, gain, cos, sin, mine_a, other_a, after):
    width, n = ht.shape[0] - IDS, ht.shape[1]
    return pl.pallas_call(
        pre_kernel,
        out_shape=(shape((n, width), bf16), shape((n, width), bf16), shape((width, n), bf16), shape((2 * KVW + IDS, n), bf16)),
        in_specs=[SCALARS] + [WHOLE] * 4 + [LEFT] * (8 + len(after)),
        out_specs=(WHOLE,) * 4,
        scratch_shapes=scratch_a(width),
        cost_estimate=BRIEF,
        compiler_params=pltpu.CompilerParams(vmem_limit_bytes=LIMIT),
        name="pre",
    )(sc, ht, gain, cos, sin, *mine_a, *other_a, *after)


def bias_of(kv):
    keys, n = kv.shape[1], kv.shape[1] // 3
    ids = kv[2 * KVW :, :].astype(f32)
    seg_k, seg_q = ids.T[:, :1], ids[:1, 2 * n :]
    j = lax.broadcasted_iota(jnp.int32, (keys, n), 0)
    i = lax.broadcasted_iota(jnp.int32, (keys, n), 1) + (keys - n)
    return jnp.where((seg_k == seg_q) & (j <= i), 0.0, -1e30).astype(f32)


def window_of(parts, whole):
    n = parts[0].shape[1]
    for w, part in enumerate(parts):
        whole[:, w * n : (w + 1) * n] = part[...]


def attend_kernel(q_ref, kv0, kv1, kv2, *rest):
    o_ref, lse_ref, bias, kv = rest[-4:]
    window_of((kv0, kv1, kv2), kv)
    bias[...] = bias_of(kv)

    def head(e, _):
        row = pl.multiple_of(e * HEAD_DIM, HEAD_DIM)
        k = kv[pl.ds(row, HEAD_DIM), :]
        v = kv[pl.ds(row + KVW, HEAD_DIM), :]
        for g in range(GROUP):
            at = pl.multiple_of((e * GROUP + g) * HEAD_DIM, HEAD_DIM)
            q = q_ref[pl.ds(at, HEAD_DIM), :]
            s = tn(k, q) * HEAD_DIM ** (-0.5) + bias[...]
            top = jnp.max(s, axis=0, keepdims=True)
            expo = jnp.exp(s - top)
            total = jnp.sum(expo, axis=0, keepdims=True)
            probs = (expo * (1.0 / total)).astype(bf16)
            o_ref[pl.ds(at, HEAD_DIM), :] = nn(v, probs).astype(bf16)
            lse_ref[pl.ds(e * GROUP + g, 1), :] = top + jnp.log(total)
        return 0

    lax.fori_loop(0, KV_HEADS, head, 0)


def attend(q, kvs, after=()):
    width, n = q.shape
    return pl.pallas_call(
        attend_kernel,
        out_shape=(shape((width, n), bf16), shape((HEADS, n), f32)),
        in_specs=[WHOLE] * 4 + [LEFT] * len(after),
        out_specs=(WHOLE,) * 2,
        scratch_shapes=[pltpu.VMEM((3 * n, n), f32), pltpu.VMEM((2 * KVW + IDS, 3 * n), bf16)],
        cost_estimate=BRIEF,
        compiler_params=pltpu.CompilerParams(vmem_limit_bytes=24 << 20),
        name="attend",
    )(q, *kvs, *after)


def attend_back_kernel(sc, p_ref, q_ref, kv0, kv1, kv2, lse_ref, do_ref, cos_ref, sin_ref, *rest):
    dq_ref, three_ref, far_ref, near_ref, own_ref, bias, kv, dqs = rest[-8:]
    n = q_ref.shape[1]
    window_of((kv0, kv1, kv2), kv)
    bias[...] = bias_of(kv)
    scale = HEAD_DIM ** (-0.5)

    def head(e, _):
        row = pl.multiple_of(e * HEAD_DIM, HEAD_DIM)
        k = kv[pl.ds(row, HEAD_DIM), :]
        v = kv[pl.ds(row + KVW, HEAD_DIM), :]
        dk = dv = None
        for g in range(GROUP):
            at = pl.multiple_of((e * GROUP + g) * HEAD_DIM, HEAD_DIM)
            q = q_ref[pl.ds(at, HEAD_DIM), :]
            do = do_ref[pl.ds(at, HEAD_DIM), :]
            s = tn(k, q) * scale + bias[...]
            probs = jnp.exp(s - lse_ref[pl.ds(e * GROUP + g, 1), :])
            dp = tn(v, do)
            inner = jnp.sum(probs * dp, axis=0, keepdims=True)
            ds = (probs * (dp - inner)).astype(bf16)
            dvg, dkg = nt(do, probs.astype(bf16)), nt(q, ds)
            dv, dk = (dvg, dkg) if g == 0 else (dv + dvg, dk + dkg)
            dqs[pl.ds(at, HEAD_DIM), :] = nn(k, ds)
        for at, grad in ((row, dk * scale), (row + KVW, dv)):
            far_ref[pl.ds(at, HEAD_DIM), :] = grad[:, :n]
            near_ref[pl.ds(at, HEAD_DIM), :] = grad[:, n : 2 * n].astype(bf16)
            own_ref[pl.ds(at, HEAD_DIM), :] = grad[:, 2 * n :]
        return 0

    lax.fori_loop(0, KV_HEADS, head, 0)
    cos, sin = cos_ref[...] * scale, sin_ref[...] * scale
    for m in range(3):
        dq = widened(rope(dqs[m * KVW : (m + 1) * KVW, :], cos, sin, True).T.astype(bf16))
        dq_ref[m] = dq
        three_ref[m] = jnp.where(sc[0] == 0, p_ref[m], dq)


def attend_back(sc, p, q, kvs, lse, do, cos, sin, after=()):
    width, n = q.shape
    block = (2 * KVW, n)
    return pl.pallas_call(
        attend_back_kernel,
        out_shape=(shape((3, n, PIECE), bf16), shape((3, n, PIECE), bf16), shape(block, f32), shape(block, bf16), shape(block, f32)),
        in_specs=[SCALARS] + [WHOLE] * 9 + [LEFT] * len(after),
        out_specs=(WHOLE,) * 5,
        scratch_shapes=[pltpu.VMEM((3 * n, n), f32), pltpu.VMEM((2 * KVW + IDS, 3 * n), bf16), pltpu.VMEM((width, n), f32)],
        cost_estimate=BRIEF,
        compiler_params=pltpu.CompilerParams(vmem_limit_bytes=32 << 20),
        name="attend_back",
    )(sc, p, q, *kvs, lse, do, cos, sin, *after)


def down_rows(kind, chip, width):
    return jnp.minimum((kind * 4 + chip) * ROWS, width - ROWS)


def fetch_ffn(mine, other, wb, wd, sem_b, sem_d, core, chip):
    rows, width = wb.shape[3], wd.shape[1]
    last = width % ROWS
    for kind, pieces in ((core, mine), (1 - core, other)):
        for who, piece in zip(whose(kind), pieces):
            at = chip ^ who
            pltpu.make_async_copy(piece.at[:, :rows], wb.at[kind, at], sem_b.at[kind, at]).start()
    for kind, pieces in ((core, mine), (1 - core, other)):
        for who, piece in zip(whose(kind), pieces):
            at = kind * 4 + (chip ^ who)

            @pl.when(at < width // ROWS)
            def _():
                into = wd.at[:, pl.ds(pl.multiple_of(at * ROWS, ROWS), ROWS)]
                pltpu.make_async_copy(piece.at[:, rows:], into, sem_d).start()

            @pl.when(at == width // ROWS)
            def _():
                pltpu.make_async_copy(piece.at[:, rows + ROWS - last :], wd.at[:, width - last :], sem_d).start()


def whole(wb, c, m):
    _, rows, n = wb.shape[2:]
    return wb[c, m].reshape(4 * rows, n)


def arrived_down(wd, sem_d):
    pltpu.make_async_copy(wd, wd, sem_d).wait()


def scratch_ffn(width, n):
    return [
        pltpu.VMEM((2, 4, 4, width // 4, n), bf16),
        pltpu.SemaphoreType.DMA((2, 4)),
        pltpu.VMEM((4, width, n), bf16),
        pltpu.SemaphoreType.DMA,
    ]


def post_kernel(last, after, sc, ot_ref, h_ref, gain_ref, gain_a, cos_ref, sin_ref, *rest):
    mine_a, other_a, mine_b, other_b = rest[:4], rest[4:8], rest[8:12], rest[12:16]
    ids_ref, rest = rest[16], rest[17 + after :]
    o_ref, h1_ref, b_ref, gate_ref, up_ref, z_ref, next_ref = rest[:7]
    more, rest = rest[7 : 7 + (0 if last else 3)], rest[7 + (0 if last else 3) :]
    wa, sem_a, wb, sem_b, wd, sem_d = rest
    core, chip = sc[0], sc[1]
    fetch(mine_a, other_a, wa, sem_a, core, chip)
    fetch_ffn(mine_b, other_b, wb, wd, sem_b, sem_d, core, chip)
    o = ot_ref[...].T
    o_ref[...] = o
    for m in range(1, 4):
        arrived(wa, sem_a, 1, m)
    h1 = h_ref[...].astype(f32) + jnp.concatenate([nn(o, wa[1, m, :, :KVW]) for m in range(1, 4)], axis=1)
    h1_ref[...] = h1
    b = normed(h1, gain_ref[...]).astype(bf16)
    b_ref[...] = b
    n = wb.shape[4]
    total = h1
    for m in range(4):
        cols = slice(m * n, (m + 1) * n)
        arrived(wb, sem_b, 0, m)
        gate = nn(b, whole(wb, 0, m))
        arrived(wb, sem_b, 1, m)
        up = nn(b, whole(wb, 1, m))
        gate_ref[:, cols] = gate.astype(bf16)
        up_ref[:, cols] = up.astype(bf16)
        z = (gate / (1.0 + jnp.exp(-gate)) * up).astype(bf16)
        z_ref[:, cols] = z
        if m == 0:
            arrived_down(wd, sem_d)
        total = total + nt(z, wd[m])
    next_ref[...] = total.astype(bf16).T if last else total
    if last:
        arrived(wa, sem_a, 1, 0)
        for m in range(4):
            arrived(wa, sem_a, 0, m)
    else:
        project(total, gain_a, cos_ref, sin_ref, ids_ref[2 * KVW :, :], wa, sem_a, *more)


def post(last, after, sc, ot, h, gain, gain_a, cos, sin, kv, wa, wb):
    width, n = ot.shape
    hidden = wb[0][0].shape[2] * 4
    outs = [shape((n, width), bf16), shape((n, width), f32), shape((n, width), bf16)] + [shape((n, hidden), bf16)] * 3
    outs += [shape((width, n), bf16) if last else shape((n, width), f32)]
    if not last:
        outs += [shape((n, width), bf16), shape((width, n), bf16), shape((2 * KVW + IDS, n), bf16)]
    return pl.pallas_call(
        functools.partial(post_kernel, last, len(after)),
        out_shape=tuple(outs),
        in_specs=[SCALARS] + [WHOLE] * 6 + [LEFT] * 16 + [WHOLE] + [LEFT] * len(after),
        out_specs=(WHOLE,) * len(outs),
        scratch_shapes=scratch_a(width) + scratch_ffn(width, hidden // 4),
        cost_estimate=BRIEF,
        compiler_params=pltpu.CompilerParams(vmem_limit_bytes=LIMIT),
        name="post",
    )(sc, ot, h, gain, gain_a, cos, sin, *wa[0], *wa[1], *wb[0], *wb[1], kv, *after)


def ffn_back(state, core, refs, weights):
    gate_ref, up_ref, h1_ref, gain_ref, gb_ref, keep_ref, send_ref, g1_ref, p_ref, dgain_ref, do_ref = refs
    wa, sem_a, wb, sem_b, wd, sem_d = weights
    gb = state.astype(bf16)
    gb_ref[...] = gb
    n = wb.shape[4]
    first = core == 0
    arrived_down(wd, sem_d)
    db = None
    for m in range(4):
        cols = slice(m * n, (m + 1) * n)
        dz = nn(gb, wd[m])
        gate, up = gate_ref[:, cols].astype(f32), up_ref[:, cols].astype(f32)
        sig = 1.0 / (1.0 + jnp.exp(-gate))
        dup = (dz * (gate * sig)).astype(bf16)
        dgate = (dz * up * (sig * (1.0 + gate * (1.0 - sig)))).astype(bf16)
        keep_ref[:, cols] = jnp.where(first, dgate, dup)
        send_ref[:, cols] = jnp.where(first, dup, dgate)
        arrived(wb, sem_b, 0, m)
        part = nt(dgate, whole(wb, 0, m))
        arrived(wb, sem_b, 1, m)
        part = part + nt(dup, whole(wb, 1, m))
        db = part if m == 0 else db + part
    dx, dgain = norm_back(h1_ref[...], gain_ref[...], db)
    dgain_ref[...] = dgain
    g1 = state + dx
    g1_ref[...] = g1
    low = g1.astype(bf16)
    do = None
    for p in range(3):
        part = low[:, p * KVW : (p + 1) * KVW]
        p_ref[p] = widened(part)
        arrived(wa, sem_a, 1, p + 1)
        part = nt(wa[1, p + 1, :, :KVW], part)
        do = part if p == 0 else do + part
    do_ref[...] = do.astype(bf16)


def finish_a(wa, sem_a, *left):
    for at in left:
        arrived(wa, sem_a, *at)


def query_back(dq_ref, wa, sem_a):
    da = None
    for m in range(3):
        arrived(wa, sem_a, 0, m)
        part = nt(dq_ref[m, :, :KVW], wa[0, m, :, :KVW])
        da = part if m == 0 else da + part
    return da


def project_back(da, own_ref, near_ref, far_ref, core, cos_ref, sin_ref, dk_ref, dv_ref, one_ref, h, gain, wa, sem_a):
    cos, sin = cos_ref[...], sin_ref[...]
    grad = own_ref[...] + far_ref[...].astype(f32) + jnp.where(core == 0, near_ref[...].astype(f32), 0.0)
    dk = rope(grad[:KVW], cos, sin, True).T.astype(bf16)
    dv = grad[KVW:].T.astype(bf16)
    dk_ref[...] = widened(dk)
    dv_ref[...] = widened(dv)
    one_ref[...] = widened(jnp.where(core == 0, dv, dk))
    arrived(wa, sem_a, 0, 3)
    arrived(wa, sem_a, 1, 0)
    da = da + nt(dk, wa[0, 3, :, :KVW]) + nt(dv, wa[1, 0, :, :KVW])
    return norm_back(h, gain, da)


def back_kernel(start, end, after, sc, *rest):
    rest = list(rest)

    def take(n):
        out = rest[:n]
        del rest[:n]
        return out

    core, chip = sc[0], sc[1]
    mine_a, other_a = take(4), take(4)
    if not end:
        mine_b, other_b = take(4), take(4)
    if start:
        (g_ref,) = take(1)
    else:
        g1_in, dq_ref, own_ref, near_ref, far_ref, h_ref, gain_a, cos_ref, sin_ref = take(9)
    if not end:
        ins = take(4)
    take(after)
    if not start:
        dk_ref, dv_ref, one_ref, dgain_a = take(4)
    if end:
        (g_out,) = take(1)
    else:
        outs = take(7)
    wa, sem_a = take(2)
    fetch(mine_a, other_a, wa, sem_a, core, chip)
    if not end:
        wb, sem_b, wd, sem_d = take(4)
        fetch_ffn(mine_b, other_b, wb, wd, sem_b, sem_d, core, chip)
    if start:
        state = g_ref[...].T.astype(f32)
    else:
        da = query_back(dq_ref, wa, sem_a)
        dx, dgain = project_back(da, own_ref, near_ref, far_ref, core, cos_ref, sin_ref, dk_ref, dv_ref, one_ref, h_ref[...].astype(f32), gain_a[...], wa, sem_a)
        dgain_a[...] = dgain
        state = g1_in[...] + dx
    if end:
        g_out[...] = state.astype(bf16).T
        finish_a(wa, sem_a, (1, 1), (1, 2), (1, 3))
    else:
        ffn_back(state, core, (*ins, *outs), (wa, sem_a, wb, sem_b, wd, sem_d))
        if start:
            finish_a(wa, sem_a, (1, 0), (0, 0), (0, 1), (0, 2), (0, 3))


def back(start, end, sc, weights, tail, ffn, after=()):
    wa, wb = weights
    width = wa[0][0].shape[0]
    args = [sc, *wa[0], *wa[1]]
    specs = [SCALARS] + [LEFT] * 8
    scratch = scratch_a(width)
    if not end:
        args += [*wb[0], *wb[1]]
        specs += [LEFT] * 8
        scratch += scratch_ffn(width, wb[0][0].shape[2])
    args += list(tail)
    specs += [WHOLE] * len(tail)
    n = tail[0].shape[1 if start else 0]
    outs = []
    if not end:
        args += list(ffn)
        specs += [WHOLE] * len(ffn)
    if not start:
        outs += [shape((n, PIECE), bf16)] * 3 + [shape((1, width), f32)]
    if end:
        outs += [shape((width, n), bf16)]
    else:
        hidden = ffn[0].shape[1]
        outs += [shape((n, width), bf16), shape((n, hidden), bf16), shape((n, hidden), bf16)]
        outs += [shape((n, width), f32), shape((3, n, PIECE), bf16), shape((1, width), f32), shape((width, n), bf16)]
    args += list(after)
    specs += [LEFT] * len(after)
    return pl.pallas_call(
        functools.partial(back_kernel, start, end, len(after)),
        out_shape=tuple(outs),
        in_specs=specs,
        out_specs=(WHOLE,) * len(outs),
        scratch_shapes=scratch,
        cost_estimate=BRIEF,
        compiler_params=pltpu.CompilerParams(vmem_limit_bytes=LIMIT),
        name="back_end" if end else ("back_start" if start else "back_join"),
    )(*args)


def by_turn(core, chip):
    one = 1 + core
    return chip ^ one, chip ^ 3, chip, chip ^ (3 - one)


def turned(dst, blocks):
    n = blocks[0].shape[0]
    for i, block in enumerate(blocks):
        dst[:, i * n : (i + 1) * n] = block[...].T


def grad_ffn_kernel(sc, *rest):
    lefts, rights = rest[:4], rest[4:8]
    send_ref, keep_ref, left, right = rest[-4:]
    core, chip = sc[0], sc[1]
    n, cols = rights[0].shape[0], right.shape[1]
    turned(left, lefts)
    for i, m in enumerate(by_turn(core, chip)):
        at = pl.multiple_of(m * cols, 128)
        for j, block in enumerate(rights):
            right[j * n : (j + 1) * n, :] = block[:, pl.ds(at, cols)]
        out = send_ref if i < 2 else keep_ref
        out[i % 2] = nn(left[...], right[...]).astype(bf16)


def grad_ffn(sc, lefts, rights, after):
    n, width = lefts[0].shape
    cols = rights[0].shape[1] // 4
    out = shape((2, width, cols), bf16)
    return pl.pallas_call(
        grad_ffn_kernel,
        out_shape=(out, out),
        in_specs=[SCALARS] + [WHOLE] * 8 + [LEFT] * len(after),
        out_specs=(WHOLE,) * 2,
        scratch_shapes=[pltpu.VMEM((width, 4 * n), bf16), pltpu.VMEM((4 * n, cols), bf16)],
        cost_estimate=BRIEF,
        compiler_params=pltpu.CompilerParams(vmem_limit_bytes=LIMIT),
        name="grad_ffn",
    )(sc, *lefts, *rights, *after)


def grad_down_kernel(sc, *rest):
    lefts, rights = rest[:4], rest[4:8]
    send_ref, keep_ref, left, right = rest[-4:]
    n, (_, half, cols) = rights[0].shape[0], send_ref.shape
    turned(left, lefts)
    rows = pl.ds(pl.multiple_of(sc[0] * half, half), half)
    like = sc[2] & 1
    for h in range(2):
        for out, parity in ((send_ref, 1 - like), (keep_ref, like)):
            at = pl.multiple_of((2 * h + parity) * cols, 128)
            for j, block in enumerate(rights):
                right[j * n : (j + 1) * n, :] = block[:, pl.ds(at, cols)]
            out[h] = nn(left[rows, :], right[...]).astype(out.dtype)


def grad_down(sc, lefts, rights, after):
    n, width = lefts[0].shape
    cols = rights[0].shape[1] // 4
    block = (2, width // 2, cols)
    return pl.pallas_call(
        grad_down_kernel,
        out_shape=(shape(block, bf16), shape(block, bf16)),
        in_specs=[SCALARS] + [WHOLE] * 8 + [LEFT] * len(after),
        out_specs=(WHOLE,) * 2,
        scratch_shapes=[pltpu.VMEM((width, 4 * n), bf16), pltpu.VMEM((4 * n, cols), bf16)],
        cost_estimate=BRIEF,
        compiler_params=pltpu.CompilerParams(vmem_limit_bytes=LIMIT),
        name="grad_down",
    )(sc, *lefts, *rights, *after)


def grad_attention_kernel(sc, *rest):
    a_refs, o_refs, rest = rest[:4], rest[4:8], rest[8:]
    queries, keys, values, outs, threes, ones = (rest[i : i + 2] for i in range(0, 12, 2))
    gain_a, gain_f = (rest[i : i + 2] for i in (12, 14))
    send_ref, keep_ref, left, right = rest[-4:]
    core, chip = sc[0], sc[1]
    n, width = a_refs[0].shape
    turned(left.at[0], a_refs)
    gains = [g[0][...] + g[1][...] for g in (gain_a, gain_f)]
    gains = jnp.concatenate([*gains, jnp.zeros((6, width), f32)], axis=0).T
    gains = jnp.concatenate([gains, jnp.zeros((width, PIECE - KVW - 8), f32)], axis=1).astype(bf16)

    def fill(at, of_three, own_three, own_one, single):
        for j in range(2):
            for i in range(3):
                right[of_three + i, j * n : (j + 1) * n, :] = own_three[j][i]
                right[of_three + i, (j + 2) * n : (j + 3) * n, :] = threes[j][i]
            right[single, j * n : (j + 1) * n, :] = own_one[j][...]
            right[single, (j + 2) * n : (j + 3) * n, :] = ones[j][...]

    @pl.when(core == 0)
    def _():
        fill(0, 0, queries, keys, 3)

    @pl.when(core == 1)
    def _():
        turned(left.at[1], o_refs)
        fill(0, 1, outs, values, 0)

    for i, m in enumerate(by_turn(core, chip)):
        out = send_ref if i < 2 else keep_ref
        which = jnp.where(m > 0, core, 0)
        out[i % 2] = nn(left[which], right[m]).astype(bf16)
        out[i % 2, :, KVW:] = gains


def grad_attention(sc, a, o, own, got, gains, after):
    n, width = a[0].shape
    out = shape((2, width, PIECE), bf16)
    return pl.pallas_call(
        grad_attention_kernel,
        out_shape=(out, out),
        in_specs=[SCALARS] + [WHOLE] * 24 + [LEFT] * len(after),
        out_specs=(WHOLE,) * 2,
        scratch_shapes=[pltpu.VMEM((2, width, 4 * n), bf16), pltpu.VMEM((4, 4 * n, PIECE), bf16)],
        cost_estimate=BRIEF,
        compiler_params=pltpu.CompilerParams(vmem_limit_bytes=LIMIT),
        name="grad_attention",
    )(sc, *a, *o, *own, *got, *gains, *after)


def lay_kernel(count, sc, *rest):
    mine, other, outs, kept = rest[:4], rest[4:8], rest[-1 - count : -1], rest[-1]
    core, chip = sc[0], sc[1]
    for kind, pieces in ((core, mine), (1 - core, other)):
        for who, piece in zip(whose(kind), pieces):
            kept[kind, chip ^ who] = piece[...]
    n = sum(o.shape[1] for o in outs[: 4 if len(outs) > 2 else 2]) // 8
    cols = [jnp.concatenate([kept[c, m, :, :n].astype(f32) for m in range(4)], axis=1) for c in range(2)]
    if len(outs) == 2:
        outs[0][...] = cols[0]
        outs[1][...] = cols[1]
    else:
        outs[0][...] = cols[0][:, : 3 * n]
        outs[1][...] = cols[0][:, 3 * n :]
        outs[2][...] = cols[1][:, :n]
        outs[3][...] = cols[1][:, n:]
        gains = kept[0, 0, :, n : n + 8].astype(f32) + kept[1, 0, :, n : n + 8].astype(f32)
        outs[4][...] = gains.T[:2]


def lay(sc, mine, other, widths, after):
    rows, n = mine[0].shape
    outs = tuple(shape((rows, w), f32) for w in widths)
    if len(widths) > 2:
        outs += (shape((2, rows), f32),)
    return pl.pallas_call(
        functools.partial(lay_kernel, len(outs)),
        out_shape=outs,
        in_specs=[SCALARS] + [WHOLE] * 8 + [LEFT] * len(after),
        out_specs=(WHOLE,) * len(outs),
        scratch_shapes=[pltpu.VMEM((2, 4, rows, n), bf16)],
        cost_estimate=BRIEF,
        compiler_params=pltpu.CompilerParams(vmem_limit_bytes=24 << 20),
        name="lay",
    )(sc, *mine, *other, *after)


def pick_first_kernel(sc, q_ref, k_ref, v_ref, o_ref, gain_ref, out_ref):
    rows = out_ref.shape[0]
    which = sc[0] * 4 + sc[1]
    pad = jnp.zeros((6, rows), f32)
    gains = jnp.concatenate([gain_ref[...], pad], axis=0).T.astype(bf16)
    rest = jnp.zeros((rows, PIECE - KVW - 8), bf16)
    for at in range(8):

        @pl.when(which == at)
        def _():
            if at in (3, 4):
                piece = (k_ref if at == 3 else v_ref)[...].T
            else:
                source, m = (q_ref, at) if at < 3 else (o_ref, at - 5)
                piece = source[:, m * KVW : (m + 1) * KVW]
            out_ref[...] = jnp.concatenate([piece, gains, rest], axis=1)


def pick_first(sc, query, key, value, out, gains):
    return pl.pallas_call(
        pick_first_kernel,
        out_shape=shape((query.shape[0], PIECE), bf16),
        in_specs=[SCALARS] + [WHOLE] * 5,
        out_specs=WHOLE,
        cost_estimate=BRIEF,
        compiler_params=pltpu.CompilerParams(vmem_limit_bytes=16 << 20),
        name="pick_first",
    )(sc, query, key, value, out, gains)


def pick_kernel(sc, gate, up, down, *rest):
    out_ref, sems = rest[-2:]
    rows, cols = out_ref.shape[0] - ROWS, out_ref.shape[1]
    into = out_ref.at[:rows]
    start = pl.multiple_of(down_rows(sc[0], sc[1], down.shape[0]), 64)
    copy = pltpu.make_async_copy(down.at[pl.ds(start, ROWS), :], out_ref.at[rows:], sems.at[1])
    copy.start()
    at = pl.ds(pl.multiple_of(sc[1] * cols, 128), cols)
    for c, source in ((0, gate), (1, up)):

        @pl.when(sc[0] == c)
        def _():
            pltpu.make_async_copy(source.at[:, at], into, sems.at[0]).start()

    pltpu.make_async_copy(gate.at[:, at], into, sems.at[0]).wait()
    copy.wait()


def pick(sc, gate, up, down, after):
    return pl.pallas_call(
        pick_kernel,
        out_shape=shape((gate.shape[0] + ROWS, gate.shape[1] // 4), bf16),
        in_specs=[SCALARS] + [LEFT] * (3 + len(after)),
        out_specs=WHOLE,
        scratch_shapes=[pltpu.SemaphoreType.DMA((2,))],
        cost_estimate=BRIEF,
        compiler_params=pltpu.CompilerParams(vmem_limit_bytes=16 << 20),
        name="pick",
    )(sc, gate, up, down, *after)


def gains_kernel(first_ref, out_ref):
    for j in range(4):
        n = first_ref.shape[1]
        out_ref[:, j * n : (j + 1) * n] = first_ref[j, :, KVW : KVW + 8].astype(f32).T[:2]


def gains_of(first):
    return pl.pallas_call(
        gains_kernel,
        out_shape=shape((2, 4 * first.shape[1]), f32),
        in_specs=[WHOLE],
        out_specs=WHOLE,
        cost_estimate=BRIEF,
        compiler_params=pltpu.CompilerParams(vmem_limit_bytes=16 << 20),
        name="gains",
    )(first)


def stack_kernel(sc, *rest):
    parts, out_ref, sems = rest[:4], rest[-2], rest[-1]
    copies = [pltpu.make_async_copy(p, out_ref.at[sc[2] ^ s], sems.at[s]) for s, p in enumerate(parts)]
    for copy in copies:
        copy.start()
    for copy in copies:
        copy.wait()


def stack(sc, parts, after=()):
    return pl.pallas_call(
        stack_kernel,
        out_shape=shape((4,) + parts[0].shape, parts[0].dtype),
        in_specs=[SCALARS] + [LEFT] * (4 + len(after)),
        out_specs=WHOLE,
        scratch_shapes=[pltpu.SemaphoreType.DMA((4,))],
        cost_estimate=BRIEF,
        compiler_params=pltpu.CompilerParams(vmem_limit_bytes=16 << 20),
        name="stack",
    )(sc, *parts, *after)


def small(kernel, sc, args, outs, scratch, after, name):
    return pl.pallas_call(
        kernel,
        out_shape=tuple(outs),
        in_specs=[SCALARS] + [WHOLE] * len(args) + [LEFT] * len(after),
        out_specs=(WHOLE,) * len(outs),
        scratch_shapes=scratch,
        cost_estimate=BRIEF,
        compiler_params=pltpu.CompilerParams(vmem_limit_bytes=32 << 20),
        name=name,
    )(sc, *args, *after)


def sum_first(sc, keep, got, after):
    def kernel(sc, keep_ref, got_ref, *rest):
        later_ref, own_ref = rest[-2:]
        later_ref[...] = (keep_ref[1].astype(f32) + got_ref[1].astype(f32)).astype(bf16)
        own_ref[...] = keep_ref[0].astype(f32) + got_ref[0].astype(f32)

    block = keep.shape[1:]
    return small(kernel, sc, [keep, got], [shape(block, bf16), shape(block, f32)], [], after, "sum_first")


def sum_second(sc, own, got, after):
    def kernel(sc, own_ref, got_ref, *rest):
        send_ref, keep_ref, total = rest[-3:]
        n = total.shape[1]
        for j in range(4):
            rows = slice(j * n, (j + 1) * n)
            total[j] = own_ref[rows, :] + got_ref[rows, :].astype(f32)
        like = sc[2] & 1
        for h in range(2):
            send_ref[h] = total[2 * h + 1 - like].astype(bf16)
            keep_ref[h] = total[2 * h + like]

    rows, cols = own.shape
    part = (rows // 4, cols)
    outs = [shape((2,) + part, bf16), shape((2,) + part, f32)]
    return small(kernel, sc, [own, got], outs, [pltpu.VMEM((4,) + part, f32)], after, "sum_second")


def sum_third(sc, keep, got, after):
    def kernel(sc, keep_ref, got_ref, *rest):
        send_ref, own_ref = rest[-2:]
        h = sc[2] >> 1
        send_ref[...] = (keep_ref[1 - h].astype(f32) + got_ref[1 - h].astype(f32)).astype(bf16)
        own_ref[...] = keep_ref[h].astype(f32) + got_ref[h].astype(f32)

    part = keep.shape[1:]
    return small(kernel, sc, [keep, got], [shape(part, bf16), shape(part, f32)], [], after, "sum_third")


def down_split(sc, own, got, after):
    def kernel(sc, own_ref, got_ref, *rest):
        send_ref, kept_ref, total = rest[-3:]
        n = total.shape[1]
        for m in range(4):
            rows = slice(m * n, (m + 1) * n)
            total[m] = own_ref[rows, :] + got_ref[rows, :].astype(f32)
        for i, m in enumerate(by_turn(sc[0], sc[1])):
            out = send_ref if i < 2 else kept_ref
            out[i % 2] = total[m].astype(bf16)

    rows, cols = own.shape
    out = shape((2, rows // 4, cols), bf16)
    return small(kernel, sc, [own, got], [out, out], [pltpu.VMEM((4, rows // 4, cols), f32)], after, "down_split")


def sum_two(sc, own, got, after):
    def kernel(sc, own_ref, got_ref, *rest):
        rest[-1][...] = (own_ref[...] + got_ref[...].astype(f32)).astype(bf16)

    return small(kernel, sc, [own, got], [shape(own.shape, bf16)], [], after, "sum_two")[0]


def lay_down(sc, mine, other, after):
    def kernel(sc, *rest):
        out_ref, total = rest[-2:]
        n = total.shape[2]
        for kind, pieces in ((sc[0], rest[:4]), (1 - sc[0], rest[4:8])):
            for who, piece in zip(whose(kind), pieces):
                total[kind, sc[1] ^ who] = piece[...].astype(f32)
        for c in range(2):
            for m in range(4):
                at = (c * 4 + m) * n
                out_ref[at : at + n, :] = total[c, m]

    n, cols = mine[0].shape
    return small(kernel, sc, [*mine, *other], [shape((8 * n, cols), f32)], [pltpu.VMEM((2, 4, n, cols), f32)], after, "lay_down")[0]


def hold(value, after):
    return pl.pallas_call(
        lambda *refs: None,
        out_shape=shape(value.shape, value.dtype),
        in_specs=[LEFT] * (1 + len(after)),
        out_specs=LEFT,
        input_output_aliases={0: 0},
        cost_estimate=BRIEF,
        compiler_params=pltpu.CompilerParams(vmem_limit_bytes=1 << 20),
        name="hold",
    )(value, *after)


def far_sum(sc, far, near, after):
    def kernel(sc, far_ref, near_ref, *rest):
        rest[-1][...] = (far_ref[...] + jnp.where(sc[0] == 1, near_ref[...].astype(f32), 0.0)).astype(bf16)

    return small(kernel, sc, [far, near], [shape(far.shape, bf16)], [], after, "far_sum")[0]


CORE, SIDE, BACK = 1, 2, 4
rope_base = 10000.0
RUNS = 2


def flip(value, bit, bit1=None):
    count = lax.axis_size("dp")
    bits = (bit, bit if bit1 is None else bit1)
    return lax.ppermute(value, "dp", [(i, i ^ bits[i & 1]) for i in range(count)])


def flip_z(value, bit, where=lambda d, z: True):
    count, depth = lax.axis_size("dp"), lax.axis_size("fsdp")
    pairs = [(d * depth + z, d * depth + (z ^ bit)) for d in range(count) for z in range(depth) if where(d, z)]
    return lax.ppermute(value, ("dp", "fsdp"), pairs)


def home_to_work(value, back=False):
    count, depth = lax.axis_size("dp"), lax.axis_size("fsdp")
    pairs = []
    for d in range(count):
        for z in range(depth):
            there = (d & ~1) | (z & 1), 2 * (d & 1) + (z >> 1)
            pair = (d * depth + z, there[0] * depth + there[1])
            pairs.append(pair[::-1] if back else pair)
    return lax.ppermute(value, ("dp", "fsdp"), pairs)


def place():
    d, z = lax.axis_index("dp"), lax.axis_index("fsdp")
    return d & 1, (d >> 1) & 3, z


def turns(shard):
    far = flip_z(shard, 2)
    return shard, flip_z(shard, 1), far, flip_z(far, 1)


def plane_gather(piece):
    first, second = flip(piece, SIDE, BACK), flip(piece, BACK, SIDE)
    mine = (piece, first, second, flip(first, BACK, SIDE))
    return mine, tuple(flip(p, CORE) for p in mine)


def window(own):
    core, _, _ = place()
    depth = lax.axis_size("fsdp")
    far = lax.ppermute(own, "fsdp", [(z, z + 1) for z in range(0, depth, 2)])
    near = flip(jnp.where(core == 0, own, far), CORE)
    return far, near, own


def unwindow(sc, far, near, after=()):
    depth = lax.axis_size("fsdp")
    near = flip(near, CORE)
    far = far_sum(sc, far, near, after)
    return near, far, lax.ppermute(far, "fsdp", [(z + 1, z) for z in range(0, depth, 2)])


def over_groups(value):
    bit = 8
    while bit < lax.axis_size("dp"):
        value = (value.astype(f32) + flip(value, bit).astype(f32)).astype(bf16)
        bit *= 2
    return value


def spread(piece):
    return piece, flip(piece, SIDE, BACK), flip(piece, BACK, SIDE), flip(piece, SIDE | BACK)


def across(pieces):
    return tuple(flip(p, CORE) for p in pieces)


def body(tokens, segment_ids, attn_gain, query_weight, key_weight, value_weight, out_weight, ffn_gain, gate_weight, up_weight, down_weight, cotangent):
    core, chip, z = place()
    sc = jnp.stack([core, chip, z]).astype(jnp.int32)
    _, stretch, width = tokens.shape
    rows, depth = query_weight.shape[0], lax.axis_size("fsdp")
    block = 2 * (z & 1) + core
    positions = (block * stretch + jnp.arange(stretch)).astype(f32)
    freq = rope_base ** (-2.0 * jnp.arange(HEAD_DIM // 2, dtype=f32) / HEAD_DIM)
    angle = freq[:, None] * positions[None, :]
    cos, sin = jnp.cos(angle), jnp.sin(angle)

    gains = jnp.stack([attn_gain, ffn_gain]).astype(f32)
    parts_a = turns(pick_first(sc, query_weight, key_weight.T, value_weight.T, out_weight, gains))
    ids = jnp.broadcast_to((segment_ids[0] + 1).astype(bf16), (IDS, stretch))
    tokens = home_to_work(jnp.concatenate([tokens[0].T, ids]))
    piece_b = pick(sc, gate_weight, up_weight, down_weight.T, parts_a[1:2])
    whole_a = stack(sc, parts_a, [piece_b])
    gains = gains_of(whole_a)
    gain_a, gain_f = gains[:1], gains[1:]
    wa = plane_gather(whole_a.reshape(depth * rows, PIECE))
    far_b = hold(flip_z(piece_b, 2), [wa[0][1], wa[0][2]])
    whole_b = stack(sc, (piece_b, flip_z(piece_b, 1), far_b, flip_z(far_b, 1)), [wa[0][3]])
    first_b, second_b = flip(whole_b, SIDE, BACK), flip(whole_b, BACK, SIDE)

    h_0, a0, q0, own = pre(sc, tokens, gain_a, cos, sin, *wa, [whole_b])
    kv0 = window(own)
    first_b = hold(first_b, [kv0[0], second_b])
    opposite_b = flip(first_b, BACK, SIDE)
    o0, lse0 = attend(q0, kv0)
    wb = whole_b, first_b, second_b, hold(opposite_b, [o0])
    wb = wb, across(wb)
    weights = wa, wb
    mixed0, h1_0, b0, gate0, up0, z0, h_1, a1, q1, own = post(False, [], sc, o0, h_0, gain_f, gain_a, cos, sin, own, *weights)
    kv1 = window(own)
    across_0 = across((a0, b0, mixed0, z0))
    cot = home_to_work(hold(cotangent[0].T, [kv1[1]]))
    o1, lse1 = attend(q1, kv1, across_0)
    mixed1, h1_1, b1, gate1, up1, z1, output = post(True, [cot], sc, o1, h_1, gain_f, gain_a, cos, sin, own, *weights)
    across_1 = across((a1, b1, mixed1, z1))

    gb1, act1, away1, g1, p1, dgain_f1, do = back(True, False, sc, weights, [cot], [gate1, up1, h1_1, gain_f])
    across_2 = across((gb1, away1))
    dq1, three1, far, near, own = attend_back(sc, p1, q1, kv1, lse1, do, cos, sin, [*across_1])
    near, _, far = unwindow(sc, far, near)
    (three1,) = across((three1,))
    output = home_to_work(hold(output, [far]), back=True)
    tail = [g1, dq1, own, near, far, h_1, gain_a, cos, sin]
    dk1, dv1, one1, dgain_a1, gb0, act0, away0, g1, p0, dgain_f0, do = back(False, False, sc, weights, tail, [gate0, up0, h1_0, gain_f], [three1, *across_2])

    away0, gb0_, one1 = across((away0, gb0, one1))
    dq0, three0, far, near, own = attend_back(sc, p0, q0, kv0, lse0, do, cos, sin, [one1, output])
    near, down_far, far = unwindow(sc, far, near)
    send_b, keep_b = grad_ffn(sc, [b1, b0, across_1[1], across_0[1]], [act1, act0, across_2[1], away0], [down_far])
    got_b = flip(send_b, SIDE, BACK)
    send_d, keep_d = grad_down(sc, [gb1, gb0, across_2[0], gb0_], [z1, z0, across_1[3], across_0[3]], [send_b])
    got_d = flip_z(send_d, 1)
    (three0,) = across((three0,))
    tail = [g1, dq0, own, near, far, h_0, gain_a, cos, sin]
    dk0, dv0, one0, dgain_a0, grad_tokens = back(False, True, sc, weights, tail, None, [send_d, three0])

    own = [dq1, dq0, dk1, dk0, dv1, dv0, p1, p0]
    got = [three1, three0, one1, flip(one0, CORE)]
    send_a, keep_a = grad_attention(sc, [a1, a0, across_1[0], across_0[0]], [mixed1, mixed0, across_1[2], across_0[2]], own, got, [dgain_a1, dgain_a0, dgain_f1, dgain_f0], [])
    got_a = flip(send_a, SIDE, BACK)
    later_b, own_b = sum_first(sc, keep_b, got_b, [send_a])
    more_b = flip(later_b, BACK, SIDE)
    send_d, keep_d = sum_third(sc, keep_d, got_d, [later_b])
    got_d = flip_z(send_d, 2)
    later_a, own_a = sum_first(sc, keep_a, got_a, [send_d])
    more_a = flip(later_a, BACK, SIDE)
    send_b, ring_b = sum_second(sc, own_b, more_b, [later_a])
    got_b = flip_z(send_b, 1)
    send_a, ring_a = sum_second(sc, own_a, more_a, [send_b])
    got_a = flip_z(send_a, 1)
    send_b, ring_b = sum_third(sc, ring_b, got_b, [send_a])
    got_b = flip_z(send_b, 2)
    send_d, keep_d = down_split(sc, keep_d, got_d, [send_b])
    got_d = flip(send_d, SIDE, BACK)
    send_a, ring_a = sum_third(sc, ring_a, got_a, [send_d])
    got_a = flip_z(send_a, 2)
    piece_b = over_groups(sum_two(sc, ring_b, got_b, [send_a]))
    all_b = spread(piece_b)
    later_d, own_d = sum_first(sc, keep_d, got_d, [piece_b])
    more_d = flip(later_d, BACK, SIDE)
    piece_a = over_groups(sum_two(sc, ring_a, got_a, [later_d]))
    all_a = spread(piece_a)
    piece_d = over_groups(sum_two(sc, own_d, more_d, [piece_a]))
    grad_gate, grad_up = lay(sc, all_b, across(all_b), (gate_weight.shape[1],) * 2, [piece_d])
    all_d = spread(piece_d)
    grad_query, grad_key, grad_value, grad_out, dgains = lay(sc, all_a, across(all_a), (width, KVW, KVW, width), [grad_gate])
    grad_down_ = lay_down(sc, all_d, across(all_d), [grad_query])
    grad_tokens = home_to_work(hold(grad_tokens, [piece_a]), back=True)
    grad_tokens, output = grad_tokens.astype(f32).T, output.T
    return (output[None], grad_tokens[None], dgains[0], grad_query, grad_key, grad_value, grad_out, dgains[1], grad_gate, grad_up, grad_down_.T)


def solution(mesh):
    wide, rows, shard = P("dp", "fsdp", None), P("dp", "fsdp"), P("fsdp", None)
    in_specs = (wide, rows, P("fsdp"), shard, shard, shard, shard, P("fsdp"), shard, shard, shard, wide)
    out_specs = (wide, wide, P("fsdp"), shard, shard, shard, shard, P("fsdp"), shard, shard, shard)
    return jax.shard_map(body, mesh=mesh, in_specs=in_specs, out_specs=out_specs, check_vma=False)
```

```python
import functools
import jax
import jax.numpy as jnp
from jax import lax
from jax.sharding import PartitionSpec as P
from jax.experimental import pallas as pl
from jax.experimental.pallas import tpu as pltpu

f32, bf16 = jnp.float32, jnp.bfloat16
eps = 1e-05
HEADS, KV_HEADS, HEAD_DIM, GROUP, KVW = 15, 5, 64, 3, 320
IDS = 16
ROWS = 128
PIECE = 384
LIMIT = 58 << 20
WHOLE = pl.BlockSpec(memory_space=pltpu.VMEM)
LEFT = pl.BlockSpec(memory_space=pl.ANY)
SCALARS = pl.BlockSpec(memory_space=pltpu.SMEM)
BRIEF = pl.CostEstimate(flops=1024, bytes_accessed=1024, transcendentals=0)


def contract(a, b, i, j):
    return lax.dot_general(a, b, (((i,), (j,)), ((), ())), preferred_element_type=f32)


def nn(a, b):
    return contract(a, b, 1, 0)


def nt(a, b):
    return contract(a, b, 1, 1)


def tn(a, b):
    return contract(a, b, 0, 0)


def whose(core):
    return 0, 1 + core, 2 - core, 3


def fetch(mine, other, kept, sems, core, chip):
    for kind, pieces in ((core, mine), (1 - core, other)):
        for who, piece in zip(whose(kind), pieces):
            at = chip ^ who
            pltpu.make_async_copy(piece, kept.at[kind, at], sems.at[kind, at]).start()


def arrived(kept, sems, *at):
    pltpu.make_async_copy(kept.at[at], kept.at[at], sems.at[at]).wait()


def normed(x, gain):
    return x * lax.rsqrt(jnp.mean(x * x, axis=-1, keepdims=True) + eps) * gain


def norm_back(x, gain, grad):
    r = lax.rsqrt(jnp.mean(x * x, axis=-1, keepdims=True) + eps)
    hat = x * r
    scaled = grad * gain
    dx = r * (scaled - hat * jnp.mean(scaled * hat, axis=-1, keepdims=True))
    return dx, jnp.sum(grad * hat, axis=0, keepdims=True)


def widened(x):
    return jnp.concatenate([x, jnp.zeros((x.shape[0], PIECE - x.shape[1]), x.dtype)], axis=1)


def rope(u, cos, sin, back):
    heads = u.shape[0] // HEAD_DIM
    half = HEAD_DIM // 2
    out = []
    for h in range(heads):
        u1, u2 = u[h * HEAD_DIM : h * HEAD_DIM + half], u[h * HEAD_DIM + half : (h + 1) * HEAD_DIM]
        if back:
            out += [u1 * cos + u2 * sin, u2 * cos - u1 * sin]
        else:
            out += [u1 * cos - u2 * sin, u2 * cos + u1 * sin]
    return jnp.concatenate(out, axis=0)


def project(state, gain_ref, cos_ref, sin_ref, ids, kept, sems, a_ref, q_ref, kv_ref):
    a = normed(state, gain_ref[...]).astype(bf16)
    a_ref[...] = a
    cos, sin = cos_ref[...], sin_ref[...]
    arrived(kept, sems, 0, 3)
    kv_ref[:KVW, :] = rope(nn(a, kept[0, 3, :, :KVW]).T, cos, sin, False).astype(bf16)
    arrived(kept, sems, 1, 0)
    kv_ref[2 * KVW :, :] = ids
    kv_ref[KVW : 2 * KVW, :] = nn(a, kept[1, 0, :, :KVW]).T.astype(bf16)
    for m in range(3):
        arrived(kept, sems, 0, m)
        q_ref[pl.ds(m * KVW, KVW), :] = rope(nn(a, kept[0, m, :, :KVW]).T, cos, sin, False).astype(bf16)


def pre_kernel(sc, ht_ref, gain_ref, cos_ref, sin_ref, *rest):
    width = ht_ref.shape[0] - IDS
    mine, other = rest[:4], rest[4:8]
    h_ref, a_ref, q_ref, kv_ref, kept, sems = rest[-6:]
    core, chip = sc[0], sc[1]
    fetch(mine, other, kept, sems, core, chip)
    h = ht_ref[:width, :].T
    h_ref[...] = h
    project(h.astype(f32), gain_ref, cos_ref, sin_ref, ht_ref[width:, :], kept, sems, a_ref, q_ref, kv_ref)
    for m in range(1, 4):
        arrived(kept, sems, 1, m)


def scratch_a(width):
    return [pltpu.VMEM((2, 4, width, PIECE), bf16), pltpu.SemaphoreType.DMA((2, 4))]


def shape(s, d):
    return jax.ShapeDtypeStruct(s, d)


def pre(sc, ht, gain, cos, sin, mine_a, other_a, after):
    width, n = ht.shape[0] - IDS, ht.shape[1]
    return pl.pallas_call(
        pre_kernel,
        out_shape=(shape((n, width), bf16), shape((n, width), bf16), shape((width, n), bf16), shape((2 * KVW + IDS, n), bf16)),
        in_specs=[SCALARS] + [WHOLE] * 4 + [LEFT] * (8 + len(after)),
        out_specs=(WHOLE,) * 4,
        scratch_shapes=scratch_a(width),
        cost_estimate=BRIEF,
        compiler_params=pltpu.CompilerParams(vmem_limit_bytes=LIMIT),
        name="pre",
    )(sc, ht, gain, cos, sin, *mine_a, *other_a, *after)


def bias_of(kv):
    keys, n = kv.shape[1], kv.shape[1] // 3
    ids = kv[2 * KVW :, :].astype(f32)
    seg_k, seg_q = ids.T[:, :1], ids[:1, 2 * n :]
    j = lax.broadcasted_iota(jnp.int32, (keys, n), 0)
    i = lax.broadcasted_iota(jnp.int32, (keys, n), 1) + (keys - n)
    return jnp.where((seg_k == seg_q) & (j <= i), 0.0, -1e30).astype(f32)


def window_of(parts, whole):
    n = parts[0].shape[1]
    for w, part in enumerate(parts):
        whole[:, w * n : (w + 1) * n] = part[...]


def attend_kernel(q_ref, kv0, kv1, kv2, *rest):
    o_ref, lse_ref, bias, kv = rest[-4:]
    window_of((kv0, kv1, kv2), kv)
    bias[...] = bias_of(kv)

    def head(e, _):
        row = pl.multiple_of(e * HEAD_DIM, HEAD_DIM)
        k = kv[pl.ds(row, HEAD_DIM), :]
        v = kv[pl.ds(row + KVW, HEAD_DIM), :]
        for g in range(GROUP):
            at = pl.multiple_of((e * GROUP + g) * HEAD_DIM, HEAD_DIM)
            q = q_ref[pl.ds(at, HEAD_DIM), :]
            s = tn(k, q) * HEAD_DIM ** (-0.5) + bias[...]
            top = jnp.max(s, axis=0, keepdims=True)
            expo = jnp.exp(s - top)
            total = jnp.sum(expo, axis=0, keepdims=True)
            probs = (expo * (1.0 / total)).astype(bf16)
            o_ref[pl.ds(at, HEAD_DIM), :] = nn(v, probs).astype(bf16)
            lse_ref[pl.ds(e * GROUP + g, 1), :] = top + jnp.log(total)
        return 0

    lax.fori_loop(0, KV_HEADS, head, 0)


def attend(q, kvs, after=()):
    width, n = q.shape
    return pl.pallas_call(
        attend_kernel,
        out_shape=(shape((width, n), bf16), shape((HEADS, n), f32)),
        in_specs=[WHOLE] * 4 + [LEFT] * len(after),
        out_specs=(WHOLE,) * 2,
        scratch_shapes=[pltpu.VMEM((3 * n, n), f32), pltpu.VMEM((2 * KVW + IDS, 3 * n), bf16)],
        cost_estimate=BRIEF,
        compiler_params=pltpu.CompilerParams(vmem_limit_bytes=24 << 20),
        name="attend",
    )(q, *kvs, *after)


def attend_back_kernel(sc, p_ref, q_ref, kv0, kv1, kv2, lse_ref, do_ref, cos_ref, sin_ref, *rest):
    dq_ref, three_ref, far_ref, near_ref, own_ref, bias, kv, dqs = rest[-8:]
    n = q_ref.shape[1]
    window_of((kv0, kv1, kv2), kv)
    bias[...] = bias_of(kv)
    scale = HEAD_DIM ** (-0.5)

    def head(e, _):
        row = pl.multiple_of(e * HEAD_DIM, HEAD_DIM)
        k = kv[pl.ds(row, HEAD_DIM), :]
        v = kv[pl.ds(row + KVW, HEAD_DIM), :]
        dk = dv = None
        for g in range(GROUP):
            at = pl.multiple_of((e * GROUP + g) * HEAD_DIM, HEAD_DIM)
            q = q_ref[pl.ds(at, HEAD_DIM), :]
            do = do_ref[pl.ds(at, HEAD_DIM), :]
            s = tn(k, q) * scale + bias[...]
            probs = jnp.exp(s - lse_ref[pl.ds(e * GROUP + g, 1), :])
            dp = tn(v, do)
            inner = jnp.sum(probs * dp, axis=0, keepdims=True)
            ds = (probs * (dp - inner)).astype(bf16)
            dvg, dkg = nt(do, probs.astype(bf16)), nt(q, ds)
            dv, dk = (dvg, dkg) if g == 0 else (dv + dvg, dk + dkg)
            dqs[pl.ds(at, HEAD_DIM), :] = nn(k, ds)
        for at, grad in ((row, dk * scale), (row + KVW, dv)):
            far_ref[pl.ds(at, HEAD_DIM), :] = grad[:, :n]
            near_ref[pl.ds(at, HEAD_DIM), :] = grad[:, n : 2 * n].astype(bf16)
            own_ref[pl.ds(at, HEAD_DIM), :] = grad[:, 2 * n :]
        return 0

    lax.fori_loop(0, KV_HEADS, head, 0)
    cos, sin = cos_ref[...] * scale, sin_ref[...] * scale
    for m in range(3):
        dq = widened(rope(dqs[m * KVW : (m + 1) * KVW, :], cos, sin, True).T.astype(bf16))
        dq_ref[m] = dq
        three_ref[m] = jnp.where(sc[0] == 0, p_ref[m], dq)


def attend_back(sc, p, q, kvs, lse, do, cos, sin, after=()):
    width, n = q.shape
    block = (2 * KVW, n)
    return pl.pallas_call(
        attend_back_kernel,
        out_shape=(shape((3, n, PIECE), bf16), shape((3, n, PIECE), bf16), shape(block, f32), shape(block, bf16), shape(block, f32)),
        in_specs=[SCALARS] + [WHOLE] * 9 + [LEFT] * len(after),
        out_specs=(WHOLE,) * 5,
        scratch_shapes=[pltpu.VMEM((3 * n, n), f32), pltpu.VMEM((2 * KVW + IDS, 3 * n), bf16), pltpu.VMEM((width, n), f32)],
        cost_estimate=BRIEF,
        compiler_params=pltpu.CompilerParams(vmem_limit_bytes=32 << 20),
        name="attend_back",
    )(sc, p, q, *kvs, lse, do, cos, sin, *after)


def down_rows(kind, chip, width):
    return jnp.minimum((kind * 4 + chip) * ROWS, width - ROWS)


def fetch_ffn(mine, other, wb, wd, sem_b, sem_d, core, chip):
    rows, width = wb.shape[3], wd.shape[1]
    last = width % ROWS
    for kind, pieces in ((core, mine), (1 - core, other)):
        for who, piece in zip(whose(kind), pieces):
            at = chip ^ who
            pltpu.make_async_copy(piece.at[:, :rows], wb.at[kind, at], sem_b.at[kind, at]).start()
    for kind, pieces in ((core, mine), (1 - core, other)):
        for who, piece in zip(whose(kind), pieces):
            at = kind * 4 + (chip ^ who)

            @pl.when(at < width // ROWS)
            def _():
                into = wd.at[:, pl.ds(pl.multiple_of(at * ROWS, ROWS), ROWS)]
                pltpu.make_async_copy(piece.at[:, rows:], into, sem_d).start()

            @pl.when(at == width // ROWS)
            def _():
                pltpu.make_async_copy(piece.at[:, rows + ROWS - last :], wd.at[:, width - last :], sem_d).start()


def whole(wb, c, m):
    _, rows, n = wb.shape[2:]
    return wb[c, m].reshape(4 * rows, n)


def arrived_down(wd, sem_d):
    pltpu.make_async_copy(wd, wd, sem_d).wait()


def scratch_ffn(width, n):
    return [
        pltpu.VMEM((2, 4, 4, width // 4, n), bf16),
        pltpu.SemaphoreType.DMA((2, 4)),
        pltpu.VMEM((4, width, n), bf16),
        pltpu.SemaphoreType.DMA,
    ]


def post_kernel(last, after, sc, ot_ref, h_ref, gain_ref, gain_a, cos_ref, sin_ref, *rest):
    mine_a, other_a, mine_b, other_b = rest[:4], rest[4:8], rest[8:12], rest[12:16]
    ids_ref, rest = rest[16], rest[17 + after :]
    o_ref, h1_ref, b_ref, gate_ref, up_ref, z_ref, next_ref = rest[:7]
    more, rest = rest[7 : 7 + (0 if last else 3)], rest[7 + (0 if last else 3) :]
    wa, sem_a, wb, sem_b, wd, sem_d = rest
    core, chip = sc[0], sc[1]
    fetch(mine_a, other_a, wa, sem_a, core, chip)
    fetch_ffn(mine_b, other_b, wb, wd, sem_b, sem_d, core, chip)
    o = ot_ref[...].T
    o_ref[...] = o
    for m in range(1, 4):
        arrived(wa, sem_a, 1, m)
    h1 = h_ref[...].astype(f32) + jnp.concatenate([nn(o, wa[1, m, :, :KVW]) for m in range(1, 4)], axis=1)
    h1_ref[...] = h1
    b = normed(h1, gain_ref[...]).astype(bf16)
    b_ref[...] = b
    n = wb.shape[4]
    total = h1
    for m in range(4):
        cols = slice(m * n, (m + 1) * n)
        arrived(wb, sem_b, 0, m)
        gate = nn(b, whole(wb, 0, m))
        arrived(wb, sem_b, 1, m)
        up = nn(b, whole(wb, 1, m))
        gate_ref[:, cols] = gate.astype(bf16)
        up_ref[:, cols] = up.astype(bf16)
        z = (gate / (1.0 + jnp.exp(-gate)) * up).astype(bf16)
        z_ref[:, cols] = z
        if m == 0:
            arrived_down(wd, sem_d)
        total = total + nt(z, wd[m])
    next_ref[...] = total.astype(bf16).T if last else total
    if last:
        arrived(wa, sem_a, 1, 0)
        for m in range(4):
            arrived(wa, sem_a, 0, m)
    else:
        project(total, gain_a, cos_ref, sin_ref, ids_ref[2 * KVW :, :], wa, sem_a, *more)


def post(last, after, sc, ot, h, gain, gain_a, cos, sin, kv, wa, wb):
    width, n = ot.shape
    hidden = wb[0][0].shape[2] * 4
    outs = [shape((n, width), bf16), shape((n, width), f32), shape((n, width), bf16)] + [shape((n, hidden), bf16)] * 3
    outs += [shape((width, n), bf16) if last else shape((n, width), f32)]
    if not last:
        outs += [shape((n, width), bf16), shape((width, n), bf16), shape((2 * KVW + IDS, n), bf16)]
    return pl.pallas_call(
        functools.partial(post_kernel, last, len(after)),
        out_shape=tuple(outs),
        in_specs=[SCALARS] + [WHOLE] * 6 + [LEFT] * 16 + [WHOLE] + [LEFT] * len(after),
        out_specs=(WHOLE,) * len(outs),
        scratch_shapes=scratch_a(width) + scratch_ffn(width, hidden // 4),
        cost_estimate=BRIEF,
        compiler_params=pltpu.CompilerParams(vmem_limit_bytes=LIMIT),
        name="post",
    )(sc, ot, h, gain, gain_a, cos, sin, *wa[0], *wa[1], *wb[0], *wb[1], kv, *after)


def ffn_back(state, core, refs, weights):
    gate_ref, up_ref, h1_ref, gain_ref, gb_ref, keep_ref, send_ref, g1_ref, p_ref, dgain_ref, do_ref = refs
    wa, sem_a, wb, sem_b, wd, sem_d = weights
    gb = state.astype(bf16)
    gb_ref[...] = gb
    n = wb.shape[4]
    first = core == 0
    arrived_down(wd, sem_d)
    db = None
    for m in range(4):
        cols = slice(m * n, (m + 1) * n)
        dz = nn(gb, wd[m])
        gate, up = gate_ref[:, cols].astype(f32), up_ref[:, cols].astype(f32)
        sig = 1.0 / (1.0 + jnp.exp(-gate))
        dup = (dz * (gate * sig)).astype(bf16)
        dgate = (dz * up * (sig * (1.0 + gate * (1.0 - sig)))).astype(bf16)
        keep_ref[:, cols] = jnp.where(first, dgate, dup)
        send_ref[:, cols] = jnp.where(first, dup, dgate)
        arrived(wb, sem_b, 0, m)
        part = nt(dgate, whole(wb, 0, m))
        arrived(wb, sem_b, 1, m)
        part = part + nt(dup, whole(wb, 1, m))
        db = part if m == 0 else db + part
    dx, dgain = norm_back(h1_ref[...], gain_ref[...], db)
    dgain_ref[...] = dgain
    g1 = state + dx
    g1_ref[...] = g1
    low = g1.astype(bf16)
    do = None
    for p in range(3):
        part = low[:, p * KVW : (p + 1) * KVW]
        p_ref[p] = widened(part)
        arrived(wa, sem_a, 1, p + 1)
        part = nt(wa[1, p + 1, :, :KVW], part)
        do = part if p == 0 else do + part
    do_ref[...] = do.astype(bf16)


def finish_a(wa, sem_a, *left):
    for at in left:
        arrived(wa, sem_a, *at)


def query_back(dq_ref, wa, sem_a):
    da = None
    for m in range(3):
        arrived(wa, sem_a, 0, m)
        part = nt(dq_ref[m, :, :KVW], wa[0, m, :, :KVW])
        da = part if m == 0 else da + part
    return da


def project_back(da, own_ref, near_ref, far_ref, core, cos_ref, sin_ref, dk_ref, dv_ref, one_ref, h, gain, wa, sem_a):
    cos, sin = cos_ref[...], sin_ref[...]
    grad = own_ref[...] + far_ref[...].astype(f32) + jnp.where(core == 0, near_ref[...].astype(f32), 0.0)
    dk = rope(grad[:KVW], cos, sin, True).T.astype(bf16)
    dv = grad[KVW:].T.astype(bf16)
    dk_ref[...] = widened(dk)
    dv_ref[...] = widened(dv)
    one_ref[...] = widened(jnp.where(core == 0, dv, dk))
    arrived(wa, sem_a, 0, 3)
    arrived(wa, sem_a, 1, 0)
    da = da + nt(dk, wa[0, 3, :, :KVW]) + nt(dv, wa[1, 0, :, :KVW])
    return norm_back(h, gain, da)


def back_kernel(start, end, after, sc, *rest):
    rest = list(rest)

    def take(n):
        out = rest[:n]
        del rest[:n]
        return out

    core, chip = sc[0], sc[1]
    mine_a, other_a = take(4), take(4)
    if not end:
        mine_b, other_b = take(4), take(4)
    if start:
        (g_ref,) = take(1)
    else:
        g1_in, dq_ref, own_ref, near_ref, far_ref, h_ref, gain_a, cos_ref, sin_ref = take(9)
        if end:
            (last_ref,) = take(1)
    if not end:
        ins = take(4)
    take(after)
    if not start:
        dk_ref, dv_ref, one_ref, dgain_a = take(4)
    if end:
        (g_out,) = take(1)
    else:
        outs = take(7)
    wa, sem_a = take(2)
    fetch(mine_a, other_a, wa, sem_a, core, chip)
    if not end:
        wb, sem_b, wd, sem_d = take(4)
        fetch_ffn(mine_b, other_b, wb, wd, sem_b, sem_d, core, chip)
    if start:
        state = g_ref[...].T.astype(f32)
    else:
        da = query_back(dq_ref, wa, sem_a)
        dx, dgain = project_back(da, own_ref, near_ref, far_ref, core, cos_ref, sin_ref, dk_ref, dv_ref, one_ref, h_ref[...].astype(f32), gain_a[...], wa, sem_a)
        dgain_a[...] = dgain
        state = g1_in[...] + dx
    if end:
        width = state.shape[1]
        g_out[:width, :] = last_ref[...]
        g_out[width:, :] = state.astype(bf16).T
        finish_a(wa, sem_a, (1, 1), (1, 2), (1, 3))
    else:
        ffn_back(state, core, (*ins, *outs), (wa, sem_a, wb, sem_b, wd, sem_d))
        if start:
            finish_a(wa, sem_a, (1, 0), (0, 0), (0, 1), (0, 2), (0, 3))


def back(start, end, sc, weights, tail, ffn, after=()):
    wa, wb = weights
    width = wa[0][0].shape[0]
    args = [sc, *wa[0], *wa[1]]
    specs = [SCALARS] + [LEFT] * 8
    scratch = scratch_a(width)
    if not end:
        args += [*wb[0], *wb[1]]
        specs += [LEFT] * 8
        scratch += scratch_ffn(width, wb[0][0].shape[2])
    args += list(tail)
    specs += [WHOLE] * len(tail)
    n = tail[0].shape[1 if start else 0]
    outs = []
    if not end:
        args += list(ffn)
        specs += [WHOLE] * len(ffn)
    if not start:
        outs += [shape((n, PIECE), bf16)] * 3 + [shape((1, width), f32)]
    if end:
        outs += [shape((2 * width, n), bf16)]
    else:
        hidden = ffn[0].shape[1]
        outs += [shape((n, width), bf16), shape((n, hidden), bf16), shape((n, hidden), bf16)]
        outs += [shape((n, width), f32), shape((3, n, PIECE), bf16), shape((1, width), f32), shape((width, n), bf16)]
    args += list(after)
    specs += [LEFT] * len(after)
    return pl.pallas_call(
        functools.partial(back_kernel, start, end, len(after)),
        out_shape=tuple(outs),
        in_specs=specs,
        out_specs=(WHOLE,) * len(outs),
        scratch_shapes=scratch,
        cost_estimate=BRIEF,
        compiler_params=pltpu.CompilerParams(vmem_limit_bytes=LIMIT),
        name="back_end" if end else ("back_start" if start else "back_join"),
    )(*args)


def by_turn(core, chip):
    one = 1 + core
    return chip ^ one, chip ^ 3, chip, chip ^ (3 - one)


def turned(dst, blocks):
    n = blocks[0].shape[0]
    for i, block in enumerate(blocks):
        dst[:, i * n : (i + 1) * n] = block[...].T


def grad_ffn_kernel(sc, *rest):
    lefts, rights = rest[:4], rest[4:8]
    send_ref, keep_ref, left, right = rest[-4:]
    core, chip = sc[0], sc[1]
    n, cols = rights[0].shape[0], right.shape[1]
    turned(left, lefts)
    for i, m in enumerate(by_turn(core, chip)):
        at = pl.multiple_of(m * cols, 128)
        for j, block in enumerate(rights):
            right[j * n : (j + 1) * n, :] = block[:, pl.ds(at, cols)]
        out = send_ref if i < 2 else keep_ref
        out[i % 2] = nn(left[...], right[...]).astype(bf16)


def grad_ffn(sc, lefts, rights, after):
    n, width = lefts[0].shape
    cols = rights[0].shape[1] // 4
    out = shape((2, width, cols), bf16)
    return pl.pallas_call(
        grad_ffn_kernel,
        out_shape=(out, out),
        in_specs=[SCALARS] + [WHOLE] * 8 + [LEFT] * len(after),
        out_specs=(WHOLE,) * 2,
        scratch_shapes=[pltpu.VMEM((width, 4 * n), bf16), pltpu.VMEM((4 * n, cols), bf16)],
        cost_estimate=BRIEF,
        compiler_params=pltpu.CompilerParams(vmem_limit_bytes=LIMIT),
        name="grad_ffn",
    )(sc, *lefts, *rights, *after)


def grad_down_kernel(sc, *rest):
    lefts, rights = rest[:4], rest[4:8]
    send_ref, keep_ref, left, right = rest[-4:]
    n, (_, half, cols) = rights[0].shape[0], send_ref.shape
    turned(left, lefts)
    rows = pl.ds(pl.multiple_of(sc[0] * half, half), half)
    like = sc[2] & 1
    for h in range(2):
        for out, parity in ((send_ref, 1 - like), (keep_ref, like)):
            at = pl.multiple_of((2 * h + parity) * cols, 128)
            for j, block in enumerate(rights):
                right[j * n : (j + 1) * n, :] = block[:, pl.ds(at, cols)]
            out[h] = nn(left[rows, :], right[...]).astype(out.dtype)


def grad_down(sc, lefts, rights, after):
    n, width = lefts[0].shape
    cols = rights[0].shape[1] // 4
    block = (2, width // 2, cols)
    return pl.pallas_call(
        grad_down_kernel,
        out_shape=(shape(block, bf16), shape(block, bf16)),
        in_specs=[SCALARS] + [WHOLE] * 8 + [LEFT] * len(after),
        out_specs=(WHOLE,) * 2,
        scratch_shapes=[pltpu.VMEM((width, 4 * n), bf16), pltpu.VMEM((4 * n, cols), bf16)],
        cost_estimate=BRIEF,
        compiler_params=pltpu.CompilerParams(vmem_limit_bytes=LIMIT),
        name="grad_down",
    )(sc, *lefts, *rights, *after)


def grad_attention_kernel(sc, *rest):
    a_refs, o_refs, rest = rest[:4], rest[4:8], rest[8:]
    queries, keys, values, outs, threes, ones = (rest[i : i + 2] for i in range(0, 12, 2))
    gain_a, gain_f = (rest[i : i + 2] for i in (12, 14))
    *sends, keep_ref, left, right = rest[-5:]
    core, chip = sc[0], sc[1]
    n, width = a_refs[0].shape
    turned(left.at[0], a_refs)
    gains = [g[0][...] + g[1][...] for g in (gain_a, gain_f)]
    gains = jnp.concatenate([*gains, jnp.zeros((6, width), f32)], axis=0).T
    gains = jnp.concatenate([gains, jnp.zeros((width, PIECE - KVW - 8), f32)], axis=1).astype(bf16)

    def fill(at, of_three, own_three, own_one, single):
        for j in range(2):
            for i in range(3):
                right[of_three + i, j * n : (j + 1) * n, :] = own_three[j][i]
                right[of_three + i, (j + 2) * n : (j + 3) * n, :] = threes[j][i]
            right[single, j * n : (j + 1) * n, :] = own_one[j][...]
            right[single, (j + 2) * n : (j + 3) * n, :] = ones[j][...]

    @pl.when(core == 0)
    def _():
        fill(0, 0, queries, keys, 3)

    @pl.when(core == 1)
    def _():
        turned(left.at[1], o_refs)
        fill(0, 1, outs, values, 0)

    for i, m in enumerate(by_turn(core, chip)):
        out = sends[i] if i < 2 else keep_ref.at[i - 2]
        which = jnp.where(m > 0, core, 0)
        out[...] = nn(left[which], right[m]).astype(bf16)
        out[:, KVW:] = gains


def grad_attention(sc, a, o, own, got, gains, after):
    n, width = a[0].shape
    out = shape((width, PIECE), bf16)
    return pl.pallas_call(
        grad_attention_kernel,
        out_shape=(out, out, shape((2, width, PIECE), bf16)),
        in_specs=[SCALARS] + [WHOLE] * 24 + [LEFT] * len(after),
        out_specs=(WHOLE,) * 3,
        scratch_shapes=[pltpu.VMEM((2, width, 4 * n), bf16), pltpu.VMEM((4, 4 * n, PIECE), bf16)],
        cost_estimate=BRIEF,
        compiler_params=pltpu.CompilerParams(vmem_limit_bytes=LIMIT),
        name="grad_attention",
    )(sc, *a, *o, *own, *got, *gains, *after)


def lay_kernel(count, sc, *rest):
    mine, other, outs, kept = rest[:4], rest[4:8], rest[-1 - count : -1], rest[-1]
    core, chip = sc[0], sc[1]
    for kind, pieces in ((core, mine), (1 - core, other)):
        for who, piece in zip(whose(kind), pieces):
            kept[kind, chip ^ who] = piece[...]
    n = sum(o.shape[1] for o in outs[: 4 if len(outs) > 2 else 2]) // 8
    cols = [jnp.concatenate([kept[c, m, :, :n].astype(f32) for m in range(4)], axis=1) for c in range(2)]
    if len(outs) == 2:
        outs[0][...] = cols[0]
        outs[1][...] = cols[1]
    else:
        outs[0][...] = cols[0][:, : 3 * n]
        outs[1][...] = cols[0][:, 3 * n :]
        outs[2][...] = cols[1][:, :n]
        outs[3][...] = cols[1][:, n:]
        gains = kept[0, 0, :, n : n + 8].astype(f32) + kept[1, 0, :, n : n + 8].astype(f32)
        outs[4][...] = gains.T[:2]


def lay(sc, mine, other, widths, after):
    rows, n = mine[0].shape
    outs = tuple(shape((rows, w), f32) for w in widths)
    if len(widths) > 2:
        outs += (shape((2, rows), f32),)
    return pl.pallas_call(
        functools.partial(lay_kernel, len(outs)),
        out_shape=outs,
        in_specs=[SCALARS] + [WHOLE] * 8 + [LEFT] * len(after),
        out_specs=(WHOLE,) * len(outs),
        scratch_shapes=[pltpu.VMEM((2, 4, rows, n), bf16)],
        cost_estimate=BRIEF,
        compiler_params=pltpu.CompilerParams(vmem_limit_bytes=24 << 20),
        name="lay",
    )(sc, *mine, *other, *after)


def pick_first_kernel(sc, q_ref, k_ref, v_ref, o_ref, gain_ref, out_ref):
    rows = out_ref.shape[0]
    which = sc[0] * 4 + sc[1]
    pad = jnp.zeros((6, rows), f32)
    gains = jnp.concatenate([gain_ref[...], pad], axis=0).T.astype(bf16)
    rest = jnp.zeros((rows, PIECE - KVW - 8), bf16)
    for at in range(8):

        @pl.when(which == at)
        def _():
            if at in (3, 4):
                piece = (k_ref if at == 3 else v_ref)[...].T
            else:
                source, m = (q_ref, at) if at < 3 else (o_ref, at - 5)
                piece = source[:, m * KVW : (m + 1) * KVW]
            out_ref[...] = jnp.concatenate([piece, gains, rest], axis=1)


def pick_first(sc, query, key, value, out, gains):
    return pl.pallas_call(
        pick_first_kernel,
        out_shape=shape((query.shape[0], PIECE), bf16),
        in_specs=[SCALARS] + [WHOLE] * 5,
        out_specs=WHOLE,
        cost_estimate=BRIEF,
        compiler_params=pltpu.CompilerParams(vmem_limit_bytes=16 << 20),
        name="pick_first",
    )(sc, query, key, value, out, gains)


def pick_kernel(sc, gate, up, down, *rest):
    out_ref, sems = rest[-2:]
    rows, cols = out_ref.shape[0] - ROWS, out_ref.shape[1]
    into = out_ref.at[:rows]
    start = pl.multiple_of(down_rows(sc[0], sc[1], down.shape[0]), 64)
    copy = pltpu.make_async_copy(down.at[pl.ds(start, ROWS), :], out_ref.at[rows:], sems.at[1])
    copy.start()
    at = pl.ds(pl.multiple_of(sc[1] * cols, 128), cols)
    for c, source in ((0, gate), (1, up)):

        @pl.when(sc[0] == c)
        def _():
            pltpu.make_async_copy(source.at[:, at], into, sems.at[0]).start()

    pltpu.make_async_copy(gate.at[:, at], into, sems.at[0]).wait()
    copy.wait()


def pick(sc, gate, up, down, after):
    return pl.pallas_call(
        pick_kernel,
        out_shape=shape((gate.shape[0] + ROWS, gate.shape[1] // 4), bf16),
        in_specs=[SCALARS] + [LEFT] * (3 + len(after)),
        out_specs=WHOLE,
        scratch_shapes=[pltpu.SemaphoreType.DMA((2,))],
        cost_estimate=BRIEF,
        compiler_params=pltpu.CompilerParams(vmem_limit_bytes=16 << 20),
        name="pick",
    )(sc, gate, up, down, *after)


def gains_kernel(first_ref, out_ref):
    for j in range(4):
        n = first_ref.shape[1]
        out_ref[:, j * n : (j + 1) * n] = first_ref[j, :, KVW : KVW + 8].astype(f32).T[:2]


def gains_of(first):
    return pl.pallas_call(
        gains_kernel,
        out_shape=shape((2, 4 * first.shape[1]), f32),
        in_specs=[WHOLE],
        out_specs=WHOLE,
        cost_estimate=BRIEF,
        compiler_params=pltpu.CompilerParams(vmem_limit_bytes=16 << 20),
        name="gains",
    )(first)


def stack_kernel(sc, *rest):
    parts, out_ref, sems = rest[:4], rest[-2], rest[-1]
    copies = [pltpu.make_async_copy(p, out_ref.at[sc[2] ^ s], sems.at[s]) for s, p in enumerate(parts)]
    for copy in copies:
        copy.start()
    for copy in copies:
        copy.wait()


def stack(sc, parts, after=()):
    return pl.pallas_call(
        stack_kernel,
        out_shape=shape((4,) + parts[0].shape, parts[0].dtype),
        in_specs=[SCALARS] + [LEFT] * (4 + len(after)),
        out_specs=WHOLE,
        scratch_shapes=[pltpu.SemaphoreType.DMA((4,))],
        cost_estimate=BRIEF,
        compiler_params=pltpu.CompilerParams(vmem_limit_bytes=16 << 20),
        name="stack",
    )(sc, *parts, *after)


def small(kernel, sc, args, outs, scratch, after, name):
    return pl.pallas_call(
        kernel,
        out_shape=tuple(outs),
        in_specs=[SCALARS] + [WHOLE] * len(args) + [LEFT] * len(after),
        out_specs=(WHOLE,) * len(outs),
        scratch_shapes=scratch,
        cost_estimate=BRIEF,
        compiler_params=pltpu.CompilerParams(vmem_limit_bytes=32 << 20),
        name=name,
    )(sc, *args, *after)


def sum_first(sc, keep, got, after, parts=1):
    def kernel(sc, keep_ref, *rest):
        own_got, later_got = rest[:2] if len(got) == 2 else (rest[0].at[0], rest[0].at[1])
        own_ref = rest[-1]
        for i, later_ref in enumerate(rest[-1 - parts : -1]):
            n = later_ref.shape[0]
            rows = slice(i * n, (i + 1) * n)
            later_ref[...] = (keep_ref[1, rows].astype(f32) + later_got[rows].astype(f32)).astype(bf16)
        own_ref[...] = keep_ref[0].astype(f32) + own_got[...].astype(f32)

    rows, cols = keep.shape[1:]
    outs = [shape((rows // parts, cols), bf16)] * parts + [shape((rows, cols), f32)]
    return small(kernel, sc, [keep, *got], outs, [], after, "sum_first")


def sum_second(sc, own, got, after):
    def kernel(sc, own_ref, *rest):
        gots, (send_ref, keep_ref, total) = rest[: len(got)], rest[-3:]
        n = total.shape[1]
        for j in range(4):
            part, at = divmod(j * n, gots[0].shape[0])
            total[j] = own_ref[j * n : (j + 1) * n, :] + gots[part][at : at + n, :].astype(f32)
        like = sc[2] & 1
        for h in range(2):
            send_ref[h] = total[2 * h + 1 - like].astype(bf16)
            keep_ref[h] = total[2 * h + like]

    rows, cols = own.shape
    part = (rows // 4, cols)
    outs = [shape((2,) + part, bf16), shape((2,) + part, f32)]
    return small(kernel, sc, [own, *got], outs, [pltpu.VMEM((4,) + part, f32)], after, "sum_second")


def sum_third(sc, keep, got, after):
    def kernel(sc, keep_ref, got_ref, *rest):
        send_ref, own_ref = rest[-2:]
        h = sc[2] >> 1
        send_ref[...] = (keep_ref[1 - h].astype(f32) + got_ref[1 - h].astype(f32)).astype(bf16)
        own_ref[...] = keep_ref[h].astype(f32) + got_ref[h].astype(f32)

    part = keep.shape[1:]
    return small(kernel, sc, [keep, got], [shape(part, bf16), shape(part, f32)], [], after, "sum_third")


def down_split(sc, own, got, after):
    def kernel(sc, own_ref, got_ref, *rest):
        send_ref, kept_ref, total = rest[-3:]
        n = total.shape[1]
        for m in range(4):
            rows = slice(m * n, (m + 1) * n)
            total[m] = own_ref[rows, :] + got_ref[rows, :].astype(f32)
        for i, m in enumerate(by_turn(sc[0], sc[1])):
            out = send_ref if i < 2 else kept_ref
            out[i % 2] = total[m].astype(bf16)

    rows, cols = own.shape
    out = shape((2, rows // 4, cols), bf16)
    return small(kernel, sc, [own, got], [out, out], [pltpu.VMEM((4, rows // 4, cols), f32)], after, "down_split")


def sum_two(sc, own, got, after):
    def kernel(sc, own_ref, got_ref, *rest):
        rest[-1][...] = (own_ref[...] + got_ref[...].astype(f32)).astype(bf16)

    return small(kernel, sc, [own, got], [shape(own.shape, bf16)], [], after, "sum_two")[0]


def lay_down(sc, mine, other, after):
    def kernel(sc, *rest):
        out_ref, total = rest[-2:]
        n = total.shape[2]
        for kind, pieces in ((sc[0], rest[:4]), (1 - sc[0], rest[4:8])):
            for who, piece in zip(whose(kind), pieces):
                total[kind, sc[1] ^ who] = piece[...].astype(f32)
        for c in range(2):
            for m in range(4):
                at = (c * 4 + m) * n
                out_ref[at : at + n, :] = total[c, m]

    n, cols = mine[0].shape
    return small(kernel, sc, [*mine, *other], [shape((8 * n, cols), f32)], [pltpu.VMEM((2, 4, n, cols), f32)], after, "lay_down")[0]


def hold(value, after):
    return pl.pallas_call(
        lambda *refs: None,
        out_shape=shape(value.shape, value.dtype),
        in_specs=[LEFT] * (1 + len(after)),
        out_specs=LEFT,
        input_output_aliases={0: 0},
        cost_estimate=BRIEF,
        compiler_params=pltpu.CompilerParams(vmem_limit_bytes=1 << 20),
        name="hold",
    )(value, *after)


def far_sum(sc, far, near, after):
    def kernel(sc, far_ref, near_ref, *rest):
        rest[-1][...] = (far_ref[...] + jnp.where(sc[0] == 1, near_ref[...].astype(f32), 0.0)).astype(bf16)

    return small(kernel, sc, [far, near], [shape(far.shape, bf16)], [], after, "far_sum")[0]


CORE, SIDE, BACK = 1, 2, 4
rope_base = 10000.0
RUNS = 2


def flip(value, bit, bit1=None):
    count = lax.axis_size("dp")
    bits = (bit, bit if bit1 is None else bit1)
    return lax.ppermute(value, "dp", [(i, i ^ bits[i & 1]) for i in range(count)])


def flip_z(value, bit, where=lambda d, z: True):
    count, depth = lax.axis_size("dp"), lax.axis_size("fsdp")
    pairs = [(d * depth + z, d * depth + (z ^ bit)) for d in range(count) for z in range(depth) if where(d, z)]
    return lax.ppermute(value, ("dp", "fsdp"), pairs)


def home_to_work(value, back=False):
    count, depth = lax.axis_size("dp"), lax.axis_size("fsdp")
    pairs = []
    for d in range(count):
        for z in range(depth):
            there = (d & ~1) | (z & 1), 2 * (d & 1) + (z >> 1)
            pair = (d * depth + z, there[0] * depth + there[1])
            pairs.append(pair[::-1] if back else pair)
    return lax.ppermute(value, ("dp", "fsdp"), pairs)


def place():
    d, z = lax.axis_index("dp"), lax.axis_index("fsdp")
    return d & 1, (d >> 1) & 3, z


def turns(shard):
    far = flip_z(shard, 2)
    return shard, flip_z(shard, 1), far, flip_z(far, 1)


def plane_gather(piece):
    first, second = flip(piece, SIDE, BACK), flip(piece, BACK, SIDE)
    mine = (piece, first, second, flip(first, BACK, SIDE))
    return mine, tuple(flip(p, CORE) for p in mine)


def window(own):
    core, _, _ = place()
    depth = lax.axis_size("fsdp")
    far = lax.ppermute(own, "fsdp", [(z, z + 1) for z in range(0, depth, 2)])
    near = flip(jnp.where(core == 0, own, far), CORE)
    return far, near, own


def unwindow(sc, far, near, after=()):
    depth = lax.axis_size("fsdp")
    near = flip(near, CORE)
    far = far_sum(sc, far, near, after)
    return near, far, lax.ppermute(far, "fsdp", [(z + 1, z) for z in range(0, depth, 2)])


def over_groups(value):
    bit = 8
    while bit < lax.axis_size("dp"):
        value = (value.astype(f32) + flip(value, bit).astype(f32)).astype(bf16)
        bit *= 2
    return value


def spread(piece):
    return piece, flip(piece, SIDE, BACK), flip(piece, BACK, SIDE), flip(piece, SIDE | BACK)


def across(pieces):
    return tuple(flip(p, CORE) for p in pieces)


def body(tokens, segment_ids, attn_gain, query_weight, key_weight, value_weight, out_weight, ffn_gain, gate_weight, up_weight, down_weight, cotangent):
    core, chip, z = place()
    sc = jnp.stack([core, chip, z]).astype(jnp.int32)
    _, stretch, width = tokens.shape
    rows, depth = query_weight.shape[0], lax.axis_size("fsdp")
    block = 2 * (z & 1) + core
    positions = (block * stretch + jnp.arange(stretch)).astype(f32)
    freq = rope_base ** (-2.0 * jnp.arange(HEAD_DIM // 2, dtype=f32) / HEAD_DIM)
    angle = freq[:, None] * positions[None, :]
    cos, sin = jnp.cos(angle), jnp.sin(angle)

    gains = jnp.stack([attn_gain, ffn_gain]).astype(f32)
    parts_a = turns(pick_first(sc, query_weight, key_weight.T, value_weight.T, out_weight, gains))
    ids = jnp.broadcast_to((segment_ids[0] + 1).astype(bf16), (IDS, stretch))
    tokens = home_to_work(jnp.concatenate([tokens[0].T, ids]))
    piece_b = pick(sc, gate_weight, up_weight, down_weight.T, parts_a[1:2])
    whole_a = stack(sc, parts_a, [piece_b])
    gains = gains_of(whole_a)
    gain_a, gain_f = gains[:1], gains[1:]
    wa = plane_gather(whole_a.reshape(depth * rows, PIECE))
    side_b = flip_z(piece_b, 1)
    far_b = hold(flip_z(piece_b, 2), [wa[0][1], wa[0][2], side_b])
    whole_b = stack(sc, (piece_b, side_b, far_b, flip_z(far_b, 1)), [wa[0][3]])
    first_b, second_b = flip(whole_b, SIDE, BACK), flip(whole_b, BACK, SIDE)

    h_0, a0, q0, own = pre(sc, tokens, gain_a, cos, sin, *wa, [whole_b])
    kv0 = window(own)
    first_b = hold(first_b, [kv0[0], second_b])
    opposite_b = flip(first_b, BACK, SIDE)
    o0, lse0 = attend(q0, kv0)
    wb = whole_b, first_b, second_b, hold(opposite_b, [o0])
    wb = wb, across(wb)
    weights = wa, wb
    mixed0, h1_0, b0, gate0, up0, z0, h_1, a1, q1, own = post(False, [], sc, o0, h_0, gain_f, gain_a, cos, sin, own, *weights)
    kv1 = window(own)
    across_0 = across((a0, b0, mixed0, z0))
    cot = home_to_work(hold(cotangent[0].T, [kv1[1]]))
    o1, lse1 = attend(q1, kv1, across_0)
    mixed1, h1_1, b1, gate1, up1, z1, output = post(True, [cot], sc, o1, h_1, gain_f, gain_a, cos, sin, own, *weights)
    across_1 = across((a1, b1, mixed1, z1))

    gb1, act1, away1, g1, p1, dgain_f1, do = back(True, False, sc, weights, [cot], [gate1, up1, h1_1, gain_f])
    across_2 = across((gb1, away1))
    dq1, three1, far, near, own = attend_back(sc, p1, q1, kv1, lse1, do, cos, sin, [*across_1])
    near, _, far = unwindow(sc, far, near)
    (three1,) = across((three1,))
    tail = [g1, dq1, own, near, far, h_1, gain_a, cos, sin]
    dk1, dv1, one1, dgain_a1, gb0, act0, away0, g1, p0, dgain_f0, do = back(False, False, sc, weights, tail, [gate0, up0, h1_0, gain_f], [three1, *across_2])

    away0, gb0_, one1 = across((away0, gb0, one1))
    send_b, keep_b = grad_ffn(sc, [b1, b0, across_1[1], across_0[1]], [act1, act0, across_2[1], away0], [])
    got_b = flip(send_b, SIDE, BACK)
    send_d, keep_d = grad_down(sc, [gb1, gb0, across_2[0], gb0_], [z1, z0, across_1[3], across_0[3]], [send_b])
    got_d = flip_z(send_d, 1)
    dq0, three0, far, near, own = attend_back(sc, p0, q0, kv0, lse0, do, cos, sin, [one1, send_d])
    near, down_far, far = unwindow(sc, far, near)
    (three0,) = across((three0,))
    later_b, own_b = sum_first(sc, keep_b, [got_b], [far])
    more_b = flip(later_b, BACK, SIDE)
    send_d, keep_d = sum_third(sc, keep_d, got_d, [later_b])
    got_d = flip_z(send_d, 2)
    tail = [g1, dq0, own, near, far, h_0, gain_a, cos, sin, output]
    dk0, dv0, one0, dgain_a0, leaving = back(False, True, sc, weights, tail, None, [send_d])
    own = [dq1, dq0, dk1, dk0, dv1, dv0, p1, p0]
    got = [three1, three0, one1, flip(one0, CORE)]
    *send_a, keep_a = grad_attention(sc, [a1, a0, across_1[0], across_0[0]], [mixed1, mixed0, across_1[2], across_0[2]], own, got, [dgain_a1, dgain_a0, dgain_f1, dgain_f0], [send_d])
    got_a = [flip(v, SIDE, BACK) for v in send_a]
    send_b, ring_b = sum_second(sc, own_b, [more_b], send_a)
    got_b = flip_z(send_b, 1)
    *later_a, own_a = sum_first(sc, keep_a, got_a, [ring_b], 2)
    more_a = [flip(v, BACK, SIDE) for v in later_a]
    send_d, keep_d = down_split(sc, keep_d, got_d, [own_a])
    got_d = flip(send_d, SIDE, BACK)
    send_b, ring_b = sum_third(sc, ring_b, got_b, [send_d])
    got_b = flip_z(send_b, 2)
    send_a, ring_a = sum_second(sc, own_a, more_a, [send_b])
    got_a = flip_z(send_a, 1)
    piece_b = over_groups(sum_two(sc, ring_b, got_b, [send_a]))
    all_b = spread(piece_b)
    send_a, ring_a = sum_third(sc, ring_a, got_a, [piece_b])
    got_a = flip_z(send_a, 2)
    later_d, own_d = sum_first(sc, keep_d, [got_d], [send_a])
    more_d = flip(later_d, BACK, SIDE)
    piece_a = over_groups(sum_two(sc, ring_a, got_a, [later_d]))
    all_a = spread(piece_a)
    piece_d = over_groups(sum_two(sc, own_d, more_d, [piece_a]))
    grad_gate, grad_up = lay(sc, all_b, across(all_b), (gate_weight.shape[1],) * 2, [piece_d])
    all_d = spread(piece_d)
    grad_query, grad_key, grad_value, grad_out, dgains = lay(sc, all_a, across(all_a), (width, KVW, KVW, width), [grad_gate])
    grad_down_ = lay_down(sc, all_d, across(all_d), [grad_query])
    leaving = home_to_work(hold(leaving, [piece_b]), back=True)
    output, grad_tokens = leaving[:width].T, leaving[width:].astype(f32).T
    return (output[None], grad_tokens[None], dgains[0], grad_query, grad_key, grad_value, grad_out, dgains[1], grad_gate, grad_up, grad_down_.T)


def solution(mesh):
    wide, rows, shard = P("dp", "fsdp", None), P("dp", "fsdp"), P("fsdp", None)
    in_specs = (wide, rows, P("fsdp"), shard, shard, shard, shard, P("fsdp"), shard, shard, shard, wide)
    out_specs = (wide, wide, P("fsdp"), shard, shard, shard, shard, P("fsdp"), shard, shard, shard)
    return jax.shard_map(body, mesh=mesh, in_specs=in_specs, out_specs=out_specs, check_vma=False)
```

```python
import functools
import jax
import jax.numpy as jnp
from jax import lax
from jax.sharding import PartitionSpec as P
from jax.experimental import pallas as pl
from jax.experimental.pallas import tpu as pltpu

f32, bf16 = jnp.float32, jnp.bfloat16
eps = 1e-05
HEADS, KV_HEADS, HEAD_DIM, GROUP, KVW = 15, 5, 64, 3, 320
IDS = 16
ROWS = 128
PIECE = 384
LIMIT = 58 << 20
WHOLE = pl.BlockSpec(memory_space=pltpu.VMEM)
LEFT = pl.BlockSpec(memory_space=pl.ANY)
SCALARS = pl.BlockSpec(memory_space=pltpu.SMEM)
BRIEF = pl.CostEstimate(flops=1024, bytes_accessed=1024, transcendentals=0)


def contract(a, b, i, j):
    return lax.dot_general(a, b, (((i,), (j,)), ((), ())), preferred_element_type=f32)


def nn(a, b):
    return contract(a, b, 1, 0)


def nt(a, b):
    return contract(a, b, 1, 1)


def tn(a, b):
    return contract(a, b, 0, 0)


def whose(core):
    return 0, 1 + core, 2 - core, 3


def fetch(mine, other, kept, sems, core, chip):
    for kind, pieces in ((core, mine), (1 - core, other)):
        for who, piece in zip(whose(kind), pieces):
            at = chip ^ who
            pltpu.make_async_copy(piece, kept.at[kind, at], sems.at[kind, at]).start()


def arrived(kept, sems, *at):
    pltpu.make_async_copy(kept.at[at], kept.at[at], sems.at[at]).wait()


def normed(x, gain):
    return x * lax.rsqrt(jnp.mean(x * x, axis=-1, keepdims=True) + eps) * gain


def norm_back(x, gain, grad):
    r = lax.rsqrt(jnp.mean(x * x, axis=-1, keepdims=True) + eps)
    hat = x * r
    scaled = grad * gain
    dx = r * (scaled - hat * jnp.mean(scaled * hat, axis=-1, keepdims=True))
    return dx, jnp.sum(grad * hat, axis=0, keepdims=True)


def widened(x):
    return jnp.concatenate([x, jnp.zeros((x.shape[0], PIECE - x.shape[1]), x.dtype)], axis=1)


def rope(u, cos, sin, back):
    heads = u.shape[0] // HEAD_DIM
    half = HEAD_DIM // 2
    out = []
    for h in range(heads):
        u1, u2 = u[h * HEAD_DIM : h * HEAD_DIM + half], u[h * HEAD_DIM + half : (h + 1) * HEAD_DIM]
        if back:
            out += [u1 * cos + u2 * sin, u2 * cos - u1 * sin]
        else:
            out += [u1 * cos - u2 * sin, u2 * cos + u1 * sin]
    return jnp.concatenate(out, axis=0)


def project(state, gain_ref, cos_ref, sin_ref, ids, kept, sems, a_ref, q_ref, kv_ref):
    a = normed(state, gain_ref[...]).astype(bf16)
    a_ref[...] = a
    cos, sin = cos_ref[...], sin_ref[...]
    arrived(kept, sems, 0, 3)
    kv_ref[:KVW, :] = rope(nn(a, kept[0, 3, :, :KVW]).T, cos, sin, False).astype(bf16)
    arrived(kept, sems, 1, 0)
    kv_ref[2 * KVW :, :] = ids
    kv_ref[KVW : 2 * KVW, :] = nn(a, kept[1, 0, :, :KVW]).T.astype(bf16)
    for m in range(3):
        arrived(kept, sems, 0, m)
        q_ref[pl.ds(m * KVW, KVW), :] = rope(nn(a, kept[0, m, :, :KVW]).T, cos, sin, False).astype(bf16)


def pre_kernel(sc, ht_ref, gain_ref, cos_ref, sin_ref, *rest):
    width = ht_ref.shape[0] - IDS
    mine, other = rest[:4], rest[4:8]
    h_ref, a_ref, q_ref, kv_ref, kept, sems = rest[-6:]
    core, chip = sc[0], sc[1]
    fetch(mine, other, kept, sems, core, chip)
    h = ht_ref[:width, :].T
    h_ref[...] = h
    project(h.astype(f32), gain_ref, cos_ref, sin_ref, ht_ref[width:, :], kept, sems, a_ref, q_ref, kv_ref)
    for m in range(1, 4):
        arrived(kept, sems, 1, m)


def scratch_a(width):
    return [pltpu.VMEM((2, 4, width, PIECE), bf16), pltpu.SemaphoreType.DMA((2, 4))]


def shape(s, d):
    return jax.ShapeDtypeStruct(s, d)


def pre(sc, ht, gain, cos, sin, mine_a, other_a, after):
    width, n = ht.shape[0] - IDS, ht.shape[1]
    return pl.pallas_call(
        pre_kernel,
        out_shape=(shape((n, width), bf16), shape((n, width), bf16), shape((width, n), bf16), shape((2 * KVW + IDS, n), bf16)),
        in_specs=[SCALARS] + [WHOLE] * 4 + [LEFT] * (8 + len(after)),
        out_specs=(WHOLE,) * 4,
        scratch_shapes=scratch_a(width),
        cost_estimate=BRIEF,
        compiler_params=pltpu.CompilerParams(vmem_limit_bytes=LIMIT),
        name="pre",
    )(sc, ht, gain, cos, sin, *mine_a, *other_a, *after)


def bias_of(kv):
    keys, n = kv.shape[1], kv.shape[1] // 3
    ids = kv[2 * KVW :, :].astype(f32)
    seg_k, seg_q = ids.T[:, :1], ids[:1, 2 * n :]
    j = lax.broadcasted_iota(jnp.int32, (keys, n), 0)
    i = lax.broadcasted_iota(jnp.int32, (keys, n), 1) + (keys - n)
    return jnp.where((seg_k == seg_q) & (j <= i), 0.0, -1e30).astype(f32)


def window_of(parts, whole):
    n = parts[0].shape[1]
    for w, part in enumerate(parts):
        whole[:, w * n : (w + 1) * n] = part[...]


def attend_kernel(q_ref, kv0, kv1, kv2, *rest):
    o_ref, lse_ref, bias, kv = rest[-4:]
    window_of((kv0, kv1, kv2), kv)
    bias[...] = bias_of(kv)

    def head(e, _):
        row = pl.multiple_of(e * HEAD_DIM, HEAD_DIM)
        k = kv[pl.ds(row, HEAD_DIM), :]
        v = kv[pl.ds(row + KVW, HEAD_DIM), :]
        for g in range(GROUP):
            at = pl.multiple_of((e * GROUP + g) * HEAD_DIM, HEAD_DIM)
            q = q_ref[pl.ds(at, HEAD_DIM), :]
            s = tn(k, q) * HEAD_DIM ** (-0.5) + bias[...]
            top = jnp.max(s, axis=0, keepdims=True)
            expo = jnp.exp(s - top)
            total = jnp.sum(expo, axis=0, keepdims=True)
            probs = (expo * (1.0 / total)).astype(bf16)
            o_ref[pl.ds(at, HEAD_DIM), :] = nn(v, probs).astype(bf16)
            lse_ref[pl.ds(e * GROUP + g, 1), :] = top + jnp.log(total)
        return 0

    lax.fori_loop(0, KV_HEADS, head, 0)


def attend(q, kvs, after=()):
    width, n = q.shape
    return pl.pallas_call(
        attend_kernel,
        out_shape=(shape((width, n), bf16), shape((HEADS, n), f32)),
        in_specs=[WHOLE] * 4 + [LEFT] * len(after),
        out_specs=(WHOLE,) * 2,
        scratch_shapes=[pltpu.VMEM((3 * n, n), f32), pltpu.VMEM((2 * KVW + IDS, 3 * n), bf16)],
        cost_estimate=BRIEF,
        compiler_params=pltpu.CompilerParams(vmem_limit_bytes=24 << 20),
        name="attend",
    )(q, *kvs, *after)


def attend_back_kernel(sc, p_ref, q_ref, kv0, kv1, kv2, lse_ref, do_ref, cos_ref, sin_ref, *rest):
    dq_ref, three_ref, far_ref, near_ref, own_ref, bias, kv, dqs = rest[-8:]
    n = q_ref.shape[1]
    window_of((kv0, kv1, kv2), kv)
    bias[...] = bias_of(kv)
    scale = HEAD_DIM ** (-0.5)

    def head(e, _):
        row = pl.multiple_of(e * HEAD_DIM, HEAD_DIM)
        k = kv[pl.ds(row, HEAD_DIM), :]
        v = kv[pl.ds(row + KVW, HEAD_DIM), :]
        dk = dv = None
        for g in range(GROUP):
            at = pl.multiple_of((e * GROUP + g) * HEAD_DIM, HEAD_DIM)
            q = q_ref[pl.ds(at, HEAD_DIM), :]
            do = do_ref[pl.ds(at, HEAD_DIM), :]
            s = tn(k, q) * scale + bias[...]
            probs = jnp.exp(s - lse_ref[pl.ds(e * GROUP + g, 1), :])
            dp = tn(v, do)
            inner = jnp.sum(probs * dp, axis=0, keepdims=True)
            ds = (probs * (dp - inner)).astype(bf16)
            dvg, dkg = nt(do, probs.astype(bf16)), nt(q, ds)
            dv, dk = (dvg, dkg) if g == 0 else (dv + dvg, dk + dkg)
            dqs[pl.ds(at, HEAD_DIM), :] = nn(k, ds)
        for at, grad in ((row, dk * scale), (row + KVW, dv)):
            far_ref[pl.ds(at, HEAD_DIM), :] = grad[:, :n]
            near_ref[pl.ds(at, HEAD_DIM), :] = grad[:, n : 2 * n].astype(bf16)
            own_ref[pl.ds(at, HEAD_DIM), :] = grad[:, 2 * n :]
        return 0

    lax.fori_loop(0, KV_HEADS, head, 0)
    cos, sin = cos_ref[...] * scale, sin_ref[...] * scale
    for m in range(3):
        dq = widened(rope(dqs[m * KVW : (m + 1) * KVW, :], cos, sin, True).T.astype(bf16))
        dq_ref[m] = dq
        three_ref[m] = jnp.where(sc[0] == 0, p_ref[m], dq)


def attend_back(sc, p, q, kvs, lse, do, cos, sin, after=()):
    width, n = q.shape
    block = (2 * KVW, n)
    return pl.pallas_call(
        attend_back_kernel,
        out_shape=(shape((3, n, PIECE), bf16), shape((3, n, PIECE), bf16), shape(block, f32), shape(block, bf16), shape(block, f32)),
        in_specs=[SCALARS] + [WHOLE] * 9 + [LEFT] * len(after),
        out_specs=(WHOLE,) * 5,
        scratch_shapes=[pltpu.VMEM((3 * n, n), f32), pltpu.VMEM((2 * KVW + IDS, 3 * n), bf16), pltpu.VMEM((width, n), f32)],
        cost_estimate=BRIEF,
        compiler_params=pltpu.CompilerParams(vmem_limit_bytes=32 << 20),
        name="attend_back",
    )(sc, p, q, *kvs, lse, do, cos, sin, *after)


def down_rows(kind, chip, width):
    return jnp.minimum((kind * 4 + chip) * ROWS, width - ROWS)


def fetch_ffn(mine, other, wb, wd, sem_b, sem_d, core, chip):
    rows, width = wb.shape[3], wd.shape[1]
    last = width % ROWS
    for kind, pieces in ((core, mine), (1 - core, other)):
        for who, piece in zip(whose(kind), pieces):
            at = chip ^ who
            pltpu.make_async_copy(piece.at[:, :rows], wb.at[kind, at], sem_b.at[kind, at]).start()
    for kind, pieces in ((core, mine), (1 - core, other)):
        for who, piece in zip(whose(kind), pieces):
            at = kind * 4 + (chip ^ who)

            @pl.when(at < width // ROWS)
            def _():
                into = wd.at[:, pl.ds(pl.multiple_of(at * ROWS, ROWS), ROWS)]
                pltpu.make_async_copy(piece.at[:, rows:], into, sem_d).start()

            @pl.when(at == width // ROWS)
            def _():
                pltpu.make_async_copy(piece.at[:, rows + ROWS - last :], wd.at[:, width - last :], sem_d).start()


def whole(wb, c, m):
    _, rows, n = wb.shape[2:]
    return wb[c, m].reshape(4 * rows, n)


def arrived_down(wd, sem_d):
    pltpu.make_async_copy(wd, wd, sem_d).wait()


def scratch_ffn(width, n):
    return [
        pltpu.VMEM((2, 4, 4, width // 4, n), bf16),
        pltpu.SemaphoreType.DMA((2, 4)),
        pltpu.VMEM((4, width, n), bf16),
        pltpu.SemaphoreType.DMA,
    ]


def post_kernel(last, after, sc, ot_ref, h_ref, gain_ref, gain_a, cos_ref, sin_ref, *rest):
    mine_a, other_a, mine_b, other_b = rest[:4], rest[4:8], rest[8:12], rest[12:16]
    ids_ref, rest = rest[16], rest[17 + after :]
    o_ref, h1_ref, b_ref, gate_ref, up_ref, z_ref, next_ref = rest[:7]
    more, rest = rest[7 : 7 + (0 if last else 3)], rest[7 + (0 if last else 3) :]
    wa, sem_a, wb, sem_b, wd, sem_d = rest
    core, chip = sc[0], sc[1]
    fetch(mine_a, other_a, wa, sem_a, core, chip)
    fetch_ffn(mine_b, other_b, wb, wd, sem_b, sem_d, core, chip)
    o = ot_ref[...].T
    o_ref[...] = o
    for m in range(1, 4):
        arrived(wa, sem_a, 1, m)
    h1 = h_ref[...].astype(f32) + jnp.concatenate([nn(o, wa[1, m, :, :KVW]) for m in range(1, 4)], axis=1)
    h1_ref[...] = h1
    b = normed(h1, gain_ref[...]).astype(bf16)
    b_ref[...] = b
    n = wb.shape[4]
    total = h1
    for m in range(4):
        cols = slice(m * n, (m + 1) * n)
        arrived(wb, sem_b, 0, m)
        gate = nn(b, whole(wb, 0, m))
        arrived(wb, sem_b, 1, m)
        up = nn(b, whole(wb, 1, m))
        gate_ref[:, cols] = gate.astype(bf16)
        up_ref[:, cols] = up.astype(bf16)
        z = (gate / (1.0 + jnp.exp(-gate)) * up).astype(bf16)
        z_ref[:, cols] = z
        if m == 0:
            arrived_down(wd, sem_d)
        total = total + nt(z, wd[m])
    next_ref[...] = total.astype(bf16).T if last else total
    if last:
        arrived(wa, sem_a, 1, 0)
        for m in range(4):
            arrived(wa, sem_a, 0, m)
    else:
        project(total, gain_a, cos_ref, sin_ref, ids_ref[2 * KVW :, :], wa, sem_a, *more)


def post(last, after, sc, ot, h, gain, gain_a, cos, sin, kv, wa, wb):
    width, n = ot.shape
    hidden = wb[0][0].shape[2] * 4
    outs = [shape((n, width), bf16), shape((n, width), f32), shape((n, width), bf16)] + [shape((n, hidden), bf16)] * 3
    outs += [shape((width, n), bf16) if last else shape((n, width), f32)]
    if not last:
        outs += [shape((n, width), bf16), shape((width, n), bf16), shape((2 * KVW + IDS, n), bf16)]
    return pl.pallas_call(
        functools.partial(post_kernel, last, len(after)),
        out_shape=tuple(outs),
        in_specs=[SCALARS] + [WHOLE] * 6 + [LEFT] * 16 + [WHOLE] + [LEFT] * len(after),
        out_specs=(WHOLE,) * len(outs),
        scratch_shapes=scratch_a(width) + scratch_ffn(width, hidden // 4),
        cost_estimate=BRIEF,
        compiler_params=pltpu.CompilerParams(vmem_limit_bytes=LIMIT),
        name="post",
    )(sc, ot, h, gain, gain_a, cos, sin, *wa[0], *wa[1], *wb[0], *wb[1], kv, *after)


def ffn_back(state, core, refs, weights):
    gate_ref, up_ref, h1_ref, gain_ref, gb_ref, keep_ref, send_ref, g1_ref, p_ref, dgain_ref, do_ref = refs
    wa, sem_a, wb, sem_b, wd, sem_d = weights
    gb = state.astype(bf16)
    gb_ref[...] = gb
    n = wb.shape[4]
    first = core == 0
    arrived_down(wd, sem_d)
    db = None
    for m in range(4):
        cols = slice(m * n, (m + 1) * n)
        dz = nn(gb, wd[m])
        gate, up = gate_ref[:, cols].astype(f32), up_ref[:, cols].astype(f32)
        sig = 1.0 / (1.0 + jnp.exp(-gate))
        dup = (dz * (gate * sig)).astype(bf16)
        dgate = (dz * up * (sig * (1.0 + gate * (1.0 - sig)))).astype(bf16)
        keep_ref[:, cols] = jnp.where(first, dgate, dup)
        send_ref[:, cols] = jnp.where(first, dup, dgate)
        arrived(wb, sem_b, 0, m)
        part = nt(dgate, whole(wb, 0, m))
        arrived(wb, sem_b, 1, m)
        part = part + nt(dup, whole(wb, 1, m))
        db = part if m == 0 else db + part
    dx, dgain = norm_back(h1_ref[...], gain_ref[...], db)
    dgain_ref[...] = dgain
    g1 = state + dx
    g1_ref[...] = g1
    low = g1.astype(bf16)
    do = None
    for p in range(3):
        part = low[:, p * KVW : (p + 1) * KVW]
        p_ref[p] = widened(part)
        arrived(wa, sem_a, 1, p + 1)
        part = nt(wa[1, p + 1, :, :KVW], part)
        do = part if p == 0 else do + part
    do_ref[...] = do.astype(bf16)


def finish_a(wa, sem_a, *left):
    for at in left:
        arrived(wa, sem_a, *at)


def query_back(dq_ref, wa, sem_a):
    da = None
    for m in range(3):
        arrived(wa, sem_a, 0, m)
        part = nt(dq_ref[m, :, :KVW], wa[0, m, :, :KVW])
        da = part if m == 0 else da + part
    return da


def project_back(da, own_ref, near_ref, far_ref, core, cos_ref, sin_ref, dk_ref, dv_ref, one_ref, h, gain, wa, sem_a):
    cos, sin = cos_ref[...], sin_ref[...]
    grad = own_ref[...] + far_ref[...].astype(f32) + jnp.where(core == 0, near_ref[...].astype(f32), 0.0)
    dk = rope(grad[:KVW], cos, sin, True).T.astype(bf16)
    dv = grad[KVW:].T.astype(bf16)
    dk_ref[...] = widened(dk)
    dv_ref[...] = widened(dv)
    one_ref[...] = widened(jnp.where(core == 0, dv, dk))
    arrived(wa, sem_a, 0, 3)
    arrived(wa, sem_a, 1, 0)
    da = da + nt(dk, wa[0, 3, :, :KVW]) + nt(dv, wa[1, 0, :, :KVW])
    return norm_back(h, gain, da)


def back_kernel(start, end, after, sc, *rest):
    rest = list(rest)

    def take(n):
        out = rest[:n]
        del rest[:n]
        return out

    core, chip = sc[0], sc[1]
    mine_a, other_a = take(4), take(4)
    if not end:
        mine_b, other_b = take(4), take(4)
    if start:
        (g_ref,) = take(1)
    else:
        g1_in, dq_ref, own_ref, near_ref, far_ref, h_ref, gain_a, cos_ref, sin_ref = take(9)
        if end:
            (last_ref,) = take(1)
    if not end:
        ins = take(4)
    take(after)
    if not start:
        dk_ref, dv_ref, one_ref, dgain_a = take(4)
    if end:
        (g_out,) = take(1)
    else:
        outs = take(7)
    wa, sem_a = take(2)
    fetch(mine_a, other_a, wa, sem_a, core, chip)
    if not end:
        wb, sem_b, wd, sem_d = take(4)
        fetch_ffn(mine_b, other_b, wb, wd, sem_b, sem_d, core, chip)
    if start:
        state = g_ref[...].T.astype(f32)
    else:
        da = query_back(dq_ref, wa, sem_a)
        dx, dgain = project_back(da, own_ref, near_ref, far_ref, core, cos_ref, sin_ref, dk_ref, dv_ref, one_ref, h_ref[...].astype(f32), gain_a[...], wa, sem_a)
        dgain_a[...] = dgain
        state = g1_in[...] + dx
    if end:
        width = state.shape[1]
        g_out[:width, :] = last_ref[...]
        g_out[width:, :] = state.astype(bf16).T
        finish_a(wa, sem_a, (1, 1), (1, 2), (1, 3))
    else:
        ffn_back(state, core, (*ins, *outs), (wa, sem_a, wb, sem_b, wd, sem_d))
        if start:
            finish_a(wa, sem_a, (1, 0), (0, 0), (0, 1), (0, 2), (0, 3))


def back(start, end, sc, weights, tail, ffn, after=()):
    wa, wb = weights
    width = wa[0][0].shape[0]
    args = [sc, *wa[0], *wa[1]]
    specs = [SCALARS] + [LEFT] * 8
    scratch = scratch_a(width)
    if not end:
        args += [*wb[0], *wb[1]]
        specs += [LEFT] * 8
        scratch += scratch_ffn(width, wb[0][0].shape[2])
    args += list(tail)
    specs += [WHOLE] * len(tail)
    n = tail[0].shape[1 if start else 0]
    outs = []
    if not end:
        args += list(ffn)
        specs += [WHOLE] * len(ffn)
    if not start:
        outs += [shape((n, PIECE), bf16)] * 3 + [shape((1, width), f32)]
    if end:
        outs += [shape((2 * width, n), bf16)]
    else:
        hidden = ffn[0].shape[1]
        outs += [shape((n, width), bf16), shape((n, hidden), bf16), shape((n, hidden), bf16)]
        outs += [shape((n, width), f32), shape((3, n, PIECE), bf16), shape((1, width), f32), shape((width, n), bf16)]
    args += list(after)
    specs += [LEFT] * len(after)
    return pl.pallas_call(
        functools.partial(back_kernel, start, end, len(after)),
        out_shape=tuple(outs),
        in_specs=specs,
        out_specs=(WHOLE,) * len(outs),
        scratch_shapes=scratch,
        cost_estimate=BRIEF,
        compiler_params=pltpu.CompilerParams(vmem_limit_bytes=LIMIT),
        name="back_end" if end else ("back_start" if start else "back_join"),
    )(*args)


def by_turn(core, chip):
    one = 1 + core
    return chip ^ one, chip ^ 3, chip, chip ^ (3 - one)


def turned(dst, blocks):
    n = blocks[0].shape[0]
    for i, block in enumerate(blocks):
        dst[:, i * n : (i + 1) * n] = block[...].T


def grad_ffn_kernel(sc, *rest):
    lefts, rights = rest[:4], rest[4:8]
    send_ref, keep_ref, left, right = rest[-4:]
    core, chip = sc[0], sc[1]
    n, cols = rights[0].shape[0], right.shape[1]
    turned(left, lefts)
    for i, m in enumerate(by_turn(core, chip)):
        at = pl.multiple_of(m * cols, 128)
        for j, block in enumerate(rights):
            right[j * n : (j + 1) * n, :] = block[:, pl.ds(at, cols)]
        out = send_ref if i < 2 else keep_ref
        out[i % 2] = nn(left[...], right[...]).astype(bf16)


def grad_ffn(sc, lefts, rights, after):
    n, width = lefts[0].shape
    cols = rights[0].shape[1] // 4
    out = shape((2, width, cols), bf16)
    return pl.pallas_call(
        grad_ffn_kernel,
        out_shape=(out, out),
        in_specs=[SCALARS] + [WHOLE] * 8 + [LEFT] * len(after),
        out_specs=(WHOLE,) * 2,
        scratch_shapes=[pltpu.VMEM((width, 4 * n), bf16), pltpu.VMEM((4 * n, cols), bf16)],
        cost_estimate=BRIEF,
        compiler_params=pltpu.CompilerParams(vmem_limit_bytes=LIMIT),
        name="grad_ffn",
    )(sc, *lefts, *rights, *after)


def grad_down_kernel(sc, *rest):
    lefts, rights = rest[:4], rest[4:8]
    send_ref, keep_ref, left, right = rest[-4:]
    n, (_, half, cols) = rights[0].shape[0], send_ref.shape
    turned(left, lefts)
    rows = pl.ds(pl.multiple_of(sc[0] * half, half), half)
    like = sc[2] & 1
    for h in range(2):
        for out, parity in ((send_ref, 1 - like), (keep_ref, like)):
            at = pl.multiple_of((2 * h + parity) * cols, 128)
            for j, block in enumerate(rights):
                right[j * n : (j + 1) * n, :] = block[:, pl.ds(at, cols)]
            out[h] = nn(left[rows, :], right[...]).astype(out.dtype)


def grad_down(sc, lefts, rights, after):
    n, width = lefts[0].shape
    cols = rights[0].shape[1] // 4
    block = (2, width // 2, cols)
    return pl.pallas_call(
        grad_down_kernel,
        out_shape=(shape(block, bf16), shape(block, bf16)),
        in_specs=[SCALARS] + [WHOLE] * 8 + [LEFT] * len(after),
        out_specs=(WHOLE,) * 2,
        scratch_shapes=[pltpu.VMEM((width, 4 * n), bf16), pltpu.VMEM((4 * n, cols), bf16)],
        cost_estimate=BRIEF,
        compiler_params=pltpu.CompilerParams(vmem_limit_bytes=LIMIT),
        name="grad_down",
    )(sc, *lefts, *rights, *after)


def grad_attention_kernel(sc, *rest):
    a_refs, o_refs, rest = rest[:4], rest[4:8], rest[8:]
    queries, keys, values, outs, threes, ones = (rest[i : i + 2] for i in range(0, 12, 2))
    gain_a, gain_f = (rest[i : i + 2] for i in (12, 14))
    *sends, keep_ref, left, right = rest[-5:]
    core, chip = sc[0], sc[1]
    n, width = a_refs[0].shape
    turned(left.at[0], a_refs)
    gains = [g[0][...] + g[1][...] for g in (gain_a, gain_f)]
    gains = jnp.concatenate([*gains, jnp.zeros((6, width), f32)], axis=0).T
    gains = jnp.concatenate([gains, jnp.zeros((width, PIECE - KVW - 8), f32)], axis=1).astype(bf16)

    def fill(at, of_three, own_three, own_one, single):
        for j in range(2):
            for i in range(3):
                right[of_three + i, j * n : (j + 1) * n, :] = own_three[j][i]
                right[of_three + i, (j + 2) * n : (j + 3) * n, :] = threes[j][i]
            right[single, j * n : (j + 1) * n, :] = own_one[j][...]
            right[single, (j + 2) * n : (j + 3) * n, :] = ones[j][...]

    @pl.when(core == 0)
    def _():
        fill(0, 0, queries, keys, 3)

    @pl.when(core == 1)
    def _():
        turned(left.at[1], o_refs)
        fill(0, 1, outs, values, 0)

    for i, m in enumerate(by_turn(core, chip)):
        out = sends[i] if i < 2 else keep_ref.at[i - 2]
        which = jnp.where(m > 0, core, 0)
        out[...] = nn(left[which], right[m]).astype(bf16)
        out[:, KVW:] = gains


def grad_attention(sc, a, o, own, got, gains, after):
    n, width = a[0].shape
    out = shape((width, PIECE), bf16)
    return pl.pallas_call(
        grad_attention_kernel,
        out_shape=(out, out, shape((2, width, PIECE), bf16)),
        in_specs=[SCALARS] + [WHOLE] * 24 + [LEFT] * len(after),
        out_specs=(WHOLE,) * 3,
        scratch_shapes=[pltpu.VMEM((2, width, 4 * n), bf16), pltpu.VMEM((4, 4 * n, PIECE), bf16)],
        cost_estimate=BRIEF,
        compiler_params=pltpu.CompilerParams(vmem_limit_bytes=LIMIT),
        name="grad_attention",
    )(sc, *a, *o, *own, *got, *gains, *after)


def lay_kernel(count, sc, *rest):
    mine, other, outs, kept = rest[:4], rest[4:8], rest[-1 - count : -1], rest[-1]
    core, chip = sc[0], sc[1]
    for kind, pieces in ((core, mine), (1 - core, other)):
        for who, piece in zip(whose(kind), pieces):
            kept[kind, chip ^ who] = piece[...]
    n = sum(o.shape[1] for o in outs[: 4 if len(outs) > 2 else 2]) // 8
    cols = [jnp.concatenate([kept[c, m, :, :n].astype(f32) for m in range(4)], axis=1) for c in range(2)]
    if len(outs) == 2:
        outs[0][...] = cols[0]
        outs[1][...] = cols[1]
    else:
        outs[0][...] = cols[0][:, : 3 * n]
        outs[1][...] = cols[0][:, 3 * n :]
        outs[2][...] = cols[1][:, :n]
        outs[3][...] = cols[1][:, n:]
        gains = kept[0, 0, :, n : n + 8].astype(f32) + kept[1, 0, :, n : n + 8].astype(f32)
        outs[4][...] = gains.T[:2]


def lay(sc, mine, other, widths, after):
    rows, n = mine[0].shape
    outs = tuple(shape((rows, w), f32) for w in widths)
    if len(widths) > 2:
        outs += (shape((2, rows), f32),)
    return pl.pallas_call(
        functools.partial(lay_kernel, len(outs)),
        out_shape=outs,
        in_specs=[SCALARS] + [WHOLE] * 8 + [LEFT] * len(after),
        out_specs=(WHOLE,) * len(outs),
        scratch_shapes=[pltpu.VMEM((2, 4, rows, n), bf16)],
        cost_estimate=BRIEF,
        compiler_params=pltpu.CompilerParams(vmem_limit_bytes=24 << 20),
        name="lay",
    )(sc, *mine, *other, *after)


def pick_first_kernel(sc, q_ref, k_ref, v_ref, o_ref, gain_ref, out_ref):
    rows = out_ref.shape[0]
    which = sc[0] * 4 + sc[1]
    pad = jnp.zeros((6, rows), f32)
    gains = jnp.concatenate([gain_ref[...], pad], axis=0).T.astype(bf16)
    rest = jnp.zeros((rows, PIECE - KVW - 8), bf16)
    for at in range(8):

        @pl.when(which == at)
        def _():
            if at in (3, 4):
                piece = (k_ref if at == 3 else v_ref)[...].T
            else:
                source, m = (q_ref, at) if at < 3 else (o_ref, at - 5)
                piece = source[:, m * KVW : (m + 1) * KVW]
            out_ref[...] = jnp.concatenate([piece, gains, rest], axis=1)


def pick_first(sc, query, key, value, out, gains):
    return pl.pallas_call(
        pick_first_kernel,
        out_shape=shape((query.shape[0], PIECE), bf16),
        in_specs=[SCALARS] + [WHOLE] * 5,
        out_specs=WHOLE,
        cost_estimate=BRIEF,
        compiler_params=pltpu.CompilerParams(vmem_limit_bytes=16 << 20),
        name="pick_first",
    )(sc, query, key, value, out, gains)


def pick_kernel(sc, gate, up, down, *rest):
    out_ref, sems = rest[-2:]
    rows, cols = out_ref.shape[0] - ROWS, out_ref.shape[1]
    into = out_ref.at[:rows]
    start = pl.multiple_of(down_rows(sc[0], sc[1], down.shape[0]), 64)
    copy = pltpu.make_async_copy(down.at[pl.ds(start, ROWS), :], out_ref.at[rows:], sems.at[1])
    copy.start()
    at = pl.ds(pl.multiple_of(sc[1] * cols, 128), cols)
    for c, source in ((0, gate), (1, up)):

        @pl.when(sc[0] == c)
        def _():
            pltpu.make_async_copy(source.at[:, at], into, sems.at[0]).start()

    pltpu.make_async_copy(gate.at[:, at], into, sems.at[0]).wait()
    copy.wait()


def pick(sc, gate, up, down, after):
    return pl.pallas_call(
        pick_kernel,
        out_shape=shape((gate.shape[0] + ROWS, gate.shape[1] // 4), bf16),
        in_specs=[SCALARS] + [LEFT] * (3 + len(after)),
        out_specs=WHOLE,
        scratch_shapes=[pltpu.SemaphoreType.DMA((2,))],
        cost_estimate=BRIEF,
        compiler_params=pltpu.CompilerParams(vmem_limit_bytes=16 << 20),
        name="pick",
    )(sc, gate, up, down, *after)


def gains_kernel(first_ref, out_ref):
    for j in range(4):
        n = first_ref.shape[1]
        out_ref[:, j * n : (j + 1) * n] = first_ref[j, :, KVW : KVW + 8].astype(f32).T[:2]


def gains_of(first):
    return pl.pallas_call(
        gains_kernel,
        out_shape=shape((2, 4 * first.shape[1]), f32),
        in_specs=[WHOLE],
        out_specs=WHOLE,
        cost_estimate=BRIEF,
        compiler_params=pltpu.CompilerParams(vmem_limit_bytes=16 << 20),
        name="gains",
    )(first)


def stack_kernel(sc, *rest):
    parts, out_ref, sems = rest[:4], rest[-2], rest[-1]
    copies = [pltpu.make_async_copy(p, out_ref.at[sc[2] ^ s], sems.at[s]) for s, p in enumerate(parts)]
    for copy in copies:
        copy.start()
    for copy in copies:
        copy.wait()


def stack(sc, parts, after=()):
    return pl.pallas_call(
        stack_kernel,
        out_shape=shape((4,) + parts[0].shape, parts[0].dtype),
        in_specs=[SCALARS] + [LEFT] * (4 + len(after)),
        out_specs=WHOLE,
        scratch_shapes=[pltpu.SemaphoreType.DMA((4,))],
        cost_estimate=BRIEF,
        compiler_params=pltpu.CompilerParams(vmem_limit_bytes=16 << 20),
        name="stack",
    )(sc, *parts, *after)


def small(kernel, sc, args, outs, scratch, after, name):
    return pl.pallas_call(
        kernel,
        out_shape=tuple(outs),
        in_specs=[SCALARS] + [WHOLE] * len(args) + [LEFT] * len(after),
        out_specs=(WHOLE,) * len(outs),
        scratch_shapes=scratch,
        cost_estimate=BRIEF,
        compiler_params=pltpu.CompilerParams(vmem_limit_bytes=32 << 20),
        name=name,
    )(sc, *args, *after)


def sum_first(sc, keep, got, after, parts=1):
    def kernel(sc, keep_ref, *rest):
        own_got, later_got = rest[:2] if len(got) == 2 else (rest[0].at[0], rest[0].at[1])
        own_ref = rest[-1]
        for i, later_ref in enumerate(rest[-1 - parts : -1]):
            n = later_ref.shape[0]
            rows = slice(i * n, (i + 1) * n)
            later_ref[...] = (keep_ref[1, rows].astype(f32) + later_got[rows].astype(f32)).astype(bf16)
        own_ref[...] = keep_ref[0].astype(f32) + own_got[...].astype(f32)

    rows, cols = keep.shape[1:]
    outs = [shape((rows // parts, cols), bf16)] * parts + [shape((rows, cols), f32)]
    return small(kernel, sc, [keep, *got], outs, [], after, "sum_first")


def sum_second(sc, own, got, after):
    def kernel(sc, own_ref, *rest):
        gots, (send_ref, keep_ref, total) = rest[: len(got)], rest[-3:]
        n = total.shape[1]
        for j in range(4):
            part, at = divmod(j * n, gots[0].shape[0])
            total[j] = own_ref[j * n : (j + 1) * n, :] + gots[part][at : at + n, :].astype(f32)
        like = sc[2] & 1
        for h in range(2):
            send_ref[h] = total[2 * h + 1 - like].astype(bf16)
            keep_ref[h] = total[2 * h + like]

    rows, cols = own.shape
    part = (rows // 4, cols)
    outs = [shape((2,) + part, bf16), shape((2,) + part, f32)]
    return small(kernel, sc, [own, *got], outs, [pltpu.VMEM((4,) + part, f32)], after, "sum_second")


def sum_third(sc, keep, got, after):
    def kernel(sc, keep_ref, got_ref, *rest):
        send_ref, own_ref = rest[-2:]
        h = sc[2] >> 1
        send_ref[...] = (keep_ref[1 - h].astype(f32) + got_ref[1 - h].astype(f32)).astype(bf16)
        own_ref[...] = keep_ref[h].astype(f32) + got_ref[h].astype(f32)

    part = keep.shape[1:]
    return small(kernel, sc, [keep, got], [shape(part, bf16), shape(part, f32)], [], after, "sum_third")


def down_split(sc, own, got, after):
    def kernel(sc, own_ref, got_ref, *rest):
        send_ref, kept_ref, total = rest[-3:]
        n = total.shape[1]
        for m in range(4):
            rows = slice(m * n, (m + 1) * n)
            total[m] = own_ref[rows, :] + got_ref[rows, :].astype(f32)
        for i, m in enumerate(by_turn(sc[0], sc[1])):
            out = send_ref if i < 2 else kept_ref
            out[i % 2] = total[m].astype(bf16)

    rows, cols = own.shape
    out = shape((2, rows // 4, cols), bf16)
    return small(kernel, sc, [own, got], [out, out], [pltpu.VMEM((4, rows // 4, cols), f32)], after, "down_split")


def sum_two(sc, own, got, after):
    def kernel(sc, own_ref, got_ref, *rest):
        rest[-1][...] = (own_ref[...] + got_ref[...].astype(f32)).astype(bf16)

    return small(kernel, sc, [own, got], [shape(own.shape, bf16)], [], after, "sum_two")[0]


def lay_down(sc, mine, other, after):
    def kernel(sc, *rest):
        out_ref, total = rest[-2:]
        n = total.shape[2]
        for kind, pieces in ((sc[0], rest[:4]), (1 - sc[0], rest[4:8])):
            for who, piece in zip(whose(kind), pieces):
                total[kind, sc[1] ^ who] = piece[...].astype(f32)
        for c in range(2):
            for m in range(4):
                at = (c * 4 + m) * n
                out_ref[at : at + n, :] = total[c, m]

    n, cols = mine[0].shape
    return small(kernel, sc, [*mine, *other], [shape((8 * n, cols), f32)], [pltpu.VMEM((2, 4, n, cols), f32)], after, "lay_down")[0]


def hold(value, after):
    return pl.pallas_call(
        lambda *refs: None,
        out_shape=shape(value.shape, value.dtype),
        in_specs=[LEFT] * (1 + len(after)),
        out_specs=LEFT,
        input_output_aliases={0: 0},
        cost_estimate=BRIEF,
        compiler_params=pltpu.CompilerParams(vmem_limit_bytes=1 << 20),
        name="hold",
    )(value, *after)


def far_sum(sc, far, near, after):
    def kernel(sc, far_ref, near_ref, *rest):
        rest[-1][...] = (far_ref[...] + jnp.where(sc[0] == 1, near_ref[...].astype(f32), 0.0)).astype(bf16)

    return small(kernel, sc, [far, near], [shape(far.shape, bf16)], [], after, "far_sum")[0]


CORE, SIDE, BACK = 1, 2, 4
rope_base = 10000.0
RUNS = 2


def flip(value, bit, bit1=None):
    count = lax.axis_size("dp")
    bits = (bit, bit if bit1 is None else bit1)
    return lax.ppermute(value, "dp", [(i, i ^ bits[i & 1]) for i in range(count)])


def flip_z(value, bit, where=lambda d, z: True):
    count, depth = lax.axis_size("dp"), lax.axis_size("fsdp")
    pairs = [(d * depth + z, d * depth + (z ^ bit)) for d in range(count) for z in range(depth) if where(d, z)]
    return lax.ppermute(value, ("dp", "fsdp"), pairs)


def home_to_work(value, back=False):
    count, depth = lax.axis_size("dp"), lax.axis_size("fsdp")
    pairs = []
    for d in range(count):
        for z in range(depth):
            there = (d & ~1) | (z & 1), 2 * (d & 1) + (z >> 1)
            pair = (d * depth + z, there[0] * depth + there[1])
            pairs.append(pair[::-1] if back else pair)
    return lax.ppermute(value, ("dp", "fsdp"), pairs)


def place():
    d, z = lax.axis_index("dp"), lax.axis_index("fsdp")
    return d & 1, (d >> 1) & 3, z


def turns(shard):
    far = flip_z(shard, 2)
    return shard, flip_z(shard, 1), far, flip_z(far, 1)


def plane_gather(piece):
    first, second = flip(piece, SIDE, BACK), flip(piece, BACK, SIDE)
    mine = (piece, first, second, flip(first, BACK, SIDE))
    return mine, tuple(flip(p, CORE) for p in mine)


def window(own):
    core, _, _ = place()
    depth = lax.axis_size("fsdp")
    far = lax.ppermute(own, "fsdp", [(z, z + 1) for z in range(0, depth, 2)])
    near = flip(jnp.where(core == 0, own, far), CORE)
    return far, near, own


def unwindow(sc, far, near, after=()):
    depth = lax.axis_size("fsdp")
    near = flip(near, CORE)
    far = far_sum(sc, far, near, after)
    return near, far, lax.ppermute(far, "fsdp", [(z + 1, z) for z in range(0, depth, 2)])


def over_groups(value):
    bit = 8
    while bit < lax.axis_size("dp"):
        value = (value.astype(f32) + flip(value, bit).astype(f32)).astype(bf16)
        bit *= 2
    return value


def spread(piece):
    return piece, flip(piece, SIDE, BACK), flip(piece, BACK, SIDE), flip(piece, SIDE | BACK)


def across(pieces):
    return tuple(flip(p, CORE) for p in pieces)


def body(tokens, segment_ids, attn_gain, query_weight, key_weight, value_weight, out_weight, ffn_gain, gate_weight, up_weight, down_weight, cotangent):
    core, chip, z = place()
    sc = jnp.stack([core, chip, z]).astype(jnp.int32)
    _, stretch, width = tokens.shape
    rows, depth = query_weight.shape[0], lax.axis_size("fsdp")
    block = 2 * (z & 1) + core
    positions = (block * stretch + jnp.arange(stretch)).astype(f32)
    freq = rope_base ** (-2.0 * jnp.arange(HEAD_DIM // 2, dtype=f32) / HEAD_DIM)
    angle = freq[:, None] * positions[None, :]
    cos, sin = jnp.cos(angle), jnp.sin(angle)

    gains = jnp.stack([attn_gain, ffn_gain]).astype(f32)
    parts_a = turns(pick_first(sc, query_weight, key_weight.T, value_weight.T, out_weight, gains))
    ids = jnp.broadcast_to((segment_ids[0] + 1).astype(bf16), (IDS, stretch))
    tokens = home_to_work(jnp.concatenate([tokens[0].T, ids]))
    piece_b = pick(sc, gate_weight, up_weight, down_weight.T, parts_a[1:2])
    whole_a = stack(sc, parts_a, [piece_b])
    gains = gains_of(whole_a)
    gain_a, gain_f = gains[:1], gains[1:]
    wa = plane_gather(whole_a.reshape(depth * rows, PIECE))
    side_b = flip_z(piece_b, 1)
    far_b = hold(flip_z(piece_b, 2), [wa[0][1], wa[0][2], side_b])
    whole_b = stack(sc, (piece_b, side_b, far_b, flip_z(far_b, 1)), [wa[0][3]])
    first_b, second_b = flip(whole_b, SIDE, BACK), flip(whole_b, BACK, SIDE)

    h_0, a0, q0, own = pre(sc, tokens, gain_a, cos, sin, *wa, [whole_b])
    kv0 = window(own)
    first_b = hold(first_b, [kv0[0], second_b])
    opposite_b = flip(first_b, BACK, SIDE)
    o0, lse0 = attend(q0, kv0)
    wb = whole_b, first_b, second_b, hold(opposite_b, [o0])
    wb = wb, across(wb)
    weights = wa, wb
    cot = home_to_work(cotangent[0].T)
    mixed0, h1_0, b0, gate0, up0, z0, h_1, a1, q1, own = post(False, [], sc, o0, h_0, gain_f, gain_a, cos, sin, own, *weights)
    kv1 = window(own)
    across_0 = across((a0, b0, mixed0, z0))
    o1, lse1 = attend(q1, kv1, across_0)
    mixed1, h1_1, b1, gate1, up1, z1, output = post(True, [cot], sc, o1, h_1, gain_f, gain_a, cos, sin, own, *weights)
    across_1 = across((a1, b1, mixed1, z1))

    gb1, act1, away1, g1, p1, dgain_f1, do = back(True, False, sc, weights, [cot], [gate1, up1, h1_1, gain_f])
    across_2 = across((gb1, away1))
    dq1, three1, far, near, own = attend_back(sc, p1, q1, kv1, lse1, do, cos, sin, [*across_1])
    near, _, far = unwindow(sc, far, near)
    (three1,) = across((three1,))
    tail = [g1, dq1, own, near, far, h_1, gain_a, cos, sin]
    dk1, dv1, one1, dgain_a1, gb0, act0, away0, g1, p0, dgain_f0, do = back(False, False, sc, weights, tail, [gate0, up0, h1_0, gain_f], [three1, *across_2])

    away0, gb0_, one1 = across((away0, gb0, one1))
    send_b, keep_b = grad_ffn(sc, [b1, b0, across_1[1], across_0[1]], [act1, act0, across_2[1], away0], [])
    got_b = flip(send_b, SIDE, BACK)
    dq0, three0, far, near, own = attend_back(sc, p0, q0, kv0, lse0, do, cos, sin, [one1, send_b])
    near, down_far, far = unwindow(sc, far, near)
    send_d, keep_d = grad_down(sc, [gb1, gb0, across_2[0], gb0_], [z1, z0, across_1[3], across_0[3]], [down_far])
    got_d = flip_z(send_d, 1)
    (three0,) = across((three0,))
    tail = [g1, dq0, own, near, far, h_0, gain_a, cos, sin, output]
    dk0, dv0, one0, dgain_a0, leaving = back(False, True, sc, weights, tail, None, [send_d])
    later_b, own_b = sum_first(sc, keep_b, [got_b], [one0])
    more_b = flip(later_b, BACK, SIDE)
    own = [dq1, dq0, dk1, dk0, dv1, dv0, p1, p0]
    got = [three1, three0, one1, flip(one0, CORE)]
    *send_a, keep_a = grad_attention(sc, [a1, a0, across_1[0], across_0[0]], [mixed1, mixed0, across_1[2], across_0[2]], own, got, [dgain_a1, dgain_a0, dgain_f1, dgain_f0], [later_b])
    got_a = [flip(v, SIDE, BACK) for v in send_a]
    send_d, keep_d = sum_third(sc, keep_d, got_d, send_a)
    got_d = flip_z(send_d, 2)
    send_b, ring_b = sum_second(sc, own_b, [more_b], [send_d])
    got_b = flip_z(send_b, 1)
    *later_a, own_a = sum_first(sc, keep_a, got_a, [ring_b], 2)
    more_a = [flip(v, BACK, SIDE) for v in later_a]
    send_d, keep_d = down_split(sc, keep_d, got_d, [own_a])
    got_d = flip(send_d, SIDE, BACK)
    send_b, ring_b = sum_third(sc, ring_b, got_b, [send_d])
    got_b = flip_z(send_b, 2)
    send_a, ring_a = sum_second(sc, own_a, more_a, [send_b])
    got_a = flip_z(send_a, 1)
    piece_b = over_groups(sum_two(sc, ring_b, got_b, [send_a]))
    all_b = spread(piece_b)
    send_a, ring_a = sum_third(sc, ring_a, got_a, [piece_b])
    got_a = flip_z(send_a, 2)
    later_d, own_d = sum_first(sc, keep_d, [got_d], [send_a])
    more_d = flip(later_d, BACK, SIDE)
    piece_a = over_groups(sum_two(sc, ring_a, got_a, [later_d]))
    all_a = spread(piece_a)
    piece_d = over_groups(sum_two(sc, own_d, more_d, [piece_a]))
    grad_gate, grad_up = lay(sc, all_b, across(all_b), (gate_weight.shape[1],) * 2, [piece_d])
    all_d = spread(piece_d)
    grad_query, grad_key, grad_value, grad_out, dgains = lay(sc, all_a, across(all_a), (width, KVW, KVW, width), [grad_gate])
    grad_down_ = lay_down(sc, all_d, across(all_d), [grad_query])
    leaving = home_to_work(hold(leaving, [piece_b]), back=True)
    output, grad_tokens = leaving[:width].T, leaving[width:].astype(f32).T
    return (output[None], grad_tokens[None], dgains[0], grad_query, grad_key, grad_value, grad_out, dgains[1], grad_gate, grad_up, grad_down_.T)


def solution(mesh):
    wide, rows, shard = P("dp", "fsdp", None), P("dp", "fsdp"), P("fsdp", None)
    in_specs = (wide, rows, P("fsdp"), shard, shard, shard, shard, P("fsdp"), shard, shard, shard, wide)
    out_specs = (wide, wide, P("fsdp"), shard, shard, shard, shard, P("fsdp"), shard, shard, shard)
    return jax.shard_map(body, mesh=mesh, in_specs=in_specs, out_specs=out_specs, check_vma=False)
```

```python
import functools
import jax
import jax.numpy as jnp
from jax import lax
from jax.sharding import PartitionSpec as P
from jax.experimental import pallas as pl
from jax.experimental.pallas import tpu as pltpu

f32, bf16 = jnp.float32, jnp.bfloat16
eps = 1e-05
HEADS, KV_HEADS, HEAD_DIM, GROUP, KVW = 15, 5, 64, 3, 320
IDS = 16
ROWS = 128
PIECE = 384
LIMIT = 58 << 20
WHOLE = pl.BlockSpec(memory_space=pltpu.VMEM)
LEFT = pl.BlockSpec(memory_space=pl.ANY)
SCALARS = pl.BlockSpec(memory_space=pltpu.SMEM)
BRIEF = pl.CostEstimate(flops=1024, bytes_accessed=1024, transcendentals=0)


def contract(a, b, i, j):
    return lax.dot_general(a, b, (((i,), (j,)), ((), ())), preferred_element_type=f32)


def nn(a, b):
    return contract(a, b, 1, 0)


def nt(a, b):
    return contract(a, b, 1, 1)


def tn(a, b):
    return contract(a, b, 0, 0)


def whose(core):
    return 0, 1 + core, 2 - core, 3


def fetch(mine, other, kept, sems, core, chip, only=None, turns=range(4)):
    for j in turns:
        for kind, pieces in ((core, mine), (1 - core, other)):
            at = chip ^ whose(kind)[j]

            def copy():
                pltpu.make_async_copy(pieces[j], kept.at[kind, at], sems.at[kind, at]).start()

            if only is None:
                copy()
            else:
                pl.when(kind == only)(copy)


def arrived(kept, sems, *at):
    pltpu.make_async_copy(kept.at[at], kept.at[at], sems.at[at]).wait()


def normed(x, gain):
    return x * lax.rsqrt(jnp.mean(x * x, axis=-1, keepdims=True) + eps) * gain


def norm_back(x, gain, grad):
    r = lax.rsqrt(jnp.mean(x * x, axis=-1, keepdims=True) + eps)
    hat = x * r
    scaled = grad * gain
    dx = r * (scaled - hat * jnp.mean(scaled * hat, axis=-1, keepdims=True))
    return dx, jnp.sum(grad * hat, axis=0, keepdims=True)


def widened(x):
    return jnp.concatenate([x, jnp.zeros((x.shape[0], PIECE - x.shape[1]), x.dtype)], axis=1)


def rope(u, cos, sin, back):
    heads = u.shape[0] // HEAD_DIM
    half = HEAD_DIM // 2
    out = []
    for h in range(heads):
        u1, u2 = u[h * HEAD_DIM : h * HEAD_DIM + half], u[h * HEAD_DIM + half : (h + 1) * HEAD_DIM]
        if back:
            out += [u1 * cos + u2 * sin, u2 * cos - u1 * sin]
        else:
            out += [u1 * cos - u2 * sin, u2 * cos + u1 * sin]
    return jnp.concatenate(out, axis=0)


def project(state, gain_ref, cos_ref, sin_ref, ids, kept, sems, a_ref, q_ref, kv_ref):
    a = normed(state, gain_ref[...]).astype(bf16)
    a_ref[...] = a
    cos, sin = cos_ref[...], sin_ref[...]
    arrived(kept, sems, 0, 3)
    kv_ref[:KVW, :] = rope(nn(a, kept[0, 3, :, :KVW]).T, cos, sin, False).astype(bf16)
    arrived(kept, sems, 1, 0)
    kv_ref[2 * KVW :, :] = ids
    kv_ref[KVW : 2 * KVW, :] = nn(a, kept[1, 0, :, :KVW]).T.astype(bf16)
    for m in range(3):
        arrived(kept, sems, 0, m)
        q_ref[pl.ds(m * KVW, KVW), :] = rope(nn(a, kept[0, m, :, :KVW]).T, cos, sin, False).astype(bf16)


def pre_kernel(sc, ht_ref, gain_ref, cos_ref, sin_ref, *rest):
    width = ht_ref.shape[0] - IDS
    mine, other = rest[:4], rest[4:8]
    h_ref, a_ref, q_ref, kv_ref, kept, sems = rest[-6:]
    core, chip = sc[0], sc[1]
    fetch(mine, other, kept, sems, core, chip)
    h = ht_ref[:width, :].T
    h_ref[...] = h
    project(h.astype(f32), gain_ref, cos_ref, sin_ref, ht_ref[width:, :], kept, sems, a_ref, q_ref, kv_ref)
    for m in range(1, 4):
        arrived(kept, sems, 1, m)


def scratch_a(width):
    return [pltpu.VMEM((2, 4, width, PIECE), bf16), pltpu.SemaphoreType.DMA((2, 4))]


def shape(s, d):
    return jax.ShapeDtypeStruct(s, d)


def pre(sc, ht, gain, cos, sin, mine_a, other_a, after):
    width, n = ht.shape[0] - IDS, ht.shape[1]
    return pl.pallas_call(
        pre_kernel,
        out_shape=(shape((n, width), bf16), shape((n, width), bf16), shape((width, n), bf16), shape((2 * KVW + IDS, n), bf16)),
        in_specs=[SCALARS] + [WHOLE] * 4 + [LEFT] * (8 + len(after)),
        out_specs=(WHOLE,) * 4,
        scratch_shapes=scratch_a(width),
        cost_estimate=BRIEF,
        compiler_params=pltpu.CompilerParams(vmem_limit_bytes=LIMIT),
        name="pre",
    )(sc, ht, gain, cos, sin, *mine_a, *other_a, *after)


def bias_of(kv):
    keys, n = kv.shape[1], kv.shape[1] // 3
    ids = kv[2 * KVW :, :].astype(f32)
    seg_k, seg_q = ids.T[:, :1], ids[:1, 2 * n :]
    j = lax.broadcasted_iota(jnp.int32, (keys, n), 0)
    i = lax.broadcasted_iota(jnp.int32, (keys, n), 1) + (keys - n)
    return jnp.where((seg_k == seg_q) & (j <= i), 0.0, -1e30).astype(f32)


def window_of(parts, whole):
    n = parts[0].shape[1]
    for w, part in enumerate(parts):
        whole[:, w * n : (w + 1) * n] = part[...]


def attend_kernel(q_ref, kv0, kv1, kv2, *rest):
    o_ref, lse_ref, bias, kv = rest[-4:]
    window_of((kv0, kv1, kv2), kv)
    bias[...] = bias_of(kv)

    def head(e, _):
        row = pl.multiple_of(e * HEAD_DIM, HEAD_DIM)
        k = kv[pl.ds(row, HEAD_DIM), :]
        v = kv[pl.ds(row + KVW, HEAD_DIM), :]
        for g in range(GROUP):
            at = pl.multiple_of((e * GROUP + g) * HEAD_DIM, HEAD_DIM)
            q = q_ref[pl.ds(at, HEAD_DIM), :]
            s = tn(k, q) * HEAD_DIM ** (-0.5) + bias[...]
            top = jnp.max(s, axis=0, keepdims=True)
            expo = jnp.exp(s - top)
            total = jnp.sum(expo, axis=0, keepdims=True)
            probs = (expo * (1.0 / total)).astype(bf16)
            o_ref[pl.ds(at, HEAD_DIM), :] = nn(v, probs).astype(bf16)
            lse_ref[pl.ds(e * GROUP + g, 1), :] = top + jnp.log(total)
        return 0

    lax.fori_loop(0, KV_HEADS, head, 0)


def attend(q, kvs, after=()):
    width, n = q.shape
    return pl.pallas_call(
        attend_kernel,
        out_shape=(shape((width, n), bf16), shape((HEADS, n), f32)),
        in_specs=[WHOLE] * 4 + [LEFT] * len(after),
        out_specs=(WHOLE,) * 2,
        scratch_shapes=[pltpu.VMEM((3 * n, n), f32), pltpu.VMEM((2 * KVW + IDS, 3 * n), bf16)],
        cost_estimate=BRIEF,
        compiler_params=pltpu.CompilerParams(vmem_limit_bytes=24 << 20),
        name="attend",
    )(q, *kvs, *after)


def attend_back_kernel(sc, p_ref, q_ref, kv0, kv1, kv2, lse_ref, do_ref, cos_ref, sin_ref, *rest):
    dq_ref, three_ref, far_ref, near_ref, own_ref, bias, kv, dqs = rest[-8:]
    n = q_ref.shape[1]
    window_of((kv0, kv1, kv2), kv)
    bias[...] = bias_of(kv)
    scale = HEAD_DIM ** (-0.5)

    def head(e, _):
        row = pl.multiple_of(e * HEAD_DIM, HEAD_DIM)
        k = kv[pl.ds(row, HEAD_DIM), :]
        v = kv[pl.ds(row + KVW, HEAD_DIM), :]
        dk = dv = None
        for g in range(GROUP):
            at = pl.multiple_of((e * GROUP + g) * HEAD_DIM, HEAD_DIM)
            q = q_ref[pl.ds(at, HEAD_DIM), :]
            do = do_ref[pl.ds(at, HEAD_DIM), :]
            s = tn(k, q) * scale + bias[...]
            probs = jnp.exp(s - lse_ref[pl.ds(e * GROUP + g, 1), :])
            dp = tn(v, do)
            inner = jnp.sum(probs * dp, axis=0, keepdims=True)
            ds = (probs * (dp - inner)).astype(bf16)
            dvg, dkg = nt(do, probs.astype(bf16)), nt(q, ds)
            dv, dk = (dvg, dkg) if g == 0 else (dv + dvg, dk + dkg)
            dqs[pl.ds(at, HEAD_DIM), :] = nn(k, ds)
        for at, grad in ((row, dk * scale), (row + KVW, dv)):
            far_ref[pl.ds(at, HEAD_DIM), :] = grad[:, :n]
            near_ref[pl.ds(at, HEAD_DIM), :] = grad[:, n : 2 * n].astype(bf16)
            own_ref[pl.ds(at, HEAD_DIM), :] = grad[:, 2 * n :]
        return 0

    lax.fori_loop(0, KV_HEADS, head, 0)
    cos, sin = cos_ref[...] * scale, sin_ref[...] * scale
    for m in range(3):
        dq = widened(rope(dqs[m * KVW : (m + 1) * KVW, :], cos, sin, True).T.astype(bf16))
        dq_ref[m] = dq
        three_ref[m] = jnp.where(sc[0] == 0, p_ref[m], dq)


def attend_back(sc, p, q, kvs, lse, do, cos, sin, after=()):
    width, n = q.shape
    block = (2 * KVW, n)
    return pl.pallas_call(
        attend_back_kernel,
        out_shape=(shape((3, n, PIECE), bf16), shape((3, n, PIECE), bf16), shape(block, f32), shape(block, bf16), shape(block, f32)),
        in_specs=[SCALARS] + [WHOLE] * 9 + [LEFT] * len(after),
        out_specs=(WHOLE,) * 5,
        scratch_shapes=[pltpu.VMEM((3 * n, n), f32), pltpu.VMEM((2 * KVW + IDS, 3 * n), bf16), pltpu.VMEM((width, n), f32)],
        cost_estimate=BRIEF,
        compiler_params=pltpu.CompilerParams(vmem_limit_bytes=32 << 20),
        name="attend_back",
    )(sc, p, q, *kvs, lse, do, cos, sin, *after)


def down_rows(kind, chip, width):
    return jnp.minimum((kind * 4 + chip) * ROWS, width - ROWS)


def fetch_down(mine, other, wb, wd, sem_d, core, chip):
    rows, width = wb.shape[3], wd.shape[1]
    last = width % ROWS
    for kind, pieces in ((core, mine), (1 - core, other)):
        for who, piece in zip(whose(kind), pieces):
            at = kind * 4 + (chip ^ who)

            @pl.when(at < width // ROWS)
            def _():
                into = wd.at[:, pl.ds(pl.multiple_of(at * ROWS, ROWS), ROWS)]
                pltpu.make_async_copy(piece.at[:, rows:], into, sem_d).start()

            @pl.when(at == width // ROWS)
            def _():
                pltpu.make_async_copy(piece.at[:, rows + ROWS - last :], wd.at[:, width - last :], sem_d).start()


def fetch_both(mine, other, wb, sem_b, core, chip, turns=range(4)):
    rows = wb.shape[3]
    fetch([p.at[:, :rows] for p in mine], [p.at[:, :rows] for p in other], wb, sem_b, core, chip, turns=turns)


def whole(wb, c, m):
    _, rows, n = wb.shape[2:]
    return wb[c, m].reshape(4 * rows, n)


def arrived_down(wd, sem_d):
    pltpu.make_async_copy(wd, wd, sem_d).wait()


def scratch_ffn(width, n):
    return [
        pltpu.VMEM((2, 4, 4, width // 4, n), bf16),
        pltpu.SemaphoreType.DMA((2, 4)),
        pltpu.VMEM((4, width, n), bf16),
        pltpu.SemaphoreType.DMA,
    ]


def post_kernel(last, after, sc, ot_ref, h_ref, gain_ref, gain_a, cos_ref, sin_ref, *rest):
    mine_a, other_a, mine_b, other_b = rest[:4], rest[4:8], rest[8:12], rest[12:16]
    ids_ref, rest = rest[16], rest[17 + after :]
    o_ref, h1_ref, b_ref, gate_ref, up_ref, z_ref, next_ref = rest[:7]
    more, rest = rest[7 : 7 + (0 if last else 3)], rest[7 + (0 if last else 3) :]
    wa, sem_a, wb, sem_b, wd, sem_d = rest
    core, chip = sc[0], sc[1]
    fetch(mine_a, other_a, wa, sem_a, core, chip, 1)
    fetch_both(mine_b, other_b, wb, sem_b, core, chip, (0, 1))
    fetch_down(mine_b, other_b, wb, wd, sem_d, core, chip)
    fetch_both(mine_b, other_b, wb, sem_b, core, chip, (2, 3))
    if not last:
        fetch(mine_a, other_a, wa, sem_a, core, chip, 0)
    o = ot_ref[...].T
    o_ref[...] = o
    for m in range(1, 4):
        arrived(wa, sem_a, 1, m)
    h1 = h_ref[...].astype(f32) + jnp.concatenate([nn(o, wa[1, m, :, :KVW]) for m in range(1, 4)], axis=1)
    h1_ref[...] = h1
    b = normed(h1, gain_ref[...]).astype(bf16)
    b_ref[...] = b
    n = wb.shape[4]
    total = h1
    for i in range(4):
        m = chip ^ i
        cols = pl.ds(pl.multiple_of(m * n, 128), n)
        arrived(wb, sem_b, 0, m)
        gate = nn(b, whole(wb, 0, m))
        arrived(wb, sem_b, 1, m)
        up = nn(b, whole(wb, 1, m))
        gate_ref[:, cols] = gate.astype(bf16)
        up_ref[:, cols] = up.astype(bf16)
        z = (gate / (1.0 + jnp.exp(-gate)) * up).astype(bf16)
        z_ref[:, cols] = z
        if i == 0:
            arrived_down(wd, sem_d)
        total = total + nt(z, wd[m])
    next_ref[...] = total.astype(bf16).T if last else total
    if last:
        arrived(wa, sem_a, 1, 0)
    else:
        project(total, gain_a, cos_ref, sin_ref, ids_ref[2 * KVW :, :], wa, sem_a, *more)


def post(last, after, sc, ot, h, gain, gain_a, cos, sin, kv, wa, wb):
    width, n = ot.shape
    hidden = wb[0][0].shape[2] * 4
    outs = [shape((n, width), bf16), shape((n, width), f32), shape((n, width), bf16)] + [shape((n, hidden), bf16)] * 3
    outs += [shape((width, n), bf16) if last else shape((n, width), f32)]
    if not last:
        outs += [shape((n, width), bf16), shape((width, n), bf16), shape((2 * KVW + IDS, n), bf16)]
    return pl.pallas_call(
        functools.partial(post_kernel, last, len(after)),
        out_shape=tuple(outs),
        in_specs=[SCALARS] + [WHOLE] * 6 + [LEFT] * 16 + [WHOLE] + [LEFT] * len(after),
        out_specs=(WHOLE,) * len(outs),
        scratch_shapes=scratch_a(width) + scratch_ffn(width, hidden // 4),
        cost_estimate=BRIEF,
        compiler_params=pltpu.CompilerParams(vmem_limit_bytes=LIMIT),
        name="post",
    )(sc, ot, h, gain, gain_a, cos, sin, *wa[0], *wa[1], *wb[0], *wb[1], kv, *after)


def ffn_back(state, core, chip, refs, weights):
    gate_ref, up_ref, h1_ref, gain_ref, gb_ref, keep_ref, send_ref, g1_ref, p_ref, dgain_ref, do_ref = refs
    wa, sem_a, wb, sem_b, wd, sem_d = weights
    gb = state.astype(bf16)
    gb_ref[...] = gb
    n = wb.shape[4]
    first = core == 0
    arrived_down(wd, sem_d)
    db = None
    for i in range(4):
        m = chip ^ i
        cols = pl.ds(pl.multiple_of(m * n, 128), n)
        dz = nn(gb, wd[m])
        gate, up = gate_ref[:, cols].astype(f32), up_ref[:, cols].astype(f32)
        sig = 1.0 / (1.0 + jnp.exp(-gate))
        dup = (dz * (gate * sig)).astype(bf16)
        dgate = (dz * up * (sig * (1.0 + gate * (1.0 - sig)))).astype(bf16)
        keep_ref[:, cols] = jnp.where(first, dgate, dup)
        send_ref[:, cols] = jnp.where(first, dup, dgate)
        arrived(wb, sem_b, 0, m)
        part = nt(dgate, whole(wb, 0, m))
        arrived(wb, sem_b, 1, m)
        part = part + nt(dup, whole(wb, 1, m))
        db = part if i == 0 else db + part
    dx, dgain = norm_back(h1_ref[...], gain_ref[...], db)
    dgain_ref[...] = dgain
    g1 = state + dx
    g1_ref[...] = g1
    low = g1.astype(bf16)
    do = None
    for p in range(3):
        part = low[:, p * KVW : (p + 1) * KVW]
        p_ref[p] = widened(part)
        arrived(wa, sem_a, 1, p + 1)
        part = nt(wa[1, p + 1, :, :KVW], part)
        do = part if p == 0 else do + part
    do_ref[...] = do.astype(bf16)


def finish_a(wa, sem_a, *left):
    for at in left:
        arrived(wa, sem_a, *at)


def query_back(dq_ref, wa, sem_a):
    da = None
    for m in range(3):
        arrived(wa, sem_a, 0, m)
        part = nt(dq_ref[m, :, :KVW], wa[0, m, :, :KVW])
        da = part if m == 0 else da + part
    return da


def project_back(da, own_ref, near_ref, far_ref, core, cos_ref, sin_ref, dk_ref, dv_ref, one_ref, h, gain, wa, sem_a):
    cos, sin = cos_ref[...], sin_ref[...]
    grad = own_ref[...] + far_ref[...].astype(f32) + jnp.where(core == 0, near_ref[...].astype(f32), 0.0)
    dk = rope(grad[:KVW], cos, sin, True).T.astype(bf16)
    dv = grad[KVW:].T.astype(bf16)
    dk_ref[...] = widened(dk)
    dv_ref[...] = widened(dv)
    one_ref[...] = widened(jnp.where(core == 0, dv, dk))
    arrived(wa, sem_a, 0, 3)
    arrived(wa, sem_a, 1, 0)
    da = da + nt(dk, wa[0, 3, :, :KVW]) + nt(dv, wa[1, 0, :, :KVW])
    return norm_back(h, gain, da)


def back_kernel(start, end, after, sc, *rest):
    rest = list(rest)

    def take(n):
        out = rest[:n]
        del rest[:n]
        return out

    core, chip = sc[0], sc[1]
    mine_a, other_a = take(4), take(4)
    if not end:
        mine_b, other_b = take(4), take(4)
    if start:
        (g_ref,) = take(1)
    else:
        g1_in, dq_ref, own_ref, near_ref, far_ref, h_ref, gain_a, cos_ref, sin_ref = take(9)
        if end:
            (last_ref,) = take(1)
    if not end:
        ins = take(4)
    take(after)
    if not start:
        dk_ref, dv_ref, one_ref, dgain_a = take(4)
    if end:
        (g_out,) = take(1)
    else:
        outs = take(7)
    wa, sem_a = take(2)
    if not start:
        fetch(mine_a, other_a, wa, sem_a, core, chip, 0)
        fetch(mine_a, other_a, wa, sem_a, core, chip, 1)
    if not end:
        wb, sem_b, wd, sem_d = take(4)
        fetch_down(mine_b, other_b, wb, wd, sem_d, core, chip)
        fetch_both(mine_b, other_b, wb, sem_b, core, chip)
    if start:
        fetch(mine_a, other_a, wa, sem_a, core, chip, 1)
    if start:
        state = g_ref[...].T.astype(f32)
    else:
        da = query_back(dq_ref, wa, sem_a)
        dx, dgain = project_back(da, own_ref, near_ref, far_ref, core, cos_ref, sin_ref, dk_ref, dv_ref, one_ref, h_ref[...].astype(f32), gain_a[...], wa, sem_a)
        dgain_a[...] = dgain
        state = g1_in[...] + dx
    if end:
        width = state.shape[1]
        g_out[:width, :] = last_ref[...]
        g_out[width:, :] = state.astype(bf16).T
        finish_a(wa, sem_a, (1, 1), (1, 2), (1, 3))
    else:
        ffn_back(state, core, chip, (*ins, *outs), (wa, sem_a, wb, sem_b, wd, sem_d))
        if start:
            finish_a(wa, sem_a, (1, 0))


def back(start, end, sc, weights, tail, ffn, after=()):
    wa, wb = weights
    width = wa[0][0].shape[0]
    args = [sc, *wa[0], *wa[1]]
    specs = [SCALARS] + [LEFT] * 8
    scratch = scratch_a(width)
    if not end:
        args += [*wb[0], *wb[1]]
        specs += [LEFT] * 8
        scratch += scratch_ffn(width, wb[0][0].shape[2])
    args += list(tail)
    specs += [WHOLE] * len(tail)
    n = tail[0].shape[1 if start else 0]
    outs = []
    if not end:
        args += list(ffn)
        specs += [WHOLE] * len(ffn)
    if not start:
        outs += [shape((n, PIECE), bf16)] * 3 + [shape((1, width), f32)]
    if end:
        outs += [shape((2 * width, n), bf16)]
    else:
        hidden = ffn[0].shape[1]
        outs += [shape((n, width), bf16), shape((n, hidden), bf16), shape((n, hidden), bf16)]
        outs += [shape((n, width), f32), shape((3, n, PIECE), bf16), shape((1, width), f32), shape((width, n), bf16)]
    args += list(after)
    specs += [LEFT] * len(after)
    return pl.pallas_call(
        functools.partial(back_kernel, start, end, len(after)),
        out_shape=tuple(outs),
        in_specs=specs,
        out_specs=(WHOLE,) * len(outs),
        scratch_shapes=scratch,
        cost_estimate=BRIEF,
        compiler_params=pltpu.CompilerParams(vmem_limit_bytes=LIMIT),
        name="back_end" if end else ("back_start" if start else "back_join"),
    )(*args)


def by_turn(core, chip):
    one = 1 + core
    return chip ^ one, chip ^ 3, chip, chip ^ (3 - one)


def turned(dst, blocks):
    n = blocks[0].shape[0]
    for i, block in enumerate(blocks):
        dst[:, i * n : (i + 1) * n] = block[...].T


def grad_ffn_kernel(sc, *rest):
    lefts, rights = rest[:4], rest[4:8]
    send_ref, keep_ref, left, right = rest[-4:]
    core, chip = sc[0], sc[1]
    n, cols = rights[0].shape[0], right.shape[1]
    turned(left, lefts)
    for i, m in enumerate(by_turn(core, chip)):
        at = pl.multiple_of(m * cols, 128)
        for j, block in enumerate(rights):
            right[j * n : (j + 1) * n, :] = block[:, pl.ds(at, cols)]
        out = send_ref if i < 2 else keep_ref
        out[i % 2] = nn(left[...], right[...]).astype(bf16)


def grad_ffn(sc, lefts, rights, after):
    n, width = lefts[0].shape
    cols = rights[0].shape[1] // 4
    out = shape((2, width, cols), bf16)
    return pl.pallas_call(
        grad_ffn_kernel,
        out_shape=(out, out),
        in_specs=[SCALARS] + [WHOLE] * 8 + [LEFT] * len(after),
        out_specs=(WHOLE,) * 2,
        scratch_shapes=[pltpu.VMEM((width, 4 * n), bf16), pltpu.VMEM((4 * n, cols), bf16)],
        cost_estimate=BRIEF,
        compiler_params=pltpu.CompilerParams(vmem_limit_bytes=LIMIT),
        name="grad_ffn",
    )(sc, *lefts, *rights, *after)


def grad_down_kernel(sc, *rest):
    lefts, rights = rest[:4], rest[4:8]
    send_ref, keep_ref, left, right = rest[-4:]
    n, (_, half, cols) = rights[0].shape[0], send_ref.shape
    turned(left, lefts)
    rows = pl.ds(pl.multiple_of(sc[0] * half, half), half)
    like = sc[2] & 1
    for h in range(2):
        for out, parity in ((send_ref, 1 - like), (keep_ref, like)):
            at = pl.multiple_of((2 * h + parity) * cols, 128)
            for j, block in enumerate(rights):
                right[j * n : (j + 1) * n, :] = block[:, pl.ds(at, cols)]
            out[h] = nn(left[rows, :], right[...]).astype(out.dtype)


def grad_down(sc, lefts, rights, after):
    n, width = lefts[0].shape
    cols = rights[0].shape[1] // 4
    block = (2, width // 2, cols)
    return pl.pallas_call(
        grad_down_kernel,
        out_shape=(shape(block, bf16), shape(block, bf16)),
        in_specs=[SCALARS] + [WHOLE] * 8 + [LEFT] * len(after),
        out_specs=(WHOLE,) * 2,
        scratch_shapes=[pltpu.VMEM((width, 4 * n), bf16), pltpu.VMEM((4 * n, cols), bf16)],
        cost_estimate=BRIEF,
        compiler_params=pltpu.CompilerParams(vmem_limit_bytes=LIMIT),
        name="grad_down",
    )(sc, *lefts, *rights, *after)


def grad_attention_kernel(sc, *rest):
    a_refs, o_refs, rest = rest[:4], rest[4:8], rest[8:]
    queries, keys, values, outs, threes, ones = (rest[i : i + 2] for i in range(0, 12, 2))
    gain_a, gain_f = (rest[i : i + 2] for i in (12, 14))
    *sends, keep_ref, left, right = rest[-5:]
    core, chip = sc[0], sc[1]
    n, width = a_refs[0].shape
    turned(left.at[0], a_refs)
    gains = [g[0][...] + g[1][...] for g in (gain_a, gain_f)]
    gains = jnp.concatenate([*gains, jnp.zeros((6, width), f32)], axis=0).T
    gains = jnp.concatenate([gains, jnp.zeros((width, PIECE - KVW - 8), f32)], axis=1).astype(bf16)

    def fill(at, of_three, own_three, own_one, single):
        for j in range(2):
            for i in range(3):
                right[of_three + i, j * n : (j + 1) * n, :] = own_three[j][i]
                right[of_three + i, (j + 2) * n : (j + 3) * n, :] = threes[j][i]
            right[single, j * n : (j + 1) * n, :] = own_one[j][...]
            right[single, (j + 2) * n : (j + 3) * n, :] = ones[j][...]

    @pl.when(core == 0)
    def _():
        fill(0, 0, queries, keys, 3)

    @pl.when(core == 1)
    def _():
        turned(left.at[1], o_refs)
        fill(0, 1, outs, values, 0)

    for i, m in enumerate(by_turn(core, chip)):
        out = sends[i] if i < 2 else keep_ref.at[i - 2]
        which = jnp.where(m > 0, core, 0)
        out[...] = nn(left[which], right[m]).astype(bf16)
        out[:, KVW:] = gains


def grad_attention(sc, a, o, own, got, gains, after):
    n, width = a[0].shape
    out = shape((width, PIECE), bf16)
    return pl.pallas_call(
        grad_attention_kernel,
        out_shape=(out, out, shape((2, width, PIECE), bf16)),
        in_specs=[SCALARS] + [WHOLE] * 24 + [LEFT] * len(after),
        out_specs=(WHOLE,) * 3,
        scratch_shapes=[pltpu.VMEM((2, width, 4 * n), bf16), pltpu.VMEM((4, 4 * n, PIECE), bf16)],
        cost_estimate=BRIEF,
        compiler_params=pltpu.CompilerParams(vmem_limit_bytes=LIMIT),
        name="grad_attention",
    )(sc, *a, *o, *own, *got, *gains, *after)


def lay_kernel(count, sc, *rest):
    mine, other, outs, kept = rest[:4], rest[4:8], rest[-1 - count : -1], rest[-1]
    core, chip = sc[0], sc[1]
    for kind, pieces in ((core, mine), (1 - core, other)):
        for who, piece in zip(whose(kind), pieces):
            kept[kind, chip ^ who] = piece[...]
    n = sum(o.shape[1] for o in outs[: 4 if len(outs) > 2 else 2]) // 8
    cols = [jnp.concatenate([kept[c, m, :, :n].astype(f32) for m in range(4)], axis=1) for c in range(2)]
    if len(outs) == 2:
        outs[0][...] = cols[0]
        outs[1][...] = cols[1]
    else:
        outs[0][...] = cols[0][:, : 3 * n]
        outs[1][...] = cols[0][:, 3 * n :]
        outs[2][...] = cols[1][:, :n]
        outs[3][...] = cols[1][:, n:]
        gains = kept[0, 0, :, n : n + 8].astype(f32) + kept[1, 0, :, n : n + 8].astype(f32)
        outs[4][...] = gains.T[:2]


def lay(sc, mine, other, widths, after):
    rows, n = mine[0].shape
    outs = tuple(shape((rows, w), f32) for w in widths)
    if len(widths) > 2:
        outs += (shape((2, rows), f32),)
    return pl.pallas_call(
        functools.partial(lay_kernel, len(outs)),
        out_shape=outs,
        in_specs=[SCALARS] + [WHOLE] * 8 + [LEFT] * len(after),
        out_specs=(WHOLE,) * len(outs),
        scratch_shapes=[pltpu.VMEM((2, 4, rows, n), bf16)],
        cost_estimate=BRIEF,
        compiler_params=pltpu.CompilerParams(vmem_limit_bytes=24 << 20),
        name="lay",
    )(sc, *mine, *other, *after)


def pick_first_kernel(sc, q_ref, k_ref, v_ref, o_ref, gain_ref, out_ref):
    rows = out_ref.shape[0]
    which = sc[0] * 4 + sc[1]
    pad = jnp.zeros((6, rows), f32)
    gains = jnp.concatenate([gain_ref[...], pad], axis=0).T.astype(bf16)
    rest = jnp.zeros((rows, PIECE - KVW - 8), bf16)
    for at in range(8):

        @pl.when(which == at)
        def _():
            if at in (3, 4):
                piece = (k_ref if at == 3 else v_ref)[...].T
            else:
                source, m = (q_ref, at) if at < 3 else (o_ref, at - 5)
                piece = source[:, m * KVW : (m + 1) * KVW]
            out_ref[...] = jnp.concatenate([piece, gains, rest], axis=1)


def pick_first(sc, query, key, value, out, gains):
    return pl.pallas_call(
        pick_first_kernel,
        out_shape=shape((query.shape[0], PIECE), bf16),
        in_specs=[SCALARS] + [WHOLE] * 5,
        out_specs=WHOLE,
        cost_estimate=BRIEF,
        compiler_params=pltpu.CompilerParams(vmem_limit_bytes=16 << 20),
        name="pick_first",
    )(sc, query, key, value, out, gains)


def pick_kernel(sc, gate, up, down, *rest):
    out_ref, sems = rest[-2:]
    rows, cols = out_ref.shape[0] - ROWS, out_ref.shape[1]
    into = out_ref.at[:rows]
    start = pl.multiple_of(down_rows(sc[0], sc[1], down.shape[0]), 64)
    copy = pltpu.make_async_copy(down.at[pl.ds(start, ROWS), :], out_ref.at[rows:], sems.at[1])
    copy.start()
    at = pl.ds(pl.multiple_of(sc[1] * cols, 128), cols)
    for c, source in ((0, gate), (1, up)):

        @pl.when(sc[0] == c)
        def _():
            pltpu.make_async_copy(source.at[:, at], into, sems.at[0]).start()

    pltpu.make_async_copy(gate.at[:, at], into, sems.at[0]).wait()
    copy.wait()


def pick(sc, gate, up, down, after):
    return pl.pallas_call(
        pick_kernel,
        out_shape=shape((gate.shape[0] + ROWS, gate.shape[1] // 4), bf16),
        in_specs=[SCALARS] + [LEFT] * (3 + len(after)),
        out_specs=WHOLE,
        scratch_shapes=[pltpu.SemaphoreType.DMA((2,))],
        cost_estimate=BRIEF,
        compiler_params=pltpu.CompilerParams(vmem_limit_bytes=16 << 20),
        name="pick",
    )(sc, gate, up, down, *after)


def gains_kernel(first_ref, out_ref):
    for j in range(4):
        n = first_ref.shape[1]
        out_ref[:, j * n : (j + 1) * n] = first_ref[j, :, KVW : KVW + 8].astype(f32).T[:2]


def gains_of(first):
    return pl.pallas_call(
        gains_kernel,
        out_shape=shape((2, 4 * first.shape[1]), f32),
        in_specs=[WHOLE],
        out_specs=WHOLE,
        cost_estimate=BRIEF,
        compiler_params=pltpu.CompilerParams(vmem_limit_bytes=16 << 20),
        name="gains",
    )(first)


def stack_kernel(sc, *rest):
    parts, out_ref, sems = rest[:4], rest[-2], rest[-1]
    copies = [pltpu.make_async_copy(p, out_ref.at[sc[2] ^ s], sems.at[s]) for s, p in enumerate(parts)]
    for copy in copies:
        copy.start()
    for copy in copies:
        copy.wait()


def stack(sc, parts, after=()):
    return pl.pallas_call(
        stack_kernel,
        out_shape=shape((4,) + parts[0].shape, parts[0].dtype),
        in_specs=[SCALARS] + [LEFT] * (4 + len(after)),
        out_specs=WHOLE,
        scratch_shapes=[pltpu.SemaphoreType.DMA((4,))],
        cost_estimate=BRIEF,
        compiler_params=pltpu.CompilerParams(vmem_limit_bytes=16 << 20),
        name="stack",
    )(sc, *parts, *after)


def small(kernel, sc, args, outs, scratch, after, name):
    return pl.pallas_call(
        kernel,
        out_shape=tuple(outs),
        in_specs=[SCALARS] + [WHOLE] * len(args) + [LEFT] * len(after),
        out_specs=(WHOLE,) * len(outs),
        scratch_shapes=scratch,
        cost_estimate=BRIEF,
        compiler_params=pltpu.CompilerParams(vmem_limit_bytes=32 << 20),
        name=name,
    )(sc, *args, *after)


def sum_first(sc, keep, got, after, parts=1):
    def kernel(sc, keep_ref, *rest):
        own_got, later_got = rest[:2] if len(got) == 2 else (rest[0].at[0], rest[0].at[1])
        own_ref = rest[-1]
        for i, later_ref in enumerate(rest[-1 - parts : -1]):
            n = later_ref.shape[0]
            rows = slice(i * n, (i + 1) * n)
            later_ref[...] = (keep_ref[1, rows].astype(f32) + later_got[rows].astype(f32)).astype(bf16)
        own_ref[...] = keep_ref[0].astype(f32) + own_got[...].astype(f32)

    rows, cols = keep.shape[1:]
    outs = [shape((rows // parts, cols), bf16)] * parts + [shape((rows, cols), f32)]
    return small(kernel, sc, [keep, *got], outs, [], after, "sum_first")


def sum_second(sc, own, got, after):
    def kernel(sc, own_ref, *rest):
        gots, (send_ref, keep_ref, total) = rest[: len(got)], rest[-3:]
        n = total.shape[1]
        for j in range(4):
            part, at = divmod(j * n, gots[0].shape[0])
            total[j] = own_ref[j * n : (j + 1) * n, :] + gots[part][at : at + n, :].astype(f32)
        like = sc[2] & 1
        for h in range(2):
            send_ref[h] = total[2 * h + 1 - like].astype(bf16)
            keep_ref[h] = total[2 * h + like]

    rows, cols = own.shape
    part = (rows // 4, cols)
    outs = [shape((2,) + part, bf16), shape((2,) + part, f32)]
    return small(kernel, sc, [own, *got], outs, [pltpu.VMEM((4,) + part, f32)], after, "sum_second")


def sum_third(sc, keep, got, after):
    def kernel(sc, keep_ref, got_ref, *rest):
        send_ref, own_ref = rest[-2:]
        h = sc[2] >> 1
        send_ref[...] = (keep_ref[1 - h].astype(f32) + got_ref[1 - h].astype(f32)).astype(bf16)
        own_ref[...] = keep_ref[h].astype(f32) + got_ref[h].astype(f32)

    part = keep.shape[1:]
    return small(kernel, sc, [keep, got], [shape(part, bf16), shape(part, f32)], [], after, "sum_third")


def down_split(sc, own, got, after):
    def kernel(sc, own_ref, got_ref, *rest):
        send_ref, kept_ref, total = rest[-3:]
        n = total.shape[1]
        for m in range(4):
            rows = slice(m * n, (m + 1) * n)
            total[m] = own_ref[rows, :] + got_ref[rows, :].astype(f32)
        for i, m in enumerate(by_turn(sc[0], sc[1])):
            out = send_ref if i < 2 else kept_ref
            out[i % 2] = total[m].astype(bf16)

    rows, cols = own.shape
    out = shape((2, rows // 4, cols), bf16)
    return small(kernel, sc, [own, got], [out, out], [pltpu.VMEM((4, rows // 4, cols), f32)], after, "down_split")


def sum_two(sc, own, got, after):
    def kernel(sc, own_ref, got_ref, *rest):
        rest[-1][...] = (own_ref[...] + got_ref[...].astype(f32)).astype(bf16)

    return small(kernel, sc, [own, got], [shape(own.shape, bf16)], [], after, "sum_two")[0]


def lay_down(sc, mine, other, after):
    def kernel(sc, *rest):
        out_ref, total = rest[-2:]
        n = total.shape[2]
        for kind, pieces in ((sc[0], rest[:4]), (1 - sc[0], rest[4:8])):
            for who, piece in zip(whose(kind), pieces):
                total[kind, sc[1] ^ who] = piece[...].astype(f32)
        for c in range(2):
            for m in range(4):
                at = (c * 4 + m) * n
                out_ref[at : at + n, :] = total[c, m]

    n, cols = mine[0].shape
    return small(kernel, sc, [*mine, *other], [shape((8 * n, cols), f32)], [pltpu.VMEM((2, 4, n, cols), f32)], after, "lay_down")[0]


def hold(value, after):
    return pl.pallas_call(
        lambda *refs: None,
        out_shape=shape(value.shape, value.dtype),
        in_specs=[LEFT] * (1 + len(after)),
        out_specs=LEFT,
        input_output_aliases={0: 0},
        cost_estimate=BRIEF,
        compiler_params=pltpu.CompilerParams(vmem_limit_bytes=1 << 20),
        name="hold",
    )(value, *after)


def far_sum(sc, far, near, after):
    def kernel(sc, far_ref, near_ref, *rest):
        rest[-1][...] = (far_ref[...] + jnp.where(sc[0] == 1, near_ref[...].astype(f32), 0.0)).astype(bf16)

    return small(kernel, sc, [far, near], [shape(far.shape, bf16)], [], after, "far_sum")[0]


CORE, SIDE, BACK = 1, 2, 4
rope_base = 10000.0
RUNS = 2


def flip(value, bit, bit1=None):
    count = lax.axis_size("dp")
    bits = (bit, bit if bit1 is None else bit1)
    return lax.ppermute(value, "dp", [(i, i ^ bits[i & 1]) for i in range(count)])


def flip_z(value, bit, where=lambda d, z: True):
    count, depth = lax.axis_size("dp"), lax.axis_size("fsdp")
    pairs = [(d * depth + z, d * depth + (z ^ bit)) for d in range(count) for z in range(depth) if where(d, z)]
    return lax.ppermute(value, ("dp", "fsdp"), pairs)


def home_to_work(value, back=False):
    count, depth = lax.axis_size("dp"), lax.axis_size("fsdp")
    pairs = []
    for d in range(count):
        for z in range(depth):
            there = (d & ~1) | (z & 1), 2 * (d & 1) + (z >> 1)
            pair = (d * depth + z, there[0] * depth + there[1])
            pairs.append(pair[::-1] if back else pair)
    return lax.ppermute(value, ("dp", "fsdp"), pairs)


def place():
    d, z = lax.axis_index("dp"), lax.axis_index("fsdp")
    return d & 1, (d >> 1) & 3, z


def turns(shard):
    far = flip_z(shard, 2)
    return shard, flip_z(shard, 1), far, flip_z(far, 1)


def plane_gather(piece):
    first, second = flip(piece, SIDE, BACK), flip(piece, BACK, SIDE)
    mine = (piece, first, second, flip(first, BACK, SIDE))
    return mine, tuple(flip(p, CORE) for p in mine)


def window(own):
    core, _, _ = place()
    depth = lax.axis_size("fsdp")
    far = lax.ppermute(own, "fsdp", [(z, z + 1) for z in range(0, depth, 2)])
    near = flip(jnp.where(core == 0, own, far), CORE)
    return far, near, own


def unwindow(sc, far, near, after=()):
    depth = lax.axis_size("fsdp")
    near = flip(near, CORE)
    far = far_sum(sc, far, near, after)
    return near, far, lax.ppermute(far, "fsdp", [(z + 1, z) for z in range(0, depth, 2)])


def over_groups(value):
    bit = 8
    while bit < lax.axis_size("dp"):
        value = (value.astype(f32) + flip(value, bit).astype(f32)).astype(bf16)
        bit *= 2
    return value


def spread(piece):
    return piece, flip(piece, SIDE, BACK), flip(piece, BACK, SIDE), flip(piece, SIDE | BACK)


def across(pieces):
    return tuple(flip(p, CORE) for p in pieces)


def body(tokens, segment_ids, attn_gain, query_weight, key_weight, value_weight, out_weight, ffn_gain, gate_weight, up_weight, down_weight, cotangent):
    core, chip, z = place()
    sc = jnp.stack([core, chip, z]).astype(jnp.int32)
    _, stretch, width = tokens.shape
    rows, depth = query_weight.shape[0], lax.axis_size("fsdp")
    block = 2 * (z & 1) + core
    positions = (block * stretch + jnp.arange(stretch)).astype(f32)
    freq = rope_base ** (-2.0 * jnp.arange(HEAD_DIM // 2, dtype=f32) / HEAD_DIM)
    angle = freq[:, None] * positions[None, :]
    cos, sin = jnp.cos(angle), jnp.sin(angle)

    gains = jnp.stack([attn_gain, ffn_gain]).astype(f32)
    parts_a = turns(pick_first(sc, query_weight, key_weight.T, value_weight.T, out_weight, gains))
    ids = jnp.broadcast_to((segment_ids[0] + 1).astype(bf16), (IDS, stretch))
    tokens = home_to_work(jnp.concatenate([tokens[0].T, ids]))
    piece_b = pick(sc, gate_weight, up_weight, down_weight.T, parts_a[1:2])
    whole_a = stack(sc, parts_a, [piece_b])
    gains = gains_of(whole_a)
    gain_a, gain_f = gains[:1], gains[1:]
    wa = plane_gather(whole_a.reshape(depth * rows, PIECE))
    side_b = flip_z(piece_b, 1)
    far_b = hold(flip_z(piece_b, 2), [wa[0][1], wa[0][2], side_b])
    whole_b = stack(sc, (piece_b, side_b, far_b, flip_z(far_b, 1)), [wa[0][3]])
    first_b, second_b = flip(whole_b, SIDE, BACK), flip(whole_b, BACK, SIDE)

    h_0, a0, q0, own = pre(sc, tokens, gain_a, cos, sin, *wa, [whole_b])
    kv0 = window(own)
    first_b = hold(first_b, [kv0[0], second_b])
    opposite_b = flip(first_b, BACK, SIDE)
    o0, lse0 = attend(q0, kv0)
    wb = whole_b, first_b, second_b, hold(opposite_b, [o0])
    wb = wb, across(wb)
    weights = wa, wb
    cot = home_to_work(cotangent[0].T)
    mixed0, h1_0, b0, gate0, up0, z0, h_1, a1, q1, own = post(False, [], sc, o0, h_0, gain_f, gain_a, cos, sin, own, *weights)
    kv1 = window(own)
    across_0 = across((a0, b0, mixed0, z0))
    o1, lse1 = attend(q1, kv1, across_0)
    mixed1, h1_1, b1, gate1, up1, z1, output = post(True, [cot], sc, o1, h_1, gain_f, gain_a, cos, sin, own, *weights)
    across_1 = across((a1, b1, mixed1, z1))

    gb1, act1, away1, g1, p1, dgain_f1, do = back(True, False, sc, weights, [cot], [gate1, up1, h1_1, gain_f])
    across_2 = across((gb1, away1))
    dq1, three1, far, near, own = attend_back(sc, p1, q1, kv1, lse1, do, cos, sin, [*across_1])
    near, _, far = unwindow(sc, far, near)
    (three1,) = across((three1,))
    tail = [g1, dq1, own, near, far, h_1, gain_a, cos, sin]
    dk1, dv1, one1, dgain_a1, gb0, act0, away0, g1, p0, dgain_f0, do = back(False, False, sc, weights, tail, [gate0, up0, h1_0, gain_f], [three1, *across_2])

    away0, gb0_, one1 = across((away0, gb0, one1))
    send_b, keep_b = grad_ffn(sc, [b1, b0, across_1[1], across_0[1]], [act1, act0, across_2[1], away0], [])
    got_b = flip(send_b, SIDE, BACK)
    dq0, three0, far, near, own = attend_back(sc, p0, q0, kv0, lse0, do, cos, sin, [one1, send_b])
    near, down_far, far = unwindow(sc, far, near)
    send_d, keep_d = grad_down(sc, [gb1, gb0, across_2[0], gb0_], [z1, z0, across_1[3], across_0[3]], [down_far])
    got_d = flip_z(send_d, 1)
    (three0,) = across((three0,))
    tail = [g1, dq0, own, near, far, h_0, gain_a, cos, sin, output]
    dk0, dv0, one0, dgain_a0, leaving = back(False, True, sc, weights, tail, None, [send_d])
    later_b, own_b = sum_first(sc, keep_b, [got_b], [one0])
    more_b = flip(later_b, BACK, SIDE)
    own = [dq1, dq0, dk1, dk0, dv1, dv0, p1, p0]
    got = [three1, three0, one1, flip(one0, CORE)]
    *send_a, keep_a = grad_attention(sc, [a1, a0, across_1[0], across_0[0]], [mixed1, mixed0, across_1[2], across_0[2]], own, got, [dgain_a1, dgain_a0, dgain_f1, dgain_f0], [later_b])
    got_a = [flip(v, SIDE, BACK) for v in send_a]
    send_d, keep_d = sum_third(sc, keep_d, got_d, send_a)
    got_d = flip_z(send_d, 2)
    send_b, ring_b = sum_second(sc, own_b, [more_b], [send_d])
    got_b = flip_z(send_b, 1)
    *later_a, own_a = sum_first(sc, keep_a, got_a, [ring_b], 2)
    more_a = [flip(v, BACK, SIDE) for v in later_a]
    send_b, ring_b = sum_third(sc, ring_b, got_b, [own_a])
    got_b = flip_z(send_b, 2)
    send_a, ring_a = sum_second(sc, own_a, more_a, [send_b])
    got_a = flip_z(send_a, 1)
    send_d, keep_d = down_split(sc, keep_d, got_d, [send_a])
    got_d = flip(send_d, SIDE, BACK)
    later_d, own_d = sum_first(sc, keep_d, [got_d], [send_d])
    more_d = flip(later_d, BACK, SIDE)
    piece_b = over_groups(sum_two(sc, ring_b, got_b, [later_d]))
    all_b = spread(piece_b)
    send_a, ring_a = sum_third(sc, ring_a, got_a, [piece_b])
    got_a = flip_z(send_a, 2)
    piece_d = over_groups(sum_two(sc, own_d, more_d, [send_a]))
    all_d = spread(piece_d)
    piece_a = over_groups(sum_two(sc, ring_a, got_a, [piece_d]))
    all_a = spread(piece_a)
    grad_gate, grad_up = lay(sc, all_b, across(all_b), (gate_weight.shape[1],) * 2, [piece_a])
    grad_down_ = lay_down(sc, all_d, across(all_d), [grad_gate])
    grad_query, grad_key, grad_value, grad_out, dgains = lay(sc, all_a, across(all_a), (width, KVW, KVW, width), [grad_down_])
    leaving = home_to_work(hold(leaving, [piece_b]), back=True)
    output, grad_tokens = leaving[:width].T, leaving[width:].astype(f32).T
    return (output[None], grad_tokens[None], dgains[0], grad_query, grad_key, grad_value, grad_out, dgains[1], grad_gate, grad_up, grad_down_.T)


def solution(mesh):
    wide, rows, shard = P("dp", "fsdp", None), P("dp", "fsdp"), P("fsdp", None)
    in_specs = (wide, rows, P("fsdp"), shard, shard, shard, shard, P("fsdp"), shard, shard, shard, wide)
    out_specs = (wide, wide, P("fsdp"), shard, shard, shard, shard, P("fsdp"), shard, shard, shard)
    return jax.shard_map(body, mesh=mesh, in_specs=in_specs, out_specs=out_specs, check_vma=False)
```

```python
import functools
import jax
import jax.numpy as jnp
from jax import lax
from jax.sharding import PartitionSpec as P
from jax.experimental import pallas as pl
from jax.experimental.pallas import tpu as pltpu

f32, bf16 = jnp.float32, jnp.bfloat16
eps = 1e-05
HEADS, KV_HEADS, HEAD_DIM, GROUP, KVW = 15, 5, 64, 3, 320
IDS = 16
ROWS = 128
PIECE = 384
LIMIT = 58 << 20
WHOLE = pl.BlockSpec(memory_space=pltpu.VMEM)
LEFT = pl.BlockSpec(memory_space=pl.ANY)
SCALARS = pl.BlockSpec(memory_space=pltpu.SMEM)
TOKEN = jax.ShapeDtypeStruct((8, 128), f32)
BRIEF = pl.CostEstimate(flops=1024, bytes_accessed=1024, transcendentals=0)


def contract(a, b, i, j):
    return lax.dot_general(a, b, (((i,), (j,)), ((), ())), preferred_element_type=f32)


def nn(a, b):
    return contract(a, b, 1, 0)


def nt(a, b):
    return contract(a, b, 1, 1)


def tn(a, b):
    return contract(a, b, 0, 0)


def whose(core):
    return 0, 1 + core, 2 - core, 3


def fetch(mine, other, kept, sems, core, chip, only=None, turns=range(4)):
    for j in turns:
        for kind, pieces in ((core, mine), (1 - core, other)):
            at = chip ^ whose(kind)[j]

            def copy():
                pltpu.make_async_copy(pieces[j], kept.at[kind, at], sems.at[kind, at]).start()

            if only is None:
                copy()
            else:
                pl.when(kind == only)(copy)


def arrived(kept, sems, *at):
    pltpu.make_async_copy(kept.at[at], kept.at[at], sems.at[at]).wait()


def normed(x, gain):
    return x * lax.rsqrt(jnp.mean(x * x, axis=-1, keepdims=True) + eps) * gain


def norm_back(x, gain, grad):
    r = lax.rsqrt(jnp.mean(x * x, axis=-1, keepdims=True) + eps)
    hat = x * r
    scaled = grad * gain
    dx = r * (scaled - hat * jnp.mean(scaled * hat, axis=-1, keepdims=True))
    return dx, jnp.sum(grad * hat, axis=0, keepdims=True)


def widened(x):
    return jnp.concatenate([x, jnp.zeros((x.shape[0], PIECE - x.shape[1]), x.dtype)], axis=1)


def rope(u, cos, sin, back):
    heads = u.shape[0] // HEAD_DIM
    half = HEAD_DIM // 2
    out = []
    for h in range(heads):
        u1, u2 = u[h * HEAD_DIM : h * HEAD_DIM + half], u[h * HEAD_DIM + half : (h + 1) * HEAD_DIM]
        if back:
            out += [u1 * cos + u2 * sin, u2 * cos - u1 * sin]
        else:
            out += [u1 * cos - u2 * sin, u2 * cos + u1 * sin]
    return jnp.concatenate(out, axis=0)


def project(state, gain_ref, cos_ref, sin_ref, ids, kept, sems, a_ref, q_ref, kv_ref):
    a = normed(state, gain_ref[...]).astype(bf16)
    a_ref[...] = a
    cos, sin = cos_ref[...], sin_ref[...]
    arrived(kept, sems, 0, 3)
    kv_ref[:KVW, :] = rope(nn(a, kept[0, 3, :, :KVW]).T, cos, sin, False).astype(bf16)
    arrived(kept, sems, 1, 0)
    kv_ref[2 * KVW :, :] = ids
    kv_ref[KVW : 2 * KVW, :] = nn(a, kept[1, 0, :, :KVW]).T.astype(bf16)
    for m in range(3):
        arrived(kept, sems, 0, m)
        q_ref[pl.ds(m * KVW, KVW), :] = rope(nn(a, kept[0, m, :, :KVW]).T, cos, sin, False).astype(bf16)


def pre_kernel(sc, ht_ref, gain_ref, cos_ref, sin_ref, *rest):
    width = ht_ref.shape[0] - IDS
    mine, other = rest[:4], rest[4:8]
    h_ref, a_ref, q_ref, kv_ref, kept, sems = rest[-6:]
    core, chip = sc[0], sc[1]
    fetch(mine, other, kept, sems, core, chip)
    h = ht_ref[:width, :].T
    h_ref[...] = h
    project(h.astype(f32), gain_ref, cos_ref, sin_ref, ht_ref[width:, :], kept, sems, a_ref, q_ref, kv_ref)
    for m in range(1, 4):
        arrived(kept, sems, 1, m)


def scratch_a(width):
    return [pltpu.VMEM((2, 4, width, PIECE), bf16), pltpu.SemaphoreType.DMA((2, 4))]


def shape(s, d):
    return jax.ShapeDtypeStruct(s, d)


def pre(sc, ht, gain, cos, sin, mine_a, other_a, after):
    width, n = ht.shape[0] - IDS, ht.shape[1]
    return pl.pallas_call(
        pre_kernel,
        out_shape=(shape((n, width), bf16), shape((n, width), bf16), shape((width, n), bf16), shape((2 * KVW + IDS, n), bf16)),
        in_specs=[SCALARS] + [WHOLE] * 4 + [LEFT] * (8 + len(after)),
        out_specs=(WHOLE,) * 4,
        scratch_shapes=scratch_a(width),
        cost_estimate=BRIEF,
        compiler_params=pltpu.CompilerParams(vmem_limit_bytes=LIMIT),
        name="pre",
    )(sc, ht, gain, cos, sin, *mine_a, *other_a, *after)


def bias_of(kv):
    keys, n = kv.shape[1], kv.shape[1] // 3
    ids = kv[2 * KVW :, :].astype(f32)
    seg_k, seg_q = ids.T[:, :1], ids[:1, 2 * n :]
    j = lax.broadcasted_iota(jnp.int32, (keys, n), 0)
    i = lax.broadcasted_iota(jnp.int32, (keys, n), 1) + (keys - n)
    return jnp.where((seg_k == seg_q) & (j <= i), 0.0, -1e30).astype(f32)


def window_of(parts, whole):
    n = parts[0].shape[1]
    for w, part in enumerate(parts):
        whole[:, w * n : (w + 1) * n] = part[...]


def attend_kernel(q_ref, kv0, kv1, kv2, *rest):
    o_ref, lse_ref, bias, kv = rest[-4:]
    window_of((kv0, kv1, kv2), kv)
    bias[...] = bias_of(kv)

    def head(e, _):
        row = pl.multiple_of(e * HEAD_DIM, HEAD_DIM)
        k = kv[pl.ds(row, HEAD_DIM), :]
        v = kv[pl.ds(row + KVW, HEAD_DIM), :]
        for g in range(GROUP):
            at = pl.multiple_of((e * GROUP + g) * HEAD_DIM, HEAD_DIM)
            q = q_ref[pl.ds(at, HEAD_DIM), :]
            s = tn(k, q) * HEAD_DIM ** (-0.5) + bias[...]
            top = jnp.max(s, axis=0, keepdims=True)
            expo = jnp.exp(s - top)
            total = jnp.sum(expo, axis=0, keepdims=True)
            probs = (expo * (1.0 / total)).astype(bf16)
            o_ref[pl.ds(at, HEAD_DIM), :] = nn(v, probs).astype(bf16)
            lse_ref[pl.ds(e * GROUP + g, 1), :] = top + jnp.log(total)
        return 0

    lax.fori_loop(0, KV_HEADS, head, 0)


def attend(q, kvs, after=()):
    width, n = q.shape
    return pl.pallas_call(
        attend_kernel,
        out_shape=(shape((width, n), bf16), shape((HEADS, n), f32)),
        in_specs=[WHOLE] * 4 + [LEFT] * len(after),
        out_specs=(WHOLE,) * 2,
        scratch_shapes=[pltpu.VMEM((3 * n, n), f32), pltpu.VMEM((2 * KVW + IDS, 3 * n), bf16)],
        cost_estimate=BRIEF,
        compiler_params=pltpu.CompilerParams(vmem_limit_bytes=24 << 20),
        name="attend",
    )(q, *kvs, *after)


def attend_back_kernel(sc, p_ref, q_ref, kv0, kv1, kv2, lse_ref, do_ref, cos_ref, sin_ref, *rest):
    dq_ref, three_ref, far_ref, near_ref, own_ref, bias, kv, dqs = rest[-8:]
    n = q_ref.shape[1]
    window_of((kv0, kv1, kv2), kv)
    bias[...] = bias_of(kv)
    scale = HEAD_DIM ** (-0.5)

    def head(e, _):
        row = pl.multiple_of(e * HEAD_DIM, HEAD_DIM)
        k = kv[pl.ds(row, HEAD_DIM), :]
        v = kv[pl.ds(row + KVW, HEAD_DIM), :]
        dk = dv = None
        for g in range(GROUP):
            at = pl.multiple_of((e * GROUP + g) * HEAD_DIM, HEAD_DIM)
            q = q_ref[pl.ds(at, HEAD_DIM), :]
            do = do_ref[pl.ds(at, HEAD_DIM), :]
            s = tn(k, q) * scale + bias[...]
            probs = jnp.exp(s - lse_ref[pl.ds(e * GROUP + g, 1), :])
            dp = tn(v, do)
            inner = jnp.sum(probs * dp, axis=0, keepdims=True)
            ds = (probs * (dp - inner)).astype(bf16)
            dvg, dkg = nt(do, probs.astype(bf16)), nt(q, ds)
            dv, dk = (dvg, dkg) if g == 0 else (dv + dvg, dk + dkg)
            dqs[pl.ds(at, HEAD_DIM), :] = nn(k, ds)
        for at, grad in ((row, dk * scale), (row + KVW, dv)):
            far_ref[pl.ds(at, HEAD_DIM), :] = grad[:, :n]
            near_ref[pl.ds(at, HEAD_DIM), :] = grad[:, n : 2 * n].astype(bf16)
            own_ref[pl.ds(at, HEAD_DIM), :] = grad[:, 2 * n :]
        return 0

    lax.fori_loop(0, KV_HEADS, head, 0)
    cos, sin = cos_ref[...] * scale, sin_ref[...] * scale
    for m in range(3):
        dq = widened(rope(dqs[m * KVW : (m + 1) * KVW, :], cos, sin, True).T.astype(bf16))
        dq_ref[m] = dq
        three_ref[m] = jnp.where(sc[0] == 0, p_ref[m], dq)


def attend_back(sc, p, q, kvs, lse, do, cos, sin, after=()):
    width, n = q.shape
    block = (2 * KVW, n)
    return pl.pallas_call(
        attend_back_kernel,
        out_shape=(shape((3, n, PIECE), bf16), shape((3, n, PIECE), bf16), shape(block, f32), shape(block, bf16), shape(block, f32)),
        in_specs=[SCALARS] + [WHOLE] * 9 + [LEFT] * len(after),
        out_specs=(WHOLE,) * 5,
        scratch_shapes=[pltpu.VMEM((3 * n, n), f32), pltpu.VMEM((2 * KVW + IDS, 3 * n), bf16), pltpu.VMEM((width, n), f32)],
        cost_estimate=BRIEF,
        compiler_params=pltpu.CompilerParams(vmem_limit_bytes=32 << 20),
        name="attend_back",
    )(sc, p, q, *kvs, lse, do, cos, sin, *after)


def down_rows(kind, chip, width):
    return jnp.minimum((kind * 4 + chip) * ROWS, width - ROWS)


def fetch_down(mine, other, wb, wd, sem_d, core, chip):
    rows, width = wb.shape[3], wd.shape[1]
    last = width % ROWS
    for kind, pieces in ((core, mine), (1 - core, other)):
        for who, piece in zip(whose(kind), pieces):
            at = kind * 4 + (chip ^ who)

            @pl.when(at < width // ROWS)
            def _():
                into = wd.at[:, pl.ds(pl.multiple_of(at * ROWS, ROWS), ROWS)]
                pltpu.make_async_copy(piece.at[:, rows:], into, sem_d).start()

            @pl.when(at == width // ROWS)
            def _():
                pltpu.make_async_copy(piece.at[:, rows + ROWS - last :], wd.at[:, width - last :], sem_d).start()


def fetch_both(mine, other, wb, sem_b, core, chip, turns=range(4)):
    rows = wb.shape[3]
    fetch([p.at[:, :rows] for p in mine], [p.at[:, :rows] for p in other], wb, sem_b, core, chip, turns=turns)


def whole(wb, c, m):
    _, rows, n = wb.shape[2:]
    return wb[c, m].reshape(4 * rows, n)


def arrived_down(wd, sem_d):
    pltpu.make_async_copy(wd, wd, sem_d).wait()


def scratch_ffn(width, n):
    return [
        pltpu.VMEM((2, 4, 4, width // 4, n), bf16),
        pltpu.SemaphoreType.DMA((2, 4)),
        pltpu.VMEM((4, width, n), bf16),
        pltpu.SemaphoreType.DMA,
    ]


def post_kernel(last, after, sc, ot_ref, h_ref, gain_ref, gain_a, cos_ref, sin_ref, *rest):
    mine_a, other_a, mine_b, other_b = rest[:4], rest[4:8], rest[8:12], rest[12:16]
    ids_ref, rest = rest[16], rest[17 + after :]
    o_ref, h1_ref, b_ref, gate_ref, up_ref, z_ref, next_ref = rest[:7]
    more, rest = rest[7 : 7 + (0 if last else 3)], rest[7 + (0 if last else 3) :]
    wa, sem_a, wb, sem_b, wd, sem_d = rest
    core, chip = sc[0], sc[1]
    fetch(mine_a, other_a, wa, sem_a, core, chip, 1)
    fetch_both(mine_b, other_b, wb, sem_b, core, chip, (0, 1))
    fetch_down(mine_b, other_b, wb, wd, sem_d, core, chip)
    fetch_both(mine_b, other_b, wb, sem_b, core, chip, (2, 3))
    if not last:
        fetch(mine_a, other_a, wa, sem_a, core, chip, 0)
    o = ot_ref[...].T
    o_ref[...] = o
    for m in range(1, 4):
        arrived(wa, sem_a, 1, m)
    h1 = h_ref[...].astype(f32) + jnp.concatenate([nn(o, wa[1, m, :, :KVW]) for m in range(1, 4)], axis=1)
    h1_ref[...] = h1
    b = normed(h1, gain_ref[...]).astype(bf16)
    b_ref[...] = b
    n = wb.shape[4]
    total = h1
    for i in range(4):
        m = chip ^ i
        cols = pl.ds(pl.multiple_of(m * n, 128), n)
        arrived(wb, sem_b, 0, m)
        gate = nn(b, whole(wb, 0, m))
        arrived(wb, sem_b, 1, m)
        up = nn(b, whole(wb, 1, m))
        gate_ref[:, cols] = gate.astype(bf16)
        up_ref[:, cols] = up.astype(bf16)
        z = (gate / (1.0 + jnp.exp(-gate)) * up).astype(bf16)
        z_ref[:, cols] = z
        if i == 0:
            arrived_down(wd, sem_d)
        total = total + nt(z, wd[m])
    next_ref[...] = total.astype(bf16).T if last else total
    if last:
        arrived(wa, sem_a, 1, 0)
    else:
        project(total, gain_a, cos_ref, sin_ref, ids_ref[2 * KVW :, :], wa, sem_a, *more)


def post(last, after, sc, ot, h, gain, gain_a, cos, sin, kv, wa, wb):
    width, n = ot.shape
    hidden = wb[0][0].shape[2] * 4
    outs = [shape((n, width), bf16), shape((n, width), f32), shape((n, width), bf16)] + [shape((n, hidden), bf16)] * 3
    outs += [shape((width, n), bf16) if last else shape((n, width), f32)]
    if not last:
        outs += [shape((n, width), bf16), shape((width, n), bf16), shape((2 * KVW + IDS, n), bf16)]
    return pl.pallas_call(
        functools.partial(post_kernel, last, len(after)),
        out_shape=tuple(outs),
        in_specs=[SCALARS] + [WHOLE] * 6 + [LEFT] * 16 + [WHOLE] + [LEFT] * len(after),
        out_specs=(WHOLE,) * len(outs),
        scratch_shapes=scratch_a(width) + scratch_ffn(width, hidden // 4),
        cost_estimate=BRIEF,
        compiler_params=pltpu.CompilerParams(vmem_limit_bytes=LIMIT),
        name="post",
    )(sc, ot, h, gain, gain_a, cos, sin, *wa[0], *wa[1], *wb[0], *wb[1], kv, *after)


def ffn_back(state, core, chip, refs, weights):
    gate_ref, up_ref, h1_ref, gain_ref, gb_ref, keep_ref, send_ref, g1_ref, p_ref, dgain_ref, do_ref = refs
    wa, sem_a, wb, sem_b, wd, sem_d = weights
    gb = state.astype(bf16)
    gb_ref[...] = gb
    n = wb.shape[4]
    first = core == 0
    arrived_down(wd, sem_d)
    db = None
    for i in range(4):
        m = chip ^ i
        cols = pl.ds(pl.multiple_of(m * n, 128), n)
        dz = nn(gb, wd[m])
        gate, up = gate_ref[:, cols].astype(f32), up_ref[:, cols].astype(f32)
        sig = 1.0 / (1.0 + jnp.exp(-gate))
        dup = (dz * (gate * sig)).astype(bf16)
        dgate = (dz * up * (sig * (1.0 + gate * (1.0 - sig)))).astype(bf16)
        keep_ref[:, cols] = jnp.where(first, dgate, dup)
        send_ref[:, cols] = jnp.where(first, dup, dgate)
        arrived(wb, sem_b, 0, m)
        part = nt(dgate, whole(wb, 0, m))
        arrived(wb, sem_b, 1, m)
        part = part + nt(dup, whole(wb, 1, m))
        db = part if i == 0 else db + part
    dx, dgain = norm_back(h1_ref[...], gain_ref[...], db)
    dgain_ref[...] = dgain
    g1 = state + dx
    g1_ref[...] = g1
    low = g1.astype(bf16)
    do = None
    for p in range(3):
        part = low[:, p * KVW : (p + 1) * KVW]
        p_ref[p] = widened(part)
        arrived(wa, sem_a, 1, p + 1)
        part = nt(wa[1, p + 1, :, :KVW], part)
        do = part if p == 0 else do + part
    do_ref[...] = do.astype(bf16)


def finish_a(wa, sem_a, *left):
    for at in left:
        arrived(wa, sem_a, *at)


def query_back(dq_ref, wa, sem_a):
    da = None
    for m in range(3):
        arrived(wa, sem_a, 0, m)
        part = nt(dq_ref[m, :, :KVW], wa[0, m, :, :KVW])
        da = part if m == 0 else da + part
    return da


def project_back(da, own_ref, near_ref, far_ref, core, cos_ref, sin_ref, dk_ref, dv_ref, one_ref, h, gain, wa, sem_a):
    cos, sin = cos_ref[...], sin_ref[...]
    grad = own_ref[...] + far_ref[...].astype(f32) + jnp.where(core == 0, near_ref[...].astype(f32), 0.0)
    dk = rope(grad[:KVW], cos, sin, True).T.astype(bf16)
    dv = grad[KVW:].T.astype(bf16)
    dk_ref[...] = widened(dk)
    dv_ref[...] = widened(dv)
    one_ref[...] = widened(jnp.where(core == 0, dv, dk))
    arrived(wa, sem_a, 0, 3)
    arrived(wa, sem_a, 1, 0)
    da = da + nt(dk, wa[0, 3, :, :KVW]) + nt(dv, wa[1, 0, :, :KVW])
    return norm_back(h, gain, da)


def back_kernel(start, end, after, sc, *rest):
    rest = list(rest)

    def take(n):
        out = rest[:n]
        del rest[:n]
        return out

    core, chip = sc[0], sc[1]
    mine_a, other_a = take(4), take(4)
    if not end:
        mine_b, other_b = take(4), take(4)
    if start:
        (g_ref,) = take(1)
    else:
        g1_in, dq_ref, own_ref, near_ref, far_ref, h_ref, gain_a, cos_ref, sin_ref = take(9)
        if end:
            (last_ref,) = take(1)
    if not end:
        ins = take(4)
    take(after)
    if not start:
        dk_ref, dv_ref, one_ref, dgain_a = take(4)
    if end:
        (g_out,) = take(1)
    else:
        outs = take(7)
    wa, sem_a = take(2)
    if not start:
        fetch(mine_a, other_a, wa, sem_a, core, chip, 0)
        fetch(mine_a, other_a, wa, sem_a, core, chip, 1)
    if not end:
        wb, sem_b, wd, sem_d = take(4)
        fetch_down(mine_b, other_b, wb, wd, sem_d, core, chip)
        fetch_both(mine_b, other_b, wb, sem_b, core, chip)
    if start:
        fetch(mine_a, other_a, wa, sem_a, core, chip, 1)
    if start:
        state = g_ref[...].T.astype(f32)
    else:
        da = query_back(dq_ref, wa, sem_a)
        dx, dgain = project_back(da, own_ref, near_ref, far_ref, core, cos_ref, sin_ref, dk_ref, dv_ref, one_ref, h_ref[...].astype(f32), gain_a[...], wa, sem_a)
        dgain_a[...] = dgain
        state = g1_in[...] + dx
    if end:
        width = state.shape[1]
        g_out[:width, :] = last_ref[...]
        g_out[width:, :] = state.astype(bf16).T
        finish_a(wa, sem_a, (1, 1), (1, 2), (1, 3))
    else:
        ffn_back(state, core, chip, (*ins, *outs), (wa, sem_a, wb, sem_b, wd, sem_d))
        if start:
            finish_a(wa, sem_a, (1, 0))


def back(start, end, sc, weights, tail, ffn, after=()):
    wa, wb = weights
    width = wa[0][0].shape[0]
    args = [sc, *wa[0], *wa[1]]
    specs = [SCALARS] + [LEFT] * 8
    scratch = scratch_a(width)
    if not end:
        args += [*wb[0], *wb[1]]
        specs += [LEFT] * 8
        scratch += scratch_ffn(width, wb[0][0].shape[2])
    args += list(tail)
    specs += [WHOLE] * len(tail)
    n = tail[0].shape[1 if start else 0]
    outs = []
    if not end:
        args += list(ffn)
        specs += [WHOLE] * len(ffn)
    if not start:
        outs += [shape((n, PIECE), bf16)] * 3 + [shape((1, width), f32)]
    if end:
        outs += [shape((2 * width, n), bf16)]
    else:
        hidden = ffn[0].shape[1]
        outs += [shape((n, width), bf16), shape((n, hidden), bf16), shape((n, hidden), bf16)]
        outs += [shape((n, width), f32), shape((3, n, PIECE), bf16), shape((1, width), f32), shape((width, n), bf16)]
    args += list(after)
    specs += [LEFT] * len(after)
    return pl.pallas_call(
        functools.partial(back_kernel, start, end, len(after)),
        out_shape=tuple(outs),
        in_specs=specs,
        out_specs=(WHOLE,) * len(outs),
        scratch_shapes=scratch,
        cost_estimate=BRIEF,
        compiler_params=pltpu.CompilerParams(vmem_limit_bytes=LIMIT),
        name="back_end" if end else ("back_start" if start else "back_join"),
    )(*args)


def by_turn(core, chip):
    one = 1 + core
    return chip ^ one, chip ^ 3, chip, chip ^ (3 - one)


def turned(dst, blocks):
    n = blocks[0].shape[0]
    for i, block in enumerate(blocks):
        dst[:, i * n : (i + 1) * n] = block[...].T


def grad_ffn_kernel(sc, *rest):
    lefts, rights = rest[:4], rest[4:8]
    send_ref, keep_ref, token_ref, left, right = rest[-5:]
    token_ref[...] = jnp.zeros_like(token_ref)
    core, chip = sc[0], sc[1]
    n, cols = rights[0].shape[0], right.shape[1]
    turned(left, lefts)
    for i, m in enumerate(by_turn(core, chip)):
        at = pl.multiple_of(m * cols, 128)
        for j, block in enumerate(rights):
            right[j * n : (j + 1) * n, :] = block[:, pl.ds(at, cols)]
        out = send_ref if i < 2 else keep_ref
        out[i % 2] = nn(left[...], right[...]).astype(bf16)


def grad_ffn(sc, lefts, rights, after):
    n, width = lefts[0].shape
    cols = rights[0].shape[1] // 4
    out = shape((2, width, cols), bf16)
    return pl.pallas_call(
        grad_ffn_kernel,
        out_shape=(out, out, TOKEN),
        in_specs=[SCALARS] + [WHOLE] * 8 + [LEFT] * len(after),
        out_specs=(WHOLE,) * 3,
        scratch_shapes=[pltpu.VMEM((width, 4 * n), bf16), pltpu.VMEM((4 * n, cols), bf16)],
        cost_estimate=BRIEF,
        compiler_params=pltpu.CompilerParams(vmem_limit_bytes=LIMIT),
        name="grad_ffn",
    )(sc, *lefts, *rights, *after)


def grad_down_kernel(sc, *rest):
    lefts, rights = rest[:4], rest[4:8]
    send_ref, keep_ref, token_ref, left, right = rest[-5:]
    token_ref[...] = jnp.zeros_like(token_ref)
    n, (_, half, cols) = rights[0].shape[0], send_ref.shape
    turned(left, lefts)
    rows = pl.ds(pl.multiple_of(sc[0] * half, half), half)
    like = sc[2] & 1
    for h in range(2):
        for out, parity in ((send_ref, 1 - like), (keep_ref, like)):
            at = pl.multiple_of((2 * h + parity) * cols, 128)
            for j, block in enumerate(rights):
                right[j * n : (j + 1) * n, :] = block[:, pl.ds(at, cols)]
            out[h] = nn(left[rows, :], right[...]).astype(out.dtype)


def grad_down(sc, lefts, rights, after):
    n, width = lefts[0].shape
    cols = rights[0].shape[1] // 4
    block = (2, width // 2, cols)
    return pl.pallas_call(
        grad_down_kernel,
        out_shape=(shape(block, bf16), shape(block, bf16), TOKEN),
        in_specs=[SCALARS] + [WHOLE] * 8 + [LEFT] * len(after),
        out_specs=(WHOLE,) * 3,
        scratch_shapes=[pltpu.VMEM((width, 4 * n), bf16), pltpu.VMEM((4 * n, cols), bf16)],
        cost_estimate=BRIEF,
        compiler_params=pltpu.CompilerParams(vmem_limit_bytes=LIMIT),
        name="grad_down",
    )(sc, *lefts, *rights, *after)


def grad_attention_kernel(sc, *rest):
    a_refs, o_refs, rest = rest[:4], rest[4:8], rest[8:]
    queries, keys, values, outs, threes, ones = (rest[i : i + 2] for i in range(0, 12, 2))
    gain_a, gain_f = (rest[i : i + 2] for i in (12, 14))
    *sends, keep_ref, token_ref, left, right = rest[-6:]
    token_ref[...] = jnp.zeros_like(token_ref)
    core, chip = sc[0], sc[1]
    n, width = a_refs[0].shape
    turned(left.at[0], a_refs)
    gains = [g[0][...] + g[1][...] for g in (gain_a, gain_f)]
    gains = jnp.concatenate([*gains, jnp.zeros((6, width), f32)], axis=0).T
    gains = jnp.concatenate([gains, jnp.zeros((width, PIECE - KVW - 8), f32)], axis=1).astype(bf16)

    def fill(at, of_three, own_three, own_one, single):
        for j in range(2):
            for i in range(3):
                right[of_three + i, j * n : (j + 1) * n, :] = own_three[j][i]
                right[of_three + i, (j + 2) * n : (j + 3) * n, :] = threes[j][i]
            right[single, j * n : (j + 1) * n, :] = own_one[j][...]
            right[single, (j + 2) * n : (j + 3) * n, :] = ones[j][...]

    @pl.when(core == 0)
    def _():
        fill(0, 0, queries, keys, 3)

    @pl.when(core == 1)
    def _():
        turned(left.at[1], o_refs)
        fill(0, 1, outs, values, 0)

    for i, m in enumerate(by_turn(core, chip)):
        out = sends[i] if i < 2 else keep_ref.at[i - 2]
        which = jnp.where(m > 0, core, 0)
        out[...] = nn(left[which], right[m]).astype(bf16)
        out[:, KVW:] = gains


def grad_attention(sc, a, o, own, got, gains, after):
    n, width = a[0].shape
    out = shape((width, PIECE), bf16)
    return pl.pallas_call(
        grad_attention_kernel,
        out_shape=(out, out, shape((2, width, PIECE), bf16), TOKEN),
        in_specs=[SCALARS] + [WHOLE] * 24 + [LEFT] * len(after),
        out_specs=(WHOLE,) * 4,
        scratch_shapes=[pltpu.VMEM((2, width, 4 * n), bf16), pltpu.VMEM((4, 4 * n, PIECE), bf16)],
        cost_estimate=BRIEF,
        compiler_params=pltpu.CompilerParams(vmem_limit_bytes=LIMIT),
        name="grad_attention",
    )(sc, *a, *o, *own, *got, *gains, *after)


def lay_kernel(count, sc, *rest):
    mine, other, outs, kept = rest[:4], rest[4:8], rest[-1 - count : -1], rest[-1]
    core, chip = sc[0], sc[1]
    for kind, pieces in ((core, mine), (1 - core, other)):
        for who, piece in zip(whose(kind), pieces):
            kept[kind, chip ^ who] = piece[...]
    n = sum(o.shape[1] for o in outs[: 4 if len(outs) > 2 else 2]) // 8
    cols = [jnp.concatenate([kept[c, m, :, :n].astype(f32) for m in range(4)], axis=1) for c in range(2)]
    if len(outs) == 2:
        outs[0][...] = cols[0]
        outs[1][...] = cols[1]
    else:
        outs[0][...] = cols[0][:, : 3 * n]
        outs[1][...] = cols[0][:, 3 * n :]
        outs[2][...] = cols[1][:, :n]
        outs[3][...] = cols[1][:, n:]
        gains = kept[0, 0, :, n : n + 8].astype(f32) + kept[1, 0, :, n : n + 8].astype(f32)
        outs[4][...] = gains.T[:2]


def lay(sc, mine, other, widths, after):
    rows, n = mine[0].shape
    outs = tuple(shape((rows, w), f32) for w in widths)
    if len(widths) > 2:
        outs += (shape((2, rows), f32),)
    return pl.pallas_call(
        functools.partial(lay_kernel, len(outs)),
        out_shape=outs,
        in_specs=[SCALARS] + [WHOLE] * 8 + [LEFT] * len(after),
        out_specs=(WHOLE,) * len(outs),
        scratch_shapes=[pltpu.VMEM((2, 4, rows, n), bf16)],
        cost_estimate=BRIEF,
        compiler_params=pltpu.CompilerParams(vmem_limit_bytes=24 << 20),
        name="lay",
    )(sc, *mine, *other, *after)


def pick_first_kernel(sc, q_ref, k_ref, v_ref, o_ref, gain_ref, out_ref, wide, tall, sem):
    rows = out_ref.shape[0]
    which = sc[0] * 4 + sc[1]

    def bring(source, into, first, last):
        @pl.when((which >= first) & (which <= last))
        def _():
            copy = pltpu.make_async_copy(source, into, sem)
            copy.start()
            copy.wait()

    bring(q_ref, wide, 0, 2)
    bring(k_ref, tall, 3, 3)
    bring(v_ref, tall, 4, 4)
    bring(o_ref, wide, 5, 7)
    pad = jnp.zeros((6, rows), f32)
    gains = jnp.concatenate([gain_ref[...], pad], axis=0).T.astype(bf16)
    rest = jnp.zeros((rows, PIECE - KVW - 8), bf16)
    for m in range(4):

        @pl.when((which == m) | (which == (m + 5 if m < 3 else 4)))
        def _():
            piece = wide[:, m * KVW : (m + 1) * KVW] if m < 3 else tall[...].T
            out_ref[...] = jnp.concatenate([piece, gains, rest], axis=1)


def pick_first(sc, query, key, value, out, gains):
    return pl.pallas_call(
        pick_first_kernel,
        out_shape=shape((query.shape[0], PIECE), bf16),
        in_specs=[SCALARS] + [LEFT] * 4 + [WHOLE],
        out_specs=WHOLE,
        scratch_shapes=[pltpu.VMEM(query.shape, bf16), pltpu.VMEM(key.shape, bf16), pltpu.SemaphoreType.DMA],
        cost_estimate=BRIEF,
        compiler_params=pltpu.CompilerParams(vmem_limit_bytes=LIMIT),
        name="pick_first",
    )(sc, query, key, value, out, gains)


def pick_kernel(sc, gate, up, down, *rest):
    out_ref, sems = rest[-2:]
    rows, cols = out_ref.shape[0] - ROWS, out_ref.shape[1]
    into = out_ref.at[:rows]
    start = pl.multiple_of(down_rows(sc[0], sc[1], down.shape[0]), 64)
    copy = pltpu.make_async_copy(down.at[pl.ds(start, ROWS), :], out_ref.at[rows:], sems.at[1])
    copy.start()
    at = pl.ds(pl.multiple_of(sc[1] * cols, 128), cols)
    for c, source in ((0, gate), (1, up)):

        @pl.when(sc[0] == c)
        def _():
            pltpu.make_async_copy(source.at[:, at], into, sems.at[0]).start()

    pltpu.make_async_copy(gate.at[:, at], into, sems.at[0]).wait()
    copy.wait()


def pick(sc, gate, up, down, after):
    return pl.pallas_call(
        pick_kernel,
        out_shape=shape((gate.shape[0] + ROWS, gate.shape[1] // 4), bf16),
        in_specs=[SCALARS] + [LEFT] * (3 + len(after)),
        out_specs=WHOLE,
        scratch_shapes=[pltpu.SemaphoreType.DMA((2,))],
        cost_estimate=BRIEF,
        compiler_params=pltpu.CompilerParams(vmem_limit_bytes=16 << 20),
        name="pick",
    )(sc, gate, up, down, *after)


def gains_kernel(first_ref, out_ref):
    for j in range(4):
        n = first_ref.shape[1]
        out_ref[:, j * n : (j + 1) * n] = first_ref[j, :, KVW : KVW + 8].astype(f32).T[:2]


def gains_of(first):
    return pl.pallas_call(
        gains_kernel,
        out_shape=shape((2, 4 * first.shape[1]), f32),
        in_specs=[WHOLE],
        out_specs=WHOLE,
        cost_estimate=BRIEF,
        compiler_params=pltpu.CompilerParams(vmem_limit_bytes=16 << 20),
        name="gains",
    )(first)


def stack_kernel(sc, *rest):
    parts, out_ref, sems = rest[:4], rest[-2], rest[-1]
    copies = [pltpu.make_async_copy(p, out_ref.at[sc[2] ^ s], sems.at[s]) for s, p in enumerate(parts)]
    for copy in copies:
        copy.start()
    for copy in copies:
        copy.wait()


def stack(sc, parts, after=()):
    return pl.pallas_call(
        stack_kernel,
        out_shape=shape((4,) + parts[0].shape, parts[0].dtype),
        in_specs=[SCALARS] + [LEFT] * (4 + len(after)),
        out_specs=WHOLE,
        scratch_shapes=[pltpu.SemaphoreType.DMA((4,))],
        cost_estimate=BRIEF,
        compiler_params=pltpu.CompilerParams(vmem_limit_bytes=16 << 20),
        name="stack",
    )(sc, *parts, *after)


def small(kernel, sc, args, outs, scratch, after, name):
    def with_token(*refs):
        at = len(refs) - len(scratch) - 1
        refs[at][...] = jnp.zeros_like(refs[at])
        kernel(*refs[:at], *refs[at + 1 :])

    return pl.pallas_call(
        with_token,
        out_shape=(*outs, TOKEN),
        in_specs=[SCALARS] + [WHOLE] * len(args) + [LEFT] * len(after),
        out_specs=(WHOLE,) * (len(outs) + 1),
        scratch_shapes=scratch,
        cost_estimate=BRIEF,
        compiler_params=pltpu.CompilerParams(vmem_limit_bytes=32 << 20),
        name=name,
    )(sc, *args, *after)


def sum_first(sc, keep, got, after, parts=1):
    def kernel(sc, keep_ref, *rest):
        own_got, later_got = rest[:2] if len(got) == 2 else (rest[0].at[0], rest[0].at[1])
        own_ref = rest[-1]
        for i, later_ref in enumerate(rest[-1 - parts : -1]):
            n = later_ref.shape[0]
            rows = slice(i * n, (i + 1) * n)
            later_ref[...] = (keep_ref[1, rows].astype(f32) + later_got[rows].astype(f32)).astype(bf16)
        own_ref[...] = keep_ref[0].astype(f32) + own_got[...].astype(f32)

    rows, cols = keep.shape[1:]
    outs = [shape((rows // parts, cols), bf16)] * parts + [shape((rows, cols), f32)]
    return small(kernel, sc, [keep, *got], outs, [], after, "sum_first")


def sum_second(sc, own, got, after):
    def kernel(sc, own_ref, *rest):
        gots, (send_ref, keep_ref, total) = rest[: len(got)], rest[-3:]
        n = total.shape[1]
        for j in range(4):
            part, at = divmod(j * n, gots[0].shape[0])
            total[j] = own_ref[j * n : (j + 1) * n, :] + gots[part][at : at + n, :].astype(f32)
        like = sc[2] & 1
        for h in range(2):
            send_ref[h] = total[2 * h + 1 - like].astype(bf16)
            keep_ref[h] = total[2 * h + like]

    rows, cols = own.shape
    part = (rows // 4, cols)
    outs = [shape((2,) + part, bf16), shape((2,) + part, f32)]
    return small(kernel, sc, [own, *got], outs, [pltpu.VMEM((4,) + part, f32)], after, "sum_second")


def sum_third(sc, keep, got, after):
    def kernel(sc, keep_ref, got_ref, *rest):
        send_ref, own_ref = rest[-2:]
        h = sc[2] >> 1
        send_ref[...] = (keep_ref[1 - h].astype(f32) + got_ref[1 - h].astype(f32)).astype(bf16)
        own_ref[...] = keep_ref[h].astype(f32) + got_ref[h].astype(f32)

    part = keep.shape[1:]
    return small(kernel, sc, [keep, got], [shape(part, bf16), shape(part, f32)], [], after, "sum_third")


def down_split(sc, own, got, after):
    def kernel(sc, own_ref, got_ref, *rest):
        send_ref, kept_ref, total = rest[-3:]
        n = total.shape[1]
        for m in range(4):
            rows = slice(m * n, (m + 1) * n)
            total[m] = own_ref[rows, :] + got_ref[rows, :].astype(f32)
        for i, m in enumerate(by_turn(sc[0], sc[1])):
            out = send_ref if i < 2 else kept_ref
            out[i % 2] = total[m].astype(bf16)

    rows, cols = own.shape
    out = shape((2, rows // 4, cols), bf16)
    return small(kernel, sc, [own, got], [out, out], [pltpu.VMEM((4, rows // 4, cols), f32)], after, "down_split")


def sum_two(sc, own, got, after):
    def kernel(sc, own_ref, got_ref, *rest):
        rest[-1][...] = (own_ref[...] + got_ref[...].astype(f32)).astype(bf16)

    return small(kernel, sc, [own, got], [shape(own.shape, bf16)], [], after, "sum_two")


def lay_down(sc, mine, other, after):
    def kernel(sc, *rest):
        out_ref, total = rest[-2:]
        n = total.shape[2]
        for kind, pieces in ((sc[0], rest[:4]), (1 - sc[0], rest[4:8])):
            for who, piece in zip(whose(kind), pieces):
                total[kind, sc[1] ^ who] = piece[...].astype(f32)
        for c in range(2):
            for m in range(4):
                at = (c * 4 + m) * n
                out_ref[at : at + n, :] = total[c, m]

    n, cols = mine[0].shape
    return small(kernel, sc, [*mine, *other], [shape((8 * n, cols), f32)], [pltpu.VMEM((2, 4, n, cols), f32)], after, "lay_down")[0]


def hold(value, after):
    return pl.pallas_call(
        lambda *refs: None,
        out_shape=shape(value.shape, value.dtype),
        in_specs=[LEFT] * (1 + len(after)),
        out_specs=LEFT,
        input_output_aliases={0: 0},
        cost_estimate=BRIEF,
        compiler_params=pltpu.CompilerParams(vmem_limit_bytes=1 << 20),
        name="hold",
    )(value, *after)


def far_sum(sc, far, near, after):
    def kernel(sc, far_ref, near_ref, *rest):
        rest[-1][...] = (far_ref[...] + jnp.where(sc[0] == 1, near_ref[...].astype(f32), 0.0)).astype(bf16)

    return small(kernel, sc, [far, near], [shape(far.shape, bf16)], [], after, "far_sum")


CORE, SIDE, BACK = 1, 2, 4
rope_base = 10000.0
RUNS = 2


def flip(value, bit, bit1=None):
    count = lax.axis_size("dp")
    bits = (bit, bit if bit1 is None else bit1)
    return lax.ppermute(value, "dp", [(i, i ^ bits[i & 1]) for i in range(count)])


def flip_z(value, bit, where=lambda d, z: True):
    count, depth = lax.axis_size("dp"), lax.axis_size("fsdp")
    pairs = [(d * depth + z, d * depth + (z ^ bit)) for d in range(count) for z in range(depth) if where(d, z)]
    return lax.ppermute(value, ("dp", "fsdp"), pairs)


def home_to_work(value, back=False):
    count, depth = lax.axis_size("dp"), lax.axis_size("fsdp")
    pairs = []
    for d in range(count):
        for z in range(depth):
            there = (d & ~1) | (z & 1), 2 * (d & 1) + (z >> 1)
            pair = (d * depth + z, there[0] * depth + there[1])
            pairs.append(pair[::-1] if back else pair)
    return lax.ppermute(value, ("dp", "fsdp"), pairs)


def place():
    d, z = lax.axis_index("dp"), lax.axis_index("fsdp")
    return d & 1, (d >> 1) & 3, z


def turns(shard):
    far = flip_z(shard, 2)
    return shard, flip_z(shard, 1), far, flip_z(far, 1)


def plane_gather(piece):
    first, second = flip(piece, SIDE, BACK), flip(piece, BACK, SIDE)
    mine = (piece, first, second, flip(first, BACK, SIDE))
    return mine, tuple(flip(p, CORE) for p in mine)


def window(own):
    core, _, _ = place()
    depth = lax.axis_size("fsdp")
    far = lax.ppermute(own, "fsdp", [(z, z + 1) for z in range(0, depth, 2)])
    near = flip(jnp.where(core == 0, own, far), CORE)
    return far, near, own


def unwindow(sc, far, near):
    depth = lax.axis_size("fsdp")
    near = flip(near, CORE)
    far, token = far_sum(sc, far, near, [])
    return near, token, lax.ppermute(far, "fsdp", [(z + 1, z) for z in range(0, depth, 2)])


def over_groups(value):
    bit = 8
    while bit < lax.axis_size("dp"):
        value = (value.astype(f32) + flip(value, bit).astype(f32)).astype(bf16)
        bit *= 2
    return value


def spread(piece):
    return piece, flip(piece, SIDE, BACK), flip(piece, BACK, SIDE), flip(piece, SIDE | BACK)


def across(pieces):
    return tuple(flip(p, CORE) for p in pieces)


def body(tokens, segment_ids, attn_gain, query_weight, key_weight, value_weight, out_weight, ffn_gain, gate_weight, up_weight, down_weight, cotangent):
    core, chip, z = place()
    sc = jnp.stack([core, chip, z]).astype(jnp.int32)
    _, stretch, width = tokens.shape
    rows, depth = query_weight.shape[0], lax.axis_size("fsdp")
    block = 2 * (z & 1) + core
    positions = (block * stretch + jnp.arange(stretch)).astype(f32)
    freq = rope_base ** (-2.0 * jnp.arange(HEAD_DIM // 2, dtype=f32) / HEAD_DIM)
    angle = freq[:, None] * positions[None, :]
    cos, sin = jnp.cos(angle), jnp.sin(angle)

    gains = jnp.stack([attn_gain, ffn_gain]).astype(f32)
    parts_a = turns(pick_first(sc, query_weight, key_weight.T, value_weight.T, out_weight, gains))
    ids = jnp.broadcast_to((segment_ids[0] + 1).astype(bf16), (IDS, stretch))
    tokens = home_to_work(jnp.concatenate([tokens[0].T, ids]))
    piece_b = pick(sc, gate_weight, up_weight, down_weight.T, parts_a[1:2])
    whole_a = stack(sc, parts_a, [piece_b])
    gains = gains_of(whole_a)
    gain_a, gain_f = gains[:1], gains[1:]
    wa = plane_gather(whole_a.reshape(depth * rows, PIECE))
    side_b = flip_z(piece_b, 1)
    far_b = hold(flip_z(piece_b, 2), [wa[0][1], wa[0][2], side_b])
    whole_b = stack(sc, (piece_b, side_b, far_b, flip_z(far_b, 1)), [wa[0][3]])
    first_b, second_b = flip(whole_b, SIDE, BACK), flip(whole_b, BACK, SIDE)

    h_0, a0, q0, own = pre(sc, tokens, gain_a, cos, sin, *wa, [whole_b])
    kv0 = window(own)
    first_b = hold(first_b, [kv0[0], second_b])
    opposite_b = flip(first_b, BACK, SIDE)
    o0, lse0 = attend(q0, kv0)
    wb = whole_b, first_b, second_b, hold(opposite_b, [o0])
    wb = wb, across(wb)
    weights = wa, wb
    cot = home_to_work(cotangent[0].T)
    mixed0, h1_0, b0, gate0, up0, z0, h_1, a1, q1, own = post(False, [], sc, o0, h_0, gain_f, gain_a, cos, sin, own, *weights)
    kv1 = window(own)
    across_0 = across((a0, b0, mixed0, z0))
    o1, lse1 = attend(q1, kv1, across_0)
    mixed1, h1_1, b1, gate1, up1, z1, output = post(True, [cot], sc, o1, h_1, gain_f, gain_a, cos, sin, own, *weights)
    across_1 = across((a1, b1, mixed1, z1))

    gb1, act1, away1, g1, p1, dgain_f1, do = back(True, False, sc, weights, [cot], [gate1, up1, h1_1, gain_f])
    across_2 = across((gb1, away1))
    dq1, three1, far, near, own = attend_back(sc, p1, q1, kv1, lse1, do, cos, sin)
    near, _, far = unwindow(sc, far, near)
    (three1,) = across((three1,))
    tail = [g1, dq1, own, near, far, h_1, gain_a, cos, sin]
    dk1, dv1, one1, dgain_a1, gb0, act0, away0, g1, p0, dgain_f0, do = back(False, False, sc, weights, tail, [gate0, up0, h1_0, gain_f], [three1, *across_2, *across_1])

    away0, gb0_, one1 = across((away0, gb0, one1))
    send_b, keep_b, done = grad_ffn(sc, [b1, b0, across_1[1], across_0[1]], [act1, act0, across_2[1], away0], [])
    got_b = flip(send_b, SIDE, BACK)
    dq0, three0, far, near, own = attend_back(sc, p0, q0, kv0, lse0, do, cos, sin, [one1, done])
    near, done, far = unwindow(sc, far, near)
    send_d, keep_d, done = grad_down(sc, [gb1, gb0, across_2[0], gb0_], [z1, z0, across_1[3], across_0[3]], [done])
    got_d = flip_z(send_d, 1)
    (three0,) = across((three0,))
    tail = [g1, dq0, own, near, far, h_0, gain_a, cos, sin, output]
    dk0, dv0, one0, dgain_a0, leaving = back(False, True, sc, weights, tail, None, [done])
    later_b, own_b, done = sum_first(sc, keep_b, [got_b], [dgain_a0])
    more_b = flip(later_b, BACK, SIDE)
    own = [dq1, dq0, dk1, dk0, dv1, dv0, p1, p0]
    got = [three1, three0, one1, flip(one0, CORE)]
    *send_a, keep_a, done = grad_attention(sc, [a1, a0, across_1[0], across_0[0]], [mixed1, mixed0, across_1[2], across_0[2]], own, got, [dgain_a1, dgain_a0, dgain_f1, dgain_f0], [done])
    got_a = [flip(v, SIDE, BACK) for v in send_a]
    send_d, keep_d, done = sum_third(sc, keep_d, got_d, [done])
    got_d = flip_z(send_d, 2)
    send_b, ring_b, done = sum_second(sc, own_b, [more_b], [done])
    got_b = flip_z(send_b, 1)
    *later_a, own_a, done = sum_first(sc, keep_a, got_a, [done], 2)
    more_a = [flip(v, BACK, SIDE) for v in later_a]
    send_b, ring_b, done = sum_third(sc, ring_b, got_b, [done])
    got_b = flip_z(send_b, 2)
    send_a, ring_a, done = sum_second(sc, own_a, more_a, [done])
    got_a = flip_z(send_a, 1)
    send_d, keep_d, done = down_split(sc, keep_d, got_d, [done])
    got_d = flip(send_d, SIDE, BACK)
    later_d, own_d, done = sum_first(sc, keep_d, [got_d], [done])
    more_d = flip(later_d, BACK, SIDE)
    piece_b, done = sum_two(sc, ring_b, got_b, [done])
    all_b = spread(over_groups(piece_b))
    send_a, ring_a, first = sum_third(sc, ring_a, got_a, [done])
    got_a = flip_z(send_a, 2)
    piece_d, done = sum_two(sc, own_d, more_d, [first])
    all_d = spread(over_groups(piece_d))
    piece_a, done = sum_two(sc, ring_a, got_a, [done])
    all_a = spread(over_groups(piece_a))
    grad_gate, grad_up = lay(sc, all_b, across(all_b), (gate_weight.shape[1],) * 2, [done])
    grad_down_ = lay_down(sc, all_d, across(all_d), [done])
    grad_query, grad_key, grad_value, grad_out, dgains = lay(sc, all_a, across(all_a), (width, KVW, KVW, width), [done])
    leaving = home_to_work(hold(leaving, [first]), back=True)
    output, grad_tokens = leaving[:width].T, leaving[width:].astype(f32).T
    return (output[None], grad_tokens[None], dgains[0], grad_query, grad_key, grad_value, grad_out, dgains[1], grad_gate, grad_up, grad_down_.T)


def solution(mesh):
    wide, rows, shard = P("dp", "fsdp", None), P("dp", "fsdp"), P("fsdp", None)
    in_specs = (wide, rows, P("fsdp"), shard, shard, shard, shard, P("fsdp"), shard, shard, shard, wide)
    out_specs = (wide, wide, P("fsdp"), shard, shard, shard, shard, P("fsdp"), shard, shard, shard)
    return jax.shard_map(body, mesh=mesh, in_specs=in_specs, out_specs=out_specs, check_vma=False)
```

```python
import functools
import jax
import jax.numpy as jnp
from jax import lax
from jax.sharding import PartitionSpec as P
from jax.experimental import pallas as pl
from jax.experimental.pallas import tpu as pltpu

f32, bf16 = jnp.float32, jnp.bfloat16
eps = 1e-05
HEADS, KV_HEADS, HEAD_DIM, GROUP, KVW = 15, 5, 64, 3, 320
IDS = 16
ROWS = 128
PIECE = 384
LIMIT = 58 << 20
WHOLE = pl.BlockSpec(memory_space=pltpu.VMEM)
LEFT = pl.BlockSpec(memory_space=pl.ANY)
SCALARS = pl.BlockSpec(memory_space=pltpu.SMEM)
TOKEN = jax.ShapeDtypeStruct((8, 128), f32)
BRIEF = pl.CostEstimate(flops=1024, bytes_accessed=1024, transcendentals=0)


def contract(a, b, i, j):
    return lax.dot_general(a, b, (((i,), (j,)), ((), ())), preferred_element_type=f32)


def nn(a, b):
    return contract(a, b, 1, 0)


def nt(a, b):
    return contract(a, b, 1, 1)


def tn(a, b):
    return contract(a, b, 0, 0)


def whose(core):
    return 0, 1 + core, 2 - core, 3


def fetch(mine, other, kept, sems, core, chip, only=None, turns=range(4)):
    for j in turns:
        for kind, pieces in ((core, mine), (1 - core, other)):
            at = chip ^ whose(kind)[j]

            def copy():
                pltpu.make_async_copy(pieces[j], kept.at[kind, at], sems.at[kind, at]).start()

            if only is None:
                copy()
            else:
                pl.when(kind == only)(copy)


def arrived(kept, sems, *at):
    pltpu.make_async_copy(kept.at[at], kept.at[at], sems.at[at]).wait()


def normed(x, gain):
    return x * lax.rsqrt(jnp.mean(x * x, axis=-1, keepdims=True) + eps) * gain


def norm_back(x, gain, grad):
    r = lax.rsqrt(jnp.mean(x * x, axis=-1, keepdims=True) + eps)
    hat = x * r
    scaled = grad * gain
    dx = r * (scaled - hat * jnp.mean(scaled * hat, axis=-1, keepdims=True))
    return dx, jnp.sum(grad * hat, axis=0, keepdims=True)


def widened(x):
    return jnp.concatenate([x, jnp.zeros((x.shape[0], PIECE - x.shape[1]), x.dtype)], axis=1)


def rope(u, cos, sin, back):
    heads = u.shape[0] // HEAD_DIM
    half = HEAD_DIM // 2
    out = []
    for h in range(heads):
        u1, u2 = u[h * HEAD_DIM : h * HEAD_DIM + half], u[h * HEAD_DIM + half : (h + 1) * HEAD_DIM]
        if back:
            out += [u1 * cos + u2 * sin, u2 * cos - u1 * sin]
        else:
            out += [u1 * cos - u2 * sin, u2 * cos + u1 * sin]
    return jnp.concatenate(out, axis=0)


def project(state, gain_ref, cos_ref, sin_ref, ids, kept, sems, a_ref, q_ref, kv_ref):
    a = normed(state, gain_ref[...]).astype(bf16)
    a_ref[...] = a
    cos, sin = cos_ref[...], sin_ref[...]
    arrived(kept, sems, 0, 3)
    kv_ref[:KVW, :] = rope(nn(a, kept[0, 3, :, :KVW]).T, cos, sin, False).astype(bf16)
    arrived(kept, sems, 1, 0)
    kv_ref[2 * KVW :, :] = ids
    kv_ref[KVW : 2 * KVW, :] = nn(a, kept[1, 0, :, :KVW]).T.astype(bf16)
    for m in range(3):
        arrived(kept, sems, 0, m)
        q_ref[pl.ds(m * KVW, KVW), :] = rope(nn(a, kept[0, m, :, :KVW]).T, cos, sin, False).astype(bf16)


def pre_kernel(sc, ht_ref, gain_ref, cos_ref, sin_ref, *rest):
    width = ht_ref.shape[0] - IDS
    mine, other = rest[:4], rest[4:8]
    h_ref, a_ref, q_ref, kv_ref, kept, sems = rest[-6:]
    core, chip = sc[0], sc[1]
    fetch(mine, other, kept, sems, core, chip)
    h = ht_ref[:width, :].T
    h_ref[...] = h
    project(h.astype(f32), gain_ref, cos_ref, sin_ref, ht_ref[width:, :], kept, sems, a_ref, q_ref, kv_ref)
    for m in range(1, 4):
        arrived(kept, sems, 1, m)


def scratch_a(width):
    return [pltpu.VMEM((2, 4, width, PIECE), bf16), pltpu.SemaphoreType.DMA((2, 4))]


def shape(s, d):
    return jax.ShapeDtypeStruct(s, d)


def pre(sc, ht, gain, cos, sin, mine_a, other_a, after):
    width, n = ht.shape[0] - IDS, ht.shape[1]
    return pl.pallas_call(
        pre_kernel,
        out_shape=(shape((n, width), bf16), shape((n, width), bf16), shape((width, n), bf16), shape((2 * KVW + IDS, n), bf16)),
        in_specs=[SCALARS] + [WHOLE] * 4 + [LEFT] * (8 + len(after)),
        out_specs=(WHOLE,) * 4,
        scratch_shapes=scratch_a(width),
        cost_estimate=BRIEF,
        compiler_params=pltpu.CompilerParams(vmem_limit_bytes=LIMIT),
        name="pre",
    )(sc, ht, gain, cos, sin, *mine_a, *other_a, *after)


def bias_of(kv):
    keys, n = kv.shape[1], kv.shape[1] // 3
    ids = kv[2 * KVW :, :].astype(f32)
    seg_k, seg_q = ids.T[:, :1], ids[:1, 2 * n :]
    j = lax.broadcasted_iota(jnp.int32, (keys, n), 0)
    i = lax.broadcasted_iota(jnp.int32, (keys, n), 1) + (keys - n)
    return jnp.where((seg_k == seg_q) & (j <= i), 0.0, -1e30).astype(f32)


def window_of(parts, whole):
    n = parts[0].shape[1]
    for w, part in enumerate(parts):
        whole[:, w * n : (w + 1) * n] = part[...]


def attend_kernel(q_ref, kv0, kv1, kv2, *rest):
    o_ref, lse_ref, bias, kv = rest[-4:]
    window_of((kv0, kv1, kv2), kv)
    bias[...] = bias_of(kv)

    def head(e, _):
        row = pl.multiple_of(e * HEAD_DIM, HEAD_DIM)
        k = kv[pl.ds(row, HEAD_DIM), :]
        v = kv[pl.ds(row + KVW, HEAD_DIM), :]
        for g in range(GROUP):
            at = pl.multiple_of((e * GROUP + g) * HEAD_DIM, HEAD_DIM)
            q = q_ref[pl.ds(at, HEAD_DIM), :]
            s = tn(k, q) * HEAD_DIM ** (-0.5) + bias[...]
            top = jnp.max(s, axis=0, keepdims=True)
            expo = jnp.exp(s - top)
            total = jnp.sum(expo, axis=0, keepdims=True)
            probs = (expo * (1.0 / total)).astype(bf16)
            o_ref[pl.ds(at, HEAD_DIM), :] = nn(v, probs).astype(bf16)
            lse_ref[pl.ds(e * GROUP + g, 1), :] = top + jnp.log(total)
        return 0

    lax.fori_loop(0, KV_HEADS, head, 0)


def attend(q, kvs, after=()):
    width, n = q.shape
    return pl.pallas_call(
        attend_kernel,
        out_shape=(shape((width, n), bf16), shape((HEADS, n), f32)),
        in_specs=[WHOLE] * 4 + [LEFT] * len(after),
        out_specs=(WHOLE,) * 2,
        scratch_shapes=[pltpu.VMEM((3 * n, n), f32), pltpu.VMEM((2 * KVW + IDS, 3 * n), bf16)],
        cost_estimate=BRIEF,
        compiler_params=pltpu.CompilerParams(vmem_limit_bytes=24 << 20),
        name="attend",
    )(q, *kvs, *after)


def attend_back_kernel(sc, p_ref, q_ref, kv0, kv1, kv2, lse_ref, do_ref, cos_ref, sin_ref, *rest):
    dq_ref, three_ref, far_ref, near_ref, own_ref, bias, kv, dqs = rest[-8:]
    n = q_ref.shape[1]
    window_of((kv0, kv1, kv2), kv)
    bias[...] = bias_of(kv)
    scale = HEAD_DIM ** (-0.5)

    def head(e, _):
        row = pl.multiple_of(e * HEAD_DIM, HEAD_DIM)
        k = kv[pl.ds(row, HEAD_DIM), :]
        v = kv[pl.ds(row + KVW, HEAD_DIM), :]
        dk = dv = None
        for g in range(GROUP):
            at = pl.multiple_of((e * GROUP + g) * HEAD_DIM, HEAD_DIM)
            q = q_ref[pl.ds(at, HEAD_DIM), :]
            do = do_ref[pl.ds(at, HEAD_DIM), :]
            s = tn(k, q) * scale + bias[...]
            probs = jnp.exp(s - lse_ref[pl.ds(e * GROUP + g, 1), :])
            dp = tn(v, do)
            inner = jnp.sum(probs * dp, axis=0, keepdims=True)
            ds = (probs * (dp - inner)).astype(bf16)
            dvg, dkg = nt(do, probs.astype(bf16)), nt(q, ds)
            dv, dk = (dvg, dkg) if g == 0 else (dv + dvg, dk + dkg)
            dqs[pl.ds(at, HEAD_DIM), :] = nn(k, ds)
        for at, grad in ((row, dk * scale), (row + KVW, dv)):
            far_ref[pl.ds(at, HEAD_DIM), :] = grad[:, :n]
            near_ref[pl.ds(at, HEAD_DIM), :] = grad[:, n : 2 * n].astype(bf16)
            own_ref[pl.ds(at, HEAD_DIM), :] = grad[:, 2 * n :]
        return 0

    lax.fori_loop(0, KV_HEADS, head, 0)
    cos, sin = cos_ref[...] * scale, sin_ref[...] * scale
    for m in range(3):
        dq = widened(rope(dqs[m * KVW : (m + 1) * KVW, :], cos, sin, True).T.astype(bf16))
        dq_ref[m] = dq
        three_ref[m] = jnp.where(sc[0] == 0, p_ref[m], dq)


def attend_back(sc, p, q, kvs, lse, do, cos, sin, after=()):
    width, n = q.shape
    block = (2 * KVW, n)
    return pl.pallas_call(
        attend_back_kernel,
        out_shape=(shape((3, n, PIECE), bf16), shape((3, n, PIECE), bf16), shape(block, f32), shape(block, bf16), shape(block, f32)),
        in_specs=[SCALARS] + [WHOLE] * 9 + [LEFT] * len(after),
        out_specs=(WHOLE,) * 5,
        scratch_shapes=[pltpu.VMEM((3 * n, n), f32), pltpu.VMEM((2 * KVW + IDS, 3 * n), bf16), pltpu.VMEM((width, n), f32)],
        cost_estimate=BRIEF,
        compiler_params=pltpu.CompilerParams(vmem_limit_bytes=32 << 20),
        name="attend_back",
    )(sc, p, q, *kvs, lse, do, cos, sin, *after)


def down_rows(kind, chip, width):
    return jnp.minimum((kind * 4 + chip) * ROWS, width - ROWS)


def fetch_down(mine, other, wb, wd, sem_d, core, chip):
    rows, width = wb.shape[3], wd.shape[1]
    last = width % ROWS
    for kind, pieces in ((core, mine), (1 - core, other)):
        for who, piece in zip(whose(kind), pieces):
            at = kind * 4 + (chip ^ who)

            @pl.when(at < width // ROWS)
            def _():
                into = wd.at[:, pl.ds(pl.multiple_of(at * ROWS, ROWS), ROWS)]
                pltpu.make_async_copy(piece.at[:, rows:], into, sem_d).start()

            @pl.when(at == width // ROWS)
            def _():
                pltpu.make_async_copy(piece.at[:, rows + ROWS - last :], wd.at[:, width - last :], sem_d).start()


def fetch_both(mine, other, wb, sem_b, core, chip, turns=range(4)):
    rows = wb.shape[3]
    fetch([p.at[:, :rows] for p in mine], [p.at[:, :rows] for p in other], wb, sem_b, core, chip, turns=turns)


def whole(wb, c, m):
    _, rows, n = wb.shape[2:]
    return wb[c, m].reshape(4 * rows, n)


def arrived_down(wd, sem_d):
    pltpu.make_async_copy(wd, wd, sem_d).wait()


def scratch_ffn(width, n):
    return [
        pltpu.VMEM((2, 4, 4, width // 4, n), bf16),
        pltpu.SemaphoreType.DMA((2, 4)),
        pltpu.VMEM((4, width, n), bf16),
        pltpu.SemaphoreType.DMA,
    ]


def post_kernel(last, after, sc, ot_ref, h_ref, gain_ref, gain_a, cos_ref, sin_ref, *rest):
    mine_a, other_a, mine_b, other_b = rest[:4], rest[4:8], rest[8:12], rest[12:16]
    ids_ref, rest = rest[16], rest[17 + after :]
    o_ref, h1_ref, b_ref, gate_ref, up_ref, z_ref, next_ref = rest[:7]
    more, rest = rest[7 : 7 + (0 if last else 3)], rest[7 + (0 if last else 3) :]
    wa, sem_a, wb, sem_b, wd, sem_d = rest
    core, chip = sc[0], sc[1]
    fetch(mine_a, other_a, wa, sem_a, core, chip, 1)
    fetch_both(mine_b, other_b, wb, sem_b, core, chip, (0, 1))
    fetch_down(mine_b, other_b, wb, wd, sem_d, core, chip)
    fetch_both(mine_b, other_b, wb, sem_b, core, chip, (2, 3))
    if not last:
        fetch(mine_a, other_a, wa, sem_a, core, chip, 0)
    o = ot_ref[...].T
    o_ref[...] = o
    for m in range(1, 4):
        arrived(wa, sem_a, 1, m)
    h1 = h_ref[...].astype(f32) + jnp.concatenate([nn(o, wa[1, m, :, :KVW]) for m in range(1, 4)], axis=1)
    h1_ref[...] = h1
    b = normed(h1, gain_ref[...]).astype(bf16)
    b_ref[...] = b
    n = wb.shape[4]
    total = h1
    for i in range(4):
        m = chip ^ i
        cols = pl.ds(pl.multiple_of(m * n, 128), n)
        arrived(wb, sem_b, 0, m)
        gate = nn(b, whole(wb, 0, m))
        arrived(wb, sem_b, 1, m)
        up = nn(b, whole(wb, 1, m))
        gate_ref[:, cols] = gate.astype(bf16)
        up_ref[:, cols] = up.astype(bf16)
        z = (gate / (1.0 + jnp.exp(-gate)) * up).astype(bf16)
        z_ref[:, cols] = z
        if i == 0:
            arrived_down(wd, sem_d)
        total = total + nt(z, wd[m])
    next_ref[...] = total.astype(bf16).T if last else total
    if last:
        arrived(wa, sem_a, 1, 0)
    else:
        project(total, gain_a, cos_ref, sin_ref, ids_ref[2 * KVW :, :], wa, sem_a, *more)


def post(last, after, sc, ot, h, gain, gain_a, cos, sin, kv, wa, wb):
    width, n = ot.shape
    hidden = wb[0][0].shape[2] * 4
    outs = [shape((n, width), bf16), shape((n, width), f32), shape((n, width), bf16)] + [shape((n, hidden), bf16)] * 3
    outs += [shape((width, n), bf16) if last else shape((n, width), f32)]
    if not last:
        outs += [shape((n, width), bf16), shape((width, n), bf16), shape((2 * KVW + IDS, n), bf16)]
    return pl.pallas_call(
        functools.partial(post_kernel, last, len(after)),
        out_shape=tuple(outs),
        in_specs=[SCALARS] + [WHOLE] * 6 + [LEFT] * 16 + [WHOLE] + [LEFT] * len(after),
        out_specs=(WHOLE,) * len(outs),
        scratch_shapes=scratch_a(width) + scratch_ffn(width, hidden // 4),
        cost_estimate=BRIEF,
        compiler_params=pltpu.CompilerParams(vmem_limit_bytes=LIMIT),
        name="post",
    )(sc, ot, h, gain, gain_a, cos, sin, *wa[0], *wa[1], *wb[0], *wb[1], kv, *after)


def ffn_back(state, core, chip, refs, weights):
    gate_ref, up_ref, h1_ref, gain_ref, gb_ref, keep_ref, send_ref, g1_ref, p_ref, dgain_ref, do_ref = refs
    wa, sem_a, wb, sem_b, wd, sem_d = weights
    gb = state.astype(bf16)
    gb_ref[...] = gb
    n = wb.shape[4]
    first = core == 0
    arrived_down(wd, sem_d)
    db = None
    for i in range(4):
        m = chip ^ i
        cols = pl.ds(pl.multiple_of(m * n, 128), n)
        dz = nn(gb, wd[m])
        gate, up = gate_ref[:, cols].astype(f32), up_ref[:, cols].astype(f32)
        sig = 1.0 / (1.0 + jnp.exp(-gate))
        dup = (dz * (gate * sig)).astype(bf16)
        dgate = (dz * up * (sig * (1.0 + gate * (1.0 - sig)))).astype(bf16)
        keep_ref[:, cols] = jnp.where(first, dgate, dup)
        send_ref[:, cols] = jnp.where(first, dup, dgate)
        arrived(wb, sem_b, 0, m)
        part = nt(dgate, whole(wb, 0, m))
        arrived(wb, sem_b, 1, m)
        part = part + nt(dup, whole(wb, 1, m))
        db = part if i == 0 else db + part
    dx, dgain = norm_back(h1_ref[...], gain_ref[...], db)
    dgain_ref[...] = dgain
    g1 = state + dx
    g1_ref[...] = g1
    low = g1.astype(bf16)
    do = None
    for p in range(3):
        part = low[:, p * KVW : (p + 1) * KVW]
        p_ref[p] = widened(part)
        arrived(wa, sem_a, 1, p + 1)
        part = nt(wa[1, p + 1, :, :KVW], part)
        do = part if p == 0 else do + part
    do_ref[...] = do.astype(bf16)


def finish_a(wa, sem_a, *left):
    for at in left:
        arrived(wa, sem_a, *at)


def query_back(dq_ref, wa, sem_a):
    da = None
    for m in range(3):
        arrived(wa, sem_a, 0, m)
        part = nt(dq_ref[m, :, :KVW], wa[0, m, :, :KVW])
        da = part if m == 0 else da + part
    return da


def project_back(da, own_ref, near_ref, far_ref, core, cos_ref, sin_ref, dk_ref, dv_ref, one_ref, h, gain, wa, sem_a):
    cos, sin = cos_ref[...], sin_ref[...]
    grad = own_ref[...] + far_ref[...].astype(f32) + jnp.where(core == 0, near_ref[...].astype(f32), 0.0)
    dk = rope(grad[:KVW], cos, sin, True).T.astype(bf16)
    dv = grad[KVW:].T.astype(bf16)
    dk_ref[...] = widened(dk)
    dv_ref[...] = widened(dv)
    one_ref[...] = widened(jnp.where(core == 0, dv, dk))
    arrived(wa, sem_a, 0, 3)
    arrived(wa, sem_a, 1, 0)
    da = da + nt(dk, wa[0, 3, :, :KVW]) + nt(dv, wa[1, 0, :, :KVW])
    return norm_back(h, gain, da)


def back_kernel(start, end, after, sc, *rest):
    rest = list(rest)

    def take(n):
        out = rest[:n]
        del rest[:n]
        return out

    core, chip = sc[0], sc[1]
    mine_a, other_a = take(4), take(4)
    if not end:
        mine_b, other_b = take(4), take(4)
    if start:
        (g_ref,) = take(1)
    else:
        g1_in, dq_ref, own_ref, near_ref, far_ref, h_ref, gain_a, cos_ref, sin_ref = take(9)
        if end:
            (last_ref,) = take(1)
    if not end:
        ins = take(4)
    take(after)
    if not start:
        dk_ref, dv_ref, one_ref, dgain_a = take(4)
    if end:
        (g_out,) = take(1)
    else:
        outs = take(7)
    wa, sem_a = take(2)
    if not start:
        fetch(mine_a, other_a, wa, sem_a, core, chip, 0)
        fetch(mine_a, other_a, wa, sem_a, core, chip, 1)
    if not end:
        wb, sem_b, wd, sem_d = take(4)
        fetch_down(mine_b, other_b, wb, wd, sem_d, core, chip)
        fetch_both(mine_b, other_b, wb, sem_b, core, chip)
    if start:
        fetch(mine_a, other_a, wa, sem_a, core, chip, 1)
    if start:
        state = g_ref[...].T.astype(f32)
    else:
        da = query_back(dq_ref, wa, sem_a)
        dx, dgain = project_back(da, own_ref, near_ref, far_ref, core, cos_ref, sin_ref, dk_ref, dv_ref, one_ref, h_ref[...].astype(f32), gain_a[...], wa, sem_a)
        dgain_a[...] = dgain
        state = g1_in[...] + dx
    if end:
        width = state.shape[1]
        g_out[:width, :] = last_ref[...]
        g_out[width:, :] = state.astype(bf16).T
        finish_a(wa, sem_a, (1, 1), (1, 2), (1, 3))
    else:
        ffn_back(state, core, chip, (*ins, *outs), (wa, sem_a, wb, sem_b, wd, sem_d))
        if start:
            finish_a(wa, sem_a, (1, 0))


def back(start, end, sc, weights, tail, ffn, after=()):
    wa, wb = weights
    width = wa[0][0].shape[0]
    args = [sc, *wa[0], *wa[1]]
    specs = [SCALARS] + [LEFT] * 8
    scratch = scratch_a(width)
    if not end:
        args += [*wb[0], *wb[1]]
        specs += [LEFT] * 8
        scratch += scratch_ffn(width, wb[0][0].shape[2])
    args += list(tail)
    specs += [WHOLE] * len(tail)
    n = tail[0].shape[1 if start else 0]
    outs = []
    if not end:
        args += list(ffn)
        specs += [WHOLE] * len(ffn)
    if not start:
        outs += [shape((n, PIECE), bf16)] * 3 + [shape((1, width), f32)]
    if end:
        outs += [shape((2 * width, n), bf16)]
    else:
        hidden = ffn[0].shape[1]
        outs += [shape((n, width), bf16), shape((n, hidden), bf16), shape((n, hidden), bf16)]
        outs += [shape((n, width), f32), shape((3, n, PIECE), bf16), shape((1, width), f32), shape((width, n), bf16)]
    args += list(after)
    specs += [LEFT] * len(after)
    return pl.pallas_call(
        functools.partial(back_kernel, start, end, len(after)),
        out_shape=tuple(outs),
        in_specs=specs,
        out_specs=(WHOLE,) * len(outs),
        scratch_shapes=scratch,
        cost_estimate=BRIEF,
        compiler_params=pltpu.CompilerParams(vmem_limit_bytes=LIMIT),
        name="back_end" if end else ("back_start" if start else "back_join"),
    )(*args)


def by_turn(core, chip):
    one = 1 + core
    return chip ^ one, chip ^ 3, chip, chip ^ (3 - one)


def turned(dst, blocks):
    n = blocks[0].shape[0]
    for i, block in enumerate(blocks):
        dst[:, i * n : (i + 1) * n] = block[...].T


def grad_ffn_kernel(sc, *rest):
    lefts, rights = rest[:4], rest[4:8]
    send_ref, keep_ref, token_ref, left, right = rest[-5:]
    token_ref[...] = jnp.zeros_like(token_ref)
    core, chip = sc[0], sc[1]
    n, cols = rights[0].shape[0], right.shape[1]
    turned(left, lefts)
    for i, m in enumerate(by_turn(core, chip)):
        at = pl.multiple_of(m * cols, 128)
        for j, block in enumerate(rights):
            right[j * n : (j + 1) * n, :] = block[:, pl.ds(at, cols)]
        out = send_ref if i < 2 else keep_ref
        out[i % 2] = nn(left[...], right[...]).astype(bf16)


def grad_ffn(sc, lefts, rights, after):
    n, width = lefts[0].shape
    cols = rights[0].shape[1] // 4
    out = shape((2, width, cols), bf16)
    return pl.pallas_call(
        grad_ffn_kernel,
        out_shape=(out, out, TOKEN),
        in_specs=[SCALARS] + [WHOLE] * 8 + [LEFT] * len(after),
        out_specs=(WHOLE,) * 3,
        scratch_shapes=[pltpu.VMEM((width, 4 * n), bf16), pltpu.VMEM((4 * n, cols), bf16)],
        cost_estimate=BRIEF,
        compiler_params=pltpu.CompilerParams(vmem_limit_bytes=LIMIT),
        name="grad_ffn",
    )(sc, *lefts, *rights, *after)


def grad_down_kernel(sc, *rest):
    lefts, rights = rest[:4], rest[4:8]
    send_ref, keep_ref, token_ref, left, right = rest[-5:]
    token_ref[...] = jnp.zeros_like(token_ref)
    n, (_, half, cols) = rights[0].shape[0], send_ref.shape
    turned(left, lefts)
    rows = pl.ds(pl.multiple_of(sc[0] * half, half), half)
    like = sc[2] & 1
    for h in range(2):
        for out, parity in ((send_ref, 1 - like), (keep_ref, like)):
            at = pl.multiple_of((2 * h + parity) * cols, 128)
            for j, block in enumerate(rights):
                right[j * n : (j + 1) * n, :] = block[:, pl.ds(at, cols)]
            out[h] = nn(left[rows, :], right[...]).astype(out.dtype)


def grad_down(sc, lefts, rights, after):
    n, width = lefts[0].shape
    cols = rights[0].shape[1] // 4
    block = (2, width // 2, cols)
    return pl.pallas_call(
        grad_down_kernel,
        out_shape=(shape(block, bf16), shape(block, bf16), TOKEN),
        in_specs=[SCALARS] + [WHOLE] * 8 + [LEFT] * len(after),
        out_specs=(WHOLE,) * 3,
        scratch_shapes=[pltpu.VMEM((width, 4 * n), bf16), pltpu.VMEM((4 * n, cols), bf16)],
        cost_estimate=BRIEF,
        compiler_params=pltpu.CompilerParams(vmem_limit_bytes=LIMIT),
        name="grad_down",
    )(sc, *lefts, *rights, *after)


def grad_attention_kernel(sc, *rest):
    a_refs, o_refs, rest = rest[:4], rest[4:8], rest[8:]
    queries, keys, values, outs, threes, ones = (rest[i : i + 2] for i in range(0, 12, 2))
    gain_a, gain_f = (rest[i : i + 2] for i in (12, 14))
    *sends, keep_ref, token_ref, left, right = rest[-6:]
    token_ref[...] = jnp.zeros_like(token_ref)
    core, chip = sc[0], sc[1]
    n, width = a_refs[0].shape
    turned(left.at[0], a_refs)
    gains = [g[0][...] + g[1][...] for g in (gain_a, gain_f)]
    gains = jnp.concatenate([*gains, jnp.zeros((6, width), f32)], axis=0).T
    gains = jnp.concatenate([gains, jnp.zeros((width, PIECE - KVW - 8), f32)], axis=1).astype(bf16)

    def fill(at, of_three, own_three, own_one, single):
        for j in range(2):
            for i in range(3):
                right[of_three + i, j * n : (j + 1) * n, :] = own_three[j][i]
                right[of_three + i, (j + 2) * n : (j + 3) * n, :] = threes[j][i]
            right[single, j * n : (j + 1) * n, :] = own_one[j][...]
            right[single, (j + 2) * n : (j + 3) * n, :] = ones[j][...]

    @pl.when(core == 0)
    def _():
        fill(0, 0, queries, keys, 3)

    @pl.when(core == 1)
    def _():
        turned(left.at[1], o_refs)
        fill(0, 1, outs, values, 0)

    for i, m in enumerate(by_turn(core, chip)):
        out = sends[i] if i < 2 else keep_ref.at[i - 2]
        which = jnp.where(m > 0, core, 0)
        out[...] = nn(left[which], right[m]).astype(bf16)
        out[:, KVW:] = gains


def grad_attention(sc, a, o, own, got, gains, after):
    n, width = a[0].shape
    out = shape((width, PIECE), bf16)
    return pl.pallas_call(
        grad_attention_kernel,
        out_shape=(out, out, shape((2, width, PIECE), bf16), TOKEN),
        in_specs=[SCALARS] + [WHOLE] * 24 + [LEFT] * len(after),
        out_specs=(WHOLE,) * 4,
        scratch_shapes=[pltpu.VMEM((2, width, 4 * n), bf16), pltpu.VMEM((4, 4 * n, PIECE), bf16)],
        cost_estimate=BRIEF,
        compiler_params=pltpu.CompilerParams(vmem_limit_bytes=LIMIT),
        name="grad_attention",
    )(sc, *a, *o, *own, *got, *gains, *after)


def lay_kernel(count, sc, *rest):
    mine, other, outs, kept = rest[:4], rest[4:8], rest[-1 - count : -1], rest[-1]
    core, chip = sc[0], sc[1]
    for kind, pieces in ((core, mine), (1 - core, other)):
        for who, piece in zip(whose(kind), pieces):
            kept[kind, chip ^ who] = piece[...]
    n = sum(o.shape[1] for o in outs[: 4 if len(outs) > 2 else 2]) // 8
    cols = [jnp.concatenate([kept[c, m, :, :n].astype(f32) for m in range(4)], axis=1) for c in range(2)]
    if len(outs) == 2:
        outs[0][...] = cols[0]
        outs[1][...] = cols[1]
    else:
        outs[0][...] = cols[0][:, : 3 * n]
        outs[1][...] = cols[0][:, 3 * n :]
        outs[2][...] = cols[1][:, :n]
        outs[3][...] = cols[1][:, n:]
        gains = kept[0, 0, :, n : n + 8].astype(f32) + kept[1, 0, :, n : n + 8].astype(f32)
        outs[4][...] = gains.T[:2]


def lay(sc, mine, other, widths, after):
    rows, n = mine[0].shape
    outs = tuple(shape((rows, w), f32) for w in widths)
    if len(widths) > 2:
        outs += (shape((2, rows), f32),)
    return pl.pallas_call(
        functools.partial(lay_kernel, len(outs)),
        out_shape=outs,
        in_specs=[SCALARS] + [WHOLE] * 8 + [LEFT] * len(after),
        out_specs=(WHOLE,) * len(outs),
        scratch_shapes=[pltpu.VMEM((2, 4, rows, n), bf16)],
        cost_estimate=BRIEF,
        compiler_params=pltpu.CompilerParams(vmem_limit_bytes=24 << 20),
        name="lay",
    )(sc, *mine, *other, *after)


def pick_first_kernel(sc, q_ref, k_ref, v_ref, o_ref, gain_ref, out_ref, wide, tall, sem):
    rows = out_ref.shape[0]
    which = sc[0] * 4 + sc[1]

    def bring(source, into, first, last):
        @pl.when((which >= first) & (which <= last))
        def _():
            copy = pltpu.make_async_copy(source, into, sem)
            copy.start()
            copy.wait()

    bring(q_ref, wide, 0, 2)
    bring(k_ref, tall, 3, 3)
    bring(v_ref, tall, 4, 4)
    bring(o_ref, wide, 5, 7)
    pad = jnp.zeros((6, rows), f32)
    gains = jnp.concatenate([gain_ref[...], pad], axis=0).T.astype(bf16)
    rest = jnp.zeros((rows, PIECE - KVW - 8), bf16)
    for m in range(4):

        @pl.when((which == m) | (which == (m + 5 if m < 3 else 4)))
        def _():
            piece = wide[:, m * KVW : (m + 1) * KVW] if m < 3 else tall[...].T
            out_ref[...] = jnp.concatenate([piece, gains, rest], axis=1)


def pick_first(sc, query, key, value, out, gains):
    return pl.pallas_call(
        pick_first_kernel,
        out_shape=shape((query.shape[0], PIECE), bf16),
        in_specs=[SCALARS] + [LEFT] * 4 + [WHOLE],
        out_specs=WHOLE,
        scratch_shapes=[pltpu.VMEM(query.shape, bf16), pltpu.VMEM(key.shape, bf16), pltpu.SemaphoreType.DMA],
        cost_estimate=BRIEF,
        compiler_params=pltpu.CompilerParams(vmem_limit_bytes=LIMIT),
        name="pick_first",
    )(sc, query, key, value, out, gains)


def pick_kernel(sc, gate, up, down, *rest):
    out_ref, sems = rest[-2:]
    rows, cols = out_ref.shape[0] - ROWS, out_ref.shape[1]
    into = out_ref.at[:rows]
    start = pl.multiple_of(down_rows(sc[0], sc[1], down.shape[0]), 64)
    copy = pltpu.make_async_copy(down.at[pl.ds(start, ROWS), :], out_ref.at[rows:], sems.at[1])
    copy.start()
    at = pl.ds(pl.multiple_of(sc[1] * cols, 128), cols)
    for c, source in ((0, gate), (1, up)):

        @pl.when(sc[0] == c)
        def _():
            pltpu.make_async_copy(source.at[:, at], into, sems.at[0]).start()

    pltpu.make_async_copy(gate.at[:, at], into, sems.at[0]).wait()
    copy.wait()


def pick(sc, gate, up, down, after):
    return pl.pallas_call(
        pick_kernel,
        out_shape=shape((gate.shape[0] + ROWS, gate.shape[1] // 4), bf16),
        in_specs=[SCALARS] + [LEFT] * (3 + len(after)),
        out_specs=WHOLE,
        scratch_shapes=[pltpu.SemaphoreType.DMA((2,))],
        cost_estimate=BRIEF,
        compiler_params=pltpu.CompilerParams(vmem_limit_bytes=16 << 20),
        name="pick",
    )(sc, gate, up, down, *after)


def gains_kernel(first_ref, out_ref):
    for j in range(4):
        n = first_ref.shape[1]
        out_ref[:, j * n : (j + 1) * n] = first_ref[j, :, KVW : KVW + 8].astype(f32).T[:2]


def gains_of(first):
    return pl.pallas_call(
        gains_kernel,
        out_shape=shape((2, 4 * first.shape[1]), f32),
        in_specs=[WHOLE],
        out_specs=WHOLE,
        cost_estimate=BRIEF,
        compiler_params=pltpu.CompilerParams(vmem_limit_bytes=16 << 20),
        name="gains",
    )(first)


def stack_kernel(sc, *rest):
    parts, out_ref, sems = rest[:4], rest[-2], rest[-1]
    copies = [pltpu.make_async_copy(p, out_ref.at[sc[2] ^ s], sems.at[s]) for s, p in enumerate(parts)]
    for copy in copies:
        copy.start()
    for copy in copies:
        copy.wait()


def stack(sc, parts, after=()):
    return pl.pallas_call(
        stack_kernel,
        out_shape=shape((4,) + parts[0].shape, parts[0].dtype),
        in_specs=[SCALARS] + [LEFT] * (4 + len(after)),
        out_specs=WHOLE,
        scratch_shapes=[pltpu.SemaphoreType.DMA((4,))],
        cost_estimate=BRIEF,
        compiler_params=pltpu.CompilerParams(vmem_limit_bytes=16 << 20),
        name="stack",
    )(sc, *parts, *after)


def small(kernel, sc, args, outs, scratch, after, name):
    def with_token(*refs):
        at = len(refs) - len(scratch) - 1
        refs[at][...] = jnp.zeros_like(refs[at])
        kernel(*refs[:at], *refs[at + 1 :])

    return pl.pallas_call(
        with_token,
        out_shape=(*outs, TOKEN),
        in_specs=[SCALARS] + [WHOLE] * len(args) + [LEFT] * len(after),
        out_specs=(WHOLE,) * (len(outs) + 1),
        scratch_shapes=scratch,
        cost_estimate=BRIEF,
        compiler_params=pltpu.CompilerParams(vmem_limit_bytes=32 << 20),
        name=name,
    )(sc, *args, *after)


def sum_first(sc, keep, got, after, parts=1):
    def kernel(sc, keep_ref, *rest):
        own_got, later_got = rest[:2] if len(got) == 2 else (rest[0].at[0], rest[0].at[1])
        own_ref = rest[-1]
        for i, later_ref in enumerate(rest[-1 - parts : -1]):
            n = later_ref.shape[0]
            rows = slice(i * n, (i + 1) * n)
            later_ref[...] = (keep_ref[1, rows].astype(f32) + later_got[rows].astype(f32)).astype(bf16)
        own_ref[...] = keep_ref[0].astype(f32) + own_got[...].astype(f32)

    rows, cols = keep.shape[1:]
    outs = [shape((rows // parts, cols), bf16)] * parts + [shape((rows, cols), f32)]
    return small(kernel, sc, [keep, *got], outs, [], after, "sum_first")


def sum_second(sc, own, got, after):
    def kernel(sc, own_ref, *rest):
        gots, (send_ref, keep_ref, total) = rest[: len(got)], rest[-3:]
        n = total.shape[1]
        for j in range(4):
            part, at = divmod(j * n, gots[0].shape[0])
            total[j] = own_ref[j * n : (j + 1) * n, :] + gots[part][at : at + n, :].astype(f32)
        like = sc[2] & 1
        for h in range(2):
            send_ref[h] = total[2 * h + 1 - like].astype(bf16)
            keep_ref[h] = total[2 * h + like]

    rows, cols = own.shape
    part = (rows // 4, cols)
    outs = [shape((2,) + part, bf16), shape((2,) + part, f32)]
    return small(kernel, sc, [own, *got], outs, [pltpu.VMEM((4,) + part, f32)], after, "sum_second")


def sum_third(sc, keep, got, after):
    def kernel(sc, keep_ref, got_ref, *rest):
        send_ref, own_ref = rest[-2:]
        h = sc[2] >> 1
        send_ref[...] = (keep_ref[1 - h].astype(f32) + got_ref[1 - h].astype(f32)).astype(bf16)
        own_ref[...] = keep_ref[h].astype(f32) + got_ref[h].astype(f32)

    part = keep.shape[1:]
    return small(kernel, sc, [keep, got], [shape(part, bf16), shape(part, f32)], [], after, "sum_third")


def down_split(sc, own, got, after):
    def kernel(sc, own_ref, got_ref, *rest):
        send_ref, kept_ref, total = rest[-3:]
        n = total.shape[1]
        for m in range(4):
            rows = slice(m * n, (m + 1) * n)
            total[m] = own_ref[rows, :] + got_ref[rows, :].astype(f32)
        for i, m in enumerate(by_turn(sc[0], sc[1])):
            out = send_ref if i < 2 else kept_ref
            out[i % 2] = total[m].astype(bf16)

    rows, cols = own.shape
    out = shape((2, rows // 4, cols), bf16)
    return small(kernel, sc, [own, got], [out, out], [pltpu.VMEM((4, rows // 4, cols), f32)], after, "down_split")


def sum_two(sc, own, got, after):
    def kernel(sc, own_ref, got_ref, *rest):
        rest[-1][...] = (own_ref[...] + got_ref[...].astype(f32)).astype(bf16)

    return small(kernel, sc, [own, got], [shape(own.shape, bf16)], [], after, "sum_two")


def lay_down(sc, mine, other, after):
    def kernel(sc, *rest):
        out_ref, total = rest[-2:]
        n = total.shape[2]
        for kind, pieces in ((sc[0], rest[:4]), (1 - sc[0], rest[4:8])):
            for who, piece in zip(whose(kind), pieces):
                total[kind, sc[1] ^ who] = piece[...].astype(f32)
        for c in range(2):
            for m in range(4):
                at = (c * 4 + m) * n
                out_ref[at : at + n, :] = total[c, m]

    n, cols = mine[0].shape
    return small(kernel, sc, [*mine, *other], [shape((8 * n, cols), f32)], [pltpu.VMEM((2, 4, n, cols), f32)], after, "lay_down")[0]


def hold(value, after):
    return pl.pallas_call(
        lambda *refs: None,
        out_shape=shape(value.shape, value.dtype),
        in_specs=[LEFT] * (1 + len(after)),
        out_specs=LEFT,
        input_output_aliases={0: 0},
        cost_estimate=BRIEF,
        compiler_params=pltpu.CompilerParams(vmem_limit_bytes=1 << 20),
        name="hold",
    )(value, *after)


def far_sum(sc, far, near, after):
    def kernel(sc, far_ref, near_ref, *rest):
        rest[-1][...] = (far_ref[...] + jnp.where(sc[0] == 1, near_ref[...].astype(f32), 0.0)).astype(bf16)

    return small(kernel, sc, [far, near], [shape(far.shape, bf16)], [], after, "far_sum")


CORE, SIDE, BACK = 1, 2, 4
rope_base = 10000.0
RUNS = 2


def flip(value, bit, bit1=None):
    count = lax.axis_size("dp")
    bits = (bit, bit if bit1 is None else bit1)
    return lax.ppermute(value, "dp", [(i, i ^ bits[i & 1]) for i in range(count)])


def flip_z(value, bit, where=lambda d, z: True):
    count, depth = lax.axis_size("dp"), lax.axis_size("fsdp")
    pairs = [(d * depth + z, d * depth + (z ^ bit)) for d in range(count) for z in range(depth) if where(d, z)]
    return lax.ppermute(value, ("dp", "fsdp"), pairs)


def home_to_work(value, back=False):
    count, depth = lax.axis_size("dp"), lax.axis_size("fsdp")
    pairs = []
    for d in range(count):
        for z in range(depth):
            there = (d & ~1) | (z & 1), 2 * (d & 1) + (z >> 1)
            pair = (d * depth + z, there[0] * depth + there[1])
            pairs.append(pair[::-1] if back else pair)
    return lax.ppermute(value, ("dp", "fsdp"), pairs)


def place():
    d, z = lax.axis_index("dp"), lax.axis_index("fsdp")
    return d & 1, (d >> 1) & 3, z


def turns(shard):
    far = flip_z(shard, 2)
    return shard, flip_z(shard, 1), far, flip_z(far, 1)


def plane_gather(piece):
    first, second = flip(piece, SIDE, BACK), flip(piece, BACK, SIDE)
    mine = (piece, first, second, flip(first, BACK, SIDE))
    return mine, tuple(flip(p, CORE) for p in mine)


def window(own):
    core, _, _ = place()
    depth = lax.axis_size("fsdp")
    far = lax.ppermute(own, "fsdp", [(z, z + 1) for z in range(0, depth, 2)])
    near = flip(jnp.where(core == 0, own, far), CORE)
    return far, near, own


def unwindow(sc, far, near):
    depth = lax.axis_size("fsdp")
    near = flip(near, CORE)
    far, token = far_sum(sc, far, near, [])
    return near, token, lax.ppermute(far, "fsdp", [(z + 1, z) for z in range(0, depth, 2)])


def over_groups(value):
    bit = 8
    while bit < lax.axis_size("dp"):
        value = (value.astype(f32) + flip(value, bit).astype(f32)).astype(bf16)
        bit *= 2
    return value


def spread(piece):
    return piece, flip(piece, SIDE, BACK), flip(piece, BACK, SIDE), flip(piece, SIDE | BACK)


def across(pieces):
    return tuple(flip(p, CORE) for p in pieces)


def body(tokens, segment_ids, attn_gain, query_weight, key_weight, value_weight, out_weight, ffn_gain, gate_weight, up_weight, down_weight, cotangent):
    core, chip, z = place()
    sc = jnp.stack([core, chip, z]).astype(jnp.int32)
    _, stretch, width = tokens.shape
    rows, depth = query_weight.shape[0], lax.axis_size("fsdp")
    block = 2 * (z & 1) + core
    positions = (block * stretch + jnp.arange(stretch)).astype(f32)
    freq = rope_base ** (-2.0 * jnp.arange(HEAD_DIM // 2, dtype=f32) / HEAD_DIM)
    angle = freq[:, None] * positions[None, :]
    cos, sin = jnp.cos(angle), jnp.sin(angle)

    gains = jnp.stack([attn_gain, ffn_gain]).astype(f32)
    parts_a = turns(pick_first(sc, query_weight, key_weight.T, value_weight.T, out_weight, gains))
    ids = jnp.broadcast_to((segment_ids[0] + 1).astype(bf16), (IDS, stretch))
    tokens = home_to_work(jnp.concatenate([tokens[0].T, ids]))
    piece_b = pick(sc, gate_weight, up_weight, down_weight.T, [])
    side_b = flip_z(piece_b, 1)
    far_b = flip_z(piece_b, 2)
    whole_a = stack(sc, parts_a, [far_b, side_b])
    gains = gains_of(whole_a)
    gain_a, gain_f = gains[:1], gains[1:]
    wa = plane_gather(whole_a.reshape(depth * rows, PIECE))
    whole_b = stack(sc, (piece_b, side_b, far_b, flip_z(far_b, 1)), [wa[0][1], wa[0][2]])
    first_b, second_b = flip(whole_b, SIDE, BACK), flip(whole_b, BACK, SIDE)

    h_0, a0, q0, own = pre(sc, tokens, gain_a, cos, sin, *wa, [whole_b])
    kv0 = window(own)
    first_b = hold(first_b, [kv0[0], second_b])
    opposite_b = flip(first_b, BACK, SIDE)
    o0, lse0 = attend(q0, kv0)
    cot = home_to_work(cotangent[0].T)
    wb = whole_b, first_b, second_b, hold(opposite_b, [o0, cot])
    wb = wb, across(wb)
    weights = wa, wb
    mixed0, h1_0, b0, gate0, up0, z0, h_1, a1, q1, own = post(False, [], sc, o0, h_0, gain_f, gain_a, cos, sin, own, *weights)
    kv1 = window(own)
    across_0 = across((a0, b0, mixed0, z0))
    o1, lse1 = attend(q1, kv1, across_0)
    mixed1, h1_1, b1, gate1, up1, z1, output = post(True, [], sc, o1, h_1, gain_f, gain_a, cos, sin, own, *weights)
    across_1 = across((a1, b1, mixed1, z1))

    gb1, act1, away1, g1, p1, dgain_f1, do = back(True, False, sc, weights, [cot], [gate1, up1, h1_1, gain_f])
    across_2 = across((gb1, away1))
    dq1, three1, far, near, own = attend_back(sc, p1, q1, kv1, lse1, do, cos, sin)
    near, _, far = unwindow(sc, far, near)
    (three1,) = across((three1,))
    tail = [g1, dq1, own, near, far, h_1, gain_a, cos, sin]
    dk1, dv1, one1, dgain_a1, gb0, act0, away0, g1, p0, dgain_f0, do = back(False, False, sc, weights, tail, [gate0, up0, h1_0, gain_f], [three1, *across_2, *across_1])

    away0, gb0_, one1 = across((away0, gb0, one1))
    send_b, keep_b, done = grad_ffn(sc, [b1, b0, across_1[1], across_0[1]], [act1, act0, across_2[1], away0], [])
    got_b = flip(send_b, SIDE, BACK)
    dq0, three0, far, near, own = attend_back(sc, p0, q0, kv0, lse0, do, cos, sin, [one1, done])
    near, done, far = unwindow(sc, far, near)
    send_d, keep_d, done = grad_down(sc, [gb1, gb0, across_2[0], gb0_], [z1, z0, across_1[3], across_0[3]], [done])
    got_d = flip_z(send_d, 1)
    (three0,) = across((three0,))
    tail = [g1, dq0, own, near, far, h_0, gain_a, cos, sin, output]
    dk0, dv0, one0, dgain_a0, leaving = back(False, True, sc, weights, tail, None, [done, three0])
    later_b, own_b, done = sum_first(sc, keep_b, [got_b], [dgain_a0])
    more_b = flip(later_b, BACK, SIDE)
    own = [dq1, dq0, dk1, dk0, dv1, dv0, p1, p0]
    got = [three1, three0, one1, flip(one0, CORE)]
    *send_a, keep_a, done = grad_attention(sc, [a1, a0, across_1[0], across_0[0]], [mixed1, mixed0, across_1[2], across_0[2]], own, got, [dgain_a1, dgain_a0, dgain_f1, dgain_f0], [done])
    got_a = [flip(v, SIDE, BACK) for v in send_a]
    send_d, keep_d, done = sum_third(sc, keep_d, got_d, [done])
    got_d = flip_z(send_d, 2)
    send_b, ring_b, done = sum_second(sc, own_b, [more_b], [done])
    got_b = flip_z(send_b, 1)
    *later_a, own_a, done = sum_first(sc, keep_a, got_a, [done], 2)
    more_a = [flip(v, BACK, SIDE) for v in later_a]
    send_b, ring_b, done = sum_third(sc, ring_b, got_b, [done])
    got_b = flip_z(send_b, 2)
    send_a, ring_a, done = sum_second(sc, own_a, more_a, [done])
    got_a = flip_z(send_a, 1)
    send_d, keep_d, done = down_split(sc, keep_d, got_d, [done])
    got_d = flip(send_d, SIDE, BACK)
    later_d, own_d, done = sum_first(sc, keep_d, [got_d], [done])
    more_d = flip(later_d, BACK, SIDE)
    piece_b, done = sum_two(sc, ring_b, got_b, [done])
    all_b = spread(over_groups(piece_b))
    send_a, ring_a, first = sum_third(sc, ring_a, got_a, [done])
    got_a = flip_z(send_a, 2)
    piece_d, done = sum_two(sc, own_d, more_d, [first])
    all_d = spread(over_groups(piece_d))
    piece_a, done = sum_two(sc, ring_a, got_a, [done])
    all_a = spread(over_groups(piece_a))
    grad_gate, grad_up = lay(sc, all_b, across(all_b), (gate_weight.shape[1],) * 2, [done])
    grad_down_ = lay_down(sc, all_d, across(all_d), [done])
    grad_query, grad_key, grad_value, grad_out, dgains = lay(sc, all_a, across(all_a), (width, KVW, KVW, width), [done])
    leaving = home_to_work(hold(leaving, [first]), back=True)
    output, grad_tokens = leaving[:width].T, leaving[width:].astype(f32).T
    return (output[None], grad_tokens[None], dgains[0], grad_query, grad_key, grad_value, grad_out, dgains[1], grad_gate, grad_up, grad_down_.T)


def solution(mesh):
    wide, rows, shard = P("dp", "fsdp", None), P("dp", "fsdp"), P("fsdp", None)
    in_specs = (wide, rows, P("fsdp"), shard, shard, shard, shard, P("fsdp"), shard, shard, shard, wide)
    out_specs = (wide, wide, P("fsdp"), shard, shard, shard, shard, P("fsdp"), shard, shard, shard)
    return jax.shard_map(body, mesh=mesh, in_specs=in_specs, out_specs=out_specs, check_vma=False)
```

```python
import functools
import jax
import jax.numpy as jnp
from jax import lax
from jax.sharding import PartitionSpec as P
from jax.experimental import pallas as pl
from jax.experimental.pallas import tpu as pltpu

f32, bf16 = jnp.float32, jnp.bfloat16
eps = 1e-05
HEADS, KV_HEADS, HEAD_DIM, GROUP, KVW = 15, 5, 64, 3, 320
IDS = 16
ROWS = 128
PIECE = 384
LIMIT = 58 << 20
WHOLE = pl.BlockSpec(memory_space=pltpu.VMEM)
LEFT = pl.BlockSpec(memory_space=pl.ANY)
SCALARS = pl.BlockSpec(memory_space=pltpu.SMEM)
TOKEN = jax.ShapeDtypeStruct((8, 128), f32)
BRIEF = pl.CostEstimate(flops=1024, bytes_accessed=1024, transcendentals=0)


def contract(a, b, i, j):
    return lax.dot_general(a, b, (((i,), (j,)), ((), ())), preferred_element_type=f32)


def nn(a, b):
    return contract(a, b, 1, 0)


def nt(a, b):
    return contract(a, b, 1, 1)


def tn(a, b):
    return contract(a, b, 0, 0)


def whose(core):
    return 0, 1 + core, 2 - core, 3


def fetch(mine, other, kept, sems, core, chip, only=None, turns=range(4)):
    for j in turns:
        for kind, pieces in ((core, mine), (1 - core, other)):
            at = chip ^ whose(kind)[j]

            def copy():
                pltpu.make_async_copy(pieces[j], kept.at[kind, at], sems.at[kind, at]).start()

            if only is None:
                copy()
            else:
                pl.when(kind == only)(copy)


def leave(kept, out, sem, cols=None):
    if cols is not None:
        kept, out = kept.at[:, cols], out.at[:, cols]
    pltpu.make_async_copy(kept, out, sem).start()


def gone(kepts, outs, sems):
    for i, (kept, out) in enumerate(zip(kepts, outs)):
        pltpu.make_async_copy(kept, out, sems.at[i]).wait()


def arrived(kept, sems, *at):
    pltpu.make_async_copy(kept.at[at], kept.at[at], sems.at[at]).wait()


def normed(x, gain):
    return x * lax.rsqrt(jnp.mean(x * x, axis=-1, keepdims=True) + eps) * gain


def norm_back(x, gain, grad):
    r = lax.rsqrt(jnp.mean(x * x, axis=-1, keepdims=True) + eps)
    hat = x * r
    scaled = grad * gain
    dx = r * (scaled - hat * jnp.mean(scaled * hat, axis=-1, keepdims=True))
    return dx, jnp.sum(grad * hat, axis=0, keepdims=True)


def widened(x):
    return jnp.concatenate([x, jnp.zeros((x.shape[0], PIECE - x.shape[1]), x.dtype)], axis=1)


def rope(u, cos, sin, back):
    heads = u.shape[0] // HEAD_DIM
    half = HEAD_DIM // 2
    out = []
    for h in range(heads):
        u1, u2 = u[h * HEAD_DIM : h * HEAD_DIM + half], u[h * HEAD_DIM + half : (h + 1) * HEAD_DIM]
        if back:
            out += [u1 * cos + u2 * sin, u2 * cos - u1 * sin]
        else:
            out += [u1 * cos - u2 * sin, u2 * cos + u1 * sin]
    return jnp.concatenate(out, axis=0)


def project(state, gain_ref, cos_ref, sin_ref, ids, kept, sems, a_ref, q_ref, kv_ref):
    a = normed(state, gain_ref[...]).astype(bf16)
    a_ref[...] = a
    cos, sin = cos_ref[...], sin_ref[...]
    arrived(kept, sems, 0, 3)
    kv_ref[:KVW, :] = rope(nn(a, kept[0, 3, :, :KVW]).T, cos, sin, False).astype(bf16)
    arrived(kept, sems, 1, 0)
    kv_ref[2 * KVW :, :] = ids
    kv_ref[KVW : 2 * KVW, :] = nn(a, kept[1, 0, :, :KVW]).T.astype(bf16)
    for m in range(3):
        arrived(kept, sems, 0, m)
        q_ref[pl.ds(m * KVW, KVW), :] = rope(nn(a, kept[0, m, :, :KVW]).T, cos, sin, False).astype(bf16)


def pre_kernel(sc, ht_ref, gain_ref, cos_ref, sin_ref, *rest):
    width = ht_ref.shape[0] - IDS
    mine, other = rest[:4], rest[4:8]
    h_ref, a_ref, q_ref, kv_ref, kept, sems = rest[-6:]
    core, chip = sc[0], sc[1]
    fetch(mine, other, kept, sems, core, chip)
    h = ht_ref[:width, :].T
    h_ref[...] = h
    project(h.astype(f32), gain_ref, cos_ref, sin_ref, ht_ref[width:, :], kept, sems, a_ref, q_ref, kv_ref)
    for m in range(1, 4):
        arrived(kept, sems, 1, m)


def scratch_a(width):
    return [pltpu.VMEM((2, 4, width, PIECE), bf16), pltpu.SemaphoreType.DMA((2, 4))]


def shape(s, d):
    return jax.ShapeDtypeStruct(s, d)


def pre(sc, ht, gain, cos, sin, mine_a, other_a, after):
    width, n = ht.shape[0] - IDS, ht.shape[1]
    return pl.pallas_call(
        pre_kernel,
        out_shape=(shape((n, width), bf16), shape((n, width), bf16), shape((width, n), bf16), shape((2 * KVW + IDS, n), bf16)),
        in_specs=[SCALARS] + [WHOLE] * 4 + [LEFT] * (8 + len(after)),
        out_specs=(WHOLE,) * 4,
        scratch_shapes=scratch_a(width),
        cost_estimate=BRIEF,
        compiler_params=pltpu.CompilerParams(vmem_limit_bytes=LIMIT),
        name="pre",
    )(sc, ht, gain, cos, sin, *mine_a, *other_a, *after)


def bias_of(kv):
    keys, n = kv.shape[1], kv.shape[1] // 3
    ids = kv[2 * KVW :, :].astype(f32)
    seg_k, seg_q = ids.T[:, :1], ids[:1, 2 * n :]
    j = lax.broadcasted_iota(jnp.int32, (keys, n), 0)
    i = lax.broadcasted_iota(jnp.int32, (keys, n), 1) + (keys - n)
    return jnp.where((seg_k == seg_q) & (j <= i), 0.0, -1e30).astype(f32)


def window_of(parts, whole):
    n = parts[0].shape[1]
    for w, part in enumerate(parts):
        whole[:, w * n : (w + 1) * n] = part[...]


def attend_kernel(q_ref, kv0, kv1, kv2, *rest):
    o_ref, lse_ref, bias, kv = rest[-4:]
    window_of((kv0, kv1, kv2), kv)
    bias[...] = bias_of(kv)

    def head(e, _):
        row = pl.multiple_of(e * HEAD_DIM, HEAD_DIM)
        k = kv[pl.ds(row, HEAD_DIM), :]
        v = kv[pl.ds(row + KVW, HEAD_DIM), :]
        for g in range(GROUP):
            at = pl.multiple_of((e * GROUP + g) * HEAD_DIM, HEAD_DIM)
            q = q_ref[pl.ds(at, HEAD_DIM), :]
            s = tn(k, q) * HEAD_DIM ** (-0.5) + bias[...]
            top = jnp.max(s, axis=0, keepdims=True)
            expo = jnp.exp(s - top)
            total = jnp.sum(expo, axis=0, keepdims=True)
            probs = (expo * (1.0 / total)).astype(bf16)
            o_ref[pl.ds(at, HEAD_DIM), :] = nn(v, probs).astype(bf16)
            lse_ref[pl.ds(e * GROUP + g, 1), :] = top + jnp.log(total)
        return 0

    lax.fori_loop(0, KV_HEADS, head, 0)


def attend(q, kvs, after=()):
    width, n = q.shape
    return pl.pallas_call(
        attend_kernel,
        out_shape=(shape((width, n), bf16), shape((HEADS, n), f32)),
        in_specs=[WHOLE] * 4 + [LEFT] * len(after),
        out_specs=(WHOLE,) * 2,
        scratch_shapes=[pltpu.VMEM((3 * n, n), f32), pltpu.VMEM((2 * KVW + IDS, 3 * n), bf16)],
        cost_estimate=BRIEF,
        compiler_params=pltpu.CompilerParams(vmem_limit_bytes=24 << 20),
        name="attend",
    )(q, *kvs, *after)


def attend_back_kernel(sc, p_ref, q_ref, kv0, kv1, kv2, lse_ref, do_ref, cos_ref, sin_ref, *rest):
    dq_ref, three_ref, far_ref, near_ref, own_ref, bias, kv, dqs = rest[-8:]
    n = q_ref.shape[1]
    window_of((kv0, kv1, kv2), kv)
    bias[...] = bias_of(kv)
    scale = HEAD_DIM ** (-0.5)

    def head(e, _):
        row = pl.multiple_of(e * HEAD_DIM, HEAD_DIM)
        k = kv[pl.ds(row, HEAD_DIM), :]
        v = kv[pl.ds(row + KVW, HEAD_DIM), :]
        dk = dv = None
        for g in range(GROUP):
            at = pl.multiple_of((e * GROUP + g) * HEAD_DIM, HEAD_DIM)
            q = q_ref[pl.ds(at, HEAD_DIM), :]
            do = do_ref[pl.ds(at, HEAD_DIM), :]
            s = tn(k, q) * scale + bias[...]
            probs = jnp.exp(s - lse_ref[pl.ds(e * GROUP + g, 1), :])
            dp = tn(v, do)
            inner = jnp.sum(probs * dp, axis=0, keepdims=True)
            ds = (probs * (dp - inner)).astype(bf16)
            dvg, dkg = nt(do, probs.astype(bf16)), nt(q, ds)
            dv, dk = (dvg, dkg) if g == 0 else (dv + dvg, dk + dkg)
            dqs[pl.ds(at, HEAD_DIM), :] = nn(k, ds)
        for at, grad in ((row, dk * scale), (row + KVW, dv)):
            far_ref[pl.ds(at, HEAD_DIM), :] = grad[:, :n]
            near_ref[pl.ds(at, HEAD_DIM), :] = grad[:, n : 2 * n].astype(bf16)
            own_ref[pl.ds(at, HEAD_DIM), :] = grad[:, 2 * n :]
        return 0

    lax.fori_loop(0, KV_HEADS, head, 0)
    cos, sin = cos_ref[...] * scale, sin_ref[...] * scale
    for m in range(3):
        dq = widened(rope(dqs[m * KVW : (m + 1) * KVW, :], cos, sin, True).T.astype(bf16))
        dq_ref[m] = dq
        three_ref[m] = jnp.where(sc[0] == 0, p_ref[m], dq)


def attend_back(sc, p, q, kvs, lse, do, cos, sin, after=()):
    width, n = q.shape
    block = (2 * KVW, n)
    return pl.pallas_call(
        attend_back_kernel,
        out_shape=(shape((3, n, PIECE), bf16), shape((3, n, PIECE), bf16), shape(block, f32), shape(block, bf16), shape(block, f32)),
        in_specs=[SCALARS] + [WHOLE] * 9 + [LEFT] * len(after),
        out_specs=(WHOLE,) * 5,
        scratch_shapes=[pltpu.VMEM((3 * n, n), f32), pltpu.VMEM((2 * KVW + IDS, 3 * n), bf16), pltpu.VMEM((width, n), f32)],
        cost_estimate=BRIEF,
        compiler_params=pltpu.CompilerParams(vmem_limit_bytes=32 << 20),
        name="attend_back",
    )(sc, p, q, *kvs, lse, do, cos, sin, *after)


def down_rows(kind, chip, width):
    return jnp.minimum((kind * 4 + chip) * ROWS, width - ROWS)


def fetch_down(mine, other, wb, wd, sem_d, core, chip):
    rows, width = wb.shape[3], wd.shape[1]
    last = width % ROWS
    for kind, pieces in ((core, mine), (1 - core, other)):
        for who, piece in zip(whose(kind), pieces):
            at = kind * 4 + (chip ^ who)

            @pl.when(at < width // ROWS)
            def _():
                into = wd.at[:, pl.ds(pl.multiple_of(at * ROWS, ROWS), ROWS)]
                pltpu.make_async_copy(piece.at[:, rows:], into, sem_d).start()

            @pl.when(at == width // ROWS)
            def _():
                pltpu.make_async_copy(piece.at[:, rows + ROWS - last :], wd.at[:, width - last :], sem_d).start()


def fetch_both(mine, other, wb, sem_b, core, chip, turns=range(4)):
    rows = wb.shape[3]
    fetch([p.at[:, :rows] for p in mine], [p.at[:, :rows] for p in other], wb, sem_b, core, chip, turns=turns)


def whole(wb, c, m):
    _, rows, n = wb.shape[2:]
    return wb[c, m].reshape(4 * rows, n)


def arrived_down(wd, sem_d):
    pltpu.make_async_copy(wd, wd, sem_d).wait()


def scratch_ffn(width, n):
    return [
        pltpu.VMEM((2, 4, 4, width // 4, n), bf16),
        pltpu.SemaphoreType.DMA((2, 4)),
        pltpu.VMEM((4, width, n), bf16),
        pltpu.SemaphoreType.DMA,
    ]


def post_kernel(last, after, sc, ot_ref, h_ref, gain_ref, gain_a, cos_ref, sin_ref, *rest):
    mine_a, other_a, mine_b, other_b = rest[:4], rest[4:8], rest[8:12], rest[12:16]
    ids_ref, rest = rest[16], rest[17 + after :]
    hbm, next_ref = rest[:6], rest[6]
    more, rest = rest[7 : 7 + (0 if last else 3)], rest[7 + (0 if last else 3) :]
    wa, sem_a, wb, sem_b, wd, sem_d, *stage, sem_out = rest
    o_ref, h1_ref, b_ref, gate_ref, up_ref, z_ref = stage
    core, chip = sc[0], sc[1]
    fetch(mine_a, other_a, wa, sem_a, core, chip, 1)
    fetch_both(mine_b, other_b, wb, sem_b, core, chip, (0, 1))
    fetch_down(mine_b, other_b, wb, wd, sem_d, core, chip)
    fetch_both(mine_b, other_b, wb, sem_b, core, chip, (2, 3))
    if not last:
        fetch(mine_a, other_a, wa, sem_a, core, chip, 0)
    o = ot_ref[...].T
    o_ref[...] = o
    leave(o_ref, hbm[0], sem_out.at[0])
    for m in range(1, 4):
        arrived(wa, sem_a, 1, m)
    h1 = h_ref[...].astype(f32) + jnp.concatenate([nn(o, wa[1, m, :, :KVW]) for m in range(1, 4)], axis=1)
    h1_ref[...] = h1
    leave(h1_ref, hbm[1], sem_out.at[1])
    b = normed(h1, gain_ref[...]).astype(bf16)
    b_ref[...] = b
    leave(b_ref, hbm[2], sem_out.at[2])
    n = wb.shape[4]
    total = h1
    for i in range(4):
        m = chip ^ i
        cols = pl.ds(pl.multiple_of(m * n, 128), n)
        arrived(wb, sem_b, 0, m)
        gate = nn(b, whole(wb, 0, m))
        arrived(wb, sem_b, 1, m)
        up = nn(b, whole(wb, 1, m))
        gate_ref[:, cols] = gate.astype(bf16)
        up_ref[:, cols] = up.astype(bf16)
        z = (gate / (1.0 + jnp.exp(-gate)) * up).astype(bf16)
        z_ref[:, cols] = z
        for j in range(3, 6):
            leave(stage[j], hbm[j], sem_out.at[j], cols)
        if i == 0:
            arrived_down(wd, sem_d)
        total = total + nt(z, wd[m])
    next_ref[...] = total.astype(bf16).T if last else total
    if last:
        arrived(wa, sem_a, 1, 0)
    else:
        project(total, gain_a, cos_ref, sin_ref, ids_ref[2 * KVW :, :], wa, sem_a, *more)
    gone(stage, hbm, sem_out)


def post(last, after, sc, ot, h, gain, gain_a, cos, sin, kv, wa, wb):
    width, n = ot.shape
    hidden = wb[0][0].shape[2] * 4
    outs = [shape((n, width), bf16), shape((n, width), f32), shape((n, width), bf16)] + [shape((n, hidden), bf16)] * 3
    outs += [shape((width, n), bf16) if last else shape((n, width), f32)]
    if not last:
        outs += [shape((n, width), bf16), shape((width, n), bf16), shape((2 * KVW + IDS, n), bf16)]
    return pl.pallas_call(
        functools.partial(post_kernel, last, len(after)),
        out_shape=tuple(outs),
        in_specs=[SCALARS] + [WHOLE] * 6 + [LEFT] * 16 + [WHOLE] + [LEFT] * len(after),
        out_specs=(LEFT,) * 6 + (WHOLE,) * (len(outs) - 6),
        scratch_shapes=scratch_a(width) + scratch_ffn(width, hidden // 4) + [pltpu.VMEM(o.shape, o.dtype) for o in outs[:6]] + [pltpu.SemaphoreType.DMA((6,))],
        cost_estimate=BRIEF,
        compiler_params=pltpu.CompilerParams(vmem_limit_bytes=LIMIT),
        name="post",
    )(sc, ot, h, gain, gain_a, cos, sin, *wa[0], *wa[1], *wb[0], *wb[1], kv, *after)


def ffn_back(state, core, chip, refs, weights, stage, sems, hbm):
    gate_ref, up_ref, h1_ref, gain_ref, gb_ref, keep_ref, send_ref, g1_ref, p_ref, dgain_ref, do_ref = refs
    wa, sem_a, wb, sem_b, wd, sem_d = weights
    gb = state.astype(bf16)
    gb_ref[...] = gb
    leave(gb_ref, hbm[3], sems.at[3])
    n = wb.shape[4]
    first = core == 0
    arrived_down(wd, sem_d)
    db = None
    for i in range(4):
        m = chip ^ i
        cols = pl.ds(pl.multiple_of(m * n, 128), n)
        dz = nn(gb, wd[m])
        if i == 0:
            for j in range(2):
                pltpu.make_async_copy(hbm[j], stage[j], sems.at[j]).wait()
        gate, up = gate_ref[:, cols].astype(f32), up_ref[:, cols].astype(f32)
        sig = 1.0 / (1.0 + jnp.exp(-gate))
        dup = (dz * (gate * sig)).astype(bf16)
        dgate = (dz * up * (sig * (1.0 + gate * (1.0 - sig)))).astype(bf16)
        keep_ref[:, cols] = jnp.where(first, dgate, dup)
        send_ref[:, cols] = jnp.where(first, dup, dgate)
        leave(keep_ref, hbm[4], sems.at[4], cols)
        leave(send_ref, hbm[5], sems.at[5], cols)
        arrived(wb, sem_b, 0, m)
        part = nt(dgate, whole(wb, 0, m))
        arrived(wb, sem_b, 1, m)
        part = part + nt(dup, whole(wb, 1, m))
        db = part if i == 0 else db + part
    pltpu.make_async_copy(hbm[2], stage[2], sems.at[2]).wait()
    dx, dgain = norm_back(h1_ref[...], gain_ref[...], db)
    dgain_ref[...] = dgain
    g1 = state + dx
    g1_ref[...] = g1
    leave(g1_ref, hbm[6], sems.at[6])
    low = g1.astype(bf16)
    do = None
    for p in range(3):
        part = low[:, p * KVW : (p + 1) * KVW]
        p_ref[p] = widened(part)
        arrived(wa, sem_a, 1, p + 1)
        part = nt(wa[1, p + 1, :, :KVW], part)
        do = part if p == 0 else do + part
    do_ref[...] = do.astype(bf16)


def finish_a(wa, sem_a, *left):
    for at in left:
        arrived(wa, sem_a, *at)


def query_back(dq_ref, wa, sem_a):
    da = None
    for m in range(3):
        arrived(wa, sem_a, 0, m)
        part = nt(dq_ref[m, :, :KVW], wa[0, m, :, :KVW])
        da = part if m == 0 else da + part
    return da


def project_back(da, own_ref, near_ref, far_ref, core, cos_ref, sin_ref, dk_ref, dv_ref, one_ref, h, gain, wa, sem_a):
    cos, sin = cos_ref[...], sin_ref[...]
    grad = own_ref[...] + far_ref[...].astype(f32) + jnp.where(core == 0, near_ref[...].astype(f32), 0.0)
    dk = rope(grad[:KVW], cos, sin, True).T.astype(bf16)
    dv = grad[KVW:].T.astype(bf16)
    dk_ref[...] = widened(dk)
    dv_ref[...] = widened(dv)
    one_ref[...] = widened(jnp.where(core == 0, dv, dk))
    arrived(wa, sem_a, 0, 3)
    arrived(wa, sem_a, 1, 0)
    da = da + nt(dk, wa[0, 3, :, :KVW]) + nt(dv, wa[1, 0, :, :KVW])
    return norm_back(h, gain, da)


def back_kernel(start, end, after, sc, *rest):
    rest = list(rest)

    def take(n):
        out = rest[:n]
        del rest[:n]
        return out

    core, chip = sc[0], sc[1]
    mine_a, other_a = take(4), take(4)
    if not end:
        mine_b, other_b = take(4), take(4)
    if start:
        (g_ref,) = take(1)
    else:
        g1_in, dq_ref, own_ref, near_ref, far_ref, h_ref, gain_a, cos_ref, sin_ref = take(9)
        if end:
            (last_ref,) = take(1)
    if not end:
        ins = take(4)
    take(after)
    if not start:
        dk_ref, dv_ref, one_ref, dgain_a = take(4)
    if end:
        (g_out,) = take(1)
    else:
        outs = take(7)
    wa, sem_a = take(2)
    if not start:
        fetch(mine_a, other_a, wa, sem_a, core, chip, 0)
        fetch(mine_a, other_a, wa, sem_a, core, chip, 1)
    if not end:
        wb, sem_b, wd, sem_d = take(4)
        stage, (sems,) = take(7), take(1)
        hbm = [*ins[:3], *outs[:4]]
        fetch_down(mine_b, other_b, wb, wd, sem_d, core, chip)
        for j in range(3):
            pltpu.make_async_copy(hbm[j], stage[j], sems.at[j]).start()
        fetch_both(mine_b, other_b, wb, sem_b, core, chip)
    if start:
        fetch(mine_a, other_a, wa, sem_a, core, chip, 1)
    if start:
        state = g_ref[...].T.astype(f32)
    else:
        da = query_back(dq_ref, wa, sem_a)
        dx, dgain = project_back(da, own_ref, near_ref, far_ref, core, cos_ref, sin_ref, dk_ref, dv_ref, one_ref, h_ref[...].astype(f32), gain_a[...], wa, sem_a)
        dgain_a[...] = dgain
        state = g1_in[...] + dx
    if end:
        width = state.shape[1]
        g_out[:width, :] = last_ref[...]
        g_out[width:, :] = state.astype(bf16).T
        finish_a(wa, sem_a, (1, 1), (1, 2), (1, 3))
    else:
        refs = (*stage[:3], ins[3], *stage[3:], *outs[4:])
        ffn_back(state, core, chip, refs, (wa, sem_a, wb, sem_b, wd, sem_d), stage, sems, hbm)
        gone(stage[3:], hbm[3:], sems.at[pl.ds(3, 4)])
        if start:
            finish_a(wa, sem_a, (1, 0))


def back(start, end, sc, weights, tail, ffn, after=()):
    wa, wb = weights
    width = wa[0][0].shape[0]
    args = [sc, *wa[0], *wa[1]]
    specs = [SCALARS] + [LEFT] * 8
    scratch = scratch_a(width)
    if not end:
        args += [*wb[0], *wb[1]]
        specs += [LEFT] * 8
        scratch += scratch_ffn(width, wb[0][0].shape[2])
    args += list(tail)
    specs += [WHOLE] * len(tail)
    n = tail[0].shape[1 if start else 0]
    outs = []
    if not end:
        args += list(ffn)
        specs += [LEFT] * 3 + [WHOLE]
    if not start:
        outs += [shape((n, PIECE), bf16)] * 3 + [shape((1, width), f32)]
    if end:
        outs += [shape((2 * width, n), bf16)]
    else:
        hidden = ffn[0].shape[1]
        outs += [shape((n, width), bf16), shape((n, hidden), bf16), shape((n, hidden), bf16)]
        outs += [shape((n, width), f32), shape((3, n, PIECE), bf16), shape((1, width), f32), shape((width, n), bf16)]
    out_specs = [WHOLE] * len(outs)
    if not end:
        at = 0 if start else 4
        out_specs[at : at + 4] = [LEFT] * 4
        scratch += [pltpu.VMEM(x.shape, x.dtype) for x in (*ffn[:3], *outs[at : at + 4])]
        scratch += [pltpu.SemaphoreType.DMA((7,))]
    args += list(after)
    specs += [LEFT] * len(after)
    return pl.pallas_call(
        functools.partial(back_kernel, start, end, len(after)),
        out_shape=tuple(outs),
        in_specs=specs,
        out_specs=tuple(out_specs),
        scratch_shapes=scratch,
        cost_estimate=BRIEF,
        compiler_params=pltpu.CompilerParams(vmem_limit_bytes=LIMIT),
        name="back_end" if end else ("back_start" if start else "back_join"),
    )(*args)


def by_turn(core, chip):
    one = 1 + core
    return chip ^ one, chip ^ 3, chip, chip ^ (3 - one)


def turned(dst, blocks):
    n = blocks[0].shape[0]
    for i, block in enumerate(blocks):
        dst[:, i * n : (i + 1) * n] = block[...].T


def grad_ffn_kernel(sc, *rest):
    lefts, rights = rest[:4], rest[4:8]
    send_ref, keep_ref, token_ref, left, right = rest[-5:]
    token_ref[...] = jnp.zeros_like(token_ref)
    core, chip = sc[0], sc[1]
    n, cols = rights[0].shape[0], right.shape[1]
    turned(left, lefts)
    for i, m in enumerate(by_turn(core, chip)):
        at = pl.multiple_of(m * cols, 128)
        for j, block in enumerate(rights):
            right[j * n : (j + 1) * n, :] = block[:, pl.ds(at, cols)]
        out = send_ref if i < 2 else keep_ref
        out[i % 2] = nn(left[...], right[...]).astype(bf16)


def grad_ffn(sc, lefts, rights, after):
    n, width = lefts[0].shape
    cols = rights[0].shape[1] // 4
    out = shape((2, width, cols), bf16)
    return pl.pallas_call(
        grad_ffn_kernel,
        out_shape=(out, out, TOKEN),
        in_specs=[SCALARS] + [WHOLE] * 8 + [LEFT] * len(after),
        out_specs=(WHOLE,) * 3,
        scratch_shapes=[pltpu.VMEM((width, 4 * n), bf16), pltpu.VMEM((4 * n, cols), bf16)],
        cost_estimate=BRIEF,
        compiler_params=pltpu.CompilerParams(vmem_limit_bytes=LIMIT),
        name="grad_ffn",
    )(sc, *lefts, *rights, *after)


def grad_down_kernel(sc, *rest):
    lefts, rights = rest[:4], rest[4:8]
    send_ref, keep_ref, token_ref, left, right = rest[-5:]
    token_ref[...] = jnp.zeros_like(token_ref)
    n, (_, half, cols) = rights[0].shape[0], send_ref.shape
    turned(left, lefts)
    rows = pl.ds(pl.multiple_of(sc[0] * half, half), half)
    like = sc[2] & 1
    for h in range(2):
        for out, parity in ((send_ref, 1 - like), (keep_ref, like)):
            at = pl.multiple_of((2 * h + parity) * cols, 128)
            for j, block in enumerate(rights):
                right[j * n : (j + 1) * n, :] = block[:, pl.ds(at, cols)]
            out[h] = nn(left[rows, :], right[...]).astype(out.dtype)


def grad_down(sc, lefts, rights, after):
    n, width = lefts[0].shape
    cols = rights[0].shape[1] // 4
    block = (2, width // 2, cols)
    return pl.pallas_call(
        grad_down_kernel,
        out_shape=(shape(block, bf16), shape(block, bf16), TOKEN),
        in_specs=[SCALARS] + [WHOLE] * 8 + [LEFT] * len(after),
        out_specs=(WHOLE,) * 3,
        scratch_shapes=[pltpu.VMEM((width, 4 * n), bf16), pltpu.VMEM((4 * n, cols), bf16)],
        cost_estimate=BRIEF,
        compiler_params=pltpu.CompilerParams(vmem_limit_bytes=LIMIT),
        name="grad_down",
    )(sc, *lefts, *rights, *after)


def grad_attention_kernel(sc, *rest):
    a_refs, o_refs, rest = rest[:4], rest[4:8], rest[8:]
    queries, keys, values, outs, threes, ones = (rest[i : i + 2] for i in range(0, 12, 2))
    gain_a, gain_f = (rest[i : i + 2] for i in (12, 14))
    *sends, keep_ref, token_ref, left, right = rest[-6:]
    token_ref[...] = jnp.zeros_like(token_ref)
    core, chip = sc[0], sc[1]
    n, width = a_refs[0].shape
    turned(left.at[0], a_refs)
    gains = [g[0][...] + g[1][...] for g in (gain_a, gain_f)]
    gains = jnp.concatenate([*gains, jnp.zeros((6, width), f32)], axis=0).T
    gains = jnp.concatenate([gains, jnp.zeros((width, PIECE - KVW - 8), f32)], axis=1).astype(bf16)

    def fill(at, of_three, own_three, own_one, single):
        for j in range(2):
            for i in range(3):
                right[of_three + i, j * n : (j + 1) * n, :] = own_three[j][i]
                right[of_three + i, (j + 2) * n : (j + 3) * n, :] = threes[j][i]
            right[single, j * n : (j + 1) * n, :] = own_one[j][...]
            right[single, (j + 2) * n : (j + 3) * n, :] = ones[j][...]

    @pl.when(core == 0)
    def _():
        fill(0, 0, queries, keys, 3)

    @pl.when(core == 1)
    def _():
        turned(left.at[1], o_refs)
        fill(0, 1, outs, values, 0)

    for i, m in enumerate(by_turn(core, chip)):
        out = sends[i] if i < 2 else keep_ref.at[i - 2]
        which = jnp.where(m > 0, core, 0)
        out[...] = nn(left[which], right[m]).astype(bf16)
        out[:, KVW:] = gains


def grad_attention(sc, a, o, own, got, gains, after):
    n, width = a[0].shape
    out = shape((width, PIECE), bf16)
    return pl.pallas_call(
        grad_attention_kernel,
        out_shape=(out, out, shape((2, width, PIECE), bf16), TOKEN),
        in_specs=[SCALARS] + [WHOLE] * 24 + [LEFT] * len(after),
        out_specs=(WHOLE,) * 4,
        scratch_shapes=[pltpu.VMEM((2, width, 4 * n), bf16), pltpu.VMEM((4, 4 * n, PIECE), bf16)],
        cost_estimate=BRIEF,
        compiler_params=pltpu.CompilerParams(vmem_limit_bytes=LIMIT),
        name="grad_attention",
    )(sc, *a, *o, *own, *got, *gains, *after)


def lay_kernel(count, sc, *rest):
    mine, other, outs, kept = rest[:4], rest[4:8], rest[-1 - count : -1], rest[-1]
    core, chip = sc[0], sc[1]
    for kind, pieces in ((core, mine), (1 - core, other)):
        for who, piece in zip(whose(kind), pieces):
            kept[kind, chip ^ who] = piece[...]
    n = sum(o.shape[1] for o in outs[: 4 if len(outs) > 2 else 2]) // 8
    cols = [jnp.concatenate([kept[c, m, :, :n].astype(f32) for m in range(4)], axis=1) for c in range(2)]
    if len(outs) == 2:
        outs[0][...] = cols[0]
        outs[1][...] = cols[1]
    else:
        outs[0][...] = cols[0][:, : 3 * n]
        outs[1][...] = cols[0][:, 3 * n :]
        outs[2][...] = cols[1][:, :n]
        outs[3][...] = cols[1][:, n:]
        gains = kept[0, 0, :, n : n + 8].astype(f32) + kept[1, 0, :, n : n + 8].astype(f32)
        outs[4][...] = gains.T[:2]


def lay(sc, mine, other, widths, after):
    rows, n = mine[0].shape
    outs = tuple(shape((rows, w), f32) for w in widths)
    if len(widths) > 2:
        outs += (shape((2, rows), f32),)
    return pl.pallas_call(
        functools.partial(lay_kernel, len(outs)),
        out_shape=outs,
        in_specs=[SCALARS] + [WHOLE] * 8 + [LEFT] * len(after),
        out_specs=(WHOLE,) * len(outs),
        scratch_shapes=[pltpu.VMEM((2, 4, rows, n), bf16)],
        cost_estimate=BRIEF,
        compiler_params=pltpu.CompilerParams(vmem_limit_bytes=24 << 20),
        name="lay",
    )(sc, *mine, *other, *after)


def pick_first_kernel(sc, q_ref, k_ref, v_ref, o_ref, gain_ref, out_ref, wide, tall, sem):
    rows = out_ref.shape[0]
    which = sc[0] * 4 + sc[1]

    def bring(source, into, first, last):
        @pl.when((which >= first) & (which <= last))
        def _():
            copy = pltpu.make_async_copy(source, into, sem)
            copy.start()
            copy.wait()

    bring(q_ref, wide, 0, 2)
    bring(k_ref, tall, 3, 3)
    bring(v_ref, tall, 4, 4)
    bring(o_ref, wide, 5, 7)
    pad = jnp.zeros((6, rows), f32)
    gains = jnp.concatenate([gain_ref[...], pad], axis=0).T.astype(bf16)
    rest = jnp.zeros((rows, PIECE - KVW - 8), bf16)
    for m in range(4):

        @pl.when((which == m) | (which == (m + 5 if m < 3 else 4)))
        def _():
            piece = wide[:, m * KVW : (m + 1) * KVW] if m < 3 else tall[...].T
            out_ref[...] = jnp.concatenate([piece, gains, rest], axis=1)


def pick_first(sc, query, key, value, out, gains):
    return pl.pallas_call(
        pick_first_kernel,
        out_shape=shape((query.shape[0], PIECE), bf16),
        in_specs=[SCALARS] + [LEFT] * 4 + [WHOLE],
        out_specs=WHOLE,
        scratch_shapes=[pltpu.VMEM(query.shape, bf16), pltpu.VMEM(key.shape, bf16), pltpu.SemaphoreType.DMA],
        cost_estimate=BRIEF,
        compiler_params=pltpu.CompilerParams(vmem_limit_bytes=LIMIT),
        name="pick_first",
    )(sc, query, key, value, out, gains)


def pick_kernel(sc, gate, up, down, *rest):
    out_ref, sems = rest[-2:]
    rows, cols = out_ref.shape[0] - ROWS, out_ref.shape[1]
    into = out_ref.at[:rows]
    start = pl.multiple_of(down_rows(sc[0], sc[1], down.shape[0]), 64)
    copy = pltpu.make_async_copy(down.at[pl.ds(start, ROWS), :], out_ref.at[rows:], sems.at[1])
    copy.start()
    at = pl.ds(pl.multiple_of(sc[1] * cols, 128), cols)
    for c, source in ((0, gate), (1, up)):

        @pl.when(sc[0] == c)
        def _():
            pltpu.make_async_copy(source.at[:, at], into, sems.at[0]).start()

    pltpu.make_async_copy(gate.at[:, at], into, sems.at[0]).wait()
    copy.wait()


def pick(sc, gate, up, down, after):
    return pl.pallas_call(
        pick_kernel,
        out_shape=shape((gate.shape[0] + ROWS, gate.shape[1] // 4), bf16),
        in_specs=[SCALARS] + [LEFT] * (3 + len(after)),
        out_specs=WHOLE,
        scratch_shapes=[pltpu.SemaphoreType.DMA((2,))],
        cost_estimate=BRIEF,
        compiler_params=pltpu.CompilerParams(vmem_limit_bytes=16 << 20),
        name="pick",
    )(sc, gate, up, down, *after)


def gains_kernel(first_ref, out_ref):
    for j in range(4):
        n = first_ref.shape[1]
        out_ref[:, j * n : (j + 1) * n] = first_ref[j, :, KVW : KVW + 8].astype(f32).T[:2]


def gains_of(first):
    return pl.pallas_call(
        gains_kernel,
        out_shape=shape((2, 4 * first.shape[1]), f32),
        in_specs=[WHOLE],
        out_specs=WHOLE,
        cost_estimate=BRIEF,
        compiler_params=pltpu.CompilerParams(vmem_limit_bytes=16 << 20),
        name="gains",
    )(first)


def stack_kernel(sc, *rest):
    parts, out_ref, sems = rest[:4], rest[-2], rest[-1]
    copies = [pltpu.make_async_copy(p, out_ref.at[sc[2] ^ s], sems.at[s]) for s, p in enumerate(parts)]
    for copy in copies:
        copy.start()
    for copy in copies:
        copy.wait()


def stack(sc, parts, after=()):
    return pl.pallas_call(
        stack_kernel,
        out_shape=shape((4,) + parts[0].shape, parts[0].dtype),
        in_specs=[SCALARS] + [LEFT] * (4 + len(after)),
        out_specs=WHOLE,
        scratch_shapes=[pltpu.SemaphoreType.DMA((4,))],
        cost_estimate=BRIEF,
        compiler_params=pltpu.CompilerParams(vmem_limit_bytes=16 << 20),
        name="stack",
    )(sc, *parts, *after)


def small(kernel, sc, args, outs, scratch, after, name):
    def with_token(*refs):
        at = len(refs) - len(scratch) - 1
        refs[at][...] = jnp.zeros_like(refs[at])
        kernel(*refs[:at], *refs[at + 1 :])

    return pl.pallas_call(
        with_token,
        out_shape=(*outs, TOKEN),
        in_specs=[SCALARS] + [WHOLE] * len(args) + [LEFT] * len(after),
        out_specs=(WHOLE,) * (len(outs) + 1),
        scratch_shapes=scratch,
        cost_estimate=BRIEF,
        compiler_params=pltpu.CompilerParams(vmem_limit_bytes=32 << 20),
        name=name,
    )(sc, *args, *after)


def sum_first(sc, keep, got, after, parts=1):
    def kernel(sc, keep_ref, *rest):
        own_got, later_got = rest[:2] if len(got) == 2 else (rest[0].at[0], rest[0].at[1])
        own_ref = rest[-1]
        for i, later_ref in enumerate(rest[-1 - parts : -1]):
            n = later_ref.shape[0]
            rows = slice(i * n, (i + 1) * n)
            later_ref[...] = (keep_ref[1, rows].astype(f32) + later_got[rows].astype(f32)).astype(bf16)
        own_ref[...] = keep_ref[0].astype(f32) + own_got[...].astype(f32)

    rows, cols = keep.shape[1:]
    outs = [shape((rows // parts, cols), bf16)] * parts + [shape((rows, cols), f32)]
    return small(kernel, sc, [keep, *got], outs, [], after, "sum_first")


def sum_second(sc, own, got, after):
    def kernel(sc, own_ref, *rest):
        gots, (send_ref, keep_ref, total) = rest[: len(got)], rest[-3:]
        n = total.shape[1]
        for j in range(4):
            part, at = divmod(j * n, gots[0].shape[0])
            total[j] = own_ref[j * n : (j + 1) * n, :] + gots[part][at : at + n, :].astype(f32)
        like = sc[2] & 1
        for h in range(2):
            send_ref[h] = total[2 * h + 1 - like].astype(bf16)
            keep_ref[h] = total[2 * h + like]

    rows, cols = own.shape
    part = (rows // 4, cols)
    outs = [shape((2,) + part, bf16), shape((2,) + part, f32)]
    return small(kernel, sc, [own, *got], outs, [pltpu.VMEM((4,) + part, f32)], after, "sum_second")


def sum_third(sc, keep, got, after):
    def kernel(sc, keep_ref, got_ref, *rest):
        send_ref, own_ref = rest[-2:]
        h = sc[2] >> 1
        send_ref[...] = (keep_ref[1 - h].astype(f32) + got_ref[1 - h].astype(f32)).astype(bf16)
        own_ref[...] = keep_ref[h].astype(f32) + got_ref[h].astype(f32)

    part = keep.shape[1:]
    return small(kernel, sc, [keep, got], [shape(part, bf16), shape(part, f32)], [], after, "sum_third")


def down_split(sc, own, got, after):
    def kernel(sc, own_ref, got_ref, *rest):
        send_ref, kept_ref, total = rest[-3:]
        n = total.shape[1]
        for m in range(4):
            rows = slice(m * n, (m + 1) * n)
            total[m] = own_ref[rows, :] + got_ref[rows, :].astype(f32)
        for i, m in enumerate(by_turn(sc[0], sc[1])):
            out = send_ref if i < 2 else kept_ref
            out[i % 2] = total[m].astype(bf16)

    rows, cols = own.shape
    out = shape((2, rows // 4, cols), bf16)
    return small(kernel, sc, [own, got], [out, out], [pltpu.VMEM((4, rows // 4, cols), f32)], after, "down_split")


def sum_two(sc, own, got, after):
    def kernel(sc, own_ref, got_ref, *rest):
        rest[-1][...] = (own_ref[...] + got_ref[...].astype(f32)).astype(bf16)

    return small(kernel, sc, [own, got], [shape(own.shape, bf16)], [], after, "sum_two")


def lay_down(sc, mine, other, after):
    def kernel(sc, *rest):
        out_ref, total = rest[-2:]
        n = total.shape[2]
        for kind, pieces in ((sc[0], rest[:4]), (1 - sc[0], rest[4:8])):
            for who, piece in zip(whose(kind), pieces):
                total[kind, sc[1] ^ who] = piece[...].astype(f32)
        for c in range(2):
            for m in range(4):
                at = (c * 4 + m) * n
                out_ref[at : at + n, :] = total[c, m]

    n, cols = mine[0].shape
    return small(kernel, sc, [*mine, *other], [shape((8 * n, cols), f32)], [pltpu.VMEM((2, 4, n, cols), f32)], after, "lay_down")[0]


def hold(value, after):
    return pl.pallas_call(
        lambda *refs: None,
        out_shape=shape(value.shape, value.dtype),
        in_specs=[LEFT] * (1 + len(after)),
        out_specs=LEFT,
        input_output_aliases={0: 0},
        cost_estimate=BRIEF,
        compiler_params=pltpu.CompilerParams(vmem_limit_bytes=1 << 20),
        name="hold",
    )(value, *after)


def far_sum(sc, far, near, after):
    def kernel(sc, far_ref, near_ref, *rest):
        rest[-1][...] = (far_ref[...] + jnp.where(sc[0] == 1, near_ref[...].astype(f32), 0.0)).astype(bf16)

    return small(kernel, sc, [far, near], [shape(far.shape, bf16)], [], after, "far_sum")


CORE, SIDE, BACK = 1, 2, 4
rope_base = 10000.0
RUNS = 2


def flip(value, bit, bit1=None):
    count = lax.axis_size("dp")
    bits = (bit, bit if bit1 is None else bit1)
    return lax.ppermute(value, "dp", [(i, i ^ bits[i & 1]) for i in range(count)])


def flip_z(value, bit, where=lambda d, z: True):
    count, depth = lax.axis_size("dp"), lax.axis_size("fsdp")
    pairs = [(d * depth + z, d * depth + (z ^ bit)) for d in range(count) for z in range(depth) if where(d, z)]
    return lax.ppermute(value, ("dp", "fsdp"), pairs)


def home_to_work(value, back=False):
    count, depth = lax.axis_size("dp"), lax.axis_size("fsdp")
    pairs = []
    for d in range(count):
        for z in range(depth):
            there = (d & ~1) | (z & 1), 2 * (d & 1) + (z >> 1)
            pair = (d * depth + z, there[0] * depth + there[1])
            pairs.append(pair[::-1] if back else pair)
    return lax.ppermute(value, ("dp", "fsdp"), pairs)


def place():
    d, z = lax.axis_index("dp"), lax.axis_index("fsdp")
    return d & 1, (d >> 1) & 3, z


def turns(shard):
    far = flip_z(shard, 2)
    return shard, flip_z(shard, 1), far, flip_z(far, 1)


def plane_gather(piece):
    first, second = flip(piece, SIDE, BACK), flip(piece, BACK, SIDE)
    mine = (piece, first, second, flip(first, BACK, SIDE))
    return mine, tuple(flip(p, CORE) for p in mine)


def window(own):
    core, _, _ = place()
    depth = lax.axis_size("fsdp")
    far = lax.ppermute(own, "fsdp", [(z, z + 1) for z in range(0, depth, 2)])
    near = flip(jnp.where(core == 0, own, far), CORE)
    return far, near, own


def unwindow(sc, far, near):
    depth = lax.axis_size("fsdp")
    near = flip(near, CORE)
    far, token = far_sum(sc, far, near, [])
    return near, token, lax.ppermute(far, "fsdp", [(z + 1, z) for z in range(0, depth, 2)])


def over_groups(value):
    bit = 8
    while bit < lax.axis_size("dp"):
        value = (value.astype(f32) + flip(value, bit).astype(f32)).astype(bf16)
        bit *= 2
    return value


def spread(piece):
    return piece, flip(piece, SIDE, BACK), flip(piece, BACK, SIDE), flip(piece, SIDE | BACK)


def across(pieces):
    return tuple(flip(p, CORE) for p in pieces)


def body(tokens, segment_ids, attn_gain, query_weight, key_weight, value_weight, out_weight, ffn_gain, gate_weight, up_weight, down_weight, cotangent):
    core, chip, z = place()
    sc = jnp.stack([core, chip, z]).astype(jnp.int32)
    _, stretch, width = tokens.shape
    rows, depth = query_weight.shape[0], lax.axis_size("fsdp")
    block = 2 * (z & 1) + core
    positions = (block * stretch + jnp.arange(stretch)).astype(f32)
    freq = rope_base ** (-2.0 * jnp.arange(HEAD_DIM // 2, dtype=f32) / HEAD_DIM)
    angle = freq[:, None] * positions[None, :]
    cos, sin = jnp.cos(angle), jnp.sin(angle)

    gains = jnp.stack([attn_gain, ffn_gain]).astype(f32)
    parts_a = turns(pick_first(sc, query_weight, key_weight.T, value_weight.T, out_weight, gains))
    ids = jnp.broadcast_to((segment_ids[0] + 1).astype(bf16), (IDS, stretch))
    tokens = home_to_work(jnp.concatenate([tokens[0].T, ids]))
    piece_b = pick(sc, gate_weight, up_weight, down_weight.T, parts_a[1:2])
    whole_a = stack(sc, parts_a, [piece_b])
    gains = gains_of(whole_a)
    gain_a, gain_f = gains[:1], gains[1:]
    wa = plane_gather(whole_a.reshape(depth * rows, PIECE))
    side_b = flip_z(piece_b, 1)
    far_b = hold(flip_z(piece_b, 2), [wa[0][1], wa[0][2], side_b])
    whole_b = stack(sc, (piece_b, side_b, far_b, flip_z(far_b, 1)), [wa[0][3]])
    first_b, second_b = flip(whole_b, SIDE, BACK), flip(whole_b, BACK, SIDE)

    h_0, a0, q0, own = pre(sc, tokens, gain_a, cos, sin, *wa, [whole_b])
    kv0 = window(own)
    first_b = hold(first_b, [kv0[0], second_b])
    opposite_b = flip(first_b, BACK, SIDE)
    o0, lse0 = attend(q0, kv0)
    wb = whole_b, first_b, second_b, hold(opposite_b, [o0])
    wb = wb, across(wb)
    weights = wa, wb
    cot = home_to_work(cotangent[0].T)
    mixed0, h1_0, b0, gate0, up0, z0, h_1, a1, q1, own = post(False, [], sc, o0, h_0, gain_f, gain_a, cos, sin, own, *weights)
    kv1 = window(own)
    across_0 = across((a0, b0, mixed0, z0))
    o1, lse1 = attend(q1, kv1, across_0)
    mixed1, h1_1, b1, gate1, up1, z1, output = post(True, [cot], sc, o1, h_1, gain_f, gain_a, cos, sin, own, *weights)
    across_1 = across((a1, b1, mixed1, z1))

    gb1, act1, away1, g1, p1, dgain_f1, do = back(True, False, sc, weights, [cot], [gate1, up1, h1_1, gain_f])
    across_2 = across((gb1, away1))
    dq1, three1, far, near, own = attend_back(sc, p1, q1, kv1, lse1, do, cos, sin)
    near, _, far = unwindow(sc, far, near)
    (three1,) = across((three1,))
    tail = [g1, dq1, own, near, far, h_1, gain_a, cos, sin]
    dk1, dv1, one1, dgain_a1, gb0, act0, away0, g1, p0, dgain_f0, do = back(False, False, sc, weights, tail, [gate0, up0, h1_0, gain_f], [three1, *across_2, *across_1])

    away0, gb0_, one1 = across((away0, gb0, one1))
    send_b, keep_b, done = grad_ffn(sc, [b1, b0, across_1[1], across_0[1]], [act1, act0, across_2[1], away0], [])
    got_b = flip(send_b, SIDE, BACK)
    dq0, three0, far, near, own = attend_back(sc, p0, q0, kv0, lse0, do, cos, sin, [one1, done])
    near, done, far = unwindow(sc, far, near)
    send_d, keep_d, done = grad_down(sc, [gb1, gb0, across_2[0], gb0_], [z1, z0, across_1[3], across_0[3]], [done])
    got_d = flip_z(send_d, 1)
    (three0,) = across((three0,))
    tail = [g1, dq0, own, near, far, h_0, gain_a, cos, sin, output]
    dk0, dv0, one0, dgain_a0, leaving = back(False, True, sc, weights, tail, None, [done])
    later_b, own_b, done = sum_first(sc, keep_b, [got_b], [dgain_a0])
    more_b = flip(later_b, BACK, SIDE)
    own = [dq1, dq0, dk1, dk0, dv1, dv0, p1, p0]
    got = [three1, three0, one1, flip(one0, CORE)]
    *send_a, keep_a, done = grad_attention(sc, [a1, a0, across_1[0], across_0[0]], [mixed1, mixed0, across_1[2], across_0[2]], own, got, [dgain_a1, dgain_a0, dgain_f1, dgain_f0], [done])
    got_a = [flip(v, SIDE, BACK) for v in send_a]
    send_d, keep_d, done = sum_third(sc, keep_d, got_d, [done])
    got_d = flip_z(send_d, 2)
    send_b, ring_b, done = sum_second(sc, own_b, [more_b], [done])
    got_b = flip_z(send_b, 1)
    *later_a, own_a, done = sum_first(sc, keep_a, got_a, [done], 2)
    more_a = [flip(v, BACK, SIDE) for v in later_a]
    send_b, ring_b, done = sum_third(sc, ring_b, got_b, [done])
    got_b = flip_z(send_b, 2)
    send_a, ring_a, done = sum_second(sc, own_a, more_a, [done])
    got_a = flip_z(send_a, 1)
    send_d, keep_d, done = down_split(sc, keep_d, got_d, [done])
    got_d = flip(send_d, SIDE, BACK)
    later_d, own_d, done = sum_first(sc, keep_d, [got_d], [done])
    more_d = flip(later_d, BACK, SIDE)
    piece_b, done = sum_two(sc, ring_b, got_b, [done])
    all_b = spread(over_groups(piece_b))
    send_a, ring_a, first = sum_third(sc, ring_a, got_a, [done])
    got_a = flip_z(send_a, 2)
    piece_d, done = sum_two(sc, own_d, more_d, [first])
    all_d = spread(over_groups(piece_d))
    piece_a, done = sum_two(sc, ring_a, got_a, [done])
    all_a = spread(over_groups(piece_a))
    grad_gate, grad_up = lay(sc, all_b, across(all_b), (gate_weight.shape[1],) * 2, [done])
    grad_down_ = lay_down(sc, all_d, across(all_d), [done])
    grad_query, grad_key, grad_value, grad_out, dgains = lay(sc, all_a, across(all_a), (width, KVW, KVW, width), [done])
    leaving = home_to_work(hold(leaving, [first]), back=True)
    output, grad_tokens = leaving[:width].T, leaving[width:].astype(f32).T
    return (output[None], grad_tokens[None], dgains[0], grad_query, grad_key, grad_value, grad_out, dgains[1], grad_gate, grad_up, grad_down_.T)


def solution(mesh):
    wide, rows, shard = P("dp", "fsdp", None), P("dp", "fsdp"), P("fsdp", None)
    in_specs = (wide, rows, P("fsdp"), shard, shard, shard, shard, P("fsdp"), shard, shard, shard, wide)
    out_specs = (wide, wide, P("fsdp"), shard, shard, shard, shard, P("fsdp"), shard, shard, shard)
    return jax.shard_map(body, mesh=mesh, in_specs=in_specs, out_specs=out_specs, check_vma=False)
```

```python
import functools
import jax
import jax.numpy as jnp
from jax import lax
from jax.sharding import PartitionSpec as P
from jax.experimental import pallas as pl
from jax.experimental.pallas import tpu as pltpu

f32, bf16 = jnp.float32, jnp.bfloat16
eps = 1e-05
HEADS, KV_HEADS, HEAD_DIM, GROUP, KVW = 15, 5, 64, 3, 320
IDS = 16
ROWS = 128
PIECE = 384
LIMIT = 58 << 20
WHOLE = pl.BlockSpec(memory_space=pltpu.VMEM)
LEFT = pl.BlockSpec(memory_space=pl.ANY)
SCALARS = pl.BlockSpec(memory_space=pltpu.SMEM)
TOKEN = jax.ShapeDtypeStruct((8, 128), f32)
BRIEF = pl.CostEstimate(flops=1024, bytes_accessed=1024, transcendentals=0)


def contract(a, b, i, j):
    return lax.dot_general(a, b, (((i,), (j,)), ((), ())), preferred_element_type=f32)


def nn(a, b):
    return contract(a, b, 1, 0)


def nt(a, b):
    return contract(a, b, 1, 1)


def tn(a, b):
    return contract(a, b, 0, 0)


def whose(core):
    return 0, 1 + core, 2 - core, 3


def fetch(mine, other, kept, sems, core, chip, only=None, turns=range(4)):
    for j in turns:
        for kind, pieces in ((core, mine), (1 - core, other)):
            at = chip ^ whose(kind)[j]

            def copy():
                pltpu.make_async_copy(pieces[j], kept.at[kind, at], sems.at[kind, at]).start()

            if only is None:
                copy()
            else:
                pl.when(kind == only)(copy)


def leave(kept, out, sem, cols=None):
    if cols is not None:
        kept, out = kept.at[:, cols], out.at[:, cols]
    pltpu.make_async_copy(kept, out, sem).start()


def gone(kepts, outs, sems):
    for i, (kept, out) in enumerate(zip(kepts, outs)):
        pltpu.make_async_copy(kept, out, sems.at[i]).wait()


def arrived(kept, sems, *at):
    pltpu.make_async_copy(kept.at[at], kept.at[at], sems.at[at]).wait()


def normed(x, gain):
    return x * lax.rsqrt(jnp.mean(x * x, axis=-1, keepdims=True) + eps) * gain


def norm_back(x, gain, grad):
    r = lax.rsqrt(jnp.mean(x * x, axis=-1, keepdims=True) + eps)
    hat = x * r
    scaled = grad * gain
    dx = r * (scaled - hat * jnp.mean(scaled * hat, axis=-1, keepdims=True))
    return dx, jnp.sum(grad * hat, axis=0, keepdims=True)


def widened(x):
    return jnp.concatenate([x, jnp.zeros((x.shape[0], PIECE - x.shape[1]), x.dtype)], axis=1)


def rope(u, cos, sin, back):
    heads = u.shape[0] // HEAD_DIM
    half = HEAD_DIM // 2
    out = []
    for h in range(heads):
        u1, u2 = u[h * HEAD_DIM : h * HEAD_DIM + half], u[h * HEAD_DIM + half : (h + 1) * HEAD_DIM]
        if back:
            out += [u1 * cos + u2 * sin, u2 * cos - u1 * sin]
        else:
            out += [u1 * cos - u2 * sin, u2 * cos + u1 * sin]
    return jnp.concatenate(out, axis=0)


def project(state, gain_ref, cos_ref, sin_ref, ids, kept, sems, a_ref, q_ref, kv_ref):
    a = normed(state, gain_ref[...]).astype(bf16)
    a_ref[...] = a
    cos, sin = cos_ref[...], sin_ref[...]
    arrived(kept, sems, 0, 3)
    kv_ref[:KVW, :] = rope(nn(a, kept[0, 3, :, :KVW]).T, cos, sin, False).astype(bf16)
    arrived(kept, sems, 1, 0)
    kv_ref[2 * KVW :, :] = ids
    kv_ref[KVW : 2 * KVW, :] = nn(a, kept[1, 0, :, :KVW]).T.astype(bf16)
    for m in range(3):
        arrived(kept, sems, 0, m)
        q_ref[pl.ds(m * KVW, KVW), :] = rope(nn(a, kept[0, m, :, :KVW]).T, cos, sin, False).astype(bf16)


def pre_kernel(sc, ht_ref, gain_ref, cos_ref, sin_ref, *rest):
    width = ht_ref.shape[0] - IDS
    mine, other = rest[:4], rest[4:8]
    h_ref, a_ref, q_ref, kv_ref, kept, sems = rest[-6:]
    core, chip = sc[0], sc[1]
    fetch(mine, other, kept, sems, core, chip)
    h = ht_ref[:width, :].T
    h_ref[...] = h
    project(h.astype(f32), gain_ref, cos_ref, sin_ref, ht_ref[width:, :], kept, sems, a_ref, q_ref, kv_ref)
    for m in range(1, 4):
        arrived(kept, sems, 1, m)


def scratch_a(width):
    return [pltpu.VMEM((2, 4, width, PIECE), bf16), pltpu.SemaphoreType.DMA((2, 4))]


def shape(s, d):
    return jax.ShapeDtypeStruct(s, d)


def pre(sc, ht, gain, cos, sin, mine_a, other_a, after):
    width, n = ht.shape[0] - IDS, ht.shape[1]
    return pl.pallas_call(
        pre_kernel,
        out_shape=(shape((n, width), bf16), shape((n, width), bf16), shape((width, n), bf16), shape((2 * KVW + IDS, n), bf16)),
        in_specs=[SCALARS] + [WHOLE] * 4 + [LEFT] * (8 + len(after)),
        out_specs=(WHOLE,) * 4,
        scratch_shapes=scratch_a(width),
        cost_estimate=BRIEF,
        compiler_params=pltpu.CompilerParams(vmem_limit_bytes=LIMIT),
        name="pre",
    )(sc, ht, gain, cos, sin, *mine_a, *other_a, *after)


def bias_of(kv):
    keys, n = kv.shape[1], kv.shape[1] // 3
    ids = kv[2 * KVW :, :].astype(f32)
    seg_k, seg_q = ids.T[:, :1], ids[:1, 2 * n :]
    j = lax.broadcasted_iota(jnp.int32, (keys, n), 0)
    i = lax.broadcasted_iota(jnp.int32, (keys, n), 1) + (keys - n)
    return jnp.where((seg_k == seg_q) & (j <= i), 0.0, -1e30).astype(f32)


def window_of(parts, whole):
    n = parts[0].shape[1]
    for w, part in enumerate(parts):
        whole[:, w * n : (w + 1) * n] = part[...]


def attend_kernel(q_ref, kv0, kv1, kv2, *rest):
    o_ref, lse_ref, bias, kv = rest[-4:]
    window_of((kv0, kv1, kv2), kv)
    bias[...] = bias_of(kv)

    def head(e, _):
        row = pl.multiple_of(e * HEAD_DIM, HEAD_DIM)
        k = kv[pl.ds(row, HEAD_DIM), :]
        v = kv[pl.ds(row + KVW, HEAD_DIM), :]
        for g in range(GROUP):
            at = pl.multiple_of((e * GROUP + g) * HEAD_DIM, HEAD_DIM)
            q = q_ref[pl.ds(at, HEAD_DIM), :]
            s = tn(k, q) * HEAD_DIM ** (-0.5) + bias[...]
            top = jnp.max(s, axis=0, keepdims=True)
            expo = jnp.exp(s - top)
            total = jnp.sum(expo, axis=0, keepdims=True)
            probs = (expo * (1.0 / total)).astype(bf16)
            o_ref[pl.ds(at, HEAD_DIM), :] = nn(v, probs).astype(bf16)
            lse_ref[pl.ds(e * GROUP + g, 1), :] = top + jnp.log(total)
        return 0

    lax.fori_loop(0, KV_HEADS, head, 0)


def attend(q, kvs, after=()):
    width, n = q.shape
    return pl.pallas_call(
        attend_kernel,
        out_shape=(shape((width, n), bf16), shape((HEADS, n), f32)),
        in_specs=[WHOLE] * 4 + [LEFT] * len(after),
        out_specs=(WHOLE,) * 2,
        scratch_shapes=[pltpu.VMEM((3 * n, n), f32), pltpu.VMEM((2 * KVW + IDS, 3 * n), bf16)],
        cost_estimate=BRIEF,
        compiler_params=pltpu.CompilerParams(vmem_limit_bytes=24 << 20),
        name="attend",
    )(q, *kvs, *after)


def attend_back_kernel(sc, p_ref, q_ref, kv0, kv1, kv2, lse_ref, do_ref, cos_ref, sin_ref, *rest):
    dq_ref, three_ref, far_ref, near_ref, own_ref, bias, kv, dqs = rest[-8:]
    n = q_ref.shape[1]
    window_of((kv0, kv1, kv2), kv)
    bias[...] = bias_of(kv)
    scale = HEAD_DIM ** (-0.5)

    def head(e, _):
        row = pl.multiple_of(e * HEAD_DIM, HEAD_DIM)
        k = kv[pl.ds(row, HEAD_DIM), :]
        v = kv[pl.ds(row + KVW, HEAD_DIM), :]
        dk = dv = None
        for g in range(GROUP):
            at = pl.multiple_of((e * GROUP + g) * HEAD_DIM, HEAD_DIM)
            q = q_ref[pl.ds(at, HEAD_DIM), :]
            do = do_ref[pl.ds(at, HEAD_DIM), :]
            s = tn(k, q) * scale + bias[...]
            probs = jnp.exp(s - lse_ref[pl.ds(e * GROUP + g, 1), :])
            dp = tn(v, do)
            inner = jnp.sum(probs * dp, axis=0, keepdims=True)
            ds = (probs * (dp - inner)).astype(bf16)
            dvg, dkg = nt(do, probs.astype(bf16)), nt(q, ds)
            dv, dk = (dvg, dkg) if g == 0 else (dv + dvg, dk + dkg)
            dqs[pl.ds(at, HEAD_DIM), :] = nn(k, ds)
        for at, grad in ((row, dk * scale), (row + KVW, dv)):
            far_ref[pl.ds(at, HEAD_DIM), :] = grad[:, :n]
            near_ref[pl.ds(at, HEAD_DIM), :] = grad[:, n : 2 * n].astype(bf16)
            own_ref[pl.ds(at, HEAD_DIM), :] = grad[:, 2 * n :]
        return 0

    lax.fori_loop(0, KV_HEADS, head, 0)
    cos, sin = cos_ref[...] * scale, sin_ref[...] * scale
    for m in range(3):
        dq = widened(rope(dqs[m * KVW : (m + 1) * KVW, :], cos, sin, True).T.astype(bf16))
        dq_ref[m] = dq
        three_ref[m] = jnp.where(sc[0] == 0, p_ref[m], dq)


def attend_back(sc, p, q, kvs, lse, do, cos, sin, after=()):
    width, n = q.shape
    block = (2 * KVW, n)
    return pl.pallas_call(
        attend_back_kernel,
        out_shape=(shape((3, n, PIECE), bf16), shape((3, n, PIECE), bf16), shape(block, f32), shape(block, bf16), shape(block, f32)),
        in_specs=[SCALARS] + [WHOLE] * 9 + [LEFT] * len(after),
        out_specs=(WHOLE,) * 5,
        scratch_shapes=[pltpu.VMEM((3 * n, n), f32), pltpu.VMEM((2 * KVW + IDS, 3 * n), bf16), pltpu.VMEM((width, n), f32)],
        cost_estimate=BRIEF,
        compiler_params=pltpu.CompilerParams(vmem_limit_bytes=32 << 20),
        name="attend_back",
    )(sc, p, q, *kvs, lse, do, cos, sin, *after)


def down_rows(kind, chip, width):
    return jnp.minimum((kind * 4 + chip) * ROWS, width - ROWS)


def fetch_down(mine, other, wb, wd, sem_d, core, chip):
    rows, width = wb.shape[3], wd.shape[1]
    last = width % ROWS
    for kind, pieces in ((core, mine), (1 - core, other)):
        for who, piece in zip(whose(kind), pieces):
            at = kind * 4 + (chip ^ who)

            @pl.when(at < width // ROWS)
            def _():
                into = wd.at[:, pl.ds(pl.multiple_of(at * ROWS, ROWS), ROWS)]
                pltpu.make_async_copy(piece.at[:, rows:], into, sem_d).start()

            @pl.when(at == width // ROWS)
            def _():
                pltpu.make_async_copy(piece.at[:, rows + ROWS - last :], wd.at[:, width - last :], sem_d).start()


def fetch_both(mine, other, wb, sem_b, core, chip, turns=range(4)):
    rows = wb.shape[3]
    fetch([p.at[:, :rows] for p in mine], [p.at[:, :rows] for p in other], wb, sem_b, core, chip, turns=turns)


def whole(wb, c, m):
    _, rows, n = wb.shape[2:]
    return wb[c, m].reshape(4 * rows, n)


def arrived_down(wd, sem_d):
    pltpu.make_async_copy(wd, wd, sem_d).wait()


def scratch_ffn(width, n):
    return [
        pltpu.VMEM((2, 4, 4, width // 4, n), bf16),
        pltpu.SemaphoreType.DMA((2, 4)),
        pltpu.VMEM((4, width, n), bf16),
        pltpu.SemaphoreType.DMA,
    ]


def post_kernel(last, after, sc, ot_ref, h_ref, gain_ref, gain_a, cos_ref, sin_ref, *rest):
    mine_a, other_a, mine_b, other_b = rest[:4], rest[4:8], rest[8:12], rest[12:16]
    ids_ref, rest = rest[16], rest[17 + after :]
    hbm, next_ref = rest[:6], rest[6]
    more, rest = rest[7 : 7 + (0 if last else 3)], rest[7 + (0 if last else 3) :]
    wa, sem_a, wb, sem_b, wd, sem_d, *stage, sem_out = rest
    o_ref, h1_ref, b_ref, gate_ref, up_ref, z_ref = stage
    core, chip = sc[0], sc[1]
    fetch(mine_a, other_a, wa, sem_a, core, chip, 1)
    fetch_both(mine_b, other_b, wb, sem_b, core, chip, (0, 1))
    fetch_down(mine_b, other_b, wb, wd, sem_d, core, chip)
    fetch_both(mine_b, other_b, wb, sem_b, core, chip, (2, 3))
    if not last:
        fetch(mine_a, other_a, wa, sem_a, core, chip, 0)
    o = ot_ref[...].T
    o_ref[...] = o
    leave(o_ref, hbm[0], sem_out.at[0])
    for m in range(1, 4):
        arrived(wa, sem_a, 1, m)
    h1 = h_ref[...].astype(f32) + jnp.concatenate([nn(o, wa[1, m, :, :KVW]) for m in range(1, 4)], axis=1)
    h1_ref[...] = h1
    leave(h1_ref, hbm[1], sem_out.at[1])
    b = normed(h1, gain_ref[...]).astype(bf16)
    b_ref[...] = b
    leave(b_ref, hbm[2], sem_out.at[2])
    n = wb.shape[4]
    total = h1
    for i in range(4):
        m = chip ^ i
        cols = pl.ds(pl.multiple_of(m * n, 128), n)
        arrived(wb, sem_b, 0, m)
        gate = nn(b, whole(wb, 0, m))
        arrived(wb, sem_b, 1, m)
        up = nn(b, whole(wb, 1, m))
        gate_ref[:, cols] = gate.astype(bf16)
        up_ref[:, cols] = up.astype(bf16)
        z = (gate / (1.0 + jnp.exp(-gate)) * up).astype(bf16)
        z_ref[:, cols] = z
        for j in range(3, 6):
            leave(stage[j], hbm[j], sem_out.at[j], cols)
        if i == 0:
            arrived_down(wd, sem_d)
        total = total + nt(z, wd[m])
    next_ref[...] = total.astype(bf16).T if last else total
    if last:
        arrived(wa, sem_a, 1, 0)
    else:
        project(total, gain_a, cos_ref, sin_ref, ids_ref[2 * KVW :, :], wa, sem_a, *more)
    gone(stage, hbm, sem_out)


def post(last, after, sc, ot, h, gain, gain_a, cos, sin, kv, wa, wb):
    width, n = ot.shape
    hidden = wb[0][0].shape[2] * 4
    outs = [shape((n, width), bf16), shape((n, width), f32), shape((n, width), bf16)] + [shape((n, hidden), bf16)] * 3
    outs += [shape((width, n), bf16) if last else shape((n, width), f32)]
    if not last:
        outs += [shape((n, width), bf16), shape((width, n), bf16), shape((2 * KVW + IDS, n), bf16)]
    return pl.pallas_call(
        functools.partial(post_kernel, last, len(after)),
        out_shape=tuple(outs),
        in_specs=[SCALARS] + [WHOLE] * 6 + [LEFT] * 16 + [WHOLE] + [LEFT] * len(after),
        out_specs=(LEFT,) * 6 + (WHOLE,) * (len(outs) - 6),
        scratch_shapes=scratch_a(width) + scratch_ffn(width, hidden // 4) + [pltpu.VMEM(o.shape, o.dtype) for o in outs[:6]] + [pltpu.SemaphoreType.DMA((6,))],
        cost_estimate=BRIEF,
        compiler_params=pltpu.CompilerParams(vmem_limit_bytes=LIMIT),
        name="post",
    )(sc, ot, h, gain, gain_a, cos, sin, *wa[0], *wa[1], *wb[0], *wb[1], kv, *after)


def ffn_back(state, core, chip, refs, weights, stage, sems, hbm):
    gate_ref, up_ref, h1_ref, gain_ref, gb_ref, keep_ref, send_ref, g1_ref, p_ref, dgain_ref, do_ref = refs
    wa, sem_a, wb, sem_b, wd, sem_d = weights
    gb = state.astype(bf16)
    gb_ref[...] = gb
    leave(gb_ref, hbm[3], sems.at[3])
    n = wb.shape[4]
    first = core == 0
    arrived_down(wd, sem_d)
    db = None
    for i in range(4):
        m = chip ^ i
        cols = pl.ds(pl.multiple_of(m * n, 128), n)
        dz = nn(gb, wd[m])
        if i == 0:
            for j in range(2):
                pltpu.make_async_copy(hbm[j], stage[j], sems.at[j]).wait()
        gate, up = gate_ref[:, cols].astype(f32), up_ref[:, cols].astype(f32)
        sig = 1.0 / (1.0 + jnp.exp(-gate))
        dup = (dz * (gate * sig)).astype(bf16)
        dgate = (dz * up * (sig * (1.0 + gate * (1.0 - sig)))).astype(bf16)
        keep_ref[:, cols] = jnp.where(first, dgate, dup)
        send_ref[:, cols] = jnp.where(first, dup, dgate)
        leave(keep_ref, hbm[4], sems.at[4], cols)
        leave(send_ref, hbm[5], sems.at[5], cols)
        arrived(wb, sem_b, 0, m)
        part = nt(dgate, whole(wb, 0, m))
        arrived(wb, sem_b, 1, m)
        part = part + nt(dup, whole(wb, 1, m))
        db = part if i == 0 else db + part
    pltpu.make_async_copy(hbm[2], stage[2], sems.at[2]).wait()
    dx, dgain = norm_back(h1_ref[...], gain_ref[...], db)
    dgain_ref[...] = dgain
    g1 = state + dx
    g1_ref[...] = g1
    leave(g1_ref, hbm[6], sems.at[6])
    low = g1.astype(bf16)
    do = None
    for p in range(3):
        part = low[:, p * KVW : (p + 1) * KVW]
        p_ref[p] = widened(part)
        arrived(wa, sem_a, 1, p + 1)
        part = nt(wa[1, p + 1, :, :KVW], part)
        do = part if p == 0 else do + part
    do_ref[...] = do.astype(bf16)


def finish_a(wa, sem_a, *left):
    for at in left:
        arrived(wa, sem_a, *at)


def query_back(dq_ref, wa, sem_a):
    da = None
    for m in range(3):
        arrived(wa, sem_a, 0, m)
        part = nt(dq_ref[m, :, :KVW], wa[0, m, :, :KVW])
        da = part if m == 0 else da + part
    return da


def project_back(da, own_ref, near_ref, far_ref, core, cos_ref, sin_ref, dk_ref, dv_ref, one_ref, h, gain, wa, sem_a):
    cos, sin = cos_ref[...], sin_ref[...]
    grad = own_ref[...] + far_ref[...].astype(f32) + jnp.where(core == 0, near_ref[...].astype(f32), 0.0)
    dk = rope(grad[:KVW], cos, sin, True).T.astype(bf16)
    dv = grad[KVW:].T.astype(bf16)
    dk_ref[...] = widened(dk)
    dv_ref[...] = widened(dv)
    one_ref[...] = widened(jnp.where(core == 0, dv, dk))
    arrived(wa, sem_a, 0, 3)
    arrived(wa, sem_a, 1, 0)
    da = da + nt(dk, wa[0, 3, :, :KVW]) + nt(dv, wa[1, 0, :, :KVW])
    return norm_back(h, gain, da)


def back_kernel(start, end, after, sc, *rest):
    rest = list(rest)

    def take(n):
        out = rest[:n]
        del rest[:n]
        return out

    core, chip = sc[0], sc[1]
    mine_a, other_a = take(4), take(4)
    if not end:
        mine_b, other_b = take(4), take(4)
    if start:
        (g_ref,) = take(1)
    else:
        g1_in, dq_ref, own_ref, near_ref, far_ref, h_ref, gain_a, cos_ref, sin_ref = take(9)
        if end:
            (last_ref,) = take(1)
    if not end:
        ins = take(4)
    take(after)
    if not start:
        dk_ref, dv_ref, one_ref, dgain_a = take(4)
    if end:
        (g_out,) = take(1)
    else:
        outs = take(7)
    wa, sem_a = take(2)
    if not start:
        fetch(mine_a, other_a, wa, sem_a, core, chip, 0)
        fetch(mine_a, other_a, wa, sem_a, core, chip, 1)
    if not end:
        wb, sem_b, wd, sem_d = take(4)
        stage, (sems,) = take(7), take(1)
        hbm = [*ins[:3], *outs[:4]]
        fetch_down(mine_b, other_b, wb, wd, sem_d, core, chip)
        for j in range(3):
            pltpu.make_async_copy(hbm[j], stage[j], sems.at[j]).start()
        fetch_both(mine_b, other_b, wb, sem_b, core, chip)
    if start:
        fetch(mine_a, other_a, wa, sem_a, core, chip, 1)
    if start:
        state = g_ref[...].T.astype(f32)
    else:
        da = query_back(dq_ref, wa, sem_a)
        dx, dgain = project_back(da, own_ref, near_ref, far_ref, core, cos_ref, sin_ref, dk_ref, dv_ref, one_ref, h_ref[...].astype(f32), gain_a[...], wa, sem_a)
        dgain_a[...] = dgain
        state = g1_in[...] + dx
    if end:
        width = state.shape[1]
        g_out[:width, :] = last_ref[...]
        g_out[width:, :] = state.astype(bf16).T
        finish_a(wa, sem_a, (1, 1), (1, 2), (1, 3))
    else:
        refs = (*stage[:3], ins[3], *stage[3:], *outs[4:])
        ffn_back(state, core, chip, refs, (wa, sem_a, wb, sem_b, wd, sem_d), stage, sems, hbm)
        gone(stage[3:], hbm[3:], sems.at[pl.ds(3, 4)])
        if start:
            finish_a(wa, sem_a, (1, 0))


def back(start, end, sc, weights, tail, ffn, after=()):
    wa, wb = weights
    width = wa[0][0].shape[0]
    args = [sc, *wa[0], *wa[1]]
    specs = [SCALARS] + [LEFT] * 8
    scratch = scratch_a(width)
    if not end:
        args += [*wb[0], *wb[1]]
        specs += [LEFT] * 8
        scratch += scratch_ffn(width, wb[0][0].shape[2])
    args += list(tail)
    specs += [WHOLE] * len(tail)
    n = tail[0].shape[1 if start else 0]
    outs = []
    if not end:
        args += list(ffn)
        specs += [LEFT] * 3 + [WHOLE]
    if not start:
        outs += [shape((n, PIECE), bf16)] * 3 + [shape((1, width), f32)]
    if end:
        outs += [shape((2 * width, n), bf16)]
    else:
        hidden = ffn[0].shape[1]
        outs += [shape((n, width), bf16), shape((n, hidden), bf16), shape((n, hidden), bf16)]
        outs += [shape((n, width), f32), shape((3, n, PIECE), bf16), shape((1, width), f32), shape((width, n), bf16)]
    out_specs = [WHOLE] * len(outs)
    if not end:
        at = 0 if start else 4
        out_specs[at : at + 4] = [LEFT] * 4
        scratch += [pltpu.VMEM(x.shape, x.dtype) for x in (*ffn[:3], *outs[at : at + 4])]
        scratch += [pltpu.SemaphoreType.DMA((7,))]
    args += list(after)
    specs += [LEFT] * len(after)
    return pl.pallas_call(
        functools.partial(back_kernel, start, end, len(after)),
        out_shape=tuple(outs),
        in_specs=specs,
        out_specs=tuple(out_specs),
        scratch_shapes=scratch,
        cost_estimate=BRIEF,
        compiler_params=pltpu.CompilerParams(vmem_limit_bytes=LIMIT),
        name="back_end" if end else ("back_start" if start else "back_join"),
    )(*args)


def by_turn(core, chip):
    one = 1 + core
    return chip ^ one, chip ^ 3, chip, chip ^ (3 - one)


def turned(dst, blocks):
    n = blocks[0].shape[0]
    for i, block in enumerate(blocks):
        dst[:, i * n : (i + 1) * n] = block[...].T


def grad_ffn_kernel(sc, *rest):
    lefts, rights = rest[:4], rest[4:8]
    send_ref, keep_ref, token_ref, left, right = rest[-5:]
    token_ref[...] = jnp.zeros_like(token_ref)
    core, chip = sc[0], sc[1]
    n, cols = rights[0].shape[0], right.shape[1]
    turned(left, lefts)
    for i, m in enumerate(by_turn(core, chip)):
        at = pl.multiple_of(m * cols, 128)
        for j, block in enumerate(rights):
            right[j * n : (j + 1) * n, :] = block[:, pl.ds(at, cols)]
        out = send_ref if i < 2 else keep_ref
        out[i % 2] = nn(left[...], right[...]).astype(bf16)


def grad_ffn(sc, lefts, rights, after):
    n, width = lefts[0].shape
    cols = rights[0].shape[1] // 4
    out = shape((2, width, cols), bf16)
    return pl.pallas_call(
        grad_ffn_kernel,
        out_shape=(out, out, TOKEN),
        in_specs=[SCALARS] + [WHOLE] * 8 + [LEFT] * len(after),
        out_specs=(WHOLE,) * 3,
        scratch_shapes=[pltpu.VMEM((width, 4 * n), bf16), pltpu.VMEM((4 * n, cols), bf16)],
        cost_estimate=BRIEF,
        compiler_params=pltpu.CompilerParams(vmem_limit_bytes=LIMIT),
        name="grad_ffn",
    )(sc, *lefts, *rights, *after)


def grad_down_kernel(sc, *rest):
    lefts, rights = rest[:4], rest[4:8]
    send_ref, keep_ref, token_ref, left, right = rest[-5:]
    token_ref[...] = jnp.zeros_like(token_ref)
    n, (_, half, cols) = rights[0].shape[0], send_ref.shape
    turned(left, lefts)
    rows = pl.ds(pl.multiple_of(sc[0] * half, half), half)
    like = sc[2] & 1
    for h in range(2):
        for out, parity in ((send_ref, 1 - like), (keep_ref, like)):
            at = pl.multiple_of((2 * h + parity) * cols, 128)
            for j, block in enumerate(rights):
                right[j * n : (j + 1) * n, :] = block[:, pl.ds(at, cols)]
            out[h] = nn(left[rows, :], right[...]).astype(out.dtype)


def grad_down(sc, lefts, rights, after):
    n, width = lefts[0].shape
    cols = rights[0].shape[1] // 4
    block = (2, width // 2, cols)
    return pl.pallas_call(
        grad_down_kernel,
        out_shape=(shape(block, bf16), shape(block, bf16), TOKEN),
        in_specs=[SCALARS] + [WHOLE] * 8 + [LEFT] * len(after),
        out_specs=(WHOLE,) * 3,
        scratch_shapes=[pltpu.VMEM((width, 4 * n), bf16), pltpu.VMEM((4 * n, cols), bf16)],
        cost_estimate=BRIEF,
        compiler_params=pltpu.CompilerParams(vmem_limit_bytes=LIMIT),
        name="grad_down",
    )(sc, *lefts, *rights, *after)


def grad_attention_kernel(first, sc, *rest):
    a_refs, o_refs, rest = rest[:4], rest[4:8], rest[8:]
    queries, keys, values, outs, threes, ones = (rest[i : i + 2] for i in range(0, 12, 2))
    gain_a, gain_f = (rest[i : i + 2] for i in (12, 14))
    *outs_of, token_ref, left, right = rest[-5:]
    token_ref[...] = jnp.zeros_like(token_ref)
    core, chip = sc[0], sc[1]
    n, width = a_refs[0].shape
    turned(left.at[0], a_refs)
    gains = [g[0][...] + g[1][...] for g in (gain_a, gain_f)]
    gains = jnp.concatenate([*gains, jnp.zeros((6, width), f32)], axis=0).T
    gains = jnp.concatenate([gains, jnp.zeros((width, PIECE - KVW - 8), f32)], axis=1).astype(bf16)

    def fill(at, of_three, own_three, own_one, single):
        for j in range(2):
            for i in range(3):
                right[of_three + i, j * n : (j + 1) * n, :] = own_three[j][i]
                right[of_three + i, (j + 2) * n : (j + 3) * n, :] = threes[j][i]
            right[single, j * n : (j + 1) * n, :] = own_one[j][...]
            right[single, (j + 2) * n : (j + 3) * n, :] = ones[j][...]

    @pl.when(core == 0)
    def _():
        fill(0, 0, queries, keys, 3)

    @pl.when(core == 1)
    def _():
        turned(left.at[1], o_refs)
        fill(0, 1, outs, values, 0)

    for out, m in zip(outs_of, by_turn(core, chip)[first : first + 2]):
        which = jnp.where(m > 0, core, 0)
        out[...] = nn(left[which], right[m]).astype(bf16)
        out[:, KVW:] = gains


def grad_attention(first, sc, a, o, own, got, gains, after):
    n, width = a[0].shape
    out = shape((width, PIECE), bf16)
    return pl.pallas_call(
        functools.partial(grad_attention_kernel, first),
        out_shape=(out, out, TOKEN),
        in_specs=[SCALARS] + [WHOLE] * 24 + [LEFT] * len(after),
        out_specs=(WHOLE,) * 3,
        scratch_shapes=[pltpu.VMEM((2, width, 4 * n), bf16), pltpu.VMEM((4, 4 * n, PIECE), bf16)],
        cost_estimate=BRIEF,
        compiler_params=pltpu.CompilerParams(vmem_limit_bytes=LIMIT),
        name="grad_attention",
    )(sc, *a, *o, *own, *got, *gains, *after)


def lay_kernel(count, sc, *rest):
    token_ref = rest[-2]
    token_ref[...] = jnp.zeros_like(token_ref)
    rest = (*rest[:-2], rest[-1])
    mine, other, outs, kept = rest[:4], rest[4:8], rest[-1 - count : -1], rest[-1]
    core, chip = sc[0], sc[1]
    for kind, pieces in ((core, mine), (1 - core, other)):
        for who, piece in zip(whose(kind), pieces):
            kept[kind, chip ^ who] = piece[...]
    n = sum(o.shape[1] for o in outs[: 4 if len(outs) > 2 else 2]) // 8
    cols = [jnp.concatenate([kept[c, m, :, :n].astype(f32) for m in range(4)], axis=1) for c in range(2)]
    if len(outs) == 2:
        outs[0][...] = cols[0]
        outs[1][...] = cols[1]
    else:
        outs[0][...] = cols[0][:, : 3 * n]
        outs[1][...] = cols[0][:, 3 * n :]
        outs[2][...] = cols[1][:, :n]
        outs[3][...] = cols[1][:, n:]
        gains = kept[0, 0, :, n : n + 8].astype(f32) + kept[1, 0, :, n : n + 8].astype(f32)
        outs[4][...] = gains.T[:2]


def lay(sc, mine, other, widths, after):
    rows, n = mine[0].shape
    outs = tuple(shape((rows, w), f32) for w in widths)
    if len(widths) > 2:
        outs += (shape((2, rows), f32),)
    return pl.pallas_call(
        functools.partial(lay_kernel, len(outs)),
        out_shape=(*outs, TOKEN),
        in_specs=[SCALARS] + [WHOLE] * 8 + [LEFT] * len(after),
        out_specs=(WHOLE,) * (len(outs) + 1),
        scratch_shapes=[pltpu.VMEM((2, 4, rows, n), bf16)],
        cost_estimate=BRIEF,
        compiler_params=pltpu.CompilerParams(vmem_limit_bytes=24 << 20),
        name="lay",
    )(sc, *mine, *other, *after)


def pick_first_kernel(sc, q_ref, k_ref, v_ref, o_ref, gain_ref, out_ref, wide, tall, sem):
    rows = out_ref.shape[0]
    which = sc[0] * 4 + sc[1]

    def bring(source, into, first, last):
        @pl.when((which >= first) & (which <= last))
        def _():
            copy = pltpu.make_async_copy(source, into, sem)
            copy.start()
            copy.wait()

    bring(q_ref, wide, 0, 2)
    bring(k_ref, tall, 3, 3)
    bring(v_ref, tall, 4, 4)
    bring(o_ref, wide, 5, 7)
    pad = jnp.zeros((6, rows), f32)
    gains = jnp.concatenate([gain_ref[...], pad], axis=0).T.astype(bf16)
    rest = jnp.zeros((rows, PIECE - KVW - 8), bf16)
    for m in range(4):

        @pl.when((which == m) | (which == (m + 5 if m < 3 else 4)))
        def _():
            piece = wide[:, m * KVW : (m + 1) * KVW] if m < 3 else tall[...].T
            out_ref[...] = jnp.concatenate([piece, gains, rest], axis=1)


def pick_first(sc, query, key, value, out, gains):
    return pl.pallas_call(
        pick_first_kernel,
        out_shape=shape((query.shape[0], PIECE), bf16),
        in_specs=[SCALARS] + [LEFT] * 4 + [WHOLE],
        out_specs=WHOLE,
        scratch_shapes=[pltpu.VMEM(query.shape, bf16), pltpu.VMEM(key.shape, bf16), pltpu.SemaphoreType.DMA],
        cost_estimate=BRIEF,
        compiler_params=pltpu.CompilerParams(vmem_limit_bytes=LIMIT),
        name="pick_first",
    )(sc, query, key, value, out, gains)


def pick_kernel(sc, gate, up, down, *rest):
    out_ref, sems = rest[-2:]
    rows, cols = out_ref.shape[0] - ROWS, out_ref.shape[1]
    into = out_ref.at[:rows]
    start = pl.multiple_of(down_rows(sc[0], sc[1], down.shape[0]), 64)
    copy = pltpu.make_async_copy(down.at[pl.ds(start, ROWS), :], out_ref.at[rows:], sems.at[1])
    copy.start()
    at = pl.ds(pl.multiple_of(sc[1] * cols, 128), cols)
    for c, source in ((0, gate), (1, up)):

        @pl.when(sc[0] == c)
        def _():
            pltpu.make_async_copy(source.at[:, at], into, sems.at[0]).start()

    pltpu.make_async_copy(gate.at[:, at], into, sems.at[0]).wait()
    copy.wait()


def pick(sc, gate, up, down, after):
    return pl.pallas_call(
        pick_kernel,
        out_shape=shape((gate.shape[0] + ROWS, gate.shape[1] // 4), bf16),
        in_specs=[SCALARS] + [LEFT] * (3 + len(after)),
        out_specs=WHOLE,
        scratch_shapes=[pltpu.SemaphoreType.DMA((2,))],
        cost_estimate=BRIEF,
        compiler_params=pltpu.CompilerParams(vmem_limit_bytes=16 << 20),
        name="pick",
    )(sc, gate, up, down, *after)


def gains_kernel(first_ref, out_ref):
    for j in range(4):
        n = first_ref.shape[1]
        out_ref[:, j * n : (j + 1) * n] = first_ref[j, :, KVW : KVW + 8].astype(f32).T[:2]


def gains_of(first):
    return pl.pallas_call(
        gains_kernel,
        out_shape=shape((2, 4 * first.shape[1]), f32),
        in_specs=[WHOLE],
        out_specs=WHOLE,
        cost_estimate=BRIEF,
        compiler_params=pltpu.CompilerParams(vmem_limit_bytes=16 << 20),
        name="gains",
    )(first)


def stack_kernel(sc, *rest):
    parts, out_ref, sems = rest[:4], rest[-2], rest[-1]
    copies = [pltpu.make_async_copy(p, out_ref.at[sc[2] ^ s], sems.at[s]) for s, p in enumerate(parts)]
    for copy in copies:
        copy.start()
    for copy in copies:
        copy.wait()


def stack(sc, parts, after=()):
    return pl.pallas_call(
        stack_kernel,
        out_shape=shape((4,) + parts[0].shape, parts[0].dtype),
        in_specs=[SCALARS] + [LEFT] * (4 + len(after)),
        out_specs=WHOLE,
        scratch_shapes=[pltpu.SemaphoreType.DMA((4,))],
        cost_estimate=BRIEF,
        compiler_params=pltpu.CompilerParams(vmem_limit_bytes=16 << 20),
        name="stack",
    )(sc, *parts, *after)


def small(kernel, sc, args, outs, scratch, after, name):
    def with_token(*refs):
        at = len(refs) - len(scratch) - 1
        refs[at][...] = jnp.zeros_like(refs[at])
        kernel(*refs[:at], *refs[at + 1 :])

    return pl.pallas_call(
        with_token,
        out_shape=(*outs, TOKEN),
        in_specs=[SCALARS] + [WHOLE] * len(args) + [LEFT] * len(after),
        out_specs=(WHOLE,) * (len(outs) + 1),
        scratch_shapes=scratch,
        cost_estimate=BRIEF,
        compiler_params=pltpu.CompilerParams(vmem_limit_bytes=32 << 20),
        name=name,
    )(sc, *args, *after)


def sum_first(sc, keep, got, after, parts=1):
    def kernel(sc, *refs):
        rest = list(refs)

        def both(arrays):
            if len(arrays) == 2:
                return rest.pop(0), rest.pop(0)
            ref = rest.pop(0)
            return ref.at[0], ref.at[1]

        (own_kept, later_kept), (own_got, later_got) = both(keep), both(got)
        own_ref = rest[-1]
        for i, later_ref in enumerate(rest[-1 - parts : -1]):
            n = later_ref.shape[0]
            rows = slice(i * n, (i + 1) * n)
            later_ref[...] = (later_kept[rows].astype(f32) + later_got[rows].astype(f32)).astype(bf16)
        own_ref[...] = own_kept[...].astype(f32) + own_got[...].astype(f32)

    rows, cols = keep[0].shape[-2:]
    outs = [shape((rows // parts, cols), bf16)] * parts + [shape((rows, cols), f32)]
    return small(kernel, sc, [*keep, *got], outs, [], after, "sum_first")


def sum_second(sc, own, got, after):
    def kernel(sc, own_ref, *rest):
        gots, (send_ref, keep_ref, total) = rest[: len(got)], rest[-3:]
        n = total.shape[1]
        for j in range(4):
            part, at = divmod(j * n, gots[0].shape[0])
            total[j] = own_ref[j * n : (j + 1) * n, :] + gots[part][at : at + n, :].astype(f32)
        like = sc[2] & 1
        for h in range(2):
            send_ref[h] = total[2 * h + 1 - like].astype(bf16)
            keep_ref[h] = total[2 * h + like]

    rows, cols = own.shape
    part = (rows // 4, cols)
    outs = [shape((2,) + part, bf16), shape((2,) + part, f32)]
    return small(kernel, sc, [own, *got], outs, [pltpu.VMEM((4,) + part, f32)], after, "sum_second")


def sum_third(sc, keep, got, after):
    def kernel(sc, keep_ref, got_ref, *rest):
        send_ref, own_ref = rest[-2:]
        h = sc[2] >> 1
        send_ref[...] = (keep_ref[1 - h].astype(f32) + got_ref[1 - h].astype(f32)).astype(bf16)
        own_ref[...] = keep_ref[h].astype(f32) + got_ref[h].astype(f32)

    part = keep.shape[1:]
    return small(kernel, sc, [keep, got], [shape(part, bf16), shape(part, f32)], [], after, "sum_third")


def down_split(sc, own, got, after):
    def kernel(sc, own_ref, got_ref, *rest):
        send_ref, kept_ref, total = rest[-3:]
        n = total.shape[1]
        for m in range(4):
            rows = slice(m * n, (m + 1) * n)
            total[m] = own_ref[rows, :] + got_ref[rows, :].astype(f32)
        for i, m in enumerate(by_turn(sc[0], sc[1])):
            out = send_ref if i < 2 else kept_ref
            out[i % 2] = total[m].astype(bf16)

    rows, cols = own.shape
    out = shape((2, rows // 4, cols), bf16)
    return small(kernel, sc, [own, got], [out, out], [pltpu.VMEM((4, rows // 4, cols), f32)], after, "down_split")


def sum_two(sc, own, got, after):
    def kernel(sc, own_ref, got_ref, *rest):
        rest[-1][...] = (own_ref[...] + got_ref[...].astype(f32)).astype(bf16)

    return small(kernel, sc, [own, got], [shape(own.shape, bf16)], [], after, "sum_two")


def lay_down(sc, mine, other, after):
    def kernel(sc, *rest):
        out_ref, total = rest[-2:]
        n = total.shape[2]
        for kind, pieces in ((sc[0], rest[:4]), (1 - sc[0], rest[4:8])):
            for who, piece in zip(whose(kind), pieces):
                total[kind, sc[1] ^ who] = piece[...].astype(f32)
        for c in range(2):
            for m in range(4):
                at = (c * 4 + m) * n
                out_ref[at : at + n, :] = total[c, m]

    n, cols = mine[0].shape
    return small(kernel, sc, [*mine, *other], [shape((8 * n, cols), f32)], [pltpu.VMEM((2, 4, n, cols), f32)], after, "lay_down")


def hold(value, after):
    return pl.pallas_call(
        lambda *refs: None,
        out_shape=shape(value.shape, value.dtype),
        in_specs=[LEFT] * (1 + len(after)),
        out_specs=LEFT,
        input_output_aliases={0: 0},
        cost_estimate=BRIEF,
        compiler_params=pltpu.CompilerParams(vmem_limit_bytes=1 << 20),
        name="hold",
    )(value, *after)


def far_sum(sc, far, near, after):
    def kernel(sc, far_ref, near_ref, *rest):
        rest[-1][...] = (far_ref[...] + jnp.where(sc[0] == 1, near_ref[...].astype(f32), 0.0)).astype(bf16)

    return small(kernel, sc, [far, near], [shape(far.shape, bf16)], [], after, "far_sum")


def depart(sc, both, after):
    def kernel(sc, both_ref, *rest):
        out_ref, grad_ref = rest[-2:]
        n = out_ref.shape[0]
        out_ref[...] = both_ref[:n, :]
        grad_ref[...] = both_ref[n:, :].astype(f32)

    block = (both.shape[0] // 2, both.shape[1])
    return small(kernel, sc, [both], [shape(block, bf16), shape(block, f32)], [], after, "depart")


CORE, SIDE, BACK = 1, 2, 4
rope_base = 10000.0
RUNS = 2


def flip(value, bit, bit1=None):
    count = lax.axis_size("dp")
    bits = (bit, bit if bit1 is None else bit1)
    return lax.ppermute(value, "dp", [(i, i ^ bits[i & 1]) for i in range(count)])


def flip_z(value, bit, where=lambda d, z: True):
    count, depth = lax.axis_size("dp"), lax.axis_size("fsdp")
    pairs = [(d * depth + z, d * depth + (z ^ bit)) for d in range(count) for z in range(depth) if where(d, z)]
    return lax.ppermute(value, ("dp", "fsdp"), pairs)


def home_to_work(value, back=False):
    count, depth = lax.axis_size("dp"), lax.axis_size("fsdp")
    pairs = []
    for d in range(count):
        for z in range(depth):
            there = (d & ~1) | (z & 1), 2 * (d & 1) + (z >> 1)
            pair = (d * depth + z, there[0] * depth + there[1])
            pairs.append(pair[::-1] if back else pair)
    return lax.ppermute(value, ("dp", "fsdp"), pairs)


def place():
    d, z = lax.axis_index("dp"), lax.axis_index("fsdp")
    return d & 1, (d >> 1) & 3, z


def turns(shard):
    far = flip_z(shard, 2)
    return shard, flip_z(shard, 1), far, flip_z(far, 1)


def plane_gather(piece):
    first, second = flip(piece, SIDE, BACK), flip(piece, BACK, SIDE)
    mine = (piece, first, second, flip(first, BACK, SIDE))
    return mine, tuple(flip(p, CORE) for p in mine)


def window(own):
    core, _, _ = place()
    depth = lax.axis_size("fsdp")
    far = lax.ppermute(own, "fsdp", [(z, z + 1) for z in range(0, depth, 2)])
    near = flip(jnp.where(core == 0, own, far), CORE)
    return far, near, own


def unwindow(sc, far, near):
    depth = lax.axis_size("fsdp")
    near = flip(near, CORE)
    far, token = far_sum(sc, far, near, [])
    return near, token, lax.ppermute(far, "fsdp", [(z + 1, z) for z in range(0, depth, 2)])


def over_groups(value):
    bit = 8
    while bit < lax.axis_size("dp"):
        value = (value.astype(f32) + flip(value, bit).astype(f32)).astype(bf16)
        bit *= 2
    return value


def spread(piece):
    return piece, flip(piece, SIDE, BACK), flip(piece, BACK, SIDE), flip(piece, SIDE | BACK)


def across(pieces):
    return tuple(flip(p, CORE) for p in pieces)


def body(tokens, segment_ids, attn_gain, query_weight, key_weight, value_weight, out_weight, ffn_gain, gate_weight, up_weight, down_weight, cotangent):
    core, chip, z = place()
    sc = jnp.stack([core, chip, z]).astype(jnp.int32)
    _, stretch, width = tokens.shape
    rows, depth = query_weight.shape[0], lax.axis_size("fsdp")
    block = 2 * (z & 1) + core
    positions = (block * stretch + jnp.arange(stretch)).astype(f32)
    freq = rope_base ** (-2.0 * jnp.arange(HEAD_DIM // 2, dtype=f32) / HEAD_DIM)
    angle = freq[:, None] * positions[None, :]
    cos, sin = jnp.cos(angle), jnp.sin(angle)

    gains = jnp.stack([attn_gain, ffn_gain]).astype(f32)
    parts_a = turns(pick_first(sc, query_weight, key_weight.T, value_weight.T, out_weight, gains))
    ids = jnp.broadcast_to((segment_ids[0] + 1).astype(bf16), (IDS, stretch))
    tokens = home_to_work(jnp.concatenate([tokens[0].T, ids]))
    piece_b = pick(sc, gate_weight, up_weight, down_weight.T, parts_a[1:2])
    whole_a = stack(sc, parts_a, [piece_b])
    gains = gains_of(whole_a)
    gain_a, gain_f = gains[:1], gains[1:]
    wa = plane_gather(whole_a.reshape(depth * rows, PIECE))
    side_b = flip_z(piece_b, 1)
    far_b = hold(flip_z(piece_b, 2), [wa[0][1], wa[0][2], side_b])
    whole_b = stack(sc, (piece_b, side_b, far_b, flip_z(far_b, 1)), [wa[0][3]])
    first_b, second_b = flip(whole_b, SIDE, BACK), flip(whole_b, BACK, SIDE)

    h_0, a0, q0, own = pre(sc, tokens, gain_a, cos, sin, *wa, [whole_b])
    kv0 = window(own)
    first_b = hold(first_b, [kv0[0], second_b])
    opposite_b = flip(first_b, BACK, SIDE)
    o0, lse0 = attend(q0, kv0)
    wb = whole_b, first_b, second_b, hold(opposite_b, [o0])
    wb = wb, across(wb)
    weights = wa, wb
    cot = home_to_work(cotangent[0].T)
    mixed0, h1_0, b0, gate0, up0, z0, h_1, a1, q1, own = post(False, [], sc, o0, h_0, gain_f, gain_a, cos, sin, own, *weights)
    kv1 = window(own)
    across_0 = across((a0, b0, mixed0, z0))
    o1, lse1 = attend(q1, kv1, across_0)
    mixed1, h1_1, b1, gate1, up1, z1, output = post(True, [cot], sc, o1, h_1, gain_f, gain_a, cos, sin, own, *weights)
    across_1 = across((a1, b1, mixed1, z1))

    gb1, act1, away1, g1, p1, dgain_f1, do = back(True, False, sc, weights, [cot], [gate1, up1, h1_1, gain_f])
    across_2 = across((gb1, away1))
    dq1, three1, far, near, own = attend_back(sc, p1, q1, kv1, lse1, do, cos, sin)
    near, _, far = unwindow(sc, far, near)
    (three1,) = across((three1,))
    tail = [g1, dq1, own, near, far, h_1, gain_a, cos, sin]
    dk1, dv1, one1, dgain_a1, gb0, act0, away0, g1, p0, dgain_f0, do = back(False, False, sc, weights, tail, [gate0, up0, h1_0, gain_f], [three1, *across_2, *across_1])

    away0, gb0_, one1 = across((away0, gb0, one1))
    send_b, keep_b, done = grad_ffn(sc, [b1, b0, across_1[1], across_0[1]], [act1, act0, across_2[1], away0], [])
    got_b = flip(send_b, SIDE, BACK)
    dq0, three0, far, near, own = attend_back(sc, p0, q0, kv0, lse0, do, cos, sin, [one1, done])
    near, done, far = unwindow(sc, far, near)
    send_d, keep_d, done = grad_down(sc, [gb1, gb0, across_2[0], gb0_], [z1, z0, across_1[3], across_0[3]], [done])
    got_d = flip_z(send_d, 1)
    (three0,) = across((three0,))
    tail = [g1, dq0, own, near, far, h_0, gain_a, cos, sin, output]
    dk0, dv0, one0, dgain_a0, leaving = back(False, True, sc, weights, tail, None, [done])
    later_b, own_b, done = sum_first(sc, [keep_b], [got_b], [dgain_a0])
    more_b = flip(later_b, BACK, SIDE)
    own = [dq1, dq0, dk1, dk0, dv1, dv0, p1, p0]
    got = [three1, three0, one1, flip(one0, CORE)]
    args = [a1, a0, across_1[0], across_0[0]], [mixed1, mixed0, across_1[2], across_0[2]], own, got, [dgain_a1, dgain_a0, dgain_f1, dgain_f0]
    *send_a, done = grad_attention(0, sc, *args, [done])
    got_a = [flip(v, SIDE, BACK) for v in send_a]
    send_d, keep_d, done = sum_third(sc, keep_d, got_d, [done])
    got_d = flip_z(send_d, 2)
    send_b, ring_b, done = sum_second(sc, own_b, [more_b], [done])
    got_b = flip_z(send_b, 1)
    *keep_a, done = grad_attention(2, sc, *args, [done])
    *later_a, own_a, done = sum_first(sc, keep_a, got_a, [done], 2)
    more_a = [flip(v, BACK, SIDE) for v in later_a]
    send_b, ring_b, done = sum_third(sc, ring_b, got_b, [done])
    got_b = flip_z(send_b, 2)
    send_a, ring_a, done = sum_second(sc, own_a, more_a, [done])
    got_a = flip_z(send_a, 1)
    send_d, keep_d, done = down_split(sc, keep_d, got_d, [done])
    got_d = flip(send_d, SIDE, BACK)
    later_d, own_d, done = sum_first(sc, [keep_d], [got_d], [done])
    more_d = flip(later_d, BACK, SIDE)
    piece_b, done = sum_two(sc, ring_b, got_b, [done])
    all_b = spread(over_groups(piece_b))
    send_a, ring_a, first = sum_third(sc, ring_a, got_a, [done])
    got_a = flip_z(send_a, 2)
    piece_d, done = sum_two(sc, own_d, more_d, [first])
    all_d = spread(over_groups(piece_d))
    piece_a, done = sum_two(sc, ring_a, got_a, [done])
    all_a = spread(over_groups(piece_a))
    grad_gate, grad_up, done = lay(sc, all_b, across(all_b), (gate_weight.shape[1],) * 2, [done])
    leaving = home_to_work(hold(leaving, [first]), back=True)
    output, grad_tokens, done = depart(sc, leaving, [done])
    grad_down_, done = lay_down(sc, all_d, across(all_d), [done])
    grad_query, grad_key, grad_value, grad_out, dgains, _ = lay(sc, all_a, across(all_a), (width, KVW, KVW, width), [done])
    output, grad_tokens = output.T, grad_tokens.T
    return (output[None], grad_tokens[None], dgains[0], grad_query, grad_key, grad_value, grad_out, dgains[1], grad_gate, grad_up, grad_down_.T)


def solution(mesh):
    wide, rows, shard = P("dp", "fsdp", None), P("dp", "fsdp"), P("fsdp", None)
    in_specs = (wide, rows, P("fsdp"), shard, shard, shard, shard, P("fsdp"), shard, shard, shard, wide)
    out_specs = (wide, wide, P("fsdp"), shard, shard, shard, shard, P("fsdp"), shard, shard, shard)
    return jax.shard_map(body, mesh=mesh, in_specs=in_specs, out_specs=out_specs, check_vma=False)
```

```python
import functools
import jax
import jax.numpy as jnp
from jax import lax
from jax.sharding import PartitionSpec as P
from jax.experimental import pallas as pl
from jax.experimental.pallas import tpu as pltpu

f32, bf16 = jnp.float32, jnp.bfloat16
eps = 1e-05
HEADS, KV_HEADS, HEAD_DIM, GROUP, KVW = 15, 5, 64, 3, 320
IDS = 16
ROWS = 128
PIECE = 384
LIMIT = 58 << 20
WHOLE = pl.BlockSpec(memory_space=pltpu.VMEM)
LEFT = pl.BlockSpec(memory_space=pl.ANY)
SCALARS = pl.BlockSpec(memory_space=pltpu.SMEM)
TOKEN = jax.ShapeDtypeStruct((8, 128), f32)
BRIEF = pl.CostEstimate(flops=1024, bytes_accessed=1024, transcendentals=0)


def contract(a, b, i, j):
    return lax.dot_general(a, b, (((i,), (j,)), ((), ())), preferred_element_type=f32)


def nn(a, b):
    return contract(a, b, 1, 0)


def nt(a, b):
    return contract(a, b, 1, 1)


def tn(a, b):
    return contract(a, b, 0, 0)


def whose(core):
    return 0, 1 + core, 2 - core, 3


def fetch(mine, other, kept, sems, core, chip, only=None, turns=range(4)):
    for j in turns:
        for kind, pieces in ((core, mine), (1 - core, other)):
            at = chip ^ whose(kind)[j]

            def copy():
                pltpu.make_async_copy(pieces[j], kept.at[kind, at], sems.at[kind, at]).start()

            if only is None:
                copy()
            else:
                pl.when(kind == only)(copy)


def leave(kept, out, sem, cols=None):
    if cols is not None:
        kept, out = kept.at[:, cols], out.at[:, cols]
    pltpu.make_async_copy(kept, out, sem).start()


def gone(kepts, outs, sems):
    for i, (kept, out) in enumerate(zip(kepts, outs)):
        pltpu.make_async_copy(kept, out, sems.at[i]).wait()


def arrived(kept, sems, *at):
    pltpu.make_async_copy(kept.at[at], kept.at[at], sems.at[at]).wait()


def normed(x, gain):
    return x * lax.rsqrt(jnp.mean(x * x, axis=-1, keepdims=True) + eps) * gain


def norm_back(x, gain, grad):
    r = lax.rsqrt(jnp.mean(x * x, axis=-1, keepdims=True) + eps)
    hat = x * r
    scaled = grad * gain
    dx = r * (scaled - hat * jnp.mean(scaled * hat, axis=-1, keepdims=True))
    return dx, jnp.sum(grad * hat, axis=0, keepdims=True)


def widened(x):
    return jnp.concatenate([x, jnp.zeros((x.shape[0], PIECE - x.shape[1]), x.dtype)], axis=1)


def rope(u, cos, sin, back):
    heads = u.shape[0] // HEAD_DIM
    half = HEAD_DIM // 2
    out = []
    for h in range(heads):
        u1, u2 = u[h * HEAD_DIM : h * HEAD_DIM + half], u[h * HEAD_DIM + half : (h + 1) * HEAD_DIM]
        if back:
            out += [u1 * cos + u2 * sin, u2 * cos - u1 * sin]
        else:
            out += [u1 * cos - u2 * sin, u2 * cos + u1 * sin]
    return jnp.concatenate(out, axis=0)


def project(state, gain_ref, cos_ref, sin_ref, ids, kept, sems, a_ref, q_ref, kv_ref):
    a = normed(state, gain_ref[...]).astype(bf16)
    a_ref[...] = a
    cos, sin = cos_ref[...], sin_ref[...]
    arrived(kept, sems, 0, 3)
    kv_ref[:KVW, :] = rope(nn(a, kept[0, 3, :, :KVW]).T, cos, sin, False).astype(bf16)
    arrived(kept, sems, 1, 0)
    kv_ref[2 * KVW :, :] = ids
    kv_ref[KVW : 2 * KVW, :] = nn(a, kept[1, 0, :, :KVW]).T.astype(bf16)
    for m in range(3):
        arrived(kept, sems, 0, m)
        q_ref[pl.ds(m * KVW, KVW), :] = rope(nn(a, kept[0, m, :, :KVW]).T, cos, sin, False).astype(bf16)


def pre_kernel(sc, ht_ref, gain_ref, cos_ref, sin_ref, *rest):
    width = ht_ref.shape[0] - IDS
    mine, other = rest[:4], rest[4:8]
    h_ref, a_ref, q_ref, kv_ref, kept, sems = rest[-6:]
    core, chip = sc[0], sc[1]
    fetch(mine, other, kept, sems, core, chip)
    h = ht_ref[:width, :].T
    h_ref[...] = h
    project(h.astype(f32), gain_ref, cos_ref, sin_ref, ht_ref[width:, :], kept, sems, a_ref, q_ref, kv_ref)
    for m in range(1, 4):
        arrived(kept, sems, 1, m)


def scratch_a(width):
    return [pltpu.VMEM((2, 4, width, PIECE), bf16), pltpu.SemaphoreType.DMA((2, 4))]


def shape(s, d):
    return jax.ShapeDtypeStruct(s, d)


def pre(sc, ht, gain, cos, sin, mine_a, other_a, after):
    width, n = ht.shape[0] - IDS, ht.shape[1]
    return pl.pallas_call(
        pre_kernel,
        out_shape=(shape((n, width), bf16), shape((n, width), bf16), shape((width, n), bf16), shape((2 * KVW + IDS, n), bf16)),
        in_specs=[SCALARS] + [WHOLE] * 4 + [LEFT] * (8 + len(after)),
        out_specs=(WHOLE,) * 4,
        scratch_shapes=scratch_a(width),
        cost_estimate=BRIEF,
        compiler_params=pltpu.CompilerParams(vmem_limit_bytes=LIMIT),
        name="pre",
    )(sc, ht, gain, cos, sin, *mine_a, *other_a, *after)


def bias_of(kv):
    keys, n = kv.shape[1], kv.shape[1] // 3
    ids = kv[2 * KVW :, :].astype(f32)
    seg_k, seg_q = ids.T[:, :1], ids[:1, 2 * n :]
    j = lax.broadcasted_iota(jnp.int32, (keys, n), 0)
    i = lax.broadcasted_iota(jnp.int32, (keys, n), 1) + (keys - n)
    return jnp.where((seg_k == seg_q) & (j <= i), 0.0, -1e30).astype(f32)


def window_of(parts, whole):
    n = parts[0].shape[1]
    for w, part in enumerate(parts):
        whole[:, w * n : (w + 1) * n] = part[...]


def attend_kernel(q_ref, kv0, kv1, kv2, *rest):
    o_ref, lse_ref, bias, kv = rest[-4:]
    window_of((kv0, kv1, kv2), kv)
    bias[...] = bias_of(kv)

    def head(e, _):
        row = pl.multiple_of(e * HEAD_DIM, HEAD_DIM)
        k = kv[pl.ds(row, HEAD_DIM), :]
        v = kv[pl.ds(row + KVW, HEAD_DIM), :]
        for g in range(GROUP):
            at = pl.multiple_of((e * GROUP + g) * HEAD_DIM, HEAD_DIM)
            q = q_ref[pl.ds(at, HEAD_DIM), :]
            s = tn(k, q) * HEAD_DIM ** (-0.5) + bias[...]
            top = jnp.max(s, axis=0, keepdims=True)
            expo = jnp.exp(s - top)
            total = jnp.sum(expo, axis=0, keepdims=True)
            probs = (expo * (1.0 / total)).astype(bf16)
            o_ref[pl.ds(at, HEAD_DIM), :] = nn(v, probs).astype(bf16)
            lse_ref[pl.ds(e * GROUP + g, 1), :] = top + jnp.log(total)
        return 0

    lax.fori_loop(0, KV_HEADS, head, 0)


def attend(q, kvs, after=()):
    width, n = q.shape
    return pl.pallas_call(
        attend_kernel,
        out_shape=(shape((width, n), bf16), shape((HEADS, n), f32)),
        in_specs=[WHOLE] * 4 + [LEFT] * len(after),
        out_specs=(WHOLE,) * 2,
        scratch_shapes=[pltpu.VMEM((3 * n, n), f32), pltpu.VMEM((2 * KVW + IDS, 3 * n), bf16)],
        cost_estimate=BRIEF,
        compiler_params=pltpu.CompilerParams(vmem_limit_bytes=24 << 20),
        name="attend",
    )(q, *kvs, *after)


def attend_back_kernel(sc, p_ref, q_ref, kv0, kv1, kv2, lse_ref, do_ref, cos_ref, sin_ref, *rest):
    dq_ref, three_ref, far_ref, near_ref, own_ref, bias, kv, dqs = rest[-8:]
    n = q_ref.shape[1]
    window_of((kv0, kv1, kv2), kv)
    bias[...] = bias_of(kv)
    scale = HEAD_DIM ** (-0.5)

    def head(e, _):
        row = pl.multiple_of(e * HEAD_DIM, HEAD_DIM)
        k = kv[pl.ds(row, HEAD_DIM), :]
        v = kv[pl.ds(row + KVW, HEAD_DIM), :]
        dk = dv = None
        for g in range(GROUP):
            at = pl.multiple_of((e * GROUP + g) * HEAD_DIM, HEAD_DIM)
            q = q_ref[pl.ds(at, HEAD_DIM), :]
            do = do_ref[pl.ds(at, HEAD_DIM), :]
            s = tn(k, q) * scale + bias[...]
            probs = jnp.exp(s - lse_ref[pl.ds(e * GROUP + g, 1), :])
            dp = tn(v, do)
            inner = jnp.sum(probs * dp, axis=0, keepdims=True)
            ds = (probs * (dp - inner)).astype(bf16)
            dvg, dkg = nt(do, probs.astype(bf16)), nt(q, ds)
            dv, dk = (dvg, dkg) if g == 0 else (dv + dvg, dk + dkg)
            dqs[pl.ds(at, HEAD_DIM), :] = nn(k, ds)
        for at, grad in ((row, dk * scale), (row + KVW, dv)):
            far_ref[pl.ds(at, HEAD_DIM), :] = grad[:, :n]
            near_ref[pl.ds(at, HEAD_DIM), :] = grad[:, n : 2 * n].astype(bf16)
            own_ref[pl.ds(at, HEAD_DIM), :] = grad[:, 2 * n :]
        return 0

    lax.fori_loop(0, KV_HEADS, head, 0)
    cos, sin = cos_ref[...] * scale, sin_ref[...] * scale
    for m in range(3):
        dq = widened(rope(dqs[m * KVW : (m + 1) * KVW, :], cos, sin, True).T.astype(bf16))
        dq_ref[m] = dq
        three_ref[m] = jnp.where(sc[0] == 0, p_ref[m], dq)


def attend_back(sc, p, q, kvs, lse, do, cos, sin, after=()):
    width, n = q.shape
    block = (2 * KVW, n)
    return pl.pallas_call(
        attend_back_kernel,
        out_shape=(shape((3, n, PIECE), bf16), shape((3, n, PIECE), bf16), shape(block, f32), shape(block, bf16), shape(block, f32)),
        in_specs=[SCALARS] + [WHOLE] * 9 + [LEFT] * len(after),
        out_specs=(WHOLE,) * 5,
        scratch_shapes=[pltpu.VMEM((3 * n, n), f32), pltpu.VMEM((2 * KVW + IDS, 3 * n), bf16), pltpu.VMEM((width, n), f32)],
        cost_estimate=BRIEF,
        compiler_params=pltpu.CompilerParams(vmem_limit_bytes=32 << 20),
        name="attend_back",
    )(sc, p, q, *kvs, lse, do, cos, sin, *after)


def down_rows(kind, chip, width):
    return jnp.minimum((kind * 4 + chip) * ROWS, width - ROWS)


def fetch_down(mine, other, wb, wd, sem_d, core, chip):
    rows, width = wb.shape[3], wd.shape[1]
    last = width % ROWS
    for kind, pieces in ((core, mine), (1 - core, other)):
        for who, piece in zip(whose(kind), pieces):
            at = kind * 4 + (chip ^ who)

            @pl.when(at < width // ROWS)
            def _():
                into = wd.at[:, pl.ds(pl.multiple_of(at * ROWS, ROWS), ROWS)]
                pltpu.make_async_copy(piece.at[:, rows:], into, sem_d).start()

            @pl.when(at == width // ROWS)
            def _():
                pltpu.make_async_copy(piece.at[:, rows + ROWS - last :], wd.at[:, width - last :], sem_d).start()


def fetch_both(mine, other, wb, sem_b, core, chip, turns=range(4)):
    rows = wb.shape[3]
    fetch([p.at[:, :rows] for p in mine], [p.at[:, :rows] for p in other], wb, sem_b, core, chip, turns=turns)


def whole(wb, c, m):
    _, rows, n = wb.shape[2:]
    return wb[c, m].reshape(4 * rows, n)


def arrived_down(wd, sem_d):
    pltpu.make_async_copy(wd, wd, sem_d).wait()


def scratch_ffn(width, n):
    return [
        pltpu.VMEM((2, 4, 4, width // 4, n), bf16),
        pltpu.SemaphoreType.DMA((2, 4)),
        pltpu.VMEM((4, width, n), bf16),
        pltpu.SemaphoreType.DMA,
    ]


def post_kernel(last, after, sc, ot_ref, h_ref, gain_ref, gain_a, cos_ref, sin_ref, *rest):
    mine_a, other_a, mine_b, other_b = rest[:4], rest[4:8], rest[8:12], rest[12:16]
    ids_ref, rest = rest[16], rest[17 + after :]
    hbm, next_ref = rest[:6], rest[6]
    more, rest = rest[7 : 7 + (0 if last else 3)], rest[7 + (0 if last else 3) :]
    wa, sem_a, wb, sem_b, wd, sem_d, *stage, sem_out = rest
    o_ref, h1_ref, b_ref, gate_ref, up_ref, z_ref = stage
    core, chip = sc[0], sc[1]
    fetch(mine_a, other_a, wa, sem_a, core, chip, 1)
    fetch_both(mine_b, other_b, wb, sem_b, core, chip, (0, 1))
    fetch_down(mine_b, other_b, wb, wd, sem_d, core, chip)
    fetch_both(mine_b, other_b, wb, sem_b, core, chip, (2, 3))
    if not last:
        fetch(mine_a, other_a, wa, sem_a, core, chip, 0)
    o = ot_ref[...].T
    o_ref[...] = o
    leave(o_ref, hbm[0], sem_out.at[0])
    for m in range(1, 4):
        arrived(wa, sem_a, 1, m)
    h1 = h_ref[...].astype(f32) + jnp.concatenate([nn(o, wa[1, m, :, :KVW]) for m in range(1, 4)], axis=1)
    h1_ref[...] = h1
    leave(h1_ref, hbm[1], sem_out.at[1])
    b = normed(h1, gain_ref[...]).astype(bf16)
    b_ref[...] = b
    leave(b_ref, hbm[2], sem_out.at[2])
    n = wb.shape[4]
    total = h1
    for i in range(4):
        m = chip ^ i
        cols = pl.ds(pl.multiple_of(m * n, 128), n)
        arrived(wb, sem_b, 0, m)
        gate = nn(b, whole(wb, 0, m))
        arrived(wb, sem_b, 1, m)
        up = nn(b, whole(wb, 1, m))
        gate_ref[:, cols] = gate.astype(bf16)
        up_ref[:, cols] = up.astype(bf16)
        z = (gate / (1.0 + jnp.exp(-gate)) * up).astype(bf16)
        z_ref[:, cols] = z
        for j in range(3, 6):
            leave(stage[j], hbm[j], sem_out.at[j], cols)
        if i == 0:
            arrived_down(wd, sem_d)
        total = total + nt(z, wd[m])
    next_ref[...] = total.astype(bf16).T if last else total
    if last:
        arrived(wa, sem_a, 1, 0)
    else:
        project(total, gain_a, cos_ref, sin_ref, ids_ref[2 * KVW :, :], wa, sem_a, *more)
    gone(stage, hbm, sem_out)


def post(last, after, sc, ot, h, gain, gain_a, cos, sin, kv, wa, wb):
    width, n = ot.shape
    hidden = wb[0][0].shape[2] * 4
    outs = [shape((n, width), bf16), shape((n, width), f32), shape((n, width), bf16)] + [shape((n, hidden), bf16)] * 3
    outs += [shape((width, n), bf16) if last else shape((n, width), f32)]
    if not last:
        outs += [shape((n, width), bf16), shape((width, n), bf16), shape((2 * KVW + IDS, n), bf16)]
    return pl.pallas_call(
        functools.partial(post_kernel, last, len(after)),
        out_shape=tuple(outs),
        in_specs=[SCALARS] + [WHOLE] * 6 + [LEFT] * 16 + [WHOLE] + [LEFT] * len(after),
        out_specs=(LEFT,) * 6 + (WHOLE,) * (len(outs) - 6),
        scratch_shapes=scratch_a(width) + scratch_ffn(width, hidden // 4) + [pltpu.VMEM(o.shape, o.dtype) for o in outs[:6]] + [pltpu.SemaphoreType.DMA((6,))],
        cost_estimate=BRIEF,
        compiler_params=pltpu.CompilerParams(vmem_limit_bytes=LIMIT),
        name="post",
    )(sc, ot, h, gain, gain_a, cos, sin, *wa[0], *wa[1], *wb[0], *wb[1], kv, *after)


def ffn_back(state, core, chip, refs, weights, stage, sems, hbm):
    gate_ref, up_ref, h1_ref, gain_ref, gb_ref, keep_ref, send_ref, g1_ref, p_ref, dgain_ref, do_ref = refs
    wa, sem_a, wb, sem_b, wd, sem_d = weights
    gb = state.astype(bf16)
    gb_ref[...] = gb
    leave(gb_ref, hbm[3], sems.at[3])
    n = wb.shape[4]
    first = core == 0
    arrived_down(wd, sem_d)
    db = None
    for i in range(4):
        m = chip ^ i
        cols = pl.ds(pl.multiple_of(m * n, 128), n)
        dz = nn(gb, wd[m])
        if i == 0:
            for j in range(2):
                pltpu.make_async_copy(hbm[j], stage[j], sems.at[j]).wait()
        gate, up = gate_ref[:, cols].astype(f32), up_ref[:, cols].astype(f32)
        sig = 1.0 / (1.0 + jnp.exp(-gate))
        dup = (dz * (gate * sig)).astype(bf16)
        dgate = (dz * up * (sig * (1.0 + gate * (1.0 - sig)))).astype(bf16)
        keep_ref[:, cols] = jnp.where(first, dgate, dup)
        send_ref[:, cols] = jnp.where(first, dup, dgate)
        leave(keep_ref, hbm[4], sems.at[4], cols)
        leave(send_ref, hbm[5], sems.at[5], cols)
        arrived(wb, sem_b, 0, m)
        part = nt(dgate, whole(wb, 0, m))
        arrived(wb, sem_b, 1, m)
        part = part + nt(dup, whole(wb, 1, m))
        db = part if i == 0 else db + part
    pltpu.make_async_copy(hbm[2], stage[2], sems.at[2]).wait()
    dx, dgain = norm_back(h1_ref[...], gain_ref[...], db)
    dgain_ref[...] = dgain
    g1 = state + dx
    g1_ref[...] = g1
    leave(g1_ref, hbm[6], sems.at[6])
    low = g1.astype(bf16)
    do = None
    for p in range(3):
        part = low[:, p * KVW : (p + 1) * KVW]
        p_ref[p] = widened(part)
        arrived(wa, sem_a, 1, p + 1)
        part = nt(wa[1, p + 1, :, :KVW], part)
        do = part if p == 0 else do + part
    do_ref[...] = do.astype(bf16)


def finish_a(wa, sem_a, *left):
    for at in left:
        arrived(wa, sem_a, *at)


def query_back(dq_ref, wa, sem_a):
    da = None
    for m in range(3):
        arrived(wa, sem_a, 0, m)
        part = nt(dq_ref[m, :, :KVW], wa[0, m, :, :KVW])
        da = part if m == 0 else da + part
    return da


def project_back(da, own_ref, near_ref, far_ref, core, cos_ref, sin_ref, dk_ref, dv_ref, one_ref, h, gain, wa, sem_a):
    cos, sin = cos_ref[...], sin_ref[...]
    grad = own_ref[...] + far_ref[...].astype(f32) + jnp.where(core == 0, near_ref[...].astype(f32), 0.0)
    dk = rope(grad[:KVW], cos, sin, True).T.astype(bf16)
    dv = grad[KVW:].T.astype(bf16)
    dk_ref[...] = widened(dk)
    dv_ref[...] = widened(dv)
    one_ref[...] = widened(jnp.where(core == 0, dv, dk))
    arrived(wa, sem_a, 0, 3)
    arrived(wa, sem_a, 1, 0)
    da = da + nt(dk, wa[0, 3, :, :KVW]) + nt(dv, wa[1, 0, :, :KVW])
    return norm_back(h, gain, da)


def back_kernel(start, end, after, sc, *rest):
    rest = list(rest)

    def take(n):
        out = rest[:n]
        del rest[:n]
        return out

    core, chip = sc[0], sc[1]
    mine_a, other_a = take(4), take(4)
    if not end:
        mine_b, other_b = take(4), take(4)
    if start:
        (g_ref,) = take(1)
    else:
        g1_in, dq_ref, own_ref, near_ref, far_ref, h_ref, gain_a, cos_ref, sin_ref = take(9)
        if end:
            (last_ref,) = take(1)
    if not end:
        ins = take(4)
    take(after)
    if not start:
        dk_ref, dv_ref, one_ref, dgain_a = take(4)
    if end:
        (g_out,) = take(1)
    else:
        outs = take(7)
    wa, sem_a = take(2)
    if not start:
        fetch(mine_a, other_a, wa, sem_a, core, chip, 0)
        fetch(mine_a, other_a, wa, sem_a, core, chip, 1)
    if not end:
        wb, sem_b, wd, sem_d = take(4)
        stage, (sems,) = take(7), take(1)
        hbm = [*ins[:3], *outs[:4]]
        fetch_down(mine_b, other_b, wb, wd, sem_d, core, chip)
        for j in range(3):
            pltpu.make_async_copy(hbm[j], stage[j], sems.at[j]).start()
        fetch_both(mine_b, other_b, wb, sem_b, core, chip)
    if start:
        fetch(mine_a, other_a, wa, sem_a, core, chip, 1)
    if start:
        state = g_ref[...].T.astype(f32)
    else:
        da = query_back(dq_ref, wa, sem_a)
        dx, dgain = project_back(da, own_ref, near_ref, far_ref, core, cos_ref, sin_ref, dk_ref, dv_ref, one_ref, h_ref[...].astype(f32), gain_a[...], wa, sem_a)
        dgain_a[...] = dgain
        state = g1_in[...] + dx
    if end:
        width = state.shape[1]
        g_out[:width, :] = last_ref[...]
        g_out[width:, :] = state.astype(bf16).T
        finish_a(wa, sem_a, (1, 1), (1, 2), (1, 3))
    else:
        refs = (*stage[:3], ins[3], *stage[3:], *outs[4:])
        ffn_back(state, core, chip, refs, (wa, sem_a, wb, sem_b, wd, sem_d), stage, sems, hbm)
        gone(stage[3:], hbm[3:], sems.at[pl.ds(3, 4)])
        if start:
            finish_a(wa, sem_a, (1, 0))


def back(start, end, sc, weights, tail, ffn, after=()):
    wa, wb = weights
    width = wa[0][0].shape[0]
    args = [sc, *wa[0], *wa[1]]
    specs = [SCALARS] + [LEFT] * 8
    scratch = scratch_a(width)
    if not end:
        args += [*wb[0], *wb[1]]
        specs += [LEFT] * 8
        scratch += scratch_ffn(width, wb[0][0].shape[2])
    args += list(tail)
    specs += [WHOLE] * len(tail)
    n = tail[0].shape[1 if start else 0]
    outs = []
    if not end:
        args += list(ffn)
        specs += [LEFT] * 3 + [WHOLE]
    if not start:
        outs += [shape((n, PIECE), bf16)] * 3 + [shape((1, width), f32)]
    if end:
        outs += [shape((2 * width, n), bf16)]
    else:
        hidden = ffn[0].shape[1]
        outs += [shape((n, width), bf16), shape((n, hidden), bf16), shape((n, hidden), bf16)]
        outs += [shape((n, width), f32), shape((3, n, PIECE), bf16), shape((1, width), f32), shape((width, n), bf16)]
    out_specs = [WHOLE] * len(outs)
    if not end:
        at = 0 if start else 4
        out_specs[at : at + 4] = [LEFT] * 4
        scratch += [pltpu.VMEM(x.shape, x.dtype) for x in (*ffn[:3], *outs[at : at + 4])]
        scratch += [pltpu.SemaphoreType.DMA((7,))]
    args += list(after)
    specs += [LEFT] * len(after)
    return pl.pallas_call(
        functools.partial(back_kernel, start, end, len(after)),
        out_shape=tuple(outs),
        in_specs=specs,
        out_specs=tuple(out_specs),
        scratch_shapes=scratch,
        cost_estimate=BRIEF,
        compiler_params=pltpu.CompilerParams(vmem_limit_bytes=LIMIT),
        name="back_end" if end else ("back_start" if start else "back_join"),
    )(*args)


def by_turn(core, chip):
    one = 1 + core
    return chip ^ one, chip ^ 3, chip, chip ^ (3 - one)


def turned(dst, blocks):
    n = blocks[0].shape[0]
    for i, block in enumerate(blocks):
        dst[:, i * n : (i + 1) * n] = block[...].T


def grad_ffn_kernel(sc, *rest):
    lefts, rights = rest[:4], rest[4:8]
    send_ref, keep_ref, token_ref, left, right = rest[-5:]
    token_ref[...] = jnp.zeros_like(token_ref)
    core, chip = sc[0], sc[1]
    n, cols = rights[0].shape[0], right.shape[1]
    turned(left, lefts)
    for i, m in enumerate(by_turn(core, chip)):
        at = pl.multiple_of(m * cols, 128)
        for j, block in enumerate(rights):
            right[j * n : (j + 1) * n, :] = block[:, pl.ds(at, cols)]
        out = send_ref if i < 2 else keep_ref
        out[i % 2] = nn(left[...], right[...]).astype(bf16)


def grad_ffn(sc, lefts, rights, after):
    n, width = lefts[0].shape
    cols = rights[0].shape[1] // 4
    out = shape((2, width, cols), bf16)
    return pl.pallas_call(
        grad_ffn_kernel,
        out_shape=(out, out, TOKEN),
        in_specs=[SCALARS] + [WHOLE] * 8 + [LEFT] * len(after),
        out_specs=(WHOLE,) * 3,
        scratch_shapes=[pltpu.VMEM((width, 4 * n), bf16), pltpu.VMEM((4 * n, cols), bf16)],
        cost_estimate=BRIEF,
        compiler_params=pltpu.CompilerParams(vmem_limit_bytes=LIMIT),
        name="grad_ffn",
    )(sc, *lefts, *rights, *after)


def grad_down_kernel(sc, *rest):
    lefts, rights = rest[:4], rest[4:8]
    send_ref, keep_ref, token_ref, left, right = rest[-5:]
    token_ref[...] = jnp.zeros_like(token_ref)
    n, (_, half, cols) = rights[0].shape[0], send_ref.shape
    turned(left, lefts)
    rows = pl.ds(pl.multiple_of(sc[0] * half, half), half)
    like = sc[2] & 1
    for h in range(2):
        for out, parity in ((send_ref, 1 - like), (keep_ref, like)):
            at = pl.multiple_of((2 * h + parity) * cols, 128)
            for j, block in enumerate(rights):
                right[j * n : (j + 1) * n, :] = block[:, pl.ds(at, cols)]
            out[h] = nn(left[rows, :], right[...]).astype(out.dtype)


def grad_down(sc, lefts, rights, after):
    n, width = lefts[0].shape
    cols = rights[0].shape[1] // 4
    block = (2, width // 2, cols)
    return pl.pallas_call(
        grad_down_kernel,
        out_shape=(shape(block, bf16), shape(block, bf16), TOKEN),
        in_specs=[SCALARS] + [WHOLE] * 8 + [LEFT] * len(after),
        out_specs=(WHOLE,) * 3,
        scratch_shapes=[pltpu.VMEM((width, 4 * n), bf16), pltpu.VMEM((4 * n, cols), bf16)],
        cost_estimate=BRIEF,
        compiler_params=pltpu.CompilerParams(vmem_limit_bytes=LIMIT),
        name="grad_down",
    )(sc, *lefts, *rights, *after)


def grad_attention_kernel(first, sc, *rest):
    a_refs, o_refs, rest = rest[:4], rest[4:8], rest[8:]
    queries, keys, values, outs, threes, ones = (rest[i : i + 2] for i in range(0, 12, 2))
    gain_a, gain_f = (rest[i : i + 2] for i in (12, 14))
    *outs_of, token_ref, left, right = rest[-5:]
    token_ref[...] = jnp.zeros_like(token_ref)
    core, chip = sc[0], sc[1]
    n, width = a_refs[0].shape
    turned(left.at[0], a_refs)
    gains = [g[0][...] + g[1][...] for g in (gain_a, gain_f)]
    gains = jnp.concatenate([*gains, jnp.zeros((6, width), f32)], axis=0).T
    gains = jnp.concatenate([gains, jnp.zeros((width, PIECE - KVW - 8), f32)], axis=1).astype(bf16)

    def fill(at, of_three, own_three, own_one, single):
        for j in range(2):
            for i in range(3):
                right[of_three + i, j * n : (j + 1) * n, :] = own_three[j][i]
                right[of_three + i, (j + 2) * n : (j + 3) * n, :] = threes[j][i]
            right[single, j * n : (j + 1) * n, :] = own_one[j][...]
            right[single, (j + 2) * n : (j + 3) * n, :] = ones[j][...]

    @pl.when(core == 0)
    def _():
        fill(0, 0, queries, keys, 3)

    @pl.when(core == 1)
    def _():
        turned(left.at[1], o_refs)
        fill(0, 1, outs, values, 0)

    for out, m in zip(outs_of, by_turn(core, chip)[first : first + 2]):
        which = jnp.where(m > 0, core, 0)
        out[...] = nn(left[which], right[m]).astype(bf16)
        out[:, KVW:] = gains


def grad_attention(first, sc, a, o, own, got, gains, after):
    n, width = a[0].shape
    out = shape((width, PIECE), bf16)
    return pl.pallas_call(
        functools.partial(grad_attention_kernel, first),
        out_shape=(out, out, TOKEN),
        in_specs=[SCALARS] + [WHOLE] * 24 + [LEFT] * len(after),
        out_specs=(WHOLE,) * 3,
        scratch_shapes=[pltpu.VMEM((2, width, 4 * n), bf16), pltpu.VMEM((4, 4 * n, PIECE), bf16)],
        cost_estimate=BRIEF,
        compiler_params=pltpu.CompilerParams(vmem_limit_bytes=LIMIT),
        name="grad_attention",
    )(sc, *a, *o, *own, *got, *gains, *after)


def lay_kernel(count, sc, *rest):
    token_ref = rest[-2]
    token_ref[...] = jnp.zeros_like(token_ref)
    rest = (*rest[:-2], rest[-1])
    mine, other, outs, kept = rest[:4], rest[4:8], rest[-1 - count : -1], rest[-1]
    core, chip = sc[0], sc[1]
    for kind, pieces in ((core, mine), (1 - core, other)):
        for who, piece in zip(whose(kind), pieces):
            kept[kind, chip ^ who] = piece[...]
    n = sum(o.shape[1] for o in outs[: 4 if len(outs) > 2 else 2]) // 8
    cols = [jnp.concatenate([kept[c, m, :, :n].astype(f32) for m in range(4)], axis=1) for c in range(2)]
    if len(outs) == 2:
        outs[0][...] = cols[0]
        outs[1][...] = cols[1]
    else:
        outs[0][...] = cols[0][:, : 3 * n]
        outs[1][...] = cols[0][:, 3 * n :]
        outs[2][...] = cols[1][:, :n]
        outs[3][...] = cols[1][:, n:]
        gains = kept[0, 0, :, n : n + 8].astype(f32) + kept[1, 0, :, n : n + 8].astype(f32)
        outs[4][...] = gains.T[:2]


def lay(sc, mine, other, widths, after):
    rows, n = mine[0].shape
    outs = tuple(shape((rows, w), f32) for w in widths)
    if len(widths) > 2:
        outs += (shape((2, rows), f32),)
    return pl.pallas_call(
        functools.partial(lay_kernel, len(outs)),
        out_shape=(*outs, TOKEN),
        in_specs=[SCALARS] + [WHOLE] * 8 + [LEFT] * len(after),
        out_specs=(WHOLE,) * (len(outs) + 1),
        scratch_shapes=[pltpu.VMEM((2, 4, rows, n), bf16)],
        cost_estimate=BRIEF,
        compiler_params=pltpu.CompilerParams(vmem_limit_bytes=24 << 20),
        name="lay",
    )(sc, *mine, *other, *after)


def pick_first_kernel(sc, q_ref, k_ref, v_ref, o_ref, gain_ref, out_ref, wide, tall, sem):
    rows = out_ref.shape[0]
    which = sc[0] * 4 + sc[1]

    def bring(source, into, first, last):
        @pl.when((which >= first) & (which <= last))
        def _():
            copy = pltpu.make_async_copy(source, into, sem)
            copy.start()
            copy.wait()

    bring(q_ref, wide, 0, 2)
    bring(k_ref, tall, 3, 3)
    bring(v_ref, tall, 4, 4)
    bring(o_ref, wide, 5, 7)
    pad = jnp.zeros((6, rows), f32)
    gains = jnp.concatenate([gain_ref[...], pad], axis=0).T.astype(bf16)
    rest = jnp.zeros((rows, PIECE - KVW - 8), bf16)
    for m in range(4):

        @pl.when((which == m) | (which == (m + 5 if m < 3 else 4)))
        def _():
            piece = wide[:, m * KVW : (m + 1) * KVW] if m < 3 else tall[...].T
            out_ref[...] = jnp.concatenate([piece, gains, rest], axis=1)


def pick_first(sc, query, key, value, out, gains):
    return pl.pallas_call(
        pick_first_kernel,
        out_shape=shape((query.shape[0], PIECE), bf16),
        in_specs=[SCALARS] + [LEFT] * 4 + [WHOLE],
        out_specs=WHOLE,
        scratch_shapes=[pltpu.VMEM(query.shape, bf16), pltpu.VMEM(key.shape, bf16), pltpu.SemaphoreType.DMA],
        cost_estimate=BRIEF,
        compiler_params=pltpu.CompilerParams(vmem_limit_bytes=LIMIT),
        name="pick_first",
    )(sc, query, key, value, out, gains)


def pick_kernel(sc, gate, up, down, *rest):
    out_ref, sems = rest[-2:]
    rows, cols = out_ref.shape[0] - ROWS, out_ref.shape[1]
    into = out_ref.at[:rows]
    start = pl.multiple_of(down_rows(sc[0], sc[1], down.shape[0]), 64)
    copy = pltpu.make_async_copy(down.at[pl.ds(start, ROWS), :], out_ref.at[rows:], sems.at[1])
    copy.start()
    at = pl.ds(pl.multiple_of(sc[1] * cols, 128), cols)
    for c, source in ((0, gate), (1, up)):

        @pl.when(sc[0] == c)
        def _():
            pltpu.make_async_copy(source.at[:, at], into, sems.at[0]).start()

    pltpu.make_async_copy(gate.at[:, at], into, sems.at[0]).wait()
    copy.wait()


def pick(sc, gate, up, down, after):
    return pl.pallas_call(
        pick_kernel,
        out_shape=shape((gate.shape[0] + ROWS, gate.shape[1] // 4), bf16),
        in_specs=[SCALARS] + [LEFT] * (3 + len(after)),
        out_specs=WHOLE,
        scratch_shapes=[pltpu.SemaphoreType.DMA((2,))],
        cost_estimate=BRIEF,
        compiler_params=pltpu.CompilerParams(vmem_limit_bytes=16 << 20),
        name="pick",
    )(sc, gate, up, down, *after)


def gains_kernel(first_ref, out_ref):
    for j in range(4):
        n = first_ref.shape[1]
        out_ref[:, j * n : (j + 1) * n] = first_ref[j, :, KVW : KVW + 8].astype(f32).T[:2]


def gains_of(first):
    return pl.pallas_call(
        gains_kernel,
        out_shape=shape((2, 4 * first.shape[1]), f32),
        in_specs=[WHOLE],
        out_specs=WHOLE,
        cost_estimate=BRIEF,
        compiler_params=pltpu.CompilerParams(vmem_limit_bytes=16 << 20),
        name="gains",
    )(first)


def stack_kernel(sc, *rest):
    parts, out_ref, sems = rest[:4], rest[-2], rest[-1]
    copies = [pltpu.make_async_copy(p, out_ref.at[sc[2] ^ s], sems.at[s]) for s, p in enumerate(parts)]
    for copy in copies:
        copy.start()
    for copy in copies:
        copy.wait()


def stack(sc, parts, after=()):
    return pl.pallas_call(
        stack_kernel,
        out_shape=shape((4,) + parts[0].shape, parts[0].dtype),
        in_specs=[SCALARS] + [LEFT] * (4 + len(after)),
        out_specs=WHOLE,
        scratch_shapes=[pltpu.SemaphoreType.DMA((4,))],
        cost_estimate=BRIEF,
        compiler_params=pltpu.CompilerParams(vmem_limit_bytes=16 << 20),
        name="stack",
    )(sc, *parts, *after)


def small(kernel, sc, args, outs, scratch, after, name):
    def with_token(*refs):
        at = len(refs) - len(scratch) - 1
        refs[at][...] = jnp.zeros_like(refs[at])
        kernel(*refs[:at], *refs[at + 1 :])

    return pl.pallas_call(
        with_token,
        out_shape=(*outs, TOKEN),
        in_specs=[SCALARS] + [WHOLE] * len(args) + [LEFT] * len(after),
        out_specs=(WHOLE,) * (len(outs) + 1),
        scratch_shapes=scratch,
        cost_estimate=BRIEF,
        compiler_params=pltpu.CompilerParams(vmem_limit_bytes=32 << 20),
        name=name,
    )(sc, *args, *after)


def sum_first(sc, keep, got, after, parts=1):
    def kernel(sc, *refs):
        rest = list(refs)

        def both(arrays):
            if len(arrays) == 2:
                return rest.pop(0), rest.pop(0)
            ref = rest.pop(0)
            return ref.at[0], ref.at[1]

        (own_kept, later_kept), (own_got, later_got) = both(keep), both(got)
        own_ref = rest[-1]
        for i, later_ref in enumerate(rest[-1 - parts : -1]):
            n = later_ref.shape[0]
            rows = slice(i * n, (i + 1) * n)
            later_ref[...] = (later_kept[rows].astype(f32) + later_got[rows].astype(f32)).astype(bf16)
        own_ref[...] = own_kept[...].astype(f32) + own_got[...].astype(f32)

    rows, cols = keep[0].shape[-2:]
    outs = [shape((rows // parts, cols), bf16)] * parts + [shape((rows, cols), f32)]
    return small(kernel, sc, [*keep, *got], outs, [], after, "sum_first")


def sum_second(sc, own, got, after):
    def kernel(sc, own_ref, *rest):
        gots, (send_ref, keep_ref, total) = rest[: len(got)], rest[-3:]
        n = total.shape[1]
        for j in range(4):
            part, at = divmod(j * n, gots[0].shape[0])
            total[j] = own_ref[j * n : (j + 1) * n, :] + gots[part][at : at + n, :].astype(f32)
        like = sc[2] & 1
        for h in range(2):
            send_ref[h] = total[2 * h + 1 - like].astype(bf16)
            keep_ref[h] = total[2 * h + like]

    rows, cols = own.shape
    part = (rows // 4, cols)
    outs = [shape((2,) + part, bf16), shape((2,) + part, f32)]
    return small(kernel, sc, [own, *got], outs, [pltpu.VMEM((4,) + part, f32)], after, "sum_second")


def sum_third(sc, keep, got, after):
    def kernel(sc, keep_ref, got_ref, *rest):
        send_ref, own_ref = rest[-2:]
        h = sc[2] >> 1
        send_ref[...] = (keep_ref[1 - h].astype(f32) + got_ref[1 - h].astype(f32)).astype(bf16)
        own_ref[...] = keep_ref[h].astype(f32) + got_ref[h].astype(f32)

    part = keep.shape[1:]
    return small(kernel, sc, [keep, got], [shape(part, bf16), shape(part, f32)], [], after, "sum_third")


def down_split(sc, own, got, after):
    def kernel(sc, own_ref, got_ref, *rest):
        send_ref, kept_ref, total = rest[-3:]
        n = total.shape[1]
        for m in range(4):
            rows = slice(m * n, (m + 1) * n)
            total[m] = own_ref[rows, :] + got_ref[rows, :].astype(f32)
        for i, m in enumerate(by_turn(sc[0], sc[1])):
            out = send_ref if i < 2 else kept_ref
            out[i % 2] = total[m].astype(bf16)

    rows, cols = own.shape
    out = shape((2, rows // 4, cols), bf16)
    return small(kernel, sc, [own, got], [out, out], [pltpu.VMEM((4, rows // 4, cols), f32)], after, "down_split")


def sum_two(sc, own, got, after):
    def kernel(sc, own_ref, got_ref, *rest):
        rest[-1][...] = (own_ref[...] + got_ref[...].astype(f32)).astype(bf16)

    return small(kernel, sc, [own, got], [shape(own.shape, bf16)], [], after, "sum_two")


def lay_down(sc, mine, other, after):
    def kernel(sc, *rest):
        out_ref, total = rest[-2:]
        n = total.shape[2]
        for kind, pieces in ((sc[0], rest[:4]), (1 - sc[0], rest[4:8])):
            for who, piece in zip(whose(kind), pieces):
                total[kind, sc[1] ^ who] = piece[...].astype(f32)
        for c in range(2):
            for m in range(4):
                at = (c * 4 + m) * n
                out_ref[at : at + n, :] = total[c, m]

    n, cols = mine[0].shape
    return small(kernel, sc, [*mine, *other], [shape((8 * n, cols), f32)], [pltpu.VMEM((2, 4, n, cols), f32)], after, "lay_down")


def hold(value, after):
    return pl.pallas_call(
        lambda *refs: None,
        out_shape=shape(value.shape, value.dtype),
        in_specs=[LEFT] * (1 + len(after)),
        out_specs=LEFT,
        input_output_aliases={0: 0},
        cost_estimate=BRIEF,
        compiler_params=pltpu.CompilerParams(vmem_limit_bytes=1 << 20),
        name="hold",
    )(value, *after)


def far_sum(sc, far, near, after):
    def kernel(sc, far_ref, near_ref, *rest):
        rest[-1][...] = (far_ref[...] + jnp.where(sc[0] == 1, near_ref[...].astype(f32), 0.0)).astype(bf16)

    return small(kernel, sc, [far, near], [shape(far.shape, bf16)], [], after, "far_sum")


def depart(sc, both, after):
    def kernel(sc, both_ref, *rest):
        out_ref, grad_ref = rest[-2:]
        n = out_ref.shape[0]
        out_ref[...] = both_ref[:n, :]
        grad_ref[...] = both_ref[n:, :].astype(f32)

    block = (both.shape[0] // 2, both.shape[1])
    return small(kernel, sc, [both], [shape(block, bf16), shape(block, f32)], [], after, "depart")


def sum_both(sc, own_b, got_b, own_d, got_d, after):
    def kernel(sc, b_ref, gb_ref, d_ref, gd_ref, *rest):
        out_ref = rest[-1]
        n = b_ref.shape[0]
        out_ref[:n, :] = (b_ref[...] + gb_ref[...].astype(f32)).astype(bf16)
        out_ref[n:, :] = (d_ref[...] + gd_ref[...].astype(f32)).astype(bf16)

    rows, cols = own_b.shape[0] + own_d.shape[0], own_b.shape[1]
    return small(kernel, sc, [own_b, got_b, own_d, got_d], [shape((rows, cols), bf16)], [], after, "sum_both")


def lay_both(sc, mine, other, rows, after):
    def kernel(sc, *rest):
        gate_ref, up_ref, down_ref, kept = rest[-4:]
        cols = kept.shape[3]
        n = kept.shape[2] - rows
        for kind, pieces in ((sc[0], rest[:4]), (1 - sc[0], rest[4:8])):
            for who, piece in zip(whose(kind), pieces):
                kept[kind, sc[1] ^ who] = piece[...].astype(f32)
        for c, out in enumerate((gate_ref, up_ref)):
            for m in range(4):
                out[:, m * cols : (m + 1) * cols] = kept[c, m, :rows]
                at = (c * 4 + m) * n
                down_ref[at : at + n, :] = kept[c, m, rows:]

    total, cols = mine[0].shape
    outs = [shape((rows, 4 * cols), f32)] * 2 + [shape((8 * (total - rows), cols), f32)]
    return small(kernel, sc, [*mine, *other], outs, [pltpu.VMEM((2, 4, total, cols), f32)], after, "lay_both")


CORE, SIDE, BACK = 1, 2, 4
rope_base = 10000.0
RUNS = 2


def flip(value, bit, bit1=None):
    count = lax.axis_size("dp")
    bits = (bit, bit if bit1 is None else bit1)
    return lax.ppermute(value, "dp", [(i, i ^ bits[i & 1]) for i in range(count)])


def flip_z(value, bit, where=lambda d, z: True):
    count, depth = lax.axis_size("dp"), lax.axis_size("fsdp")
    pairs = [(d * depth + z, d * depth + (z ^ bit)) for d in range(count) for z in range(depth) if where(d, z)]
    return lax.ppermute(value, ("dp", "fsdp"), pairs)


def home_to_work(value, back=False):
    count, depth = lax.axis_size("dp"), lax.axis_size("fsdp")
    pairs = []
    for d in range(count):
        for z in range(depth):
            there = (d & ~1) | (z & 1), 2 * (d & 1) + (z >> 1)
            pair = (d * depth + z, there[0] * depth + there[1])
            pairs.append(pair[::-1] if back else pair)
    return lax.ppermute(value, ("dp", "fsdp"), pairs)


def place():
    d, z = lax.axis_index("dp"), lax.axis_index("fsdp")
    return d & 1, (d >> 1) & 3, z


def turns(shard):
    far = flip_z(shard, 2)
    return shard, flip_z(shard, 1), far, flip_z(far, 1)


def plane_gather(piece):
    first, second = flip(piece, SIDE, BACK), flip(piece, BACK, SIDE)
    mine = (piece, first, second, flip(first, BACK, SIDE))
    return mine, tuple(flip(p, CORE) for p in mine)


def window(own):
    core, _, _ = place()
    depth = lax.axis_size("fsdp")
    far = lax.ppermute(own, "fsdp", [(z, z + 1) for z in range(0, depth, 2)])
    near = flip(jnp.where(core == 0, own, far), CORE)
    return far, near, own


def unwindow(sc, far, near):
    depth = lax.axis_size("fsdp")
    near = flip(near, CORE)
    far, token = far_sum(sc, far, near, [])
    return near, token, lax.ppermute(far, "fsdp", [(z + 1, z) for z in range(0, depth, 2)])


def over_groups(value):
    bit = 8
    while bit < lax.axis_size("dp"):
        value = (value.astype(f32) + flip(value, bit).astype(f32)).astype(bf16)
        bit *= 2
    return value


def spread(piece):
    return piece, flip(piece, SIDE, BACK), flip(piece, BACK, SIDE), flip(piece, SIDE | BACK)


def across(pieces):
    return tuple(flip(p, CORE) for p in pieces)


def body(tokens, segment_ids, attn_gain, query_weight, key_weight, value_weight, out_weight, ffn_gain, gate_weight, up_weight, down_weight, cotangent):
    core, chip, z = place()
    sc = jnp.stack([core, chip, z]).astype(jnp.int32)
    _, stretch, width = tokens.shape
    rows, depth = query_weight.shape[0], lax.axis_size("fsdp")
    block = 2 * (z & 1) + core
    positions = (block * stretch + jnp.arange(stretch)).astype(f32)
    freq = rope_base ** (-2.0 * jnp.arange(HEAD_DIM // 2, dtype=f32) / HEAD_DIM)
    angle = freq[:, None] * positions[None, :]
    cos, sin = jnp.cos(angle), jnp.sin(angle)

    gains = jnp.stack([attn_gain, ffn_gain]).astype(f32)
    parts_a = turns(pick_first(sc, query_weight, key_weight.T, value_weight.T, out_weight, gains))
    ids = jnp.broadcast_to((segment_ids[0] + 1).astype(bf16), (IDS, stretch))
    tokens = home_to_work(jnp.concatenate([tokens[0].T, ids]))
    piece_b = pick(sc, gate_weight, up_weight, down_weight.T, parts_a[1:2])
    whole_a = stack(sc, parts_a, [piece_b])
    gains = gains_of(whole_a)
    gain_a, gain_f = gains[:1], gains[1:]
    wa = plane_gather(whole_a.reshape(depth * rows, PIECE))
    side_b = flip_z(piece_b, 1)
    far_b = hold(flip_z(piece_b, 2), [wa[0][1], wa[0][2], side_b])
    whole_b = stack(sc, (piece_b, side_b, far_b, flip_z(far_b, 1)), [wa[0][3]])
    first_b, second_b = flip(whole_b, SIDE, BACK), flip(whole_b, BACK, SIDE)

    h_0, a0, q0, own = pre(sc, tokens, gain_a, cos, sin, *wa, [whole_b])
    kv0 = window(own)
    first_b = hold(first_b, [kv0[0], second_b])
    opposite_b = flip(first_b, BACK, SIDE)
    o0, lse0 = attend(q0, kv0)
    wb = whole_b, first_b, second_b, hold(opposite_b, [o0])
    wb = wb, across(wb)
    weights = wa, wb
    cot = home_to_work(cotangent[0].T)
    mixed0, h1_0, b0, gate0, up0, z0, h_1, a1, q1, own = post(False, [], sc, o0, h_0, gain_f, gain_a, cos, sin, own, *weights)
    kv1 = window(own)
    across_0 = across((a0, b0, mixed0, z0))
    o1, lse1 = attend(q1, kv1, across_0)
    mixed1, h1_1, b1, gate1, up1, z1, output = post(True, [cot], sc, o1, h_1, gain_f, gain_a, cos, sin, own, *weights)
    across_1 = across((a1, b1, mixed1, z1))

    gb1, act1, away1, g1, p1, dgain_f1, do = back(True, False, sc, weights, [cot], [gate1, up1, h1_1, gain_f])
    across_2 = across((gb1, away1))
    dq1, three1, far, near, own = attend_back(sc, p1, q1, kv1, lse1, do, cos, sin)
    near, _, far = unwindow(sc, far, near)
    (three1,) = across((three1,))
    tail = [g1, dq1, own, near, far, h_1, gain_a, cos, sin]
    dk1, dv1, one1, dgain_a1, gb0, act0, away0, g1, p0, dgain_f0, do = back(False, False, sc, weights, tail, [gate0, up0, h1_0, gain_f], [three1, *across_2, *across_1])

    away0, gb0_, one1 = across((away0, gb0, one1))
    send_b, keep_b, done = grad_ffn(sc, [b1, b0, across_1[1], across_0[1]], [act1, act0, across_2[1], away0], [])
    got_b = flip(send_b, SIDE, BACK)
    dq0, three0, far, near, own = attend_back(sc, p0, q0, kv0, lse0, do, cos, sin, [one1, done])
    near, done, far = unwindow(sc, far, near)
    send_d, keep_d, done = grad_down(sc, [gb1, gb0, across_2[0], gb0_], [z1, z0, across_1[3], across_0[3]], [done])
    got_d = flip_z(send_d, 1)
    (three0,) = across((three0,))
    tail = [g1, dq0, own, near, far, h_0, gain_a, cos, sin, output]
    dk0, dv0, one0, dgain_a0, leaving = back(False, True, sc, weights, tail, None, [done])
    later_b, own_b, done = sum_first(sc, [keep_b], [got_b], [dgain_a0])
    more_b = flip(later_b, BACK, SIDE)
    own = [dq1, dq0, dk1, dk0, dv1, dv0, p1, p0]
    got = [three1, three0, one1, flip(one0, CORE)]
    args = [a1, a0, across_1[0], across_0[0]], [mixed1, mixed0, across_1[2], across_0[2]], own, got, [dgain_a1, dgain_a0, dgain_f1, dgain_f0]
    *send_a, done = grad_attention(0, sc, *args, [done])
    got_a = [flip(v, SIDE, BACK) for v in send_a]
    send_d, keep_d, done = sum_third(sc, keep_d, got_d, [done])
    got_d = flip_z(send_d, 2)
    send_b, ring_b, done = sum_second(sc, own_b, [more_b], [done])
    got_b = flip_z(send_b, 1)
    *keep_a, done = grad_attention(2, sc, *args, [done])
    *later_a, own_a, done = sum_first(sc, keep_a, got_a, [done], 2)
    more_a = [flip(v, BACK, SIDE) for v in later_a]
    send_b, ring_b, done = sum_third(sc, ring_b, got_b, [done])
    got_b = flip_z(send_b, 2)
    send_a, ring_a, done = sum_second(sc, own_a, more_a, [done])
    got_a = flip_z(send_a, 1)
    send_d, keep_d, done = down_split(sc, keep_d, got_d, [done])
    got_d = flip(send_d, SIDE, BACK)
    later_d, own_d, done = sum_first(sc, [keep_d], [got_d], [done])
    more_d = flip(later_d, BACK, SIDE)
    send_a, ring_a, done = sum_third(sc, ring_a, got_a, [done])
    got_a = flip_z(send_a, 2)
    piece_b, done = sum_both(sc, ring_b, got_b, own_d, more_d, [done])
    all_b = spread(over_groups(piece_b))
    piece_a, done = sum_two(sc, ring_a, got_a, [done])
    all_a = spread(over_groups(piece_a))
    leaving = home_to_work(hold(leaving, [done]), back=True)
    grad_gate, grad_up, grad_down_, done = lay_both(sc, all_b, across(all_b), ring_a.shape[0], [done])
    grad_query, grad_key, grad_value, grad_out, dgains, done = lay(sc, all_a, across(all_a), (width, KVW, KVW, width), [done])
    output, grad_tokens, _ = depart(sc, leaving, [done])
    output, grad_tokens = output.T, grad_tokens.T
    return (output[None], grad_tokens[None], dgains[0], grad_query, grad_key, grad_value, grad_out, dgains[1], grad_gate, grad_up, grad_down_.T)


def solution(mesh):
    wide, rows, shard = P("dp", "fsdp", None), P("dp", "fsdp"), P("fsdp", None)
    in_specs = (wide, rows, P("fsdp"), shard, shard, shard, shard, P("fsdp"), shard, shard, shard, wide)
    out_specs = (wide, wide, P("fsdp"), shard, shard, shard, shard, P("fsdp"), shard, shard, shard)
    return jax.shard_map(body, mesh=mesh, in_specs=in_specs, out_specs=out_specs, check_vma=False)
```

```python
import functools
import jax
import jax.numpy as jnp
from jax import lax
from jax.sharding import PartitionSpec as P
from jax.experimental import pallas as pl
from jax.experimental.pallas import tpu as pltpu

f32, bf16 = jnp.float32, jnp.bfloat16
eps = 1e-05
HEADS, KV_HEADS, HEAD_DIM, GROUP, KVW = 15, 5, 64, 3, 320
IDS = 16
ROWS = 128
PIECE = 384
LIMIT = 58 << 20
WHOLE = pl.BlockSpec(memory_space=pltpu.VMEM)
LEFT = pl.BlockSpec(memory_space=pl.ANY)
SCALARS = pl.BlockSpec(memory_space=pltpu.SMEM)
TOKEN = jax.ShapeDtypeStruct((8, 128), f32)
BRIEF = pl.CostEstimate(flops=1024, bytes_accessed=1024, transcendentals=0)


def contract(a, b, i, j):
    return lax.dot_general(a, b, (((i,), (j,)), ((), ())), preferred_element_type=f32)


def nn(a, b):
    return contract(a, b, 1, 0)


def nt(a, b):
    return contract(a, b, 1, 1)


def tn(a, b):
    return contract(a, b, 0, 0)


def whose(core):
    return 0, 1 + core, 2 - core, 3


def fetch(mine, other, kept, sems, core, chip, only=None, turns=range(4)):
    for j in turns:
        for kind, pieces in ((core, mine), (1 - core, other)):
            at = chip ^ whose(kind)[j]

            def copy():
                pltpu.make_async_copy(pieces[j], kept.at[kind, at], sems.at[kind, at]).start()

            if only is None:
                copy()
            else:
                pl.when(kind == only)(copy)


def leave(kept, out, sem, cols=None):
    if cols is not None:
        kept, out = kept.at[:, cols], out.at[:, cols]
    pltpu.make_async_copy(kept, out, sem).start()


def gone(kepts, outs, sems):
    for i, (kept, out) in enumerate(zip(kepts, outs)):
        pltpu.make_async_copy(kept, out, sems.at[i]).wait()


def arrived(kept, sems, *at):
    pltpu.make_async_copy(kept.at[at], kept.at[at], sems.at[at]).wait()


def normed(x, gain):
    return x * lax.rsqrt(jnp.mean(x * x, axis=-1, keepdims=True) + eps) * gain


def norm_back(x, gain, grad):
    r = lax.rsqrt(jnp.mean(x * x, axis=-1, keepdims=True) + eps)
    hat = x * r
    scaled = grad * gain
    dx = r * (scaled - hat * jnp.mean(scaled * hat, axis=-1, keepdims=True))
    return dx, jnp.sum(grad * hat, axis=0, keepdims=True)


def widened(x):
    return jnp.concatenate([x, jnp.zeros((x.shape[0], PIECE - x.shape[1]), x.dtype)], axis=1)


def rope(u, cos, sin, back):
    heads = u.shape[0] // HEAD_DIM
    half = HEAD_DIM // 2
    out = []
    for h in range(heads):
        u1, u2 = u[h * HEAD_DIM : h * HEAD_DIM + half], u[h * HEAD_DIM + half : (h + 1) * HEAD_DIM]
        if back:
            out += [u1 * cos + u2 * sin, u2 * cos - u1 * sin]
        else:
            out += [u1 * cos - u2 * sin, u2 * cos + u1 * sin]
    return jnp.concatenate(out, axis=0)


def project(state, gain_ref, cos_ref, sin_ref, ids, kept, sems, a_ref, q_ref, kv_ref):
    a = normed(state, gain_ref[...]).astype(bf16)
    a_ref[...] = a
    cos, sin = cos_ref[...], sin_ref[...]
    arrived(kept, sems, 0, 3)
    kv_ref[:KVW, :] = rope(nn(a, kept[0, 3, :, :KVW]).T, cos, sin, False).astype(bf16)
    arrived(kept, sems, 1, 0)
    kv_ref[2 * KVW :, :] = ids
    kv_ref[KVW : 2 * KVW, :] = nn(a, kept[1, 0, :, :KVW]).T.astype(bf16)
    for m in range(3):
        arrived(kept, sems, 0, m)
        q_ref[pl.ds(m * KVW, KVW), :] = rope(nn(a, kept[0, m, :, :KVW]).T, cos, sin, False).astype(bf16)


def pre_kernel(sc, ht_ref, gain_ref, cos_ref, sin_ref, *rest):
    width = ht_ref.shape[0] - IDS
    mine, other = rest[:4], rest[4:8]
    h_ref, a_ref, q_ref, kv_ref, kept, sems = rest[-6:]
    core, chip = sc[0], sc[1]
    fetch(mine, other, kept, sems, core, chip)
    h = ht_ref[:width, :].T
    h_ref[...] = h
    project(h.astype(f32), gain_ref, cos_ref, sin_ref, ht_ref[width:, :], kept, sems, a_ref, q_ref, kv_ref)
    for m in range(1, 4):
        arrived(kept, sems, 1, m)


def scratch_a(width):
    return [pltpu.VMEM((2, 4, width, PIECE), bf16), pltpu.SemaphoreType.DMA((2, 4))]


def shape(s, d):
    return jax.ShapeDtypeStruct(s, d)


def pre(sc, ht, gain, cos, sin, mine_a, other_a, after):
    width, n = ht.shape[0] - IDS, ht.shape[1]
    return pl.pallas_call(
        pre_kernel,
        out_shape=(shape((n, width), bf16), shape((n, width), bf16), shape((width, n), bf16), shape((2 * KVW + IDS, n), bf16)),
        in_specs=[SCALARS] + [WHOLE] * 4 + [LEFT] * (8 + len(after)),
        out_specs=(WHOLE,) * 4,
        scratch_shapes=scratch_a(width),
        cost_estimate=BRIEF,
        compiler_params=pltpu.CompilerParams(vmem_limit_bytes=LIMIT),
        name="pre",
    )(sc, ht, gain, cos, sin, *mine_a, *other_a, *after)


def bias_of(kv):
    keys, n = kv.shape[1], kv.shape[1] // 3
    ids = kv[2 * KVW :, :].astype(f32)
    seg_k, seg_q = ids.T[:, :1], ids[:1, 2 * n :]
    j = lax.broadcasted_iota(jnp.int32, (keys, n), 0)
    i = lax.broadcasted_iota(jnp.int32, (keys, n), 1) + (keys - n)
    return jnp.where((seg_k == seg_q) & (j <= i), 0.0, -1e30).astype(f32)


def window_of(parts, whole):
    n = parts[0].shape[1]
    for w, part in enumerate(parts):
        whole[:, w * n : (w + 1) * n] = part[...]


def attend_kernel(q_ref, kv0, kv1, kv2, *rest):
    o_ref, lse_ref, bias, kv = rest[-4:]
    window_of((kv0, kv1, kv2), kv)
    bias[...] = bias_of(kv)

    def head(e, _):
        row = pl.multiple_of(e * HEAD_DIM, HEAD_DIM)
        k = kv[pl.ds(row, HEAD_DIM), :]
        v = kv[pl.ds(row + KVW, HEAD_DIM), :]
        for g in range(GROUP):
            at = pl.multiple_of((e * GROUP + g) * HEAD_DIM, HEAD_DIM)
            q = q_ref[pl.ds(at, HEAD_DIM), :]
            s = tn(k, q) * HEAD_DIM ** (-0.5) + bias[...]
            top = jnp.max(s, axis=0, keepdims=True)
            expo = jnp.exp(s - top)
            total = jnp.sum(expo, axis=0, keepdims=True)
            probs = (expo * (1.0 / total)).astype(bf16)
            o_ref[pl.ds(at, HEAD_DIM), :] = nn(v, probs).astype(bf16)
            lse_ref[pl.ds(e * GROUP + g, 1), :] = top + jnp.log(total)
        return 0

    lax.fori_loop(0, KV_HEADS, head, 0)


def attend(q, kvs, after=()):
    width, n = q.shape
    return pl.pallas_call(
        attend_kernel,
        out_shape=(shape((width, n), bf16), shape((HEADS, n), f32)),
        in_specs=[WHOLE] * 4 + [LEFT] * len(after),
        out_specs=(WHOLE,) * 2,
        scratch_shapes=[pltpu.VMEM((3 * n, n), f32), pltpu.VMEM((2 * KVW + IDS, 3 * n), bf16)],
        cost_estimate=BRIEF,
        compiler_params=pltpu.CompilerParams(vmem_limit_bytes=24 << 20),
        name="attend",
    )(q, *kvs, *after)


def attend_back_kernel(sc, p_ref, q_ref, kv0, kv1, kv2, lse_ref, do_ref, cos_ref, sin_ref, *rest):
    dq_ref, three_ref, far_ref, near_ref, own_ref, bias, kv, dqs = rest[-8:]
    n = q_ref.shape[1]
    window_of((kv0, kv1, kv2), kv)
    bias[...] = bias_of(kv)
    scale = HEAD_DIM ** (-0.5)

    def head(e, _):
        row = pl.multiple_of(e * HEAD_DIM, HEAD_DIM)
        k = kv[pl.ds(row, HEAD_DIM), :]
        v = kv[pl.ds(row + KVW, HEAD_DIM), :]
        dk = dv = None
        for g in range(GROUP):
            at = pl.multiple_of((e * GROUP + g) * HEAD_DIM, HEAD_DIM)
            q = q_ref[pl.ds(at, HEAD_DIM), :]
            do = do_ref[pl.ds(at, HEAD_DIM), :]
            s = tn(k, q) * scale + bias[...]
            probs = jnp.exp(s - lse_ref[pl.ds(e * GROUP + g, 1), :])
            dp = tn(v, do)
            inner = jnp.sum(probs * dp, axis=0, keepdims=True)
            ds = (probs * (dp - inner)).astype(bf16)
            dvg, dkg = nt(do, probs.astype(bf16)), nt(q, ds)
            dv, dk = (dvg, dkg) if g == 0 else (dv + dvg, dk + dkg)
            dqs[pl.ds(at, HEAD_DIM), :] = nn(k, ds)
        for at, grad in ((row, dk * scale), (row + KVW, dv)):
            far_ref[pl.ds(at, HEAD_DIM), :] = grad[:, :n]
            near_ref[pl.ds(at, HEAD_DIM), :] = grad[:, n : 2 * n].astype(bf16)
            own_ref[pl.ds(at, HEAD_DIM), :] = grad[:, 2 * n :]
        return 0

    lax.fori_loop(0, KV_HEADS, head, 0)
    cos, sin = cos_ref[...] * scale, sin_ref[...] * scale
    for m in range(3):
        dq = widened(rope(dqs[m * KVW : (m + 1) * KVW, :], cos, sin, True).T.astype(bf16))
        dq_ref[m] = dq
        three_ref[m] = jnp.where(sc[0] == 0, p_ref[m], dq)


def attend_back(sc, p, q, kvs, lse, do, cos, sin, after=()):
    width, n = q.shape
    block = (2 * KVW, n)
    return pl.pallas_call(
        attend_back_kernel,
        out_shape=(shape((3, n, PIECE), bf16), shape((3, n, PIECE), bf16), shape(block, f32), shape(block, bf16), shape(block, f32)),
        in_specs=[SCALARS] + [WHOLE] * 9 + [LEFT] * len(after),
        out_specs=(WHOLE,) * 5,
        scratch_shapes=[pltpu.VMEM((3 * n, n), f32), pltpu.VMEM((2 * KVW + IDS, 3 * n), bf16), pltpu.VMEM((width, n), f32)],
        cost_estimate=BRIEF,
        compiler_params=pltpu.CompilerParams(vmem_limit_bytes=32 << 20),
        name="attend_back",
    )(sc, p, q, *kvs, lse, do, cos, sin, *after)


def down_rows(kind, chip, width):
    return jnp.minimum((kind * 4 + chip) * ROWS, width - ROWS)


def fetch_down(mine, other, wb, wd, sem_d, core, chip):
    rows, width = wb.shape[3], wd.shape[1]
    last = width % ROWS
    for kind, pieces in ((core, mine), (1 - core, other)):
        for who, piece in zip(whose(kind), pieces):
            at = kind * 4 + (chip ^ who)

            @pl.when(at < width // ROWS)
            def _():
                into = wd.at[:, pl.ds(pl.multiple_of(at * ROWS, ROWS), ROWS)]
                pltpu.make_async_copy(piece.at[:, rows:], into, sem_d).start()

            @pl.when(at == width // ROWS)
            def _():
                pltpu.make_async_copy(piece.at[:, rows + ROWS - last :], wd.at[:, width - last :], sem_d).start()


def fetch_both(mine, other, wb, sem_b, core, chip, turns=range(4)):
    rows = wb.shape[3]
    fetch([p.at[:, :rows] for p in mine], [p.at[:, :rows] for p in other], wb, sem_b, core, chip, turns=turns)


def whole(wb, c, m):
    _, rows, n = wb.shape[2:]
    return wb[c, m].reshape(4 * rows, n)


def arrived_down(wd, sem_d):
    pltpu.make_async_copy(wd, wd, sem_d).wait()


def scratch_ffn(width, n):
    return [
        pltpu.VMEM((2, 4, 4, width // 4, n), bf16),
        pltpu.SemaphoreType.DMA((2, 4)),
        pltpu.VMEM((4, width, n), bf16),
        pltpu.SemaphoreType.DMA,
    ]


def post_kernel(last, after, sc, ot_ref, h_ref, gain_ref, gain_a, cos_ref, sin_ref, *rest):
    mine_a, other_a, mine_b, other_b = rest[:4], rest[4:8], rest[8:12], rest[12:16]
    ids_ref, rest = rest[16], rest[17 + after :]
    hbm, next_ref = rest[:6], rest[6]
    more, rest = rest[7 : 7 + (0 if last else 3)], rest[7 + (0 if last else 3) :]
    wa, sem_a, wb, sem_b, wd, sem_d, *stage, sem_out = rest
    o_ref, h1_ref, b_ref, gate_ref, up_ref, z_ref = stage
    core, chip = sc[0], sc[1]
    fetch(mine_a, other_a, wa, sem_a, core, chip, 1)
    fetch_both(mine_b, other_b, wb, sem_b, core, chip, (0, 1))
    fetch_down(mine_b, other_b, wb, wd, sem_d, core, chip)
    fetch_both(mine_b, other_b, wb, sem_b, core, chip, (2, 3))
    if not last:
        fetch(mine_a, other_a, wa, sem_a, core, chip, 0)
    o = ot_ref[...].T
    o_ref[...] = o
    leave(o_ref, hbm[0], sem_out.at[0])
    for m in range(1, 4):
        arrived(wa, sem_a, 1, m)
    h1 = h_ref[...].astype(f32) + jnp.concatenate([nn(o, wa[1, m, :, :KVW]) for m in range(1, 4)], axis=1)
    h1_ref[...] = h1
    leave(h1_ref, hbm[1], sem_out.at[1])
    b = normed(h1, gain_ref[...]).astype(bf16)
    b_ref[...] = b
    leave(b_ref, hbm[2], sem_out.at[2])
    n = wb.shape[4]
    total = h1
    for i in range(4):
        m = chip ^ i
        cols = pl.ds(pl.multiple_of(m * n, 128), n)
        arrived(wb, sem_b, 0, m)
        gate = nn(b, whole(wb, 0, m))
        arrived(wb, sem_b, 1, m)
        up = nn(b, whole(wb, 1, m))
        gate_ref[:, cols] = gate.astype(bf16)
        up_ref[:, cols] = up.astype(bf16)
        z = (gate / (1.0 + jnp.exp(-gate)) * up).astype(bf16)
        z_ref[:, cols] = z
        for j in range(3, 6):
            leave(stage[j], hbm[j], sem_out.at[j], cols)
        if i == 0:
            arrived_down(wd, sem_d)
        total = total + nt(z, wd[m])
    next_ref[...] = total.astype(bf16).T if last else total
    if last:
        arrived(wa, sem_a, 1, 0)
    else:
        project(total, gain_a, cos_ref, sin_ref, ids_ref[2 * KVW :, :], wa, sem_a, *more)
    gone(stage, hbm, sem_out)


def post(last, after, sc, ot, h, gain, gain_a, cos, sin, kv, wa, wb):
    width, n = ot.shape
    hidden = wb[0][0].shape[2] * 4
    outs = [shape((n, width), bf16), shape((n, width), f32), shape((n, width), bf16)] + [shape((n, hidden), bf16)] * 3
    outs += [shape((width, n), bf16) if last else shape((n, width), f32)]
    if not last:
        outs += [shape((n, width), bf16), shape((width, n), bf16), shape((2 * KVW + IDS, n), bf16)]
    return pl.pallas_call(
        functools.partial(post_kernel, last, len(after)),
        out_shape=tuple(outs),
        in_specs=[SCALARS] + [WHOLE] * 6 + [LEFT] * 16 + [WHOLE] + [LEFT] * len(after),
        out_specs=(LEFT,) * 6 + (WHOLE,) * (len(outs) - 6),
        scratch_shapes=scratch_a(width) + scratch_ffn(width, hidden // 4) + [pltpu.VMEM(o.shape, o.dtype) for o in outs[:6]] + [pltpu.SemaphoreType.DMA((6,))],
        cost_estimate=BRIEF,
        compiler_params=pltpu.CompilerParams(vmem_limit_bytes=LIMIT),
        name="post",
    )(sc, ot, h, gain, gain_a, cos, sin, *wa[0], *wa[1], *wb[0], *wb[1], kv, *after)


def ffn_back(state, core, chip, refs, weights, stage, sems, hbm):
    gate_ref, up_ref, h1_ref, gain_ref, gb_ref, keep_ref, send_ref, g1_ref, p_ref, dgain_ref, do_ref = refs
    wa, sem_a, wb, sem_b, wd, sem_d = weights
    gb = state.astype(bf16)
    gb_ref[...] = gb
    leave(gb_ref, hbm[3], sems.at[3])
    n = wb.shape[4]
    first = core == 0
    arrived_down(wd, sem_d)
    db = None
    for i in range(4):
        m = chip ^ i
        cols = pl.ds(pl.multiple_of(m * n, 128), n)
        dz = nn(gb, wd[m])
        if i == 0:
            for j in range(2):
                pltpu.make_async_copy(hbm[j], stage[j], sems.at[j]).wait()
        gate, up = gate_ref[:, cols].astype(f32), up_ref[:, cols].astype(f32)
        sig = 1.0 / (1.0 + jnp.exp(-gate))
        dup = (dz * (gate * sig)).astype(bf16)
        dgate = (dz * up * (sig * (1.0 + gate * (1.0 - sig)))).astype(bf16)
        keep_ref[:, cols] = jnp.where(first, dgate, dup)
        send_ref[:, cols] = jnp.where(first, dup, dgate)
        leave(keep_ref, hbm[4], sems.at[4], cols)
        leave(send_ref, hbm[5], sems.at[5], cols)
        arrived(wb, sem_b, 0, m)
        part = nt(dgate, whole(wb, 0, m))
        arrived(wb, sem_b, 1, m)
        part = part + nt(dup, whole(wb, 1, m))
        db = part if i == 0 else db + part
    pltpu.make_async_copy(hbm[2], stage[2], sems.at[2]).wait()
    dx, dgain = norm_back(h1_ref[...], gain_ref[...], db)
    dgain_ref[...] = dgain
    g1 = state + dx
    g1_ref[...] = g1
    leave(g1_ref, hbm[6], sems.at[6])
    low = g1.astype(bf16)
    do = None
    for p in range(3):
        part = low[:, p * KVW : (p + 1) * KVW]
        p_ref[p] = widened(part)
        arrived(wa, sem_a, 1, p + 1)
        part = nt(wa[1, p + 1, :, :KVW], part)
        do = part if p == 0 else do + part
    do_ref[...] = do.astype(bf16)


def finish_a(wa, sem_a, *left):
    for at in left:
        arrived(wa, sem_a, *at)


def query_back(dq_ref, wa, sem_a):
    da = None
    for m in range(3):
        arrived(wa, sem_a, 0, m)
        part = nt(dq_ref[m, :, :KVW], wa[0, m, :, :KVW])
        da = part if m == 0 else da + part
    return da


def project_back(da, own_ref, near_ref, far_ref, core, cos_ref, sin_ref, dk_ref, dv_ref, one_ref, h, gain, wa, sem_a):
    cos, sin = cos_ref[...], sin_ref[...]
    grad = own_ref[...] + far_ref[...].astype(f32) + jnp.where(core == 0, near_ref[...].astype(f32), 0.0)
    dk = rope(grad[:KVW], cos, sin, True).T.astype(bf16)
    dv = grad[KVW:].T.astype(bf16)
    dk_ref[...] = widened(dk)
    dv_ref[...] = widened(dv)
    one_ref[...] = widened(jnp.where(core == 0, dv, dk))
    arrived(wa, sem_a, 0, 3)
    arrived(wa, sem_a, 1, 0)
    da = da + nt(dk, wa[0, 3, :, :KVW]) + nt(dv, wa[1, 0, :, :KVW])
    return norm_back(h, gain, da)


def back_kernel(start, end, after, sc, *rest):
    rest = list(rest)

    def take(n):
        out = rest[:n]
        del rest[:n]
        return out

    core, chip = sc[0], sc[1]
    mine_a, other_a = take(4), take(4)
    if not end:
        mine_b, other_b = take(4), take(4)
    if start:
        (g_ref,) = take(1)
    else:
        g1_in, dq_ref, own_ref, near_ref, far_ref, h_ref, gain_a, cos_ref, sin_ref = take(9)
        if end:
            (last_ref,) = take(1)
    if not end:
        ins = take(4)
    take(after)
    if not start:
        dk_ref, dv_ref, one_ref, dgain_a = take(4)
    if end:
        (g_out,) = take(1)
    else:
        outs = take(7)
    wa, sem_a = take(2)
    if not start:
        fetch(mine_a, other_a, wa, sem_a, core, chip, 0)
        fetch(mine_a, other_a, wa, sem_a, core, chip, 1)
    if not end:
        wb, sem_b, wd, sem_d = take(4)
        stage, (sems,) = take(7), take(1)
        hbm = [*ins[:3], *outs[:4]]
        fetch_down(mine_b, other_b, wb, wd, sem_d, core, chip)
        for j in range(3):
            pltpu.make_async_copy(hbm[j], stage[j], sems.at[j]).start()
        fetch_both(mine_b, other_b, wb, sem_b, core, chip)
    if start:
        fetch(mine_a, other_a, wa, sem_a, core, chip, 1)
    if start:
        state = g_ref[...].T.astype(f32)
    else:
        da = query_back(dq_ref, wa, sem_a)
        dx, dgain = project_back(da, own_ref, near_ref, far_ref, core, cos_ref, sin_ref, dk_ref, dv_ref, one_ref, h_ref[...].astype(f32), gain_a[...], wa, sem_a)
        dgain_a[...] = dgain
        state = g1_in[...] + dx
    if end:
        width = state.shape[1]
        g_out[:width, :] = last_ref[...]
        g_out[width:, :] = state.astype(bf16).T
        finish_a(wa, sem_a, (1, 1), (1, 2), (1, 3))
    else:
        refs = (*stage[:3], ins[3], *stage[3:], *outs[4:])
        ffn_back(state, core, chip, refs, (wa, sem_a, wb, sem_b, wd, sem_d), stage, sems, hbm)
        gone(stage[3:], hbm[3:], sems.at[pl.ds(3, 4)])
        if start:
            finish_a(wa, sem_a, (1, 0))


def back(start, end, sc, weights, tail, ffn, after=()):
    wa, wb = weights
    width = wa[0][0].shape[0]
    args = [sc, *wa[0], *wa[1]]
    specs = [SCALARS] + [LEFT] * 8
    scratch = scratch_a(width)
    if not end:
        args += [*wb[0], *wb[1]]
        specs += [LEFT] * 8
        scratch += scratch_ffn(width, wb[0][0].shape[2])
    args += list(tail)
    specs += [WHOLE] * len(tail)
    n = tail[0].shape[1 if start else 0]
    outs = []
    if not end:
        args += list(ffn)
        specs += [LEFT] * 3 + [WHOLE]
    if not start:
        outs += [shape((n, PIECE), bf16)] * 3 + [shape((1, width), f32)]
    if end:
        outs += [shape((2 * width, n), bf16)]
    else:
        hidden = ffn[0].shape[1]
        outs += [shape((n, width), bf16), shape((n, hidden), bf16), shape((n, hidden), bf16)]
        outs += [shape((n, width), f32), shape((3, n, PIECE), bf16), shape((1, width), f32), shape((width, n), bf16)]
    out_specs = [WHOLE] * len(outs)
    if not end:
        at = 0 if start else 4
        out_specs[at : at + 4] = [LEFT] * 4
        scratch += [pltpu.VMEM(x.shape, x.dtype) for x in (*ffn[:3], *outs[at : at + 4])]
        scratch += [pltpu.SemaphoreType.DMA((7,))]
    args += list(after)
    specs += [LEFT] * len(after)
    return pl.pallas_call(
        functools.partial(back_kernel, start, end, len(after)),
        out_shape=tuple(outs),
        in_specs=specs,
        out_specs=tuple(out_specs),
        scratch_shapes=scratch,
        cost_estimate=BRIEF,
        compiler_params=pltpu.CompilerParams(vmem_limit_bytes=LIMIT),
        name="back_end" if end else ("back_start" if start else "back_join"),
    )(*args)


def by_turn(core, chip):
    one = 1 + core
    return chip ^ one, chip ^ 3, chip, chip ^ (3 - one)


def turned(dst, blocks):
    n = blocks[0].shape[0]
    for i, block in enumerate(blocks):
        dst[:, i * n : (i + 1) * n] = block[...].T


def grad_ffn_kernel(sc, *rest):
    lefts, rights = rest[:4], rest[4:8]
    send_ref, keep_ref, token_ref, left, right = rest[-5:]
    token_ref[...] = jnp.zeros_like(token_ref)
    core, chip = sc[0], sc[1]
    n, cols = rights[0].shape[0], right.shape[1]
    turned(left, lefts)
    for i, m in enumerate(by_turn(core, chip)):
        at = pl.multiple_of(m * cols, 128)
        for j, block in enumerate(rights):
            right[j * n : (j + 1) * n, :] = block[:, pl.ds(at, cols)]
        out = send_ref if i < 2 else keep_ref
        out[i % 2] = nn(left[...], right[...]).astype(bf16)


def grad_ffn(sc, lefts, rights, after):
    n, width = lefts[0].shape
    cols = rights[0].shape[1] // 4
    out = shape((2, width, cols), bf16)
    return pl.pallas_call(
        grad_ffn_kernel,
        out_shape=(out, out, TOKEN),
        in_specs=[SCALARS] + [WHOLE] * 8 + [LEFT] * len(after),
        out_specs=(WHOLE,) * 3,
        scratch_shapes=[pltpu.VMEM((width, 4 * n), bf16), pltpu.VMEM((4 * n, cols), bf16)],
        cost_estimate=BRIEF,
        compiler_params=pltpu.CompilerParams(vmem_limit_bytes=LIMIT),
        name="grad_ffn",
    )(sc, *lefts, *rights, *after)


def grad_down_kernel(sc, *rest):
    lefts, rights = rest[:4], rest[4:8]
    send_ref, keep_ref, token_ref, left, right = rest[-5:]
    token_ref[...] = jnp.zeros_like(token_ref)
    n, (_, half, cols) = rights[0].shape[0], send_ref.shape
    turned(left, lefts)
    rows = pl.ds(pl.multiple_of(sc[0] * half, half), half)
    like = sc[2] & 1
    for h in range(2):
        for out, parity in ((send_ref, 1 - like), (keep_ref, like)):
            at = pl.multiple_of((2 * h + parity) * cols, 128)
            for j, block in enumerate(rights):
                right[j * n : (j + 1) * n, :] = block[:, pl.ds(at, cols)]
            out[h] = nn(left[rows, :], right[...]).astype(out.dtype)


def grad_down(sc, lefts, rights, after):
    n, width = lefts[0].shape
    cols = rights[0].shape[1] // 4
    block = (2, width // 2, cols)
    return pl.pallas_call(
        grad_down_kernel,
        out_shape=(shape(block, bf16), shape(block, bf16), TOKEN),
        in_specs=[SCALARS] + [WHOLE] * 8 + [LEFT] * len(after),
        out_specs=(WHOLE,) * 3,
        scratch_shapes=[pltpu.VMEM((width, 4 * n), bf16), pltpu.VMEM((4 * n, cols), bf16)],
        cost_estimate=BRIEF,
        compiler_params=pltpu.CompilerParams(vmem_limit_bytes=LIMIT),
        name="grad_down",
    )(sc, *lefts, *rights, *after)


def grad_attention_kernel(first, sc, *rest):
    a_refs, o_refs, rest = rest[:4], rest[4:8], rest[8:]
    queries, keys, values, outs, threes, ones = (rest[i : i + 2] for i in range(0, 12, 2))
    gain_a, gain_f = (rest[i : i + 2] for i in (12, 14))
    *outs_of, token_ref, left, right = rest[-5:]
    token_ref[...] = jnp.zeros_like(token_ref)
    core, chip = sc[0], sc[1]
    n, width = a_refs[0].shape
    turned(left.at[0], a_refs)
    gains = [g[0][...] + g[1][...] for g in (gain_a, gain_f)]
    gains = jnp.concatenate([*gains, jnp.zeros((6, width), f32)], axis=0).T
    gains = jnp.concatenate([gains, jnp.zeros((width, PIECE - KVW - 8), f32)], axis=1).astype(bf16)

    def fill(at, of_three, own_three, own_one, single):
        for j in range(2):
            for i in range(3):
                right[of_three + i, j * n : (j + 1) * n, :] = own_three[j][i]
                right[of_three + i, (j + 2) * n : (j + 3) * n, :] = threes[j][i]
            right[single, j * n : (j + 1) * n, :] = own_one[j][...]
            right[single, (j + 2) * n : (j + 3) * n, :] = ones[j][...]

    @pl.when(core == 0)
    def _():
        fill(0, 0, queries, keys, 3)

    @pl.when(core == 1)
    def _():
        turned(left.at[1], o_refs)
        fill(0, 1, outs, values, 0)

    for out, m in zip(outs_of, by_turn(core, chip)[first : first + 2]):
        which = jnp.where(m > 0, core, 0)
        out[...] = nn(left[which], right[m]).astype(bf16)
        out[:, KVW:] = gains


def grad_attention(first, sc, a, o, own, got, gains, after):
    n, width = a[0].shape
    out = shape((width, PIECE), bf16)
    return pl.pallas_call(
        functools.partial(grad_attention_kernel, first),
        out_shape=(out, out, TOKEN),
        in_specs=[SCALARS] + [WHOLE] * 24 + [LEFT] * len(after),
        out_specs=(WHOLE,) * 3,
        scratch_shapes=[pltpu.VMEM((2, width, 4 * n), bf16), pltpu.VMEM((4, 4 * n, PIECE), bf16)],
        cost_estimate=BRIEF,
        compiler_params=pltpu.CompilerParams(vmem_limit_bytes=LIMIT),
        name="grad_attention",
    )(sc, *a, *o, *own, *got, *gains, *after)


def lay_kernel(count, sc, *rest):
    token_ref = rest[-2]
    token_ref[...] = jnp.zeros_like(token_ref)
    rest = (*rest[:-2], rest[-1])
    mine, other, outs, kept = rest[:4], rest[4:8], rest[-1 - count : -1], rest[-1]
    core, chip = sc[0], sc[1]
    for kind, pieces in ((core, mine), (1 - core, other)):
        for who, piece in zip(whose(kind), pieces):
            kept[kind, chip ^ who] = piece[...]
    n = sum(o.shape[1] for o in outs[: 4 if len(outs) > 2 else 2]) // 8
    cols = [jnp.concatenate([kept[c, m, :, :n].astype(f32) for m in range(4)], axis=1) for c in range(2)]
    if len(outs) == 2:
        outs[0][...] = cols[0]
        outs[1][...] = cols[1]
    else:
        outs[0][...] = cols[0][:, : 3 * n]
        outs[1][...] = cols[0][:, 3 * n :]
        outs[2][...] = cols[1][:, :n]
        outs[3][...] = cols[1][:, n:]
        gains = kept[0, 0, :, n : n + 8].astype(f32) + kept[1, 0, :, n : n + 8].astype(f32)
        outs[4][...] = gains.T[:2]


def lay(sc, mine, other, widths, after):
    rows, n = mine[0].shape
    outs = tuple(shape((rows, w), f32) for w in widths)
    if len(widths) > 2:
        outs += (shape((2, rows), f32),)
    return pl.pallas_call(
        functools.partial(lay_kernel, len(outs)),
        out_shape=(*outs, TOKEN),
        in_specs=[SCALARS] + [WHOLE] * 8 + [LEFT] * len(after),
        out_specs=(WHOLE,) * (len(outs) + 1),
        scratch_shapes=[pltpu.VMEM((2, 4, rows, n), bf16)],
        cost_estimate=BRIEF,
        compiler_params=pltpu.CompilerParams(vmem_limit_bytes=24 << 20),
        name="lay",
    )(sc, *mine, *other, *after)


def pick_first_kernel(sc, q_ref, k_ref, v_ref, o_ref, gain_ref, out_ref, wide, tall, sem):
    rows = out_ref.shape[0]
    which = sc[0] * 4 + sc[1]

    def bring(source, into, first, last):
        @pl.when((which >= first) & (which <= last))
        def _():
            copy = pltpu.make_async_copy(source, into, sem)
            copy.start()
            copy.wait()

    bring(q_ref, wide, 0, 2)
    bring(k_ref, tall, 3, 3)
    bring(v_ref, tall, 4, 4)
    bring(o_ref, wide, 5, 7)
    pad = jnp.zeros((6, rows), f32)
    gains = jnp.concatenate([gain_ref[...], pad], axis=0).T.astype(bf16)
    rest = jnp.zeros((rows, PIECE - KVW - 8), bf16)
    for m in range(4):

        @pl.when((which == m) | (which == (m + 5 if m < 3 else 4)))
        def _():
            piece = wide[:, m * KVW : (m + 1) * KVW] if m < 3 else tall[...].T
            out_ref[...] = jnp.concatenate([piece, gains, rest], axis=1)


def pick_first(sc, query, key, value, out, gains):
    return pl.pallas_call(
        pick_first_kernel,
        out_shape=shape((query.shape[0], PIECE), bf16),
        in_specs=[SCALARS] + [LEFT] * 4 + [WHOLE],
        out_specs=WHOLE,
        scratch_shapes=[pltpu.VMEM(query.shape, bf16), pltpu.VMEM(key.shape, bf16), pltpu.SemaphoreType.DMA],
        cost_estimate=BRIEF,
        compiler_params=pltpu.CompilerParams(vmem_limit_bytes=LIMIT),
        name="pick_first",
    )(sc, query, key, value, out, gains)


def pick_kernel(sc, gate, up, down, *rest):
    out_ref, sems = rest[-2:]
    rows, cols = out_ref.shape[0] - ROWS, out_ref.shape[1]
    into = out_ref.at[:rows]
    start = pl.multiple_of(down_rows(sc[0], sc[1], down.shape[0]), 64)
    copy = pltpu.make_async_copy(down.at[pl.ds(start, ROWS), :], out_ref.at[rows:], sems.at[1])
    copy.start()
    at = pl.ds(pl.multiple_of(sc[1] * cols, 128), cols)
    for c, source in ((0, gate), (1, up)):

        @pl.when(sc[0] == c)
        def _():
            pltpu.make_async_copy(source.at[:, at], into, sems.at[0]).start()

    pltpu.make_async_copy(gate.at[:, at], into, sems.at[0]).wait()
    copy.wait()


def pick(sc, gate, up, down, after):
    return pl.pallas_call(
        pick_kernel,
        out_shape=shape((gate.shape[0] + ROWS, gate.shape[1] // 4), bf16),
        in_specs=[SCALARS] + [LEFT] * (3 + len(after)),
        out_specs=WHOLE,
        scratch_shapes=[pltpu.SemaphoreType.DMA((2,))],
        cost_estimate=BRIEF,
        compiler_params=pltpu.CompilerParams(vmem_limit_bytes=16 << 20),
        name="pick",
    )(sc, gate, up, down, *after)


def gains_kernel(first_ref, out_ref):
    for j in range(4):
        n = first_ref.shape[1]
        out_ref[:, j * n : (j + 1) * n] = first_ref[j, :, KVW : KVW + 8].astype(f32).T[:2]


def gains_of(first):
    return pl.pallas_call(
        gains_kernel,
        out_shape=shape((2, 4 * first.shape[1]), f32),
        in_specs=[WHOLE],
        out_specs=WHOLE,
        cost_estimate=BRIEF,
        compiler_params=pltpu.CompilerParams(vmem_limit_bytes=16 << 20),
        name="gains",
    )(first)


def stack_kernel(sc, *rest):
    parts, out_ref, sems = rest[:4], rest[-2], rest[-1]
    copies = [pltpu.make_async_copy(p, out_ref.at[sc[2] ^ s], sems.at[s]) for s, p in enumerate(parts)]
    for copy in copies:
        copy.start()
    for copy in copies:
        copy.wait()


def stack(sc, parts, after=()):
    return pl.pallas_call(
        stack_kernel,
        out_shape=shape((4,) + parts[0].shape, parts[0].dtype),
        in_specs=[SCALARS] + [LEFT] * (4 + len(after)),
        out_specs=WHOLE,
        scratch_shapes=[pltpu.SemaphoreType.DMA((4,))],
        cost_estimate=BRIEF,
        compiler_params=pltpu.CompilerParams(vmem_limit_bytes=16 << 20),
        name="stack",
    )(sc, *parts, *after)


def small(kernel, sc, args, outs, scratch, after, name):
    def with_token(*refs):
        at = len(refs) - len(scratch) - 1
        refs[at][...] = jnp.zeros_like(refs[at])
        kernel(*refs[:at], *refs[at + 1 :])

    return pl.pallas_call(
        with_token,
        out_shape=(*outs, TOKEN),
        in_specs=[SCALARS] + [WHOLE] * len(args) + [LEFT] * len(after),
        out_specs=(WHOLE,) * (len(outs) + 1),
        scratch_shapes=scratch,
        cost_estimate=BRIEF,
        compiler_params=pltpu.CompilerParams(vmem_limit_bytes=32 << 20),
        name=name,
    )(sc, *args, *after)


def sum_first(sc, keep, got, after, parts=1):
    def kernel(sc, *refs):
        rest = list(refs)

        def both(arrays):
            if len(arrays) == 2:
                return rest.pop(0), rest.pop(0)
            ref = rest.pop(0)
            return ref.at[0], ref.at[1]

        (own_kept, later_kept), (own_got, later_got) = both(keep), both(got)
        own_ref = rest[-1]
        for i, later_ref in enumerate(rest[-1 - parts : -1]):
            n = later_ref.shape[0]
            rows = slice(i * n, (i + 1) * n)
            later_ref[...] = (later_kept[rows].astype(f32) + later_got[rows].astype(f32)).astype(bf16)
        own_ref[...] = own_kept[...].astype(f32) + own_got[...].astype(f32)

    rows, cols = keep[0].shape[-2:]
    outs = [shape((rows // parts, cols), bf16)] * parts + [shape((rows, cols), f32)]
    return small(kernel, sc, [*keep, *got], outs, [], after, "sum_first")


def sum_second(sc, own, got, after):
    def kernel(sc, own_ref, *rest):
        gots, (send_ref, keep_ref, total) = rest[: len(got)], rest[-3:]
        n = total.shape[1]
        for j in range(4):
            part, at = divmod(j * n, gots[0].shape[0])
            total[j] = own_ref[j * n : (j + 1) * n, :] + gots[part][at : at + n, :].astype(f32)
        like = sc[2] & 1
        for h in range(2):
            send_ref[h] = total[2 * h + 1 - like].astype(bf16)
            keep_ref[h] = total[2 * h + like]

    rows, cols = own.shape
    part = (rows // 4, cols)
    outs = [shape((2,) + part, bf16), shape((2,) + part, f32)]
    return small(kernel, sc, [own, *got], outs, [pltpu.VMEM((4,) + part, f32)], after, "sum_second")


def sum_third(sc, keep, got, after):
    def kernel(sc, keep_ref, got_ref, *rest):
        send_ref, own_ref = rest[-2:]
        h = sc[2] >> 1
        send_ref[...] = (keep_ref[1 - h].astype(f32) + got_ref[1 - h].astype(f32)).astype(bf16)
        own_ref[...] = keep_ref[h].astype(f32) + got_ref[h].astype(f32)

    part = keep.shape[1:]
    return small(kernel, sc, [keep, got], [shape(part, bf16), shape(part, f32)], [], after, "sum_third")


def down_split(sc, own, got, after):
    def kernel(sc, own_ref, got_ref, *rest):
        send_ref, kept_ref, total = rest[-3:]
        n = total.shape[1]
        for m in range(4):
            rows = slice(m * n, (m + 1) * n)
            total[m] = own_ref[rows, :] + got_ref[rows, :].astype(f32)
        for i, m in enumerate(by_turn(sc[0], sc[1])):
            out = send_ref if i < 2 else kept_ref
            out[i % 2] = total[m].astype(bf16)

    rows, cols = own.shape
    out = shape((2, rows // 4, cols), bf16)
    return small(kernel, sc, [own, got], [out, out], [pltpu.VMEM((4, rows // 4, cols), f32)], after, "down_split")


def sum_two(sc, own, got, after):
    def kernel(sc, own_ref, got_ref, *rest):
        rest[-1][...] = (own_ref[...] + got_ref[...].astype(f32)).astype(bf16)

    return small(kernel, sc, [own, got], [shape(own.shape, bf16)], [], after, "sum_two")


def lay_down(sc, mine, other, after):
    def kernel(sc, *rest):
        out_ref, total = rest[-2:]
        n = total.shape[2]
        for kind, pieces in ((sc[0], rest[:4]), (1 - sc[0], rest[4:8])):
            for who, piece in zip(whose(kind), pieces):
                total[kind, sc[1] ^ who] = piece[...].astype(f32)
        for c in range(2):
            for m in range(4):
                at = (c * 4 + m) * n
                out_ref[at : at + n, :] = total[c, m]

    n, cols = mine[0].shape
    return small(kernel, sc, [*mine, *other], [shape((8 * n, cols), f32)], [pltpu.VMEM((2, 4, n, cols), f32)], after, "lay_down")


def hold(value, after):
    return pl.pallas_call(
        lambda *refs: None,
        out_shape=shape(value.shape, value.dtype),
        in_specs=[LEFT] * (1 + len(after)),
        out_specs=LEFT,
        input_output_aliases={0: 0},
        cost_estimate=BRIEF,
        compiler_params=pltpu.CompilerParams(vmem_limit_bytes=1 << 20),
        name="hold",
    )(value, *after)


def far_sum(sc, far, near, after):
    def kernel(sc, far_ref, near_ref, *rest):
        rest[-1][...] = (far_ref[...] + jnp.where(sc[0] == 1, near_ref[...].astype(f32), 0.0)).astype(bf16)

    return small(kernel, sc, [far, near], [shape(far.shape, bf16)], [], after, "far_sum")


def depart(sc, both, after):
    def kernel(sc, both_ref, *rest):
        out_ref, grad_ref = rest[-2:]
        n = out_ref.shape[0]
        out_ref[...] = both_ref[:n, :]
        grad_ref[...] = both_ref[n:, :].astype(f32)

    block = (both.shape[0] // 2, both.shape[1])
    return small(kernel, sc, [both], [shape(block, bf16), shape(block, f32)], [], after, "depart")


def sum_both(sc, own_b, got_b, own_d, got_d, after):
    def kernel(sc, b_ref, gb_ref, d_ref, gd_ref, *rest):
        out_ref = rest[-1]
        n = b_ref.shape[0]
        out_ref[:n, :] = (b_ref[...] + gb_ref[...].astype(f32)).astype(bf16)
        out_ref[n:, :] = (d_ref[...] + gd_ref[...].astype(f32)).astype(bf16)

    rows, cols = own_b.shape[0] + own_d.shape[0], own_b.shape[1]
    return small(kernel, sc, [own_b, got_b, own_d, got_d], [shape((rows, cols), bf16)], [], after, "sum_both")


def lay_both(sc, mine, other, rows, after):
    def kernel(sc, *rest):
        gate_ref, up_ref, down_ref, kept = rest[-4:]
        cols = kept.shape[3]
        n = kept.shape[2] - rows
        for kind, pieces in ((sc[0], rest[:4]), (1 - sc[0], rest[4:8])):
            for who, piece in zip(whose(kind), pieces):
                kept[kind, sc[1] ^ who] = piece[...].astype(f32)
        for c, out in enumerate((gate_ref, up_ref)):
            for m in range(4):
                out[:, m * cols : (m + 1) * cols] = kept[c, m, :rows]
                at = (c * 4 + m) * n
                down_ref[at : at + n, :] = kept[c, m, rows:]

    total, cols = mine[0].shape
    outs = [shape((rows, 4 * cols), f32)] * 2 + [shape((8 * (total - rows), cols), f32)]
    return small(kernel, sc, [*mine, *other], outs, [pltpu.VMEM((2, 4, total, cols), f32)], after, "lay_both")


CORE, SIDE, BACK = 1, 2, 4
rope_base = 10000.0
RUNS = 2


def flip(value, bit, bit1=None):
    count = lax.axis_size("dp")
    bits = (bit, bit if bit1 is None else bit1)
    return lax.ppermute(value, "dp", [(i, i ^ bits[i & 1]) for i in range(count)])


def flip_z(value, bit, where=lambda d, z: True):
    count, depth = lax.axis_size("dp"), lax.axis_size("fsdp")
    pairs = [(d * depth + z, d * depth + (z ^ bit)) for d in range(count) for z in range(depth) if where(d, z)]
    return lax.ppermute(value, ("dp", "fsdp"), pairs)


def home_to_work(value, back=False):
    count, depth = lax.axis_size("dp"), lax.axis_size("fsdp")
    pairs = []
    for d in range(count):
        for z in range(depth):
            there = (d & ~1) | (z & 1), 2 * (d & 1) + (z >> 1)
            pair = (d * depth + z, there[0] * depth + there[1])
            pairs.append(pair[::-1] if back else pair)
    return lax.ppermute(value, ("dp", "fsdp"), pairs)


def place():
    d, z = lax.axis_index("dp"), lax.axis_index("fsdp")
    return d & 1, (d >> 1) & 3, z


def turns(shard):
    far = flip_z(shard, 2)
    return shard, flip_z(shard, 1), far, flip_z(far, 1)


def plane_gather(piece):
    first, second = flip(piece, SIDE, BACK), flip(piece, BACK, SIDE)
    mine = (piece, first, second, flip(first, BACK, SIDE))
    return mine, tuple(flip(p, CORE) for p in mine)


def window(own):
    core, _, _ = place()
    depth = lax.axis_size("fsdp")
    far = lax.ppermute(own, "fsdp", [(z, z + 1) for z in range(0, depth, 2)])
    near = flip(jnp.where(core == 0, own, far), CORE)
    return far, near, own


def unwindow(sc, far, near):
    depth = lax.axis_size("fsdp")
    near = flip(near, CORE)
    far, token = far_sum(sc, far, near, [])
    return near, token, lax.ppermute(far, "fsdp", [(z + 1, z) for z in range(0, depth, 2)])


def over_groups(value):
    bit = 8
    while bit < lax.axis_size("dp"):
        value = (value.astype(f32) + flip(value, bit).astype(f32)).astype(bf16)
        bit *= 2
    return value


def spread(piece):
    return piece, flip(piece, SIDE, BACK), flip(piece, BACK, SIDE), flip(piece, SIDE | BACK)


def across(pieces):
    return tuple(flip(p, CORE) for p in pieces)


def body(tokens, segment_ids, attn_gain, query_weight, key_weight, value_weight, out_weight, ffn_gain, gate_weight, up_weight, down_weight, cotangent):
    core, chip, z = place()
    sc = jnp.stack([core, chip, z]).astype(jnp.int32)
    _, stretch, width = tokens.shape
    rows, depth = query_weight.shape[0], lax.axis_size("fsdp")
    block = 2 * (z & 1) + core
    positions = (block * stretch + jnp.arange(stretch)).astype(f32)
    freq = rope_base ** (-2.0 * jnp.arange(HEAD_DIM // 2, dtype=f32) / HEAD_DIM)
    angle = freq[:, None] * positions[None, :]
    cos, sin = jnp.cos(angle), jnp.sin(angle)

    gains = jnp.stack([attn_gain, ffn_gain]).astype(f32)
    parts_a = turns(pick_first(sc, query_weight, key_weight.T, value_weight.T, out_weight, gains))
    ids = jnp.broadcast_to((segment_ids[0] + 1).astype(bf16), (IDS, stretch))
    tokens = home_to_work(jnp.concatenate([tokens[0].T, ids]))
    piece_b = pick(sc, gate_weight, up_weight, down_weight.T, parts_a[1:2])
    whole_a = stack(sc, parts_a, [piece_b])
    gains = gains_of(whole_a)
    gain_a, gain_f = gains[:1], gains[1:]
    wa = plane_gather(whole_a.reshape(depth * rows, PIECE))
    side_b = flip_z(piece_b, 1)
    far_b = hold(flip_z(piece_b, 2), [wa[0][1], wa[0][2], side_b])
    whole_b = stack(sc, (piece_b, side_b, far_b, flip_z(far_b, 1)), [wa[0][3]])
    first_b, second_b = flip(whole_b, SIDE, BACK), flip(whole_b, BACK, SIDE)

    h_0, a0, q0, own = pre(sc, tokens, gain_a, cos, sin, *wa, [whole_b])
    kv0 = window(own)
    first_b = hold(first_b, [kv0[0], second_b])
    opposite_b = flip(first_b, BACK, SIDE)
    o0, lse0 = attend(q0, kv0)
    wb = whole_b, first_b, second_b, hold(opposite_b, [o0])
    wb = wb, across(wb)
    weights = wa, wb
    cot = home_to_work(cotangent[0].T)
    mixed0, h1_0, b0, gate0, up0, z0, h_1, a1, q1, own = post(False, [], sc, o0, h_0, gain_f, gain_a, cos, sin, own, *weights)
    kv1 = window(own)
    across_0 = across((a0, b0, mixed0, z0))
    o1, lse1 = attend(q1, kv1, across_0)
    mixed1, h1_1, b1, gate1, up1, z1, output = post(True, [cot], sc, o1, h_1, gain_f, gain_a, cos, sin, own, *weights)
    across_1 = across((a1, b1, mixed1, z1))

    gb1, act1, away1, g1, p1, dgain_f1, do = back(True, False, sc, weights, [cot], [gate1, up1, h1_1, gain_f])
    across_2 = across((gb1, away1))
    dq1, three1, far, near, own = attend_back(sc, p1, q1, kv1, lse1, do, cos, sin)
    near, _, far = unwindow(sc, far, near)
    (three1,) = across((three1,))
    tail = [g1, dq1, own, near, far, h_1, gain_a, cos, sin]
    dk1, dv1, one1, dgain_a1, gb0, act0, away0, g1, p0, dgain_f0, do = back(False, False, sc, weights, tail, [gate0, up0, h1_0, gain_f], [three1, *across_2, *across_1])

    away0, gb0_, one1 = across((away0, gb0, one1))
    send_b, keep_b, done = grad_ffn(sc, [b1, b0, across_1[1], across_0[1]], [act1, act0, across_2[1], away0], [])
    got_b = flip(send_b, SIDE, BACK)
    dq0, three0, far, near, own = attend_back(sc, p0, q0, kv0, lse0, do, cos, sin, [one1, done])
    near, done, far = unwindow(sc, far, near)
    send_d, keep_d, done = grad_down(sc, [gb1, gb0, across_2[0], gb0_], [z1, z0, across_1[3], across_0[3]], [done])
    got_d = flip_z(send_d, 1)
    (three0,) = across((three0,))
    tail = [g1, dq0, own, near, far, h_0, gain_a, cos, sin, output]
    dk0, dv0, one0, dgain_a0, leaving = back(False, True, sc, weights, tail, None, [done])
    later_b, own_b, done = sum_first(sc, [keep_b], [got_b], [dgain_a0])
    more_b = flip(later_b, BACK, SIDE)
    own = [dq1, dq0, dk1, dk0, dv1, dv0, p1, p0]
    got = [three1, three0, one1, flip(one0, CORE)]
    args = [a1, a0, across_1[0], across_0[0]], [mixed1, mixed0, across_1[2], across_0[2]], own, got, [dgain_a1, dgain_a0, dgain_f1, dgain_f0]
    *send_a, done = grad_attention(0, sc, *args, [done])
    got_a = [flip(v, SIDE, BACK) for v in send_a]
    send_d, keep_d, done = sum_third(sc, keep_d, got_d, [done])
    got_d = flip_z(send_d, 2)
    send_b, ring_b, done = sum_second(sc, own_b, [more_b], [done])
    got_b = flip_z(send_b, 1)
    *keep_a, done = grad_attention(2, sc, *args, [done])
    *later_a, own_a, done = sum_first(sc, keep_a, got_a, [done], 2)
    more_a = [flip(v, BACK, SIDE) for v in later_a]
    send_b, ring_b, done = sum_third(sc, ring_b, got_b, [done])
    got_b = flip_z(send_b, 2)
    send_a, ring_a, done = sum_second(sc, own_a, more_a, [done])
    got_a = flip_z(send_a, 1)
    send_d, keep_d, done = down_split(sc, keep_d, got_d, [done])
    got_d = flip(send_d, SIDE, BACK)
    later_d, own_d, done = sum_first(sc, [keep_d], [got_d], [done])
    more_d = flip(later_d, BACK, SIDE)
    send_a, ring_a, first = sum_third(sc, ring_a, got_a, [done])
    got_a = flip_z(send_a, 2)
    piece_b, done = sum_both(sc, ring_b, got_b, own_d, more_d, [first])
    all_b = spread(over_groups(piece_b))
    piece_a, done = sum_two(sc, ring_a, got_a, [done, all_b[1]])
    all_a = spread(over_groups(piece_a))
    leaving = home_to_work(hold(leaving, [first]), back=True)
    output, grad_tokens, done = depart(sc, leaving, [done])
    grad_gate, grad_up, grad_down_, done = lay_both(sc, all_b, across(all_b), ring_a.shape[0], [done])
    grad_query, grad_key, grad_value, grad_out, dgains, done = lay(sc, all_a, across(all_a), (width, KVW, KVW, width), [done])
    output, grad_tokens = output.T, grad_tokens.T
    return (output[None], grad_tokens[None], dgains[0], grad_query, grad_key, grad_value, grad_out, dgains[1], grad_gate, grad_up, grad_down_.T)


def solution(mesh):
    wide, rows, shard = P("dp", "fsdp", None), P("dp", "fsdp"), P("fsdp", None)
    in_specs = (wide, rows, P("fsdp"), shard, shard, shard, shard, P("fsdp"), shard, shard, shard, wide)
    out_specs = (wide, wide, P("fsdp"), shard, shard, shard, shard, P("fsdp"), shard, shard, shard)
    return jax.shard_map(body, mesh=mesh, in_specs=in_specs, out_specs=out_specs, check_vma=False)
```
